32 devices in a mesh: dp: 8 (over z, y), space: 4 (over x, core).
Axes of the slice: x: 2, y: 2, z: 4, core: 2. Of those that a mesh axis runs over, the one named last changes fastest.
Arguments:
- activations: bfloat16 [8, 64, 32, 48, 128], P('dp', None, 'space'), may hold values from -6 to 6
- cotangent: bfloat16 [8, 64, 32, 48, 128], P('dp', None, 'space'), may hold values from -6 to 6
- mode_weights: bfloat16 [2048, 64, 128], P(('space', 'dp')), may hold values from -6 to 6
- pointwise: bfloat16 [64, 64], replicated, may hold values from -0.75 to 0.75
- offsets: float32 [64], replicated, may hold values from -3 to 3
Outputs:
- grad_in: bfloat16 [8, 64, 32, 48, 128], P('dp', None, 'space')
- grad_spectral: float32 [2048, 64, 128], P(('space', 'dp'))
The draws below stay inside these ranges and needn't reach their ends.
All inputs are finite; a program needn't handle non-finite values.
Results may differ from the reference program's by a relative error of at most 0.02.
Values may be sent and summed in bfloat16 or wider, within the bound.
No kernel may reach another device: no remote copies, remote signals or barrier semaphores. Data moves between devices by JAX's collectives and lax.ppermute only.
A program may use at most 128 MiB of HBM per device.

```python
import math
import jax
import jax.numpy as jnp
from jax import lax

C = 64
MX = 16
MY = 16
MZ = 8
NX = 32
NY = 48
NZ = 128
BATCH = 8
MODES = 2048


def block_scale(stream_key, shape, shards, low, high):
    def one(position, parts):
        steps = jax.random.uniform(jax.random.fold_in(jax.random.fold_in(stream_key, 6), position), (parts,), jnp.float32, low / len(shards), high / len(shards))
        return jnp.repeat(jnp.exp(steps), shape[position] // parts).reshape((-1,) + (1,) * (len(shape) - position - 1))

    loudness = one(*shards[0])
    for cut in shards[1:]:
        loudness = loudness * one(*cut)
    return loudness


def gaussian(rng, dims, width, bound, pieces=(), kind=jnp.bfloat16):
    drawn = width * jax.random.normal(rng, dims, jnp.float32)
    if pieces:
        drawn = drawn * block_scale(rng, dims, pieces, -0.22, 0.18)
    return jnp.clip(drawn, -bound, bound).astype(kind)


def setup_inputs(seed: int = 0) -> dict:
    keys = jax.random.split(jax.random.key(seed), 6)
    activations = gaussian(keys[0], (BATCH, C, NX, NY, NZ), 1.0, 6.0, ((0, 8), (2, 4)))
    cotangent = gaussian(keys[1], (BATCH, C, NX, NY, NZ), 1.0, 6.0, ((0, 8), (2, 4)))
    mode_weights = gaussian(keys[2], (MODES, C, 2 * C), 1.0, 6.0, ((0, 32),))
    pointwise = gaussian(keys[3], (C, C), C ** -0.5, 0.75)
    offsets = gaussian(keys[4], (C,), 0.5, 3.0, (), jnp.float32)
    return dict(activations=activations, cotangent=cotangent, mode_weights=mode_weights, pointwise=pointwise, offsets=offsets)


def centered(count):
    index = jnp.arange(count, dtype=jnp.int32)
    return jnp.where(index < count // 2, index, index - count)


def plane_tables(rows_y, rows_z, modes_y, modes_z):
    along_y = jnp.arange(rows_y, dtype=jnp.int32)[:, None, None, None]
    along_z = jnp.arange(rows_z, dtype=jnp.int32)[None, :, None, None]
    freq_y = centered(modes_y)[None, None, :, None]
    freq_z = jnp.arange(modes_z, dtype=jnp.int32)[None, None, None, :]
    phase = jnp.mod(freq_y * along_y * rows_z + freq_z * along_z * rows_y, rows_y * rows_z)
    theta = phase.astype(jnp.float32) * (2.0 * math.pi / (rows_y * rows_z))
    cosine = jnp.cos(theta)
    sine = jnp.sin(theta)
    forward = jnp.stack([cosine, -sine], -1).reshape(rows_y * rows_z, modes_y * modes_z * 2)
    scaled = jnp.where(freq_z == 0, 1.0, 2.0).astype(jnp.float32) / (rows_y * rows_z)
    inverse = jnp.stack([cosine * scaled, -sine * scaled], -1).reshape(rows_y * rows_z, modes_y * modes_z * 2).T
    return forward.astype(jnp.bfloat16), inverse.astype(jnp.bfloat16)


def line_tables(length, modes):
    along = jnp.arange(length, dtype=jnp.int32)[:, None]
    freq = centered(modes)[None, :]
    phase = jnp.mod(freq * along, length)
    theta = phase.astype(jnp.float32) * (2.0 * math.pi / length)
    cosine = jnp.cos(theta)
    sine = jnp.sin(theta)
    first = jnp.stack([cosine, -sine], -1)
    second = jnp.stack([sine, cosine], -1)
    forward = jnp.stack([first, second], 1).reshape(2 * length, 2 * modes)
    inv_first = jnp.stack([cosine.T, sine.T], -1) / length
    inv_second = jnp.stack([-sine.T, cosine.T], -1) / length
    inverse = jnp.stack([inv_first, inv_second], 1).reshape(2 * modes, 2 * length)
    return forward.astype(jnp.bfloat16), inverse.astype(jnp.bfloat16)


def expand_weights(weights):
    half = weights.shape[1]
    real_part = weights[:, :, :half]
    imag_part = weights[:, :, half:]
    upper = jnp.concatenate([real_part, imag_part], axis=2)
    lower = jnp.concatenate([-imag_part, real_part], axis=2)
    return jnp.concatenate([upper, lower], axis=1)


def outer_sum(left, right):
    return jnp.einsum("mbi,mbo->mio", left.astype(jnp.float32), right.astype(jnp.float32), precision=lax.Precision.HIGHEST)


def weight_terms(spec_in, spec_grad):
    half = spec_in.shape[2] // 2
    in_real = spec_in[:, :, :half]
    in_imag = spec_in[:, :, half:]
    gr_real = spec_grad[:, :, :half]
    gr_imag = spec_grad[:, :, half:]
    real_term = outer_sum(in_real, gr_real) + outer_sum(in_imag, gr_imag)
    imag_term = outer_sum(in_real, gr_imag) - outer_sum(in_imag, gr_real)
    return jnp.concatenate([real_term, imag_term], axis=2)


def product(left, right, form):
    return jnp.einsum(form, left.astype(jnp.float32), right.astype(jnp.float32), precision=lax.Precision.HIGHEST)


def to_spectra(planes, table):
    planes_yz = MY * MZ
    lines = planes.reshape(C, NX, planes_yz, 2).transpose(0, 2, 1, 3).reshape(C, planes_yz, 2 * NX)
    spectra = product(lines, table, "cpl,lk->cpk").astype(jnp.bfloat16)
    return spectra.reshape(C, planes_yz, MX, 2).transpose(1, 2, 3, 0).reshape(MODES, 2 * C)


def to_planes(spectra, table):
    planes_yz = MY * MZ
    lines = spectra.reshape(planes_yz, MX, 2, C).transpose(3, 0, 1, 2).reshape(C, planes_yz, 2 * MX)
    lines = product(lines, table, "cpk,kl->cpl").astype(jnp.bfloat16)
    return lines.reshape(C, planes_yz, NX, 2).transpose(0, 2, 1, 3).reshape(C, NX, 2 * planes_yz)


def gelu_slope(value):
    cdf = 0.5 * (1.0 + lax.erf(value * 0.7071067811865476))
    density = jnp.exp(-0.5 * value * value) * 0.3989422804014327
    return cdf + value * density


def reference(activations, cotangent, mode_weights, pointwise, offsets):
    plane_fwd, plane_inv = plane_tables(NY, NZ, MY, MZ)
    line_fwd, line_inv = line_tables(NX, MX)
    blocks = expand_weights(mode_weights)

    def one_sample(pair):
        field, upstream = pair
        flat = field.reshape(C, NX, NY * NZ)
        planes = product(flat, plane_fwd, "cxn,nk->cxk").astype(jnp.bfloat16)
        spec_in = to_spectra(planes, line_fwd)
        spec_out = product(spec_in, blocks, "mi,mio->mo").astype(jnp.bfloat16)
        line_back = to_planes(spec_out, line_inv)
        spectral = product(line_back, plane_inv, "cxk,kn->cxn")
        local_part = product(pointwise, flat, "io,ixn->oxn")
        summed = spectral + local_part + offsets[:, None, None]
        slope_grad = (upstream.reshape(C, NX, NY * NZ).astype(jnp.float32) * gelu_slope(summed)).astype(jnp.bfloat16)
        back_plane = product(slope_grad, plane_inv, "cxn,kn->cxk").astype(jnp.bfloat16)
        spec_grad = to_spectra(back_plane, line_inv.T)
        spec_dx = product(spec_grad, blocks, "mo,mio->mi").astype(jnp.bfloat16)
        line_dx = to_planes(spec_dx, line_fwd.T)
        total = product(line_dx, plane_fwd, "cxk,nk->cxn") + product(pointwise, slope_grad, "io,oxn->ixn")
        return total.astype(jnp.bfloat16).reshape(C, NX, NY, NZ), spec_in, spec_grad

    grad_in, all_in, all_grad = lax.map(one_sample, (activations, cotangent))
    grad_spectral = weight_terms(all_in.transpose(1, 0, 2), all_grad.transpose(1, 0, 2))
    return grad_in, grad_spectral
```

```python
import functools
import math

import jax
import jax.numpy as jnp
import ml_dtypes
import numpy as np
from jax import lax
from jax.experimental import pallas as pl
from jax.experimental.pallas import tpu as pltpu
from jax.sharding import PartitionSpec as P

MX = 16
MY = 16
MZ = 8
NX = 32


def centered(count):
    index = jnp.arange(count, dtype=jnp.int32)
    return jnp.where(index < count // 2, index, index - count)


def plane_tables(rows_y, rows_z, modes_y, modes_z):
    along_y = jnp.arange(rows_y, dtype=jnp.int32)[:, None, None, None]
    along_z = jnp.arange(rows_z, dtype=jnp.int32)[None, :, None, None]
    freq_y = centered(modes_y)[None, None, :, None]
    freq_z = jnp.arange(modes_z, dtype=jnp.int32)[None, None, None, :]
    phase = jnp.mod(freq_y * along_y * rows_z + freq_z * along_z * rows_y, rows_y * rows_z)
    theta = phase.astype(jnp.float32) * (2.0 * math.pi / (rows_y * rows_z))
    cosine = jnp.cos(theta)
    sine = jnp.sin(theta)
    forward = jnp.stack([cosine, -sine], -1).reshape(rows_y * rows_z, modes_y * modes_z * 2)
    scaled = jnp.where(freq_z == 0, 1.0, 2.0).astype(jnp.float32) / (rows_y * rows_z)
    inverse = (
        jnp.stack([cosine * scaled, -sine * scaled], -1)
        .reshape(rows_y * rows_z, modes_y * modes_z * 2)
        .T
    )
    return (forward.astype(jnp.bfloat16), inverse.astype(jnp.bfloat16))


def line_tables(length, modes):
    along = jnp.arange(length, dtype=jnp.int32)[:, None]
    freq = centered(modes)[None, :]
    phase = jnp.mod(freq * along, length)
    theta = phase.astype(jnp.float32) * (2.0 * math.pi / length)
    cosine = jnp.cos(theta)
    sine = jnp.sin(theta)
    first = jnp.stack([cosine, -sine], -1)
    second = jnp.stack([sine, cosine], -1)
    forward = jnp.stack([first, second], 1).reshape(2 * length, 2 * modes)
    inv_first = jnp.stack([cosine.T, sine.T], -1) / length
    inv_second = jnp.stack([-sine.T, cosine.T], -1) / length
    inverse = jnp.stack([inv_first, inv_second], 1).reshape(2 * modes, 2 * length)
    return (forward.astype(jnp.bfloat16), inverse.astype(jnp.bfloat16))


def expand_weights(weights):
    half = weights.shape[1]
    real_part = weights[:, :, :half]
    imag_part = weights[:, :, half:]
    upper = jnp.concatenate([real_part, imag_part], axis=2)
    lower = jnp.concatenate([-imag_part, real_part], axis=2)
    return jnp.concatenate([upper, lower], axis=1)


def outer_sum(left, right):
    return jnp.einsum("mbi,mbo->mio", left, right, preferred_element_type=jnp.float32)


def weight_terms(spec_in, spec_grad):
    half = spec_in.shape[2] // 2
    in_real = spec_in[:, :, :half]
    in_imag = spec_in[:, :, half:]
    gr_real = spec_grad[:, :, :half]
    gr_imag = spec_grad[:, :, half:]
    real_term = outer_sum(in_real, gr_real) + outer_sum(in_imag, gr_imag)
    imag_term = outer_sum(in_real, gr_imag) - outer_sum(in_imag, gr_real)
    return jnp.concatenate([real_term, imag_term], axis=2)


def to_modes(slab, table, modes_x):
    samples, channels, width, pairs = slab.shape
    moved = lax.all_to_all(slab, "space", split_axis=3, concat_axis=2, tiled=True)
    length = moved.shape[2]
    local = moved.shape[3] // 2
    lines = moved.reshape(samples, channels, length, local, 2).transpose(0, 1, 3, 2, 4)
    lines = lines.reshape(samples, channels, local, 2 * length)
    spectra = jnp.dot(lines, table, preferred_element_type=jnp.float32).astype(jnp.bfloat16)
    spectra = spectra.reshape(samples, channels, local, modes_x, 2).transpose(2, 3, 0, 4, 1)
    return spectra.reshape(local * modes_x, samples, 2 * channels)


def to_slab(spectra, table, modes_x, channels):
    count, samples, doubled = spectra.shape
    local = count // modes_x
    lines = spectra.reshape(local, modes_x, samples, 2, channels).transpose(2, 4, 0, 1, 3)
    lines = lines.reshape(samples, channels, local, 2 * modes_x)
    lines = jnp.dot(lines, table, preferred_element_type=jnp.float32).astype(jnp.bfloat16)
    length = lines.shape[3] // 2
    lines = lines.reshape(samples, channels, local, length, 2).transpose(0, 1, 3, 2, 4)
    lines = lines.reshape(samples, channels, length, 2 * local)
    return lax.all_to_all(lines, "space", split_axis=2, concat_axis=3, tiled=True)


def to_owners(spectra):
    return lax.all_to_all(spectra, "dp", split_axis=0, concat_axis=1, tiled=True)


def from_owners(spectra):
    return lax.all_to_all(spectra, "dp", split_axis=1, concat_axis=0, tiled=True)


def gelu_slope(value):
    cdf = 0.5 * (1.0 + lax.erf(value * 0.7071067811865476))
    density = jnp.exp(-0.5 * value * value) * 0.3989422804014327
    return cdf + value * density


def general_body(activations, cotangent, mode_weights, pointwise, offsets):
    samples, channels, width, rows_y, rows_z = activations.shape
    plane_fwd, plane_inv = plane_tables(rows_y, rows_z, MY, MZ)
    line_fwd, line_inv = line_tables(NX, MX)
    flat = activations.reshape(samples, channels, width, rows_y * rows_z)
    planes = jnp.dot(flat, plane_fwd, preferred_element_type=jnp.float32).astype(jnp.bfloat16)
    spec_in = to_modes(planes, line_fwd, MX)
    blocks = expand_weights(mode_weights)
    held_in = to_owners(spec_in)
    held_out = jnp.einsum(
        "mbi,mio->mbo", held_in, blocks, preferred_element_type=jnp.float32
    ).astype(jnp.bfloat16)
    spec_out = from_owners(held_out)
    returned = to_slab(spec_out, line_inv, MX, channels)
    spectral = jnp.dot(returned, plane_inv, preferred_element_type=jnp.float32)
    local_part = jnp.einsum("io,bixn->boxn", pointwise, flat, preferred_element_type=jnp.float32)
    summed = spectral + local_part + offsets[None, :, None, None]
    upstream = cotangent.reshape(flat.shape).astype(jnp.float32)
    slope_grad = (upstream * gelu_slope(summed)).astype(jnp.bfloat16)
    back_plane = jnp.dot(slope_grad, plane_inv.T, preferred_element_type=jnp.float32).astype(
        jnp.bfloat16
    )
    spec_grad = to_modes(back_plane, line_inv.T, MX)
    held_grad = to_owners(spec_grad)
    held_dx = jnp.einsum(
        "mbo,mio->mbi", held_grad, blocks, preferred_element_type=jnp.float32
    ).astype(jnp.bfloat16)
    spec_dx = from_owners(held_dx)
    grad_spectral = weight_terms(held_in, held_grad)
    line_dx = to_slab(spec_dx, line_fwd.T, MX, channels)
    total = jnp.dot(line_dx, plane_fwd.T, preferred_element_type=jnp.float32)
    total = total + jnp.einsum(
        "io,boxn->bixn", pointwise, slope_grad, preferred_element_type=jnp.float32
    )
    grad_in = total.astype(jnp.bfloat16).reshape(activations.shape)
    return (grad_in, grad_spectral)


BF16 = jnp.bfloat16
F32 = jnp.float32
GROUP = 16
TILE = 16
MIB = 1024 * 1024


def rounded(table):
    return np.asarray(table, np.float32).astype(ml_dtypes.bfloat16)


def angles(freq, points, length):
    phase = np.mod(np.outer(freq, points), length)
    return (phase * (2.0 * math.pi / length)).astype(np.float64)


def signed(count):
    index = np.arange(count)
    return np.where(index < count // 2, index, index - count)


def z_table(rows_z):
    theta = angles(np.arange(MZ), np.arange(rows_z), rows_z)
    pair = np.stack([np.cos(theta), -np.sin(theta)])
    table = np.einsum("rkz,cd->czrkd", pair, np.eye(GROUP))
    return rounded(table.reshape(GROUP * rows_z, 2 * MZ * GROUP))


def y_table(rows_y, width):
    theta = angles(signed(MY), np.arange(rows_y), rows_y)
    cosine, sine = np.cos(theta), np.sin(theta)
    turn = np.stack([np.stack([cosine, sine]), np.stack([-sine, cosine])])
    table = np.einsum("rsjy,xw->jxrswy", turn, np.eye(width))
    return rounded(table.reshape(MY * width * 2, 2 * width * rows_y))


def lane_order(channels, per):
    count = MZ * channels
    source = np.arange(count).reshape(channels // GROUP, MZ // per, per, GROUP)
    target = source.transpose(1, 2, 0, 3).reshape(-1)
    table = np.zeros((count, count))
    table[target, np.arange(count)] = 1.0
    return rounded(table)


def x_tables(samples, slabs, length):
    theta = angles(signed(MX), np.arange(length), length)
    cosine, sine = np.cos(theta), np.sin(theta)
    forward = np.stack([np.stack([cosine, sine]), np.stack([-sine, cosine])])
    inverse = np.stack([np.stack([cosine, sine]), np.stack([-sine, cosine])]) / length
    same = np.eye(samples)
    rows = MX * 2 * samples

    def lay(turn):
        turn = turn.reshape(2, 2, MX, slabs, length // slabs)
        table = np.einsum("arqsx,bd->qabsdxr", turn, same)
        return rounded(table.reshape(rows, samples * length * 2))

    return lay(forward), lay(inverse)


def dot(left, right):
    return jnp.dot(left, right, preferred_element_type=F32)


def gelu_slope_rows(value):
    size = jnp.abs(value)
    t = pl.reciprocal(1.0 + (0.3275911 * math.sqrt(0.5)) * size, approx=True)
    decay = jnp.exp2(value * value * (-0.5 * math.log2(math.e)))
    tail = 0.5 * 1.061405429 * t - 0.5 * 1.453152027
    tail = tail * t + 0.5 * 1.421413741
    tail = tail * t - 0.5 * 0.284496736
    tail = tail * t + 0.5 * 0.254829592
    part = (size * (1.0 / math.sqrt(2.0 * math.pi)) - tail * t) * decay
    return jnp.where(value >= 0.0, 1.0 + part, -part)


def analyse(field, ztab, ytab):
    spectra = dot(jnp.concatenate(field, axis=1), ztab).astype(BF16)
    half = spectra.shape[1] // 2
    return dot(ytab, jnp.concatenate([spectra[:, :half], spectra[:, half:]], axis=0))


def deliver(held, order, message, per, channels):
    ordered = dot(held, order).astype(BF16)
    parts = MZ // per
    rows = message.shape[1]
    lanes = per * channels
    for part in range(parts):
        block = ordered[:, part * lanes : (part + 1) * lanes]
        for j in range(MY):
            message[j * parts + part] = block[j * rows : (j + 1) * rows]


def receive(message, order_back, ytab_back, scale, held, per):
    parts = MZ // per
    blocks = message[...]
    blocks = blocks.reshape(MY, parts, *blocks.shape[1:])
    lanes = [blocks[:, part].reshape(-1, blocks.shape[3]) for part in range(parts)]
    ordered = dot(jnp.concatenate(lanes, axis=1), order_back[...]).astype(BF16)
    lines = dot(ytab_back[...], ordered)
    if scale is not None:
        lines = lines * scale[...]
    lines = lines.astype(BF16)
    rows = lines.shape[0] // 2
    wide = MZ * GROUP
    for group in range(held.shape[0]):
        piece = lines[:, group * wide : (group + 1) * wide]
        held[group] = jnp.concatenate([piece[:rows], piece[rows:]], axis=1)


def plane_kernel(per, channels, field, ztab, ytab, order, message, held):
    step = pl.program_id(0)
    rows_z = field.shape[-1]
    blocks = [field[0, c].reshape(-1, rows_z) for c in range(GROUP)]
    held[step] = analyse(blocks, ztab[...], ytab[...]).astype(BF16)

    @pl.when(step == pl.num_programs(0) - 1)
    def _():
        whole = jnp.concatenate([held[g] for g in range(held.shape[0])], axis=1)
        deliver(whole, order[...], message, per, channels)


def slope_kernel(
    per, channels, arrived, local, cotangent, order_back, ytab_back, ztab_back, scale, ztab, ytab, order,
    slope, message, held, back,
):
    step = pl.program_id(0)
    width, rows_y, rows_z = local.shape[1:]

    @pl.when(step == 0)
    def _():
        receive(arrived, order_back, ytab_back, scale, held, per)

    lines = held[step]
    blocks = []
    for first in range(0, GROUP, 2):
        field = dot(lines, ztab_back[:, first * rows_z : (first + 2) * rows_z])
        for offset in range(2):
            c = first + offset
            value = field[:, offset * rows_z : (offset + 1) * rows_z]
            value = value + local[c].reshape(-1, rows_z).astype(F32)
            upstream = cotangent[0, c].reshape(-1, rows_z).astype(F32)
            result = (upstream * gelu_slope_rows(value)).astype(BF16)
            slope[c] = result.reshape(width, rows_y, rows_z)
            blocks.append(result)
    plane = analyse(blocks, ztab[...], ytab[...]) * scale[:, : MZ * GROUP]
    back[step] = plane.astype(BF16)

    @pl.when(step == pl.num_programs(0) - 1)
    def _():
        whole = jnp.concatenate([back[g] for g in range(back.shape[0])], axis=1)
        deliver(whole, order[...], message, per, channels)


def field_kernel(per, arrived, local, order_back, ytab_back, ztab_back, out, held):
    step = pl.program_id(0)
    width, rows_y, rows_z = local.shape[1:]

    @pl.when(step == 0)
    def _():
        receive(arrived, order_back, ytab_back, None, held, per)

    lines = held[step]
    for first in range(0, GROUP, 2):
        field = dot(lines, ztab_back[:, first * rows_z : (first + 2) * rows_z])
        for offset in range(2):
            c = first + offset
            value = field[:, offset * rows_z : (offset + 1) * rows_z]
            value = value + local[c].reshape(-1, rows_z).astype(F32)
            out[0, c] = value.astype(BF16).reshape(width, rows_y, rows_z)


def pointwise_kernel(turned, field, mix, offsets, out, table, shift):
    channels = mix.shape[0]
    width, rows_y, rows_z = field.shape[1:]
    size = channels * TILE

    @pl.when(pl.program_id(0) == 0)
    def _():
        row = lax.broadcasted_iota(jnp.int32, (size, channels), 0) // TILE
        column = lax.broadcasted_iota(jnp.int32, (size, channels), 1)
        spread = jnp.where(row == column, 1.0, 0.0).astype(BF16)
        tall = lax.dot_general(
            spread, mix[...], (((1,), (1 if turned else 0,)), ((), ())), preferred_element_type=F32
        ).astype(BF16)
        whole = lax.dot_general(
            tall, spread, (((1,), (1,)), ((), ())), preferred_element_type=F32
        )
        place = lax.broadcasted_iota(jnp.int32, (size, size), 0) % TILE
        other = lax.broadcasted_iota(jnp.int32, (size, size), 1) % TILE
        table[...] = jnp.where(place == other, whole, 0.0).astype(BF16)
        if offsets is not None:
            for c in range(channels):
                shift[c] = jnp.full((1, rows_z), offsets[c], F32)

    for start in range(0, rows_y, TILE):
        rows = [field[:, x, start : start + TILE, :].reshape(size, rows_z) for x in range(width)]
        mixed = dot(table[...], jnp.concatenate(rows, axis=1))
        for x in range(width):
            value = mixed[:, x * rows_z : (x + 1) * rows_z].reshape(channels, TILE, rows_z)
            if offsets is not None:
                value = value + shift[...]
            out[:, x, start : start + TILE, :] = value.astype(BF16)


def spread_pair(first, second):
    nothing = jnp.zeros_like(first)
    upper = jnp.concatenate([first, nothing], axis=1)
    lower = jnp.concatenate([nothing, second], axis=1)
    return jnp.concatenate([upper, lower], axis=0)


def low_half(shape):
    return lax.broadcasted_iota(jnp.int32, shape, 1) < shape[1] // 2


def mix_kernel(per, samples, arrived, weights, line, line_back, spec_in, message, held):
    rows = 2 * samples
    lanes = 2 * weights.shape[1]
    low = low_half((samples, lanes))
    flat = arrived[...].reshape(-1, arrived.shape[2])
    spectra = dot(line[...], flat).astype(BF16)
    spec_in[...] = spectra
    for q in range(MX):
        for first in range(0, per, 2):
            block = spread_pair(weights[first * MX + q], weights[(first + 1) * MX + q])
            place = first // 2 * lanes
            terms = dot(spectra[q * rows : (q + 1) * rows, place : place + lanes], block)
            mixed = []
            for side in range(2):
                part = terms[:, side * lanes : (side + 1) * lanes]
                turned = pltpu.roll(part[samples:], lanes // 2, 1)
                mixed.append(part[:samples] + jnp.where(low, -turned, turned))
            real = jnp.where(low, mixed[0], pltpu.roll(mixed[1], lanes // 2, 1))
            imag = jnp.where(low, pltpu.roll(mixed[0], lanes // 2, 1), mixed[1])
            held[q * rows : (q + 1) * rows, place : place + lanes] = jnp.concatenate(
                [real, imag], axis=0
            ).astype(BF16)
    message[...] = dot(line_back[...], held[...]).astype(BF16).reshape(message.shape)


def mix_back_kernel(per, samples, arrived, weights, line, line_back, pairs, message, held):
    rows = 2 * samples
    lanes = 2 * weights.shape[1]
    low = low_half((samples, lanes))
    flat = arrived[...].reshape(-1, arrived.shape[2])
    spectra = dot(line[...], flat).astype(BF16).astype(F32)
    for q in range(MX):
        for first in range(0, per, 2):
            block = spread_pair(weights[first * MX + q], weights[(first + 1) * MX + q])
            place = first // 2 * lanes
            real = spectra[q * rows : q * rows + samples, place : place + lanes]
            imag = spectra[q * rows + samples : (q + 1) * rows, place : place + lanes]
            real_turned = pltpu.roll(real, lanes // 2, 1)
            imag_turned = pltpu.roll(imag, lanes // 2, 1)
            left = [jnp.where(low, real, imag_turned), jnp.where(low, imag, -real_turned)]
            right = [jnp.where(low, real_turned, imag), jnp.where(low, imag_turned, -real)]
            pair = jnp.concatenate(
                [jnp.concatenate(left, axis=0), jnp.concatenate(right, axis=0)], axis=1
            ).astype(BF16)
            pairs[q * rows : (q + 1) * rows, 2 * place : 2 * (place + lanes)] = pair
            held[q * rows : (q + 1) * rows, place : place + lanes] = lax.dot_general(
                pair, block, (((1,), (1,)), ((), ())), preferred_element_type=F32
            ).astype(BF16)
    message[...] = dot(line_back[...], held[...]).astype(BF16).reshape(message.shape)


def weight_kernel(per, samples, spec_in, pairs, out):
    rows = 2 * samples
    lanes = out.shape[2]
    half = lanes // 2
    for q in range(MX):
        for first in range(0, per, 2):
            place = first // 2 * lanes
            left = spec_in[q * rows : (q + 1) * rows, place : place + lanes]
            right = pairs[q * rows : (q + 1) * rows, 2 * place : 2 * (place + lanes)]
            outer = lax.dot_general(
                left, right, (((0,), (0,)), ((), ())), preferred_element_type=F32
            )
            out[first * MX + q] = outer[:half, :lanes]
            out[(first + 1) * MX + q] = outer[half:, lanes:]


def whole(array):
    return pl.BlockSpec(array.shape, lambda *step: (0,) * len(array.shape))


def shaped(shape, dtype):
    return jax.ShapeDtypeStruct(shape, dtype)


def params(mib):
    return pltpu.CompilerParams(vmem_limit_bytes=mib * MIB)


def cost(flops, moved, steep=0):
    return pl.CostEstimate(flops=flops, bytes_accessed=moved, transcendentals=steep)


def body(mesh_axes, devices, slabs, activations, cotangent, mode_weights, pointwise, offsets):
    _, channels, width, rows_y, rows_z = activations.shape
    samples = devices // slabs
    per = MY * MZ // devices
    groups = channels // GROUP
    field = activations.shape[1:]
    count = math.prod(field)
    ztab = z_table(rows_z)
    ytab = y_table(rows_y, width)
    order = lane_order(channels, per)
    line_fwd, line_inv = x_tables(samples, slabs, NX)
    weight = np.where(np.arange(MZ) == 0, 1.0, 2.0) / (rows_y * rows_z)
    scale = np.tile(np.repeat(weight, GROUP), groups).astype(np.float32)[None]
    ztab_t, ytab_t, order_t = (np.ascontiguousarray(t.T) for t in (ztab, ytab, order))
    fwd_t, inv_t = (np.ascontiguousarray(t.T) for t in (line_fwd, line_inv))
    message = shaped((devices, 2 * width, per * channels), BF16)
    spectra = shaped((MX * 2 * samples, per * channels), BF16)
    held_plane = pltpu.VMEM((groups, MY * width * 2, MZ * GROUP), BF16)
    held_lines = pltpu.VMEM((groups, width * rows_y, 2 * MZ * GROUP), BF16)
    group_5d = pl.BlockSpec((1, GROUP, width, rows_y, rows_z), lambda g: (0, g, 0, 0, 0))
    group_4d = pl.BlockSpec((GROUP, width, rows_y, rows_z), lambda g: (g, 0, 0, 0))
    plane_flops = 2 * count * 2 * MZ * GROUP

    def exchange(array):
        return lax.all_to_all(array, mesh_axes, split_axis=0, concat_axis=0, tiled=True)

    def mix_points(values, turned, shifts):
        step = 2
        block = pl.BlockSpec((channels, step, rows_y, rows_z), lambda x: (0, x, 0, 0))
        kernel = functools.partial(pointwise_kernel, turned)
        specs = [block, whole(pointwise)]
        operands = [values, pointwise]
        if shifts is None:
            run = lambda a, b, *rest: kernel(a, b, None, *rest)
        else:
            run = kernel
            specs.append(pl.BlockSpec(memory_space=pltpu.SMEM))
            operands.append(shifts)
        return pl.pallas_call(
            run,
            grid=(width // step,),
            in_specs=specs,
            out_specs=block,
            out_shape=shaped(field, BF16),
            scratch_shapes=[
                pltpu.VMEM((channels * TILE, channels * TILE), BF16),
                pltpu.VMEM((channels, 1, rows_z), F32),
            ],
            compiler_params=params(32),
            cost_estimate=cost(2 * count * channels * TILE, 4 * count),
        )(*operands)

    planes = pl.pallas_call(
        functools.partial(plane_kernel, per, channels),
        grid=(groups,),
        in_specs=[group_5d, whole(ztab), whole(ytab), whole(order)],
        out_specs=whole(message),
        out_shape=message,
        scratch_shapes=[held_plane],
        compiler_params=params(32),
        cost_estimate=cost(plane_flops, 2 * count),
    )(activations, ztab, ytab, order)
    arrived = exchange(planes)
    local = mix_points(activations.reshape(field), True, offsets)
    spec_in, mixed = pl.pallas_call(
        functools.partial(mix_kernel, per, samples),
        out_shape=(spectra, message),
        scratch_shapes=[pltpu.VMEM(spectra.shape, BF16)],
        compiler_params=params(16),
        cost_estimate=cost(10**8, 2 * mode_weights.size),
    )(arrived, mode_weights, line_fwd, inv_t)
    returned = exchange(mixed)
    slope, back_plane = pl.pallas_call(
        functools.partial(slope_kernel, per, channels),
        grid=(groups,),
        in_specs=[whole(message), group_4d, group_5d]
        + [whole(t) for t in (order_t, ytab_t, ztab_t, scale, ztab, ytab, order)],
        out_specs=(group_4d, whole(message)),
        out_shape=(shaped(field, BF16), message),
        scratch_shapes=[held_lines, held_plane],
        compiler_params=params(40),
        cost_estimate=cost(2 * plane_flops, 6 * count, 2 * count),
    )(returned, local, cotangent, order_t, ytab_t, ztab_t, scale, ztab, ytab, order)
    arrived_back = exchange(back_plane)
    local_back = mix_points(slope, False, None)
    pairs, mixed_back = pl.pallas_call(
        functools.partial(mix_back_kernel, per, samples),
        out_shape=(shaped((spectra.shape[0], 2 * spectra.shape[1]), BF16), message),
        scratch_shapes=[pltpu.VMEM(spectra.shape, BF16)],
        compiler_params=params(16),
        cost_estimate=cost(10**8, 2 * mode_weights.size),
    )(arrived_back, mode_weights, line_inv, fwd_t)
    returned_back = exchange(mixed_back)
    grad_spectral = pl.pallas_call(
        functools.partial(weight_kernel, per, samples),
        out_shape=shaped(mode_weights.shape, F32),
        compiler_params=params(16),
        cost_estimate=cost(10**8, 4 * mode_weights.size),
    )(spec_in, pairs)
    grad_in = pl.pallas_call(
        functools.partial(field_kernel, per),
        grid=(groups,),
        in_specs=[whole(message), group_4d, whole(order_t), whole(ytab_t), whole(ztab_t)],
        out_specs=group_5d,
        out_shape=shaped(activations.shape, BF16),
        scratch_shapes=[held_lines],
        compiler_params=params(40),
        cost_estimate=cost(plane_flops, 4 * count),
    )(returned_back, local_back, order_t, ytab_t, ztab_t)
    return (grad_in, grad_spectral)


def chosen_body(mesh_axes, devices, slabs, activations, cotangent, mode_weights, pointwise, offsets):
    samples, channels, width, rows_y, rows_z = activations.shape
    per = MY * MZ // devices
    fits = (
        samples == 1
        and MY * MZ % devices == 0
        and per in (2, 4, 8)
        and width % 8 == 0
        and channels == 64
        and rows_y % TILE == 0
        and rows_z == 128
    )
    plan = functools.partial(body, mesh_axes, devices, slabs) if fits else general_body
    return plan(activations, cotangent, mode_weights, pointwise, offsets)


def solution(mesh):
    slabs = mesh.shape["space"]
    devices = slabs * mesh.shape["dp"]
    return jax.shard_map(
        functools.partial(chosen_body, ("space", "dp"), devices, slabs),
        mesh=mesh,
        in_specs=(
            P("dp", None, "space", None, None),
            P("dp", None, "space", None, None),
            P(("space", "dp"), None, None),
            P(),
            P(),
        ),
        out_specs=(P("dp", None, "space", None, None), P(("space", "dp"), None, None)),
        check_vma=False,
    )
```

```python
import functools
import math

import jax
import jax.numpy as jnp
import ml_dtypes
import numpy as np
from jax import lax
from jax.experimental import pallas as pl
from jax.experimental.pallas import tpu as pltpu
from jax.sharding import PartitionSpec as P

MX = 16
MY = 16
MZ = 8
NX = 32


def centered(count):
    index = jnp.arange(count, dtype=jnp.int32)
    return jnp.where(index < count // 2, index, index - count)


def plane_tables(rows_y, rows_z, modes_y, modes_z):
    along_y = jnp.arange(rows_y, dtype=jnp.int32)[:, None, None, None]
    along_z = jnp.arange(rows_z, dtype=jnp.int32)[None, :, None, None]
    freq_y = centered(modes_y)[None, None, :, None]
    freq_z = jnp.arange(modes_z, dtype=jnp.int32)[None, None, None, :]
    phase = jnp.mod(freq_y * along_y * rows_z + freq_z * along_z * rows_y, rows_y * rows_z)
    theta = phase.astype(jnp.float32) * (2.0 * math.pi / (rows_y * rows_z))
    cosine = jnp.cos(theta)
    sine = jnp.sin(theta)
    forward = jnp.stack([cosine, -sine], -1).reshape(rows_y * rows_z, modes_y * modes_z * 2)
    scaled = jnp.where(freq_z == 0, 1.0, 2.0).astype(jnp.float32) / (rows_y * rows_z)
    inverse = (
        jnp.stack([cosine * scaled, -sine * scaled], -1)
        .reshape(rows_y * rows_z, modes_y * modes_z * 2)
        .T
    )
    return (forward.astype(jnp.bfloat16), inverse.astype(jnp.bfloat16))


def line_tables(length, modes):
    along = jnp.arange(length, dtype=jnp.int32)[:, None]
    freq = centered(modes)[None, :]
    phase = jnp.mod(freq * along, length)
    theta = phase.astype(jnp.float32) * (2.0 * math.pi / length)
    cosine = jnp.cos(theta)
    sine = jnp.sin(theta)
    first = jnp.stack([cosine, -sine], -1)
    second = jnp.stack([sine, cosine], -1)
    forward = jnp.stack([first, second], 1).reshape(2 * length, 2 * modes)
    inv_first = jnp.stack([cosine.T, sine.T], -1) / length
    inv_second = jnp.stack([-sine.T, cosine.T], -1) / length
    inverse = jnp.stack([inv_first, inv_second], 1).reshape(2 * modes, 2 * length)
    return (forward.astype(jnp.bfloat16), inverse.astype(jnp.bfloat16))


def expand_weights(weights):
    half = weights.shape[1]
    real_part = weights[:, :, :half]
    imag_part = weights[:, :, half:]
    upper = jnp.concatenate([real_part, imag_part], axis=2)
    lower = jnp.concatenate([-imag_part, real_part], axis=2)
    return jnp.concatenate([upper, lower], axis=1)


def outer_sum(left, right):
    return jnp.einsum("mbi,mbo->mio", left, right, preferred_element_type=jnp.float32)


def weight_terms(spec_in, spec_grad):
    half = spec_in.shape[2] // 2
    in_real = spec_in[:, :, :half]
    in_imag = spec_in[:, :, half:]
    gr_real = spec_grad[:, :, :half]
    gr_imag = spec_grad[:, :, half:]
    real_term = outer_sum(in_real, gr_real) + outer_sum(in_imag, gr_imag)
    imag_term = outer_sum(in_real, gr_imag) - outer_sum(in_imag, gr_real)
    return jnp.concatenate([real_term, imag_term], axis=2)


def to_modes(slab, table, modes_x):
    samples, channels, width, pairs = slab.shape
    moved = lax.all_to_all(slab, "space", split_axis=3, concat_axis=2, tiled=True)
    length = moved.shape[2]
    local = moved.shape[3] // 2
    lines = moved.reshape(samples, channels, length, local, 2).transpose(0, 1, 3, 2, 4)
    lines = lines.reshape(samples, channels, local, 2 * length)
    spectra = jnp.dot(lines, table, preferred_element_type=jnp.float32).astype(jnp.bfloat16)
    spectra = spectra.reshape(samples, channels, local, modes_x, 2).transpose(2, 3, 0, 4, 1)
    return spectra.reshape(local * modes_x, samples, 2 * channels)


def to_slab(spectra, table, modes_x, channels):
    count, samples, doubled = spectra.shape
    local = count // modes_x
    lines = spectra.reshape(local, modes_x, samples, 2, channels).transpose(2, 4, 0, 1, 3)
    lines = lines.reshape(samples, channels, local, 2 * modes_x)
    lines = jnp.dot(lines, table, preferred_element_type=jnp.float32).astype(jnp.bfloat16)
    length = lines.shape[3] // 2
    lines = lines.reshape(samples, channels, local, length, 2).transpose(0, 1, 3, 2, 4)
    lines = lines.reshape(samples, channels, length, 2 * local)
    return lax.all_to_all(lines, "space", split_axis=2, concat_axis=3, tiled=True)


def to_owners(spectra):
    return lax.all_to_all(spectra, "dp", split_axis=0, concat_axis=1, tiled=True)


def from_owners(spectra):
    return lax.all_to_all(spectra, "dp", split_axis=1, concat_axis=0, tiled=True)


def gelu_slope(value):
    cdf = 0.5 * (1.0 + lax.erf(value * 0.7071067811865476))
    density = jnp.exp(-0.5 * value * value) * 0.3989422804014327
    return cdf + value * density


def general_body(activations, cotangent, mode_weights, pointwise, offsets):
    samples, channels, width, rows_y, rows_z = activations.shape
    plane_fwd, plane_inv = plane_tables(rows_y, rows_z, MY, MZ)
    line_fwd, line_inv = line_tables(NX, MX)
    flat = activations.reshape(samples, channels, width, rows_y * rows_z)
    planes = jnp.dot(flat, plane_fwd, preferred_element_type=jnp.float32).astype(jnp.bfloat16)
    spec_in = to_modes(planes, line_fwd, MX)
    blocks = expand_weights(mode_weights)
    held_in = to_owners(spec_in)
    held_out = jnp.einsum(
        "mbi,mio->mbo", held_in, blocks, preferred_element_type=jnp.float32
    ).astype(jnp.bfloat16)
    spec_out = from_owners(held_out)
    returned = to_slab(spec_out, line_inv, MX, channels)
    spectral = jnp.dot(returned, plane_inv, preferred_element_type=jnp.float32)
    local_part = jnp.einsum("io,bixn->boxn", pointwise, flat, preferred_element_type=jnp.float32)
    summed = spectral + local_part + offsets[None, :, None, None]
    upstream = cotangent.reshape(flat.shape).astype(jnp.float32)
    slope_grad = (upstream * gelu_slope(summed)).astype(jnp.bfloat16)
    back_plane = jnp.dot(slope_grad, plane_inv.T, preferred_element_type=jnp.float32).astype(
        jnp.bfloat16
    )
    spec_grad = to_modes(back_plane, line_inv.T, MX)
    held_grad = to_owners(spec_grad)
    held_dx = jnp.einsum(
        "mbo,mio->mbi", held_grad, blocks, preferred_element_type=jnp.float32
    ).astype(jnp.bfloat16)
    spec_dx = from_owners(held_dx)
    grad_spectral = weight_terms(held_in, held_grad)
    line_dx = to_slab(spec_dx, line_fwd.T, MX, channels)
    total = jnp.dot(line_dx, plane_fwd.T, preferred_element_type=jnp.float32)
    total = total + jnp.einsum(
        "io,boxn->bixn", pointwise, slope_grad, preferred_element_type=jnp.float32
    )
    grad_in = total.astype(jnp.bfloat16).reshape(activations.shape)
    return (grad_in, grad_spectral)


BF16 = jnp.bfloat16
F32 = jnp.float32
GROUP = 16
TILE = 16
MIB = 1024 * 1024


def rounded(table):
    return np.asarray(table, np.float32).astype(ml_dtypes.bfloat16)


def angles(freq, points, length):
    phase = np.mod(np.outer(freq, points), length)
    return (phase * (2.0 * math.pi / length)).astype(np.float64)


def signed(count):
    index = np.arange(count)
    return np.where(index < count // 2, index, index - count)


def z_table(rows_z):
    theta = angles(np.arange(MZ), np.arange(rows_z), rows_z)
    pair = np.stack([np.cos(theta), -np.sin(theta)])
    table = np.einsum("rkz,cd->czrkd", pair, np.eye(GROUP))
    return rounded(table.reshape(GROUP * rows_z, 2 * MZ * GROUP))


def y_table(rows_y, width):
    theta = angles(signed(MY), np.arange(rows_y), rows_y)
    cosine, sine = np.cos(theta), np.sin(theta)
    turn = np.stack([np.stack([cosine, sine]), np.stack([-sine, cosine])])
    table = np.einsum("rsjy,xw->jxrswy", turn, np.eye(width))
    return rounded(table.reshape(MY * width * 2, 2 * width * rows_y))


def lane_order(channels, per):
    count = MZ * channels
    source = np.arange(count).reshape(channels // GROUP, MZ // per, per, GROUP)
    target = source.transpose(1, 2, 0, 3).reshape(-1)
    table = np.zeros((count, count))
    table[target, np.arange(count)] = 1.0
    return rounded(table)


def x_tables(samples, slabs, length):
    theta = angles(signed(MX), np.arange(length), length)
    cosine, sine = np.cos(theta), np.sin(theta)
    forward = np.stack([np.stack([cosine, sine]), np.stack([-sine, cosine])])
    inverse = np.stack([np.stack([cosine, sine]), np.stack([-sine, cosine])]) / length
    same = np.eye(samples)
    rows = MX * 2 * samples

    def lay(turn):
        turn = turn.reshape(2, 2, MX, slabs, length // slabs)
        table = np.einsum("arqsx,bd->qabsdxr", turn, same)
        return rounded(table.reshape(rows, samples * length * 2))

    return lay(forward), lay(inverse)


def dot(left, right):
    return jnp.dot(left, right, preferred_element_type=F32)


def gelu_slope_rows(value):
    decay = jnp.exp2(value * value * (-0.5 * math.log2(math.e))).astype(BF16)
    value = value.astype(BF16)

    def number(x):
        return jnp.asarray(x, BF16)

    size = jnp.abs(value)
    t = pl.reciprocal(number(1.0) + number(0.3275911 * math.sqrt(0.5)) * size, approx=True)
    tail = number(0.5 * 1.061405429) * t - number(0.5 * 1.453152027)
    tail = tail * t + number(0.5 * 1.421413741)
    tail = tail * t - number(0.5 * 0.284496736)
    tail = tail * t + number(0.5 * 0.254829592)
    part = (size * number(1.0 / math.sqrt(2.0 * math.pi)) - tail * t) * decay
    return jnp.where(value >= number(0.0), number(1.0) + part, -part)


def analyse(field, ztab, ytab):
    spectra = dot(jnp.concatenate(field, axis=1), ztab).astype(BF16)
    half = spectra.shape[1] // 2
    return dot(ytab, jnp.concatenate([spectra[:, :half], spectra[:, half:]], axis=0))


def deliver(held, order, message, per, channels):
    ordered = dot(held, order).astype(BF16)
    parts = MZ // per
    rows = message.shape[1]
    lanes = per * channels
    for part in range(parts):
        block = ordered[:, part * lanes : (part + 1) * lanes]
        for j in range(MY):
            message[j * parts + part] = block[j * rows : (j + 1) * rows]


def receive(message, order_back, ytab_back, scale, held, per):
    parts = MZ // per
    blocks = message[...]
    blocks = blocks.reshape(MY, parts, *blocks.shape[1:])
    lanes = [blocks[:, part].reshape(-1, blocks.shape[3]) for part in range(parts)]
    ordered = dot(jnp.concatenate(lanes, axis=1), order_back[...]).astype(BF16)
    lines = dot(ytab_back[...], ordered)
    if scale is not None:
        lines = lines * scale[...]
    lines = lines.astype(BF16)
    rows = lines.shape[0] // 2
    wide = MZ * GROUP
    for group in range(held.shape[0]):
        piece = lines[:, group * wide : (group + 1) * wide]
        held[group] = jnp.concatenate([piece[:rows], piece[rows:]], axis=1)


def plane_kernel(per, channels, field, ztab, ytab, order, message, held):
    step = pl.program_id(0)
    rows_z = field.shape[-1]
    blocks = [field[0, c].reshape(-1, rows_z) for c in range(GROUP)]
    held[step] = analyse(blocks, ztab[...], ytab[...]).astype(BF16)

    @pl.when(step == pl.num_programs(0) - 1)
    def _():
        whole = jnp.concatenate([held[g] for g in range(held.shape[0])], axis=1)
        deliver(whole, order[...], message, per, channels)


def slope_kernel(
    per, channels, arrived, local, cotangent, order_back, ytab_back, ztab_back, scale, ztab, ytab, order,
    slope, message, held, back,
):
    step = pl.program_id(0)
    width, rows_y, rows_z = local.shape[1:]

    @pl.when(step == 0)
    def _():
        receive(arrived, order_back, ytab_back, scale, held, per)

    lines = held[step]
    blocks = []
    for first in range(0, GROUP, 2):
        field = dot(lines, ztab_back[:, first * rows_z : (first + 2) * rows_z])
        for offset in range(2):
            c = first + offset
            value = field[:, offset * rows_z : (offset + 1) * rows_z]
            value = value + local[c].reshape(-1, rows_z).astype(F32)
            upstream = cotangent[0, c].reshape(-1, rows_z)
            result = upstream * gelu_slope_rows(value)
            slope[c] = result.reshape(width, rows_y, rows_z)
            blocks.append(result)
    plane = analyse(blocks, ztab[...], ytab[...]) * scale[:, : MZ * GROUP]
    back[step] = plane.astype(BF16)

    @pl.when(step == pl.num_programs(0) - 1)
    def _():
        whole = jnp.concatenate([back[g] for g in range(back.shape[0])], axis=1)
        deliver(whole, order[...], message, per, channels)


def field_kernel(per, arrived, local, order_back, ytab_back, ztab_back, out, held):
    step = pl.program_id(0)
    width, rows_y, rows_z = local.shape[1:]

    @pl.when(step == 0)
    def _():
        receive(arrived, order_back, ytab_back, None, held, per)

    lines = held[step]
    for first in range(0, GROUP, 2):
        field = dot(lines, ztab_back[:, first * rows_z : (first + 2) * rows_z])
        for offset in range(2):
            c = first + offset
            value = field[:, offset * rows_z : (offset + 1) * rows_z]
            value = value + local[c].reshape(-1, rows_z).astype(F32)
            out[0, c] = value.astype(BF16).reshape(width, rows_y, rows_z)


def pointwise_kernel(turned, field, mix, offsets, out, table, shift):
    channels = mix.shape[0]
    width, rows_y, rows_z = field.shape[1:]
    size = channels * TILE

    @pl.when(pl.program_id(0) == 0)
    def _():
        row = lax.broadcasted_iota(jnp.int32, (size, channels), 0) // TILE
        column = lax.broadcasted_iota(jnp.int32, (size, channels), 1)
        spread = jnp.where(row == column, 1.0, 0.0).astype(BF16)
        tall = lax.dot_general(
            spread, mix[...], (((1,), (1 if turned else 0,)), ((), ())), preferred_element_type=F32
        ).astype(BF16)
        whole = lax.dot_general(
            tall, spread, (((1,), (1,)), ((), ())), preferred_element_type=F32
        )
        place = lax.broadcasted_iota(jnp.int32, (size, size), 0) % TILE
        other = lax.broadcasted_iota(jnp.int32, (size, size), 1) % TILE
        table[...] = jnp.where(place == other, whole, 0.0).astype(BF16)
        if offsets is not None:
            for c in range(channels):
                shift[c] = jnp.full((1, rows_z), offsets[c], F32)

    for start in range(0, rows_y, TILE):
        rows = [field[:, x, start : start + TILE, :].reshape(size, rows_z) for x in range(width)]
        mixed = dot(table[...], jnp.concatenate(rows, axis=1))
        for x in range(width):
            value = mixed[:, x * rows_z : (x + 1) * rows_z].reshape(channels, TILE, rows_z)
            if offsets is not None:
                value = value + shift[...]
            out[:, x, start : start + TILE, :] = value.astype(BF16)


def spread_pair(first, second):
    nothing = jnp.zeros_like(first)
    upper = jnp.concatenate([first, nothing], axis=1)
    lower = jnp.concatenate([nothing, second], axis=1)
    return jnp.concatenate([upper, lower], axis=0)


def low_half(shape):
    return lax.broadcasted_iota(jnp.int32, shape, 1) < shape[1] // 2


def mix_kernel(per, samples, arrived, weights, line, line_back, spec_in, message, held):
    rows = 2 * samples
    lanes = 2 * weights.shape[1]
    low = low_half((samples, lanes))
    flat = arrived[...].reshape(-1, arrived.shape[2])
    spectra = dot(line[...], flat).astype(BF16)
    spec_in[...] = spectra
    for q in range(MX):
        for first in range(0, per, 2):
            block = spread_pair(weights[first * MX + q], weights[(first + 1) * MX + q])
            place = first // 2 * lanes
            terms = dot(spectra[q * rows : (q + 1) * rows, place : place + lanes], block)
            mixed = []
            for side in range(2):
                part = terms[:, side * lanes : (side + 1) * lanes]
                turned = pltpu.roll(part[samples:], lanes // 2, 1)
                mixed.append(part[:samples] + jnp.where(low, -turned, turned))
            real = jnp.where(low, mixed[0], pltpu.roll(mixed[1], lanes // 2, 1))
            imag = jnp.where(low, pltpu.roll(mixed[0], lanes // 2, 1), mixed[1])
            held[q * rows : (q + 1) * rows, place : place + lanes] = jnp.concatenate(
                [real, imag], axis=0
            ).astype(BF16)
    message[...] = dot(line_back[...], held[...]).astype(BF16).reshape(message.shape)


def mix_back_kernel(per, samples, arrived, weights, line, line_back, pairs, message, held):
    rows = 2 * samples
    lanes = 2 * weights.shape[1]
    low = low_half((samples, lanes))
    flat = arrived[...].reshape(-1, arrived.shape[2])
    spectra = dot(line[...], flat).astype(BF16).astype(F32)
    for q in range(MX):
        for first in range(0, per, 2):
            block = spread_pair(weights[first * MX + q], weights[(first + 1) * MX + q])
            place = first // 2 * lanes
            real = spectra[q * rows : q * rows + samples, place : place + lanes]
            imag = spectra[q * rows + samples : (q + 1) * rows, place : place + lanes]
            real_turned = pltpu.roll(real, lanes // 2, 1)
            imag_turned = pltpu.roll(imag, lanes // 2, 1)
            left = [jnp.where(low, real, imag_turned), jnp.where(low, imag, -real_turned)]
            right = [jnp.where(low, real_turned, imag), jnp.where(low, imag_turned, -real)]
            pair = jnp.concatenate(
                [jnp.concatenate(left, axis=0), jnp.concatenate(right, axis=0)], axis=1
            ).astype(BF16)
            pairs[q * rows : (q + 1) * rows, 2 * place : 2 * (place + lanes)] = pair
            held[q * rows : (q + 1) * rows, place : place + lanes] = lax.dot_general(
                pair, block, (((1,), (1,)), ((), ())), preferred_element_type=F32
            ).astype(BF16)
    message[...] = dot(line_back[...], held[...]).astype(BF16).reshape(message.shape)


def weight_kernel(per, samples, spec_in, pairs, out):
    rows = 2 * samples
    lanes = out.shape[2]
    half = lanes // 2
    for q in range(MX):
        for first in range(0, per, 2):
            place = first // 2 * lanes
            left = spec_in[q * rows : (q + 1) * rows, place : place + lanes]
            right = pairs[q * rows : (q + 1) * rows, 2 * place : 2 * (place + lanes)]
            outer = lax.dot_general(
                left, right, (((0,), (0,)), ((), ())), preferred_element_type=F32
            )
            out[first * MX + q] = outer[:half, :lanes]
            out[(first + 1) * MX + q] = outer[half:, lanes:]


def whole(array):
    return pl.BlockSpec(array.shape, lambda *step: (0,) * len(array.shape))


def shaped(shape, dtype):
    return jax.ShapeDtypeStruct(shape, dtype)


def params(mib):
    return pltpu.CompilerParams(vmem_limit_bytes=mib * MIB)


def cost(flops, moved, steep=0):
    return pl.CostEstimate(flops=flops, bytes_accessed=moved, transcendentals=steep)


def body(mesh_axes, devices, slabs, activations, cotangent, mode_weights, pointwise, offsets):
    _, channels, width, rows_y, rows_z = activations.shape
    samples = devices // slabs
    per = MY * MZ // devices
    groups = channels // GROUP
    field = activations.shape[1:]
    count = math.prod(field)
    ztab = z_table(rows_z)
    ytab = y_table(rows_y, width)
    order = lane_order(channels, per)
    line_fwd, line_inv = x_tables(samples, slabs, NX)
    weight = np.where(np.arange(MZ) == 0, 1.0, 2.0) / (rows_y * rows_z)
    scale = np.tile(np.repeat(weight, GROUP), groups).astype(np.float32)[None]
    ztab_t, ytab_t, order_t = (np.ascontiguousarray(t.T) for t in (ztab, ytab, order))
    fwd_t, inv_t = (np.ascontiguousarray(t.T) for t in (line_fwd, line_inv))
    message = shaped((devices, 2 * width, per * channels), BF16)
    spectra = shaped((MX * 2 * samples, per * channels), BF16)
    held_plane = pltpu.VMEM((groups, MY * width * 2, MZ * GROUP), BF16)
    held_lines = pltpu.VMEM((groups, width * rows_y, 2 * MZ * GROUP), BF16)
    group_5d = pl.BlockSpec((1, GROUP, width, rows_y, rows_z), lambda g: (0, g, 0, 0, 0))
    group_4d = pl.BlockSpec((GROUP, width, rows_y, rows_z), lambda g: (g, 0, 0, 0))
    plane_flops = 2 * count * 2 * MZ * GROUP

    def exchange(array):
        return lax.all_to_all(array, mesh_axes, split_axis=0, concat_axis=0, tiled=True)

    def mix_points(values, turned, shifts):
        step = 2
        block = pl.BlockSpec((channels, step, rows_y, rows_z), lambda x: (0, x, 0, 0))
        kernel = functools.partial(pointwise_kernel, turned)
        specs = [block, whole(pointwise)]
        operands = [values, pointwise]
        if shifts is None:
            run = lambda a, b, *rest: kernel(a, b, None, *rest)
        else:
            run = kernel
            specs.append(pl.BlockSpec(memory_space=pltpu.SMEM))
            operands.append(shifts)
        return pl.pallas_call(
            run,
            grid=(width // step,),
            in_specs=specs,
            out_specs=block,
            out_shape=shaped(field, BF16),
            scratch_shapes=[
                pltpu.VMEM((channels * TILE, channels * TILE), BF16),
                pltpu.VMEM((channels, 1, rows_z), F32),
            ],
            compiler_params=params(60),
            cost_estimate=cost(2 * count * channels * TILE, 4 * count),
        )(*operands)

    planes = pl.pallas_call(
        functools.partial(plane_kernel, per, channels),
        grid=(groups,),
        in_specs=[group_5d, whole(ztab), whole(ytab), whole(order)],
        out_specs=whole(message),
        out_shape=message,
        scratch_shapes=[held_plane],
        compiler_params=params(60),
        cost_estimate=cost(plane_flops, 2 * count),
    )(activations, ztab, ytab, order)
    arrived = exchange(planes)
    local = mix_points(activations.reshape(field), True, offsets)
    spec_in, mixed = pl.pallas_call(
        functools.partial(mix_kernel, per, samples),
        out_shape=(spectra, message),
        scratch_shapes=[pltpu.VMEM(spectra.shape, BF16)],
        compiler_params=params(60),
        cost_estimate=cost(10**8, 2 * mode_weights.size),
    )(arrived, mode_weights, line_fwd, inv_t)
    returned = exchange(mixed)
    slope, back_plane = pl.pallas_call(
        functools.partial(slope_kernel, per, channels),
        grid=(groups,),
        in_specs=[whole(message), group_4d, group_5d]
        + [whole(t) for t in (order_t, ytab_t, ztab_t, scale, ztab, ytab, order)],
        out_specs=(group_4d, whole(message)),
        out_shape=(shaped(field, BF16), message),
        scratch_shapes=[held_lines, held_plane],
        compiler_params=params(60),
        cost_estimate=cost(2 * plane_flops, 6 * count, 2 * count),
    )(returned, local, cotangent, order_t, ytab_t, ztab_t, scale, ztab, ytab, order)
    arrived_back = exchange(back_plane)
    local_back = mix_points(slope, False, None)
    pairs, mixed_back = pl.pallas_call(
        functools.partial(mix_back_kernel, per, samples),
        out_shape=(shaped((spectra.shape[0], 2 * spectra.shape[1]), BF16), message),
        scratch_shapes=[pltpu.VMEM(spectra.shape, BF16)],
        compiler_params=params(60),
        cost_estimate=cost(10**8, 2 * mode_weights.size),
    )(arrived_back, mode_weights, line_inv, fwd_t)
    returned_back = exchange(mixed_back)
    grad_spectral = pl.pallas_call(
        functools.partial(weight_kernel, per, samples),
        out_shape=shaped(mode_weights.shape, F32),
        compiler_params=params(60),
        cost_estimate=cost(10**8, 4 * mode_weights.size),
    )(spec_in, pairs)
    grad_in = pl.pallas_call(
        functools.partial(field_kernel, per),
        grid=(groups,),
        in_specs=[whole(message), group_4d, whole(order_t), whole(ytab_t), whole(ztab_t)],
        out_specs=group_5d,
        out_shape=shaped(activations.shape, BF16),
        scratch_shapes=[held_lines],
        compiler_params=params(60),
        cost_estimate=cost(plane_flops, 4 * count),
    )(returned_back, local_back, order_t, ytab_t, ztab_t)
    return (grad_in, grad_spectral)


def chosen_body(mesh_axes, devices, slabs, activations, cotangent, mode_weights, pointwise, offsets):
    samples, channels, width, rows_y, rows_z = activations.shape
    per = MY * MZ // devices
    fits = (
        samples == 1
        and MY * MZ % devices == 0
        and per in (2, 4, 8)
        and width % 8 == 0
        and channels == 64
        and rows_y % TILE == 0
        and rows_z == 128
    )
    plan = functools.partial(body, mesh_axes, devices, slabs) if fits else general_body
    return plan(activations, cotangent, mode_weights, pointwise, offsets)


def solution(mesh):
    slabs = mesh.shape["space"]
    devices = slabs * mesh.shape["dp"]
    return jax.shard_map(
        functools.partial(chosen_body, ("space", "dp"), devices, slabs),
        mesh=mesh,
        in_specs=(
            P("dp", None, "space", None, None),
            P("dp", None, "space", None, None),
            P(("space", "dp"), None, None),
            P(),
            P(),
        ),
        out_specs=(P("dp", None, "space", None, None), P(("space", "dp"), None, None)),
        check_vma=False,
    )
```

```python
import functools
import math

import jax
import jax.numpy as jnp
import ml_dtypes
import numpy as np
from jax import lax
from jax.experimental import pallas as pl
from jax.experimental.pallas import tpu as pltpu
from jax.sharding import PartitionSpec as P

MX = 16
MY = 16
MZ = 8
NX = 32


def centered(count):
    index = jnp.arange(count, dtype=jnp.int32)
    return jnp.where(index < count // 2, index, index - count)


def plane_tables(rows_y, rows_z, modes_y, modes_z):
    along_y = jnp.arange(rows_y, dtype=jnp.int32)[:, None, None, None]
    along_z = jnp.arange(rows_z, dtype=jnp.int32)[None, :, None, None]
    freq_y = centered(modes_y)[None, None, :, None]
    freq_z = jnp.arange(modes_z, dtype=jnp.int32)[None, None, None, :]
    phase = jnp.mod(freq_y * along_y * rows_z + freq_z * along_z * rows_y, rows_y * rows_z)
    theta = phase.astype(jnp.float32) * (2.0 * math.pi / (rows_y * rows_z))
    cosine = jnp.cos(theta)
    sine = jnp.sin(theta)
    forward = jnp.stack([cosine, -sine], -1).reshape(rows_y * rows_z, modes_y * modes_z * 2)
    scaled = jnp.where(freq_z == 0, 1.0, 2.0).astype(jnp.float32) / (rows_y * rows_z)
    inverse = (
        jnp.stack([cosine * scaled, -sine * scaled], -1)
        .reshape(rows_y * rows_z, modes_y * modes_z * 2)
        .T
    )
    return (forward.astype(jnp.bfloat16), inverse.astype(jnp.bfloat16))


def line_tables(length, modes):
    along = jnp.arange(length, dtype=jnp.int32)[:, None]
    freq = centered(modes)[None, :]
    phase = jnp.mod(freq * along, length)
    theta = phase.astype(jnp.float32) * (2.0 * math.pi / length)
    cosine = jnp.cos(theta)
    sine = jnp.sin(theta)
    first = jnp.stack([cosine, -sine], -1)
    second = jnp.stack([sine, cosine], -1)
    forward = jnp.stack([first, second], 1).reshape(2 * length, 2 * modes)
    inv_first = jnp.stack([cosine.T, sine.T], -1) / length
    inv_second = jnp.stack([-sine.T, cosine.T], -1) / length
    inverse = jnp.stack([inv_first, inv_second], 1).reshape(2 * modes, 2 * length)
    return (forward.astype(jnp.bfloat16), inverse.astype(jnp.bfloat16))


def expand_weights(weights):
    half = weights.shape[1]
    real_part = weights[:, :, :half]
    imag_part = weights[:, :, half:]
    upper = jnp.concatenate([real_part, imag_part], axis=2)
    lower = jnp.concatenate([-imag_part, real_part], axis=2)
    return jnp.concatenate([upper, lower], axis=1)


def outer_sum(left, right):
    return jnp.einsum("mbi,mbo->mio", left, right, preferred_element_type=jnp.float32)


def weight_terms(spec_in, spec_grad):
    half = spec_in.shape[2] // 2
    in_real = spec_in[:, :, :half]
    in_imag = spec_in[:, :, half:]
    gr_real = spec_grad[:, :, :half]
    gr_imag = spec_grad[:, :, half:]
    real_term = outer_sum(in_real, gr_real) + outer_sum(in_imag, gr_imag)
    imag_term = outer_sum(in_real, gr_imag) - outer_sum(in_imag, gr_real)
    return jnp.concatenate([real_term, imag_term], axis=2)


def to_modes(slab, table, modes_x):
    samples, channels, width, pairs = slab.shape
    moved = lax.all_to_all(slab, "space", split_axis=3, concat_axis=2, tiled=True)
    length = moved.shape[2]
    local = moved.shape[3] // 2
    lines = moved.reshape(samples, channels, length, local, 2).transpose(0, 1, 3, 2, 4)
    lines = lines.reshape(samples, channels, local, 2 * length)
    spectra = jnp.dot(lines, table, preferred_element_type=jnp.float32).astype(jnp.bfloat16)
    spectra = spectra.reshape(samples, channels, local, modes_x, 2).transpose(2, 3, 0, 4, 1)
    return spectra.reshape(local * modes_x, samples, 2 * channels)


def to_slab(spectra, table, modes_x, channels):
    count, samples, doubled = spectra.shape
    local = count // modes_x
    lines = spectra.reshape(local, modes_x, samples, 2, channels).transpose(2, 4, 0, 1, 3)
    lines = lines.reshape(samples, channels, local, 2 * modes_x)
    lines = jnp.dot(lines, table, preferred_element_type=jnp.float32).astype(jnp.bfloat16)
    length = lines.shape[3] // 2
    lines = lines.reshape(samples, channels, local, length, 2).transpose(0, 1, 3, 2, 4)
    lines = lines.reshape(samples, channels, length, 2 * local)
    return lax.all_to_all(lines, "space", split_axis=2, concat_axis=3, tiled=True)


def to_owners(spectra):
    return lax.all_to_all(spectra, "dp", split_axis=0, concat_axis=1, tiled=True)


def from_owners(spectra):
    return lax.all_to_all(spectra, "dp", split_axis=1, concat_axis=0, tiled=True)


def gelu_slope(value):
    cdf = 0.5 * (1.0 + lax.erf(value * 0.7071067811865476))
    density = jnp.exp(-0.5 * value * value) * 0.3989422804014327
    return cdf + value * density


def general_body(activations, cotangent, mode_weights, pointwise, offsets):
    samples, channels, width, rows_y, rows_z = activations.shape
    plane_fwd, plane_inv = plane_tables(rows_y, rows_z, MY, MZ)
    line_fwd, line_inv = line_tables(NX, MX)
    flat = activations.reshape(samples, channels, width, rows_y * rows_z)
    planes = jnp.dot(flat, plane_fwd, preferred_element_type=jnp.float32).astype(jnp.bfloat16)
    spec_in = to_modes(planes, line_fwd, MX)
    blocks = expand_weights(mode_weights)
    held_in = to_owners(spec_in)
    held_out = jnp.einsum(
        "mbi,mio->mbo", held_in, blocks, preferred_element_type=jnp.float32
    ).astype(jnp.bfloat16)
    spec_out = from_owners(held_out)
    returned = to_slab(spec_out, line_inv, MX, channels)
    spectral = jnp.dot(returned, plane_inv, preferred_element_type=jnp.float32)
    local_part = jnp.einsum("io,bixn->boxn", pointwise, flat, preferred_element_type=jnp.float32)
    summed = spectral + local_part + offsets[None, :, None, None]
    upstream = cotangent.reshape(flat.shape).astype(jnp.float32)
    slope_grad = (upstream * gelu_slope(summed)).astype(jnp.bfloat16)
    back_plane = jnp.dot(slope_grad, plane_inv.T, preferred_element_type=jnp.float32).astype(
        jnp.bfloat16
    )
    spec_grad = to_modes(back_plane, line_inv.T, MX)
    held_grad = to_owners(spec_grad)
    held_dx = jnp.einsum(
        "mbo,mio->mbi", held_grad, blocks, preferred_element_type=jnp.float32
    ).astype(jnp.bfloat16)
    spec_dx = from_owners(held_dx)
    grad_spectral = weight_terms(held_in, held_grad)
    line_dx = to_slab(spec_dx, line_fwd.T, MX, channels)
    total = jnp.dot(line_dx, plane_fwd.T, preferred_element_type=jnp.float32)
    total = total + jnp.einsum(
        "io,boxn->bixn", pointwise, slope_grad, preferred_element_type=jnp.float32
    )
    grad_in = total.astype(jnp.bfloat16).reshape(activations.shape)
    return (grad_in, grad_spectral)


BF16 = jnp.bfloat16
F32 = jnp.float32
GROUP = 16
TILE = 8
MIB = 1024 * 1024


def rounded(table):
    return np.asarray(table, np.float32).astype(ml_dtypes.bfloat16)


def angles(freq, points, length):
    phase = np.mod(np.outer(freq, points), length)
    return (phase * (2.0 * math.pi / length)).astype(np.float64)


def signed(count):
    index = np.arange(count)
    return np.where(index < count // 2, index, index - count)


def z_base(rows_z):
    theta = angles(np.arange(MZ), np.arange(rows_z), rows_z)
    pair = np.stack([np.cos(theta), -np.sin(theta)])
    table = np.repeat(pair.reshape(2 * MZ, rows_z), GROUP, axis=0).T
    return rounded(table).astype(np.float32)


def y_table(rows_y, width):
    theta = angles(signed(MY), np.arange(rows_y), rows_y)
    cosine, sine = np.cos(theta), np.sin(theta)
    turn = np.stack([np.stack([cosine, sine]), np.stack([-sine, cosine])])
    table = np.einsum("rsjy,xw->jxrswy", turn, np.eye(width))
    return rounded(table.reshape(MY * width * 2, 2 * width * rows_y))


def x_tables(samples, slabs, length):
    theta = angles(signed(MX), np.arange(length), length)
    cosine, sine = np.cos(theta), np.sin(theta)
    forward = np.stack([np.stack([cosine, sine]), np.stack([-sine, cosine])])
    inverse = np.stack([np.stack([cosine, sine]), np.stack([-sine, cosine])]) / length
    same = np.eye(samples)
    rows = MX * 2 * samples

    def lay(turn):
        turn = turn.reshape(2, 2, MX, slabs, length // slabs)
        table = np.einsum("arqsx,bd->qabsdxr", turn, same)
        return rounded(table.reshape(rows, samples * length * 2))

    return lay(forward), lay(inverse)


def dot(left, right):
    return jnp.dot(left, right, preferred_element_type=F32)


def gelu_slope_rows(value):
    decay = jnp.exp2(value * value * (-0.5 * math.log2(math.e))).astype(BF16)
    value = value.astype(BF16)

    def number(x):
        return jnp.asarray(x, BF16)

    size = jnp.abs(value)
    t = pl.reciprocal(number(1.0) + number(0.3275911 * math.sqrt(0.5)) * size, approx=True)
    tail = number(0.5 * 1.061405429) * t - number(0.5 * 1.453152027)
    tail = tail * t + number(0.5 * 1.421413741)
    tail = tail * t - number(0.5 * 0.284496736)
    tail = tail * t + number(0.5 * 0.254829592)
    part = (size * number(1.0 / math.sqrt(2.0 * math.pi)) - tail * t) * decay
    return jnp.where(value >= number(0.0), number(1.0) + part, -part)


def fill_z(base, table):
    rows_z, lanes = base.shape
    owner = lax.broadcasted_iota(jnp.int32, (rows_z, lanes), 1) % GROUP
    values = base[...]
    for c in range(GROUP):
        table[c * rows_z : (c + 1) * rows_z] = jnp.where(owner == c, values, 0.0).astype(BF16)


def fill_z_back(base, table):
    lanes, rows_z = base.shape
    owner = lax.broadcasted_iota(jnp.int32, (lanes, rows_z), 0) % GROUP
    values = base[...]
    for c in range(GROUP):
        table[:, c * rows_z : (c + 1) * rows_z] = jnp.where(owner == c, values, 0.0).astype(BF16)


def grouped(lane, per, channels):
    c = lane % channels
    return c // GROUP * (MZ * GROUP) + lane // channels * GROUP + c % GROUP


def fill_order(per, channels, back, table):
    count = table.shape[0]
    row = lax.broadcasted_iota(jnp.int32, (count, count), 0)
    column = lax.broadcasted_iota(jnp.int32, (count, count), 1)
    if back:
        same = grouped(row[:, :1], per, channels) == column
    else:
        same = row == grouped(column[:1], per, channels)
    table[...] = jnp.where(same, 1.0, 0.0).astype(BF16)


def analyse(field, ztab, ytab):
    spectra = dot(jnp.concatenate(field, axis=1), ztab).astype(BF16)
    half = spectra.shape[1] // 2
    return dot(ytab, jnp.concatenate([spectra[:, :half], spectra[:, half:]], axis=0))


def deliver(held, order, message, per, channels):
    joined = jnp.concatenate([held[g] for g in range(held.shape[0])], axis=1)
    ordered = dot(joined, order[...]).astype(BF16)
    parts = MZ // per
    rows = message.shape[1]
    lanes = per * channels
    for part in range(parts):
        block = ordered[:, part * lanes : (part + 1) * lanes]
        for j in range(MY):
            message[j * parts + part] = block[j * rows : (j + 1) * rows]


def receive(message, order_back, ytab_back, scale, held, per):
    parts = MZ // per
    blocks = message[...]
    blocks = blocks.reshape(MY, parts, *blocks.shape[1:])
    lanes = [blocks[:, part].reshape(-1, blocks.shape[3]) for part in range(parts)]
    ordered = dot(jnp.concatenate(lanes, axis=1), order_back[...]).astype(BF16)
    lines = dot(ytab_back[...], ordered)
    if scale is not None:
        lines = lines * scale[...]
    lines = lines.astype(BF16)
    rows = lines.shape[0] // 2
    wide = MZ * GROUP
    for group in range(held.shape[0]):
        piece = lines[:, group * wide : (group + 1) * wide]
        held[group] = jnp.concatenate([piece[:rows], piece[rows:]], axis=1)


def plane_kernel(per, channels, field, base, ytab, message, ztab, order, held):
    step = pl.program_id(0)
    rows_z = field.shape[-1]

    @pl.when(step == 0)
    def _():
        fill_z(base, ztab)
        fill_order(per, channels, False, order)

    blocks = [field[0, c].reshape(-1, rows_z) for c in range(GROUP)]
    held[step] = analyse(blocks, ztab[...], ytab[...]).astype(BF16)

    @pl.when(step == pl.num_programs(0) - 1)
    def _():
        deliver(held, order, message, per, channels)


def slope_kernel(
    per, channels, arrived, local, cotangent, base, base_back, ytab, ytab_back, scale,
    slope, message, ztab, ztab_back, order, held, back,
):
    step = pl.program_id(0)
    width, rows_y, rows_z = local.shape[1:]

    @pl.when(step == 0)
    def _():
        fill_order(per, channels, True, order)
        receive(arrived, order, ytab_back, scale, held, per)
        fill_z(base, ztab)
        fill_z_back(base_back, ztab_back)
        fill_order(per, channels, False, order)

    lines = held[step]
    blocks = []
    for first in range(0, GROUP, 2):
        field = dot(lines, ztab_back[:, first * rows_z : (first + 2) * rows_z])
        for offset in range(2):
            c = first + offset
            value = field[:, offset * rows_z : (offset + 1) * rows_z]
            value = value + local[c].reshape(-1, rows_z).astype(F32)
            upstream = cotangent[0, c].reshape(-1, rows_z)
            result = upstream * gelu_slope_rows(value)
            slope[c] = result.reshape(width, rows_y, rows_z)
            blocks.append(result)
    plane = analyse(blocks, ztab[...], ytab[...]) * scale[:, : MZ * GROUP]
    back[step] = plane.astype(BF16)

    @pl.when(step == pl.num_programs(0) - 1)
    def _():
        deliver(back, order, message, per, channels)


def field_kernel(per, channels, arrived, local, base_back, ytab_back, out, ztab_back, order, held):
    step = pl.program_id(0)
    width, rows_y, rows_z = local.shape[1:]

    @pl.when(step == 0)
    def _():
        fill_order(per, channels, True, order)
        receive(arrived, order, ytab_back, None, held, per)
        fill_z_back(base_back, ztab_back)

    lines = held[step]
    for first in range(0, GROUP, 2):
        field = dot(lines, ztab_back[:, first * rows_z : (first + 2) * rows_z])
        for offset in range(2):
            c = first + offset
            value = field[:, offset * rows_z : (offset + 1) * rows_z]
            value = value + local[c].reshape(-1, rows_z).astype(F32)
            out[0, c] = value.astype(BF16).reshape(width, rows_y, rows_z)


def pointwise_kernel(turned, field, mix, offsets, out, table, shift):
    channels = mix.shape[0]
    width, rows_y, rows_z = field.shape[1:]
    size = channels * TILE

    @pl.when(pl.program_id(0) == 0)
    def _():
        row = lax.broadcasted_iota(jnp.int32, (size, channels), 0) // TILE
        column = lax.broadcasted_iota(jnp.int32, (size, channels), 1)
        spread = jnp.where(row == column, 1.0, 0.0).astype(BF16)
        tall = lax.dot_general(
            spread, mix[...], (((1,), (1 if turned else 0,)), ((), ())), preferred_element_type=F32
        ).astype(BF16)
        whole = lax.dot_general(
            tall, spread, (((1,), (1,)), ((), ())), preferred_element_type=F32
        )
        place = lax.broadcasted_iota(jnp.int32, (size, size), 0) % TILE
        other = lax.broadcasted_iota(jnp.int32, (size, size), 1) % TILE
        table[...] = jnp.where(place == other, whole, 0.0).astype(BF16)
        if offsets is not None:
            for c in range(channels):
                shift[c] = jnp.full((1, rows_z), offsets[c], F32)

    for start in range(0, rows_y, 2 * TILE):
        pieces = [field[:, x, start : start + 2 * TILE, :].astype(F32) for x in range(width)]
        halves = []
        for row in range(0, 2 * TILE, TILE):
            rows = [piece[:, row : row + TILE].reshape(size, rows_z).astype(BF16) for piece in pieces]
            halves.append(dot(table[...], jnp.concatenate(rows, axis=1)))
        for x in range(width):
            values = [
                half[:, x * rows_z : (x + 1) * rows_z].reshape(channels, TILE, rows_z) for half in halves
            ]
            value = jnp.concatenate(values, axis=1)
            if offsets is not None:
                value = value + shift[...]
            out[:, x, start : start + 2 * TILE, :] = value.astype(BF16)


def spread_pair(first, second):
    nothing = jnp.zeros_like(first)
    upper = jnp.concatenate([first, nothing], axis=1)
    lower = jnp.concatenate([nothing, second], axis=1)
    return jnp.concatenate([upper, lower], axis=0)


def low_half(shape):
    return lax.broadcasted_iota(jnp.int32, shape, 1) < shape[1] // 2


def mix_kernel(per, samples, arrived, weights, line, line_back, spec_in, message, held):
    rows = 2 * samples
    lanes = 2 * weights.shape[1]
    low = low_half((samples, lanes))
    flat = arrived[...].reshape(-1, arrived.shape[2])
    spectra = dot(line[...], flat).astype(BF16)
    spec_in[...] = spectra
    for q in range(MX):
        for first in range(0, per, 2):
            block = spread_pair(weights[first * MX + q], weights[(first + 1) * MX + q])
            place = first // 2 * lanes
            terms = dot(spectra[q * rows : (q + 1) * rows, place : place + lanes], block)
            mixed = []
            for side in range(2):
                part = terms[:, side * lanes : (side + 1) * lanes]
                turned = pltpu.roll(part[samples:], lanes // 2, 1)
                mixed.append(part[:samples] + jnp.where(low, -turned, turned))
            real = jnp.where(low, mixed[0], pltpu.roll(mixed[1], lanes // 2, 1))
            imag = jnp.where(low, pltpu.roll(mixed[0], lanes // 2, 1), mixed[1])
            held[q * rows : (q + 1) * rows, place : place + lanes] = jnp.concatenate(
                [real, imag], axis=0
            ).astype(BF16)
    message[...] = dot(line_back[...], held[...]).astype(BF16).reshape(message.shape)


def mix_back_kernel(per, samples, arrived, weights, line, line_back, pairs, message, held):
    rows = 2 * samples
    lanes = 2 * weights.shape[1]
    low = low_half((samples, lanes))
    flat = arrived[...].reshape(-1, arrived.shape[2])
    spectra = dot(line[...], flat).astype(BF16).astype(F32)
    for q in range(MX):
        for first in range(0, per, 2):
            block = spread_pair(weights[first * MX + q], weights[(first + 1) * MX + q])
            place = first // 2 * lanes
            real = spectra[q * rows : q * rows + samples, place : place + lanes]
            imag = spectra[q * rows + samples : (q + 1) * rows, place : place + lanes]
            real_turned = pltpu.roll(real, lanes // 2, 1)
            imag_turned = pltpu.roll(imag, lanes // 2, 1)
            left = [jnp.where(low, real, imag_turned), jnp.where(low, imag, -real_turned)]
            right = [jnp.where(low, real_turned, imag), jnp.where(low, imag_turned, -real)]
            pair = jnp.concatenate(
                [jnp.concatenate(left, axis=0), jnp.concatenate(right, axis=0)], axis=1
            ).astype(BF16)
            pairs[q * rows : (q + 1) * rows, 2 * place : 2 * (place + lanes)] = pair
            held[q * rows : (q + 1) * rows, place : place + lanes] = lax.dot_general(
                pair, block, (((1,), (1,)), ((), ())), preferred_element_type=F32
            ).astype(BF16)
    message[...] = dot(line_back[...], held[...]).astype(BF16).reshape(message.shape)


def weight_kernel(per, samples, spec_in, pairs, out):
    rows = 2 * samples
    lanes = out.shape[2]
    half = lanes // 2
    for q in range(MX):
        for first in range(0, per, 2):
            place = first // 2 * lanes
            left = spec_in[q * rows : (q + 1) * rows, place : place + lanes]
            right = pairs[q * rows : (q + 1) * rows, 2 * place : 2 * (place + lanes)]
            outer = lax.dot_general(
                left, right, (((0,), (0,)), ((), ())), preferred_element_type=F32
            )
            out[first * MX + q] = outer[:half, :lanes]
            out[(first + 1) * MX + q] = outer[half:, lanes:]


def whole(array):
    return pl.BlockSpec(array.shape, lambda *step: (0,) * len(array.shape))


def shaped(shape, dtype):
    return jax.ShapeDtypeStruct(shape, dtype)


def params(mib):
    return pltpu.CompilerParams(vmem_limit_bytes=mib * MIB)


def cost(flops, moved, steep=0):
    return pl.CostEstimate(flops=flops, bytes_accessed=moved, transcendentals=steep)


def body(mesh_axes, devices, slabs, activations, cotangent, mode_weights, pointwise, offsets):
    _, channels, width, rows_y, rows_z = activations.shape
    samples = devices // slabs
    per = MY * MZ // devices
    groups = channels // GROUP
    field = activations.shape[1:]
    count = math.prod(field)
    base = z_base(rows_z)
    ytab = y_table(rows_y, width)
    line_fwd, line_inv = x_tables(samples, slabs, NX)
    weight = np.where(np.arange(MZ) == 0, 1.0, 2.0) / (rows_y * rows_z)
    scale = np.tile(np.repeat(weight, GROUP), groups).astype(np.float32)[None]
    base_t, ytab_t = (np.ascontiguousarray(t.T) for t in (base, ytab))
    fwd_t, inv_t = (np.ascontiguousarray(t.T) for t in (line_fwd, line_inv))
    message = shaped((devices, 2 * width, per * channels), BF16)
    spectra = shaped((MX * 2 * samples, per * channels), BF16)
    ztab = pltpu.VMEM((GROUP * rows_z, 2 * MZ * GROUP), BF16)
    ztab_t = pltpu.VMEM((2 * MZ * GROUP, GROUP * rows_z), BF16)
    order = pltpu.VMEM((MZ * channels, MZ * channels), BF16)
    held_plane = pltpu.VMEM((groups, MY * width * 2, MZ * GROUP), BF16)
    held_lines = pltpu.VMEM((groups, width * rows_y, 2 * MZ * GROUP), BF16)
    group_5d = pl.BlockSpec((1, GROUP, width, rows_y, rows_z), lambda g: (0, g, 0, 0, 0))
    group_4d = pl.BlockSpec((GROUP, width, rows_y, rows_z), lambda g: (g, 0, 0, 0))
    plane_flops = 2 * count * 2 * MZ * GROUP

    def exchange(array):
        return lax.all_to_all(array, mesh_axes, split_axis=0, concat_axis=0, tiled=True)

    def mix_points(values, turned, shifts):
        step = 2
        block = pl.BlockSpec((channels, step, rows_y, rows_z), lambda x: (0, x, 0, 0))
        kernel = functools.partial(pointwise_kernel, turned)
        specs = [block, whole(pointwise)]
        operands = [values, pointwise]
        if shifts is None:
            run = lambda a, b, *rest: kernel(a, b, None, *rest)
        else:
            run = kernel
            specs.append(pl.BlockSpec(memory_space=pltpu.SMEM))
            operands.append(shifts)
        return pl.pallas_call(
            run,
            grid=(width // step,),
            in_specs=specs,
            out_specs=block,
            out_shape=shaped(field, BF16),
            scratch_shapes=[
                pltpu.VMEM((channels * TILE, channels * TILE), BF16),
                pltpu.VMEM((channels, 1, rows_z), F32),
            ],
            compiler_params=params(55),
            cost_estimate=cost(2 * count * channels * TILE, 4 * count),
        )(*operands)

    planes = pl.pallas_call(
        functools.partial(plane_kernel, per, channels),
        grid=(groups,),
        in_specs=[group_5d, whole(base), whole(ytab)],
        out_specs=whole(message),
        out_shape=message,
        scratch_shapes=[ztab, order, held_plane],
        compiler_params=params(60),
        cost_estimate=cost(plane_flops, 2 * count),
    )(activations, base, ytab)
    arrived = exchange(planes)
    local = mix_points(activations.reshape(field), True, offsets)
    arrived, local = lax.optimization_barrier((arrived, local))
    spec_in, mixed = pl.pallas_call(
        functools.partial(mix_kernel, per, samples),
        out_shape=(spectra, message),
        scratch_shapes=[pltpu.VMEM(spectra.shape, BF16)],
        compiler_params=params(55),
        cost_estimate=cost(10**8, 2 * mode_weights.size),
    )(arrived, mode_weights, line_fwd, inv_t)
    returned = exchange(mixed)
    slope, back_plane = pl.pallas_call(
        functools.partial(slope_kernel, per, channels),
        grid=(groups,),
        in_specs=[whole(message), group_4d, group_5d]
        + [whole(t) for t in (base, base_t, ytab, ytab_t, scale)],
        out_specs=(group_4d, whole(message)),
        out_shape=(shaped(field, BF16), message),
        scratch_shapes=[ztab, ztab_t, order, held_lines, held_plane],
        compiler_params=params(60),
        cost_estimate=cost(2 * plane_flops, 6 * count, 2 * count),
    )(returned, local, cotangent, base, base_t, ytab, ytab_t, scale)
    arrived_back = exchange(back_plane)
    local_back = mix_points(slope, False, None)
    arrived_back, local_back = lax.optimization_barrier((arrived_back, local_back))
    pairs, mixed_back = pl.pallas_call(
        functools.partial(mix_back_kernel, per, samples),
        out_shape=(shaped((spectra.shape[0], 2 * spectra.shape[1]), BF16), message),
        scratch_shapes=[pltpu.VMEM(spectra.shape, BF16)],
        compiler_params=params(55),
        cost_estimate=cost(10**8, 2 * mode_weights.size),
    )(arrived_back, mode_weights, line_inv, fwd_t)
    returned_back = exchange(mixed_back)
    grad_spectral = pl.pallas_call(
        functools.partial(weight_kernel, per, samples),
        out_shape=shaped(mode_weights.shape, F32),
        compiler_params=params(55),
        cost_estimate=cost(10**8, 4 * mode_weights.size),
    )(spec_in, pairs)
    grad_in = pl.pallas_call(
        functools.partial(field_kernel, per, channels),
        grid=(groups,),
        in_specs=[whole(message), group_4d, whole(base_t), whole(ytab_t)],
        out_specs=group_5d,
        out_shape=shaped(activations.shape, BF16),
        scratch_shapes=[ztab_t, order, held_lines],
        compiler_params=params(60),
        cost_estimate=cost(plane_flops, 4 * count),
    )(returned_back, local_back, base_t, ytab_t)
    return (grad_in, grad_spectral)


def chosen_body(mesh_axes, devices, slabs, activations, cotangent, mode_weights, pointwise, offsets):
    samples, channels, width, rows_y, rows_z = activations.shape
    per = MY * MZ // devices
    fits = (
        samples == 1
        and MY * MZ % devices == 0
        and per in (2, 4, 8)
        and width % 8 == 0
        and channels == 64
        and rows_y % TILE == 0
        and rows_z == 128
    )
    plan = functools.partial(body, mesh_axes, devices, slabs) if fits else general_body
    return plan(activations, cotangent, mode_weights, pointwise, offsets)


def solution(mesh):
    slabs = mesh.shape["space"]
    devices = slabs * mesh.shape["dp"]
    return jax.shard_map(
        functools.partial(chosen_body, ("space", "dp"), devices, slabs),
        mesh=mesh,
        in_specs=(
            P("dp", None, "space", None, None),
            P("dp", None, "space", None, None),
            P(("space", "dp"), None, None),
            P(),
            P(),
        ),
        out_specs=(P("dp", None, "space", None, None), P(("space", "dp"), None, None)),
        check_vma=False,
    )
```

```python
import functools
import math

import jax
import jax.numpy as jnp
import ml_dtypes
import numpy as np
from jax import lax
from jax.experimental import pallas as pl
from jax.experimental.pallas import tpu as pltpu
from jax.sharding import PartitionSpec as P

MX = 16
MY = 16
MZ = 8
NX = 32


def centered(count):
    index = jnp.arange(count, dtype=jnp.int32)
    return jnp.where(index < count // 2, index, index - count)


def plane_tables(rows_y, rows_z, modes_y, modes_z):
    along_y = jnp.arange(rows_y, dtype=jnp.int32)[:, None, None, None]
    along_z = jnp.arange(rows_z, dtype=jnp.int32)[None, :, None, None]
    freq_y = centered(modes_y)[None, None, :, None]
    freq_z = jnp.arange(modes_z, dtype=jnp.int32)[None, None, None, :]
    phase = jnp.mod(freq_y * along_y * rows_z + freq_z * along_z * rows_y, rows_y * rows_z)
    theta = phase.astype(jnp.float32) * (2.0 * math.pi / (rows_y * rows_z))
    cosine = jnp.cos(theta)
    sine = jnp.sin(theta)
    forward = jnp.stack([cosine, -sine], -1).reshape(rows_y * rows_z, modes_y * modes_z * 2)
    scaled = jnp.where(freq_z == 0, 1.0, 2.0).astype(jnp.float32) / (rows_y * rows_z)
    inverse = (
        jnp.stack([cosine * scaled, -sine * scaled], -1)
        .reshape(rows_y * rows_z, modes_y * modes_z * 2)
        .T
    )
    return (forward.astype(jnp.bfloat16), inverse.astype(jnp.bfloat16))


def line_tables(length, modes):
    along = jnp.arange(length, dtype=jnp.int32)[:, None]
    freq = centered(modes)[None, :]
    phase = jnp.mod(freq * along, length)
    theta = phase.astype(jnp.float32) * (2.0 * math.pi / length)
    cosine = jnp.cos(theta)
    sine = jnp.sin(theta)
    first = jnp.stack([cosine, -sine], -1)
    second = jnp.stack([sine, cosine], -1)
    forward = jnp.stack([first, second], 1).reshape(2 * length, 2 * modes)
    inv_first = jnp.stack([cosine.T, sine.T], -1) / length
    inv_second = jnp.stack([-sine.T, cosine.T], -1) / length
    inverse = jnp.stack([inv_first, inv_second], 1).reshape(2 * modes, 2 * length)
    return (forward.astype(jnp.bfloat16), inverse.astype(jnp.bfloat16))


def expand_weights(weights):
    half = weights.shape[1]
    real_part = weights[:, :, :half]
    imag_part = weights[:, :, half:]
    upper = jnp.concatenate([real_part, imag_part], axis=2)
    lower = jnp.concatenate([-imag_part, real_part], axis=2)
    return jnp.concatenate([upper, lower], axis=1)


def outer_sum(left, right):
    return jnp.einsum("mbi,mbo->mio", left, right, preferred_element_type=jnp.float32)


def weight_terms(spec_in, spec_grad):
    half = spec_in.shape[2] // 2
    in_real = spec_in[:, :, :half]
    in_imag = spec_in[:, :, half:]
    gr_real = spec_grad[:, :, :half]
    gr_imag = spec_grad[:, :, half:]
    real_term = outer_sum(in_real, gr_real) + outer_sum(in_imag, gr_imag)
    imag_term = outer_sum(in_real, gr_imag) - outer_sum(in_imag, gr_real)
    return jnp.concatenate([real_term, imag_term], axis=2)


def to_modes(slab, table, modes_x):
    samples, channels, width, pairs = slab.shape
    moved = lax.all_to_all(slab, "space", split_axis=3, concat_axis=2, tiled=True)
    length = moved.shape[2]
    local = moved.shape[3] // 2
    lines = moved.reshape(samples, channels, length, local, 2).transpose(0, 1, 3, 2, 4)
    lines = lines.reshape(samples, channels, local, 2 * length)
    spectra = jnp.dot(lines, table, preferred_element_type=jnp.float32).astype(jnp.bfloat16)
    spectra = spectra.reshape(samples, channels, local, modes_x, 2).transpose(2, 3, 0, 4, 1)
    return spectra.reshape(local * modes_x, samples, 2 * channels)


def to_slab(spectra, table, modes_x, channels):
    count, samples, doubled = spectra.shape
    local = count // modes_x
    lines = spectra.reshape(local, modes_x, samples, 2, channels).transpose(2, 4, 0, 1, 3)
    lines = lines.reshape(samples, channels, local, 2 * modes_x)
    lines = jnp.dot(lines, table, preferred_element_type=jnp.float32).astype(jnp.bfloat16)
    length = lines.shape[3] // 2
    lines = lines.reshape(samples, channels, local, length, 2).transpose(0, 1, 3, 2, 4)
    lines = lines.reshape(samples, channels, length, 2 * local)
    return lax.all_to_all(lines, "space", split_axis=2, concat_axis=3, tiled=True)


def to_owners(spectra):
    return lax.all_to_all(spectra, "dp", split_axis=0, concat_axis=1, tiled=True)


def from_owners(spectra):
    return lax.all_to_all(spectra, "dp", split_axis=1, concat_axis=0, tiled=True)


def gelu_slope(value):
    cdf = 0.5 * (1.0 + lax.erf(value * 0.7071067811865476))
    density = jnp.exp(-0.5 * value * value) * 0.3989422804014327
    return cdf + value * density


def general_body(activations, cotangent, mode_weights, pointwise, offsets):
    samples, channels, width, rows_y, rows_z = activations.shape
    plane_fwd, plane_inv = plane_tables(rows_y, rows_z, MY, MZ)
    line_fwd, line_inv = line_tables(NX, MX)
    flat = activations.reshape(samples, channels, width, rows_y * rows_z)
    planes = jnp.dot(flat, plane_fwd, preferred_element_type=jnp.float32).astype(jnp.bfloat16)
    spec_in = to_modes(planes, line_fwd, MX)
    blocks = expand_weights(mode_weights)
    held_in = to_owners(spec_in)
    held_out = jnp.einsum(
        "mbi,mio->mbo", held_in, blocks, preferred_element_type=jnp.float32
    ).astype(jnp.bfloat16)
    spec_out = from_owners(held_out)
    returned = to_slab(spec_out, line_inv, MX, channels)
    spectral = jnp.dot(returned, plane_inv, preferred_element_type=jnp.float32)
    local_part = jnp.einsum("io,bixn->boxn", pointwise, flat, preferred_element_type=jnp.float32)
    summed = spectral + local_part + offsets[None, :, None, None]
    upstream = cotangent.reshape(flat.shape).astype(jnp.float32)
    slope_grad = (upstream * gelu_slope(summed)).astype(jnp.bfloat16)
    back_plane = jnp.dot(slope_grad, plane_inv.T, preferred_element_type=jnp.float32).astype(
        jnp.bfloat16
    )
    spec_grad = to_modes(back_plane, line_inv.T, MX)
    held_grad = to_owners(spec_grad)
    held_dx = jnp.einsum(
        "mbo,mio->mbi", held_grad, blocks, preferred_element_type=jnp.float32
    ).astype(jnp.bfloat16)
    spec_dx = from_owners(held_dx)
    grad_spectral = weight_terms(held_in, held_grad)
    line_dx = to_slab(spec_dx, line_fwd.T, MX, channels)
    total = jnp.dot(line_dx, plane_fwd.T, preferred_element_type=jnp.float32)
    total = total + jnp.einsum(
        "io,boxn->bixn", pointwise, slope_grad, preferred_element_type=jnp.float32
    )
    grad_in = total.astype(jnp.bfloat16).reshape(activations.shape)
    return (grad_in, grad_spectral)


BF16 = jnp.bfloat16
F32 = jnp.float32
GROUP = 16
TILE = 8
PARTS = 4
HALVES = 2
MIB = 1024 * 1024


def rounded(table):
    return np.asarray(table, np.float32).astype(ml_dtypes.bfloat16)


def angles(freq, points, length):
    phase = np.mod(np.outer(freq, points), length)
    return (phase * (2.0 * math.pi / length)).astype(np.float64)


def signed(count):
    index = np.arange(count)
    return np.where(index < count // 2, index, index - count)


def z_base(rows_z):
    theta = angles(np.arange(MZ), np.arange(rows_z), rows_z)
    pair = np.stack([np.cos(theta), -np.sin(theta)])
    table = np.repeat(pair.reshape(2 * MZ, rows_z), GROUP, axis=0).T
    return rounded(table).astype(np.float32)


def y_table(rows_y, width):
    theta = angles(signed(MY), np.arange(rows_y), rows_y)
    cosine, sine = np.cos(theta), np.sin(theta)
    turn = np.stack([np.stack([cosine, sine]), np.stack([-sine, cosine])])
    table = np.einsum("rsjy,xw->jxrswy", turn, np.eye(width))
    return rounded(table.reshape(MY * width * 2, 2 * width * rows_y))


def x_tables(samples, slabs, length):
    theta = angles(signed(MX), np.arange(length), length)
    cosine, sine = np.cos(theta), np.sin(theta)
    forward = np.stack([np.stack([cosine, sine]), np.stack([-sine, cosine])])
    inverse = np.stack([np.stack([cosine, sine]), np.stack([-sine, cosine])]) / length
    same = np.eye(samples)
    rows = MX * 2 * samples

    def lay(turn):
        turn = turn.reshape(2, 2, MX, slabs, length // slabs)
        table = np.einsum("arqsx,bd->qabsdxr", turn, same)
        return rounded(table.reshape(rows, samples * length * 2))

    return lay(forward), lay(inverse)


def dot(left, right):
    return jnp.dot(left, right, preferred_element_type=F32)


def gelu_slope_rows(value):
    decay = jnp.exp2(value * value * (-0.5 * math.log2(math.e))).astype(BF16)
    value = value.astype(BF16)

    def number(x):
        return jnp.asarray(x, BF16)

    size = jnp.abs(value)
    t = pl.reciprocal(number(1.0) + number(0.3275911 * math.sqrt(0.5)) * size, approx=True)
    tail = number(0.5 * 1.061405429) * t - number(0.5 * 1.453152027)
    tail = tail * t + number(0.5 * 1.421413741)
    tail = tail * t - number(0.5 * 0.284496736)
    tail = tail * t + number(0.5 * 0.254829592)
    part = (size * number(1.0 / math.sqrt(2.0 * math.pi)) - tail * t) * decay
    return jnp.where(value >= number(0.0), number(1.0) + part, -part)


def fill_z(base, table):
    rows_z, lanes = base.shape
    owner = lax.broadcasted_iota(jnp.int32, (rows_z, lanes), 1) % GROUP
    values = base[...]
    for c in range(GROUP):
        table[c * rows_z : (c + 1) * rows_z] = jnp.where(owner == c, values, 0.0).astype(BF16)


def fill_z_back(base, table):
    lanes, rows_z = base.shape
    owner = lax.broadcasted_iota(jnp.int32, (lanes, rows_z), 0) % GROUP
    values = base[...]
    for c in range(GROUP):
        table[:, c * rows_z : (c + 1) * rows_z] = jnp.where(owner == c, values, 0.0).astype(BF16)


def grouped(lane, per, channels):
    c = lane % channels
    return c // GROUP * (MZ * GROUP) + lane // channels * GROUP + c % GROUP


def fill_order(per, channels, back, table):
    count = table.shape[0]
    row = lax.broadcasted_iota(jnp.int32, (count, count), 0)
    column = lax.broadcasted_iota(jnp.int32, (count, count), 1)
    if back:
        same = grouped(row[:, :1], per, channels) == column
    else:
        same = row == grouped(column[:1], per, channels)
    table[...] = jnp.where(same, 1.0, 0.0).astype(BF16)


def analyse(field, ztab, ytab):
    spectra = dot(jnp.concatenate(field, axis=1), ztab).astype(BF16)
    half = spectra.shape[1] // 2
    return dot(ytab, jnp.concatenate([spectra[:, :half], spectra[:, half:]], axis=0))


def deliver(held, order, message, per, channels):
    joined = jnp.concatenate([held[g] for g in range(held.shape[0])], axis=1)
    ordered = dot(joined, order[...]).astype(BF16)
    parts = MZ // per
    rows = message.shape[1]
    lanes = per * channels
    for part in range(parts):
        block = ordered[:, part * lanes : (part + 1) * lanes]
        for j in range(MY):
            message[j * parts + part] = block[j * rows : (j + 1) * rows]


def receive(message, order_back, ytab_back, scale, held, per):
    parts = MZ // per
    blocks = message[...]
    blocks = blocks.reshape(MY, parts, *blocks.shape[1:])
    lanes = [blocks[:, part].reshape(-1, blocks.shape[3]) for part in range(parts)]
    ordered = dot(jnp.concatenate(lanes, axis=1), order_back[...]).astype(BF16)
    lines = dot(ytab_back[...], ordered)
    if scale is not None:
        lines = lines * scale[...]
    lines = lines.astype(BF16)
    rows = lines.shape[0] // 2
    wide = MZ * GROUP
    for group in range(held.shape[0]):
        piece = lines[:, group * wide : (group + 1) * wide]
        held[group] = jnp.concatenate([piece[:rows], piece[rows:]], axis=1)


def channel_rows(parts, c):
    part = parts[c // (GROUP // PARTS)]
    block = part[0, c % (GROUP // PARTS)] if len(part.shape) == 5 else part[c % (GROUP // PARTS)]
    return block.reshape(-1, block.shape[-1])


def plane_kernel(per, channels, *refs):
    field, (base, ytab, message, ztab, order, held) = refs[:PARTS], refs[PARTS:]
    step = pl.program_id(0)

    @pl.when(step == 0)
    def _():
        fill_z(base, ztab)
        fill_order(per, channels, False, order)

    blocks = [channel_rows(field, c) for c in range(GROUP)]
    held[step] = analyse(blocks, ztab[...], ytab[...]).astype(BF16)

    @pl.when(step == pl.num_programs(0) - 1)
    def _():
        deliver(held, order, message, per, channels)


def slope_kernel(per, channels, arrived, *refs):
    local, cotangent, refs = refs[:PARTS], refs[PARTS : 2 * PARTS], refs[2 * PARTS :]
    base, base_back, ytab, ytab_back, scale, slope, message, ztab, ztab_back, order, held, back = refs
    step = pl.program_id(0)
    width, rows_y, rows_z = slope.shape[1:]

    @pl.when(step == 0)
    def _():
        fill_order(per, channels, True, order)
        receive(arrived, order, ytab_back, scale, held, per)
        fill_z(base, ztab)
        fill_z_back(base_back, ztab_back)
        fill_order(per, channels, False, order)

    lines = held[step]
    blocks = []
    for first in range(0, GROUP, 2):
        field = dot(lines, ztab_back[:, first * rows_z : (first + 2) * rows_z])
        for offset in range(2):
            c = first + offset
            value = field[:, offset * rows_z : (offset + 1) * rows_z]
            value = value + channel_rows(local, c).astype(F32)
            result = channel_rows(cotangent, c) * gelu_slope_rows(value)
            slope[c] = result.reshape(width, rows_y, rows_z)
            blocks.append(result)
    plane = analyse(blocks, ztab[...], ytab[...]) * scale[:, : MZ * GROUP]
    back[step] = plane.astype(BF16)

    @pl.when(step == pl.num_programs(0) - 1)
    def _():
        deliver(back, order, message, per, channels)


def field_kernel(per, channels, arrived, *refs):
    local, (base_back, ytab_back, out, ztab_back, order, held) = refs[:PARTS], refs[PARTS:]
    step = pl.program_id(0)
    width, rows_y, rows_z = out.shape[2:]

    @pl.when(step == 0)
    def _():
        fill_order(per, channels, True, order)
        receive(arrived, order, ytab_back, None, held, per)
        fill_z_back(base_back, ztab_back)

    lines = held[step]
    for first in range(0, GROUP, 2):
        field = dot(lines, ztab_back[:, first * rows_z : (first + 2) * rows_z])
        for offset in range(2):
            c = first + offset
            value = field[:, offset * rows_z : (offset + 1) * rows_z]
            value = value + channel_rows(local, c).astype(F32)
            out[0, c] = value.astype(BF16).reshape(width, rows_y, rows_z)


def pointwise_kernel(turned, shifted, *refs):
    field, mix, refs = refs[:PARTS], refs[PARTS], refs[PARTS + 1 :]
    offsets, (out, table, shift) = (refs[0], refs[1:]) if shifted else (None, refs)
    channels = mix.shape[0]
    width, rows_y, rows_z = out.shape[1:]
    size = channels * TILE

    @pl.when(pl.program_id(0) == 0)
    def _():
        row = lax.broadcasted_iota(jnp.int32, (size, channels), 0) // TILE
        column = lax.broadcasted_iota(jnp.int32, (size, channels), 1)
        spread = jnp.where(row == column, 1.0, 0.0).astype(BF16)
        tall = lax.dot_general(
            spread, mix[...], (((1,), (1 if turned else 0,)), ((), ())), preferred_element_type=F32
        ).astype(BF16)
        whole = lax.dot_general(
            tall, spread, (((1,), (1,)), ((), ())), preferred_element_type=F32
        )
        place = lax.broadcasted_iota(jnp.int32, (size, size), 0) % TILE
        other = lax.broadcasted_iota(jnp.int32, (size, size), 1) % TILE
        table[...] = jnp.where(place == other, whole, 0.0).astype(BF16)
        if offsets is not None:
            for c in range(channels):
                shift[c] = jnp.full((1, rows_z), offsets[c], F32)

    for start in range(0, rows_y, 2 * TILE):
        pieces = [
            jnp.concatenate([part[:, x, start : start + 2 * TILE, :] for part in field], axis=0).astype(F32)
            for x in range(width)
        ]
        halves = []
        for row in range(0, 2 * TILE, TILE):
            rows = [piece[:, row : row + TILE].reshape(size, rows_z).astype(BF16) for piece in pieces]
            halves.append(dot(table[...], jnp.concatenate(rows, axis=1)))
        for x in range(width):
            values = [
                half[:, x * rows_z : (x + 1) * rows_z].reshape(channels, TILE, rows_z) for half in halves
            ]
            value = jnp.concatenate(values, axis=1)
            if offsets is not None:
                value = value + shift[...]
            out[:, x, start : start + 2 * TILE, :] = value.astype(BF16)


def spread_pair(first, second):
    nothing = jnp.zeros_like(first)
    upper = jnp.concatenate([first, nothing], axis=1)
    lower = jnp.concatenate([nothing, second], axis=1)
    return jnp.concatenate([upper, lower], axis=0)


def low_half(shape):
    return lax.broadcasted_iota(jnp.int32, shape, 1) < shape[1] // 2


def fill_halves(per, channels, back, table):
    count = table.shape[0]
    size = channels // HALVES
    row = lax.broadcasted_iota(jnp.int32, (count, count), 0)
    column = lax.broadcasted_iota(jnp.int32, (count, count), 1)
    halved, plain = (row[:, :1], column) if back else (column[:1], row)
    inner = halved % (per * size)
    place = inner // size * channels + halved // (per * size) * size + inner % size
    table[...] = jnp.where(place == plain, 1.0, 0.0).astype(BF16)


def mix_kernel(per, samples, arrived, weights, line, line_back, spec_in, first_half, second_half, held, order):
    rows = 2 * samples
    lanes = 2 * weights.shape[1]
    low = low_half((samples, lanes))
    flat = arrived[...].reshape(-1, arrived.shape[2])
    spectra = dot(line[...], flat).astype(BF16)
    spec_in[...] = spectra
    for q in range(MX):
        for first in range(0, per, 2):
            block = spread_pair(weights[first * MX + q], weights[(first + 1) * MX + q])
            place = first // 2 * lanes
            terms = dot(spectra[q * rows : (q + 1) * rows, place : place + lanes], block)
            mixed = []
            for side in range(2):
                part = terms[:, side * lanes : (side + 1) * lanes]
                turned = pltpu.roll(part[samples:], lanes // 2, 1)
                mixed.append(part[:samples] + jnp.where(low, -turned, turned))
            real = jnp.where(low, mixed[0], pltpu.roll(mixed[1], lanes // 2, 1))
            imag = jnp.where(low, pltpu.roll(mixed[0], lanes // 2, 1), mixed[1])
            held[q * rows : (q + 1) * rows, place : place + lanes] = jnp.concatenate(
                [real, imag], axis=0
            ).astype(BF16)
    fill_halves(per, lanes // 2, False, order)
    ordered = dot(held[...], order[...]).astype(BF16)
    for half, message in enumerate((first_half, second_half)):
        count = message.shape[2]
        lines = dot(line_back[...], ordered[:, half * count : (half + 1) * count])
        message[...] = lines.astype(BF16).reshape(message.shape)


def mix_back_kernel(
    per, samples, first_half, second_half, weights, line, line_back, pairs, message, held, order
):
    rows = 2 * samples
    lanes = 2 * weights.shape[1]
    low = low_half((samples, lanes))
    fill_halves(per, lanes // 2, True, order)
    flat = [half[...].reshape(-1, half.shape[2]) for half in (first_half, second_half)]
    halved = dot(line[...], jnp.concatenate(flat, axis=1)).astype(BF16)
    spectra = dot(halved, order[...])
    for q in range(MX):
        for first in range(0, per, 2):
            block = spread_pair(weights[first * MX + q], weights[(first + 1) * MX + q])
            place = first // 2 * lanes
            real = spectra[q * rows : q * rows + samples, place : place + lanes]
            imag = spectra[q * rows + samples : (q + 1) * rows, place : place + lanes]
            real_turned = pltpu.roll(real, lanes // 2, 1)
            imag_turned = pltpu.roll(imag, lanes // 2, 1)
            left = [jnp.where(low, real, imag_turned), jnp.where(low, imag, -real_turned)]
            right = [jnp.where(low, real_turned, imag), jnp.where(low, imag_turned, -real)]
            pair = jnp.concatenate(
                [jnp.concatenate(left, axis=0), jnp.concatenate(right, axis=0)], axis=1
            ).astype(BF16)
            pairs[q * rows : (q + 1) * rows, 2 * place : 2 * (place + lanes)] = pair
            held[q * rows : (q + 1) * rows, place : place + lanes] = lax.dot_general(
                pair, block, (((1,), (1,)), ((), ())), preferred_element_type=F32
            ).astype(BF16)
    message[...] = dot(line_back[...], held[...]).astype(BF16).reshape(message.shape)


def weight_kernel(per, samples, spec_in, pairs, out):
    rows = 2 * samples
    lanes = out.shape[2]
    half = lanes // 2
    for q in range(MX):
        for first in range(0, per, 2):
            place = first // 2 * lanes
            left = spec_in[q * rows : (q + 1) * rows, place : place + lanes]
            right = pairs[q * rows : (q + 1) * rows, 2 * place : 2 * (place + lanes)]
            outer = lax.dot_general(
                left, right, (((0,), (0,)), ((), ())), preferred_element_type=F32
            )
            out[first * MX + q] = outer[:half, :lanes]
            out[(first + 1) * MX + q] = outer[half:, lanes:]


def whole(array):
    return pl.BlockSpec(array.shape, lambda *step: (0,) * len(array.shape))


def shaped(shape, dtype):
    return jax.ShapeDtypeStruct(shape, dtype)


def params(mib):
    return pltpu.CompilerParams(vmem_limit_bytes=mib * MIB)


def cost(flops, moved, steep=0):
    return pl.CostEstimate(flops=flops, bytes_accessed=moved, transcendentals=steep)


def body(mesh_axes, devices, slabs, activations, cotangent, mode_weights, pointwise, offsets):
    _, channels, width, rows_y, rows_z = activations.shape
    samples = devices // slabs
    per = MY * MZ // devices
    groups = channels // GROUP
    field = activations.shape[1:]
    count = math.prod(field)
    base = z_base(rows_z)
    ytab = y_table(rows_y, width)
    line_fwd, line_inv = x_tables(samples, slabs, NX)
    weight = np.where(np.arange(MZ) == 0, 1.0, 2.0) / (rows_y * rows_z)
    scale = np.tile(np.repeat(weight, GROUP), groups // HALVES).astype(np.float32)[None]
    base_t, ytab_t = (np.ascontiguousarray(t.T) for t in (base, ytab))
    fwd_t, inv_t = (np.ascontiguousarray(t.T) for t in (line_fwd, line_inv))
    message = shaped((devices, 2 * width, per * channels), BF16)
    half_channels = channels // HALVES
    half_groups = groups // HALVES
    half_message = shaped((devices, 2 * width, per * half_channels), BF16)
    spectra = shaped((MX * 2 * samples, per * channels), BF16)
    ztab = pltpu.VMEM((GROUP * rows_z, 2 * MZ * GROUP), BF16)
    ztab_t = pltpu.VMEM((2 * MZ * GROUP, GROUP * rows_z), BF16)
    halves_order = pltpu.VMEM((per * channels, per * channels), BF16)
    group_5d = pl.BlockSpec((1, GROUP, width, rows_y, rows_z), lambda g: (0, g, 0, 0, 0))
    group_4d = pl.BlockSpec((GROUP, width, rows_y, rows_z), lambda g: (g, 0, 0, 0))

    def order_of(count):
        return pltpu.VMEM((MZ * count, MZ * count), BF16)

    def held_plane(count):
        return pltpu.VMEM((count, MY * width * 2, MZ * GROUP), BF16)

    def held_lines(count):
        return pltpu.VMEM((count, width * rows_y, 2 * MZ * GROUP), BF16)

    def parts_5d(first):
        size = GROUP // PARTS
        return [
            pl.BlockSpec((1, size, width, rows_y, rows_z), lambda g, i=i: (0, (g + first) * PARTS + i, 0, 0, 0))
            for i in range(PARTS)
        ]

    def parts_4d(first):
        size = GROUP // PARTS
        return [
            pl.BlockSpec((size, width, rows_y, rows_z), lambda g, i=i: ((g + first) * PARTS + i, 0, 0, 0))
            for i in range(PARTS)
        ]

    plane_flops = 2 * count * 2 * MZ * GROUP

    def exchange(array):
        return lax.all_to_all(array, mesh_axes, split_axis=0, concat_axis=0, tiled=True)

    def mix_points(pieces, turned, shifts):
        step = 2
        size = channels // PARTS
        each = PARTS // len(pieces)
        specs = [
            pl.BlockSpec((size, step, rows_y, rows_z), lambda x, i=i: (i % each, x, 0, 0)) for i in range(PARTS)
        ]
        specs.append(whole(pointwise))
        operands = [pieces[i // each] for i in range(PARTS)] + [pointwise]
        if shifts is not None:
            specs.append(pl.BlockSpec(memory_space=pltpu.SMEM))
            operands.append(shifts)
        return pl.pallas_call(
            functools.partial(pointwise_kernel, turned, shifts is not None),
            grid=(width // step,),
            in_specs=specs,
            out_specs=pl.BlockSpec((channels, step, rows_y, rows_z), lambda x: (0, x, 0, 0)),
            out_shape=shaped(field, BF16),
            scratch_shapes=[
                pltpu.VMEM((channels * TILE, channels * TILE), BF16),
                pltpu.VMEM((channels, 1, rows_z), F32),
            ],
            compiler_params=params(55),
            cost_estimate=cost(2 * count * channels * TILE, 4 * count),
        )(*operands)

    def slopes(half, arrived, local):
        first = half * half_groups
        out_shape = (shaped((half_channels,) + field[1:], BF16), half_message)
        return pl.pallas_call(
            functools.partial(slope_kernel, per, half_channels),
            grid=(half_groups,),
            in_specs=[whole(half_message)]
            + parts_4d(first)
            + parts_5d(first)
            + [whole(t) for t in (base, base_t, ytab, ytab_t, scale)],
            out_specs=(group_4d, whole(half_message)),
            out_shape=out_shape,
            scratch_shapes=[ztab, ztab_t, order_of(half_channels), held_lines(half_groups), held_plane(half_groups)],
            compiler_params=params(55),
            cost_estimate=cost(2 * plane_flops // HALVES, 6 * count // HALVES, 2 * count // HALVES),
        )(arrived, *[local] * PARTS, *[cotangent] * PARTS, base, base_t, ytab, ytab_t, scale)

    planes = pl.pallas_call(
        functools.partial(plane_kernel, per, channels),
        grid=(groups,),
        in_specs=parts_5d(0) + [whole(base), whole(ytab)],
        out_specs=whole(message),
        out_shape=message,
        scratch_shapes=[ztab, order_of(channels), held_plane(groups)],
        compiler_params=params(60),
        cost_estimate=cost(plane_flops, 2 * count),
    )(*[activations] * PARTS, base, ytab)
    arrived = exchange(planes)
    local = mix_points([activations.reshape(field)], True, offsets)
    arrived, local = lax.optimization_barrier((arrived, local))
    spec_in, *mixed = pl.pallas_call(
        functools.partial(mix_kernel, per, samples),
        out_shape=(spectra, half_message, half_message),
        scratch_shapes=[pltpu.VMEM(spectra.shape, BF16), halves_order],
        compiler_params=params(55),
        cost_estimate=cost(10**8, 2 * mode_weights.size),
    )(arrived, mode_weights, line_fwd, inv_t)
    returned = [exchange(half) for half in mixed]
    worked = [slopes(half, returned[half], local) for half in range(HALVES)]
    arrived_back = [exchange(planes_half) for _, planes_half in worked]
    local_back = mix_points([slope for slope, _ in worked], False, None)
    pairs, mixed_back = pl.pallas_call(
        functools.partial(mix_back_kernel, per, samples),
        out_shape=(shaped((spectra.shape[0], 2 * spectra.shape[1]), BF16), message),
        scratch_shapes=[pltpu.VMEM(spectra.shape, BF16), halves_order],
        compiler_params=params(55),
        cost_estimate=cost(10**8, 2 * mode_weights.size),
    )(*arrived_back, mode_weights, line_inv, fwd_t)
    returned_back = exchange(mixed_back)
    grad_spectral = pl.pallas_call(
        functools.partial(weight_kernel, per, samples),
        out_shape=shaped(mode_weights.shape, F32),
        compiler_params=params(55),
        cost_estimate=cost(10**8, 4 * mode_weights.size),
    )(spec_in, pairs)
    grad_in = pl.pallas_call(
        functools.partial(field_kernel, per, channels),
        grid=(groups,),
        in_specs=[whole(message)] + parts_4d(0) + [whole(base_t), whole(ytab_t)],
        out_specs=group_5d,
        out_shape=shaped(activations.shape, BF16),
        scratch_shapes=[ztab_t, order_of(channels), held_lines(groups)],
        compiler_params=params(60),
        cost_estimate=cost(plane_flops, 4 * count),
    )(returned_back, *[local_back] * PARTS, base_t, ytab_t)
    return (grad_in, grad_spectral)


def chosen_body(mesh_axes, devices, slabs, activations, cotangent, mode_weights, pointwise, offsets):
    samples, channels, width, rows_y, rows_z = activations.shape
    per = MY * MZ // devices
    fits = (
        samples == 1
        and MY * MZ % devices == 0
        and per in (2, 4, 8)
        and width % 8 == 0
        and channels == 64
        and rows_y % TILE == 0
        and rows_z == 128
    )
    plan = functools.partial(body, mesh_axes, devices, slabs) if fits else general_body
    return plan(activations, cotangent, mode_weights, pointwise, offsets)


def solution(mesh):
    slabs = mesh.shape["space"]
    devices = slabs * mesh.shape["dp"]
    return jax.shard_map(
        functools.partial(chosen_body, ("space", "dp"), devices, slabs),
        mesh=mesh,
        in_specs=(
            P("dp", None, "space", None, None),
            P("dp", None, "space", None, None),
            P(("space", "dp"), None, None),
            P(),
            P(),
        ),
        out_specs=(P("dp", None, "space", None, None), P(("space", "dp"), None, None)),
        check_vma=False,
    )
```

```python
import functools
import math

import jax
import jax.numpy as jnp
import ml_dtypes
import numpy as np
from jax import lax
from jax.experimental import pallas as pl
from jax.experimental.pallas import tpu as pltpu
from jax.sharding import PartitionSpec as P

MX = 16
MY = 16
MZ = 8
NX = 32


def centered(count):
    index = jnp.arange(count, dtype=jnp.int32)
    return jnp.where(index < count // 2, index, index - count)


def plane_tables(rows_y, rows_z, modes_y, modes_z):
    along_y = jnp.arange(rows_y, dtype=jnp.int32)[:, None, None, None]
    along_z = jnp.arange(rows_z, dtype=jnp.int32)[None, :, None, None]
    freq_y = centered(modes_y)[None, None, :, None]
    freq_z = jnp.arange(modes_z, dtype=jnp.int32)[None, None, None, :]
    phase = jnp.mod(freq_y * along_y * rows_z + freq_z * along_z * rows_y, rows_y * rows_z)
    theta = phase.astype(jnp.float32) * (2.0 * math.pi / (rows_y * rows_z))
    cosine = jnp.cos(theta)
    sine = jnp.sin(theta)
    forward = jnp.stack([cosine, -sine], -1).reshape(rows_y * rows_z, modes_y * modes_z * 2)
    scaled = jnp.where(freq_z == 0, 1.0, 2.0).astype(jnp.float32) / (rows_y * rows_z)
    inverse = (
        jnp.stack([cosine * scaled, -sine * scaled], -1)
        .reshape(rows_y * rows_z, modes_y * modes_z * 2)
        .T
    )
    return (forward.astype(jnp.bfloat16), inverse.astype(jnp.bfloat16))


def line_tables(length, modes):
    along = jnp.arange(length, dtype=jnp.int32)[:, None]
    freq = centered(modes)[None, :]
    phase = jnp.mod(freq * along, length)
    theta = phase.astype(jnp.float32) * (2.0 * math.pi / length)
    cosine = jnp.cos(theta)
    sine = jnp.sin(theta)
    first = jnp.stack([cosine, -sine], -1)
    second = jnp.stack([sine, cosine], -1)
    forward = jnp.stack([first, second], 1).reshape(2 * length, 2 * modes)
    inv_first = jnp.stack([cosine.T, sine.T], -1) / length
    inv_second = jnp.stack([-sine.T, cosine.T], -1) / length
    inverse = jnp.stack([inv_first, inv_second], 1).reshape(2 * modes, 2 * length)
    return (forward.astype(jnp.bfloat16), inverse.astype(jnp.bfloat16))


def expand_weights(weights):
    half = weights.shape[1]
    real_part = weights[:, :, :half]
    imag_part = weights[:, :, half:]
    upper = jnp.concatenate([real_part, imag_part], axis=2)
    lower = jnp.concatenate([-imag_part, real_part], axis=2)
    return jnp.concatenate([upper, lower], axis=1)


def outer_sum(left, right):
    return jnp.einsum("mbi,mbo->mio", left, right, preferred_element_type=jnp.float32)


def weight_terms(spec_in, spec_grad):
    half = spec_in.shape[2] // 2
    in_real = spec_in[:, :, :half]
    in_imag = spec_in[:, :, half:]
    gr_real = spec_grad[:, :, :half]
    gr_imag = spec_grad[:, :, half:]
    real_term = outer_sum(in_real, gr_real) + outer_sum(in_imag, gr_imag)
    imag_term = outer_sum(in_real, gr_imag) - outer_sum(in_imag, gr_real)
    return jnp.concatenate([real_term, imag_term], axis=2)


def to_modes(slab, table, modes_x):
    samples, channels, width, pairs = slab.shape
    moved = lax.all_to_all(slab, "space", split_axis=3, concat_axis=2, tiled=True)
    length = moved.shape[2]
    local = moved.shape[3] // 2
    lines = moved.reshape(samples, channels, length, local, 2).transpose(0, 1, 3, 2, 4)
    lines = lines.reshape(samples, channels, local, 2 * length)
    spectra = jnp.dot(lines, table, preferred_element_type=jnp.float32).astype(jnp.bfloat16)
    spectra = spectra.reshape(samples, channels, local, modes_x, 2).transpose(2, 3, 0, 4, 1)
    return spectra.reshape(local * modes_x, samples, 2 * channels)


def to_slab(spectra, table, modes_x, channels):
    count, samples, doubled = spectra.shape
    local = count // modes_x
    lines = spectra.reshape(local, modes_x, samples, 2, channels).transpose(2, 4, 0, 1, 3)
    lines = lines.reshape(samples, channels, local, 2 * modes_x)
    lines = jnp.dot(lines, table, preferred_element_type=jnp.float32).astype(jnp.bfloat16)
    length = lines.shape[3] // 2
    lines = lines.reshape(samples, channels, local, length, 2).transpose(0, 1, 3, 2, 4)
    lines = lines.reshape(samples, channels, length, 2 * local)
    return lax.all_to_all(lines, "space", split_axis=2, concat_axis=3, tiled=True)


def to_owners(spectra):
    return lax.all_to_all(spectra, "dp", split_axis=0, concat_axis=1, tiled=True)


def from_owners(spectra):
    return lax.all_to_all(spectra, "dp", split_axis=1, concat_axis=0, tiled=True)


def gelu_slope(value):
    cdf = 0.5 * (1.0 + lax.erf(value * 0.7071067811865476))
    density = jnp.exp(-0.5 * value * value) * 0.3989422804014327
    return cdf + value * density


def general_body(activations, cotangent, mode_weights, pointwise, offsets):
    samples, channels, width, rows_y, rows_z = activations.shape
    plane_fwd, plane_inv = plane_tables(rows_y, rows_z, MY, MZ)
    line_fwd, line_inv = line_tables(NX, MX)
    flat = activations.reshape(samples, channels, width, rows_y * rows_z)
    planes = jnp.dot(flat, plane_fwd, preferred_element_type=jnp.float32).astype(jnp.bfloat16)
    spec_in = to_modes(planes, line_fwd, MX)
    blocks = expand_weights(mode_weights)
    held_in = to_owners(spec_in)
    held_out = jnp.einsum(
        "mbi,mio->mbo", held_in, blocks, preferred_element_type=jnp.float32
    ).astype(jnp.bfloat16)
    spec_out = from_owners(held_out)
    returned = to_slab(spec_out, line_inv, MX, channels)
    spectral = jnp.dot(returned, plane_inv, preferred_element_type=jnp.float32)
    local_part = jnp.einsum("io,bixn->boxn", pointwise, flat, preferred_element_type=jnp.float32)
    summed = spectral + local_part + offsets[None, :, None, None]
    upstream = cotangent.reshape(flat.shape).astype(jnp.float32)
    slope_grad = (upstream * gelu_slope(summed)).astype(jnp.bfloat16)
    back_plane = jnp.dot(slope_grad, plane_inv.T, preferred_element_type=jnp.float32).astype(
        jnp.bfloat16
    )
    spec_grad = to_modes(back_plane, line_inv.T, MX)
    held_grad = to_owners(spec_grad)
    held_dx = jnp.einsum(
        "mbo,mio->mbi", held_grad, blocks, preferred_element_type=jnp.float32
    ).astype(jnp.bfloat16)
    spec_dx = from_owners(held_dx)
    grad_spectral = weight_terms(held_in, held_grad)
    line_dx = to_slab(spec_dx, line_fwd.T, MX, channels)
    total = jnp.dot(line_dx, plane_fwd.T, preferred_element_type=jnp.float32)
    total = total + jnp.einsum(
        "io,boxn->bixn", pointwise, slope_grad, preferred_element_type=jnp.float32
    )
    grad_in = total.astype(jnp.bfloat16).reshape(activations.shape)
    return (grad_in, grad_spectral)


BF16 = jnp.bfloat16
F32 = jnp.float32
GROUP = 16
TILE = 8
MIB = 1024 * 1024


def rounded(table):
    return np.asarray(table, np.float32).astype(ml_dtypes.bfloat16)


def angles(freq, points, length):
    phase = np.mod(np.outer(freq, points), length)
    return (phase * (2.0 * math.pi / length)).astype(np.float64)


def signed(count):
    index = np.arange(count)
    return np.where(index < count // 2, index, index - count)


def z_base(rows_z):
    theta = angles(np.arange(MZ), np.arange(rows_z), rows_z)
    pair = np.stack([np.cos(theta), -np.sin(theta)])
    table = np.repeat(pair.reshape(2 * MZ, rows_z), GROUP, axis=0).T
    return rounded(table).astype(np.float32)


def y_table(rows_y, width):
    theta = angles(signed(MY), np.arange(rows_y), rows_y)
    cosine, sine = np.cos(theta), np.sin(theta)
    turn = np.stack([np.stack([cosine, sine]), np.stack([-sine, cosine])])
    table = np.einsum("rsjy,xw->jxrswy", turn, np.eye(width))
    return rounded(table.reshape(MY * width * 2, 2 * width * rows_y))


def x_tables(samples, slabs, length):
    theta = angles(signed(MX), np.arange(length), length)
    cosine, sine = np.cos(theta), np.sin(theta)
    forward = np.stack([np.stack([cosine, sine]), np.stack([-sine, cosine])])
    inverse = np.stack([np.stack([cosine, sine]), np.stack([-sine, cosine])]) / length
    same = np.eye(samples)
    rows = MX * 2 * samples

    def lay(turn):
        turn = turn.reshape(2, 2, MX, slabs, length // slabs)
        table = np.einsum("arqsx,bd->qabsdxr", turn, same)
        return rounded(table.reshape(rows, samples * length * 2))

    return lay(forward), lay(inverse)


def dot(left, right):
    return jnp.dot(left, right, preferred_element_type=F32)


def gelu_slope_rows(value):
    decay = jnp.exp2(value * value * (-0.5 * math.log2(math.e))).astype(BF16)
    value = value.astype(BF16)

    def number(x):
        return jnp.asarray(x, BF16)

    size = jnp.abs(value)
    t = pl.reciprocal(number(1.0) + number(0.3275911 * math.sqrt(0.5)) * size, approx=True)
    tail = number(0.5 * 1.061405429) * t - number(0.5 * 1.453152027)
    tail = tail * t + number(0.5 * 1.421413741)
    tail = tail * t - number(0.5 * 0.284496736)
    tail = tail * t + number(0.5 * 0.254829592)
    part = (size * number(1.0 / math.sqrt(2.0 * math.pi)) - tail * t) * decay
    return jnp.where(value >= number(0.0), number(1.0) + part, -part)


def fill_z(base, table):
    rows_z, lanes = base.shape
    owner = lax.broadcasted_iota(jnp.int32, (rows_z, lanes), 1) % GROUP
    values = base[...]
    for c in range(GROUP):
        table[c * rows_z : (c + 1) * rows_z] = jnp.where(owner == c, values, 0.0).astype(BF16)


def fill_z_back(base, table):
    lanes, rows_z = base.shape
    owner = lax.broadcasted_iota(jnp.int32, (lanes, rows_z), 0) % GROUP
    values = base[...]
    for c in range(GROUP):
        table[:, c * rows_z : (c + 1) * rows_z] = jnp.where(owner == c, values, 0.0).astype(BF16)


def grouped(lane, per, channels):
    c = lane % channels
    return c // GROUP * (MZ * GROUP) + lane // channels * GROUP + c % GROUP


def fill_order(per, channels, back, table):
    count = table.shape[0]
    row = lax.broadcasted_iota(jnp.int32, (count, count), 0)
    column = lax.broadcasted_iota(jnp.int32, (count, count), 1)
    if back:
        same = grouped(row[:, :1], per, channels) == column
    else:
        same = row == grouped(column[:1], per, channels)
    table[...] = jnp.where(same, 1.0, 0.0).astype(BF16)


def analyse(field, ztab, ytab):
    spectra = dot(jnp.concatenate(field, axis=1), ztab).astype(BF16)
    half = spectra.shape[1] // 2
    return dot(ytab, jnp.concatenate([spectra[:, :half], spectra[:, half:]], axis=0))


def deliver(held, order, message, per, channels):
    joined = jnp.concatenate([held[g] for g in range(held.shape[0])], axis=1)
    ordered = dot(joined, order[...]).astype(BF16)
    parts = MZ // per
    rows = message.shape[1]
    lanes = per * channels
    for part in range(parts):
        block = ordered[:, part * lanes : (part + 1) * lanes]
        for j in range(MY):
            message[j * parts + part] = block[j * rows : (j + 1) * rows]


def receive(message, order_back, ytab_back, scale, held, per):
    parts = MZ // per
    blocks = message[...]
    blocks = blocks.reshape(MY, parts, *blocks.shape[1:])
    lanes = [blocks[:, part].reshape(-1, blocks.shape[3]) for part in range(parts)]
    ordered = dot(jnp.concatenate(lanes, axis=1), order_back[...]).astype(BF16)
    lines = dot(ytab_back[...], ordered)
    if scale is not None:
        lines = lines * scale[...]
    lines = lines.astype(BF16)
    rows = lines.shape[0] // 2
    wide = MZ * GROUP
    for group in range(held.shape[0]):
        piece = lines[:, group * wide : (group + 1) * wide]
        held[group] = jnp.concatenate([piece[:rows], piece[rows:]], axis=1)


def move(source, target, sems, g):
    run = pl.ds(g * GROUP, GROUP)
    return pltpu.make_async_copy(source.at[run], target.at[run], sems.at[g])


def plane_kernel(per, channels, field, base, ytab, message, ztab, order, held, buffer, sems):
    groups = held.shape[0]
    rows_z = field.shape[-1]
    for g in range(groups):
        move(field.at[0], buffer, sems, g).start()
    fill_z(base, ztab)
    fill_order(per, channels, False, order)

    @pl.loop(0, groups)
    def _(g):
        move(field.at[0], buffer, sems, g).wait()
        blocks = [buffer[g * GROUP + c].reshape(-1, rows_z) for c in range(GROUP)]
        held[g] = analyse(blocks, ztab[...], ytab[...]).astype(BF16)

    deliver(held, order, message, per, channels)


def slope_kernel(
    per, channels, arrived, local, cotangent, base, base_back, ytab, ytab_back, scale,
    slope, message, ztab, ztab_back, order, held, back, local_in, cotangent_in, result, first_sum, second_sum,
    local_sems, cotangent_sems, result_sems,
):
    groups = held.shape[0]
    width, rows_y, rows_z = local.shape[1:]
    for g in range(groups):
        move(local, local_in, local_sems, g).start()
        move(cotangent.at[0], cotangent_in, cotangent_sems, g).start()
    fill_order(per, channels, True, order)
    receive(arrived, order, ytab_back, scale, held, per)
    fill_z_back(base_back, ztab_back)
    fill_z(base, ztab)
    fill_order(per, channels, False, order)
    wide = 2 * rows_y

    @pl.loop(0, groups)
    def _(g):
        move(local, local_in, local_sems, g).wait()
        move(cotangent.at[0], cotangent_in, cotangent_sems, g).wait()
        lines = held[g]
        for first in range(0, GROUP, 2):
            total = first_sum if first % 4 else second_sum
            total[...] = dot(lines, ztab_back[:, first * rows_z : (first + 2) * rows_z])
            for offset in range(2):
                c = g * GROUP + first + offset
                for x in range(0, width, 2):
                    value = total[x * rows_y : x * rows_y + wide, offset * rows_z : (offset + 1) * rows_z]
                    value = value + local_in[c, x : x + 2].reshape(wide, rows_z).astype(F32)
                    upstream = cotangent_in[c, x : x + 2].reshape(wide, rows_z)
                    answer = upstream * gelu_slope_rows(value)
                    result[c, x : x + 2] = answer.reshape(2, rows_y, rows_z)
        move(result, slope, result_sems, g).start()
        blocks = [result[g * GROUP + c].reshape(-1, rows_z) for c in range(GROUP)]
        plane = analyse(blocks, ztab[...], ytab[...]) * scale[:, : MZ * GROUP]
        back[g] = plane.astype(BF16)

    deliver(back, order, message, per, channels)
    for g in range(groups):
        move(result, slope, result_sems, g).wait()


def field_kernel(
    per, channels, arrived, local, base_back, ytab_back, out, ztab_back, order, held, local_in, result,
    local_sems, result_sems,
):
    groups = held.shape[0]
    width, rows_y, rows_z = local.shape[1:]
    for g in range(groups):
        move(local, local_in, local_sems, g).start()
    fill_order(per, channels, True, order)
    receive(arrived, order, ytab_back, None, held, per)
    fill_z_back(base_back, ztab_back)

    @pl.loop(0, groups)
    def _(g):
        move(local, local_in, local_sems, g).wait()
        lines = held[g]
        for first in range(0, GROUP, 2):
            total = dot(lines, ztab_back[:, first * rows_z : (first + 2) * rows_z])
            for offset in range(2):
                c = g * GROUP + first + offset
                value = total[:, offset * rows_z : (offset + 1) * rows_z]
                value = value + local_in[c].reshape(-1, rows_z).astype(F32)
                result[c] = value.astype(BF16).reshape(width, rows_y, rows_z)
        move(result, out.at[0], result_sems, g).start()

    for g in range(groups):
        move(result, out.at[0], result_sems, g).wait()


def pointwise_kernel(turned, field, mix, offsets, out, table, shift):
    channels = mix.shape[0]
    width, rows_y, rows_z = field.shape[1:]
    size = channels * TILE

    @pl.when(pl.program_id(0) == 0)
    def _():
        row = lax.broadcasted_iota(jnp.int32, (size, channels), 0) // TILE
        column = lax.broadcasted_iota(jnp.int32, (size, channels), 1)
        spread = jnp.where(row == column, 1.0, 0.0).astype(BF16)
        tall = lax.dot_general(
            spread, mix[...], (((1,), (1 if turned else 0,)), ((), ())), preferred_element_type=F32
        ).astype(BF16)
        whole = lax.dot_general(
            tall, spread, (((1,), (1,)), ((), ())), preferred_element_type=F32
        )
        place = lax.broadcasted_iota(jnp.int32, (size, size), 0) % TILE
        other = lax.broadcasted_iota(jnp.int32, (size, size), 1) % TILE
        table[...] = jnp.where(place == other, whole, 0.0).astype(BF16)
        if offsets is not None:
            for c in range(channels):
                shift[c] = jnp.full((1, rows_z), offsets[c], F32)

    for start in range(0, rows_y, 2 * TILE):
        pieces = [field[:, x, start : start + 2 * TILE, :].astype(F32) for x in range(width)]
        halves = []
        for row in range(0, 2 * TILE, TILE):
            rows = [piece[:, row : row + TILE].reshape(size, rows_z).astype(BF16) for piece in pieces]
            halves.append(dot(table[...], jnp.concatenate(rows, axis=1)))
        for x in range(width):
            values = [
                half[:, x * rows_z : (x + 1) * rows_z].reshape(channels, TILE, rows_z) for half in halves
            ]
            value = jnp.concatenate(values, axis=1)
            if offsets is not None:
                value = value + shift[...]
            out[:, x, start : start + 2 * TILE, :] = value.astype(BF16)


def spread_pair(first, second):
    nothing = jnp.zeros_like(first)
    upper = jnp.concatenate([first, nothing], axis=1)
    lower = jnp.concatenate([nothing, second], axis=1)
    return jnp.concatenate([upper, lower], axis=0)


def low_half(shape):
    return lax.broadcasted_iota(jnp.int32, shape, 1) < shape[1] // 2


def mix_kernel(per, samples, arrived, weights, line, line_back, spec_in, message, held):
    rows = 2 * samples
    lanes = 2 * weights.shape[1]
    low = low_half((samples, lanes))
    flat = arrived[...].reshape(-1, arrived.shape[2])
    spectra = dot(line[...], flat).astype(BF16)
    spec_in[...] = spectra
    for q in range(MX):
        for first in range(0, per, 2):
            block = spread_pair(weights[first * MX + q], weights[(first + 1) * MX + q])
            place = first // 2 * lanes
            terms = dot(spectra[q * rows : (q + 1) * rows, place : place + lanes], block)
            mixed = []
            for side in range(2):
                part = terms[:, side * lanes : (side + 1) * lanes]
                turned = pltpu.roll(part[samples:], lanes // 2, 1)
                mixed.append(part[:samples] + jnp.where(low, -turned, turned))
            real = jnp.where(low, mixed[0], pltpu.roll(mixed[1], lanes // 2, 1))
            imag = jnp.where(low, pltpu.roll(mixed[0], lanes // 2, 1), mixed[1])
            held[q * rows : (q + 1) * rows, place : place + lanes] = jnp.concatenate(
                [real, imag], axis=0
            ).astype(BF16)
    message[...] = dot(line_back[...], held[...]).astype(BF16).reshape(message.shape)


def mix_back_kernel(per, samples, arrived, weights, line, line_back, pairs, message, held):
    rows = 2 * samples
    lanes = 2 * weights.shape[1]
    low = low_half((samples, lanes))
    flat = arrived[...].reshape(-1, arrived.shape[2])
    spectra = dot(line[...], flat).astype(BF16).astype(F32)
    for q in range(MX):
        for first in range(0, per, 2):
            block = spread_pair(weights[first * MX + q], weights[(first + 1) * MX + q])
            place = first // 2 * lanes
            real = spectra[q * rows : q * rows + samples, place : place + lanes]
            imag = spectra[q * rows + samples : (q + 1) * rows, place : place + lanes]
            real_turned = pltpu.roll(real, lanes // 2, 1)
            imag_turned = pltpu.roll(imag, lanes // 2, 1)
            left = [jnp.where(low, real, imag_turned), jnp.where(low, imag, -real_turned)]
            right = [jnp.where(low, real_turned, imag), jnp.where(low, imag_turned, -real)]
            pair = jnp.concatenate(
                [jnp.concatenate(left, axis=0), jnp.concatenate(right, axis=0)], axis=1
            ).astype(BF16)
            pairs[q * rows : (q + 1) * rows, 2 * place : 2 * (place + lanes)] = pair
            held[q * rows : (q + 1) * rows, place : place + lanes] = lax.dot_general(
                pair, block, (((1,), (1,)), ((), ())), preferred_element_type=F32
            ).astype(BF16)
    message[...] = dot(line_back[...], held[...]).astype(BF16).reshape(message.shape)


def weight_kernel(per, samples, spec_in, pairs, out):
    rows = 2 * samples
    lanes = out.shape[2]
    half = lanes // 2
    for q in range(MX):
        for first in range(0, per, 2):
            place = first // 2 * lanes
            left = spec_in[q * rows : (q + 1) * rows, place : place + lanes]
            right = pairs[q * rows : (q + 1) * rows, 2 * place : 2 * (place + lanes)]
            outer = lax.dot_general(
                left, right, (((0,), (0,)), ((), ())), preferred_element_type=F32
            )
            out[first * MX + q] = outer[:half, :lanes]
            out[(first + 1) * MX + q] = outer[half:, lanes:]


def whole(array):
    return pl.BlockSpec(array.shape, lambda *step: (0,) * len(array.shape))


def shaped(shape, dtype):
    return jax.ShapeDtypeStruct(shape, dtype)


def params(mib):
    return pltpu.CompilerParams(vmem_limit_bytes=mib * MIB)


def cost(flops, moved, steep=0):
    return pl.CostEstimate(flops=flops, bytes_accessed=moved, transcendentals=steep)


def body(mesh_axes, devices, slabs, activations, cotangent, mode_weights, pointwise, offsets):
    _, channels, width, rows_y, rows_z = activations.shape
    samples = devices // slabs
    per = MY * MZ // devices
    groups = channels // GROUP
    field = activations.shape[1:]
    count = math.prod(field)
    base = z_base(rows_z)
    ytab = y_table(rows_y, width)
    line_fwd, line_inv = x_tables(samples, slabs, NX)
    weight = np.where(np.arange(MZ) == 0, 1.0, 2.0) / (rows_y * rows_z)
    scale = np.tile(np.repeat(weight, GROUP), groups).astype(np.float32)[None]
    base_t, ytab_t = (np.ascontiguousarray(t.T) for t in (base, ytab))
    fwd_t, inv_t = (np.ascontiguousarray(t.T) for t in (line_fwd, line_inv))
    message = shaped((devices, 2 * width, per * channels), BF16)
    spectra = shaped((MX * 2 * samples, per * channels), BF16)
    ztab = pltpu.VMEM((GROUP * rows_z, 2 * MZ * GROUP), BF16)
    ztab_t = pltpu.VMEM((2 * MZ * GROUP, GROUP * rows_z), BF16)
    order = pltpu.VMEM((MZ * channels, MZ * channels), BF16)
    held_plane = pltpu.VMEM((groups, MY * width * 2, MZ * GROUP), BF16)
    held_lines = pltpu.VMEM((groups, width * rows_y, 2 * MZ * GROUP), BF16)
    buffer = pltpu.VMEM(field, BF16)
    sums = pltpu.VMEM((width * rows_y, 2 * rows_z), F32)
    sems = pltpu.SemaphoreType.DMA((groups,))
    far = pl.BlockSpec(memory_space=pltpu.HBM)
    plane_flops = 2 * count * 2 * MZ * GROUP

    def exchange(array):
        return lax.all_to_all(array, mesh_axes, split_axis=0, concat_axis=0, tiled=True)

    def mix_points(values, turned, shifts):
        step = 2
        block = pl.BlockSpec((channels, step, rows_y, rows_z), lambda x: (0, x, 0, 0))
        kernel = functools.partial(pointwise_kernel, turned)
        specs = [block, whole(pointwise)]
        operands = [values, pointwise]
        if shifts is None:
            run = lambda a, b, *rest: kernel(a, b, None, *rest)
        else:
            run = kernel
            specs.append(pl.BlockSpec(memory_space=pltpu.SMEM))
            operands.append(shifts)
        return pl.pallas_call(
            run,
            grid=(width // step,),
            in_specs=specs,
            out_specs=block,
            out_shape=shaped(field, BF16),
            scratch_shapes=[
                pltpu.VMEM((channels * TILE, channels * TILE), BF16),
                pltpu.VMEM((channels, 1, rows_z), F32),
            ],
            compiler_params=params(55),
            cost_estimate=cost(2 * count * channels * TILE, 4 * count),
        )(*operands)

    planes = pl.pallas_call(
        functools.partial(plane_kernel, per, channels),
        in_specs=[far, whole(base), whole(ytab)],
        out_specs=whole(message),
        out_shape=message,
        scratch_shapes=[ztab, order, held_plane, buffer, sems],
        compiler_params=params(55),
        cost_estimate=cost(plane_flops, 2 * count),
    )(activations, base, ytab)
    arrived = exchange(planes)
    local = mix_points(activations.reshape(field), True, offsets)
    arrived, local = lax.optimization_barrier((arrived, local))
    spec_in, mixed = pl.pallas_call(
        functools.partial(mix_kernel, per, samples),
        out_shape=(spectra, message),
        scratch_shapes=[pltpu.VMEM(spectra.shape, BF16)],
        compiler_params=params(16),
        cost_estimate=cost(10**8, 2 * mode_weights.size),
    )(arrived, mode_weights, line_fwd, inv_t)
    returned = exchange(mixed)
    slope, back_plane = pl.pallas_call(
        functools.partial(slope_kernel, per, channels),
        in_specs=[whole(message), far, far]
        + [whole(t) for t in (base, base_t, ytab, ytab_t, scale)],
        out_specs=(far, whole(message)),
        out_shape=(shaped(field, BF16), message),
        scratch_shapes=[ztab, ztab_t, order, held_lines, held_plane]
        + [buffer] * 3
        + [sums] * 2
        + [sems] * 3,
        compiler_params=params(55),
        cost_estimate=cost(2 * plane_flops, 6 * count, 2 * count),
    )(returned, local, cotangent, base, base_t, ytab, ytab_t, scale)
    arrived_back = exchange(back_plane)
    local_back = mix_points(slope, False, None)
    arrived_back, local_back = lax.optimization_barrier((arrived_back, local_back))
    pairs, mixed_back = pl.pallas_call(
        functools.partial(mix_back_kernel, per, samples),
        out_shape=(shaped((spectra.shape[0], 2 * spectra.shape[1]), BF16), message),
        scratch_shapes=[pltpu.VMEM(spectra.shape, BF16)],
        compiler_params=params(16),
        cost_estimate=cost(10**8, 2 * mode_weights.size),
    )(arrived_back, mode_weights, line_inv, fwd_t)
    returned_back = exchange(mixed_back)
    grad_spectral = pl.pallas_call(
        functools.partial(weight_kernel, per, samples),
        out_shape=shaped(mode_weights.shape, F32),
        compiler_params=params(16),
        cost_estimate=cost(10**8, 4 * mode_weights.size),
    )(spec_in, pairs)
    grad_in = pl.pallas_call(
        functools.partial(field_kernel, per, channels),
        in_specs=[whole(message), far, whole(base_t), whole(ytab_t)],
        out_specs=far,
        out_shape=shaped(activations.shape, BF16),
        scratch_shapes=[ztab_t, order, held_lines, buffer, buffer, sems, sems],
        compiler_params=params(55),
        cost_estimate=cost(plane_flops, 4 * count),
    )(returned_back, local_back, base_t, ytab_t)
    return (grad_in, grad_spectral)


def chosen_body(mesh_axes, devices, slabs, activations, cotangent, mode_weights, pointwise, offsets):
    samples, channels, width, rows_y, rows_z = activations.shape
    per = MY * MZ // devices
    fits = (
        samples == 1
        and MY * MZ % devices == 0
        and per in (2, 4, 8)
        and width % 8 == 0
        and channels == 64
        and rows_y % TILE == 0
        and rows_z == 128
    )
    plan = functools.partial(body, mesh_axes, devices, slabs) if fits else general_body
    return plan(activations, cotangent, mode_weights, pointwise, offsets)


def solution(mesh):
    slabs = mesh.shape["space"]
    devices = slabs * mesh.shape["dp"]
    return jax.shard_map(
        functools.partial(chosen_body, ("space", "dp"), devices, slabs),
        mesh=mesh,
        in_specs=(
            P("dp", None, "space", None, None),
            P("dp", None, "space", None, None),
            P(("space", "dp"), None, None),
            P(),
            P(),
        ),
        out_specs=(P("dp", None, "space", None, None), P(("space", "dp"), None, None)),
        check_vma=False,
    )
```

```python
import functools
import math

import jax
import jax.numpy as jnp
import ml_dtypes
import numpy as np
from jax import lax
from jax.experimental import pallas as pl
from jax.experimental.pallas import tpu as pltpu
from jax.sharding import PartitionSpec as P

MX = 16
MY = 16
MZ = 8
NX = 32


def centered(count):
    index = jnp.arange(count, dtype=jnp.int32)
    return jnp.where(index < count // 2, index, index - count)


def plane_tables(rows_y, rows_z, modes_y, modes_z):
    along_y = jnp.arange(rows_y, dtype=jnp.int32)[:, None, None, None]
    along_z = jnp.arange(rows_z, dtype=jnp.int32)[None, :, None, None]
    freq_y = centered(modes_y)[None, None, :, None]
    freq_z = jnp.arange(modes_z, dtype=jnp.int32)[None, None, None, :]
    phase = jnp.mod(freq_y * along_y * rows_z + freq_z * along_z * rows_y, rows_y * rows_z)
    theta = phase.astype(jnp.float32) * (2.0 * math.pi / (rows_y * rows_z))
    cosine = jnp.cos(theta)
    sine = jnp.sin(theta)
    forward = jnp.stack([cosine, -sine], -1).reshape(rows_y * rows_z, modes_y * modes_z * 2)
    scaled = jnp.where(freq_z == 0, 1.0, 2.0).astype(jnp.float32) / (rows_y * rows_z)
    inverse = (
        jnp.stack([cosine * scaled, -sine * scaled], -1)
        .reshape(rows_y * rows_z, modes_y * modes_z * 2)
        .T
    )
    return (forward.astype(jnp.bfloat16), inverse.astype(jnp.bfloat16))


def line_tables(length, modes):
    along = jnp.arange(length, dtype=jnp.int32)[:, None]
    freq = centered(modes)[None, :]
    phase = jnp.mod(freq * along, length)
    theta = phase.astype(jnp.float32) * (2.0 * math.pi / length)
    cosine = jnp.cos(theta)
    sine = jnp.sin(theta)
    first = jnp.stack([cosine, -sine], -1)
    second = jnp.stack([sine, cosine], -1)
    forward = jnp.stack([first, second], 1).reshape(2 * length, 2 * modes)
    inv_first = jnp.stack([cosine.T, sine.T], -1) / length
    inv_second = jnp.stack([-sine.T, cosine.T], -1) / length
    inverse = jnp.stack([inv_first, inv_second], 1).reshape(2 * modes, 2 * length)
    return (forward.astype(jnp.bfloat16), inverse.astype(jnp.bfloat16))


def expand_weights(weights):
    half = weights.shape[1]
    real_part = weights[:, :, :half]
    imag_part = weights[:, :, half:]
    upper = jnp.concatenate([real_part, imag_part], axis=2)
    lower = jnp.concatenate([-imag_part, real_part], axis=2)
    return jnp.concatenate([upper, lower], axis=1)


def outer_sum(left, right):
    return jnp.einsum("mbi,mbo->mio", left, right, preferred_element_type=jnp.float32)


def weight_terms(spec_in, spec_grad):
    half = spec_in.shape[2] // 2
    in_real = spec_in[:, :, :half]
    in_imag = spec_in[:, :, half:]
    gr_real = spec_grad[:, :, :half]
    gr_imag = spec_grad[:, :, half:]
    real_term = outer_sum(in_real, gr_real) + outer_sum(in_imag, gr_imag)
    imag_term = outer_sum(in_real, gr_imag) - outer_sum(in_imag, gr_real)
    return jnp.concatenate([real_term, imag_term], axis=2)


def to_modes(slab, table, modes_x):
    samples, channels, width, pairs = slab.shape
    moved = lax.all_to_all(slab, "space", split_axis=3, concat_axis=2, tiled=True)
    length = moved.shape[2]
    local = moved.shape[3] // 2
    lines = moved.reshape(samples, channels, length, local, 2).transpose(0, 1, 3, 2, 4)
    lines = lines.reshape(samples, channels, local, 2 * length)
    spectra = jnp.dot(lines, table, preferred_element_type=jnp.float32).astype(jnp.bfloat16)
    spectra = spectra.reshape(samples, channels, local, modes_x, 2).transpose(2, 3, 0, 4, 1)
    return spectra.reshape(local * modes_x, samples, 2 * channels)


def to_slab(spectra, table, modes_x, channels):
    count, samples, doubled = spectra.shape
    local = count // modes_x
    lines = spectra.reshape(local, modes_x, samples, 2, channels).transpose(2, 4, 0, 1, 3)
    lines = lines.reshape(samples, channels, local, 2 * modes_x)
    lines = jnp.dot(lines, table, preferred_element_type=jnp.float32).astype(jnp.bfloat16)
    length = lines.shape[3] // 2
    lines = lines.reshape(samples, channels, local, length, 2).transpose(0, 1, 3, 2, 4)
    lines = lines.reshape(samples, channels, length, 2 * local)
    return lax.all_to_all(lines, "space", split_axis=2, concat_axis=3, tiled=True)


def to_owners(spectra):
    return lax.all_to_all(spectra, "dp", split_axis=0, concat_axis=1, tiled=True)


def from_owners(spectra):
    return lax.all_to_all(spectra, "dp", split_axis=1, concat_axis=0, tiled=True)


def gelu_slope(value):
    cdf = 0.5 * (1.0 + lax.erf(value * 0.7071067811865476))
    density = jnp.exp(-0.5 * value * value) * 0.3989422804014327
    return cdf + value * density


def general_body(activations, cotangent, mode_weights, pointwise, offsets):
    samples, channels, width, rows_y, rows_z = activations.shape
    plane_fwd, plane_inv = plane_tables(rows_y, rows_z, MY, MZ)
    line_fwd, line_inv = line_tables(NX, MX)
    flat = activations.reshape(samples, channels, width, rows_y * rows_z)
    planes = jnp.dot(flat, plane_fwd, preferred_element_type=jnp.float32).astype(jnp.bfloat16)
    spec_in = to_modes(planes, line_fwd, MX)
    blocks = expand_weights(mode_weights)
    held_in = to_owners(spec_in)
    held_out = jnp.einsum(
        "mbi,mio->mbo", held_in, blocks, preferred_element_type=jnp.float32
    ).astype(jnp.bfloat16)
    spec_out = from_owners(held_out)
    returned = to_slab(spec_out, line_inv, MX, channels)
    spectral = jnp.dot(returned, plane_inv, preferred_element_type=jnp.float32)
    local_part = jnp.einsum("io,bixn->boxn", pointwise, flat, preferred_element_type=jnp.float32)
    summed = spectral + local_part + offsets[None, :, None, None]
    upstream = cotangent.reshape(flat.shape).astype(jnp.float32)
    slope_grad = (upstream * gelu_slope(summed)).astype(jnp.bfloat16)
    back_plane = jnp.dot(slope_grad, plane_inv.T, preferred_element_type=jnp.float32).astype(
        jnp.bfloat16
    )
    spec_grad = to_modes(back_plane, line_inv.T, MX)
    held_grad = to_owners(spec_grad)
    held_dx = jnp.einsum(
        "mbo,mio->mbi", held_grad, blocks, preferred_element_type=jnp.float32
    ).astype(jnp.bfloat16)
    spec_dx = from_owners(held_dx)
    grad_spectral = weight_terms(held_in, held_grad)
    line_dx = to_slab(spec_dx, line_fwd.T, MX, channels)
    total = jnp.dot(line_dx, plane_fwd.T, preferred_element_type=jnp.float32)
    total = total + jnp.einsum(
        "io,boxn->bixn", pointwise, slope_grad, preferred_element_type=jnp.float32
    )
    grad_in = total.astype(jnp.bfloat16).reshape(activations.shape)
    return (grad_in, grad_spectral)


BF16 = jnp.bfloat16
F32 = jnp.float32
GROUP = 16
TILE = 8
MIB = 1024 * 1024


def rounded(table):
    return np.asarray(table, np.float32).astype(ml_dtypes.bfloat16)


def angles(freq, points, length):
    phase = np.mod(np.outer(freq, points), length)
    return (phase * (2.0 * math.pi / length)).astype(np.float64)


def signed(count):
    index = np.arange(count)
    return np.where(index < count // 2, index, index - count)


def z_base(rows_z):
    theta = angles(np.arange(MZ), np.arange(rows_z), rows_z)
    pair = np.stack([np.cos(theta), -np.sin(theta)])
    table = np.repeat(pair.reshape(2 * MZ, rows_z), GROUP, axis=0).T
    return rounded(table).astype(np.float32)


def y_table(rows_y, width):
    theta = angles(signed(MY), np.arange(rows_y), rows_y)
    cosine, sine = np.cos(theta), np.sin(theta)
    turn = np.stack([np.stack([cosine, sine]), np.stack([-sine, cosine])])
    table = np.einsum("rsjy,xw->jxrswy", turn, np.eye(width))
    return rounded(table.reshape(MY * width * 2, 2 * width * rows_y))


def x_tables(samples, slabs, length):
    theta = angles(signed(MX), np.arange(length), length)
    cosine, sine = np.cos(theta), np.sin(theta)
    forward = np.stack([np.stack([cosine, sine]), np.stack([-sine, cosine])])
    inverse = np.stack([np.stack([cosine, sine]), np.stack([-sine, cosine])]) / length
    same = np.eye(samples)
    rows = MX * 2 * samples

    def lay(turn):
        turn = turn.reshape(2, 2, MX, slabs, length // slabs)
        table = np.einsum("arqsx,bd->qabsdxr", turn, same)
        return rounded(table.reshape(rows, samples * length * 2))

    return lay(forward), lay(inverse)


def dot(left, right):
    return jnp.dot(left, right, preferred_element_type=F32)


def gelu_slope_rows(value):
    decay = jnp.exp2(value * value * (-0.5 * math.log2(math.e))).astype(BF16)
    value = value.astype(BF16)

    def number(x):
        return jnp.asarray(x, BF16)

    size = jnp.abs(value)
    t = pl.reciprocal(number(1.0) + number(0.3275911 * math.sqrt(0.5)) * size, approx=True)
    tail = number(0.5 * 1.061405429) * t - number(0.5 * 1.453152027)
    tail = tail * t + number(0.5 * 1.421413741)
    tail = tail * t - number(0.5 * 0.284496736)
    tail = tail * t + number(0.5 * 0.254829592)
    part = (size * number(1.0 / math.sqrt(2.0 * math.pi)) - tail * t) * decay
    return jnp.where(value >= number(0.0), number(1.0) + part, -part)


def fill_z(base, table):
    rows_z, lanes = base.shape
    owner = lax.broadcasted_iota(jnp.int32, (rows_z, lanes), 1) % GROUP
    values = base[...]
    for c in range(GROUP):
        table[c * rows_z : (c + 1) * rows_z] = jnp.where(owner == c, values, 0.0).astype(BF16)


def fill_z_back(base, table):
    lanes, rows_z = base.shape
    owner = lax.broadcasted_iota(jnp.int32, (lanes, rows_z), 0) % GROUP
    values = base[...]
    for c in range(GROUP):
        table[:, c * rows_z : (c + 1) * rows_z] = jnp.where(owner == c, values, 0.0).astype(BF16)


def grouped(lane, per, channels):
    c = lane % channels
    return c // GROUP * (MZ * GROUP) + lane // channels * GROUP + c % GROUP


def fill_order(per, channels, back, table):
    count = table.shape[0]
    row = lax.broadcasted_iota(jnp.int32, (count, count), 0)
    column = lax.broadcasted_iota(jnp.int32, (count, count), 1)
    if back:
        same = grouped(row[:, :1], per, channels) == column
    else:
        same = row == grouped(column[:1], per, channels)
    table[...] = jnp.where(same, 1.0, 0.0).astype(BF16)


def analyse(field, ztab, ytab):
    middle = len(field) // 2
    depth = ztab.shape[0] // 2
    spectra = dot(jnp.concatenate(field[:middle], axis=1), ztab[:depth])
    spectra = (spectra + dot(jnp.concatenate(field[middle:], axis=1), ztab[depth:])).astype(BF16)
    half = spectra.shape[1] // 2
    return dot(ytab, jnp.concatenate([spectra[:, :half], spectra[:, half:]], axis=0))


def deliver(held, order, message, per, channels):
    joined = jnp.concatenate([held[g] for g in range(held.shape[0])], axis=1)
    ordered = dot(joined, order[...]).astype(BF16)
    parts = MZ // per
    rows = message.shape[1]
    lanes = per * channels
    for part in range(parts):
        block = ordered[:, part * lanes : (part + 1) * lanes]
        for j in range(MY):
            message[j * parts + part] = block[j * rows : (j + 1) * rows]


def receive(message, order_back, ytab_back, scale, held, per):
    parts = MZ // per
    blocks = message[...]
    blocks = blocks.reshape(MY, parts, *blocks.shape[1:])
    lanes = [blocks[:, part].reshape(-1, blocks.shape[3]) for part in range(parts)]
    ordered = dot(jnp.concatenate(lanes, axis=1), order_back[...]).astype(BF16)
    lines = dot(ytab_back[...], ordered)
    if scale is not None:
        lines = lines * scale[...]
    lines = lines.astype(BF16)
    rows = lines.shape[0] // 2
    wide = MZ * GROUP
    for group in range(held.shape[0]):
        piece = lines[:, group * wide : (group + 1) * wide]
        held[group] = jnp.concatenate([piece[:rows], piece[rows:]], axis=1)


def move(source, target, sems, g):
    run = pl.ds(g * GROUP, GROUP)
    return pltpu.make_async_copy(source.at[run], target.at[run], sems.at[g])


def plane_kernel(per, channels, field, base, ytab, message, ztab, order, held, buffer, sems):
    groups = held.shape[0]
    rows_z = field.shape[-1]
    move(field.at[0], buffer, sems, 0).start()
    fill_z(base, ztab)
    move(field.at[0], buffer, sems, 1).start()
    fill_order(per, channels, False, order)

    @pl.loop(0, groups)
    def _(g):
        move(field.at[0], buffer, sems, g).wait()

        @pl.when(g + 2 < groups)
        def _():
            move(field.at[0], buffer, sems, g + 2).start()

        blocks = [buffer[g * GROUP + c].reshape(-1, rows_z) for c in range(GROUP)]
        held[g] = analyse(blocks, ztab[...], ytab[...]).astype(BF16)

    deliver(held, order, message, per, channels)


def slope_kernel(
    per, channels, arrived, local, cotangent, base, base_back, ytab, ytab_back, scale,
    slope, message, ztab, ztab_back, order, held, back, local_in, cotangent_in, result, first_sum, second_sum,
    local_sems, cotangent_sems, result_sems,
):
    groups = held.shape[0]
    width, rows_y, rows_z = local.shape[1:]

    def fetch(g):
        move(local, local_in, local_sems, g).start()
        move(cotangent.at[0], cotangent_in, cotangent_sems, g).start()

    fetch(0)
    fill_order(per, channels, True, order)
    receive(arrived, order, ytab_back, scale, held, per)
    fetch(1)
    fill_z_back(base_back, ztab_back)
    fill_z(base, ztab)
    fill_order(per, channels, False, order)
    wide = 2 * rows_y

    @pl.loop(0, groups)
    def _(g):
        move(local, local_in, local_sems, g).wait()
        move(cotangent.at[0], cotangent_in, cotangent_sems, g).wait()

        @pl.when(g + 2 < groups)
        def _():
            fetch(g + 2)

        lines = held[g]
        for first in range(0, GROUP, 2):
            total = first_sum if first % 4 else second_sum
            total[...] = dot(lines, ztab_back[:, first * rows_z : (first + 2) * rows_z])
            for offset in range(2):
                c = g * GROUP + first + offset
                for x in range(0, width, 2):
                    value = total[x * rows_y : x * rows_y + wide, offset * rows_z : (offset + 1) * rows_z]
                    value = value + local_in[c, x : x + 2].reshape(wide, rows_z).astype(F32)
                    upstream = cotangent_in[c, x : x + 2].reshape(wide, rows_z)
                    answer = upstream * gelu_slope_rows(value)
                    result[c, x : x + 2] = answer.reshape(2, rows_y, rows_z)
        move(result, slope, result_sems, g).start()
        blocks = [result[g * GROUP + c].reshape(-1, rows_z) for c in range(GROUP)]
        plane = analyse(blocks, ztab[...], ytab[...]) * scale[:, : MZ * GROUP]
        back[g] = plane.astype(BF16)

    deliver(back, order, message, per, channels)
    for g in range(groups):
        move(result, slope, result_sems, g).wait()


def field_kernel(
    per, channels, arrived, local, base_back, ytab_back, out, ztab_back, order, held, local_in, result,
    local_sems, result_sems,
):
    groups = held.shape[0]
    width, rows_y, rows_z = local.shape[1:]
    move(local, local_in, local_sems, 0).start()
    fill_order(per, channels, True, order)
    receive(arrived, order, ytab_back, None, held, per)
    move(local, local_in, local_sems, 1).start()
    fill_z_back(base_back, ztab_back)

    @pl.loop(0, groups)
    def _(g):
        move(local, local_in, local_sems, g).wait()

        @pl.when(g + 2 < groups)
        def _():
            move(local, local_in, local_sems, g + 2).start()

        lines = held[g]
        for first in range(0, GROUP, 2):
            total = dot(lines, ztab_back[:, first * rows_z : (first + 2) * rows_z])
            for offset in range(2):
                c = g * GROUP + first + offset
                value = total[:, offset * rows_z : (offset + 1) * rows_z]
                value = value + local_in[c].reshape(-1, rows_z).astype(F32)
                result[c] = value.astype(BF16).reshape(width, rows_y, rows_z)
        move(result, out.at[0], result_sems, g).start()

    for g in range(groups):
        move(result, out.at[0], result_sems, g).wait()


def pointwise_kernel(turned, field, mix, offsets, out, table, shift):
    channels = mix.shape[0]
    width, rows_y, rows_z = field.shape[1:]
    size = channels * TILE

    @pl.when(pl.program_id(0) == 0)
    def _():
        row = lax.broadcasted_iota(jnp.int32, (size, channels), 0) // TILE
        column = lax.broadcasted_iota(jnp.int32, (size, channels), 1)
        spread = jnp.where(row == column, 1.0, 0.0).astype(BF16)
        tall = lax.dot_general(
            spread, mix[...], (((1,), (1 if turned else 0,)), ((), ())), preferred_element_type=F32
        ).astype(BF16)
        whole = lax.dot_general(
            tall, spread, (((1,), (1,)), ((), ())), preferred_element_type=F32
        )
        place = lax.broadcasted_iota(jnp.int32, (size, size), 0) % TILE
        other = lax.broadcasted_iota(jnp.int32, (size, size), 1) % TILE
        table[...] = jnp.where(place == other, whole, 0.0).astype(BF16)
        if offsets is not None:
            for c in range(channels):
                shift[c] = jnp.full((1, rows_z), offsets[c], F32)

    for start in range(0, rows_y, 2 * TILE):
        pieces = [field[:, x, start : start + 2 * TILE, :].astype(F32) for x in range(width)]
        halves = []
        for row in range(0, 2 * TILE, TILE):
            rows = [piece[:, row : row + TILE].reshape(size, rows_z).astype(BF16) for piece in pieces]
            halves.append(dot(table[...], jnp.concatenate(rows, axis=1)))
        for x in range(width):
            values = [
                half[:, x * rows_z : (x + 1) * rows_z].reshape(channels, TILE, rows_z) for half in halves
            ]
            value = jnp.concatenate(values, axis=1)
            if offsets is not None:
                value = value + shift[...]
            out[:, x, start : start + 2 * TILE, :] = value.astype(BF16)


def spread_pair(first, second):
    nothing = jnp.zeros_like(first)
    upper = jnp.concatenate([first, nothing], axis=1)
    lower = jnp.concatenate([nothing, second], axis=1)
    return jnp.concatenate([upper, lower], axis=0)


def low_half(shape):
    return lax.broadcasted_iota(jnp.int32, shape, 1) < shape[1] // 2


def mix_kernel(per, samples, arrived, weights, line, line_back, spec_in, message, held):
    rows = 2 * samples
    lanes = 2 * weights.shape[1]
    low = low_half((samples, lanes))
    flat = arrived[...].reshape(-1, arrived.shape[2])
    spectra = dot(line[...], flat).astype(BF16)
    spec_in[...] = spectra
    for q in range(MX):
        for first in range(0, per, 2):
            block = spread_pair(weights[first * MX + q], weights[(first + 1) * MX + q])
            place = first // 2 * lanes
            terms = dot(spectra[q * rows : (q + 1) * rows, place : place + lanes], block)
            mixed = []
            for side in range(2):
                part = terms[:, side * lanes : (side + 1) * lanes]
                turned = pltpu.roll(part[samples:], lanes // 2, 1)
                mixed.append(part[:samples] + jnp.where(low, -turned, turned))
            real = jnp.where(low, mixed[0], pltpu.roll(mixed[1], lanes // 2, 1))
            imag = jnp.where(low, pltpu.roll(mixed[0], lanes // 2, 1), mixed[1])
            held[q * rows : (q + 1) * rows, place : place + lanes] = jnp.concatenate(
                [real, imag], axis=0
            ).astype(BF16)
    message[...] = dot(line_back[...], held[...]).astype(BF16).reshape(message.shape)


def mix_back_kernel(per, samples, arrived, weights, line, line_back, pairs, message, held):
    rows = 2 * samples
    lanes = 2 * weights.shape[1]
    low = low_half((samples, lanes))
    flat = arrived[...].reshape(-1, arrived.shape[2])
    spectra = dot(line[...], flat).astype(BF16).astype(F32)
    for q in range(MX):
        for first in range(0, per, 2):
            block = spread_pair(weights[first * MX + q], weights[(first + 1) * MX + q])
            place = first // 2 * lanes
            real = spectra[q * rows : q * rows + samples, place : place + lanes]
            imag = spectra[q * rows + samples : (q + 1) * rows, place : place + lanes]
            real_turned = pltpu.roll(real, lanes // 2, 1)
            imag_turned = pltpu.roll(imag, lanes // 2, 1)
            left = [jnp.where(low, real, imag_turned), jnp.where(low, imag, -real_turned)]
            right = [jnp.where(low, real_turned, imag), jnp.where(low, imag_turned, -real)]
            pair = jnp.concatenate(
                [jnp.concatenate(left, axis=0), jnp.concatenate(right, axis=0)], axis=1
            ).astype(BF16)
            pairs[q * rows : (q + 1) * rows, 2 * place : 2 * (place + lanes)] = pair
            held[q * rows : (q + 1) * rows, place : place + lanes] = lax.dot_general(
                pair, block, (((1,), (1,)), ((), ())), preferred_element_type=F32
            ).astype(BF16)
    message[...] = dot(line_back[...], held[...]).astype(BF16).reshape(message.shape)


def weight_kernel(per, samples, spec_in, pairs, out):
    rows = 2 * samples
    lanes = out.shape[2]
    half = lanes // 2
    for q in range(MX):
        for first in range(0, per, 2):
            place = first // 2 * lanes
            left = spec_in[q * rows : (q + 1) * rows, place : place + lanes]
            right = pairs[q * rows : (q + 1) * rows, 2 * place : 2 * (place + lanes)]
            outer = lax.dot_general(
                left, right, (((0,), (0,)), ((), ())), preferred_element_type=F32
            )
            out[first * MX + q] = outer[:half, :lanes]
            out[(first + 1) * MX + q] = outer[half:, lanes:]


def whole(array):
    return pl.BlockSpec(array.shape, lambda *step: (0,) * len(array.shape))


def shaped(shape, dtype):
    return jax.ShapeDtypeStruct(shape, dtype)


def params(mib):
    return pltpu.CompilerParams(vmem_limit_bytes=mib * MIB)


def cost(flops, moved, steep=0):
    return pl.CostEstimate(flops=flops, bytes_accessed=moved, transcendentals=steep)


def body(mesh_axes, devices, slabs, activations, cotangent, mode_weights, pointwise, offsets):
    _, channels, width, rows_y, rows_z = activations.shape
    samples = devices // slabs
    per = MY * MZ // devices
    groups = channels // GROUP
    field = activations.shape[1:]
    count = math.prod(field)
    base = z_base(rows_z)
    ytab = y_table(rows_y, width)
    line_fwd, line_inv = x_tables(samples, slabs, NX)
    weight = np.where(np.arange(MZ) == 0, 1.0, 2.0) / (rows_y * rows_z)
    scale = np.tile(np.repeat(weight, GROUP), groups).astype(np.float32)[None]
    base_t, ytab_t = (np.ascontiguousarray(t.T) for t in (base, ytab))
    fwd_t, inv_t = (np.ascontiguousarray(t.T) for t in (line_fwd, line_inv))
    message = shaped((devices, 2 * width, per * channels), BF16)
    spectra = shaped((MX * 2 * samples, per * channels), BF16)
    ztab = pltpu.VMEM((GROUP * rows_z, 2 * MZ * GROUP), BF16)
    ztab_t = pltpu.VMEM((2 * MZ * GROUP, GROUP * rows_z), BF16)
    order = pltpu.VMEM((MZ * channels, MZ * channels), BF16)
    held_plane = pltpu.VMEM((groups, MY * width * 2, MZ * GROUP), BF16)
    held_lines = pltpu.VMEM((groups, width * rows_y, 2 * MZ * GROUP), BF16)
    buffer = pltpu.VMEM(field, BF16)
    sums = pltpu.VMEM((width * rows_y, 2 * rows_z), F32)
    sems = pltpu.SemaphoreType.DMA((groups,))
    far = pl.BlockSpec(memory_space=pltpu.HBM)
    plane_flops = 2 * count * 2 * MZ * GROUP

    def exchange(array):
        return lax.all_to_all(array, mesh_axes, split_axis=0, concat_axis=0, tiled=True)

    def mix_points(values, turned, shifts):
        step = 2
        block = pl.BlockSpec((channels, step, rows_y, rows_z), lambda x: (0, x, 0, 0))
        kernel = functools.partial(pointwise_kernel, turned)
        specs = [block, whole(pointwise)]
        operands = [values, pointwise]
        if shifts is None:
            run = lambda a, b, *rest: kernel(a, b, None, *rest)
        else:
            run = kernel
            specs.append(pl.BlockSpec(memory_space=pltpu.SMEM))
            operands.append(shifts)
        return pl.pallas_call(
            run,
            grid=(width // step,),
            in_specs=specs,
            out_specs=block,
            out_shape=shaped(field, BF16),
            scratch_shapes=[
                pltpu.VMEM((channels * TILE, channels * TILE), BF16),
                pltpu.VMEM((channels, 1, rows_z), F32),
            ],
            compiler_params=params(55),
            cost_estimate=cost(2 * count * channels * TILE, 4 * count),
        )(*operands)

    planes = pl.pallas_call(
        functools.partial(plane_kernel, per, channels),
        in_specs=[far, whole(base), whole(ytab)],
        out_specs=whole(message),
        out_shape=message,
        scratch_shapes=[ztab, order, held_plane, buffer, sems],
        compiler_params=params(55),
        cost_estimate=cost(plane_flops, 2 * count),
    )(activations, base, ytab)
    arrived = exchange(planes)
    local = mix_points(activations.reshape(field), True, offsets)
    arrived, local = lax.optimization_barrier((arrived, local))
    spec_in, mixed = pl.pallas_call(
        functools.partial(mix_kernel, per, samples),
        out_shape=(spectra, message),
        scratch_shapes=[pltpu.VMEM(spectra.shape, BF16)],
        compiler_params=params(16),
        cost_estimate=cost(10**8, 2 * mode_weights.size),
    )(arrived, mode_weights, line_fwd, inv_t)
    returned = exchange(mixed)
    slope, back_plane = pl.pallas_call(
        functools.partial(slope_kernel, per, channels),
        in_specs=[whole(message), far, far]
        + [whole(t) for t in (base, base_t, ytab, ytab_t, scale)],
        out_specs=(far, whole(message)),
        out_shape=(shaped(field, BF16), message),
        scratch_shapes=[ztab, ztab_t, order, held_lines, held_plane]
        + [buffer] * 3
        + [sums] * 2
        + [sems] * 3,
        compiler_params=params(55),
        cost_estimate=cost(2 * plane_flops, 6 * count, 2 * count),
    )(returned, local, cotangent, base, base_t, ytab, ytab_t, scale)
    arrived_back = exchange(back_plane)
    local_back = mix_points(slope, False, None)
    arrived_back, local_back = lax.optimization_barrier((arrived_back, local_back))
    pairs, mixed_back = pl.pallas_call(
        functools.partial(mix_back_kernel, per, samples),
        out_shape=(shaped((spectra.shape[0], 2 * spectra.shape[1]), BF16), message),
        scratch_shapes=[pltpu.VMEM(spectra.shape, BF16)],
        compiler_params=params(16),
        cost_estimate=cost(10**8, 2 * mode_weights.size),
    )(arrived_back, mode_weights, line_inv, fwd_t)
    returned_back = exchange(mixed_back)
    grad_spectral = pl.pallas_call(
        functools.partial(weight_kernel, per, samples),
        out_shape=shaped(mode_weights.shape, F32),
        compiler_params=params(16),
        cost_estimate=cost(10**8, 4 * mode_weights.size),
    )(spec_in, pairs)
    grad_in = pl.pallas_call(
        functools.partial(field_kernel, per, channels),
        in_specs=[whole(message), far, whole(base_t), whole(ytab_t)],
        out_specs=far,
        out_shape=shaped(activations.shape, BF16),
        scratch_shapes=[ztab_t, order, held_lines, buffer, buffer, sems, sems],
        compiler_params=params(55),
        cost_estimate=cost(plane_flops, 4 * count),
    )(returned_back, local_back, base_t, ytab_t)
    return (grad_in, grad_spectral)


def chosen_body(mesh_axes, devices, slabs, activations, cotangent, mode_weights, pointwise, offsets):
    samples, channels, width, rows_y, rows_z = activations.shape
    per = MY * MZ // devices
    fits = (
        samples == 1
        and MY * MZ % devices == 0
        and per in (2, 4, 8)
        and width % 8 == 0
        and channels == 64
        and rows_y % TILE == 0
        and rows_z == 128
    )
    plan = functools.partial(body, mesh_axes, devices, slabs) if fits else general_body
    return plan(activations, cotangent, mode_weights, pointwise, offsets)


def solution(mesh):
    slabs = mesh.shape["space"]
    devices = slabs * mesh.shape["dp"]
    return jax.shard_map(
        functools.partial(chosen_body, ("space", "dp"), devices, slabs),
        mesh=mesh,
        in_specs=(
            P("dp", None, "space", None, None),
            P("dp", None, "space", None, None),
            P(("space", "dp"), None, None),
            P(),
            P(),
        ),
        out_specs=(P("dp", None, "space", None, None), P(("space", "dp"), None, None)),
        check_vma=False,
    )
```

```python
import functools
import math

import jax
import jax.numpy as jnp
import ml_dtypes
import numpy as np
from jax import lax
from jax.experimental import pallas as pl
from jax.experimental.pallas import tpu as pltpu
from jax.sharding import PartitionSpec as P

MX = 16
MY = 16
MZ = 8
NX = 32


def centered(count):
    index = jnp.arange(count, dtype=jnp.int32)
    return jnp.where(index < count // 2, index, index - count)


def plane_tables(rows_y, rows_z, modes_y, modes_z):
    along_y = jnp.arange(rows_y, dtype=jnp.int32)[:, None, None, None]
    along_z = jnp.arange(rows_z, dtype=jnp.int32)[None, :, None, None]
    freq_y = centered(modes_y)[None, None, :, None]
    freq_z = jnp.arange(modes_z, dtype=jnp.int32)[None, None, None, :]
    phase = jnp.mod(freq_y * along_y * rows_z + freq_z * along_z * rows_y, rows_y * rows_z)
    theta = phase.astype(jnp.float32) * (2.0 * math.pi / (rows_y * rows_z))
    cosine = jnp.cos(theta)
    sine = jnp.sin(theta)
    forward = jnp.stack([cosine, -sine], -1).reshape(rows_y * rows_z, modes_y * modes_z * 2)
    scaled = jnp.where(freq_z == 0, 1.0, 2.0).astype(jnp.float32) / (rows_y * rows_z)
    inverse = (
        jnp.stack([cosine * scaled, -sine * scaled], -1)
        .reshape(rows_y * rows_z, modes_y * modes_z * 2)
        .T
    )
    return (forward.astype(jnp.bfloat16), inverse.astype(jnp.bfloat16))


def line_tables(length, modes):
    along = jnp.arange(length, dtype=jnp.int32)[:, None]
    freq = centered(modes)[None, :]
    phase = jnp.mod(freq * along, length)
    theta = phase.astype(jnp.float32) * (2.0 * math.pi / length)
    cosine = jnp.cos(theta)
    sine = jnp.sin(theta)
    first = jnp.stack([cosine, -sine], -1)
    second = jnp.stack([sine, cosine], -1)
    forward = jnp.stack([first, second], 1).reshape(2 * length, 2 * modes)
    inv_first = jnp.stack([cosine.T, sine.T], -1) / length
    inv_second = jnp.stack([-sine.T, cosine.T], -1) / length
    inverse = jnp.stack([inv_first, inv_second], 1).reshape(2 * modes, 2 * length)
    return (forward.astype(jnp.bfloat16), inverse.astype(jnp.bfloat16))


def expand_weights(weights):
    half = weights.shape[1]
    real_part = weights[:, :, :half]
    imag_part = weights[:, :, half:]
    upper = jnp.concatenate([real_part, imag_part], axis=2)
    lower = jnp.concatenate([-imag_part, real_part], axis=2)
    return jnp.concatenate([upper, lower], axis=1)


def outer_sum(left, right):
    return jnp.einsum("mbi,mbo->mio", left, right, preferred_element_type=jnp.float32)


def weight_terms(spec_in, spec_grad):
    half = spec_in.shape[2] // 2
    in_real = spec_in[:, :, :half]
    in_imag = spec_in[:, :, half:]
    gr_real = spec_grad[:, :, :half]
    gr_imag = spec_grad[:, :, half:]
    real_term = outer_sum(in_real, gr_real) + outer_sum(in_imag, gr_imag)
    imag_term = outer_sum(in_real, gr_imag) - outer_sum(in_imag, gr_real)
    return jnp.concatenate([real_term, imag_term], axis=2)


def to_modes(slab, table, modes_x):
    samples, channels, width, pairs = slab.shape
    moved = lax.all_to_all(slab, "space", split_axis=3, concat_axis=2, tiled=True)
    length = moved.shape[2]
    local = moved.shape[3] // 2
    lines = moved.reshape(samples, channels, length, local, 2).transpose(0, 1, 3, 2, 4)
    lines = lines.reshape(samples, channels, local, 2 * length)
    spectra = jnp.dot(lines, table, preferred_element_type=jnp.float32).astype(jnp.bfloat16)
    spectra = spectra.reshape(samples, channels, local, modes_x, 2).transpose(2, 3, 0, 4, 1)
    return spectra.reshape(local * modes_x, samples, 2 * channels)


def to_slab(spectra, table, modes_x, channels):
    count, samples, doubled = spectra.shape
    local = count // modes_x
    lines = spectra.reshape(local, modes_x, samples, 2, channels).transpose(2, 4, 0, 1, 3)
    lines = lines.reshape(samples, channels, local, 2 * modes_x)
    lines = jnp.dot(lines, table, preferred_element_type=jnp.float32).astype(jnp.bfloat16)
    length = lines.shape[3] // 2
    lines = lines.reshape(samples, channels, local, length, 2).transpose(0, 1, 3, 2, 4)
    lines = lines.reshape(samples, channels, length, 2 * local)
    return lax.all_to_all(lines, "space", split_axis=2, concat_axis=3, tiled=True)


def to_owners(spectra):
    return lax.all_to_all(spectra, "dp", split_axis=0, concat_axis=1, tiled=True)


def from_owners(spectra):
    return lax.all_to_all(spectra, "dp", split_axis=1, concat_axis=0, tiled=True)


def gelu_slope(value):
    cdf = 0.5 * (1.0 + lax.erf(value * 0.7071067811865476))
    density = jnp.exp(-0.5 * value * value) * 0.3989422804014327
    return cdf + value * density


def general_body(activations, cotangent, mode_weights, pointwise, offsets):
    samples, channels, width, rows_y, rows_z = activations.shape
    plane_fwd, plane_inv = plane_tables(rows_y, rows_z, MY, MZ)
    line_fwd, line_inv = line_tables(NX, MX)
    flat = activations.reshape(samples, channels, width, rows_y * rows_z)
    planes = jnp.dot(flat, plane_fwd, preferred_element_type=jnp.float32).astype(jnp.bfloat16)
    spec_in = to_modes(planes, line_fwd, MX)
    blocks = expand_weights(mode_weights)
    held_in = to_owners(spec_in)
    held_out = jnp.einsum(
        "mbi,mio->mbo", held_in, blocks, preferred_element_type=jnp.float32
    ).astype(jnp.bfloat16)
    spec_out = from_owners(held_out)
    returned = to_slab(spec_out, line_inv, MX, channels)
    spectral = jnp.dot(returned, plane_inv, preferred_element_type=jnp.float32)
    local_part = jnp.einsum("io,bixn->boxn", pointwise, flat, preferred_element_type=jnp.float32)
    summed = spectral + local_part + offsets[None, :, None, None]
    upstream = cotangent.reshape(flat.shape).astype(jnp.float32)
    slope_grad = (upstream * gelu_slope(summed)).astype(jnp.bfloat16)
    back_plane = jnp.dot(slope_grad, plane_inv.T, preferred_element_type=jnp.float32).astype(
        jnp.bfloat16
    )
    spec_grad = to_modes(back_plane, line_inv.T, MX)
    held_grad = to_owners(spec_grad)
    held_dx = jnp.einsum(
        "mbo,mio->mbi", held_grad, blocks, preferred_element_type=jnp.float32
    ).astype(jnp.bfloat16)
    spec_dx = from_owners(held_dx)
    grad_spectral = weight_terms(held_in, held_grad)
    line_dx = to_slab(spec_dx, line_fwd.T, MX, channels)
    total = jnp.dot(line_dx, plane_fwd.T, preferred_element_type=jnp.float32)
    total = total + jnp.einsum(
        "io,boxn->bixn", pointwise, slope_grad, preferred_element_type=jnp.float32
    )
    grad_in = total.astype(jnp.bfloat16).reshape(activations.shape)
    return (grad_in, grad_spectral)


BF16 = jnp.bfloat16
F32 = jnp.float32
GROUP = 16
TILE = 8
PARTS = 4
MIB = 1024 * 1024


def rounded(table):
    return np.asarray(table, np.float32).astype(ml_dtypes.bfloat16)


def angles(freq, points, length):
    phase = np.mod(np.outer(freq, points), length)
    return (phase * (2.0 * math.pi / length)).astype(np.float64)


def signed(count):
    index = np.arange(count)
    return np.where(index < count // 2, index, index - count)


def z_base(rows_z):
    theta = angles(np.arange(MZ), np.arange(rows_z), rows_z)
    pair = np.stack([np.cos(theta), -np.sin(theta)])
    table = np.repeat(pair.reshape(2 * MZ, rows_z), GROUP, axis=0).T
    return rounded(table).astype(np.float32)


def y_table(rows_y, width):
    theta = angles(signed(MY), np.arange(rows_y), rows_y)
    cosine, sine = np.cos(theta), np.sin(theta)
    turn = np.stack([np.stack([cosine, sine]), np.stack([-sine, cosine])])
    table = np.einsum("rsjy,xw->jxrswy", turn, np.eye(width))
    return rounded(table.reshape(MY * width * 2, 2 * width * rows_y))


def x_tables(samples, slabs, length):
    theta = angles(signed(MX), np.arange(length), length)
    cosine, sine = np.cos(theta), np.sin(theta)
    forward = np.stack([np.stack([cosine, sine]), np.stack([-sine, cosine])])
    inverse = np.stack([np.stack([cosine, sine]), np.stack([-sine, cosine])]) / length
    same = np.eye(samples)
    rows = MX * 2 * samples

    def lay(turn):
        turn = turn.reshape(2, 2, MX, slabs, length // slabs)
        table = np.einsum("arqsx,bd->qabsdxr", turn, same)
        return rounded(table.reshape(rows, samples * length * 2))

    return lay(forward), lay(inverse)


def dot(left, right):
    return jnp.dot(left, right, preferred_element_type=F32)


def gelu_slope_rows(value):
    decay = jnp.exp2(value * value * (-0.5 * math.log2(math.e))).astype(BF16)
    value = value.astype(BF16)

    def number(x):
        return jnp.asarray(x, BF16)

    size = jnp.abs(value)
    t = pl.reciprocal(number(1.0) + number(0.3275911 * math.sqrt(0.5)) * size, approx=True)
    tail = number(0.5 * 1.061405429) * t - number(0.5 * 1.453152027)
    tail = tail * t + number(0.5 * 1.421413741)
    tail = tail * t - number(0.5 * 0.284496736)
    tail = tail * t + number(0.5 * 0.254829592)
    part = (size * number(1.0 / math.sqrt(2.0 * math.pi)) - tail * t) * decay
    return jnp.where(value >= number(0.0), number(1.0) + part, -part)


def fill_z(base, table):
    rows_z, lanes = base.shape
    owner = lax.broadcasted_iota(jnp.int32, (rows_z, lanes), 1) % GROUP
    values = base[...]
    for c in range(GROUP):
        table[c * rows_z : (c + 1) * rows_z] = jnp.where(owner == c, values, 0.0).astype(BF16)


def fill_z_back(base, table):
    lanes, rows_z = base.shape
    owner = lax.broadcasted_iota(jnp.int32, (lanes, rows_z), 0) % GROUP
    values = base[...]
    for c in range(GROUP):
        table[:, c * rows_z : (c + 1) * rows_z] = jnp.where(owner == c, values, 0.0).astype(BF16)


def grouped(lane, per, channels):
    c = lane % channels
    return c // GROUP * (MZ * GROUP) + lane // channels * GROUP + c % GROUP


def fill_order(per, channels, back, table):
    count = table.shape[0]
    row = lax.broadcasted_iota(jnp.int32, (count, count), 0)
    column = lax.broadcasted_iota(jnp.int32, (count, count), 1)
    if back:
        same = grouped(row[:, :1], per, channels) == column
    else:
        same = row == grouped(column[:1], per, channels)
    table[...] = jnp.where(same, 1.0, 0.0).astype(BF16)


def analyse(field, ztab, ytab):
    middle = len(field) // 2
    depth = ztab.shape[0] // 2
    spectra = dot(jnp.concatenate(field[:middle], axis=1), ztab[:depth])
    spectra = (spectra + dot(jnp.concatenate(field[middle:], axis=1), ztab[depth:])).astype(BF16)
    half = spectra.shape[1] // 2
    return dot(ytab, jnp.concatenate([spectra[:, :half], spectra[:, half:]], axis=0))


def deliver(held, order, message, per, channels):
    joined = jnp.concatenate([held[g] for g in range(held.shape[0])], axis=1)
    ordered = dot(joined, order[...]).astype(BF16)
    parts = MZ // per
    rows = message.shape[1]
    lanes = per * channels
    for part in range(parts):
        block = ordered[:, part * lanes : (part + 1) * lanes]
        for j in range(MY):
            message[j * parts + part] = block[j * rows : (j + 1) * rows]


def receive(message, order_back, ytab_back, scale, held, per):
    parts = MZ // per
    blocks = message[...]
    blocks = blocks.reshape(MY, parts, *blocks.shape[1:])
    lanes = [blocks[:, part].reshape(-1, blocks.shape[3]) for part in range(parts)]
    ordered = dot(jnp.concatenate(lanes, axis=1), order_back[...]).astype(BF16)
    lines = dot(ytab_back[...], ordered)
    if scale is not None:
        lines = lines * scale[...]
    lines = lines.astype(BF16)
    rows = lines.shape[0] // 2
    wide = MZ * GROUP
    for group in range(held.shape[0]):
        piece = lines[:, group * wide : (group + 1) * wide]
        held[group] = jnp.concatenate([piece[:rows], piece[rows:]], axis=1)


class Move:
    def __init__(self, source, target, sems):
        self.source, self.target, self.sems = source, target, sems

    def copies(self, g):
        size = GROUP // PARTS
        for part in range(PARTS):
            run = pl.ds(g * GROUP + part * size, size)
            yield pltpu.make_async_copy(self.source.at[run], self.target.at[run], self.sems.at[g * PARTS + part])

    def start(self, g):
        for copy in self.copies(g):
            copy.start()

    def wait(self, g):
        for copy in self.copies(g):
            copy.wait()


def plane_kernel(per, channels, field, base, ytab, message, ztab, order, held, buffer, sems):
    groups = held.shape[0]
    rows_z = field.shape[-1]
    incoming = Move(field.at[0], buffer, sems)
    for g in range(groups):
        incoming.start(g)
    fill_z(base, ztab)
    fill_order(per, channels, False, order)

    @pl.loop(0, groups)
    def _(g):
        incoming.wait(g)
        blocks = [buffer[g * GROUP + c].reshape(-1, rows_z) for c in range(GROUP)]
        held[g] = analyse(blocks, ztab[...], ytab[...]).astype(BF16)

    deliver(held, order, message, per, channels)


def slope_kernel(
    per, channels, arrived, local, cotangent, base, base_back, ytab, ytab_back, scale,
    slope, message, ztab, ztab_back, order, held, back, local_in, cotangent_in, result, first_sum, second_sum,
    local_sems, cotangent_sems, result_sems,
):
    groups = held.shape[0]
    width, rows_y, rows_z = local.shape[1:]
    incoming = (Move(local, local_in, local_sems), Move(cotangent.at[0], cotangent_in, cotangent_sems))
    outgoing = Move(result, slope, result_sems)
    for g in range(groups):
        for each in incoming:
            each.start(g)
    fill_order(per, channels, True, order)
    receive(arrived, order, ytab_back, scale, held, per)
    fill_z_back(base_back, ztab_back)
    fill_z(base, ztab)
    fill_order(per, channels, False, order)
    wide = 2 * rows_y

    @pl.loop(0, groups)
    def _(g):
        for each in incoming:
            each.wait(g)
        lines = held[g]
        for first in range(0, GROUP, 2):
            total = first_sum if first % 4 else second_sum
            total[...] = dot(lines, ztab_back[:, first * rows_z : (first + 2) * rows_z])
            for offset in range(2):
                c = g * GROUP + first + offset
                for x in range(0, width, 2):
                    value = total[x * rows_y : x * rows_y + wide, offset * rows_z : (offset + 1) * rows_z]
                    value = value + local_in[c, x : x + 2].reshape(wide, rows_z).astype(F32)
                    upstream = cotangent_in[c, x : x + 2].reshape(wide, rows_z)
                    answer = upstream * gelu_slope_rows(value)
                    result[c, x : x + 2] = answer.reshape(2, rows_y, rows_z)
        outgoing.start(g)
        blocks = [result[g * GROUP + c].reshape(-1, rows_z) for c in range(GROUP)]
        plane = analyse(blocks, ztab[...], ytab[...]) * scale[:, : MZ * GROUP]
        back[g] = plane.astype(BF16)

    deliver(back, order, message, per, channels)
    for g in range(groups):
        outgoing.wait(g)


def field_kernel(
    per, channels, arrived, local, base_back, ytab_back, out, ztab_back, order, held, local_in, result,
    local_sems, result_sems,
):
    groups = held.shape[0]
    width, rows_y, rows_z = local.shape[1:]
    incoming = Move(local, local_in, local_sems)
    outgoing = Move(result, out.at[0], result_sems)
    for g in range(groups):
        incoming.start(g)
    fill_order(per, channels, True, order)
    receive(arrived, order, ytab_back, None, held, per)
    fill_z_back(base_back, ztab_back)

    @pl.loop(0, groups)
    def _(g):
        incoming.wait(g)
        lines = held[g]
        for first in range(0, GROUP, 2):
            total = dot(lines, ztab_back[:, first * rows_z : (first + 2) * rows_z])
            for offset in range(2):
                c = g * GROUP + first + offset
                value = total[:, offset * rows_z : (offset + 1) * rows_z]
                value = value + local_in[c].reshape(-1, rows_z).astype(F32)
                result[c] = value.astype(BF16).reshape(width, rows_y, rows_z)
        outgoing.start(g)

    for g in range(groups):
        outgoing.wait(g)


def pointwise_kernel(turned, field, mix, offsets, out, table, shift):
    channels = mix.shape[0]
    width, rows_y, rows_z = field.shape[1:]
    size = channels * TILE

    @pl.when(pl.program_id(0) == 0)
    def _():
        row = lax.broadcasted_iota(jnp.int32, (size, channels), 0) // TILE
        column = lax.broadcasted_iota(jnp.int32, (size, channels), 1)
        spread = jnp.where(row == column, 1.0, 0.0).astype(BF16)
        tall = lax.dot_general(
            spread, mix[...], (((1,), (1 if turned else 0,)), ((), ())), preferred_element_type=F32
        ).astype(BF16)
        whole = lax.dot_general(
            tall, spread, (((1,), (1,)), ((), ())), preferred_element_type=F32
        )
        place = lax.broadcasted_iota(jnp.int32, (size, size), 0) % TILE
        other = lax.broadcasted_iota(jnp.int32, (size, size), 1) % TILE
        table[...] = jnp.where(place == other, whole, 0.0).astype(BF16)
        if offsets is not None:
            for c in range(channels):
                shift[c] = jnp.full((1, rows_z), offsets[c], F32)

    for start in range(0, rows_y, 2 * TILE):
        pieces = [field[:, x, start : start + 2 * TILE, :].astype(F32) for x in range(width)]
        halves = []
        for row in range(0, 2 * TILE, TILE):
            rows = [piece[:, row : row + TILE].reshape(size, rows_z).astype(BF16) for piece in pieces]
            halves.append(dot(table[...], jnp.concatenate(rows, axis=1)))
        for x in range(width):
            values = [
                half[:, x * rows_z : (x + 1) * rows_z].reshape(channels, TILE, rows_z) for half in halves
            ]
            value = jnp.concatenate(values, axis=1)
            if offsets is not None:
                value = value + shift[...]
            out[:, x, start : start + 2 * TILE, :] = value.astype(BF16)


def spread_pair(first, second):
    nothing = jnp.zeros_like(first)
    upper = jnp.concatenate([first, nothing], axis=1)
    lower = jnp.concatenate([nothing, second], axis=1)
    return jnp.concatenate([upper, lower], axis=0)


def low_half(shape):
    return lax.broadcasted_iota(jnp.int32, shape, 1) < shape[1] // 2


def mix_kernel(per, samples, arrived, weights, line, line_back, spec_in, message, held):
    rows = 2 * samples
    lanes = 2 * weights.shape[1]
    low = low_half((samples, lanes))
    flat = arrived[...].reshape(-1, arrived.shape[2])
    spectra = dot(line[...], flat).astype(BF16)
    spec_in[...] = spectra
    for q in range(MX):
        for first in range(0, per, 2):
            block = spread_pair(weights[first * MX + q], weights[(first + 1) * MX + q])
            place = first // 2 * lanes
            terms = dot(spectra[q * rows : (q + 1) * rows, place : place + lanes], block)
            mixed = []
            for side in range(2):
                part = terms[:, side * lanes : (side + 1) * lanes]
                turned = pltpu.roll(part[samples:], lanes // 2, 1)
                mixed.append(part[:samples] + jnp.where(low, -turned, turned))
            real = jnp.where(low, mixed[0], pltpu.roll(mixed[1], lanes // 2, 1))
            imag = jnp.where(low, pltpu.roll(mixed[0], lanes // 2, 1), mixed[1])
            held[q * rows : (q + 1) * rows, place : place + lanes] = jnp.concatenate(
                [real, imag], axis=0
            ).astype(BF16)
    message[...] = dot(line_back[...], held[...]).astype(BF16).reshape(message.shape)


def mix_back_kernel(per, samples, arrived, weights, line, line_back, pairs, message, held):
    rows = 2 * samples
    lanes = 2 * weights.shape[1]
    low = low_half((samples, lanes))
    flat = arrived[...].reshape(-1, arrived.shape[2])
    spectra = dot(line[...], flat).astype(BF16).astype(F32)
    for q in range(MX):
        for first in range(0, per, 2):
            block = spread_pair(weights[first * MX + q], weights[(first + 1) * MX + q])
            place = first // 2 * lanes
            real = spectra[q * rows : q * rows + samples, place : place + lanes]
            imag = spectra[q * rows + samples : (q + 1) * rows, place : place + lanes]
            real_turned = pltpu.roll(real, lanes // 2, 1)
            imag_turned = pltpu.roll(imag, lanes // 2, 1)
            left = [jnp.where(low, real, imag_turned), jnp.where(low, imag, -real_turned)]
            right = [jnp.where(low, real_turned, imag), jnp.where(low, imag_turned, -real)]
            pair = jnp.concatenate(
                [jnp.concatenate(left, axis=0), jnp.concatenate(right, axis=0)], axis=1
            ).astype(BF16)
            pairs[q * rows : (q + 1) * rows, 2 * place : 2 * (place + lanes)] = pair
            held[q * rows : (q + 1) * rows, place : place + lanes] = lax.dot_general(
                pair, block, (((1,), (1,)), ((), ())), preferred_element_type=F32
            ).astype(BF16)
    message[...] = dot(line_back[...], held[...]).astype(BF16).reshape(message.shape)


def weight_kernel(per, samples, spec_in, pairs, out):
    rows = 2 * samples
    lanes = out.shape[2]
    half = lanes // 2
    for q in range(MX):
        for first in range(0, per, 2):
            place = first // 2 * lanes
            left = spec_in[q * rows : (q + 1) * rows, place : place + lanes]
            right = pairs[q * rows : (q + 1) * rows, 2 * place : 2 * (place + lanes)]
            outer = lax.dot_general(
                left, right, (((0,), (0,)), ((), ())), preferred_element_type=F32
            )
            out[first * MX + q] = outer[:half, :lanes]
            out[(first + 1) * MX + q] = outer[half:, lanes:]


def whole(array):
    return pl.BlockSpec(array.shape, lambda *step: (0,) * len(array.shape))


def shaped(shape, dtype):
    return jax.ShapeDtypeStruct(shape, dtype)


def params(mib):
    return pltpu.CompilerParams(vmem_limit_bytes=mib * MIB)


def cost(flops, moved, steep=0):
    return pl.CostEstimate(flops=flops, bytes_accessed=moved, transcendentals=steep)


def body(mesh_axes, devices, slabs, activations, cotangent, mode_weights, pointwise, offsets):
    _, channels, width, rows_y, rows_z = activations.shape
    samples = devices // slabs
    per = MY * MZ // devices
    groups = channels // GROUP
    field = activations.shape[1:]
    count = math.prod(field)
    base = z_base(rows_z)
    ytab = y_table(rows_y, width)
    line_fwd, line_inv = x_tables(samples, slabs, NX)
    weight = np.where(np.arange(MZ) == 0, 1.0, 2.0) / (rows_y * rows_z)
    scale = np.tile(np.repeat(weight, GROUP), groups).astype(np.float32)[None]
    base_t, ytab_t = (np.ascontiguousarray(t.T) for t in (base, ytab))
    fwd_t, inv_t = (np.ascontiguousarray(t.T) for t in (line_fwd, line_inv))
    message = shaped((devices, 2 * width, per * channels), BF16)
    spectra = shaped((MX * 2 * samples, per * channels), BF16)
    ztab = pltpu.VMEM((GROUP * rows_z, 2 * MZ * GROUP), BF16)
    ztab_t = pltpu.VMEM((2 * MZ * GROUP, GROUP * rows_z), BF16)
    order = pltpu.VMEM((MZ * channels, MZ * channels), BF16)
    held_plane = pltpu.VMEM((groups, MY * width * 2, MZ * GROUP), BF16)
    held_lines = pltpu.VMEM((groups, width * rows_y, 2 * MZ * GROUP), BF16)
    buffer = pltpu.VMEM(field, BF16)
    sums = pltpu.VMEM((width * rows_y, 2 * rows_z), F32)
    sems = pltpu.SemaphoreType.DMA((groups * PARTS,))
    far = pl.BlockSpec(memory_space=pltpu.HBM)
    plane_flops = 2 * count * 2 * MZ * GROUP

    def exchange(array):
        return lax.all_to_all(array, mesh_axes, split_axis=0, concat_axis=0, tiled=True)

    def mix_points(values, turned, shifts):
        step = 2
        block = pl.BlockSpec((channels, step, rows_y, rows_z), lambda x: (0, x, 0, 0))
        kernel = functools.partial(pointwise_kernel, turned)
        specs = [block, whole(pointwise)]
        operands = [values, pointwise]
        if shifts is None:
            run = lambda a, b, *rest: kernel(a, b, None, *rest)
        else:
            run = kernel
            specs.append(pl.BlockSpec(memory_space=pltpu.SMEM))
            operands.append(shifts)
        return pl.pallas_call(
            run,
            grid=(width // step,),
            in_specs=specs,
            out_specs=block,
            out_shape=shaped(field, BF16),
            scratch_shapes=[
                pltpu.VMEM((channels * TILE, channels * TILE), BF16),
                pltpu.VMEM((channels, 1, rows_z), F32),
            ],
            compiler_params=params(55),
            cost_estimate=cost(2 * count * channels * TILE, 4 * count),
        )(*operands)

    planes = pl.pallas_call(
        functools.partial(plane_kernel, per, channels),
        in_specs=[far, whole(base), whole(ytab)],
        out_specs=whole(message),
        out_shape=message,
        scratch_shapes=[ztab, order, held_plane, buffer, sems],
        compiler_params=params(55),
        cost_estimate=cost(plane_flops, 2 * count),
    )(activations, base, ytab)
    arrived = exchange(planes)
    local = mix_points(activations.reshape(field), True, offsets)
    arrived, local = lax.optimization_barrier((arrived, local))
    spec_in, mixed = pl.pallas_call(
        functools.partial(mix_kernel, per, samples),
        out_shape=(spectra, message),
        scratch_shapes=[pltpu.VMEM(spectra.shape, BF16)],
        compiler_params=params(16),
        cost_estimate=cost(10**8, 2 * mode_weights.size),
    )(arrived, mode_weights, line_fwd, inv_t)
    returned = exchange(mixed)
    slope, back_plane = pl.pallas_call(
        functools.partial(slope_kernel, per, channels),
        in_specs=[whole(message), far, far]
        + [whole(t) for t in (base, base_t, ytab, ytab_t, scale)],
        out_specs=(far, whole(message)),
        out_shape=(shaped(field, BF16), message),
        scratch_shapes=[ztab, ztab_t, order, held_lines, held_plane]
        + [buffer] * 3
        + [sums] * 2
        + [sems] * 3,
        compiler_params=params(55),
        cost_estimate=cost(2 * plane_flops, 6 * count, 2 * count),
    )(returned, local, cotangent, base, base_t, ytab, ytab_t, scale)
    arrived_back = exchange(back_plane)
    local_back = mix_points(slope, False, None)
    arrived_back, local_back = lax.optimization_barrier((arrived_back, local_back))
    pairs, mixed_back = pl.pallas_call(
        functools.partial(mix_back_kernel, per, samples),
        out_shape=(shaped((spectra.shape[0], 2 * spectra.shape[1]), BF16), message),
        scratch_shapes=[pltpu.VMEM(spectra.shape, BF16)],
        compiler_params=params(16),
        cost_estimate=cost(10**8, 2 * mode_weights.size),
    )(arrived_back, mode_weights, line_inv, fwd_t)
    returned_back = exchange(mixed_back)
    grad_spectral = pl.pallas_call(
        functools.partial(weight_kernel, per, samples),
        out_shape=shaped(mode_weights.shape, F32),
        compiler_params=params(16),
        cost_estimate=cost(10**8, 4 * mode_weights.size),
    )(spec_in, pairs)
    grad_in = pl.pallas_call(
        functools.partial(field_kernel, per, channels),
        in_specs=[whole(message), far, whole(base_t), whole(ytab_t)],
        out_specs=far,
        out_shape=shaped(activations.shape, BF16),
        scratch_shapes=[ztab_t, order, held_lines, buffer, buffer, sems, sems],
        compiler_params=params(55),
        cost_estimate=cost(plane_flops, 4 * count),
    )(returned_back, local_back, base_t, ytab_t)
    return (grad_in, grad_spectral)


def chosen_body(mesh_axes, devices, slabs, activations, cotangent, mode_weights, pointwise, offsets):
    samples, channels, width, rows_y, rows_z = activations.shape
    per = MY * MZ // devices
    fits = (
        samples == 1
        and MY * MZ % devices == 0
        and per in (2, 4, 8)
        and width % 8 == 0
        and channels == 64
        and rows_y % TILE == 0
        and rows_z == 128
    )
    plan = functools.partial(body, mesh_axes, devices, slabs) if fits else general_body
    return plan(activations, cotangent, mode_weights, pointwise, offsets)


def solution(mesh):
    slabs = mesh.shape["space"]
    devices = slabs * mesh.shape["dp"]
    return jax.shard_map(
        functools.partial(chosen_body, ("space", "dp"), devices, slabs),
        mesh=mesh,
        in_specs=(
            P("dp", None, "space", None, None),
            P("dp", None, "space", None, None),
            P(("space", "dp"), None, None),
            P(),
            P(),
        ),
        out_specs=(P("dp", None, "space", None, None), P(("space", "dp"), None, None)),
        check_vma=False,
    )
```

```python
import functools
import math

import jax
import jax.numpy as jnp
import ml_dtypes
import numpy as np
from jax import lax
from jax.experimental import pallas as pl
from jax.experimental.pallas import tpu as pltpu
from jax.sharding import PartitionSpec as P

MX = 16
MY = 16
MZ = 8
NX = 32


def centered(count):
    index = jnp.arange(count, dtype=jnp.int32)
    return jnp.where(index < count // 2, index, index - count)


def plane_tables(rows_y, rows_z, modes_y, modes_z):
    along_y = jnp.arange(rows_y, dtype=jnp.int32)[:, None, None, None]
    along_z = jnp.arange(rows_z, dtype=jnp.int32)[None, :, None, None]
    freq_y = centered(modes_y)[None, None, :, None]
    freq_z = jnp.arange(modes_z, dtype=jnp.int32)[None, None, None, :]
    phase = jnp.mod(freq_y * along_y * rows_z + freq_z * along_z * rows_y, rows_y * rows_z)
    theta = phase.astype(jnp.float32) * (2.0 * math.pi / (rows_y * rows_z))
    cosine = jnp.cos(theta)
    sine = jnp.sin(theta)
    forward = jnp.stack([cosine, -sine], -1).reshape(rows_y * rows_z, modes_y * modes_z * 2)
    scaled = jnp.where(freq_z == 0, 1.0, 2.0).astype(jnp.float32) / (rows_y * rows_z)
    inverse = (
        jnp.stack([cosine * scaled, -sine * scaled], -1)
        .reshape(rows_y * rows_z, modes_y * modes_z * 2)
        .T
    )
    return (forward.astype(jnp.bfloat16), inverse.astype(jnp.bfloat16))


def line_tables(length, modes):
    along = jnp.arange(length, dtype=jnp.int32)[:, None]
    freq = centered(modes)[None, :]
    phase = jnp.mod(freq * along, length)
    theta = phase.astype(jnp.float32) * (2.0 * math.pi / length)
    cosine = jnp.cos(theta)
    sine = jnp.sin(theta)
    first = jnp.stack([cosine, -sine], -1)
    second = jnp.stack([sine, cosine], -1)
    forward = jnp.stack([first, second], 1).reshape(2 * length, 2 * modes)
    inv_first = jnp.stack([cosine.T, sine.T], -1) / length
    inv_second = jnp.stack([-sine.T, cosine.T], -1) / length
    inverse = jnp.stack([inv_first, inv_second], 1).reshape(2 * modes, 2 * length)
    return (forward.astype(jnp.bfloat16), inverse.astype(jnp.bfloat16))


def expand_weights(weights):
    half = weights.shape[1]
    real_part = weights[:, :, :half]
    imag_part = weights[:, :, half:]
    upper = jnp.concatenate([real_part, imag_part], axis=2)
    lower = jnp.concatenate([-imag_part, real_part], axis=2)
    return jnp.concatenate([upper, lower], axis=1)


def outer_sum(left, right):
    return jnp.einsum("mbi,mbo->mio", left, right, preferred_element_type=jnp.float32)


def weight_terms(spec_in, spec_grad):
    half = spec_in.shape[2] // 2
    in_real = spec_in[:, :, :half]
    in_imag = spec_in[:, :, half:]
    gr_real = spec_grad[:, :, :half]
    gr_imag = spec_grad[:, :, half:]
    real_term = outer_sum(in_real, gr_real) + outer_sum(in_imag, gr_imag)
    imag_term = outer_sum(in_real, gr_imag) - outer_sum(in_imag, gr_real)
    return jnp.concatenate([real_term, imag_term], axis=2)


def to_modes(slab, table, modes_x):
    samples, channels, width, pairs = slab.shape
    moved = lax.all_to_all(slab, "space", split_axis=3, concat_axis=2, tiled=True)
    length = moved.shape[2]
    local = moved.shape[3] // 2
    lines = moved.reshape(samples, channels, length, local, 2).transpose(0, 1, 3, 2, 4)
    lines = lines.reshape(samples, channels, local, 2 * length)
    spectra = jnp.dot(lines, table, preferred_element_type=jnp.float32).astype(jnp.bfloat16)
    spectra = spectra.reshape(samples, channels, local, modes_x, 2).transpose(2, 3, 0, 4, 1)
    return spectra.reshape(local * modes_x, samples, 2 * channels)


def to_slab(spectra, table, modes_x, channels):
    count, samples, doubled = spectra.shape
    local = count // modes_x
    lines = spectra.reshape(local, modes_x, samples, 2, channels).transpose(2, 4, 0, 1, 3)
    lines = lines.reshape(samples, channels, local, 2 * modes_x)
    lines = jnp.dot(lines, table, preferred_element_type=jnp.float32).astype(jnp.bfloat16)
    length = lines.shape[3] // 2
    lines = lines.reshape(samples, channels, local, length, 2).transpose(0, 1, 3, 2, 4)
    lines = lines.reshape(samples, channels, length, 2 * local)
    return lax.all_to_all(lines, "space", split_axis=2, concat_axis=3, tiled=True)


def to_owners(spectra):
    return lax.all_to_all(spectra, "dp", split_axis=0, concat_axis=1, tiled=True)


def from_owners(spectra):
    return lax.all_to_all(spectra, "dp", split_axis=1, concat_axis=0, tiled=True)


def gelu_slope(value):
    cdf = 0.5 * (1.0 + lax.erf(value * 0.7071067811865476))
    density = jnp.exp(-0.5 * value * value) * 0.3989422804014327
    return cdf + value * density


def general_body(activations, cotangent, mode_weights, pointwise, offsets):
    samples, channels, width, rows_y, rows_z = activations.shape
    plane_fwd, plane_inv = plane_tables(rows_y, rows_z, MY, MZ)
    line_fwd, line_inv = line_tables(NX, MX)
    flat = activations.reshape(samples, channels, width, rows_y * rows_z)
    planes = jnp.dot(flat, plane_fwd, preferred_element_type=jnp.float32).astype(jnp.bfloat16)
    spec_in = to_modes(planes, line_fwd, MX)
    blocks = expand_weights(mode_weights)
    held_in = to_owners(spec_in)
    held_out = jnp.einsum(
        "mbi,mio->mbo", held_in, blocks, preferred_element_type=jnp.float32
    ).astype(jnp.bfloat16)
    spec_out = from_owners(held_out)
    returned = to_slab(spec_out, line_inv, MX, channels)
    spectral = jnp.dot(returned, plane_inv, preferred_element_type=jnp.float32)
    local_part = jnp.einsum("io,bixn->boxn", pointwise, flat, preferred_element_type=jnp.float32)
    summed = spectral + local_part + offsets[None, :, None, None]
    upstream = cotangent.reshape(flat.shape).astype(jnp.float32)
    slope_grad = (upstream * gelu_slope(summed)).astype(jnp.bfloat16)
    back_plane = jnp.dot(slope_grad, plane_inv.T, preferred_element_type=jnp.float32).astype(
        jnp.bfloat16
    )
    spec_grad = to_modes(back_plane, line_inv.T, MX)
    held_grad = to_owners(spec_grad)
    held_dx = jnp.einsum(
        "mbo,mio->mbi", held_grad, blocks, preferred_element_type=jnp.float32
    ).astype(jnp.bfloat16)
    spec_dx = from_owners(held_dx)
    grad_spectral = weight_terms(held_in, held_grad)
    line_dx = to_slab(spec_dx, line_fwd.T, MX, channels)
    total = jnp.dot(line_dx, plane_fwd.T, preferred_element_type=jnp.float32)
    total = total + jnp.einsum(
        "io,boxn->bixn", pointwise, slope_grad, preferred_element_type=jnp.float32
    )
    grad_in = total.astype(jnp.bfloat16).reshape(activations.shape)
    return (grad_in, grad_spectral)


BF16 = jnp.bfloat16
F32 = jnp.float32
GROUP = 16
TILE = 8
PARTS = 4
MIB = 1024 * 1024


def rounded(table):
    return np.asarray(table, np.float32).astype(ml_dtypes.bfloat16)


def angles(freq, points, length):
    phase = np.mod(np.outer(freq, points), length)
    return (phase * (2.0 * math.pi / length)).astype(np.float64)


def signed(count):
    index = np.arange(count)
    return np.where(index < count // 2, index, index - count)


def z_base(rows_z):
    theta = angles(np.arange(MZ), np.arange(rows_z), rows_z)
    pair = np.stack([np.cos(theta), -np.sin(theta)])
    table = np.repeat(pair.reshape(2 * MZ, rows_z), GROUP, axis=0).T
    return rounded(table).astype(np.float32)


def y_table(rows_y, width):
    theta = angles(signed(MY), np.arange(rows_y), rows_y)
    cosine, sine = np.cos(theta), np.sin(theta)
    turn = np.stack([np.stack([cosine, sine]), np.stack([-sine, cosine])])
    table = np.einsum("rsjy,xw->jxrswy", turn, np.eye(width))
    return rounded(table.reshape(MY * width * 2, 2 * width * rows_y))


def x_tables(samples, slabs, length):
    theta = angles(signed(MX), np.arange(length), length)
    cosine, sine = np.cos(theta), np.sin(theta)
    forward = np.stack([np.stack([cosine, sine]), np.stack([-sine, cosine])])
    inverse = np.stack([np.stack([cosine, sine]), np.stack([-sine, cosine])]) / length
    same = np.eye(samples)
    rows = MX * 2 * samples

    def lay(turn):
        turn = turn.reshape(2, 2, MX, slabs, length // slabs)
        table = np.einsum("arqsx,bd->qabsdxr", turn, same)
        return rounded(table.reshape(rows, samples * length * 2))

    return lay(forward), lay(inverse)


def dot(left, right):
    return jnp.dot(left, right, preferred_element_type=F32)


def gelu_slope_rows(value):
    decay = jnp.exp2(value * value * (-0.5 * math.log2(math.e))).astype(BF16)
    value = value.astype(BF16)

    def number(x):
        return jnp.asarray(x, BF16)

    size = jnp.abs(value)
    t = pl.reciprocal(number(1.0) + number(0.3275911 * math.sqrt(0.5)) * size, approx=True)
    tail = number(0.5 * 1.061405429) * t - number(0.5 * 1.453152027)
    tail = tail * t + number(0.5 * 1.421413741)
    tail = tail * t - number(0.5 * 0.284496736)
    tail = tail * t + number(0.5 * 0.254829592)
    part = (size * number(1.0 / math.sqrt(2.0 * math.pi)) - tail * t) * decay
    return jnp.where(value >= number(0.0), number(1.0) + part, -part)


def over(index, size):
    return lax.shift_right_logical(index, jnp.int32(size.bit_length() - 1))


def within(index, size):
    return jnp.bitwise_and(index, jnp.int32(size - 1))


def fill_z(base, table):
    rows_z, lanes = base.shape
    owner = within(lax.broadcasted_iota(jnp.int32, (rows_z, lanes), 1), GROUP)
    values = base[...]
    for c in range(GROUP):
        table[c * rows_z : (c + 1) * rows_z] = jnp.where(owner == c, values, 0.0).astype(BF16)


def fill_z_back(base, table):
    lanes, rows_z = base.shape
    owner = within(lax.broadcasted_iota(jnp.int32, (lanes, rows_z), 0), GROUP)
    values = base[...]
    for c in range(GROUP):
        table[:, c * rows_z : (c + 1) * rows_z] = jnp.where(owner == c, values, 0.0).astype(BF16)


def grouped(lane, per, channels):
    c = within(lane, channels)
    return over(c, GROUP) * (MZ * GROUP) + over(lane, channels) * GROUP + within(c, GROUP)


def fill_order(per, channels, back, table):
    count = table.shape[0]
    row = lax.broadcasted_iota(jnp.int32, (count, count), 0)
    column = lax.broadcasted_iota(jnp.int32, (count, count), 1)
    if back:
        same = grouped(row[:, :1], per, channels) == column
    else:
        same = row == grouped(column[:1], per, channels)
    table[...] = jnp.where(same, 1.0, 0.0).astype(BF16)


def analyse(field, ztab, ytab):
    middle = len(field) // 2
    depth = ztab.shape[0] // 2
    spectra = dot(jnp.concatenate(field[:middle], axis=1), ztab[:depth])
    spectra = (spectra + dot(jnp.concatenate(field[middle:], axis=1), ztab[depth:])).astype(BF16)
    half = spectra.shape[1] // 2
    return dot(ytab, jnp.concatenate([spectra[:, :half], spectra[:, half:]], axis=0))


def deliver(held, order, message, per, channels):
    joined = jnp.concatenate([held[g] for g in range(held.shape[0])], axis=1)
    ordered = dot(joined, order[...]).astype(BF16)
    parts = MZ // per
    rows = message.shape[1]
    lanes = per * channels
    for part in range(parts):
        block = ordered[:, part * lanes : (part + 1) * lanes]
        for j in range(MY):
            message[j * parts + part] = block[j * rows : (j + 1) * rows]


def receive(message, order_back, ytab_back, scale, held, per):
    parts = MZ // per
    blocks = message[...]
    blocks = blocks.reshape(MY, parts, *blocks.shape[1:])
    lanes = [blocks[:, part].reshape(-1, blocks.shape[3]) for part in range(parts)]
    ordered = dot(jnp.concatenate(lanes, axis=1), order_back[...]).astype(BF16)
    lines = dot(ytab_back[...], ordered)
    if scale is not None:
        lines = lines * scale[...]
    lines = lines.astype(BF16)
    rows = lines.shape[0] // 2
    wide = MZ * GROUP
    for group in range(held.shape[0]):
        piece = lines[:, group * wide : (group + 1) * wide]
        held[group] = jnp.concatenate([piece[:rows], piece[rows:]], axis=1)


class Move:
    def __init__(self, source, target, sems):
        self.source, self.target, self.sems = source, target, sems

    def copies(self, g):
        size = GROUP // PARTS
        for part in range(PARTS):
            run = pl.ds(g * GROUP + part * size, size)
            yield pltpu.make_async_copy(self.source.at[run], self.target.at[run], self.sems.at[g * PARTS + part])

    def start(self, g):
        for copy in self.copies(g):
            copy.start()

    def wait(self, g):
        for copy in self.copies(g):
            copy.wait()


def plane_kernel(per, channels, field, base, ytab, message, ztab, order, held, buffer, sems):
    groups = held.shape[0]
    rows_z = field.shape[-1]
    incoming = Move(field.at[0], buffer, sems)
    for g in range(groups):
        incoming.start(g)
    fill_z(base, ztab)
    fill_order(per, channels, False, order)

    @pl.loop(0, groups)
    def _(g):
        incoming.wait(g)
        blocks = [buffer[g * GROUP + c].reshape(-1, rows_z) for c in range(GROUP)]
        held[g] = analyse(blocks, ztab[...], ytab[...]).astype(BF16)

    deliver(held, order, message, per, channels)


def slope_kernel(
    per, channels, arrived, local, cotangent, base, base_back, ytab, ytab_back, scale,
    slope, message, ztab, ztab_back, order, held, back, local_in, cotangent_in, result, first_sum, second_sum,
    local_sems, cotangent_sems, result_sems,
):
    groups = held.shape[0]
    width, rows_y, rows_z = local.shape[1:]
    incoming = (Move(local, local_in, local_sems), Move(cotangent.at[0], cotangent_in, cotangent_sems))
    outgoing = Move(result, slope, result_sems)
    for g in range(groups):
        for each in incoming:
            each.start(g)
    fill_order(per, channels, True, order)
    receive(arrived, order, ytab_back, scale, held, per)
    fill_z_back(base_back, ztab_back)
    fill_z(base, ztab)
    fill_order(per, channels, False, order)
    wide = 2 * rows_y

    @pl.loop(0, groups)
    def _(g):
        for each in incoming:
            each.wait(g)
        lines = held[g]
        for first in range(0, GROUP, 2):
            total = first_sum if first % 4 else second_sum
            total[...] = dot(lines, ztab_back[:, first * rows_z : (first + 2) * rows_z])
            for offset in range(2):
                c = g * GROUP + first + offset
                for x in range(0, width, 2):
                    value = total[x * rows_y : x * rows_y + wide, offset * rows_z : (offset + 1) * rows_z]
                    value = value + local_in[c, x : x + 2].reshape(wide, rows_z).astype(F32)
                    upstream = cotangent_in[c, x : x + 2].reshape(wide, rows_z)
                    answer = upstream * gelu_slope_rows(value)
                    result[c, x : x + 2] = answer.reshape(2, rows_y, rows_z)
        outgoing.start(g)
        blocks = [result[g * GROUP + c].reshape(-1, rows_z) for c in range(GROUP)]
        plane = analyse(blocks, ztab[...], ytab[...]) * scale[:, : MZ * GROUP]
        back[g] = plane.astype(BF16)

    deliver(back, order, message, per, channels)
    for g in range(groups):
        outgoing.wait(g)


def field_kernel(
    per, channels, arrived, local, base_back, ytab_back, out, ztab_back, order, held, local_in, result,
    local_sems, result_sems,
):
    groups = held.shape[0]
    width, rows_y, rows_z = local.shape[1:]
    incoming = Move(local, local_in, local_sems)
    outgoing = Move(result, out.at[0], result_sems)
    for g in range(groups):
        incoming.start(g)
    fill_order(per, channels, True, order)
    receive(arrived, order, ytab_back, None, held, per)
    fill_z_back(base_back, ztab_back)

    @pl.loop(0, groups)
    def _(g):
        incoming.wait(g)
        lines = held[g]
        for first in range(0, GROUP, 2):
            total = dot(lines, ztab_back[:, first * rows_z : (first + 2) * rows_z])
            for offset in range(2):
                c = g * GROUP + first + offset
                value = total[:, offset * rows_z : (offset + 1) * rows_z]
                value = value + local_in[c].reshape(-1, rows_z).astype(F32)
                result[c] = value.astype(BF16).reshape(width, rows_y, rows_z)
        outgoing.start(g)

    for g in range(groups):
        outgoing.wait(g)


def pointwise_kernel(turned, field, mix, offsets, out, table, shift):
    channels = mix.shape[0]
    width, rows_y, rows_z = field.shape[1:]
    size = channels * TILE

    @pl.when(pl.program_id(0) == 0)
    def _():
        row = over(lax.broadcasted_iota(jnp.int32, (size, channels), 0), TILE)
        column = lax.broadcasted_iota(jnp.int32, (size, channels), 1)
        spread = jnp.where(row == column, 1.0, 0.0).astype(BF16)
        tall = lax.dot_general(
            spread, mix[...], (((1,), (1 if turned else 0,)), ((), ())), preferred_element_type=F32
        ).astype(BF16)
        whole = lax.dot_general(
            tall, spread, (((1,), (1,)), ((), ())), preferred_element_type=F32
        )
        place = within(lax.broadcasted_iota(jnp.int32, (size, size), 0), TILE)
        other = within(lax.broadcasted_iota(jnp.int32, (size, size), 1), TILE)
        table[...] = jnp.where(place == other, whole, 0.0).astype(BF16)
        if offsets is not None:
            for c in range(channels):
                shift[c] = jnp.full((1, rows_z), offsets[c], F32)

    for start in range(0, rows_y, 2 * TILE):
        pieces = [field[:, x, start : start + 2 * TILE, :].astype(F32) for x in range(width)]
        halves = []
        for row in range(0, 2 * TILE, TILE):
            rows = [piece[:, row : row + TILE].reshape(size, rows_z).astype(BF16) for piece in pieces]
            halves.append(dot(table[...], jnp.concatenate(rows, axis=1)))
        for x in range(width):
            values = [
                half[:, x * rows_z : (x + 1) * rows_z].reshape(channels, TILE, rows_z) for half in halves
            ]
            value = jnp.concatenate(values, axis=1)
            if offsets is not None:
                value = value + shift[...]
            out[:, x, start : start + 2 * TILE, :] = value.astype(BF16)


def spread_pair(first, second):
    nothing = jnp.zeros_like(first)
    upper = jnp.concatenate([first, nothing], axis=1)
    lower = jnp.concatenate([nothing, second], axis=1)
    return jnp.concatenate([upper, lower], axis=0)


def low_half(shape):
    return lax.broadcasted_iota(jnp.int32, shape, 1) < shape[1] // 2


def mix_kernel(per, samples, arrived, weights, line, line_back, spec_in, message, held):
    rows = 2 * samples
    lanes = 2 * weights.shape[1]
    low = low_half((samples, lanes))
    flat = arrived[...].reshape(-1, arrived.shape[2])
    spectra = dot(line[...], flat).astype(BF16)
    spec_in[...] = spectra
    for q in range(MX):
        for first in range(0, per, 2):
            block = spread_pair(weights[first * MX + q], weights[(first + 1) * MX + q])
            place = first // 2 * lanes
            terms = dot(spectra[q * rows : (q + 1) * rows, place : place + lanes], block)
            mixed = []
            for side in range(2):
                part = terms[:, side * lanes : (side + 1) * lanes]
                turned = pltpu.roll(part[samples:], lanes // 2, 1)
                mixed.append(part[:samples] + jnp.where(low, -turned, turned))
            real = jnp.where(low, mixed[0], pltpu.roll(mixed[1], lanes // 2, 1))
            imag = jnp.where(low, pltpu.roll(mixed[0], lanes // 2, 1), mixed[1])
            held[q * rows : (q + 1) * rows, place : place + lanes] = jnp.concatenate(
                [real, imag], axis=0
            ).astype(BF16)
    message[...] = dot(line_back[...], held[...]).astype(BF16).reshape(message.shape)


def mix_back_kernel(per, samples, arrived, weights, line, line_back, pairs, message, held):
    rows = 2 * samples
    lanes = 2 * weights.shape[1]
    low = low_half((samples, lanes))
    flat = arrived[...].reshape(-1, arrived.shape[2])
    spectra = dot(line[...], flat).astype(BF16).astype(F32)
    for q in range(MX):
        for first in range(0, per, 2):
            block = spread_pair(weights[first * MX + q], weights[(first + 1) * MX + q])
            place = first // 2 * lanes
            real = spectra[q * rows : q * rows + samples, place : place + lanes]
            imag = spectra[q * rows + samples : (q + 1) * rows, place : place + lanes]
            real_turned = pltpu.roll(real, lanes // 2, 1)
            imag_turned = pltpu.roll(imag, lanes // 2, 1)
            left = [jnp.where(low, real, imag_turned), jnp.where(low, imag, -real_turned)]
            right = [jnp.where(low, real_turned, imag), jnp.where(low, imag_turned, -real)]
            pair = jnp.concatenate(
                [jnp.concatenate(left, axis=0), jnp.concatenate(right, axis=0)], axis=1
            ).astype(BF16)
            pairs[q * rows : (q + 1) * rows, 2 * place : 2 * (place + lanes)] = pair
            held[q * rows : (q + 1) * rows, place : place + lanes] = lax.dot_general(
                pair, block, (((1,), (1,)), ((), ())), preferred_element_type=F32
            ).astype(BF16)
    message[...] = dot(line_back[...], held[...]).astype(BF16).reshape(message.shape)


def weight_kernel(per, samples, spec_in, pairs, out):
    rows = 2 * samples
    lanes = out.shape[2]
    half = lanes // 2
    for q in range(MX):
        for first in range(0, per, 2):
            place = first // 2 * lanes
            left = spec_in[q * rows : (q + 1) * rows, place : place + lanes]
            right = pairs[q * rows : (q + 1) * rows, 2 * place : 2 * (place + lanes)]
            outer = lax.dot_general(
                left, right, (((0,), (0,)), ((), ())), preferred_element_type=F32
            )
            out[first * MX + q] = outer[:half, :lanes]
            out[(first + 1) * MX + q] = outer[half:, lanes:]


def whole(array):
    return pl.BlockSpec(array.shape, lambda *step: (0,) * len(array.shape))


def shaped(shape, dtype):
    return jax.ShapeDtypeStruct(shape, dtype)


def params(mib):
    return pltpu.CompilerParams(vmem_limit_bytes=mib * MIB)


def cost(flops, moved, steep=0):
    return pl.CostEstimate(flops=flops, bytes_accessed=moved, transcendentals=steep)


def body(mesh_axes, devices, slabs, activations, cotangent, mode_weights, pointwise, offsets):
    _, channels, width, rows_y, rows_z = activations.shape
    samples = devices // slabs
    per = MY * MZ // devices
    groups = channels // GROUP
    field = activations.shape[1:]
    count = math.prod(field)
    base = z_base(rows_z)
    ytab = y_table(rows_y, width)
    line_fwd, line_inv = x_tables(samples, slabs, NX)
    weight = np.where(np.arange(MZ) == 0, 1.0, 2.0) / (rows_y * rows_z)
    scale = np.tile(np.repeat(weight, GROUP), groups).astype(np.float32)[None]
    base_t, ytab_t = (np.ascontiguousarray(t.T) for t in (base, ytab))
    fwd_t, inv_t = (np.ascontiguousarray(t.T) for t in (line_fwd, line_inv))
    message = shaped((devices, 2 * width, per * channels), BF16)
    spectra = shaped((MX * 2 * samples, per * channels), BF16)
    ztab = pltpu.VMEM((GROUP * rows_z, 2 * MZ * GROUP), BF16)
    ztab_t = pltpu.VMEM((2 * MZ * GROUP, GROUP * rows_z), BF16)
    order = pltpu.VMEM((MZ * channels, MZ * channels), BF16)
    held_plane = pltpu.VMEM((groups, MY * width * 2, MZ * GROUP), BF16)
    held_lines = pltpu.VMEM((groups, width * rows_y, 2 * MZ * GROUP), BF16)
    buffer = pltpu.VMEM(field, BF16)
    sums = pltpu.VMEM((width * rows_y, 2 * rows_z), F32)
    sems = pltpu.SemaphoreType.DMA((groups * PARTS,))
    far = pl.BlockSpec(memory_space=pltpu.HBM)
    plane_flops = 2 * count * 2 * MZ * GROUP

    def exchange(array):
        return lax.all_to_all(array, mesh_axes, split_axis=0, concat_axis=0, tiled=True)

    def mix_points(values, turned, shifts):
        step = 2
        block = pl.BlockSpec((channels, step, rows_y, rows_z), lambda x: (0, x, 0, 0))
        kernel = functools.partial(pointwise_kernel, turned)
        specs = [block, whole(pointwise)]
        operands = [values, pointwise]
        if shifts is None:
            run = lambda a, b, *rest: kernel(a, b, None, *rest)
        else:
            run = kernel
            specs.append(pl.BlockSpec(memory_space=pltpu.SMEM))
            operands.append(shifts)
        return pl.pallas_call(
            run,
            grid=(width // step,),
            in_specs=specs,
            out_specs=block,
            out_shape=shaped(field, BF16),
            scratch_shapes=[
                pltpu.VMEM((channels * TILE, channels * TILE), BF16),
                pltpu.VMEM((channels, 1, rows_z), F32),
            ],
            compiler_params=params(55),
            cost_estimate=cost(2 * count * channels * TILE, 4 * count),
        )(*operands)

    planes = pl.pallas_call(
        functools.partial(plane_kernel, per, channels),
        in_specs=[far, whole(base), whole(ytab)],
        out_specs=whole(message),
        out_shape=message,
        scratch_shapes=[ztab, order, held_plane, buffer, sems],
        compiler_params=params(55),
        cost_estimate=cost(plane_flops, 2 * count),
    )(activations, base, ytab)
    arrived = exchange(planes)
    local = mix_points(activations.reshape(field), True, offsets)
    arrived, local = lax.optimization_barrier((arrived, local))
    spec_in, mixed = pl.pallas_call(
        functools.partial(mix_kernel, per, samples),
        out_shape=(spectra, message),
        scratch_shapes=[pltpu.VMEM(spectra.shape, BF16)],
        compiler_params=params(16),
        cost_estimate=cost(10**8, 2 * mode_weights.size),
    )(arrived, mode_weights, line_fwd, inv_t)
    returned = exchange(mixed)
    slope, back_plane = pl.pallas_call(
        functools.partial(slope_kernel, per, channels),
        in_specs=[whole(message), far, far]
        + [whole(t) for t in (base, base_t, ytab, ytab_t, scale)],
        out_specs=(far, whole(message)),
        out_shape=(shaped(field, BF16), message),
        scratch_shapes=[ztab, ztab_t, order, held_lines, held_plane]
        + [buffer] * 3
        + [sums] * 2
        + [sems] * 3,
        compiler_params=params(55),
        cost_estimate=cost(2 * plane_flops, 6 * count, 2 * count),
    )(returned, local, cotangent, base, base_t, ytab, ytab_t, scale)
    arrived_back = exchange(back_plane)
    local_back = mix_points(slope, False, None)
    arrived_back, local_back = lax.optimization_barrier((arrived_back, local_back))
    pairs, mixed_back = pl.pallas_call(
        functools.partial(mix_back_kernel, per, samples),
        out_shape=(shaped((spectra.shape[0], 2 * spectra.shape[1]), BF16), message),
        scratch_shapes=[pltpu.VMEM(spectra.shape, BF16)],
        compiler_params=params(16),
        cost_estimate=cost(10**8, 2 * mode_weights.size),
    )(arrived_back, mode_weights, line_inv, fwd_t)
    returned_back = exchange(mixed_back)
    grad_spectral = pl.pallas_call(
        functools.partial(weight_kernel, per, samples),
        out_shape=shaped(mode_weights.shape, F32),
        compiler_params=params(16),
        cost_estimate=cost(10**8, 4 * mode_weights.size),
    )(spec_in, pairs)
    grad_in = pl.pallas_call(
        functools.partial(field_kernel, per, channels),
        in_specs=[whole(message), far, whole(base_t), whole(ytab_t)],
        out_specs=far,
        out_shape=shaped(activations.shape, BF16),
        scratch_shapes=[ztab_t, order, held_lines, buffer, buffer, sems, sems],
        compiler_params=params(55),
        cost_estimate=cost(plane_flops, 4 * count),
    )(returned_back, local_back, base_t, ytab_t)
    return (grad_in, grad_spectral)


def chosen_body(mesh_axes, devices, slabs, activations, cotangent, mode_weights, pointwise, offsets):
    samples, channels, width, rows_y, rows_z = activations.shape
    per = MY * MZ // devices
    fits = (
        samples == 1
        and MY * MZ % devices == 0
        and per in (2, 4, 8)
        and width % 8 == 0
        and channels == 64
        and rows_y % TILE == 0
        and rows_z == 128
    )
    plan = functools.partial(body, mesh_axes, devices, slabs) if fits else general_body
    return plan(activations, cotangent, mode_weights, pointwise, offsets)


def solution(mesh):
    slabs = mesh.shape["space"]
    devices = slabs * mesh.shape["dp"]
    return jax.shard_map(
        functools.partial(chosen_body, ("space", "dp"), devices, slabs),
        mesh=mesh,
        in_specs=(
            P("dp", None, "space", None, None),
            P("dp", None, "space", None, None),
            P(("space", "dp"), None, None),
            P(),
            P(),
        ),
        out_specs=(P("dp", None, "space", None, None), P(("space", "dp"), None, None)),
        check_vma=False,
    )
```

```python
import functools
import math

import jax
import jax.numpy as jnp
import ml_dtypes
import numpy as np
from jax import lax
from jax.experimental import pallas as pl
from jax.experimental.pallas import tpu as pltpu
from jax.sharding import PartitionSpec as P

MX = 16
MY = 16
MZ = 8
NX = 32


def centered(count):
    index = jnp.arange(count, dtype=jnp.int32)
    return jnp.where(index < count // 2, index, index - count)


def plane_tables(rows_y, rows_z, modes_y, modes_z):
    along_y = jnp.arange(rows_y, dtype=jnp.int32)[:, None, None, None]
    along_z = jnp.arange(rows_z, dtype=jnp.int32)[None, :, None, None]
    freq_y = centered(modes_y)[None, None, :, None]
    freq_z = jnp.arange(modes_z, dtype=jnp.int32)[None, None, None, :]
    phase = jnp.mod(freq_y * along_y * rows_z + freq_z * along_z * rows_y, rows_y * rows_z)
    theta = phase.astype(jnp.float32) * (2.0 * math.pi / (rows_y * rows_z))
    cosine = jnp.cos(theta)
    sine = jnp.sin(theta)
    forward = jnp.stack([cosine, -sine], -1).reshape(rows_y * rows_z, modes_y * modes_z * 2)
    scaled = jnp.where(freq_z == 0, 1.0, 2.0).astype(jnp.float32) / (rows_y * rows_z)
    inverse = (
        jnp.stack([cosine * scaled, -sine * scaled], -1)
        .reshape(rows_y * rows_z, modes_y * modes_z * 2)
        .T
    )
    return (forward.astype(jnp.bfloat16), inverse.astype(jnp.bfloat16))


def line_tables(length, modes):
    along = jnp.arange(length, dtype=jnp.int32)[:, None]
    freq = centered(modes)[None, :]
    phase = jnp.mod(freq * along, length)
    theta = phase.astype(jnp.float32) * (2.0 * math.pi / length)
    cosine = jnp.cos(theta)
    sine = jnp.sin(theta)
    first = jnp.stack([cosine, -sine], -1)
    second = jnp.stack([sine, cosine], -1)
    forward = jnp.stack([first, second], 1).reshape(2 * length, 2 * modes)
    inv_first = jnp.stack([cosine.T, sine.T], -1) / length
    inv_second = jnp.stack([-sine.T, cosine.T], -1) / length
    inverse = jnp.stack([inv_first, inv_second], 1).reshape(2 * modes, 2 * length)
    return (forward.astype(jnp.bfloat16), inverse.astype(jnp.bfloat16))


def expand_weights(weights):
    half = weights.shape[1]
    real_part = weights[:, :, :half]
    imag_part = weights[:, :, half:]
    upper = jnp.concatenate([real_part, imag_part], axis=2)
    lower = jnp.concatenate([-imag_part, real_part], axis=2)
    return jnp.concatenate([upper, lower], axis=1)


def outer_sum(left, right):
    return jnp.einsum("mbi,mbo->mio", left, right, preferred_element_type=jnp.float32)


def weight_terms(spec_in, spec_grad):
    half = spec_in.shape[2] // 2
    in_real = spec_in[:, :, :half]
    in_imag = spec_in[:, :, half:]
    gr_real = spec_grad[:, :, :half]
    gr_imag = spec_grad[:, :, half:]
    real_term = outer_sum(in_real, gr_real) + outer_sum(in_imag, gr_imag)
    imag_term = outer_sum(in_real, gr_imag) - outer_sum(in_imag, gr_real)
    return jnp.concatenate([real_term, imag_term], axis=2)


def to_modes(slab, table, modes_x):
    samples, channels, width, pairs = slab.shape
    moved = lax.all_to_all(slab, "space", split_axis=3, concat_axis=2, tiled=True)
    length = moved.shape[2]
    local = moved.shape[3] // 2
    lines = moved.reshape(samples, channels, length, local, 2).transpose(0, 1, 3, 2, 4)
    lines = lines.reshape(samples, channels, local, 2 * length)
    spectra = jnp.dot(lines, table, preferred_element_type=jnp.float32).astype(jnp.bfloat16)
    spectra = spectra.reshape(samples, channels, local, modes_x, 2).transpose(2, 3, 0, 4, 1)
    return spectra.reshape(local * modes_x, samples, 2 * channels)


def to_slab(spectra, table, modes_x, channels):
    count, samples, doubled = spectra.shape
    local = count // modes_x
    lines = spectra.reshape(local, modes_x, samples, 2, channels).transpose(2, 4, 0, 1, 3)
    lines = lines.reshape(samples, channels, local, 2 * modes_x)
    lines = jnp.dot(lines, table, preferred_element_type=jnp.float32).astype(jnp.bfloat16)
    length = lines.shape[3] // 2
    lines = lines.reshape(samples, channels, local, length, 2).transpose(0, 1, 3, 2, 4)
    lines = lines.reshape(samples, channels, length, 2 * local)
    return lax.all_to_all(lines, "space", split_axis=2, concat_axis=3, tiled=True)


def to_owners(spectra):
    return lax.all_to_all(spectra, "dp", split_axis=0, concat_axis=1, tiled=True)


def from_owners(spectra):
    return lax.all_to_all(spectra, "dp", split_axis=1, concat_axis=0, tiled=True)


def gelu_slope(value):
    cdf = 0.5 * (1.0 + lax.erf(value * 0.7071067811865476))
    density = jnp.exp(-0.5 * value * value) * 0.3989422804014327
    return cdf + value * density


def general_body(activations, cotangent, mode_weights, pointwise, offsets):
    samples, channels, width, rows_y, rows_z = activations.shape
    plane_fwd, plane_inv = plane_tables(rows_y, rows_z, MY, MZ)
    line_fwd, line_inv = line_tables(NX, MX)
    flat = activations.reshape(samples, channels, width, rows_y * rows_z)
    planes = jnp.dot(flat, plane_fwd, preferred_element_type=jnp.float32).astype(jnp.bfloat16)
    spec_in = to_modes(planes, line_fwd, MX)
    blocks = expand_weights(mode_weights)
    held_in = to_owners(spec_in)
    held_out = jnp.einsum(
        "mbi,mio->mbo", held_in, blocks, preferred_element_type=jnp.float32
    ).astype(jnp.bfloat16)
    spec_out = from_owners(held_out)
    returned = to_slab(spec_out, line_inv, MX, channels)
    spectral = jnp.dot(returned, plane_inv, preferred_element_type=jnp.float32)
    local_part = jnp.einsum("io,bixn->boxn", pointwise, flat, preferred_element_type=jnp.float32)
    summed = spectral + local_part + offsets[None, :, None, None]
    upstream = cotangent.reshape(flat.shape).astype(jnp.float32)
    slope_grad = (upstream * gelu_slope(summed)).astype(jnp.bfloat16)
    back_plane = jnp.dot(slope_grad, plane_inv.T, preferred_element_type=jnp.float32).astype(
        jnp.bfloat16
    )
    spec_grad = to_modes(back_plane, line_inv.T, MX)
    held_grad = to_owners(spec_grad)
    held_dx = jnp.einsum(
        "mbo,mio->mbi", held_grad, blocks, preferred_element_type=jnp.float32
    ).astype(jnp.bfloat16)
    spec_dx = from_owners(held_dx)
    grad_spectral = weight_terms(held_in, held_grad)
    line_dx = to_slab(spec_dx, line_fwd.T, MX, channels)
    total = jnp.dot(line_dx, plane_fwd.T, preferred_element_type=jnp.float32)
    total = total + jnp.einsum(
        "io,boxn->bixn", pointwise, slope_grad, preferred_element_type=jnp.float32
    )
    grad_in = total.astype(jnp.bfloat16).reshape(activations.shape)
    return (grad_in, grad_spectral)


BF16 = jnp.bfloat16
F32 = jnp.float32
GROUP = 16
TILE = 8
SLOTS = 4
STEPS = GROUP // SLOTS
MIB = 1024 * 1024


def rounded(table):
    return np.asarray(table, np.float32).astype(ml_dtypes.bfloat16)


def angles(freq, points, length):
    phase = np.mod(np.outer(freq, points), length)
    return (phase * (2.0 * math.pi / length)).astype(np.float64)


def signed(count):
    index = np.arange(count)
    return np.where(index < count // 2, index, index - count)


def z_base(rows_z):
    theta = angles(np.arange(MZ), np.arange(rows_z), rows_z)
    pair = np.stack([np.cos(theta), -np.sin(theta)])
    table = np.repeat(pair.reshape(2 * MZ, rows_z), GROUP, axis=0).T
    return rounded(table).astype(np.float32)


def y_table(rows_y, width):
    theta = angles(signed(MY), np.arange(rows_y), rows_y)
    cosine, sine = np.cos(theta), np.sin(theta)
    turn = np.stack([np.stack([cosine, sine]), np.stack([-sine, cosine])])
    table = np.einsum("rsjy,xw->jxrswy", turn, np.eye(width))
    return rounded(table.reshape(MY * width * 2, 2 * width * rows_y))


def x_tables(samples, slabs, length):
    theta = angles(signed(MX), np.arange(length), length)
    cosine, sine = np.cos(theta), np.sin(theta)
    forward = np.stack([np.stack([cosine, sine]), np.stack([-sine, cosine])])
    inverse = np.stack([np.stack([cosine, sine]), np.stack([-sine, cosine])]) / length
    same = np.eye(samples)
    rows = MX * 2 * samples

    def lay(turn):
        turn = turn.reshape(2, 2, MX, slabs, length // slabs)
        table = np.einsum("arqsx,bd->qabsdxr", turn, same)
        return rounded(table.reshape(rows, samples * length * 2))

    return lay(forward), lay(inverse)


def dot(left, right):
    return jnp.dot(left, right, preferred_element_type=F32)


def gelu_slope_rows(value):
    decay = jnp.exp2(value * value * (-0.5 * math.log2(math.e))).astype(BF16)
    value = value.astype(BF16)

    def number(x):
        return jnp.asarray(x, BF16)

    size = jnp.abs(value)
    t = pl.reciprocal(number(1.0) + number(0.3275911 * math.sqrt(0.5)) * size, approx=True)
    tail = number(0.5 * 1.061405429) * t - number(0.5 * 1.453152027)
    tail = tail * t + number(0.5 * 1.421413741)
    tail = tail * t - number(0.5 * 0.284496736)
    tail = tail * t + number(0.5 * 0.254829592)
    part = (size * number(1.0 / math.sqrt(2.0 * math.pi)) - tail * t) * decay
    return jnp.where(value >= number(0.0), number(1.0) + part, -part)


def over(index, size):
    return lax.shift_right_logical(index, jnp.int32(size.bit_length() - 1))


def within(index, size):
    return jnp.bitwise_and(index, jnp.int32(size - 1))


def fill_z(base, table):
    rows_z, lanes = base.shape
    owner = within(lax.broadcasted_iota(jnp.int32, (rows_z, lanes), 1), GROUP)
    values = base[...]
    for c in range(GROUP):
        table[c * rows_z : (c + 1) * rows_z] = jnp.where(owner == c, values, 0.0).astype(BF16)


def fill_z_back(base, table):
    lanes, rows_z = base.shape
    owner = within(lax.broadcasted_iota(jnp.int32, (lanes, rows_z), 0), GROUP)
    values = base[...]
    for c in range(GROUP):
        first = c % SLOTS * rows_z
        table[c // SLOTS, :, first : first + rows_z] = jnp.where(owner == c, values, 0.0).astype(BF16)


def grouped(lane, per, channels):
    c = within(lane, channels)
    return over(c, GROUP) * (MZ * GROUP) + over(lane, channels) * GROUP + within(c, GROUP)


def fill_order(per, channels, back, table):
    count = table.shape[0]
    row = lax.broadcasted_iota(jnp.int32, (count, count), 0)
    column = lax.broadcasted_iota(jnp.int32, (count, count), 1)
    if back:
        same = grouped(row[:, :1], per, channels) == column
    else:
        same = row == grouped(column[:1], per, channels)
    table[...] = jnp.where(same, 1.0, 0.0).astype(BF16)


def deliver(spectra, ytab, order, scale, message, per, channels):
    groups = channels // GROUP
    rows = spectra.shape[0] // groups
    wide = spectra.shape[1] // 2
    halves = []
    for r in range(2):
        blocks = [spectra[g * rows : (g + 1) * rows, r * wide : (r + 1) * wide] for g in range(groups)]
        halves.append(jnp.concatenate(blocks, axis=1).astype(BF16))
    planes = dot(ytab[...], jnp.concatenate(halves, axis=0))
    if scale is not None:
        planes = planes * scale[...]
    ordered = dot(planes.astype(BF16), order[...]).astype(BF16)
    parts = MZ // per
    count = message.shape[1]
    lanes = per * channels
    for part in range(parts):
        block = ordered[:, part * lanes : (part + 1) * lanes]
        for j in range(MY):
            message[j * parts + part] = block[j * count : (j + 1) * count]


def receive(message, order_back, ytab_back, scale, held, per):
    parts = MZ // per
    blocks = message[...]
    blocks = blocks.reshape(MY, parts, *blocks.shape[1:])
    lanes = [blocks[:, part].reshape(-1, blocks.shape[3]) for part in range(parts)]
    ordered = dot(jnp.concatenate(lanes, axis=1), order_back[...]).astype(BF16)
    lines = dot(ytab_back[...], ordered)
    if scale is not None:
        lines = lines * scale[...]
    lines = lines.astype(BF16)
    rows = lines.shape[0] // 2
    wide = MZ * GROUP
    for group in range(held.shape[0] // rows):
        piece = lines[:, group * wide : (group + 1) * wide]
        held[group * rows : (group + 1) * rows] = jnp.concatenate([piece[:rows], piece[rows:]], axis=1)


class Move:
    def __init__(self, source, target, sems):
        self.source, self.target, self.sems = source, target, sems
        self.groups = target.shape[0] // GROUP

    def copies(self, step):
        for g in range(self.groups):
            run = pl.ds(g * GROUP + step * SLOTS, SLOTS)
            sem = self.sems.at[step * self.groups + g]
            yield pltpu.make_async_copy(self.source.at[run], self.target.at[run], sem)

    def start(self, step):
        for copy in self.copies(step):
            copy.start()

    def wait(self, step):
        for copy in self.copies(step):
            copy.wait()


def start_next(step, moves):
    @pl.when(step + 1 < STEPS)
    def _():
        for each in moves:
            each.start(step + 1)


def add_spectra(field, ztab, step, spectra):
    groups = field.shape[0] // GROUP
    rows_z = field.shape[-1]
    rows = spectra.shape[0] // groups
    depth = SLOTS * rows_z
    table = ztab[pl.ds(pl.multiple_of(step * depth, depth), depth)]
    lanes = [
        jnp.concatenate(
            [field[g * GROUP + step * SLOTS + slot].reshape(rows, rows_z) for g in range(groups)], axis=0
        )
        for slot in range(SLOTS)
    ]
    spectra[...] += dot(jnp.concatenate(lanes, axis=1), table)


def plane_kernel(per, channels, field, base, ytab, message, ztab, order, spectra, buffer, sems):
    incoming = Move(field.at[0], buffer, sems)
    incoming.start(0)
    fill_z(base, ztab)
    fill_order(per, channels, False, order)
    spectra[...] = jnp.zeros_like(spectra)

    @pl.loop(0, STEPS)
    def _(step):
        start_next(step, [incoming])
        incoming.wait(step)
        add_spectra(buffer, ztab, step, spectra)

    deliver(spectra, ytab, order, None, message, per, channels)


def slope_kernel(
    per, channels, arrived, local, cotangent, base, base_back, ytab, ytab_back, scale,
    slope, message, ztab, ztab_back, order, held, spectra, local_in, cotangent_in, result, first_sum, second_sum,
    local_sems, cotangent_sems, result_sems,
):
    width, rows_y, rows_z = local.shape[1:]
    groups = channels // GROUP
    rows = width * rows_y
    wide = 2 * rows_y
    incoming = (Move(local, local_in, local_sems), Move(cotangent.at[0], cotangent_in, cotangent_sems))
    outgoing = Move(result, slope, result_sems)
    for each in incoming:
        each.start(0)
    fill_order(per, channels, True, order)
    receive(arrived, order, ytab_back, scale, held, per)
    fill_z_back(base_back, ztab_back)
    fill_z(base, ztab)
    fill_order(per, channels, False, order)
    spectra[...] = jnp.zeros_like(spectra)

    @pl.loop(0, STEPS)
    def _(step):
        start_next(step, incoming)
        for each in incoming:
            each.wait(step)
        for pair, total in enumerate((first_sum, second_sum)):
            total[...] = dot(held[...], ztab_back[step, :, 2 * pair * rows_z : 2 * (pair + 1) * rows_z])
        for pair, total in enumerate((first_sum, second_sum)):
            for g in range(groups):
                for offset in range(2):
                    c = g * GROUP + step * SLOTS + 2 * pair + offset
                    for x in range(0, width, 2):
                        place = g * rows + x * rows_y
                        value = total[place : place + wide, offset * rows_z : (offset + 1) * rows_z]
                        value = value + local_in[c, x : x + 2].reshape(wide, rows_z).astype(F32)
                        upstream = cotangent_in[c, x : x + 2].reshape(wide, rows_z)
                        answer = upstream * gelu_slope_rows(value)
                        result[c, x : x + 2] = answer.reshape(2, rows_y, rows_z)
        outgoing.start(step)
        add_spectra(result, ztab, step, spectra)

    deliver(spectra, ytab, order, scale, message, per, channels)
    for step in range(STEPS):
        outgoing.wait(step)


def field_kernel(
    per, channels, arrived, local, base_back, ytab_back, out, ztab_back, order, held, local_in, result,
    local_sems, result_sems,
):
    width, rows_y, rows_z = local.shape[1:]
    groups = channels // GROUP
    rows = width * rows_y
    incoming = Move(local, local_in, local_sems)
    outgoing = Move(result, out.at[0], result_sems)
    incoming.start(0)
    fill_order(per, channels, True, order)
    receive(arrived, order, ytab_back, None, held, per)
    fill_z_back(base_back, ztab_back)

    @pl.loop(0, STEPS)
    def _(step):
        start_next(step, [incoming])
        incoming.wait(step)
        for pair in range(SLOTS // 2):
            total = dot(held[...], ztab_back[step, :, 2 * pair * rows_z : 2 * (pair + 1) * rows_z])
            for g in range(groups):
                for offset in range(2):
                    c = g * GROUP + step * SLOTS + 2 * pair + offset
                    value = total[g * rows : (g + 1) * rows, offset * rows_z : (offset + 1) * rows_z]
                    value = value + local_in[c].reshape(rows, rows_z).astype(F32)
                    result[c] = value.astype(BF16).reshape(width, rows_y, rows_z)
        outgoing.start(step)

    for step in range(STEPS):
        outgoing.wait(step)


def pointwise_kernel(turned, field, mix, offsets, out, table, shift):
    channels = mix.shape[0]
    width, rows_y, rows_z = field.shape[1:]
    size = channels * TILE

    @pl.when(pl.program_id(0) == 0)
    def _():
        row = over(lax.broadcasted_iota(jnp.int32, (size, channels), 0), TILE)
        column = lax.broadcasted_iota(jnp.int32, (size, channels), 1)
        spread = jnp.where(row == column, 1.0, 0.0).astype(BF16)
        tall = lax.dot_general(
            spread, mix[...], (((1,), (1 if turned else 0,)), ((), ())), preferred_element_type=F32
        ).astype(BF16)
        whole = lax.dot_general(
            tall, spread, (((1,), (1,)), ((), ())), preferred_element_type=F32
        )
        place = within(lax.broadcasted_iota(jnp.int32, (size, size), 0), TILE)
        other = within(lax.broadcasted_iota(jnp.int32, (size, size), 1), TILE)
        table[...] = jnp.where(place == other, whole, 0.0).astype(BF16)
        if offsets is not None:
            for c in range(channels):
                shift[c] = jnp.full((1, rows_z), offsets[c], F32)

    for start in range(0, rows_y, 2 * TILE):
        pieces = [field[:, x, start : start + 2 * TILE, :].astype(F32) for x in range(width)]
        halves = []
        for row in range(0, 2 * TILE, TILE):
            rows = [piece[:, row : row + TILE].reshape(size, rows_z).astype(BF16) for piece in pieces]
            halves.append(dot(table[...], jnp.concatenate(rows, axis=1)))
        for x in range(width):
            values = [
                half[:, x * rows_z : (x + 1) * rows_z].reshape(channels, TILE, rows_z) for half in halves
            ]
            value = jnp.concatenate(values, axis=1)
            if offsets is not None:
                value = value + shift[...]
            out[:, x, start : start + 2 * TILE, :] = value.astype(BF16)


def spread_pair(first, second):
    nothing = jnp.zeros_like(first)
    upper = jnp.concatenate([first, nothing], axis=1)
    lower = jnp.concatenate([nothing, second], axis=1)
    return jnp.concatenate([upper, lower], axis=0)


def low_half(shape):
    return lax.broadcasted_iota(jnp.int32, shape, 1) < shape[1] // 2


def mix_kernel(per, samples, arrived, weights, line, line_back, spec_in, message, held):
    rows = 2 * samples
    lanes = 2 * weights.shape[1]
    low = low_half((samples, lanes))
    flat = arrived[...].reshape(-1, arrived.shape[2])
    spectra = dot(line[...], flat).astype(BF16)
    spec_in[...] = spectra
    for q in range(MX):
        for first in range(0, per, 2):
            block = spread_pair(weights[first * MX + q], weights[(first + 1) * MX + q])
            place = first // 2 * lanes
            terms = dot(spectra[q * rows : (q + 1) * rows, place : place + lanes], block)
            mixed = []
            for side in range(2):
                part = terms[:, side * lanes : (side + 1) * lanes]
                turned = pltpu.roll(part[samples:], lanes // 2, 1)
                mixed.append(part[:samples] + jnp.where(low, -turned, turned))
            real = jnp.where(low, mixed[0], pltpu.roll(mixed[1], lanes // 2, 1))
            imag = jnp.where(low, pltpu.roll(mixed[0], lanes // 2, 1), mixed[1])
            held[q * rows : (q + 1) * rows, place : place + lanes] = jnp.concatenate(
                [real, imag], axis=0
            ).astype(BF16)
    message[...] = dot(line_back[...], held[...]).astype(BF16).reshape(message.shape)


def mix_back_kernel(per, samples, arrived, weights, line, line_back, pairs, message, held):
    rows = 2 * samples
    lanes = 2 * weights.shape[1]
    low = low_half((samples, lanes))
    flat = arrived[...].reshape(-1, arrived.shape[2])
    spectra = dot(line[...], flat).astype(BF16).astype(F32)
    for q in range(MX):
        for first in range(0, per, 2):
            block = spread_pair(weights[first * MX + q], weights[(first + 1) * MX + q])
            place = first // 2 * lanes
            real = spectra[q * rows : q * rows + samples, place : place + lanes]
            imag = spectra[q * rows + samples : (q + 1) * rows, place : place + lanes]
            real_turned = pltpu.roll(real, lanes // 2, 1)
            imag_turned = pltpu.roll(imag, lanes // 2, 1)
            left = [jnp.where(low, real, imag_turned), jnp.where(low, imag, -real_turned)]
            right = [jnp.where(low, real_turned, imag), jnp.where(low, imag_turned, -real)]
            pair = jnp.concatenate(
                [jnp.concatenate(left, axis=0), jnp.concatenate(right, axis=0)], axis=1
            ).astype(BF16)
            pairs[q * rows : (q + 1) * rows, 2 * place : 2 * (place + lanes)] = pair
            held[q * rows : (q + 1) * rows, place : place + lanes] = lax.dot_general(
                pair, block, (((1,), (1,)), ((), ())), preferred_element_type=F32
            ).astype(BF16)
    message[...] = dot(line_back[...], held[...]).astype(BF16).reshape(message.shape)


def weight_kernel(per, samples, spec_in, pairs, out):
    rows = 2 * samples
    lanes = out.shape[2]
    half = lanes // 2
    for q in range(MX):
        for first in range(0, per, 2):
            place = first // 2 * lanes
            left = spec_in[q * rows : (q + 1) * rows, place : place + lanes]
            right = pairs[q * rows : (q + 1) * rows, 2 * place : 2 * (place + lanes)]
            outer = lax.dot_general(
                left, right, (((0,), (0,)), ((), ())), preferred_element_type=F32
            )
            out[first * MX + q] = outer[:half, :lanes]
            out[(first + 1) * MX + q] = outer[half:, lanes:]


def whole(array):
    return pl.BlockSpec(array.shape, lambda *step: (0,) * len(array.shape))


def shaped(shape, dtype):
    return jax.ShapeDtypeStruct(shape, dtype)


def params(mib):
    return pltpu.CompilerParams(vmem_limit_bytes=mib * MIB)


def cost(flops, moved, steep=0):
    return pl.CostEstimate(flops=flops, bytes_accessed=moved, transcendentals=steep)


def body(mesh_axes, devices, slabs, activations, cotangent, mode_weights, pointwise, offsets):
    _, channels, width, rows_y, rows_z = activations.shape
    samples = devices // slabs
    per = MY * MZ // devices
    groups = channels // GROUP
    field = activations.shape[1:]
    count = math.prod(field)
    base = z_base(rows_z)
    ytab = y_table(rows_y, width)
    line_fwd, line_inv = x_tables(samples, slabs, NX)
    weight = np.where(np.arange(MZ) == 0, 1.0, 2.0) / (rows_y * rows_z)
    scale = np.tile(np.repeat(weight, GROUP), groups).astype(np.float32)[None]
    base_t, ytab_t = (np.ascontiguousarray(t.T) for t in (base, ytab))
    fwd_t, inv_t = (np.ascontiguousarray(t.T) for t in (line_fwd, line_inv))
    message = shaped((devices, 2 * width, per * channels), BF16)
    spectra = shaped((MX * 2 * samples, per * channels), BF16)
    ztab = pltpu.VMEM((GROUP * rows_z, 2 * MZ * GROUP), BF16)
    ztab_t = pltpu.VMEM((STEPS, 2 * MZ * GROUP, SLOTS * rows_z), BF16)
    order = pltpu.VMEM((MZ * channels, MZ * channels), BF16)
    rows = groups * width * rows_y
    held = pltpu.VMEM((rows, 2 * MZ * GROUP), BF16)
    sums = pltpu.VMEM((rows, 2 * MZ * GROUP), F32)
    pair_sums = pltpu.VMEM((rows, 2 * rows_z), F32)
    buffer = pltpu.VMEM(field, BF16)
    sems = pltpu.SemaphoreType.DMA((STEPS * groups,))
    far = pl.BlockSpec(memory_space=pltpu.HBM)
    plane_flops = 2 * count * 2 * MZ * GROUP

    def exchange(array):
        return lax.all_to_all(array, mesh_axes, split_axis=0, concat_axis=0, tiled=True)

    def mix_points(values, turned, shifts):
        step = 2
        block = pl.BlockSpec((channels, step, rows_y, rows_z), lambda x: (0, x, 0, 0))
        kernel = functools.partial(pointwise_kernel, turned)
        specs = [block, whole(pointwise)]
        operands = [values, pointwise]
        if shifts is None:
            run = lambda a, b, *rest: kernel(a, b, None, *rest)
        else:
            run = kernel
            specs.append(pl.BlockSpec(memory_space=pltpu.SMEM))
            operands.append(shifts)
        return pl.pallas_call(
            run,
            grid=(width // step,),
            in_specs=specs,
            out_specs=block,
            out_shape=shaped(field, BF16),
            scratch_shapes=[
                pltpu.VMEM((channels * TILE, channels * TILE), BF16),
                pltpu.VMEM((channels, 1, rows_z), F32),
            ],
            compiler_params=params(55),
            cost_estimate=cost(2 * count * channels * TILE, 4 * count),
        )(*operands)

    planes = pl.pallas_call(
        functools.partial(plane_kernel, per, channels),
        in_specs=[far, whole(base), whole(ytab)],
        out_specs=whole(message),
        out_shape=message,
        scratch_shapes=[ztab, order, sums, buffer, sems],
        compiler_params=params(55),
        cost_estimate=cost(plane_flops, 2 * count),
    )(activations, base, ytab)
    arrived = exchange(planes)
    local = mix_points(activations.reshape(field), True, offsets)
    arrived, local = lax.optimization_barrier((arrived, local))
    spec_in, mixed = pl.pallas_call(
        functools.partial(mix_kernel, per, samples),
        out_shape=(spectra, message),
        scratch_shapes=[pltpu.VMEM(spectra.shape, BF16)],
        compiler_params=params(16),
        cost_estimate=cost(10**8, 2 * mode_weights.size),
    )(arrived, mode_weights, line_fwd, inv_t)
    returned = exchange(mixed)
    slope, back_plane = pl.pallas_call(
        functools.partial(slope_kernel, per, channels),
        in_specs=[whole(message), far, far]
        + [whole(t) for t in (base, base_t, ytab, ytab_t, scale)],
        out_specs=(far, whole(message)),
        out_shape=(shaped(field, BF16), message),
        scratch_shapes=[ztab, ztab_t, order, held, sums] + [buffer] * 3 + [pair_sums] * 2 + [sems] * 3,
        compiler_params=params(55),
        cost_estimate=cost(2 * plane_flops, 6 * count, 2 * count),
    )(returned, local, cotangent, base, base_t, ytab, ytab_t, scale)
    arrived_back = exchange(back_plane)
    local_back = mix_points(slope, False, None)
    arrived_back, local_back = lax.optimization_barrier((arrived_back, local_back))
    pairs, mixed_back = pl.pallas_call(
        functools.partial(mix_back_kernel, per, samples),
        out_shape=(shaped((spectra.shape[0], 2 * spectra.shape[1]), BF16), message),
        scratch_shapes=[pltpu.VMEM(spectra.shape, BF16)],
        compiler_params=params(16),
        cost_estimate=cost(10**8, 2 * mode_weights.size),
    )(arrived_back, mode_weights, line_inv, fwd_t)
    returned_back = exchange(mixed_back)
    grad_spectral = pl.pallas_call(
        functools.partial(weight_kernel, per, samples),
        out_shape=shaped(mode_weights.shape, F32),
        compiler_params=params(16),
        cost_estimate=cost(10**8, 4 * mode_weights.size),
    )(spec_in, pairs)
    grad_in = pl.pallas_call(
        functools.partial(field_kernel, per, channels),
        in_specs=[whole(message), far, whole(base_t), whole(ytab_t)],
        out_specs=far,
        out_shape=shaped(activations.shape, BF16),
        scratch_shapes=[ztab_t, order, held, buffer, buffer, sems, sems],
        compiler_params=params(55),
        cost_estimate=cost(plane_flops, 4 * count),
    )(returned_back, local_back, base_t, ytab_t)
    return (grad_in, grad_spectral)


def chosen_body(mesh_axes, devices, slabs, activations, cotangent, mode_weights, pointwise, offsets):
    samples, channels, width, rows_y, rows_z = activations.shape
    per = MY * MZ // devices
    fits = (
        samples == 1
        and MY * MZ % devices == 0
        and per in (2, 4, 8)
        and width % 8 == 0
        and channels == 64
        and rows_y % TILE == 0
        and rows_z == 128
    )
    plan = functools.partial(body, mesh_axes, devices, slabs) if fits else general_body
    return plan(activations, cotangent, mode_weights, pointwise, offsets)


def solution(mesh):
    slabs = mesh.shape["space"]
    devices = slabs * mesh.shape["dp"]
    return jax.shard_map(
        functools.partial(chosen_body, ("space", "dp"), devices, slabs),
        mesh=mesh,
        in_specs=(
            P("dp", None, "space", None, None),
            P("dp", None, "space", None, None),
            P(("space", "dp"), None, None),
            P(),
            P(),
        ),
        out_specs=(P("dp", None, "space", None, None), P(("space", "dp"), None, None)),
        check_vma=False,
    )
```

```python
import functools
import math

import jax
import jax.numpy as jnp
import ml_dtypes
import numpy as np
from jax import lax
from jax.experimental import pallas as pl
from jax.experimental.pallas import tpu as pltpu
from jax.sharding import PartitionSpec as P

MX = 16
MY = 16
MZ = 8
NX = 32


def centered(count):
    index = jnp.arange(count, dtype=jnp.int32)
    return jnp.where(index < count // 2, index, index - count)


def plane_tables(rows_y, rows_z, modes_y, modes_z):
    along_y = jnp.arange(rows_y, dtype=jnp.int32)[:, None, None, None]
    along_z = jnp.arange(rows_z, dtype=jnp.int32)[None, :, None, None]
    freq_y = centered(modes_y)[None, None, :, None]
    freq_z = jnp.arange(modes_z, dtype=jnp.int32)[None, None, None, :]
    phase = jnp.mod(freq_y * along_y * rows_z + freq_z * along_z * rows_y, rows_y * rows_z)
    theta = phase.astype(jnp.float32) * (2.0 * math.pi / (rows_y * rows_z))
    cosine = jnp.cos(theta)
    sine = jnp.sin(theta)
    forward = jnp.stack([cosine, -sine], -1).reshape(rows_y * rows_z, modes_y * modes_z * 2)
    scaled = jnp.where(freq_z == 0, 1.0, 2.0).astype(jnp.float32) / (rows_y * rows_z)
    inverse = (
        jnp.stack([cosine * scaled, -sine * scaled], -1)
        .reshape(rows_y * rows_z, modes_y * modes_z * 2)
        .T
    )
    return (forward.astype(jnp.bfloat16), inverse.astype(jnp.bfloat16))


def line_tables(length, modes):
    along = jnp.arange(length, dtype=jnp.int32)[:, None]
    freq = centered(modes)[None, :]
    phase = jnp.mod(freq * along, length)
    theta = phase.astype(jnp.float32) * (2.0 * math.pi / length)
    cosine = jnp.cos(theta)
    sine = jnp.sin(theta)
    first = jnp.stack([cosine, -sine], -1)
    second = jnp.stack([sine, cosine], -1)
    forward = jnp.stack([first, second], 1).reshape(2 * length, 2 * modes)
    inv_first = jnp.stack([cosine.T, sine.T], -1) / length
    inv_second = jnp.stack([-sine.T, cosine.T], -1) / length
    inverse = jnp.stack([inv_first, inv_second], 1).reshape(2 * modes, 2 * length)
    return (forward.astype(jnp.bfloat16), inverse.astype(jnp.bfloat16))


def expand_weights(weights):
    half = weights.shape[1]
    real_part = weights[:, :, :half]
    imag_part = weights[:, :, half:]
    upper = jnp.concatenate([real_part, imag_part], axis=2)
    lower = jnp.concatenate([-imag_part, real_part], axis=2)
    return jnp.concatenate([upper, lower], axis=1)


def outer_sum(left, right):
    return jnp.einsum("mbi,mbo->mio", left, right, preferred_element_type=jnp.float32)


def weight_terms(spec_in, spec_grad):
    half = spec_in.shape[2] // 2
    in_real = spec_in[:, :, :half]
    in_imag = spec_in[:, :, half:]
    gr_real = spec_grad[:, :, :half]
    gr_imag = spec_grad[:, :, half:]
    real_term = outer_sum(in_real, gr_real) + outer_sum(in_imag, gr_imag)
    imag_term = outer_sum(in_real, gr_imag) - outer_sum(in_imag, gr_real)
    return jnp.concatenate([real_term, imag_term], axis=2)


def to_modes(slab, table, modes_x):
    samples, channels, width, pairs = slab.shape
    moved = lax.all_to_all(slab, "space", split_axis=3, concat_axis=2, tiled=True)
    length = moved.shape[2]
    local = moved.shape[3] // 2
    lines = moved.reshape(samples, channels, length, local, 2).transpose(0, 1, 3, 2, 4)
    lines = lines.reshape(samples, channels, local, 2 * length)
    spectra = jnp.dot(lines, table, preferred_element_type=jnp.float32).astype(jnp.bfloat16)
    spectra = spectra.reshape(samples, channels, local, modes_x, 2).transpose(2, 3, 0, 4, 1)
    return spectra.reshape(local * modes_x, samples, 2 * channels)


def to_slab(spectra, table, modes_x, channels):
    count, samples, doubled = spectra.shape
    local = count // modes_x
    lines = spectra.reshape(local, modes_x, samples, 2, channels).transpose(2, 4, 0, 1, 3)
    lines = lines.reshape(samples, channels, local, 2 * modes_x)
    lines = jnp.dot(lines, table, preferred_element_type=jnp.float32).astype(jnp.bfloat16)
    length = lines.shape[3] // 2
    lines = lines.reshape(samples, channels, local, length, 2).transpose(0, 1, 3, 2, 4)
    lines = lines.reshape(samples, channels, length, 2 * local)
    return lax.all_to_all(lines, "space", split_axis=2, concat_axis=3, tiled=True)


def to_owners(spectra):
    return lax.all_to_all(spectra, "dp", split_axis=0, concat_axis=1, tiled=True)


def from_owners(spectra):
    return lax.all_to_all(spectra, "dp", split_axis=1, concat_axis=0, tiled=True)


def gelu_slope(value):
    cdf = 0.5 * (1.0 + lax.erf(value * 0.7071067811865476))
    density = jnp.exp(-0.5 * value * value) * 0.3989422804014327
    return cdf + value * density


def general_body(activations, cotangent, mode_weights, pointwise, offsets):
    samples, channels, width, rows_y, rows_z = activations.shape
    plane_fwd, plane_inv = plane_tables(rows_y, rows_z, MY, MZ)
    line_fwd, line_inv = line_tables(NX, MX)
    flat = activations.reshape(samples, channels, width, rows_y * rows_z)
    planes = jnp.dot(flat, plane_fwd, preferred_element_type=jnp.float32).astype(jnp.bfloat16)
    spec_in = to_modes(planes, line_fwd, MX)
    blocks = expand_weights(mode_weights)
    held_in = to_owners(spec_in)
    held_out = jnp.einsum(
        "mbi,mio->mbo", held_in, blocks, preferred_element_type=jnp.float32
    ).astype(jnp.bfloat16)
    spec_out = from_owners(held_out)
    returned = to_slab(spec_out, line_inv, MX, channels)
    spectral = jnp.dot(returned, plane_inv, preferred_element_type=jnp.float32)
    local_part = jnp.einsum("io,bixn->boxn", pointwise, flat, preferred_element_type=jnp.float32)
    summed = spectral + local_part + offsets[None, :, None, None]
    upstream = cotangent.reshape(flat.shape).astype(jnp.float32)
    slope_grad = (upstream * gelu_slope(summed)).astype(jnp.bfloat16)
    back_plane = jnp.dot(slope_grad, plane_inv.T, preferred_element_type=jnp.float32).astype(
        jnp.bfloat16
    )
    spec_grad = to_modes(back_plane, line_inv.T, MX)
    held_grad = to_owners(spec_grad)
    held_dx = jnp.einsum(
        "mbo,mio->mbi", held_grad, blocks, preferred_element_type=jnp.float32
    ).astype(jnp.bfloat16)
    spec_dx = from_owners(held_dx)
    grad_spectral = weight_terms(held_in, held_grad)
    line_dx = to_slab(spec_dx, line_fwd.T, MX, channels)
    total = jnp.dot(line_dx, plane_fwd.T, preferred_element_type=jnp.float32)
    total = total + jnp.einsum(
        "io,boxn->bixn", pointwise, slope_grad, preferred_element_type=jnp.float32
    )
    grad_in = total.astype(jnp.bfloat16).reshape(activations.shape)
    return (grad_in, grad_spectral)


BF16 = jnp.bfloat16
F32 = jnp.float32
GROUP = 16
TILE = 8
SLOTS = 4
STEPS = GROUP // SLOTS
MIB = 1024 * 1024


def rounded(table):
    return np.asarray(table, np.float32).astype(ml_dtypes.bfloat16)


def angles(freq, points, length):
    phase = np.mod(np.outer(freq, points), length)
    return (phase * (2.0 * math.pi / length)).astype(np.float64)


def signed(count):
    index = np.arange(count)
    return np.where(index < count // 2, index, index - count)


def z_base(rows_z):
    theta = angles(np.arange(MZ), np.arange(rows_z), rows_z)
    pair = np.stack([np.cos(theta), -np.sin(theta)])
    table = np.repeat(pair.reshape(2 * MZ, rows_z), GROUP, axis=0).T
    return rounded(table).astype(np.float32)


def y_table(rows_y, width):
    theta = angles(signed(MY), np.arange(rows_y), rows_y)
    cosine, sine = np.cos(theta), np.sin(theta)
    turn = np.stack([np.stack([cosine, sine]), np.stack([-sine, cosine])])
    table = np.einsum("rsjy,xw->jxrswy", turn, np.eye(width))
    return rounded(table.reshape(MY * width * 2, 2 * width * rows_y))


def x_tables(samples, slabs, length):
    theta = angles(signed(MX), np.arange(length), length)
    cosine, sine = np.cos(theta), np.sin(theta)
    forward = np.stack([np.stack([cosine, sine]), np.stack([-sine, cosine])])
    inverse = np.stack([np.stack([cosine, sine]), np.stack([-sine, cosine])]) / length
    same = np.eye(samples)
    rows = MX * 2 * samples

    def lay(turn):
        turn = turn.reshape(2, 2, MX, slabs, length // slabs)
        table = np.einsum("arqsx,bd->qabsdxr", turn, same)
        return rounded(table.reshape(rows, samples * length * 2))

    return lay(forward), lay(inverse)


def dot(left, right):
    return jnp.dot(left, right, preferred_element_type=F32)


def gelu_slope_rows(value):
    decay = jnp.exp2(value * value * (-0.5 * math.log2(math.e))).astype(BF16)
    cdf = (0.5 + 0.5 * lax.erf(value * math.sqrt(0.5))).astype(BF16)
    density = value.astype(BF16) * jnp.asarray(1.0 / math.sqrt(2.0 * math.pi), BF16)
    return cdf + density * decay


def over(index, size):
    return lax.shift_right_logical(index, jnp.int32(size.bit_length() - 1))


def within(index, size):
    return jnp.bitwise_and(index, jnp.int32(size - 1))


def fill_z(base, table):
    rows_z, lanes = base.shape
    owner = within(lax.broadcasted_iota(jnp.int32, (rows_z, lanes), 1), GROUP)
    values = base[...]
    for c in range(GROUP):
        table[c * rows_z : (c + 1) * rows_z] = jnp.where(owner == c, values, 0.0).astype(BF16)


def fill_z_back(base, table):
    lanes, rows_z = base.shape
    owner = within(lax.broadcasted_iota(jnp.int32, (lanes, rows_z), 0), GROUP)
    values = base[...]
    for c in range(GROUP):
        first = c % SLOTS * rows_z
        table[c // SLOTS, :, first : first + rows_z] = jnp.where(owner == c, values, 0.0).astype(BF16)


def grouped(lane, per, channels):
    c = within(lane, channels)
    return over(c, GROUP) * (MZ * GROUP) + over(lane, channels) * GROUP + within(c, GROUP)


def fill_order(per, channels, back, table):
    count = table.shape[0]
    row = lax.broadcasted_iota(jnp.int32, (count, count), 0)
    column = lax.broadcasted_iota(jnp.int32, (count, count), 1)
    if back:
        same = grouped(row[:, :1], per, channels) == column
    else:
        same = row == grouped(column[:1], per, channels)
    table[...] = jnp.where(same, 1.0, 0.0).astype(BF16)


def deliver(spectra, ytab, order, scale, message, per, channels):
    groups = channels // GROUP
    rows = spectra.shape[0] // groups
    wide = spectra.shape[1] // 2
    halves = []
    for r in range(2):
        blocks = [spectra[g * rows : (g + 1) * rows, r * wide : (r + 1) * wide] for g in range(groups)]
        halves.append(jnp.concatenate(blocks, axis=1).astype(BF16))
    planes = dot(ytab[...], jnp.concatenate(halves, axis=0))
    if scale is not None:
        planes = planes * scale[...]
    ordered = dot(planes.astype(BF16), order[...]).astype(BF16)
    parts = MZ // per
    count = message.shape[1]
    lanes = per * channels
    for part in range(parts):
        block = ordered[:, part * lanes : (part + 1) * lanes]
        for j in range(MY):
            message[j * parts + part] = block[j * count : (j + 1) * count]


def receive(message, order_back, ytab_back, scale, held, per):
    parts = MZ // per
    blocks = message[...]
    blocks = blocks.reshape(MY, parts, *blocks.shape[1:])
    lanes = [blocks[:, part].reshape(-1, blocks.shape[3]) for part in range(parts)]
    ordered = dot(jnp.concatenate(lanes, axis=1), order_back[...]).astype(BF16)
    lines = dot(ytab_back[...], ordered)
    if scale is not None:
        lines = lines * scale[...]
    lines = lines.astype(BF16)
    rows = lines.shape[0] // 2
    wide = MZ * GROUP
    for group in range(held.shape[0] // rows):
        piece = lines[:, group * wide : (group + 1) * wide]
        held[group * rows : (group + 1) * rows] = jnp.concatenate([piece[:rows], piece[rows:]], axis=1)


class Move:
    def __init__(self, source, target, sems):
        self.source, self.target, self.sems = source, target, sems
        self.groups = target.shape[0] // GROUP

    def copies(self, step):
        for g in range(self.groups):
            run = pl.ds(g * GROUP + step * SLOTS, SLOTS)
            sem = self.sems.at[step * self.groups + g]
            yield pltpu.make_async_copy(self.source.at[run], self.target.at[run], sem)

    def start(self, step):
        for copy in self.copies(step):
            copy.start()

    def wait(self, step):
        for copy in self.copies(step):
            copy.wait()


def start_all(moves, step):
    for each in moves:
        each.start(step)


def add_spectra(field, ztab, step, spectra):
    groups = field.shape[0] // GROUP
    rows_z = field.shape[-1]
    rows = spectra.shape[0] // groups
    depth = SLOTS * rows_z
    table = ztab[pl.ds(pl.multiple_of(step * depth, depth), depth)]
    lanes = [
        jnp.concatenate(
            [field[g * GROUP + step * SLOTS + slot].reshape(rows, rows_z) for g in range(groups)], axis=0
        )
        for slot in range(SLOTS)
    ]
    spectra[...] += dot(jnp.concatenate(lanes, axis=1), table)


def plane_kernel(per, channels, field, base, ytab, message, ztab, order, spectra, buffer, sems):
    incoming = Move(field.at[0], buffer, sems)
    incoming.start(0)
    fill_z(base, ztab)
    incoming.start(1)
    fill_order(per, channels, False, order)
    incoming.start(2)
    spectra[...] = jnp.zeros_like(spectra)
    incoming.start(3)

    @pl.loop(0, STEPS)
    def _(step):
        incoming.wait(step)
        add_spectra(buffer, ztab, step, spectra)

    deliver(spectra, ytab, order, None, message, per, channels)


def slope_kernel(
    per, channels, arrived, local, cotangent, base, base_back, ytab, ytab_back, scale,
    slope, message, ztab, ztab_back, order, held, spectra, local_in, cotangent_in, result, first_sum, second_sum,
    local_sems, cotangent_sems, result_sems,
):
    width, rows_y, rows_z = local.shape[1:]
    groups = channels // GROUP
    rows = width * rows_y
    wide = 2 * rows_y
    incoming = (Move(local, local_in, local_sems), Move(cotangent.at[0], cotangent_in, cotangent_sems))
    outgoing = Move(result, slope, result_sems)
    start_all(incoming, 0)
    fill_order(per, channels, True, order)
    receive(arrived, order, ytab_back, scale, held, per)
    start_all(incoming, 1)
    fill_z_back(base_back, ztab_back)
    fill_z(base, ztab)
    start_all(incoming, 2)
    fill_order(per, channels, False, order)
    spectra[...] = jnp.zeros_like(spectra)
    start_all(incoming, 3)

    @pl.loop(0, STEPS)
    def _(step):
        for each in incoming:
            each.wait(step)
        for pair, total in enumerate((first_sum, second_sum)):
            total[...] = dot(held[...], ztab_back[step, :, 2 * pair * rows_z : 2 * (pair + 1) * rows_z])
        for pair, total in enumerate((first_sum, second_sum)):
            for g in range(groups):
                for offset in range(2):
                    c = g * GROUP + step * SLOTS + 2 * pair + offset
                    for x in range(0, width, 2):
                        place = g * rows + x * rows_y
                        value = total[place : place + wide, offset * rows_z : (offset + 1) * rows_z]
                        value = value + local_in[c, x : x + 2].reshape(wide, rows_z).astype(F32)
                        upstream = cotangent_in[c, x : x + 2].reshape(wide, rows_z)
                        answer = upstream * gelu_slope_rows(value)
                        result[c, x : x + 2] = answer.reshape(2, rows_y, rows_z)
        outgoing.start(step)
        add_spectra(result, ztab, step, spectra)

    deliver(spectra, ytab, order, scale, message, per, channels)
    for step in range(STEPS):
        outgoing.wait(step)


def field_kernel(
    per, channels, arrived, local, base_back, ytab_back, out, ztab_back, order, held, local_in, result,
    local_sems, result_sems,
):
    width, rows_y, rows_z = local.shape[1:]
    groups = channels // GROUP
    rows = width * rows_y
    incoming = Move(local, local_in, local_sems)
    outgoing = Move(result, out.at[0], result_sems)
    incoming.start(0)
    fill_order(per, channels, True, order)
    incoming.start(1)
    receive(arrived, order, ytab_back, None, held, per)
    incoming.start(2)
    fill_z_back(base_back, ztab_back)
    incoming.start(3)

    @pl.loop(0, STEPS)
    def _(step):
        incoming.wait(step)
        for pair in range(SLOTS // 2):
            total = dot(held[...], ztab_back[step, :, 2 * pair * rows_z : 2 * (pair + 1) * rows_z])
            for g in range(groups):
                for offset in range(2):
                    c = g * GROUP + step * SLOTS + 2 * pair + offset
                    value = total[g * rows : (g + 1) * rows, offset * rows_z : (offset + 1) * rows_z]
                    value = value + local_in[c].reshape(rows, rows_z).astype(F32)
                    result[c] = value.astype(BF16).reshape(width, rows_y, rows_z)
        outgoing.start(step)

    for step in range(STEPS):
        outgoing.wait(step)


def pointwise_kernel(turned, field, mix, offsets, out, table, shift):
    channels = mix.shape[0]
    width, rows_y, rows_z = field.shape[1:]
    size = channels * TILE

    @pl.when(pl.program_id(0) == 0)
    def _():
        row = over(lax.broadcasted_iota(jnp.int32, (size, channels), 0), TILE)
        column = lax.broadcasted_iota(jnp.int32, (size, channels), 1)
        spread = jnp.where(row == column, 1.0, 0.0).astype(BF16)
        tall = lax.dot_general(
            spread, mix[...], (((1,), (1 if turned else 0,)), ((), ())), preferred_element_type=F32
        ).astype(BF16)
        whole = lax.dot_general(
            tall, spread, (((1,), (1,)), ((), ())), preferred_element_type=F32
        )
        place = within(lax.broadcasted_iota(jnp.int32, (size, size), 0), TILE)
        other = within(lax.broadcasted_iota(jnp.int32, (size, size), 1), TILE)
        table[...] = jnp.where(place == other, whole, 0.0).astype(BF16)
        if offsets is not None:
            for c in range(channels):
                shift[c] = jnp.full((1, rows_z), offsets[c], F32)

    for start in range(0, rows_y, 2 * TILE):
        pieces = [field[:, x, start : start + 2 * TILE, :].astype(F32) for x in range(width)]
        halves = []
        for row in range(0, 2 * TILE, TILE):
            rows = [piece[:, row : row + TILE].reshape(size, rows_z).astype(BF16) for piece in pieces]
            halves.append(dot(table[...], jnp.concatenate(rows, axis=1)))
        for x in range(width):
            values = [
                half[:, x * rows_z : (x + 1) * rows_z].reshape(channels, TILE, rows_z) for half in halves
            ]
            value = jnp.concatenate(values, axis=1)
            if offsets is not None:
                value = value + shift[...]
            out[:, x, start : start + 2 * TILE, :] = value.astype(BF16)


def spread_pair(first, second):
    nothing = jnp.zeros_like(first)
    upper = jnp.concatenate([first, nothing], axis=1)
    lower = jnp.concatenate([nothing, second], axis=1)
    return jnp.concatenate([upper, lower], axis=0)


def low_half(shape):
    return lax.broadcasted_iota(jnp.int32, shape, 1) < shape[1] // 2


def mix_kernel(per, samples, arrived, weights, line, line_back, spec_in, message, held):
    rows = 2 * samples
    lanes = 2 * weights.shape[1]
    low = low_half((samples, lanes))
    flat = arrived[...].reshape(-1, arrived.shape[2])
    spectra = dot(line[...], flat).astype(BF16)
    spec_in[...] = spectra
    for q in range(MX):
        for first in range(0, per, 2):
            block = spread_pair(weights[first * MX + q], weights[(first + 1) * MX + q])
            place = first // 2 * lanes
            terms = dot(spectra[q * rows : (q + 1) * rows, place : place + lanes], block)
            mixed = []
            for side in range(2):
                part = terms[:, side * lanes : (side + 1) * lanes]
                turned = pltpu.roll(part[samples:], lanes // 2, 1)
                mixed.append(part[:samples] + jnp.where(low, -turned, turned))
            real = jnp.where(low, mixed[0], pltpu.roll(mixed[1], lanes // 2, 1))
            imag = jnp.where(low, pltpu.roll(mixed[0], lanes // 2, 1), mixed[1])
            held[q * rows : (q + 1) * rows, place : place + lanes] = jnp.concatenate(
                [real, imag], axis=0
            ).astype(BF16)
    message[...] = dot(line_back[...], held[...]).astype(BF16).reshape(message.shape)


def mix_back_kernel(per, samples, arrived, weights, line, line_back, pairs, message, held):
    rows = 2 * samples
    lanes = 2 * weights.shape[1]
    low = low_half((samples, lanes))
    flat = arrived[...].reshape(-1, arrived.shape[2])
    spectra = dot(line[...], flat).astype(BF16).astype(F32)
    for q in range(MX):
        for first in range(0, per, 2):
            block = spread_pair(weights[first * MX + q], weights[(first + 1) * MX + q])
            place = first // 2 * lanes
            real = spectra[q * rows : q * rows + samples, place : place + lanes]
            imag = spectra[q * rows + samples : (q + 1) * rows, place : place + lanes]
            real_turned = pltpu.roll(real, lanes // 2, 1)
            imag_turned = pltpu.roll(imag, lanes // 2, 1)
            left = [jnp.where(low, real, imag_turned), jnp.where(low, imag, -real_turned)]
            right = [jnp.where(low, real_turned, imag), jnp.where(low, imag_turned, -real)]
            pair = jnp.concatenate(
                [jnp.concatenate(left, axis=0), jnp.concatenate(right, axis=0)], axis=1
            ).astype(BF16)
            pairs[q * rows : (q + 1) * rows, 2 * place : 2 * (place + lanes)] = pair
            held[q * rows : (q + 1) * rows, place : place + lanes] = lax.dot_general(
                pair, block, (((1,), (1,)), ((), ())), preferred_element_type=F32
            ).astype(BF16)
    message[...] = dot(line_back[...], held[...]).astype(BF16).reshape(message.shape)


def weight_kernel(per, samples, spec_in, pairs, out):
    rows = 2 * samples
    lanes = out.shape[2]
    half = lanes // 2
    for q in range(MX):
        for first in range(0, per, 2):
            place = first // 2 * lanes
            left = spec_in[q * rows : (q + 1) * rows, place : place + lanes]
            right = pairs[q * rows : (q + 1) * rows, 2 * place : 2 * (place + lanes)]
            outer = lax.dot_general(
                left, right, (((0,), (0,)), ((), ())), preferred_element_type=F32
            )
            out[first * MX + q] = outer[:half, :lanes]
            out[(first + 1) * MX + q] = outer[half:, lanes:]


def whole(array):
    return pl.BlockSpec(array.shape, lambda *step: (0,) * len(array.shape))


def shaped(shape, dtype):
    return jax.ShapeDtypeStruct(shape, dtype)


def params(mib):
    return pltpu.CompilerParams(vmem_limit_bytes=mib * MIB)


def cost(flops, moved, steep=0):
    return pl.CostEstimate(flops=flops, bytes_accessed=moved, transcendentals=steep)


def body(mesh_axes, devices, slabs, activations, cotangent, mode_weights, pointwise, offsets):
    _, channels, width, rows_y, rows_z = activations.shape
    samples = devices // slabs
    per = MY * MZ // devices
    groups = channels // GROUP
    field = activations.shape[1:]
    count = math.prod(field)
    base = z_base(rows_z)
    ytab = y_table(rows_y, width)
    line_fwd, line_inv = x_tables(samples, slabs, NX)
    weight = np.where(np.arange(MZ) == 0, 1.0, 2.0) / (rows_y * rows_z)
    scale = np.tile(np.repeat(weight, GROUP), groups).astype(np.float32)[None]
    base_t, ytab_t = (np.ascontiguousarray(t.T) for t in (base, ytab))
    fwd_t, inv_t = (np.ascontiguousarray(t.T) for t in (line_fwd, line_inv))
    message = shaped((devices, 2 * width, per * channels), BF16)
    spectra = shaped((MX * 2 * samples, per * channels), BF16)
    ztab = pltpu.VMEM((GROUP * rows_z, 2 * MZ * GROUP), BF16)
    ztab_t = pltpu.VMEM((STEPS, 2 * MZ * GROUP, SLOTS * rows_z), BF16)
    order = pltpu.VMEM((MZ * channels, MZ * channels), BF16)
    rows = groups * width * rows_y
    held = pltpu.VMEM((rows, 2 * MZ * GROUP), BF16)
    sums = pltpu.VMEM((rows, 2 * MZ * GROUP), F32)
    pair_sums = pltpu.VMEM((rows, 2 * rows_z), F32)
    buffer = pltpu.VMEM(field, BF16)
    sems = pltpu.SemaphoreType.DMA((STEPS * groups,))
    far = pl.BlockSpec(memory_space=pltpu.HBM)
    plane_flops = 2 * count * 2 * MZ * GROUP

    def exchange(array):
        return lax.all_to_all(array, mesh_axes, split_axis=0, concat_axis=0, tiled=True)

    def mix_points(values, turned, shifts):
        step = 2
        block = pl.BlockSpec((channels, step, rows_y, rows_z), lambda x: (0, x, 0, 0))
        kernel = functools.partial(pointwise_kernel, turned)
        specs = [block, whole(pointwise)]
        operands = [values, pointwise]
        if shifts is None:
            run = lambda a, b, *rest: kernel(a, b, None, *rest)
        else:
            run = kernel
            specs.append(pl.BlockSpec(memory_space=pltpu.SMEM))
            operands.append(shifts)
        return pl.pallas_call(
            run,
            grid=(width // step,),
            in_specs=specs,
            out_specs=block,
            out_shape=shaped(field, BF16),
            scratch_shapes=[
                pltpu.VMEM((channels * TILE, channels * TILE), BF16),
                pltpu.VMEM((channels, 1, rows_z), F32),
            ],
            compiler_params=params(55),
            cost_estimate=cost(2 * count * channels * TILE, 4 * count),
        )(*operands)

    planes = pl.pallas_call(
        functools.partial(plane_kernel, per, channels),
        in_specs=[far, whole(base), whole(ytab)],
        out_specs=whole(message),
        out_shape=message,
        scratch_shapes=[ztab, order, sums, buffer, sems],
        compiler_params=params(55),
        cost_estimate=cost(plane_flops, 2 * count),
    )(activations, base, ytab)
    arrived = exchange(planes)
    local = mix_points(activations.reshape(field), True, offsets)
    arrived, local = lax.optimization_barrier((arrived, local))
    spec_in, mixed = pl.pallas_call(
        functools.partial(mix_kernel, per, samples),
        out_shape=(spectra, message),
        scratch_shapes=[pltpu.VMEM(spectra.shape, BF16)],
        compiler_params=params(16),
        cost_estimate=cost(10**8, 2 * mode_weights.size),
    )(arrived, mode_weights, line_fwd, inv_t)
    returned = exchange(mixed)
    slope, back_plane = pl.pallas_call(
        functools.partial(slope_kernel, per, channels),
        in_specs=[whole(message), far, far]
        + [whole(t) for t in (base, base_t, ytab, ytab_t, scale)],
        out_specs=(far, whole(message)),
        out_shape=(shaped(field, BF16), message),
        scratch_shapes=[ztab, ztab_t, order, held, sums] + [buffer] * 3 + [pair_sums] * 2 + [sems] * 3,
        compiler_params=params(55),
        cost_estimate=cost(2 * plane_flops, 6 * count, 2 * count),
    )(returned, local, cotangent, base, base_t, ytab, ytab_t, scale)
    arrived_back = exchange(back_plane)
    local_back = mix_points(slope, False, None)
    arrived_back, local_back = lax.optimization_barrier((arrived_back, local_back))
    pairs, mixed_back = pl.pallas_call(
        functools.partial(mix_back_kernel, per, samples),
        out_shape=(shaped((spectra.shape[0], 2 * spectra.shape[1]), BF16), message),
        scratch_shapes=[pltpu.VMEM(spectra.shape, BF16)],
        compiler_params=params(16),
        cost_estimate=cost(10**8, 2 * mode_weights.size),
    )(arrived_back, mode_weights, line_inv, fwd_t)
    returned_back = exchange(mixed_back)
    grad_spectral = pl.pallas_call(
        functools.partial(weight_kernel, per, samples),
        out_shape=shaped(mode_weights.shape, F32),
        compiler_params=params(16),
        cost_estimate=cost(10**8, 4 * mode_weights.size),
    )(spec_in, pairs)
    grad_in = pl.pallas_call(
        functools.partial(field_kernel, per, channels),
        in_specs=[whole(message), far, whole(base_t), whole(ytab_t)],
        out_specs=far,
        out_shape=shaped(activations.shape, BF16),
        scratch_shapes=[ztab_t, order, held, buffer, buffer, sems, sems],
        compiler_params=params(55),
        cost_estimate=cost(plane_flops, 4 * count),
    )(returned_back, local_back, base_t, ytab_t)
    return (grad_in, grad_spectral)


def chosen_body(mesh_axes, devices, slabs, activations, cotangent, mode_weights, pointwise, offsets):
    samples, channels, width, rows_y, rows_z = activations.shape
    per = MY * MZ // devices
    fits = (
        samples == 1
        and MY * MZ % devices == 0
        and per in (2, 4, 8)
        and width % 8 == 0
        and channels == 64
        and rows_y % TILE == 0
        and rows_z == 128
    )
    plan = functools.partial(body, mesh_axes, devices, slabs) if fits else general_body
    return plan(activations, cotangent, mode_weights, pointwise, offsets)


def solution(mesh):
    slabs = mesh.shape["space"]
    devices = slabs * mesh.shape["dp"]
    return jax.shard_map(
        functools.partial(chosen_body, ("space", "dp"), devices, slabs),
        mesh=mesh,
        in_specs=(
            P("dp", None, "space", None, None),
            P("dp", None, "space", None, None),
            P(("space", "dp"), None, None),
            P(),
            P(),
        ),
        out_specs=(P("dp", None, "space", None, None), P(("space", "dp"), None, None)),
        check_vma=False,
    )
```

```python
import functools
import math

import jax
import jax.numpy as jnp
import ml_dtypes
import numpy as np
from jax import lax
from jax.experimental import pallas as pl
from jax.experimental.pallas import tpu as pltpu
from jax.sharding import PartitionSpec as P

MX = 16
MY = 16
MZ = 8
NX = 32


def centered(count):
    index = jnp.arange(count, dtype=jnp.int32)
    return jnp.where(index < count // 2, index, index - count)


def plane_tables(rows_y, rows_z, modes_y, modes_z):
    along_y = jnp.arange(rows_y, dtype=jnp.int32)[:, None, None, None]
    along_z = jnp.arange(rows_z, dtype=jnp.int32)[None, :, None, None]
    freq_y = centered(modes_y)[None, None, :, None]
    freq_z = jnp.arange(modes_z, dtype=jnp.int32)[None, None, None, :]
    phase = jnp.mod(freq_y * along_y * rows_z + freq_z * along_z * rows_y, rows_y * rows_z)
    theta = phase.astype(jnp.float32) * (2.0 * math.pi / (rows_y * rows_z))
    cosine = jnp.cos(theta)
    sine = jnp.sin(theta)
    forward = jnp.stack([cosine, -sine], -1).reshape(rows_y * rows_z, modes_y * modes_z * 2)
    scaled = jnp.where(freq_z == 0, 1.0, 2.0).astype(jnp.float32) / (rows_y * rows_z)
    inverse = (
        jnp.stack([cosine * scaled, -sine * scaled], -1)
        .reshape(rows_y * rows_z, modes_y * modes_z * 2)
        .T
    )
    return (forward.astype(jnp.bfloat16), inverse.astype(jnp.bfloat16))


def line_tables(length, modes):
    along = jnp.arange(length, dtype=jnp.int32)[:, None]
    freq = centered(modes)[None, :]
    phase = jnp.mod(freq * along, length)
    theta = phase.astype(jnp.float32) * (2.0 * math.pi / length)
    cosine = jnp.cos(theta)
    sine = jnp.sin(theta)
    first = jnp.stack([cosine, -sine], -1)
    second = jnp.stack([sine, cosine], -1)
    forward = jnp.stack([first, second], 1).reshape(2 * length, 2 * modes)
    inv_first = jnp.stack([cosine.T, sine.T], -1) / length
    inv_second = jnp.stack([-sine.T, cosine.T], -1) / length
    inverse = jnp.stack([inv_first, inv_second], 1).reshape(2 * modes, 2 * length)
    return (forward.astype(jnp.bfloat16), inverse.astype(jnp.bfloat16))


def expand_weights(weights):
    half = weights.shape[1]
    real_part = weights[:, :, :half]
    imag_part = weights[:, :, half:]
    upper = jnp.concatenate([real_part, imag_part], axis=2)
    lower = jnp.concatenate([-imag_part, real_part], axis=2)
    return jnp.concatenate([upper, lower], axis=1)


def outer_sum(left, right):
    return jnp.einsum("mbi,mbo->mio", left, right, preferred_element_type=jnp.float32)


def weight_terms(spec_in, spec_grad):
    half = spec_in.shape[2] // 2
    in_real = spec_in[:, :, :half]
    in_imag = spec_in[:, :, half:]
    gr_real = spec_grad[:, :, :half]
    gr_imag = spec_grad[:, :, half:]
    real_term = outer_sum(in_real, gr_real) + outer_sum(in_imag, gr_imag)
    imag_term = outer_sum(in_real, gr_imag) - outer_sum(in_imag, gr_real)
    return jnp.concatenate([real_term, imag_term], axis=2)


def to_modes(slab, table, modes_x):
    samples, channels, width, pairs = slab.shape
    moved = lax.all_to_all(slab, "space", split_axis=3, concat_axis=2, tiled=True)
    length = moved.shape[2]
    local = moved.shape[3] // 2
    lines = moved.reshape(samples, channels, length, local, 2).transpose(0, 1, 3, 2, 4)
    lines = lines.reshape(samples, channels, local, 2 * length)
    spectra = jnp.dot(lines, table, preferred_element_type=jnp.float32).astype(jnp.bfloat16)
    spectra = spectra.reshape(samples, channels, local, modes_x, 2).transpose(2, 3, 0, 4, 1)
    return spectra.reshape(local * modes_x, samples, 2 * channels)


def to_slab(spectra, table, modes_x, channels):
    count, samples, doubled = spectra.shape
    local = count // modes_x
    lines = spectra.reshape(local, modes_x, samples, 2, channels).transpose(2, 4, 0, 1, 3)
    lines = lines.reshape(samples, channels, local, 2 * modes_x)
    lines = jnp.dot(lines, table, preferred_element_type=jnp.float32).astype(jnp.bfloat16)
    length = lines.shape[3] // 2
    lines = lines.reshape(samples, channels, local, length, 2).transpose(0, 1, 3, 2, 4)
    lines = lines.reshape(samples, channels, length, 2 * local)
    return lax.all_to_all(lines, "space", split_axis=2, concat_axis=3, tiled=True)


def to_owners(spectra):
    return lax.all_to_all(spectra, "dp", split_axis=0, concat_axis=1, tiled=True)


def from_owners(spectra):
    return lax.all_to_all(spectra, "dp", split_axis=1, concat_axis=0, tiled=True)


def gelu_slope(value):
    cdf = 0.5 * (1.0 + lax.erf(value * 0.7071067811865476))
    density = jnp.exp(-0.5 * value * value) * 0.3989422804014327
    return cdf + value * density


def general_body(activations, cotangent, mode_weights, pointwise, offsets):
    samples, channels, width, rows_y, rows_z = activations.shape
    plane_fwd, plane_inv = plane_tables(rows_y, rows_z, MY, MZ)
    line_fwd, line_inv = line_tables(NX, MX)
    flat = activations.reshape(samples, channels, width, rows_y * rows_z)
    planes = jnp.dot(flat, plane_fwd, preferred_element_type=jnp.float32).astype(jnp.bfloat16)
    spec_in = to_modes(planes, line_fwd, MX)
    blocks = expand_weights(mode_weights)
    held_in = to_owners(spec_in)
    held_out = jnp.einsum(
        "mbi,mio->mbo", held_in, blocks, preferred_element_type=jnp.float32
    ).astype(jnp.bfloat16)
    spec_out = from_owners(held_out)
    returned = to_slab(spec_out, line_inv, MX, channels)
    spectral = jnp.dot(returned, plane_inv, preferred_element_type=jnp.float32)
    local_part = jnp.einsum("io,bixn->boxn", pointwise, flat, preferred_element_type=jnp.float32)
    summed = spectral + local_part + offsets[None, :, None, None]
    upstream = cotangent.reshape(flat.shape).astype(jnp.float32)
    slope_grad = (upstream * gelu_slope(summed)).astype(jnp.bfloat16)
    back_plane = jnp.dot(slope_grad, plane_inv.T, preferred_element_type=jnp.float32).astype(
        jnp.bfloat16
    )
    spec_grad = to_modes(back_plane, line_inv.T, MX)
    held_grad = to_owners(spec_grad)
    held_dx = jnp.einsum(
        "mbo,mio->mbi", held_grad, blocks, preferred_element_type=jnp.float32
    ).astype(jnp.bfloat16)
    spec_dx = from_owners(held_dx)
    grad_spectral = weight_terms(held_in, held_grad)
    line_dx = to_slab(spec_dx, line_fwd.T, MX, channels)
    total = jnp.dot(line_dx, plane_fwd.T, preferred_element_type=jnp.float32)
    total = total + jnp.einsum(
        "io,boxn->bixn", pointwise, slope_grad, preferred_element_type=jnp.float32
    )
    grad_in = total.astype(jnp.bfloat16).reshape(activations.shape)
    return (grad_in, grad_spectral)


BF16 = jnp.bfloat16
F32 = jnp.float32
GROUP = 16
TILE = 8
SLOTS = 4
STEPS = GROUP // SLOTS
MIB = 1024 * 1024


def rounded(table):
    return np.asarray(table, np.float32).astype(ml_dtypes.bfloat16)


def angles(freq, points, length):
    phase = np.mod(np.outer(freq, points), length)
    return (phase * (2.0 * math.pi / length)).astype(np.float64)


def signed(count):
    index = np.arange(count)
    return np.where(index < count // 2, index, index - count)


def z_base(rows_z):
    theta = angles(np.arange(MZ), np.arange(rows_z), rows_z)
    pair = np.stack([np.cos(theta), -np.sin(theta)])
    table = np.repeat(pair.reshape(2 * MZ, rows_z), GROUP, axis=0).T
    return rounded(table).astype(np.float32)


def y_table(rows_y, width):
    theta = angles(signed(MY), np.arange(rows_y), rows_y)
    cosine, sine = np.cos(theta), np.sin(theta)
    turn = np.stack([np.stack([cosine, sine]), np.stack([-sine, cosine])])
    table = np.einsum("rsjy,xw->jxrswy", turn, np.eye(width))
    return rounded(table.reshape(MY * width * 2, 2 * width * rows_y))


def x_tables(samples, slabs, length):
    theta = angles(signed(MX), np.arange(length), length)
    cosine, sine = np.cos(theta), np.sin(theta)
    forward = np.stack([np.stack([cosine, sine]), np.stack([-sine, cosine])])
    inverse = np.stack([np.stack([cosine, sine]), np.stack([-sine, cosine])]) / length
    same = np.eye(samples)
    rows = MX * 2 * samples

    def lay(turn):
        turn = turn.reshape(2, 2, MX, slabs, length // slabs)
        table = np.einsum("arqsx,bd->qabsdxr", turn, same)
        return rounded(table.reshape(rows, samples * length * 2))

    return lay(forward), lay(inverse)


def dot(left, right):
    return jnp.dot(left, right, preferred_element_type=F32)


def gelu_slope_rows(value):
    decay = jnp.exp2(value * value * (-0.5 * math.log2(math.e))).astype(BF16)
    cdf = (0.5 + 0.5 * lax.erf(value * math.sqrt(0.5))).astype(BF16)
    density = value.astype(BF16) * jnp.asarray(1.0 / math.sqrt(2.0 * math.pi), BF16)
    return cdf + density * decay


def over(index, size):
    return lax.shift_right_logical(index, jnp.int32(size.bit_length() - 1))


def within(index, size):
    return jnp.bitwise_and(index, jnp.int32(size - 1))


def fill_z(base, table):
    rows_z, lanes = base.shape
    owner = within(lax.broadcasted_iota(jnp.int32, (rows_z, lanes), 1), GROUP)
    values = base[...]
    for c in range(GROUP):
        table[c * rows_z : (c + 1) * rows_z] = jnp.where(owner == c, values, 0.0).astype(BF16)


def fill_z_back(base, table):
    lanes, rows_z = base.shape
    owner = within(lax.broadcasted_iota(jnp.int32, (lanes, rows_z), 0), GROUP)
    values = base[...]
    for c in range(GROUP):
        first = c % SLOTS * rows_z
        table[c // SLOTS, :, first : first + rows_z] = jnp.where(owner == c, values, 0.0).astype(BF16)


def grouped(lane, per, channels):
    c = within(lane, channels)
    return over(c, GROUP) * (MZ * GROUP) + over(lane, channels) * GROUP + within(c, GROUP)


def fill_order(per, channels, back, table):
    count = table.shape[0]
    row = lax.broadcasted_iota(jnp.int32, (count, count), 0)
    column = lax.broadcasted_iota(jnp.int32, (count, count), 1)
    if back:
        same = grouped(row[:, :1], per, channels) == column
    else:
        same = row == grouped(column[:1], per, channels)
    table[...] = jnp.where(same, 1.0, 0.0).astype(BF16)


def deliver(spectra, ytab, order, scale, message, per, channels):
    groups = channels // GROUP
    rows = spectra.shape[0] // groups
    wide = spectra.shape[1] // 2
    halves = []
    for r in range(2):
        blocks = [spectra[g * rows : (g + 1) * rows, r * wide : (r + 1) * wide] for g in range(groups)]
        halves.append(jnp.concatenate(blocks, axis=1).astype(BF16))
    planes = dot(ytab[...], jnp.concatenate(halves, axis=0))
    if scale is not None:
        planes = planes * scale[...]
    ordered = dot(planes.astype(BF16), order[...]).astype(BF16)
    parts = MZ // per
    count = message.shape[1]
    lanes = per * channels
    for part in range(parts):
        block = ordered[:, part * lanes : (part + 1) * lanes]
        for j in range(MY):
            message[j * parts + part] = block[j * count : (j + 1) * count]


def receive(message, order_back, ytab_back, scale, held, per):
    parts = MZ // per
    blocks = message[...]
    blocks = blocks.reshape(MY, parts, *blocks.shape[1:])
    lanes = [blocks[:, part].reshape(-1, blocks.shape[3]) for part in range(parts)]
    ordered = dot(jnp.concatenate(lanes, axis=1), order_back[...]).astype(BF16)
    lines = dot(ytab_back[...], ordered)
    if scale is not None:
        lines = lines * scale[...]
    lines = lines.astype(BF16)
    rows = lines.shape[0] // 2
    wide = MZ * GROUP
    for group in range(held.shape[0] // rows):
        piece = lines[:, group * wide : (group + 1) * wide]
        held[group * rows : (group + 1) * rows] = jnp.concatenate([piece[:rows], piece[rows:]], axis=1)


class Move:
    def __init__(self, source, target, sems):
        self.source, self.target, self.sems = source, target, sems
        self.groups = target.shape[0] // GROUP

    def copies(self, step):
        for g in range(self.groups):
            run = pl.ds(g * GROUP + step * SLOTS, SLOTS)
            sem = self.sems.at[step * self.groups + g]
            yield pltpu.make_async_copy(self.source.at[run], self.target.at[run], sem)

    def start(self, step):
        for copy in self.copies(step):
            copy.start()

    def wait(self, step):
        for copy in self.copies(step):
            copy.wait()


def add_spectra(field, ztab, step, spectra):
    groups = field.shape[0] // GROUP
    rows_z = field.shape[-1]
    rows = spectra.shape[0] // groups
    depth = SLOTS * rows_z
    table = ztab[pl.ds(pl.multiple_of(step * depth, depth), depth)]
    lanes = [
        jnp.concatenate(
            [field[g * GROUP + step * SLOTS + slot].reshape(rows, rows_z) for g in range(groups)], axis=0
        )
        for slot in range(SLOTS)
    ]
    spectra[...] += dot(jnp.concatenate(lanes, axis=1), table)


def plane_kernel(
    per, channels, field, base_far, ytab_far, message, ztab, order, spectra, buffer, base, ytab, sems, table_sems
):
    incoming = Move(field.at[0], buffer, sems)
    base_copy = pltpu.make_async_copy(base_far, base, table_sems.at[0])
    ytab_copy = pltpu.make_async_copy(ytab_far, ytab, table_sems.at[1])
    base_copy.start()
    incoming.start(0)
    fill_order(per, channels, False, order)
    spectra[...] = jnp.zeros_like(spectra)
    incoming.start(1)
    base_copy.wait()
    fill_z(base, ztab)
    incoming.start(2)
    ytab_copy.start()
    incoming.start(3)

    @pl.loop(0, STEPS)
    def _(step):
        incoming.wait(step)
        add_spectra(buffer, ztab, step, spectra)

    ytab_copy.wait()
    deliver(spectra, ytab, order, None, message, per, channels)


def slope_kernel(
    per, channels, arrived, local, cotangent, base, base_back, ytab, ytab_back, scale,
    slope, message, ztab, ztab_back, order, held, spectra, cotangent_in, first_sum, second_sum, sems,
):
    width, rows_y, rows_z = local.shape[1:]
    groups = channels // GROUP
    rows = width * rows_y
    wide = 2 * rows_y
    incoming = Move(cotangent.at[0], cotangent_in, sems)
    incoming.start(0)
    fill_order(per, channels, True, order)
    receive(arrived, order, ytab_back, scale, held, per)
    incoming.start(1)
    fill_z_back(base_back, ztab_back)
    fill_z(base, ztab)
    incoming.start(2)
    fill_order(per, channels, False, order)
    spectra[...] = jnp.zeros_like(spectra)
    incoming.start(3)

    @pl.loop(0, STEPS)
    def _(step):
        incoming.wait(step)
        for pair, total in enumerate((first_sum, second_sum)):
            total[...] = dot(held[...], ztab_back[step, :, 2 * pair * rows_z : 2 * (pair + 1) * rows_z])
        for pair, total in enumerate((first_sum, second_sum)):
            for g in range(groups):
                for offset in range(2):
                    c = g * GROUP + step * SLOTS + 2 * pair + offset
                    for x in range(0, width, 2):
                        place = g * rows + x * rows_y
                        value = total[place : place + wide, offset * rows_z : (offset + 1) * rows_z]
                        value = value + local[c, x : x + 2].reshape(wide, rows_z).astype(F32)
                        upstream = cotangent_in[c, x : x + 2].reshape(wide, rows_z)
                        answer = upstream * gelu_slope_rows(value)
                        slope[c, x : x + 2] = answer.reshape(2, rows_y, rows_z)
        add_spectra(slope, ztab, step, spectra)

    deliver(spectra, ytab, order, scale, message, per, channels)


def field_kernel(
    per, channels, arrived, local, base_back, ytab_back, out, ztab_back, order, held, result, sems
):
    width, rows_y, rows_z = local.shape[1:]
    groups = channels // GROUP
    rows = width * rows_y
    outgoing = Move(result, out.at[0], sems)
    fill_order(per, channels, True, order)
    receive(arrived, order, ytab_back, None, held, per)
    fill_z_back(base_back, ztab_back)

    @pl.loop(0, STEPS)
    def _(step):
        for pair in range(SLOTS // 2):
            total = dot(held[...], ztab_back[step, :, 2 * pair * rows_z : 2 * (pair + 1) * rows_z])
            for g in range(groups):
                for offset in range(2):
                    c = g * GROUP + step * SLOTS + 2 * pair + offset
                    value = total[g * rows : (g + 1) * rows, offset * rows_z : (offset + 1) * rows_z]
                    value = value + local[c].reshape(rows, rows_z).astype(F32)
                    result[c] = value.astype(BF16).reshape(width, rows_y, rows_z)
        outgoing.start(step)

    for step in range(STEPS):
        outgoing.wait(step)


def pointwise_kernel(turned, field, mix, offsets, out, table, shift):
    channels = mix.shape[0]
    width, rows_y, rows_z = field.shape[1:]
    size = channels * TILE

    @pl.when(pl.program_id(0) == 0)
    def _():
        row = over(lax.broadcasted_iota(jnp.int32, (size, channels), 0), TILE)
        column = lax.broadcasted_iota(jnp.int32, (size, channels), 1)
        spread = jnp.where(row == column, 1.0, 0.0).astype(BF16)
        tall = lax.dot_general(
            spread, mix[...], (((1,), (1 if turned else 0,)), ((), ())), preferred_element_type=F32
        ).astype(BF16)
        whole = lax.dot_general(
            tall, spread, (((1,), (1,)), ((), ())), preferred_element_type=F32
        )
        place = within(lax.broadcasted_iota(jnp.int32, (size, size), 0), TILE)
        other = within(lax.broadcasted_iota(jnp.int32, (size, size), 1), TILE)
        table[...] = jnp.where(place == other, whole, 0.0).astype(BF16)
        if offsets is not None:
            for c in range(channels):
                shift[c] = jnp.full((1, rows_z), offsets[c], F32)

    for start in range(0, rows_y, 2 * TILE):
        pieces = [field[:, x, start : start + 2 * TILE, :].astype(F32) for x in range(width)]
        halves = []
        for row in range(0, 2 * TILE, TILE):
            rows = [piece[:, row : row + TILE].reshape(size, rows_z).astype(BF16) for piece in pieces]
            halves.append(dot(table[...], jnp.concatenate(rows, axis=1)))
        for x in range(width):
            values = [
                half[:, x * rows_z : (x + 1) * rows_z].reshape(channels, TILE, rows_z) for half in halves
            ]
            value = jnp.concatenate(values, axis=1)
            if offsets is not None:
                value = value + shift[...]
            out[:, x, start : start + 2 * TILE, :] = value.astype(BF16)


def spread_pair(first, second):
    nothing = jnp.zeros_like(first)
    upper = jnp.concatenate([first, nothing], axis=1)
    lower = jnp.concatenate([nothing, second], axis=1)
    return jnp.concatenate([upper, lower], axis=0)


def low_half(shape):
    return lax.broadcasted_iota(jnp.int32, shape, 1) < shape[1] // 2


def mix_kernel(per, samples, arrived, weights, line, line_back, spec_in, message, held):
    rows = 2 * samples
    lanes = 2 * weights.shape[1]
    low = low_half((samples, lanes))
    flat = arrived[...].reshape(-1, arrived.shape[2])
    spectra = dot(line[...], flat).astype(BF16)
    spec_in[...] = spectra
    for q in range(MX):
        for first in range(0, per, 2):
            block = spread_pair(weights[first * MX + q], weights[(first + 1) * MX + q])
            place = first // 2 * lanes
            terms = dot(spectra[q * rows : (q + 1) * rows, place : place + lanes], block)
            mixed = []
            for side in range(2):
                part = terms[:, side * lanes : (side + 1) * lanes]
                turned = pltpu.roll(part[samples:], lanes // 2, 1)
                mixed.append(part[:samples] + jnp.where(low, -turned, turned))
            real = jnp.where(low, mixed[0], pltpu.roll(mixed[1], lanes // 2, 1))
            imag = jnp.where(low, pltpu.roll(mixed[0], lanes // 2, 1), mixed[1])
            held[q * rows : (q + 1) * rows, place : place + lanes] = jnp.concatenate(
                [real, imag], axis=0
            ).astype(BF16)
    message[...] = dot(line_back[...], held[...]).astype(BF16).reshape(message.shape)


def mix_back_kernel(per, samples, arrived, weights, line, line_back, pairs, message, held):
    rows = 2 * samples
    lanes = 2 * weights.shape[1]
    low = low_half((samples, lanes))
    flat = arrived[...].reshape(-1, arrived.shape[2])
    spectra = dot(line[...], flat).astype(BF16).astype(F32)
    for q in range(MX):
        for first in range(0, per, 2):
            block = spread_pair(weights[first * MX + q], weights[(first + 1) * MX + q])
            place = first // 2 * lanes
            real = spectra[q * rows : q * rows + samples, place : place + lanes]
            imag = spectra[q * rows + samples : (q + 1) * rows, place : place + lanes]
            real_turned = pltpu.roll(real, lanes // 2, 1)
            imag_turned = pltpu.roll(imag, lanes // 2, 1)
            left = [jnp.where(low, real, imag_turned), jnp.where(low, imag, -real_turned)]
            right = [jnp.where(low, real_turned, imag), jnp.where(low, imag_turned, -real)]
            pair = jnp.concatenate(
                [jnp.concatenate(left, axis=0), jnp.concatenate(right, axis=0)], axis=1
            ).astype(BF16)
            pairs[q * rows : (q + 1) * rows, 2 * place : 2 * (place + lanes)] = pair
            held[q * rows : (q + 1) * rows, place : place + lanes] = lax.dot_general(
                pair, block, (((1,), (1,)), ((), ())), preferred_element_type=F32
            ).astype(BF16)
    message[...] = dot(line_back[...], held[...]).astype(BF16).reshape(message.shape)


def weight_kernel(per, samples, spec_in, pairs, out):
    rows = 2 * samples
    lanes = out.shape[2]
    half = lanes // 2
    for q in range(MX):
        for first in range(0, per, 2):
            place = first // 2 * lanes
            left = spec_in[q * rows : (q + 1) * rows, place : place + lanes]
            right = pairs[q * rows : (q + 1) * rows, 2 * place : 2 * (place + lanes)]
            outer = lax.dot_general(
                left, right, (((0,), (0,)), ((), ())), preferred_element_type=F32
            )
            out[first * MX + q] = outer[:half, :lanes]
            out[(first + 1) * MX + q] = outer[half:, lanes:]


def whole(array):
    return pl.BlockSpec(array.shape, lambda *step: (0,) * len(array.shape))


def shaped(shape, dtype):
    return jax.ShapeDtypeStruct(shape, dtype)


def params(mib):
    return pltpu.CompilerParams(vmem_limit_bytes=mib * MIB)


def cost(flops, moved, steep=0):
    return pl.CostEstimate(flops=flops, bytes_accessed=moved, transcendentals=steep)


def body(mesh_axes, devices, slabs, activations, cotangent, mode_weights, pointwise, offsets):
    _, channels, width, rows_y, rows_z = activations.shape
    samples = devices // slabs
    per = MY * MZ // devices
    groups = channels // GROUP
    field = activations.shape[1:]
    count = math.prod(field)
    base = z_base(rows_z)
    ytab = y_table(rows_y, width)
    line_fwd, line_inv = x_tables(samples, slabs, NX)
    weight = np.where(np.arange(MZ) == 0, 1.0, 2.0) / (rows_y * rows_z)
    scale = np.tile(np.repeat(weight, GROUP), groups).astype(np.float32)[None]
    base_t, ytab_t = (np.ascontiguousarray(t.T) for t in (base, ytab))
    fwd_t, inv_t = (np.ascontiguousarray(t.T) for t in (line_fwd, line_inv))
    message = shaped((devices, 2 * width, per * channels), BF16)
    spectra = shaped((MX * 2 * samples, per * channels), BF16)
    ztab = pltpu.VMEM((GROUP * rows_z, 2 * MZ * GROUP), BF16)
    ztab_t = pltpu.VMEM((STEPS, 2 * MZ * GROUP, SLOTS * rows_z), BF16)
    order = pltpu.VMEM((MZ * channels, MZ * channels), BF16)
    rows = groups * width * rows_y
    held = pltpu.VMEM((rows, 2 * MZ * GROUP), BF16)
    sums = pltpu.VMEM((rows, 2 * MZ * GROUP), F32)
    pair_sums = pltpu.VMEM((rows, 2 * rows_z), F32)
    buffer = pltpu.VMEM(field, BF16)
    sems = pltpu.SemaphoreType.DMA((STEPS * groups,))
    far = pl.BlockSpec(memory_space=pltpu.HBM)
    near = pl.BlockSpec(memory_space=pltpu.VMEM)
    near_field = pltpu.VMEM(field, BF16)

    def kept_far(array):
        return pltpu.with_memory_space_constraint(array, pltpu.HBM)

    plane_flops = 2 * count * 2 * MZ * GROUP

    def exchange(array):
        return lax.all_to_all(array, mesh_axes, split_axis=0, concat_axis=0, tiled=True)

    def mix_points(values, turned, shifts):
        step = 2
        block = pl.BlockSpec((channels, step, rows_y, rows_z), lambda x: (0, x, 0, 0))
        kernel = functools.partial(pointwise_kernel, turned)
        specs = [block, whole(pointwise)]
        operands = [values, pointwise]
        if shifts is None:
            run = lambda a, b, *rest: kernel(a, b, None, *rest)
        else:
            run = kernel
            specs.append(pl.BlockSpec(memory_space=pltpu.SMEM))
            operands.append(shifts)
        return pl.pallas_call(
            run,
            grid=(width // step,),
            in_specs=specs,
            out_specs=block,
            out_shape=near_field,
            scratch_shapes=[
                pltpu.VMEM((channels * TILE, channels * TILE), BF16),
                pltpu.VMEM((channels, 1, rows_z), F32),
            ],
            compiler_params=params(32),
            cost_estimate=cost(2 * count * channels * TILE, 4 * count),
        )(*operands)

    planes = pl.pallas_call(
        functools.partial(plane_kernel, per, channels),
        in_specs=[far, far, far],
        out_specs=whole(message),
        out_shape=message,
        scratch_shapes=[
            ztab,
            order,
            sums,
            buffer,
            pltpu.VMEM(base.shape, F32),
            pltpu.VMEM(ytab.shape, BF16),
            sems,
            pltpu.SemaphoreType.DMA((2,)),
        ],
        compiler_params=params(32),
        cost_estimate=cost(plane_flops, 2 * count),
    )(kept_far(activations), kept_far(base), kept_far(ytab))
    arrived = exchange(planes)
    local = mix_points(kept_far(activations.reshape(field)), True, offsets)
    arrived, local = lax.optimization_barrier((arrived, local))
    spec_in, mixed = pl.pallas_call(
        functools.partial(mix_kernel, per, samples),
        out_shape=(spectra, message),
        scratch_shapes=[pltpu.VMEM(spectra.shape, BF16)],
        compiler_params=params(16),
        cost_estimate=cost(10**8, 2 * mode_weights.size),
    )(arrived, mode_weights, line_fwd, inv_t)
    returned = exchange(mixed)
    slope, back_plane = pl.pallas_call(
        functools.partial(slope_kernel, per, channels),
        in_specs=[whole(message), near, far]
        + [whole(t) for t in (base, base_t, ytab, ytab_t, scale)],
        out_specs=(near, whole(message)),
        out_shape=(near_field, message),
        scratch_shapes=[ztab, ztab_t, order, held, sums, buffer, pair_sums, pair_sums, sems],
        compiler_params=params(32),
        cost_estimate=cost(2 * plane_flops, 6 * count, 2 * count),
    )(returned, local, kept_far(cotangent), base, base_t, ytab, ytab_t, scale)
    arrived_back = exchange(back_plane)
    local_back = mix_points(slope, False, None)
    arrived_back, local_back = lax.optimization_barrier((arrived_back, local_back))
    pairs, mixed_back = pl.pallas_call(
        functools.partial(mix_back_kernel, per, samples),
        out_shape=(shaped((spectra.shape[0], 2 * spectra.shape[1]), BF16), message),
        scratch_shapes=[pltpu.VMEM(spectra.shape, BF16)],
        compiler_params=params(16),
        cost_estimate=cost(10**8, 2 * mode_weights.size),
    )(arrived_back, mode_weights, line_inv, fwd_t)
    returned_back = exchange(mixed_back)
    grad_spectral = pl.pallas_call(
        functools.partial(weight_kernel, per, samples),
        out_shape=shaped(mode_weights.shape, F32),
        compiler_params=params(16),
        cost_estimate=cost(10**8, 4 * mode_weights.size),
    )(spec_in, pairs)
    grad_in = pl.pallas_call(
        functools.partial(field_kernel, per, channels),
        in_specs=[whole(message), near, whole(base_t), whole(ytab_t)],
        out_specs=far,
        out_shape=shaped(activations.shape, BF16),
        scratch_shapes=[ztab_t, order, held, buffer, sems],
        compiler_params=params(32),
        cost_estimate=cost(plane_flops, 4 * count),
    )(returned_back, local_back, base_t, ytab_t)
    return (grad_in, grad_spectral)


def chosen_body(mesh_axes, devices, slabs, activations, cotangent, mode_weights, pointwise, offsets):
    samples, channels, width, rows_y, rows_z = activations.shape
    per = MY * MZ // devices
    fits = (
        samples == 1
        and MY * MZ % devices == 0
        and per in (2, 4, 8)
        and width % 8 == 0
        and channels == 64
        and rows_y % TILE == 0
        and rows_z == 128
    )
    plan = functools.partial(body, mesh_axes, devices, slabs) if fits else general_body
    return plan(activations, cotangent, mode_weights, pointwise, offsets)


def solution(mesh):
    slabs = mesh.shape["space"]
    devices = slabs * mesh.shape["dp"]
    return jax.shard_map(
        functools.partial(chosen_body, ("space", "dp"), devices, slabs),
        mesh=mesh,
        in_specs=(
            P("dp", None, "space", None, None),
            P("dp", None, "space", None, None),
            P(("space", "dp"), None, None),
            P(),
            P(),
        ),
        out_specs=(P("dp", None, "space", None, None), P(("space", "dp"), None, None)),
        check_vma=False,
    )
```

```python
import functools
import math

import jax
import jax.numpy as jnp
import ml_dtypes
import numpy as np
from jax import lax
from jax.experimental import pallas as pl
from jax.experimental.pallas import tpu as pltpu
from jax.sharding import PartitionSpec as P

MX = 16
MY = 16
MZ = 8
NX = 32


def centered(count):
    index = jnp.arange(count, dtype=jnp.int32)
    return jnp.where(index < count // 2, index, index - count)


def plane_tables(rows_y, rows_z, modes_y, modes_z):
    along_y = jnp.arange(rows_y, dtype=jnp.int32)[:, None, None, None]
    along_z = jnp.arange(rows_z, dtype=jnp.int32)[None, :, None, None]
    freq_y = centered(modes_y)[None, None, :, None]
    freq_z = jnp.arange(modes_z, dtype=jnp.int32)[None, None, None, :]
    phase = jnp.mod(freq_y * along_y * rows_z + freq_z * along_z * rows_y, rows_y * rows_z)
    theta = phase.astype(jnp.float32) * (2.0 * math.pi / (rows_y * rows_z))
    cosine = jnp.cos(theta)
    sine = jnp.sin(theta)
    forward = jnp.stack([cosine, -sine], -1).reshape(rows_y * rows_z, modes_y * modes_z * 2)
    scaled = jnp.where(freq_z == 0, 1.0, 2.0).astype(jnp.float32) / (rows_y * rows_z)
    inverse = (
        jnp.stack([cosine * scaled, -sine * scaled], -1)
        .reshape(rows_y * rows_z, modes_y * modes_z * 2)
        .T
    )
    return (forward.astype(jnp.bfloat16), inverse.astype(jnp.bfloat16))


def line_tables(length, modes):
    along = jnp.arange(length, dtype=jnp.int32)[:, None]
    freq = centered(modes)[None, :]
    phase = jnp.mod(freq * along, length)
    theta = phase.astype(jnp.float32) * (2.0 * math.pi / length)
    cosine = jnp.cos(theta)
    sine = jnp.sin(theta)
    first = jnp.stack([cosine, -sine], -1)
    second = jnp.stack([sine, cosine], -1)
    forward = jnp.stack([first, second], 1).reshape(2 * length, 2 * modes)
    inv_first = jnp.stack([cosine.T, sine.T], -1) / length
    inv_second = jnp.stack([-sine.T, cosine.T], -1) / length
    inverse = jnp.stack([inv_first, inv_second], 1).reshape(2 * modes, 2 * length)
    return (forward.astype(jnp.bfloat16), inverse.astype(jnp.bfloat16))


def expand_weights(weights):
    half = weights.shape[1]
    real_part = weights[:, :, :half]
    imag_part = weights[:, :, half:]
    upper = jnp.concatenate([real_part, imag_part], axis=2)
    lower = jnp.concatenate([-imag_part, real_part], axis=2)
    return jnp.concatenate([upper, lower], axis=1)


def outer_sum(left, right):
    return jnp.einsum("mbi,mbo->mio", left, right, preferred_element_type=jnp.float32)


def weight_terms(spec_in, spec_grad):
    half = spec_in.shape[2] // 2
    in_real = spec_in[:, :, :half]
    in_imag = spec_in[:, :, half:]
    gr_real = spec_grad[:, :, :half]
    gr_imag = spec_grad[:, :, half:]
    real_term = outer_sum(in_real, gr_real) + outer_sum(in_imag, gr_imag)
    imag_term = outer_sum(in_real, gr_imag) - outer_sum(in_imag, gr_real)
    return jnp.concatenate([real_term, imag_term], axis=2)


def to_modes(slab, table, modes_x):
    samples, channels, width, pairs = slab.shape
    moved = lax.all_to_all(slab, "space", split_axis=3, concat_axis=2, tiled=True)
    length = moved.shape[2]
    local = moved.shape[3] // 2
    lines = moved.reshape(samples, channels, length, local, 2).transpose(0, 1, 3, 2, 4)
    lines = lines.reshape(samples, channels, local, 2 * length)
    spectra = jnp.dot(lines, table, preferred_element_type=jnp.float32).astype(jnp.bfloat16)
    spectra = spectra.reshape(samples, channels, local, modes_x, 2).transpose(2, 3, 0, 4, 1)
    return spectra.reshape(local * modes_x, samples, 2 * channels)


def to_slab(spectra, table, modes_x, channels):
    count, samples, doubled = spectra.shape
    local = count // modes_x
    lines = spectra.reshape(local, modes_x, samples, 2, channels).transpose(2, 4, 0, 1, 3)
    lines = lines.reshape(samples, channels, local, 2 * modes_x)
    lines = jnp.dot(lines, table, preferred_element_type=jnp.float32).astype(jnp.bfloat16)
    length = lines.shape[3] // 2
    lines = lines.reshape(samples, channels, local, length, 2).transpose(0, 1, 3, 2, 4)
    lines = lines.reshape(samples, channels, length, 2 * local)
    return lax.all_to_all(lines, "space", split_axis=2, concat_axis=3, tiled=True)


def to_owners(spectra):
    return lax.all_to_all(spectra, "dp", split_axis=0, concat_axis=1, tiled=True)


def from_owners(spectra):
    return lax.all_to_all(spectra, "dp", split_axis=1, concat_axis=0, tiled=True)


def gelu_slope(value):
    cdf = 0.5 * (1.0 + lax.erf(value * 0.7071067811865476))
    density = jnp.exp(-0.5 * value * value) * 0.3989422804014327
    return cdf + value * density


def general_body(activations, cotangent, mode_weights, pointwise, offsets):
    samples, channels, width, rows_y, rows_z = activations.shape
    plane_fwd, plane_inv = plane_tables(rows_y, rows_z, MY, MZ)
    line_fwd, line_inv = line_tables(NX, MX)
    flat = activations.reshape(samples, channels, width, rows_y * rows_z)
    planes = jnp.dot(flat, plane_fwd, preferred_element_type=jnp.float32).astype(jnp.bfloat16)
    spec_in = to_modes(planes, line_fwd, MX)
    blocks = expand_weights(mode_weights)
    held_in = to_owners(spec_in)
    held_out = jnp.einsum(
        "mbi,mio->mbo", held_in, blocks, preferred_element_type=jnp.float32
    ).astype(jnp.bfloat16)
    spec_out = from_owners(held_out)
    returned = to_slab(spec_out, line_inv, MX, channels)
    spectral = jnp.dot(returned, plane_inv, preferred_element_type=jnp.float32)
    local_part = jnp.einsum("io,bixn->boxn", pointwise, flat, preferred_element_type=jnp.float32)
    summed = spectral + local_part + offsets[None, :, None, None]
    upstream = cotangent.reshape(flat.shape).astype(jnp.float32)
    slope_grad = (upstream * gelu_slope(summed)).astype(jnp.bfloat16)
    back_plane = jnp.dot(slope_grad, plane_inv.T, preferred_element_type=jnp.float32).astype(
        jnp.bfloat16
    )
    spec_grad = to_modes(back_plane, line_inv.T, MX)
    held_grad = to_owners(spec_grad)
    held_dx = jnp.einsum(
        "mbo,mio->mbi", held_grad, blocks, preferred_element_type=jnp.float32
    ).astype(jnp.bfloat16)
    spec_dx = from_owners(held_dx)
    grad_spectral = weight_terms(held_in, held_grad)
    line_dx = to_slab(spec_dx, line_fwd.T, MX, channels)
    total = jnp.dot(line_dx, plane_fwd.T, preferred_element_type=jnp.float32)
    total = total + jnp.einsum(
        "io,boxn->bixn", pointwise, slope_grad, preferred_element_type=jnp.float32
    )
    grad_in = total.astype(jnp.bfloat16).reshape(activations.shape)
    return (grad_in, grad_spectral)


BF16 = jnp.bfloat16
F32 = jnp.float32
GROUP = 16
TILE = 8
SLOTS = 4
STEPS = GROUP // SLOTS
MIB = 1024 * 1024


def rounded(table):
    return np.asarray(table, np.float32).astype(ml_dtypes.bfloat16)


def angles(freq, points, length):
    phase = np.mod(np.outer(freq, points), length)
    return (phase * (2.0 * math.pi / length)).astype(np.float64)


def signed(count):
    index = np.arange(count)
    return np.where(index < count // 2, index, index - count)


def z_base(rows_z):
    theta = angles(np.arange(MZ), np.arange(rows_z), rows_z)
    pair = np.stack([np.cos(theta), -np.sin(theta)])
    table = np.repeat(pair.reshape(2 * MZ, rows_z), GROUP, axis=0).T
    return rounded(table).astype(np.float32)


def y_table(rows_y, width):
    theta = angles(signed(MY), np.arange(rows_y), rows_y)
    cosine, sine = np.cos(theta), np.sin(theta)
    turn = np.stack([np.stack([cosine, sine]), np.stack([-sine, cosine])])
    table = np.einsum("rsjy,xw->jxrswy", turn, np.eye(width))
    return rounded(table.reshape(MY * width * 2, 2 * width * rows_y))


def x_tables(samples, slabs, length):
    theta = angles(signed(MX), np.arange(length), length)
    cosine, sine = np.cos(theta), np.sin(theta)
    forward = np.stack([np.stack([cosine, sine]), np.stack([-sine, cosine])])
    inverse = np.stack([np.stack([cosine, sine]), np.stack([-sine, cosine])]) / length
    same = np.eye(samples)
    rows = MX * 2 * samples

    def lay(turn):
        turn = turn.reshape(2, 2, MX, slabs, length // slabs)
        table = np.einsum("arqsx,bd->qabsdxr", turn, same)
        return rounded(table.reshape(rows, samples * length * 2))

    return lay(forward), lay(inverse)


def dot(left, right):
    return jnp.dot(left, right, preferred_element_type=F32)


def gelu_slope_rows(value):
    decay = jnp.exp2(value * value * (-0.5 * math.log2(math.e))).astype(BF16)
    cdf = (0.5 + 0.5 * lax.erf(value * math.sqrt(0.5))).astype(BF16)
    density = value.astype(BF16) * jnp.asarray(1.0 / math.sqrt(2.0 * math.pi), BF16)
    return cdf + density * decay


def over(index, size):
    return lax.shift_right_logical(index, jnp.int32(size.bit_length() - 1))


def within(index, size):
    return jnp.bitwise_and(index, jnp.int32(size - 1))


def fill_z(base, table):
    rows_z, lanes = base.shape
    owner = within(lax.broadcasted_iota(jnp.int32, (rows_z, lanes), 1), GROUP)
    values = base[...]
    for c in range(GROUP):
        table[c * rows_z : (c + 1) * rows_z] = jnp.where(owner == c, values, 0.0).astype(BF16)


def fill_z_back(base, table):
    lanes, rows_z = base.shape
    owner = within(lax.broadcasted_iota(jnp.int32, (lanes, rows_z), 0), GROUP)
    values = base[...]
    for c in range(GROUP):
        first = c % SLOTS * rows_z
        table[c // SLOTS, :, first : first + rows_z] = jnp.where(owner == c, values, 0.0).astype(BF16)


def grouped(lane, per, channels):
    c = within(lane, channels)
    return over(c, GROUP) * (MZ * GROUP) + over(lane, channels) * GROUP + within(c, GROUP)


def fill_order(per, channels, back, table):
    count = table.shape[0]
    row = lax.broadcasted_iota(jnp.int32, (count, count), 0)
    column = lax.broadcasted_iota(jnp.int32, (count, count), 1)
    if back:
        same = grouped(row[:, :1], per, channels) == column
    else:
        same = row == grouped(column[:1], per, channels)
    table[...] = jnp.where(same, 1.0, 0.0).astype(BF16)


def deliver(spectra, ytab, order, scale, message, per, channels):
    groups = channels // GROUP
    rows = spectra.shape[0] // groups
    wide = spectra.shape[1] // 2
    halves = []
    for r in range(2):
        blocks = [spectra[g * rows : (g + 1) * rows, r * wide : (r + 1) * wide] for g in range(groups)]
        halves.append(jnp.concatenate(blocks, axis=1).astype(BF16))
    planes = dot(ytab[...], jnp.concatenate(halves, axis=0))
    if scale is not None:
        planes = planes * scale[...]
    ordered = dot(planes.astype(BF16), order[...]).astype(BF16)
    parts = MZ // per
    count = message.shape[1]
    lanes = per * channels
    for part in range(parts):
        block = ordered[:, part * lanes : (part + 1) * lanes]
        for j in range(MY):
            message[j * parts + part] = block[j * count : (j + 1) * count]


def receive(message, order_back, ytab_back, scale, held, per):
    parts = MZ // per
    blocks = message[...]
    blocks = blocks.reshape(MY, parts, *blocks.shape[1:])
    lanes = [blocks[:, part].reshape(-1, blocks.shape[3]) for part in range(parts)]
    ordered = dot(jnp.concatenate(lanes, axis=1), order_back[...]).astype(BF16)
    lines = dot(ytab_back[...], ordered)
    if scale is not None:
        lines = lines * scale[...]
    lines = lines.astype(BF16)
    rows = lines.shape[0] // 2
    wide = MZ * GROUP
    for group in range(held.shape[0] // rows):
        piece = lines[:, group * wide : (group + 1) * wide]
        held[group * rows : (group + 1) * rows] = jnp.concatenate([piece[:rows], piece[rows:]], axis=1)


class Move:
    def __init__(self, source, target, sems):
        self.source, self.target, self.sems = source, target, sems
        self.groups = target.shape[0] // GROUP

    def copies(self, step):
        for g in range(self.groups):
            run = pl.ds(g * GROUP + step * SLOTS, SLOTS)
            sem = self.sems.at[step * self.groups + g]
            yield pltpu.make_async_copy(self.source.at[run], self.target.at[run], sem)

    def start(self, step):
        for copy in self.copies(step):
            copy.start()

    def wait(self, step):
        for copy in self.copies(step):
            copy.wait()


def start_all(moves, step):
    for each in moves:
        each.start(step)


def add_spectra(field, ztab, first, count, spectra):
    groups = field.shape[0] // GROUP
    rows_z = field.shape[-1]
    rows = spectra.shape[0] // groups
    table = ztab[pl.ds(pl.multiple_of(first * rows_z, count * rows_z), count * rows_z)]
    lanes = [
        jnp.concatenate([field[g * GROUP + first + slot].reshape(rows, rows_z) for g in range(groups)], axis=0)
        for slot in range(count)
    ]
    spectra[...] += dot(jnp.concatenate(lanes, axis=1), table)


def plane_kernel(
    per, channels, field, base_far, ytab_far, message, ztab, order, spectra, buffer, base, ytab, sems, table_sems
):
    incoming = Move(field.at[0], buffer, sems)
    base_copy = pltpu.make_async_copy(base_far, base, table_sems.at[0])
    ytab_copy = pltpu.make_async_copy(ytab_far, ytab, table_sems.at[1])
    base_copy.start()
    incoming.start(0)
    fill_order(per, channels, False, order)
    spectra[...] = jnp.zeros_like(spectra)
    incoming.start(1)
    base_copy.wait()
    fill_z(base, ztab)
    incoming.start(2)
    ytab_copy.start()
    incoming.start(3)

    @pl.loop(0, STEPS)
    def _(step):
        incoming.wait(step)
        add_spectra(buffer, ztab, step * SLOTS, SLOTS, spectra)

    ytab_copy.wait()
    deliver(spectra, ytab, order, None, message, per, channels)


def slope_kernel(
    per, channels, arrived, local, cotangent, base, base_back, ytab, ytab_back, scale,
    slope, message, ztab, ztab_back, order, held, spectra, local_in, cotangent_in, result, first_sum, second_sum,
    local_sems, cotangent_sems, result_sems,
):
    width, rows_y, rows_z = local.shape[1:]
    groups = channels // GROUP
    rows = width * rows_y
    wide = 2 * rows_y
    incoming = (Move(local, local_in, local_sems), Move(cotangent.at[0], cotangent_in, cotangent_sems))
    outgoing = Move(result, slope, result_sems)
    start_all(incoming, 0)
    fill_order(per, channels, True, order)
    receive(arrived, order, ytab_back, scale, held, per)
    start_all(incoming, 1)
    fill_z_back(base_back, ztab_back)
    fill_z(base, ztab)
    start_all(incoming, 2)
    fill_order(per, channels, False, order)
    spectra[...] = jnp.zeros_like(spectra)
    start_all(incoming, 3)

    @pl.loop(0, STEPS)
    def _(step):
        for each in incoming:
            each.wait(step)
        for pair, total in enumerate((first_sum, second_sum)):
            total[...] = dot(held[...], ztab_back[step, :, 2 * pair * rows_z : 2 * (pair + 1) * rows_z])
        for pair, total in enumerate((first_sum, second_sum)):
            for g in range(groups):
                for offset in range(2):
                    c = g * GROUP + step * SLOTS + 2 * pair + offset
                    for x in range(0, width, 2):
                        place = g * rows + x * rows_y
                        value = total[place : place + wide, offset * rows_z : (offset + 1) * rows_z]
                        value = value + local_in[c, x : x + 2].reshape(wide, rows_z).astype(F32)
                        upstream = cotangent_in[c, x : x + 2].reshape(wide, rows_z)
                        answer = upstream * gelu_slope_rows(value)
                        result[c, x : x + 2] = answer.reshape(2, rows_y, rows_z)
            add_spectra(result, ztab, step * SLOTS + 2 * pair, 2, spectra)
        outgoing.start(step)

    deliver(spectra, ytab, order, scale, message, per, channels)
    for step in range(STEPS):
        outgoing.wait(step)


def field_kernel(
    per, channels, arrived, local, base_back, ytab_back, out, ztab_back, order, held, local_in, result,
    local_sems, result_sems,
):
    width, rows_y, rows_z = local.shape[1:]
    groups = channels // GROUP
    rows = width * rows_y
    incoming = Move(local, local_in, local_sems)
    outgoing = Move(result, out.at[0], result_sems)
    incoming.start(0)
    fill_order(per, channels, True, order)
    incoming.start(1)
    receive(arrived, order, ytab_back, None, held, per)
    incoming.start(2)
    fill_z_back(base_back, ztab_back)
    incoming.start(3)

    @pl.loop(0, STEPS)
    def _(step):
        incoming.wait(step)
        for pair in range(SLOTS // 2):
            total = dot(held[...], ztab_back[step, :, 2 * pair * rows_z : 2 * (pair + 1) * rows_z])
            for g in range(groups):
                for offset in range(2):
                    c = g * GROUP + step * SLOTS + 2 * pair + offset
                    value = total[g * rows : (g + 1) * rows, offset * rows_z : (offset + 1) * rows_z]
                    value = value + local_in[c].reshape(rows, rows_z).astype(F32)
                    result[c] = value.astype(BF16).reshape(width, rows_y, rows_z)
        outgoing.start(step)

    for step in range(STEPS):
        outgoing.wait(step)


def pointwise_kernel(turned, field, mix, offsets, out, table, shift):
    channels = mix.shape[0]
    width, rows_y, rows_z = field.shape[1:]
    size = channels * TILE

    @pl.when(pl.program_id(0) == 0)
    def _():
        row = over(lax.broadcasted_iota(jnp.int32, (size, channels), 0), TILE)
        column = lax.broadcasted_iota(jnp.int32, (size, channels), 1)
        spread = jnp.where(row == column, 1.0, 0.0).astype(BF16)
        tall = lax.dot_general(
            spread, mix[...], (((1,), (1 if turned else 0,)), ((), ())), preferred_element_type=F32
        ).astype(BF16)
        whole = lax.dot_general(
            tall, spread, (((1,), (1,)), ((), ())), preferred_element_type=F32
        )
        place = within(lax.broadcasted_iota(jnp.int32, (size, size), 0), TILE)
        other = within(lax.broadcasted_iota(jnp.int32, (size, size), 1), TILE)
        table[...] = jnp.where(place == other, whole, 0.0).astype(BF16)
        if offsets is not None:
            for c in range(channels):
                shift[c] = jnp.full((1, rows_z), offsets[c], F32)

    for start in range(0, rows_y, 2 * TILE):
        pieces = [field[:, x, start : start + 2 * TILE, :].astype(F32) for x in range(width)]
        halves = []
        for row in range(0, 2 * TILE, TILE):
            rows = [piece[:, row : row + TILE].reshape(size, rows_z).astype(BF16) for piece in pieces]
            halves.append(dot(table[...], jnp.concatenate(rows, axis=1)))
        for x in range(width):
            values = [
                half[:, x * rows_z : (x + 1) * rows_z].reshape(channels, TILE, rows_z) for half in halves
            ]
            value = jnp.concatenate(values, axis=1)
            if offsets is not None:
                value = value + shift[...]
            out[:, x, start : start + 2 * TILE, :] = value.astype(BF16)


def spread_pair(first, second):
    nothing = jnp.zeros_like(first)
    upper = jnp.concatenate([first, nothing], axis=1)
    lower = jnp.concatenate([nothing, second], axis=1)
    return jnp.concatenate([upper, lower], axis=0)


def low_half(shape):
    return lax.broadcasted_iota(jnp.int32, shape, 1) < shape[1] // 2


def mix_kernel(per, samples, arrived, weights, line, line_back, spec_in, message, held):
    rows = 2 * samples
    lanes = 2 * weights.shape[1]
    low = low_half((samples, lanes))
    flat = arrived[...].reshape(-1, arrived.shape[2])
    spectra = dot(line[...], flat).astype(BF16)
    spec_in[...] = spectra
    for q in range(MX):
        for first in range(0, per, 2):
            block = spread_pair(weights[first * MX + q], weights[(first + 1) * MX + q])
            place = first // 2 * lanes
            terms = dot(spectra[q * rows : (q + 1) * rows, place : place + lanes], block)
            mixed = []
            for side in range(2):
                part = terms[:, side * lanes : (side + 1) * lanes]
                turned = pltpu.roll(part[samples:], lanes // 2, 1)
                mixed.append(part[:samples] + jnp.where(low, -turned, turned))
            real = jnp.where(low, mixed[0], pltpu.roll(mixed[1], lanes // 2, 1))
            imag = jnp.where(low, pltpu.roll(mixed[0], lanes // 2, 1), mixed[1])
            held[q * rows : (q + 1) * rows, place : place + lanes] = jnp.concatenate(
                [real, imag], axis=0
            ).astype(BF16)
    message[...] = dot(line_back[...], held[...]).astype(BF16).reshape(message.shape)


def mix_back_kernel(per, samples, arrived, weights, line, line_back, pairs, message, held):
    rows = 2 * samples
    lanes = 2 * weights.shape[1]
    low = low_half((samples, lanes))
    flat = arrived[...].reshape(-1, arrived.shape[2])
    spectra = dot(line[...], flat).astype(BF16).astype(F32)
    for q in range(MX):
        for first in range(0, per, 2):
            block = spread_pair(weights[first * MX + q], weights[(first + 1) * MX + q])
            place = first // 2 * lanes
            real = spectra[q * rows : q * rows + samples, place : place + lanes]
            imag = spectra[q * rows + samples : (q + 1) * rows, place : place + lanes]
            real_turned = pltpu.roll(real, lanes // 2, 1)
            imag_turned = pltpu.roll(imag, lanes // 2, 1)
            left = [jnp.where(low, real, imag_turned), jnp.where(low, imag, -real_turned)]
            right = [jnp.where(low, real_turned, imag), jnp.where(low, imag_turned, -real)]
            pair = jnp.concatenate(
                [jnp.concatenate(left, axis=0), jnp.concatenate(right, axis=0)], axis=1
            ).astype(BF16)
            pairs[q * rows : (q + 1) * rows, 2 * place : 2 * (place + lanes)] = pair
            held[q * rows : (q + 1) * rows, place : place + lanes] = lax.dot_general(
                pair, block, (((1,), (1,)), ((), ())), preferred_element_type=F32
            ).astype(BF16)
    message[...] = dot(line_back[...], held[...]).astype(BF16).reshape(message.shape)


def weight_kernel(per, samples, spec_in, pairs, out):
    rows = 2 * samples
    lanes = out.shape[2]
    half = lanes // 2
    for q in range(MX):
        for first in range(0, per, 2):
            place = first // 2 * lanes
            left = spec_in[q * rows : (q + 1) * rows, place : place + lanes]
            right = pairs[q * rows : (q + 1) * rows, 2 * place : 2 * (place + lanes)]
            outer = lax.dot_general(
                left, right, (((0,), (0,)), ((), ())), preferred_element_type=F32
            )
            out[first * MX + q] = outer[:half, :lanes]
            out[(first + 1) * MX + q] = outer[half:, lanes:]


def whole(array):
    return pl.BlockSpec(array.shape, lambda *step: (0,) * len(array.shape))


def shaped(shape, dtype):
    return jax.ShapeDtypeStruct(shape, dtype)


def params(mib):
    return pltpu.CompilerParams(vmem_limit_bytes=mib * MIB)


def cost(flops, moved, steep=0):
    return pl.CostEstimate(flops=flops, bytes_accessed=moved, transcendentals=steep)


def body(mesh_axes, devices, slabs, activations, cotangent, mode_weights, pointwise, offsets):
    _, channels, width, rows_y, rows_z = activations.shape
    samples = devices // slabs
    per = MY * MZ // devices
    groups = channels // GROUP
    field = activations.shape[1:]
    count = math.prod(field)
    base = z_base(rows_z)
    ytab = y_table(rows_y, width)
    line_fwd, line_inv = x_tables(samples, slabs, NX)
    weight = np.where(np.arange(MZ) == 0, 1.0, 2.0) / (rows_y * rows_z)
    scale = np.tile(np.repeat(weight, GROUP), groups).astype(np.float32)[None]
    base_t, ytab_t = (np.ascontiguousarray(t.T) for t in (base, ytab))
    fwd_t, inv_t = (np.ascontiguousarray(t.T) for t in (line_fwd, line_inv))
    message = shaped((devices, 2 * width, per * channels), BF16)
    spectra = shaped((MX * 2 * samples, per * channels), BF16)
    ztab = pltpu.VMEM((GROUP * rows_z, 2 * MZ * GROUP), BF16)
    ztab_t = pltpu.VMEM((STEPS, 2 * MZ * GROUP, SLOTS * rows_z), BF16)
    order = pltpu.VMEM((MZ * channels, MZ * channels), BF16)
    rows = groups * width * rows_y
    held = pltpu.VMEM((rows, 2 * MZ * GROUP), BF16)
    sums = pltpu.VMEM((rows, 2 * MZ * GROUP), F32)
    pair_sums = pltpu.VMEM((rows, 2 * rows_z), F32)
    buffer = pltpu.VMEM(field, BF16)
    sems = pltpu.SemaphoreType.DMA((STEPS * groups,))
    far = pl.BlockSpec(memory_space=pltpu.HBM)
    far_field = pltpu.HBM(field, BF16)

    def kept_far(array):
        return pltpu.with_memory_space_constraint(array, pltpu.HBM)

    plane_flops = 2 * count * 2 * MZ * GROUP

    def exchange(array):
        return lax.all_to_all(array, mesh_axes, split_axis=0, concat_axis=0, tiled=True)

    def mix_points(values, turned, shifts):
        step = 2
        block = pl.BlockSpec((channels, step, rows_y, rows_z), lambda x: (0, x, 0, 0))
        kernel = functools.partial(pointwise_kernel, turned)
        specs = [block, whole(pointwise)]
        operands = [values, pointwise]
        if shifts is None:
            run = lambda a, b, *rest: kernel(a, b, None, *rest)
        else:
            run = kernel
            specs.append(pl.BlockSpec(memory_space=pltpu.SMEM))
            operands.append(shifts)
        return pl.pallas_call(
            run,
            grid=(width // step,),
            in_specs=specs,
            out_specs=block,
            out_shape=far_field,
            scratch_shapes=[
                pltpu.VMEM((channels * TILE, channels * TILE), BF16),
                pltpu.VMEM((channels, 1, rows_z), F32),
            ],
            compiler_params=params(32),
            cost_estimate=cost(2 * count * channels * TILE, 4 * count),
        )(*operands)

    planes = pl.pallas_call(
        functools.partial(plane_kernel, per, channels),
        in_specs=[far, far, far],
        out_specs=whole(message),
        out_shape=message,
        scratch_shapes=[
            ztab,
            order,
            sums,
            buffer,
            pltpu.VMEM(base.shape, F32),
            pltpu.VMEM(ytab.shape, BF16),
            sems,
            pltpu.SemaphoreType.DMA((2,)),
        ],
        compiler_params=params(32),
        cost_estimate=cost(plane_flops, 2 * count),
    )(kept_far(activations), kept_far(base), kept_far(ytab))
    arrived = exchange(planes)
    local = mix_points(kept_far(activations.reshape(field)), True, offsets)
    arrived, local = lax.optimization_barrier((arrived, local))
    spec_in, mixed = pl.pallas_call(
        functools.partial(mix_kernel, per, samples),
        out_shape=(spectra, message),
        scratch_shapes=[pltpu.VMEM(spectra.shape, BF16)],
        compiler_params=params(16),
        cost_estimate=cost(10**8, 2 * mode_weights.size),
    )(arrived, mode_weights, line_fwd, inv_t)
    returned = exchange(mixed)
    slope, back_plane = pl.pallas_call(
        functools.partial(slope_kernel, per, channels),
        in_specs=[whole(message), far, far]
        + [whole(t) for t in (base, base_t, ytab, ytab_t, scale)],
        out_specs=(far, whole(message)),
        out_shape=(far_field, message),
        scratch_shapes=[ztab, ztab_t, order, held, sums]
        + [buffer] * 3
        + [pair_sums] * 2
        + [sems] * 3,
        compiler_params=params(32),
        cost_estimate=cost(2 * plane_flops, 6 * count, 2 * count),
    )(returned, kept_far(local), kept_far(cotangent), base, base_t, ytab, ytab_t, scale)
    arrived_back = exchange(back_plane)
    local_back = mix_points(kept_far(slope), False, None)
    arrived_back, local_back = lax.optimization_barrier((arrived_back, local_back))
    pairs, mixed_back = pl.pallas_call(
        functools.partial(mix_back_kernel, per, samples),
        out_shape=(shaped((spectra.shape[0], 2 * spectra.shape[1]), BF16), message),
        scratch_shapes=[pltpu.VMEM(spectra.shape, BF16)],
        compiler_params=params(16),
        cost_estimate=cost(10**8, 2 * mode_weights.size),
    )(arrived_back, mode_weights, line_inv, fwd_t)
    returned_back = exchange(mixed_back)
    grad_spectral = pl.pallas_call(
        functools.partial(weight_kernel, per, samples),
        out_shape=shaped(mode_weights.shape, F32),
        compiler_params=params(16),
        cost_estimate=cost(10**8, 4 * mode_weights.size),
    )(spec_in, pairs)
    grad_in = pl.pallas_call(
        functools.partial(field_kernel, per, channels),
        in_specs=[whole(message), far, whole(base_t), whole(ytab_t)],
        out_specs=far,
        out_shape=shaped(activations.shape, BF16),
        scratch_shapes=[ztab_t, order, held, buffer, buffer, sems, sems],
        compiler_params=params(32),
        cost_estimate=cost(plane_flops, 4 * count),
    )(returned_back, kept_far(local_back), base_t, ytab_t)
    return (grad_in, grad_spectral)


def chosen_body(mesh_axes, devices, slabs, activations, cotangent, mode_weights, pointwise, offsets):
    samples, channels, width, rows_y, rows_z = activations.shape
    per = MY * MZ // devices
    fits = (
        samples == 1
        and MY * MZ % devices == 0
        and per in (2, 4, 8)
        and width % 8 == 0
        and channels == 64
        and rows_y % TILE == 0
        and rows_z == 128
    )
    plan = functools.partial(body, mesh_axes, devices, slabs) if fits else general_body
    return plan(activations, cotangent, mode_weights, pointwise, offsets)


def solution(mesh):
    slabs = mesh.shape["space"]
    devices = slabs * mesh.shape["dp"]
    return jax.shard_map(
        functools.partial(chosen_body, ("space", "dp"), devices, slabs),
        mesh=mesh,
        in_specs=(
            P("dp", None, "space", None, None),
            P("dp", None, "space", None, None),
            P(("space", "dp"), None, None),
            P(),
            P(),
        ),
        out_specs=(P("dp", None, "space", None, None), P(("space", "dp"), None, None)),
        check_vma=False,
    )
```

```python
import functools
import math

import jax
import jax.numpy as jnp
import ml_dtypes
import numpy as np
from jax import lax
from jax.experimental import pallas as pl
from jax.experimental.pallas import tpu as pltpu
from jax.sharding import PartitionSpec as P

MX = 16
MY = 16
MZ = 8
NX = 32


def centered(count):
    index = jnp.arange(count, dtype=jnp.int32)
    return jnp.where(index < count // 2, index, index - count)


def plane_tables(rows_y, rows_z, modes_y, modes_z):
    along_y = jnp.arange(rows_y, dtype=jnp.int32)[:, None, None, None]
    along_z = jnp.arange(rows_z, dtype=jnp.int32)[None, :, None, None]
    freq_y = centered(modes_y)[None, None, :, None]
    freq_z = jnp.arange(modes_z, dtype=jnp.int32)[None, None, None, :]
    phase = jnp.mod(freq_y * along_y * rows_z + freq_z * along_z * rows_y, rows_y * rows_z)
    theta = phase.astype(jnp.float32) * (2.0 * math.pi / (rows_y * rows_z))
    cosine = jnp.cos(theta)
    sine = jnp.sin(theta)
    forward = jnp.stack([cosine, -sine], -1).reshape(rows_y * rows_z, modes_y * modes_z * 2)
    scaled = jnp.where(freq_z == 0, 1.0, 2.0).astype(jnp.float32) / (rows_y * rows_z)
    inverse = (
        jnp.stack([cosine * scaled, -sine * scaled], -1)
        .reshape(rows_y * rows_z, modes_y * modes_z * 2)
        .T
    )
    return (forward.astype(jnp.bfloat16), inverse.astype(jnp.bfloat16))


def line_tables(length, modes):
    along = jnp.arange(length, dtype=jnp.int32)[:, None]
    freq = centered(modes)[None, :]
    phase = jnp.mod(freq * along, length)
    theta = phase.astype(jnp.float32) * (2.0 * math.pi / length)
    cosine = jnp.cos(theta)
    sine = jnp.sin(theta)
    first = jnp.stack([cosine, -sine], -1)
    second = jnp.stack([sine, cosine], -1)
    forward = jnp.stack([first, second], 1).reshape(2 * length, 2 * modes)
    inv_first = jnp.stack([cosine.T, sine.T], -1) / length
    inv_second = jnp.stack([-sine.T, cosine.T], -1) / length
    inverse = jnp.stack([inv_first, inv_second], 1).reshape(2 * modes, 2 * length)
    return (forward.astype(jnp.bfloat16), inverse.astype(jnp.bfloat16))


def expand_weights(weights):
    half = weights.shape[1]
    real_part = weights[:, :, :half]
    imag_part = weights[:, :, half:]
    upper = jnp.concatenate([real_part, imag_part], axis=2)
    lower = jnp.concatenate([-imag_part, real_part], axis=2)
    return jnp.concatenate([upper, lower], axis=1)


def outer_sum(left, right):
    return jnp.einsum("mbi,mbo->mio", left, right, preferred_element_type=jnp.float32)


def weight_terms(spec_in, spec_grad):
    half = spec_in.shape[2] // 2
    in_real = spec_in[:, :, :half]
    in_imag = spec_in[:, :, half:]
    gr_real = spec_grad[:, :, :half]
    gr_imag = spec_grad[:, :, half:]
    real_term = outer_sum(in_real, gr_real) + outer_sum(in_imag, gr_imag)
    imag_term = outer_sum(in_real, gr_imag) - outer_sum(in_imag, gr_real)
    return jnp.concatenate([real_term, imag_term], axis=2)


def to_modes(slab, table, modes_x):
    samples, channels, width, pairs = slab.shape
    moved = lax.all_to_all(slab, "space", split_axis=3, concat_axis=2, tiled=True)
    length = moved.shape[2]
    local = moved.shape[3] // 2
    lines = moved.reshape(samples, channels, length, local, 2).transpose(0, 1, 3, 2, 4)
    lines = lines.reshape(samples, channels, local, 2 * length)
    spectra = jnp.dot(lines, table, preferred_element_type=jnp.float32).astype(jnp.bfloat16)
    spectra = spectra.reshape(samples, channels, local, modes_x, 2).transpose(2, 3, 0, 4, 1)
    return spectra.reshape(local * modes_x, samples, 2 * channels)


def to_slab(spectra, table, modes_x, channels):
    count, samples, doubled = spectra.shape
    local = count // modes_x
    lines = spectra.reshape(local, modes_x, samples, 2, channels).transpose(2, 4, 0, 1, 3)
    lines = lines.reshape(samples, channels, local, 2 * modes_x)
    lines = jnp.dot(lines, table, preferred_element_type=jnp.float32).astype(jnp.bfloat16)
    length = lines.shape[3] // 2
    lines = lines.reshape(samples, channels, local, length, 2).transpose(0, 1, 3, 2, 4)
    lines = lines.reshape(samples, channels, length, 2 * local)
    return lax.all_to_all(lines, "space", split_axis=2, concat_axis=3, tiled=True)


def to_owners(spectra):
    return lax.all_to_all(spectra, "dp", split_axis=0, concat_axis=1, tiled=True)


def from_owners(spectra):
    return lax.all_to_all(spectra, "dp", split_axis=1, concat_axis=0, tiled=True)


def gelu_slope(value):
    cdf = 0.5 * (1.0 + lax.erf(value * 0.7071067811865476))
    density = jnp.exp(-0.5 * value * value) * 0.3989422804014327
    return cdf + value * density


def general_body(activations, cotangent, mode_weights, pointwise, offsets):
    samples, channels, width, rows_y, rows_z = activations.shape
    plane_fwd, plane_inv = plane_tables(rows_y, rows_z, MY, MZ)
    line_fwd, line_inv = line_tables(NX, MX)
    flat = activations.reshape(samples, channels, width, rows_y * rows_z)
    planes = jnp.dot(flat, plane_fwd, preferred_element_type=jnp.float32).astype(jnp.bfloat16)
    spec_in = to_modes(planes, line_fwd, MX)
    blocks = expand_weights(mode_weights)
    held_in = to_owners(spec_in)
    held_out = jnp.einsum(
        "mbi,mio->mbo", held_in, blocks, preferred_element_type=jnp.float32
    ).astype(jnp.bfloat16)
    spec_out = from_owners(held_out)
    returned = to_slab(spec_out, line_inv, MX, channels)
    spectral = jnp.dot(returned, plane_inv, preferred_element_type=jnp.float32)
    local_part = jnp.einsum("io,bixn->boxn", pointwise, flat, preferred_element_type=jnp.float32)
    summed = spectral + local_part + offsets[None, :, None, None]
    upstream = cotangent.reshape(flat.shape).astype(jnp.float32)
    slope_grad = (upstream * gelu_slope(summed)).astype(jnp.bfloat16)
    back_plane = jnp.dot(slope_grad, plane_inv.T, preferred_element_type=jnp.float32).astype(
        jnp.bfloat16
    )
    spec_grad = to_modes(back_plane, line_inv.T, MX)
    held_grad = to_owners(spec_grad)
    held_dx = jnp.einsum(
        "mbo,mio->mbi", held_grad, blocks, preferred_element_type=jnp.float32
    ).astype(jnp.bfloat16)
    spec_dx = from_owners(held_dx)
    grad_spectral = weight_terms(held_in, held_grad)
    line_dx = to_slab(spec_dx, line_fwd.T, MX, channels)
    total = jnp.dot(line_dx, plane_fwd.T, preferred_element_type=jnp.float32)
    total = total + jnp.einsum(
        "io,boxn->bixn", pointwise, slope_grad, preferred_element_type=jnp.float32
    )
    grad_in = total.astype(jnp.bfloat16).reshape(activations.shape)
    return (grad_in, grad_spectral)


BF16 = jnp.bfloat16
F32 = jnp.float32
GROUP = 16
TILE = 8
SLOTS = 4
STEPS = GROUP // SLOTS
MIB = 1024 * 1024


def rounded(table):
    return np.asarray(table, np.float32).astype(ml_dtypes.bfloat16)


def angles(freq, points, length):
    phase = np.mod(np.outer(freq, points), length)
    return (phase * (2.0 * math.pi / length)).astype(np.float64)


def signed(count):
    index = np.arange(count)
    return np.where(index < count // 2, index, index - count)


def z_base(rows_z):
    theta = angles(np.arange(MZ), np.arange(rows_z), rows_z)
    pair = np.stack([np.cos(theta), -np.sin(theta)])
    table = np.repeat(pair.reshape(2 * MZ, rows_z), GROUP, axis=0).T
    return rounded(table).astype(np.float32)


def y_table(rows_y, width):
    theta = angles(signed(MY), np.arange(rows_y), rows_y)
    cosine, sine = np.cos(theta), np.sin(theta)
    turn = np.stack([np.stack([cosine, sine]), np.stack([-sine, cosine])])
    table = np.einsum("rsjy,xw->jxrswy", turn, np.eye(width))
    return rounded(table.reshape(MY * width * 2, 2 * width * rows_y))


def x_tables(samples, slabs, length):
    theta = angles(signed(MX), np.arange(length), length)
    cosine, sine = np.cos(theta), np.sin(theta)
    forward = np.stack([np.stack([cosine, sine]), np.stack([-sine, cosine])])
    inverse = np.stack([np.stack([cosine, sine]), np.stack([-sine, cosine])]) / length
    same = np.eye(samples)
    rows = MX * 2 * samples

    def lay(turn):
        turn = turn.reshape(2, 2, MX, slabs, length // slabs)
        table = np.einsum("arqsx,bd->qabdsxr", turn, same)
        return rounded(table.reshape(rows, samples * length * 2))

    return lay(forward), lay(inverse)


def dot(left, right):
    return jnp.dot(left, right, preferred_element_type=F32)


def gelu_slope_rows(value):
    decay = jnp.exp2(value * value * (-0.5 * math.log2(math.e))).astype(BF16)
    cdf = (0.5 + 0.5 * lax.erf(value * math.sqrt(0.5))).astype(BF16)
    density = value.astype(BF16) * jnp.asarray(1.0 / math.sqrt(2.0 * math.pi), BF16)
    return cdf + density * decay


def over(index, size):
    return lax.shift_right_logical(index, jnp.int32(size.bit_length() - 1))


def within(index, size):
    return jnp.bitwise_and(index, jnp.int32(size - 1))


def fill_z(base, table):
    rows_z, lanes = base.shape
    owner = within(lax.broadcasted_iota(jnp.int32, (rows_z, lanes), 1), GROUP)
    values = base[...]
    for c in range(GROUP):
        table[c * rows_z : (c + 1) * rows_z] = jnp.where(owner == c, values, 0.0).astype(BF16)


def fill_z_back(base, table):
    lanes, rows_z = base.shape
    owner = within(lax.broadcasted_iota(jnp.int32, (lanes, rows_z), 0), GROUP)
    values = base[...]
    for c in range(GROUP):
        first = c % SLOTS * rows_z
        table[c // SLOTS, :, first : first + rows_z] = jnp.where(owner == c, values, 0.0).astype(BF16)


def grouped(lane, per, channels):
    c = within(lane, channels)
    return over(c, GROUP) * (MZ * GROUP) + over(lane, channels) * GROUP + within(c, GROUP)


def fill_order(per, channels, back, table):
    count = table.shape[0]
    row = lax.broadcasted_iota(jnp.int32, (count, count), 0)
    column = lax.broadcasted_iota(jnp.int32, (count, count), 1)
    if back:
        same = grouped(row[:, :1], per, channels) == column
    else:
        same = row == grouped(column[:1], per, channels)
    table[...] = jnp.where(same, 1.0, 0.0).astype(BF16)


def turned_index(index, slabs, devices):
    samples = devices // slabs
    return index % samples * slabs + index // samples


def deliver(spectra, ytab, order, scale, message, per, channels, slabs):
    groups = channels // GROUP
    rows = spectra.shape[0] // groups
    wide = spectra.shape[1] // 2
    halves = []
    for r in range(2):
        blocks = [spectra[g * rows : (g + 1) * rows, r * wide : (r + 1) * wide] for g in range(groups)]
        halves.append(jnp.concatenate(blocks, axis=1).astype(BF16))
    planes = dot(ytab[...], jnp.concatenate(halves, axis=0))
    if scale is not None:
        planes = planes * scale[...]
    ordered = dot(planes.astype(BF16), order[...]).astype(BF16)
    parts = MZ // per
    count = message.shape[1]
    lanes = per * channels
    for part in range(parts):
        block = ordered[:, part * lanes : (part + 1) * lanes]
        for j in range(MY):
            message[turned_index(j * parts + part, slabs, message.shape[0])] = block[j * count : (j + 1) * count]


def receive(message, order_back, ytab_back, scale, held, per, slabs):
    parts = MZ // per
    lanes = [
        jnp.concatenate(
            [message[turned_index(j * parts + part, slabs, message.shape[0])] for j in range(MY)], axis=0
        )
        for part in range(parts)
    ]
    ordered = dot(jnp.concatenate(lanes, axis=1), order_back[...]).astype(BF16)
    lines = dot(ytab_back[...], ordered)
    if scale is not None:
        lines = lines * scale[...]
    lines = lines.astype(BF16)
    rows = lines.shape[0] // 2
    wide = MZ * GROUP
    for group in range(held.shape[0] // rows):
        piece = lines[:, group * wide : (group + 1) * wide]
        held[group * rows : (group + 1) * rows] = jnp.concatenate([piece[:rows], piece[rows:]], axis=1)


class Move:
    def __init__(self, source, target, sems):
        self.source, self.target, self.sems = source, target, sems
        self.groups = target.shape[0] // GROUP

    def copies(self, step):
        for g in range(self.groups):
            run = pl.ds(g * GROUP + step * SLOTS, SLOTS)
            sem = self.sems.at[step * self.groups + g]
            yield pltpu.make_async_copy(self.source.at[run], self.target.at[run], sem)

    def start(self, step):
        for copy in self.copies(step):
            copy.start()

    def wait(self, step):
        for copy in self.copies(step):
            copy.wait()


def start_all(moves, step):
    for each in moves:
        each.start(step)


def add_spectra(field, ztab, first, count, spectra):
    groups = field.shape[0] // GROUP
    rows_z = field.shape[-1]
    rows = spectra.shape[0] // groups
    start = first * rows_z
    start = start if isinstance(first, int) else pl.multiple_of(start, count * rows_z)
    table = ztab[pl.ds(start, count * rows_z)]
    lanes = [
        jnp.concatenate([field[g * GROUP + first + slot].reshape(rows, rows_z) for g in range(groups)], axis=0)
        for slot in range(count)
    ]
    spectra[...] += dot(jnp.concatenate(lanes, axis=1), table)


def plane_kernel(
    per, channels, slabs, field, base_far, ytab_far, message, ztab, order, spectra, buffer, base, ytab, sems, table_sems
):
    incoming = Move(field.at[0], buffer, sems)
    base_copy = pltpu.make_async_copy(base_far, base, table_sems.at[0])
    ytab_copy = pltpu.make_async_copy(ytab_far, ytab, table_sems.at[1])
    base_copy.start()
    incoming.start(0)
    fill_order(per, channels, False, order)
    spectra[...] = jnp.zeros_like(spectra)
    incoming.start(1)
    base_copy.wait()
    fill_z(base, ztab)
    incoming.start(2)
    ytab_copy.start()
    incoming.start(3)

    @pl.loop(0, STEPS)
    def _(step):
        incoming.wait(step)
        add_spectra(buffer, ztab, step * SLOTS, SLOTS, spectra)

    ytab_copy.wait()
    deliver(spectra, ytab, order, None, message, per, channels, slabs)


def slope_kernel(
    per, channels, slabs, arrived, local, cotangent, base, base_back, ytab, ytab_back, scale,
    slope, message, ztab, ztab_back, order, held, spectra, local_in, cotangent_in, result, sums_a, sums_b, sums_c, sums_d,
    local_sems, cotangent_sems, result_sems,
):
    width, rows_y, rows_z = local.shape[1:]
    groups = channels // GROUP
    rows = width * rows_y
    wide = 2 * rows_y
    incoming = (Move(local, local_in, local_sems), Move(cotangent.at[0], cotangent_in, cotangent_sems))
    outgoing = Move(result, slope, result_sems)
    start_all(incoming, 0)
    fill_order(per, channels, True, order)
    receive(arrived, order, ytab_back, scale, held, per, slabs)
    start_all(incoming, 1)
    fill_z_back(base_back, ztab_back)
    fill_z(base, ztab)
    start_all(incoming, 2)
    fill_order(per, channels, False, order)
    spectra[...] = jnp.zeros_like(spectra)
    start_all(incoming, 3)

    totals = ((sums_a, sums_b), (sums_c, sums_d))

    def synthesise(step):
        for pair, total in enumerate(totals[step % 2]):
            total[...] = dot(held[...], ztab_back[step, :, 2 * pair * rows_z : 2 * (pair + 1) * rows_z])

    synthesise(0)
    for step in range(STEPS):
        for each in incoming:
            each.wait(step)
        if step + 1 < STEPS:
            synthesise(step + 1)
        for pair, total in enumerate(totals[step % 2]):
            for g in range(groups):
                for offset in range(2):
                    c = g * GROUP + step * SLOTS + 2 * pair + offset
                    for x in range(0, width, 2):
                        place = g * rows + x * rows_y
                        value = total[place : place + wide, offset * rows_z : (offset + 1) * rows_z]
                        value = value + local_in[c, x : x + 2].reshape(wide, rows_z).astype(F32)
                        upstream = cotangent_in[c, x : x + 2].reshape(wide, rows_z)
                        answer = upstream * gelu_slope_rows(value)
                        result[c, x : x + 2] = answer.reshape(2, rows_y, rows_z)
            add_spectra(result, ztab, step * SLOTS + 2 * pair, 2, spectra)
        outgoing.start(step)

    deliver(spectra, ytab, order, scale, message, per, channels, slabs)
    for step in range(STEPS):
        outgoing.wait(step)


def field_kernel(
    per, channels, slabs, arrived, local, base_back, ytab_back, out, ztab_back, order, held, local_in, result,
    local_sems, result_sems,
):
    width, rows_y, rows_z = local.shape[1:]
    groups = channels // GROUP
    rows = width * rows_y
    incoming = Move(local, local_in, local_sems)
    outgoing = Move(result, out.at[0], result_sems)
    incoming.start(0)
    fill_order(per, channels, True, order)
    incoming.start(1)
    receive(arrived, order, ytab_back, None, held, per, slabs)
    incoming.start(2)
    fill_z_back(base_back, ztab_back)
    incoming.start(3)

    @pl.loop(0, STEPS)
    def _(step):
        incoming.wait(step)
        for pair in range(SLOTS // 2):
            total = dot(held[...], ztab_back[step, :, 2 * pair * rows_z : 2 * (pair + 1) * rows_z])
            for g in range(groups):
                for offset in range(2):
                    c = g * GROUP + step * SLOTS + 2 * pair + offset
                    value = total[g * rows : (g + 1) * rows, offset * rows_z : (offset + 1) * rows_z]
                    value = value + local_in[c].reshape(rows, rows_z).astype(F32)
                    result[c] = value.astype(BF16).reshape(width, rows_y, rows_z)
        outgoing.start(step)

    for step in range(STEPS):
        outgoing.wait(step)


def pointwise_kernel(turned, field, mix, offsets, out, table, shift):
    channels = mix.shape[0]
    width, rows_y, rows_z = field.shape[1:]
    size = channels * TILE

    @pl.when(pl.program_id(0) == 0)
    def _():
        row = over(lax.broadcasted_iota(jnp.int32, (size, channels), 0), TILE)
        column = lax.broadcasted_iota(jnp.int32, (size, channels), 1)
        spread = jnp.where(row == column, 1.0, 0.0).astype(BF16)
        tall = lax.dot_general(
            spread, mix[...], (((1,), (1 if turned else 0,)), ((), ())), preferred_element_type=F32
        ).astype(BF16)
        whole = lax.dot_general(
            tall, spread, (((1,), (1,)), ((), ())), preferred_element_type=F32
        )
        place = within(lax.broadcasted_iota(jnp.int32, (size, size), 0), TILE)
        other = within(lax.broadcasted_iota(jnp.int32, (size, size), 1), TILE)
        table[...] = jnp.where(place == other, whole, 0.0).astype(BF16)
        if offsets is not None:
            for c in range(channels):
                shift[c] = jnp.full((1, rows_z), offsets[c], F32)

    for start in range(0, rows_y, 2 * TILE):
        pieces = [field[:, x, start : start + 2 * TILE, :].astype(F32) for x in range(width)]
        halves = []
        for row in range(0, 2 * TILE, TILE):
            rows = [piece[:, row : row + TILE].reshape(size, rows_z).astype(BF16) for piece in pieces]
            halves.append(dot(table[...], jnp.concatenate(rows, axis=1)))
        for x in range(width):
            values = [
                half[:, x * rows_z : (x + 1) * rows_z].reshape(channels, TILE, rows_z) for half in halves
            ]
            value = jnp.concatenate(values, axis=1)
            if offsets is not None:
                value = value + shift[...]
            out[:, x, start : start + 2 * TILE, :] = value.astype(BF16)


def spread_pair(first, second):
    nothing = jnp.zeros_like(first)
    upper = jnp.concatenate([first, nothing], axis=1)
    lower = jnp.concatenate([nothing, second], axis=1)
    return jnp.concatenate([upper, lower], axis=0)


def low_half(shape):
    return lax.broadcasted_iota(jnp.int32, shape, 1) < shape[1] // 2


def mix_kernel(per, samples, arrived, weights, line, line_back, spec_in, message, held):
    rows = 2 * samples
    lanes = 2 * weights.shape[1]
    low = low_half((samples, lanes))
    flat = arrived[...].reshape(-1, arrived.shape[2])
    spectra = dot(line[...], flat).astype(BF16)
    spec_in[...] = spectra
    for q in range(MX):
        for first in range(0, per, 2):
            block = spread_pair(weights[first * MX + q], weights[(first + 1) * MX + q])
            place = first // 2 * lanes
            terms = dot(spectra[q * rows : (q + 1) * rows, place : place + lanes], block)
            mixed = []
            for side in range(2):
                part = terms[:, side * lanes : (side + 1) * lanes]
                turned = pltpu.roll(part[samples:], lanes // 2, 1)
                mixed.append(part[:samples] + jnp.where(low, -turned, turned))
            real = jnp.where(low, mixed[0], pltpu.roll(mixed[1], lanes // 2, 1))
            imag = jnp.where(low, pltpu.roll(mixed[0], lanes // 2, 1), mixed[1])
            held[q * rows : (q + 1) * rows, place : place + lanes] = jnp.concatenate(
                [real, imag], axis=0
            ).astype(BF16)
    message[...] = dot(line_back[...], held[...]).astype(BF16).reshape(message.shape)


def mix_back_kernel(per, samples, arrived, weights, line, line_back, pairs, message, held):
    rows = 2 * samples
    lanes = 2 * weights.shape[1]
    low = low_half((samples, lanes))
    flat = arrived[...].reshape(-1, arrived.shape[2])
    spectra = dot(line[...], flat).astype(BF16).astype(F32)
    for q in range(MX):
        for first in range(0, per, 2):
            block = spread_pair(weights[first * MX + q], weights[(first + 1) * MX + q])
            place = first // 2 * lanes
            real = spectra[q * rows : q * rows + samples, place : place + lanes]
            imag = spectra[q * rows + samples : (q + 1) * rows, place : place + lanes]
            real_turned = pltpu.roll(real, lanes // 2, 1)
            imag_turned = pltpu.roll(imag, lanes // 2, 1)
            left = [jnp.where(low, real, imag_turned), jnp.where(low, imag, -real_turned)]
            right = [jnp.where(low, real_turned, imag), jnp.where(low, imag_turned, -real)]
            pair = jnp.concatenate(
                [jnp.concatenate(left, axis=0), jnp.concatenate(right, axis=0)], axis=1
            ).astype(BF16)
            pairs[q * rows : (q + 1) * rows, 2 * place : 2 * (place + lanes)] = pair
            held[q * rows : (q + 1) * rows, place : place + lanes] = lax.dot_general(
                pair, block, (((1,), (1,)), ((), ())), preferred_element_type=F32
            ).astype(BF16)
    message[...] = dot(line_back[...], held[...]).astype(BF16).reshape(message.shape)


def weight_kernel(per, samples, spec_in, pairs, out):
    rows = 2 * samples
    lanes = out.shape[2]
    half = lanes // 2
    for q in range(MX):
        for first in range(0, per, 2):
            place = first // 2 * lanes
            left = spec_in[q * rows : (q + 1) * rows, place : place + lanes]
            right = pairs[q * rows : (q + 1) * rows, 2 * place : 2 * (place + lanes)]
            outer = lax.dot_general(
                left, right, (((0,), (0,)), ((), ())), preferred_element_type=F32
            )
            out[first * MX + q] = outer[:half, :lanes]
            out[(first + 1) * MX + q] = outer[half:, lanes:]


def whole(array):
    return pl.BlockSpec(array.shape, lambda *step: (0,) * len(array.shape))


def shaped(shape, dtype):
    return jax.ShapeDtypeStruct(shape, dtype)


def params(mib):
    return pltpu.CompilerParams(vmem_limit_bytes=mib * MIB)


def cost(flops, moved, steep=0):
    return pl.CostEstimate(flops=flops, bytes_accessed=moved, transcendentals=steep)


def body(mesh_axes, devices, slabs, activations, cotangent, mode_weights, pointwise, offsets):
    _, channels, width, rows_y, rows_z = activations.shape
    samples = devices // slabs
    per = MY * MZ // devices
    groups = channels // GROUP
    field = activations.shape[1:]
    count = math.prod(field)
    base = z_base(rows_z)
    ytab = y_table(rows_y, width)
    line_fwd, line_inv = x_tables(samples, slabs, NX)
    weight = np.where(np.arange(MZ) == 0, 1.0, 2.0) / (rows_y * rows_z)
    scale = np.tile(np.repeat(weight, GROUP), groups).astype(np.float32)[None]
    base_t, ytab_t = (np.ascontiguousarray(t.T) for t in (base, ytab))
    fwd_t, inv_t = (np.ascontiguousarray(t.T) for t in (line_fwd, line_inv))
    message = shaped((devices, 2 * width, per * channels), BF16)
    spectra = shaped((MX * 2 * samples, per * channels), BF16)
    ztab = pltpu.VMEM((GROUP * rows_z, 2 * MZ * GROUP), BF16)
    ztab_t = pltpu.VMEM((STEPS, 2 * MZ * GROUP, SLOTS * rows_z), BF16)
    order = pltpu.VMEM((MZ * channels, MZ * channels), BF16)
    rows = groups * width * rows_y
    held = pltpu.VMEM((rows, 2 * MZ * GROUP), BF16)
    sums = pltpu.VMEM((rows, 2 * MZ * GROUP), F32)
    pair_sums = pltpu.VMEM((rows, 2 * rows_z), F32)
    buffer = pltpu.VMEM(field, BF16)
    sems = pltpu.SemaphoreType.DMA((STEPS * groups,))
    far = pl.BlockSpec(memory_space=pltpu.HBM)
    far_field = pltpu.HBM(field, BF16)

    def kept_far(array):
        return pltpu.with_memory_space_constraint(array, pltpu.HBM)

    plane_flops = 2 * count * 2 * MZ * GROUP

    def exchange(array):
        return lax.all_to_all(array, mesh_axes, split_axis=0, concat_axis=0, tiled=True)

    def mix_points(values, turned, shifts):
        step = 2
        block = pl.BlockSpec((channels, step, rows_y, rows_z), lambda x: (0, x, 0, 0))
        kernel = functools.partial(pointwise_kernel, turned)
        specs = [block, whole(pointwise)]
        operands = [values, pointwise]
        if shifts is None:
            run = lambda a, b, *rest: kernel(a, b, None, *rest)
        else:
            run = kernel
            specs.append(pl.BlockSpec(memory_space=pltpu.SMEM))
            operands.append(shifts)
        return pl.pallas_call(
            run,
            grid=(width // step,),
            in_specs=specs,
            out_specs=block,
            out_shape=far_field,
            scratch_shapes=[
                pltpu.VMEM((channels * TILE, channels * TILE), BF16),
                pltpu.VMEM((channels, 1, rows_z), F32),
            ],
            compiler_params=params(32),
            cost_estimate=cost(2 * count * channels * TILE, 4 * count),
        )(*operands)

    planes = pl.pallas_call(
        functools.partial(plane_kernel, per, channels, slabs),
        in_specs=[far, far, far],
        out_specs=whole(message),
        out_shape=message,
        scratch_shapes=[
            ztab,
            order,
            sums,
            buffer,
            pltpu.VMEM(base.shape, F32),
            pltpu.VMEM(ytab.shape, BF16),
            sems,
            pltpu.SemaphoreType.DMA((2,)),
        ],
        compiler_params=params(32),
        cost_estimate=cost(plane_flops, 2 * count),
    )(kept_far(activations), kept_far(base), kept_far(ytab))
    arrived = exchange(planes)
    local = mix_points(kept_far(activations.reshape(field)), True, offsets)
    arrived, local = lax.optimization_barrier((arrived, local))
    spec_in, mixed = pl.pallas_call(
        functools.partial(mix_kernel, per, samples),
        out_shape=(spectra, message),
        scratch_shapes=[pltpu.VMEM(spectra.shape, BF16)],
        compiler_params=params(16),
        cost_estimate=cost(10**8, 2 * mode_weights.size),
    )(arrived, mode_weights, line_fwd, inv_t)
    returned = exchange(mixed)
    slope, back_plane = pl.pallas_call(
        functools.partial(slope_kernel, per, channels, slabs),
        in_specs=[whole(message), far, far]
        + [whole(t) for t in (base, base_t, ytab, ytab_t, scale)],
        out_specs=(far, whole(message)),
        out_shape=(far_field, message),
        scratch_shapes=[ztab, ztab_t, order, held, sums]
        + [buffer] * 3
        + [pair_sums] * 4
        + [sems] * 3,
        compiler_params=params(40),
        cost_estimate=cost(2 * plane_flops, 6 * count, 2 * count),
    )(returned, kept_far(local), kept_far(cotangent), base, base_t, ytab, ytab_t, scale)
    arrived_back = exchange(back_plane)
    local_back = mix_points(kept_far(slope), False, None)
    arrived_back, local_back = lax.optimization_barrier((arrived_back, local_back))
    pairs, mixed_back = pl.pallas_call(
        functools.partial(mix_back_kernel, per, samples),
        out_shape=(shaped((spectra.shape[0], 2 * spectra.shape[1]), BF16), message),
        scratch_shapes=[pltpu.VMEM(spectra.shape, BF16)],
        compiler_params=params(16),
        cost_estimate=cost(10**8, 2 * mode_weights.size),
    )(arrived_back, mode_weights, line_inv, fwd_t)
    returned_back = exchange(mixed_back)
    grad_spectral = pl.pallas_call(
        functools.partial(weight_kernel, per, samples),
        out_shape=shaped(mode_weights.shape, F32),
        compiler_params=params(16),
        cost_estimate=cost(10**8, 4 * mode_weights.size),
    )(spec_in, pairs)
    grad_in = pl.pallas_call(
        functools.partial(field_kernel, per, channels, slabs),
        in_specs=[whole(message), far, whole(base_t), whole(ytab_t)],
        out_specs=far,
        out_shape=shaped(activations.shape, BF16),
        scratch_shapes=[ztab_t, order, held, buffer, buffer, sems, sems],
        compiler_params=params(32),
        cost_estimate=cost(plane_flops, 4 * count),
    )(returned_back, kept_far(local_back), base_t, ytab_t)
    return (grad_in, grad_spectral)


def chosen_body(mesh_axes, devices, slabs, activations, cotangent, mode_weights, pointwise, offsets):
    samples, channels, width, rows_y, rows_z = activations.shape
    per = MY * MZ // devices
    fits = (
        samples == 1
        and MY * MZ % devices == 0
        and per in (2, 4, 8)
        and width % 8 == 0
        and channels == 64
        and rows_y % TILE == 0
        and rows_z == 128
    )
    plan = functools.partial(body, mesh_axes, devices, slabs) if fits else general_body
    return plan(activations, cotangent, mode_weights, pointwise, offsets)


def solution(mesh):
    slabs = mesh.shape["space"]
    devices = slabs * mesh.shape["dp"]
    return jax.shard_map(
        functools.partial(chosen_body, ("dp", "space"), devices, slabs),
        mesh=mesh,
        in_specs=(
            P("dp", None, "space", None, None),
            P("dp", None, "space", None, None),
            P(("space", "dp"), None, None),
            P(),
            P(),
        ),
        out_specs=(P("dp", None, "space", None, None), P(("space", "dp"), None, None)),
        check_vma=False,
    )
```

```python
import functools
import math

import jax
import jax.numpy as jnp
import ml_dtypes
import numpy as np
from jax import lax
from jax.experimental import pallas as pl
from jax.experimental.pallas import tpu as pltpu
from jax.sharding import PartitionSpec as P

MX = 16
MY = 16
MZ = 8
NX = 32


def centered(count):
    index = jnp.arange(count, dtype=jnp.int32)
    return jnp.where(index < count // 2, index, index - count)


def plane_tables(rows_y, rows_z, modes_y, modes_z):
    along_y = jnp.arange(rows_y, dtype=jnp.int32)[:, None, None, None]
    along_z = jnp.arange(rows_z, dtype=jnp.int32)[None, :, None, None]
    freq_y = centered(modes_y)[None, None, :, None]
    freq_z = jnp.arange(modes_z, dtype=jnp.int32)[None, None, None, :]
    phase = jnp.mod(freq_y * along_y * rows_z + freq_z * along_z * rows_y, rows_y * rows_z)
    theta = phase.astype(jnp.float32) * (2.0 * math.pi / (rows_y * rows_z))
    cosine = jnp.cos(theta)
    sine = jnp.sin(theta)
    forward = jnp.stack([cosine, -sine], -1).reshape(rows_y * rows_z, modes_y * modes_z * 2)
    scaled = jnp.where(freq_z == 0, 1.0, 2.0).astype(jnp.float32) / (rows_y * rows_z)
    inverse = (
        jnp.stack([cosine * scaled, -sine * scaled], -1)
        .reshape(rows_y * rows_z, modes_y * modes_z * 2)
        .T
    )
    return (forward.astype(jnp.bfloat16), inverse.astype(jnp.bfloat16))


def line_tables(length, modes):
    along = jnp.arange(length, dtype=jnp.int32)[:, None]
    freq = centered(modes)[None, :]
    phase = jnp.mod(freq * along, length)
    theta = phase.astype(jnp.float32) * (2.0 * math.pi / length)
    cosine = jnp.cos(theta)
    sine = jnp.sin(theta)
    first = jnp.stack([cosine, -sine], -1)
    second = jnp.stack([sine, cosine], -1)
    forward = jnp.stack([first, second], 1).reshape(2 * length, 2 * modes)
    inv_first = jnp.stack([cosine.T, sine.T], -1) / length
    inv_second = jnp.stack([-sine.T, cosine.T], -1) / length
    inverse = jnp.stack([inv_first, inv_second], 1).reshape(2 * modes, 2 * length)
    return (forward.astype(jnp.bfloat16), inverse.astype(jnp.bfloat16))


def expand_weights(weights):
    half = weights.shape[1]
    real_part = weights[:, :, :half]
    imag_part = weights[:, :, half:]
    upper = jnp.concatenate([real_part, imag_part], axis=2)
    lower = jnp.concatenate([-imag_part, real_part], axis=2)
    return jnp.concatenate([upper, lower], axis=1)


def outer_sum(left, right):
    return jnp.einsum("mbi,mbo->mio", left, right, preferred_element_type=jnp.float32)


def weight_terms(spec_in, spec_grad):
    half = spec_in.shape[2] // 2
    in_real = spec_in[:, :, :half]
    in_imag = spec_in[:, :, half:]
    gr_real = spec_grad[:, :, :half]
    gr_imag = spec_grad[:, :, half:]
    real_term = outer_sum(in_real, gr_real) + outer_sum(in_imag, gr_imag)
    imag_term = outer_sum(in_real, gr_imag) - outer_sum(in_imag, gr_real)
    return jnp.concatenate([real_term, imag_term], axis=2)


def to_modes(slab, table, modes_x):
    samples, channels, width, pairs = slab.shape
    moved = lax.all_to_all(slab, "space", split_axis=3, concat_axis=2, tiled=True)
    length = moved.shape[2]
    local = moved.shape[3] // 2
    lines = moved.reshape(samples, channels, length, local, 2).transpose(0, 1, 3, 2, 4)
    lines = lines.reshape(samples, channels, local, 2 * length)
    spectra = jnp.dot(lines, table, preferred_element_type=jnp.float32).astype(jnp.bfloat16)
    spectra = spectra.reshape(samples, channels, local, modes_x, 2).transpose(2, 3, 0, 4, 1)
    return spectra.reshape(local * modes_x, samples, 2 * channels)


def to_slab(spectra, table, modes_x, channels):
    count, samples, doubled = spectra.shape
    local = count // modes_x
    lines = spectra.reshape(local, modes_x, samples, 2, channels).transpose(2, 4, 0, 1, 3)
    lines = lines.reshape(samples, channels, local, 2 * modes_x)
    lines = jnp.dot(lines, table, preferred_element_type=jnp.float32).astype(jnp.bfloat16)
    length = lines.shape[3] // 2
    lines = lines.reshape(samples, channels, local, length, 2).transpose(0, 1, 3, 2, 4)
    lines = lines.reshape(samples, channels, length, 2 * local)
    return lax.all_to_all(lines, "space", split_axis=2, concat_axis=3, tiled=True)


def to_owners(spectra):
    return lax.all_to_all(spectra, "dp", split_axis=0, concat_axis=1, tiled=True)


def from_owners(spectra):
    return lax.all_to_all(spectra, "dp", split_axis=1, concat_axis=0, tiled=True)


def gelu_slope(value):
    cdf = 0.5 * (1.0 + lax.erf(value * 0.7071067811865476))
    density = jnp.exp(-0.5 * value * value) * 0.3989422804014327
    return cdf + value * density


def general_body(activations, cotangent, mode_weights, pointwise, offsets):
    samples, channels, width, rows_y, rows_z = activations.shape
    plane_fwd, plane_inv = plane_tables(rows_y, rows_z, MY, MZ)
    line_fwd, line_inv = line_tables(NX, MX)
    flat = activations.reshape(samples, channels, width, rows_y * rows_z)
    planes = jnp.dot(flat, plane_fwd, preferred_element_type=jnp.float32).astype(jnp.bfloat16)
    spec_in = to_modes(planes, line_fwd, MX)
    blocks = expand_weights(mode_weights)
    held_in = to_owners(spec_in)
    held_out = jnp.einsum(
        "mbi,mio->mbo", held_in, blocks, preferred_element_type=jnp.float32
    ).astype(jnp.bfloat16)
    spec_out = from_owners(held_out)
    returned = to_slab(spec_out, line_inv, MX, channels)
    spectral = jnp.dot(returned, plane_inv, preferred_element_type=jnp.float32)
    local_part = jnp.einsum("io,bixn->boxn", pointwise, flat, preferred_element_type=jnp.float32)
    summed = spectral + local_part + offsets[None, :, None, None]
    upstream = cotangent.reshape(flat.shape).astype(jnp.float32)
    slope_grad = (upstream * gelu_slope(summed)).astype(jnp.bfloat16)
    back_plane = jnp.dot(slope_grad, plane_inv.T, preferred_element_type=jnp.float32).astype(
        jnp.bfloat16
    )
    spec_grad = to_modes(back_plane, line_inv.T, MX)
    held_grad = to_owners(spec_grad)
    held_dx = jnp.einsum(
        "mbo,mio->mbi", held_grad, blocks, preferred_element_type=jnp.float32
    ).astype(jnp.bfloat16)
    spec_dx = from_owners(held_dx)
    grad_spectral = weight_terms(held_in, held_grad)
    line_dx = to_slab(spec_dx, line_fwd.T, MX, channels)
    total = jnp.dot(line_dx, plane_fwd.T, preferred_element_type=jnp.float32)
    total = total + jnp.einsum(
        "io,boxn->bixn", pointwise, slope_grad, preferred_element_type=jnp.float32
    )
    grad_in = total.astype(jnp.bfloat16).reshape(activations.shape)
    return (grad_in, grad_spectral)


BF16 = jnp.bfloat16
F32 = jnp.float32
GROUP = 16
TILE = 8
SLOTS = 4
STEPS = GROUP // SLOTS
MIB = 1024 * 1024


def rounded(table):
    return np.asarray(table, np.float32).astype(ml_dtypes.bfloat16)


def angles(freq, points, length):
    phase = np.mod(np.outer(freq, points), length)
    return (phase * (2.0 * math.pi / length)).astype(np.float64)


def signed(count):
    index = np.arange(count)
    return np.where(index < count // 2, index, index - count)


def z_base(rows_z):
    theta = angles(np.arange(MZ), np.arange(rows_z), rows_z)
    pair = np.stack([np.cos(theta), -np.sin(theta)])
    table = np.repeat(pair.reshape(2 * MZ, rows_z), GROUP, axis=0).T
    return rounded(table).astype(np.float32)


def y_table(rows_y, width):
    theta = angles(signed(MY), np.arange(rows_y), rows_y)
    cosine, sine = np.cos(theta), np.sin(theta)
    turn = np.stack([np.stack([cosine, sine]), np.stack([-sine, cosine])])
    table = np.einsum("rsjy,xw->jxrswy", turn, np.eye(width))
    return rounded(table.reshape(MY * width * 2, 2 * width * rows_y))


def x_tables(samples, slabs, length):
    theta = angles(signed(MX), np.arange(length), length)
    cosine, sine = np.cos(theta), np.sin(theta)
    forward = np.stack([np.stack([cosine, sine]), np.stack([-sine, cosine])])
    inverse = np.stack([np.stack([cosine, sine]), np.stack([-sine, cosine])]) / length
    same = np.eye(samples)
    rows = MX * 2 * samples

    def lay(turn):
        turn = turn.reshape(2, 2, MX, slabs, length // slabs)
        table = np.einsum("arqsx,bd->qabdsxr", turn, same)
        return rounded(table.reshape(rows, samples * length * 2))

    return lay(forward), lay(inverse)


def dot(left, right):
    return jnp.dot(left, right, preferred_element_type=F32)


def gelu_slope_times(value, upstream):
    decay = jnp.exp2(value * value * (-0.5 * math.log2(math.e))).astype(BF16)
    value = value.astype(BF16)

    def number(x):
        return jnp.asarray(x, BF16)

    size = jnp.abs(value)
    t = pl.reciprocal(number(1.0) + number(0.47047 * math.sqrt(0.5)) * size, approx=True)
    tail = (number(0.5 * 0.7478556) * t - number(0.5 * 0.0958798)) * t + number(0.5 * 0.3480242)
    part = (tail * t - size * number(1.0 / math.sqrt(2.0 * math.pi))) * decay * upstream
    return jnp.where(value >= number(0.0), upstream - part, part)


def over(index, size):
    return lax.shift_right_logical(index, jnp.int32(size.bit_length() - 1))


def within(index, size):
    return jnp.bitwise_and(index, jnp.int32(size - 1))


def fill_z(base, table):
    rows_z, lanes = base.shape
    owner = within(lax.broadcasted_iota(jnp.int32, (rows_z, lanes), 1), GROUP)
    values = base[...]
    for c in range(GROUP):
        table[c * rows_z : (c + 1) * rows_z] = jnp.where(owner == c, values, 0.0).astype(BF16)


def fill_z_back(base, table):
    lanes, rows_z = base.shape
    owner = within(lax.broadcasted_iota(jnp.int32, (lanes, rows_z), 0), GROUP)
    values = base[...]
    for c in range(GROUP):
        first = c % SLOTS * rows_z
        table[c // SLOTS, :, first : first + rows_z] = jnp.where(owner == c, values, 0.0).astype(BF16)


def grouped(lane, per, channels):
    c = within(lane, channels)
    return over(c, GROUP) * (MZ * GROUP) + over(lane, channels) * GROUP + within(c, GROUP)


def fill_order(per, channels, back, table):
    count = table.shape[0]
    row = lax.broadcasted_iota(jnp.int32, (count, count), 0)
    column = lax.broadcasted_iota(jnp.int32, (count, count), 1)
    if back:
        same = grouped(row[:, :1], per, channels) == column
    else:
        same = row == grouped(column[:1], per, channels)
    table[...] = jnp.where(same, 1.0, 0.0).astype(BF16)


def turned_index(index, slabs, devices):
    samples = devices // slabs
    return index % samples * slabs + index // samples


def deliver(spectra, ytab, order, scale, message, per, channels, slabs):
    groups = channels // GROUP
    rows = spectra.shape[0] // groups
    wide = spectra.shape[1] // 2
    halves = []
    for r in range(2):
        blocks = [spectra[g * rows : (g + 1) * rows, r * wide : (r + 1) * wide] for g in range(groups)]
        halves.append(jnp.concatenate(blocks, axis=1).astype(BF16))
    planes = dot(ytab[...], jnp.concatenate(halves, axis=0))
    if scale is not None:
        planes = planes * scale[...]
    ordered = dot(planes.astype(BF16), order[...]).astype(BF16)
    parts = MZ // per
    count = message.shape[1]
    lanes = per * channels
    for part in range(parts):
        block = ordered[:, part * lanes : (part + 1) * lanes]
        for j in range(MY):
            message[turned_index(j * parts + part, slabs, message.shape[0])] = block[j * count : (j + 1) * count]


def receive(message, order_back, ytab_back, scale, held, per, slabs):
    parts = MZ // per
    lanes = [
        jnp.concatenate(
            [message[turned_index(j * parts + part, slabs, message.shape[0])] for j in range(MY)], axis=0
        )
        for part in range(parts)
    ]
    ordered = dot(jnp.concatenate(lanes, axis=1), order_back[...]).astype(BF16)
    lines = dot(ytab_back[...], ordered)
    if scale is not None:
        lines = lines * scale[...]
    lines = lines.astype(BF16)
    rows = lines.shape[0] // 2
    wide = MZ * GROUP
    for group in range(held.shape[0] // rows):
        piece = lines[:, group * wide : (group + 1) * wide]
        held[group * rows : (group + 1) * rows] = jnp.concatenate([piece[:rows], piece[rows:]], axis=1)


class Move:
    def __init__(self, source, target, sems):
        self.source, self.target, self.sems = source, target, sems
        self.groups = target.shape[0] // GROUP

    def copies(self, step):
        for g in range(self.groups):
            run = pl.ds(g * GROUP + step * SLOTS, SLOTS)
            sem = self.sems.at[step * self.groups + g]
            yield pltpu.make_async_copy(self.source.at[run], self.target.at[run], sem)

    def start(self, step):
        for copy in self.copies(step):
            copy.start()

    def wait(self, step):
        for copy in self.copies(step):
            copy.wait()


def start_all(moves, step):
    for each in moves:
        each.start(step)


def add_spectra(field, ztab, first, count, spectra):
    groups = field.shape[0] // GROUP
    rows_z = field.shape[-1]
    rows = spectra.shape[0] // groups
    start = first * rows_z
    start = start if isinstance(first, int) else pl.multiple_of(start, count * rows_z)
    table = ztab[pl.ds(start, count * rows_z)]
    lanes = [
        jnp.concatenate([field[g * GROUP + first + slot].reshape(rows, rows_z) for g in range(groups)], axis=0)
        for slot in range(count)
    ]
    spectra[...] += dot(jnp.concatenate(lanes, axis=1), table)


def plane_kernel(
    per, channels, slabs, field, base_far, ytab_far, message, ztab, order, spectra, buffer, base, ytab, sems, table_sems
):
    incoming = Move(field.at[0], buffer, sems)
    base_copy = pltpu.make_async_copy(base_far, base, table_sems.at[0])
    ytab_copy = pltpu.make_async_copy(ytab_far, ytab, table_sems.at[1])
    base_copy.start()
    incoming.start(0)
    fill_order(per, channels, False, order)
    spectra[...] = jnp.zeros_like(spectra)
    incoming.start(1)
    base_copy.wait()
    fill_z(base, ztab)
    incoming.start(2)
    ytab_copy.start()
    incoming.start(3)

    @pl.loop(0, STEPS)
    def _(step):
        incoming.wait(step)
        add_spectra(buffer, ztab, step * SLOTS, SLOTS, spectra)

    ytab_copy.wait()
    deliver(spectra, ytab, order, None, message, per, channels, slabs)


def slope_kernel(
    per, channels, slabs, arrived, local, cotangent, base, base_back, ytab, ytab_back, scale,
    slope, message, ztab, ztab_back, order, held, spectra, local_in, cotangent_in, result, first_sum, second_sum,
    local_sems, cotangent_sems, result_sems,
):
    width, rows_y, rows_z = local.shape[1:]
    groups = channels // GROUP
    rows = width * rows_y
    wide = 2 * rows_y
    incoming = (Move(local, local_in, local_sems), Move(cotangent.at[0], cotangent_in, cotangent_sems))
    outgoing = Move(result, slope, result_sems)
    start_all(incoming, 0)
    fill_order(per, channels, True, order)
    receive(arrived, order, ytab_back, scale, held, per, slabs)
    start_all(incoming, 1)
    fill_z_back(base_back, ztab_back)
    fill_z(base, ztab)
    start_all(incoming, 2)
    fill_order(per, channels, False, order)
    spectra[...] = jnp.zeros_like(spectra)
    start_all(incoming, 3)

    @pl.loop(0, STEPS)
    def _(step):
        for each in incoming:
            each.wait(step)
        for pair, total in enumerate((first_sum, second_sum)):
            total[...] = dot(held[...], ztab_back[step, :, 2 * pair * rows_z : 2 * (pair + 1) * rows_z])
        for pair, total in enumerate((first_sum, second_sum)):
            for g in range(groups):
                for offset in range(2):
                    c = g * GROUP + step * SLOTS + 2 * pair + offset
                    for x in range(0, width, 2):
                        place = g * rows + x * rows_y
                        value = total[place : place + wide, offset * rows_z : (offset + 1) * rows_z]
                        value = value + local_in[c, x : x + 2].reshape(wide, rows_z).astype(F32)
                        upstream = cotangent_in[c, x : x + 2].reshape(wide, rows_z)
                        answer = gelu_slope_times(value, upstream)
                        result[c, x : x + 2] = answer.reshape(2, rows_y, rows_z)
            add_spectra(result, ztab, step * SLOTS + 2 * pair, 2, spectra)
        outgoing.start(step)

    deliver(spectra, ytab, order, scale, message, per, channels, slabs)
    for step in range(STEPS):
        outgoing.wait(step)


def field_kernel(
    per, channels, slabs, arrived, local, base_back, ytab_back, out, ztab_back, order, held, local_in, result,
    local_sems, result_sems,
):
    width, rows_y, rows_z = local.shape[1:]
    groups = channels // GROUP
    rows = width * rows_y
    incoming = Move(local, local_in, local_sems)
    outgoing = Move(result, out.at[0], result_sems)
    incoming.start(0)
    fill_order(per, channels, True, order)
    incoming.start(1)
    receive(arrived, order, ytab_back, None, held, per, slabs)
    incoming.start(2)
    fill_z_back(base_back, ztab_back)
    incoming.start(3)

    @pl.loop(0, STEPS)
    def _(step):
        incoming.wait(step)
        for pair in range(SLOTS // 2):
            total = dot(held[...], ztab_back[step, :, 2 * pair * rows_z : 2 * (pair + 1) * rows_z])
            for g in range(groups):
                for offset in range(2):
                    c = g * GROUP + step * SLOTS + 2 * pair + offset
                    value = total[g * rows : (g + 1) * rows, offset * rows_z : (offset + 1) * rows_z]
                    value = value + local_in[c].reshape(rows, rows_z).astype(F32)
                    result[c] = value.astype(BF16).reshape(width, rows_y, rows_z)
        outgoing.start(step)

    for step in range(STEPS):
        outgoing.wait(step)


def pointwise_kernel(turned, field, mix, offsets, out, table, shift):
    channels = mix.shape[0]
    width, rows_y, rows_z = field.shape[1:]
    size = channels * TILE

    @pl.when(pl.program_id(0) == 0)
    def _():
        row = over(lax.broadcasted_iota(jnp.int32, (size, channels), 0), TILE)
        column = lax.broadcasted_iota(jnp.int32, (size, channels), 1)
        spread = jnp.where(row == column, 1.0, 0.0).astype(BF16)
        tall = lax.dot_general(
            spread, mix[...], (((1,), (1 if turned else 0,)), ((), ())), preferred_element_type=F32
        ).astype(BF16)
        whole = lax.dot_general(
            tall, spread, (((1,), (1,)), ((), ())), preferred_element_type=F32
        )
        place = within(lax.broadcasted_iota(jnp.int32, (size, size), 0), TILE)
        other = within(lax.broadcasted_iota(jnp.int32, (size, size), 1), TILE)
        table[...] = jnp.where(place == other, whole, 0.0).astype(BF16)
        if offsets is not None:
            for c in range(channels):
                shift[c] = jnp.full((1, rows_z), offsets[c], F32)

    for start in range(0, rows_y, 2 * TILE):
        pieces = [field[:, x, start : start + 2 * TILE, :].astype(F32) for x in range(width)]
        halves = []
        for row in range(0, 2 * TILE, TILE):
            rows = [piece[:, row : row + TILE].reshape(size, rows_z).astype(BF16) for piece in pieces]
            halves.append(dot(table[...], jnp.concatenate(rows, axis=1)))
        for x in range(width):
            values = [
                half[:, x * rows_z : (x + 1) * rows_z].reshape(channels, TILE, rows_z) for half in halves
            ]
            value = jnp.concatenate(values, axis=1)
            if offsets is not None:
                value = value + shift[...]
            out[:, x, start : start + 2 * TILE, :] = value.astype(BF16)


def spread_pair(first, second):
    nothing = jnp.zeros_like(first)
    upper = jnp.concatenate([first, nothing], axis=1)
    lower = jnp.concatenate([nothing, second], axis=1)
    return jnp.concatenate([upper, lower], axis=0)


def low_half(shape):
    return lax.broadcasted_iota(jnp.int32, shape, 1) < shape[1] // 2


def mix_kernel(per, samples, arrived, weights, line, line_back, spec_in, message, held):
    rows = 2 * samples
    lanes = 2 * weights.shape[1]
    low = low_half((samples, lanes))
    flat = arrived[...].reshape(-1, arrived.shape[2])
    spectra = dot(line[...], flat).astype(BF16)
    spec_in[...] = spectra
    for q in range(MX):
        for first in range(0, per, 2):
            block = spread_pair(weights[first * MX + q], weights[(first + 1) * MX + q])
            place = first // 2 * lanes
            terms = dot(spectra[q * rows : (q + 1) * rows, place : place + lanes], block)
            mixed = []
            for side in range(2):
                part = terms[:, side * lanes : (side + 1) * lanes]
                turned = pltpu.roll(part[samples:], lanes // 2, 1)
                mixed.append(part[:samples] + jnp.where(low, -turned, turned))
            real = jnp.where(low, mixed[0], pltpu.roll(mixed[1], lanes // 2, 1))
            imag = jnp.where(low, pltpu.roll(mixed[0], lanes // 2, 1), mixed[1])
            held[q * rows : (q + 1) * rows, place : place + lanes] = jnp.concatenate(
                [real, imag], axis=0
            ).astype(BF16)
    message[...] = dot(line_back[...], held[...]).astype(BF16).reshape(message.shape)


def mix_back_kernel(per, samples, arrived, weights, line, line_back, pairs, message, held):
    rows = 2 * samples
    lanes = 2 * weights.shape[1]
    low = low_half((samples, lanes))
    flat = arrived[...].reshape(-1, arrived.shape[2])
    spectra = dot(line[...], flat).astype(BF16).astype(F32)
    for q in range(MX):
        for first in range(0, per, 2):
            block = spread_pair(weights[first * MX + q], weights[(first + 1) * MX + q])
            place = first // 2 * lanes
            real = spectra[q * rows : q * rows + samples, place : place + lanes]
            imag = spectra[q * rows + samples : (q + 1) * rows, place : place + lanes]
            real_turned = pltpu.roll(real, lanes // 2, 1)
            imag_turned = pltpu.roll(imag, lanes // 2, 1)
            left = [jnp.where(low, real, imag_turned), jnp.where(low, imag, -real_turned)]
            right = [jnp.where(low, real_turned, imag), jnp.where(low, imag_turned, -real)]
            pair = jnp.concatenate(
                [jnp.concatenate(left, axis=0), jnp.concatenate(right, axis=0)], axis=1
            ).astype(BF16)
            pairs[q * rows : (q + 1) * rows, 2 * place : 2 * (place + lanes)] = pair
            held[q * rows : (q + 1) * rows, place : place + lanes] = lax.dot_general(
                pair, block, (((1,), (1,)), ((), ())), preferred_element_type=F32
            ).astype(BF16)
    message[...] = dot(line_back[...], held[...]).astype(BF16).reshape(message.shape)


def weight_kernel(per, samples, spec_in, pairs, out):
    rows = 2 * samples
    lanes = out.shape[2]
    half = lanes // 2
    for q in range(MX):
        for first in range(0, per, 2):
            place = first // 2 * lanes
            left = spec_in[q * rows : (q + 1) * rows, place : place + lanes]
            right = pairs[q * rows : (q + 1) * rows, 2 * place : 2 * (place + lanes)]
            outer = lax.dot_general(
                left, right, (((0,), (0,)), ((), ())), preferred_element_type=F32
            )
            out[first * MX + q] = outer[:half, :lanes]
            out[(first + 1) * MX + q] = outer[half:, lanes:]


def whole(array):
    return pl.BlockSpec(array.shape, lambda *step: (0,) * len(array.shape))


def shaped(shape, dtype):
    return jax.ShapeDtypeStruct(shape, dtype)


def params(mib):
    return pltpu.CompilerParams(vmem_limit_bytes=mib * MIB)


def cost(flops, moved, steep=0):
    return pl.CostEstimate(flops=flops, bytes_accessed=moved, transcendentals=steep)


def body(mesh_axes, devices, slabs, activations, cotangent, mode_weights, pointwise, offsets):
    _, channels, width, rows_y, rows_z = activations.shape
    samples = devices // slabs
    per = MY * MZ // devices
    groups = channels // GROUP
    field = activations.shape[1:]
    count = math.prod(field)
    base = z_base(rows_z)
    ytab = y_table(rows_y, width)
    line_fwd, line_inv = x_tables(samples, slabs, NX)
    weight = np.where(np.arange(MZ) == 0, 1.0, 2.0) / (rows_y * rows_z)
    scale = np.tile(np.repeat(weight, GROUP), groups).astype(np.float32)[None]
    base_t, ytab_t = (np.ascontiguousarray(t.T) for t in (base, ytab))
    fwd_t, inv_t = (np.ascontiguousarray(t.T) for t in (line_fwd, line_inv))
    message = shaped((devices, 2 * width, per * channels), BF16)
    spectra = shaped((MX * 2 * samples, per * channels), BF16)
    ztab = pltpu.VMEM((GROUP * rows_z, 2 * MZ * GROUP), BF16)
    ztab_t = pltpu.VMEM((STEPS, 2 * MZ * GROUP, SLOTS * rows_z), BF16)
    order = pltpu.VMEM((MZ * channels, MZ * channels), BF16)
    rows = groups * width * rows_y
    held = pltpu.VMEM((rows, 2 * MZ * GROUP), BF16)
    sums = pltpu.VMEM((rows, 2 * MZ * GROUP), F32)
    pair_sums = pltpu.VMEM((rows, 2 * rows_z), F32)
    buffer = pltpu.VMEM(field, BF16)
    sems = pltpu.SemaphoreType.DMA((STEPS * groups,))
    far = pl.BlockSpec(memory_space=pltpu.HBM)
    far_field = pltpu.HBM(field, BF16)

    def kept_far(array):
        return pltpu.with_memory_space_constraint(array, pltpu.HBM)

    plane_flops = 2 * count * 2 * MZ * GROUP

    def exchange(array):
        return lax.all_to_all(array, mesh_axes, split_axis=0, concat_axis=0, tiled=True)

    def mix_points(values, turned, shifts):
        step = 2
        block = pl.BlockSpec((channels, step, rows_y, rows_z), lambda x: (0, x, 0, 0))
        kernel = functools.partial(pointwise_kernel, turned)
        specs = [block, whole(pointwise)]
        operands = [values, pointwise]
        if shifts is None:
            run = lambda a, b, *rest: kernel(a, b, None, *rest)
        else:
            run = kernel
            specs.append(pl.BlockSpec(memory_space=pltpu.SMEM))
            operands.append(shifts)
        return pl.pallas_call(
            run,
            grid=(width // step,),
            in_specs=specs,
            out_specs=block,
            out_shape=far_field,
            scratch_shapes=[
                pltpu.VMEM((channels * TILE, channels * TILE), BF16),
                pltpu.VMEM((channels, 1, rows_z), F32),
            ],
            compiler_params=params(32),
            cost_estimate=cost(2 * count * channels * TILE, 4 * count),
        )(*operands)

    planes = pl.pallas_call(
        functools.partial(plane_kernel, per, channels, slabs),
        in_specs=[far, far, far],
        out_specs=whole(message),
        out_shape=message,
        scratch_shapes=[
            ztab,
            order,
            sums,
            buffer,
            pltpu.VMEM(base.shape, F32),
            pltpu.VMEM(ytab.shape, BF16),
            sems,
            pltpu.SemaphoreType.DMA((2,)),
        ],
        compiler_params=params(32),
        cost_estimate=cost(plane_flops, 2 * count),
    )(kept_far(activations), kept_far(base), kept_far(ytab))
    arrived = exchange(planes)
    local = mix_points(kept_far(activations.reshape(field)), True, offsets)
    arrived, local = lax.optimization_barrier((arrived, local))
    spec_in, mixed = pl.pallas_call(
        functools.partial(mix_kernel, per, samples),
        out_shape=(spectra, message),
        scratch_shapes=[pltpu.VMEM(spectra.shape, BF16)],
        compiler_params=params(16),
        cost_estimate=cost(10**8, 2 * mode_weights.size),
    )(arrived, mode_weights, line_fwd, inv_t)
    returned = exchange(mixed)
    slope, back_plane = pl.pallas_call(
        functools.partial(slope_kernel, per, channels, slabs),
        in_specs=[whole(message), far, far]
        + [whole(t) for t in (base, base_t, ytab, ytab_t, scale)],
        out_specs=(far, whole(message)),
        out_shape=(far_field, message),
        scratch_shapes=[ztab, ztab_t, order, held, sums]
        + [buffer] * 3
        + [pair_sums] * 2
        + [sems] * 3,
        compiler_params=params(40),
        cost_estimate=cost(2 * plane_flops, 6 * count, 2 * count),
    )(returned, kept_far(local), kept_far(cotangent), base, base_t, ytab, ytab_t, scale)
    arrived_back = exchange(back_plane)
    local_back = mix_points(kept_far(slope), False, None)
    arrived_back, local_back = lax.optimization_barrier((arrived_back, local_back))
    pairs, mixed_back = pl.pallas_call(
        functools.partial(mix_back_kernel, per, samples),
        out_shape=(shaped((spectra.shape[0], 2 * spectra.shape[1]), BF16), message),
        scratch_shapes=[pltpu.VMEM(spectra.shape, BF16)],
        compiler_params=params(16),
        cost_estimate=cost(10**8, 2 * mode_weights.size),
    )(arrived_back, mode_weights, line_inv, fwd_t)
    returned_back = exchange(mixed_back)
    grad_spectral = pl.pallas_call(
        functools.partial(weight_kernel, per, samples),
        out_shape=shaped(mode_weights.shape, F32),
        compiler_params=params(16),
        cost_estimate=cost(10**8, 4 * mode_weights.size),
    )(spec_in, pairs)
    grad_in = pl.pallas_call(
        functools.partial(field_kernel, per, channels, slabs),
        in_specs=[whole(message), far, whole(base_t), whole(ytab_t)],
        out_specs=far,
        out_shape=shaped(activations.shape, BF16),
        scratch_shapes=[ztab_t, order, held, buffer, buffer, sems, sems],
        compiler_params=params(32),
        cost_estimate=cost(plane_flops, 4 * count),
    )(returned_back, kept_far(local_back), base_t, ytab_t)
    return (grad_in, grad_spectral)


def chosen_body(mesh_axes, devices, slabs, activations, cotangent, mode_weights, pointwise, offsets):
    samples, channels, width, rows_y, rows_z = activations.shape
    per = MY * MZ // devices
    fits = (
        samples == 1
        and MY * MZ % devices == 0
        and per in (2, 4, 8)
        and width % 8 == 0
        and channels == 64
        and rows_y % TILE == 0
        and rows_z == 128
    )
    plan = functools.partial(body, mesh_axes, devices, slabs) if fits else general_body
    return plan(activations, cotangent, mode_weights, pointwise, offsets)


def solution(mesh):
    slabs = mesh.shape["space"]
    devices = slabs * mesh.shape["dp"]
    return jax.shard_map(
        functools.partial(chosen_body, ("dp", "space"), devices, slabs),
        mesh=mesh,
        in_specs=(
            P("dp", None, "space", None, None),
            P("dp", None, "space", None, None),
            P(("space", "dp"), None, None),
            P(),
            P(),
        ),
        out_specs=(P("dp", None, "space", None, None), P(("space", "dp"), None, None)),
        check_vma=False,
    )
```

```python
import functools
import math

import jax
import jax.numpy as jnp
import ml_dtypes
import numpy as np
from jax import lax
from jax.experimental import pallas as pl
from jax.experimental.pallas import tpu as pltpu
from jax.sharding import PartitionSpec as P

MX = 16
MY = 16
MZ = 8
NX = 32


def centered(count):
    index = jnp.arange(count, dtype=jnp.int32)
    return jnp.where(index < count // 2, index, index - count)


def plane_tables(rows_y, rows_z, modes_y, modes_z):
    along_y = jnp.arange(rows_y, dtype=jnp.int32)[:, None, None, None]
    along_z = jnp.arange(rows_z, dtype=jnp.int32)[None, :, None, None]
    freq_y = centered(modes_y)[None, None, :, None]
    freq_z = jnp.arange(modes_z, dtype=jnp.int32)[None, None, None, :]
    phase = jnp.mod(freq_y * along_y * rows_z + freq_z * along_z * rows_y, rows_y * rows_z)
    theta = phase.astype(jnp.float32) * (2.0 * math.pi / (rows_y * rows_z))
    cosine = jnp.cos(theta)
    sine = jnp.sin(theta)
    forward = jnp.stack([cosine, -sine], -1).reshape(rows_y * rows_z, modes_y * modes_z * 2)
    scaled = jnp.where(freq_z == 0, 1.0, 2.0).astype(jnp.float32) / (rows_y * rows_z)
    inverse = (
        jnp.stack([cosine * scaled, -sine * scaled], -1)
        .reshape(rows_y * rows_z, modes_y * modes_z * 2)
        .T
    )
    return (forward.astype(jnp.bfloat16), inverse.astype(jnp.bfloat16))


def line_tables(length, modes):
    along = jnp.arange(length, dtype=jnp.int32)[:, None]
    freq = centered(modes)[None, :]
    phase = jnp.mod(freq * along, length)
    theta = phase.astype(jnp.float32) * (2.0 * math.pi / length)
    cosine = jnp.cos(theta)
    sine = jnp.sin(theta)
    first = jnp.stack([cosine, -sine], -1)
    second = jnp.stack([sine, cosine], -1)
    forward = jnp.stack([first, second], 1).reshape(2 * length, 2 * modes)
    inv_first = jnp.stack([cosine.T, sine.T], -1) / length
    inv_second = jnp.stack([-sine.T, cosine.T], -1) / length
    inverse = jnp.stack([inv_first, inv_second], 1).reshape(2 * modes, 2 * length)
    return (forward.astype(jnp.bfloat16), inverse.astype(jnp.bfloat16))


def expand_weights(weights):
    half = weights.shape[1]
    real_part = weights[:, :, :half]
    imag_part = weights[:, :, half:]
    upper = jnp.concatenate([real_part, imag_part], axis=2)
    lower = jnp.concatenate([-imag_part, real_part], axis=2)
    return jnp.concatenate([upper, lower], axis=1)


def outer_sum(left, right):
    return jnp.einsum("mbi,mbo->mio", left, right, preferred_element_type=jnp.float32)


def weight_terms(spec_in, spec_grad):
    half = spec_in.shape[2] // 2
    in_real = spec_in[:, :, :half]
    in_imag = spec_in[:, :, half:]
    gr_real = spec_grad[:, :, :half]
    gr_imag = spec_grad[:, :, half:]
    real_term = outer_sum(in_real, gr_real) + outer_sum(in_imag, gr_imag)
    imag_term = outer_sum(in_real, gr_imag) - outer_sum(in_imag, gr_real)
    return jnp.concatenate([real_term, imag_term], axis=2)


def to_modes(slab, table, modes_x):
    samples, channels, width, pairs = slab.shape
    moved = lax.all_to_all(slab, "space", split_axis=3, concat_axis=2, tiled=True)
    length = moved.shape[2]
    local = moved.shape[3] // 2
    lines = moved.reshape(samples, channels, length, local, 2).transpose(0, 1, 3, 2, 4)
    lines = lines.reshape(samples, channels, local, 2 * length)
    spectra = jnp.dot(lines, table, preferred_element_type=jnp.float32).astype(jnp.bfloat16)
    spectra = spectra.reshape(samples, channels, local, modes_x, 2).transpose(2, 3, 0, 4, 1)
    return spectra.reshape(local * modes_x, samples, 2 * channels)


def to_slab(spectra, table, modes_x, channels):
    count, samples, doubled = spectra.shape
    local = count // modes_x
    lines = spectra.reshape(local, modes_x, samples, 2, channels).transpose(2, 4, 0, 1, 3)
    lines = lines.reshape(samples, channels, local, 2 * modes_x)
    lines = jnp.dot(lines, table, preferred_element_type=jnp.float32).astype(jnp.bfloat16)
    length = lines.shape[3] // 2
    lines = lines.reshape(samples, channels, local, length, 2).transpose(0, 1, 3, 2, 4)
    lines = lines.reshape(samples, channels, length, 2 * local)
    return lax.all_to_all(lines, "space", split_axis=2, concat_axis=3, tiled=True)


def to_owners(spectra):
    return lax.all_to_all(spectra, "dp", split_axis=0, concat_axis=1, tiled=True)


def from_owners(spectra):
    return lax.all_to_all(spectra, "dp", split_axis=1, concat_axis=0, tiled=True)


def gelu_slope(value):
    cdf = 0.5 * (1.0 + lax.erf(value * 0.7071067811865476))
    density = jnp.exp(-0.5 * value * value) * 0.3989422804014327
    return cdf + value * density


def general_body(activations, cotangent, mode_weights, pointwise, offsets):
    samples, channels, width, rows_y, rows_z = activations.shape
    plane_fwd, plane_inv = plane_tables(rows_y, rows_z, MY, MZ)
    line_fwd, line_inv = line_tables(NX, MX)
    flat = activations.reshape(samples, channels, width, rows_y * rows_z)
    planes = jnp.dot(flat, plane_fwd, preferred_element_type=jnp.float32).astype(jnp.bfloat16)
    spec_in = to_modes(planes, line_fwd, MX)
    blocks = expand_weights(mode_weights)
    held_in = to_owners(spec_in)
    held_out = jnp.einsum(
        "mbi,mio->mbo", held_in, blocks, preferred_element_type=jnp.float32
    ).astype(jnp.bfloat16)
    spec_out = from_owners(held_out)
    returned = to_slab(spec_out, line_inv, MX, channels)
    spectral = jnp.dot(returned, plane_inv, preferred_element_type=jnp.float32)
    local_part = jnp.einsum("io,bixn->boxn", pointwise, flat, preferred_element_type=jnp.float32)
    summed = spectral + local_part + offsets[None, :, None, None]
    upstream = cotangent.reshape(flat.shape).astype(jnp.float32)
    slope_grad = (upstream * gelu_slope(summed)).astype(jnp.bfloat16)
    back_plane = jnp.dot(slope_grad, plane_inv.T, preferred_element_type=jnp.float32).astype(
        jnp.bfloat16
    )
    spec_grad = to_modes(back_plane, line_inv.T, MX)
    held_grad = to_owners(spec_grad)
    held_dx = jnp.einsum(
        "mbo,mio->mbi", held_grad, blocks, preferred_element_type=jnp.float32
    ).astype(jnp.bfloat16)
    spec_dx = from_owners(held_dx)
    grad_spectral = weight_terms(held_in, held_grad)
    line_dx = to_slab(spec_dx, line_fwd.T, MX, channels)
    total = jnp.dot(line_dx, plane_fwd.T, preferred_element_type=jnp.float32)
    total = total + jnp.einsum(
        "io,boxn->bixn", pointwise, slope_grad, preferred_element_type=jnp.float32
    )
    grad_in = total.astype(jnp.bfloat16).reshape(activations.shape)
    return (grad_in, grad_spectral)


BF16 = jnp.bfloat16
F32 = jnp.float32
GROUP = 16
TILE = 8
SLOTS = 4
STEPS = GROUP // SLOTS
MIB = 1024 * 1024


def rounded(table):
    return np.asarray(table, np.float32).astype(ml_dtypes.bfloat16)


def angles(freq, points, length):
    phase = np.mod(np.outer(freq, points), length)
    return (phase * (2.0 * math.pi / length)).astype(np.float64)


def signed(count):
    index = np.arange(count)
    return np.where(index < count // 2, index, index - count)


def z_base(rows_z):
    theta = angles(np.arange(MZ), np.arange(rows_z), rows_z)
    pair = np.stack([np.cos(theta), -np.sin(theta)])
    table = np.repeat(pair.reshape(2 * MZ, rows_z), GROUP, axis=0).T
    return rounded(table).astype(np.float32)


def y_table(rows_y, width):
    theta = angles(signed(MY), np.arange(rows_y), rows_y)
    cosine, sine = np.cos(theta), np.sin(theta)
    turn = np.stack([np.stack([cosine, sine]), np.stack([-sine, cosine])])
    table = np.einsum("rsjy,xw->jxrswy", turn, np.eye(width))
    return rounded(table.reshape(MY * width * 2, 2 * width * rows_y))


def x_tables(samples, slabs, length):
    theta = angles(signed(MX), np.arange(length), length)
    cosine, sine = np.cos(theta), np.sin(theta)
    forward = np.stack([np.stack([cosine, sine]), np.stack([-sine, cosine])])
    inverse = np.stack([np.stack([cosine, sine]), np.stack([-sine, cosine])]) / length
    same = np.eye(samples)
    rows = MX * 2 * samples

    def lay(turn):
        turn = turn.reshape(2, 2, MX, slabs, length // slabs)
        table = np.einsum("arqsx,bd->qabdsxr", turn, same)
        return rounded(table.reshape(rows, samples * length * 2))

    return lay(forward), lay(inverse)


def dot(left, right):
    return jnp.dot(left, right, preferred_element_type=F32)


def doubled_slope(u):
    decay = jnp.exp2(u * u * -math.log2(math.e)).astype(BF16)
    cdf = (1.0 + lax.erf(u)).astype(BF16)
    return cdf + u.astype(BF16) * jnp.asarray(2.0 / math.sqrt(math.pi), BF16) * decay


def over(index, size):
    return lax.shift_right_logical(index, jnp.int32(size.bit_length() - 1))


def within(index, size):
    return jnp.bitwise_and(index, jnp.int32(size - 1))


def fill_z(base, table):
    rows_z, lanes = base.shape
    owner = within(lax.broadcasted_iota(jnp.int32, (rows_z, lanes), 1), GROUP)
    values = base[...]
    for c in range(GROUP):
        table[c * rows_z : (c + 1) * rows_z] = jnp.where(owner == c, values, 0.0).astype(BF16)


def fill_z_back(base, table):
    lanes, rows_z = base.shape
    owner = within(lax.broadcasted_iota(jnp.int32, (lanes, rows_z), 0), GROUP)
    values = base[...]
    for c in range(GROUP):
        first = c % SLOTS * rows_z
        table[c // SLOTS, :lanes, first : first + rows_z] = jnp.where(owner == c, values, 0.0).astype(BF16)
    pair = 2 * rows_z
    row = lax.broadcasted_iota(jnp.int32, (pair, pair), 0)
    column = lax.broadcasted_iota(jnp.int32, (pair, pair), 1)
    identity = jnp.where(row == column, 1.0, 0.0).astype(BF16)
    for step in range(STEPS):
        for first in range(0, SLOTS * rows_z, pair):
            table[step, lanes:, first : first + pair] = identity


def grouped(lane, per, channels):
    c = within(lane, channels)
    return over(c, GROUP) * (MZ * GROUP) + over(lane, channels) * GROUP + within(c, GROUP)


def fill_order(per, channels, back, table):
    count = table.shape[0]
    row = lax.broadcasted_iota(jnp.int32, (count, count), 0)
    column = lax.broadcasted_iota(jnp.int32, (count, count), 1)
    if back:
        same = grouped(row[:, :1], per, channels) == column
    else:
        same = row == grouped(column[:1], per, channels)
    table[...] = jnp.where(same, 1.0, 0.0).astype(BF16)


def turned_index(index, slabs, devices):
    samples = devices // slabs
    return index % samples * slabs + index // samples


def deliver(spectra, ytab, order, scale, message, per, channels, slabs):
    groups = channels // GROUP
    rows = spectra.shape[0] // groups
    wide = spectra.shape[1] // 2
    halves = []
    for r in range(2):
        blocks = [spectra[g * rows : (g + 1) * rows, r * wide : (r + 1) * wide] for g in range(groups)]
        halves.append(jnp.concatenate(blocks, axis=1).astype(BF16))
    planes = dot(ytab[...], jnp.concatenate(halves, axis=0))
    if scale is not None:
        planes = planes * scale[...]
    ordered = dot(planes.astype(BF16), order[...]).astype(BF16)
    parts = MZ // per
    count = message.shape[1]
    lanes = per * channels
    for part in range(parts):
        block = ordered[:, part * lanes : (part + 1) * lanes]
        for j in range(MY):
            message[turned_index(j * parts + part, slabs, message.shape[0])] = block[j * count : (j + 1) * count]


def receive(message, order_back, ytab_back, scale, held, per, slabs):
    parts = MZ // per
    lanes = [
        jnp.concatenate(
            [message[turned_index(j * parts + part, slabs, message.shape[0])] for j in range(MY)], axis=0
        )
        for part in range(parts)
    ]
    ordered = dot(jnp.concatenate(lanes, axis=1), order_back[...]).astype(BF16)
    lines = dot(ytab_back[...], ordered)
    if scale is not None:
        lines = lines * scale[...]
    lines = lines.astype(BF16)
    rows = lines.shape[0] // 2
    wide = MZ * GROUP
    for group in range(held.shape[0] // rows):
        piece = lines[:, group * wide : (group + 1) * wide]
        held[group * rows : (group + 1) * rows] = jnp.concatenate([piece[:rows], piece[rows:]], axis=1)


class Move:
    def __init__(self, source, target, sems):
        self.source, self.target, self.sems = source, target, sems
        self.groups = target.shape[0] // GROUP

    def copies(self, step):
        for g in range(self.groups):
            run = pl.ds(g * GROUP + step * SLOTS, SLOTS)
            sem = self.sems.at[step * self.groups + g]
            yield pltpu.make_async_copy(self.source.at[run], self.target.at[run], sem)

    def start(self, step):
        for copy in self.copies(step):
            copy.start()

    def wait(self, step):
        for copy in self.copies(step):
            copy.wait()


def start_all(moves, step):
    for each in moves:
        each.start(step)


def slot_lanes(field, first, count):
    groups = field.shape[0] // GROUP
    rows_z = field.shape[-1]
    lanes = [
        jnp.concatenate([field[g * GROUP + first + slot].reshape(-1, rows_z) for g in range(groups)], axis=0)
        for slot in range(count)
    ]
    return jnp.concatenate(lanes, axis=1)


def add_spectra(field, ztab, first, count, spectra):
    rows_z = field.shape[-1]
    table = ztab[pl.ds(pl.multiple_of(first * rows_z, count * rows_z), count * rows_z)]
    spectra[...] += dot(slot_lanes(field, first, count), table)


def synthesise(held, local, ztab_back, step, pair):
    wide = 2 * local.shape[-1]
    terms = jnp.concatenate([held[...], slot_lanes(local, step * SLOTS + 2 * pair, 2)], axis=1)
    return dot(terms, ztab_back[step, :, pair * wide : (pair + 1) * wide])


def plane_kernel(
    per, channels, slabs, field, base_far, ytab_far, message, ztab, order, spectra, buffer, base, ytab, sems, table_sems
):
    incoming = Move(field.at[0], buffer, sems)
    base_copy = pltpu.make_async_copy(base_far, base, table_sems.at[0])
    ytab_copy = pltpu.make_async_copy(ytab_far, ytab, table_sems.at[1])
    base_copy.start()
    incoming.start(0)
    fill_order(per, channels, False, order)
    spectra[...] = jnp.zeros_like(spectra)
    incoming.start(1)
    base_copy.wait()
    fill_z(base, ztab)
    incoming.start(2)
    ytab_copy.start()
    incoming.start(3)

    @pl.loop(0, STEPS)
    def _(step):
        incoming.wait(step)
        add_spectra(buffer, ztab, step * SLOTS, SLOTS, spectra)

    ytab_copy.wait()
    deliver(spectra, ytab, order, None, message, per, channels, slabs)


def slope_kernel(
    per, channels, slabs, arrived, local, cotangent, base, base_back, ytab, ytab_back, scale, scale_back,
    slope, message, ztab, ztab_back, order, held, spectra, local_in, cotangent_in, result, first_sum, second_sum,
    local_sems, cotangent_sems, result_sems,
):
    width, rows_y, rows_z = local.shape[1:]
    groups = channels // GROUP
    rows = width * rows_y
    wide = 2 * rows_y
    incoming = (Move(local, local_in, local_sems), Move(cotangent.at[0], cotangent_in, cotangent_sems))
    outgoing = Move(result, slope, result_sems)
    start_all(incoming, 0)
    fill_order(per, channels, True, order)
    receive(arrived, order, ytab_back, scale_back, held, per, slabs)
    start_all(incoming, 1)
    fill_z_back(base_back, ztab_back)
    fill_z(base, ztab)
    start_all(incoming, 2)
    fill_order(per, channels, False, order)
    spectra[...] = jnp.zeros_like(spectra)
    start_all(incoming, 3)

    @pl.loop(0, STEPS)
    def _(step):
        for each in incoming:
            each.wait(step)
        for pair, total in enumerate((first_sum, second_sum)):
            total[...] = synthesise(held, local_in, ztab_back, step, pair)
        for pair, total in enumerate((first_sum, second_sum)):
            for g in range(groups):
                for offset in range(2):
                    c = g * GROUP + step * SLOTS + 2 * pair + offset
                    for x in range(0, width, 2):
                        place = g * rows + x * rows_y
                        value = total[place : place + wide, offset * rows_z : (offset + 1) * rows_z]
                        upstream = cotangent_in[c, x : x + 2].reshape(wide, rows_z)
                        answer = upstream * doubled_slope(value)
                        result[c, x : x + 2] = answer.reshape(2, rows_y, rows_z)
            add_spectra(result, ztab, step * SLOTS + 2 * pair, 2, spectra)
        outgoing.start(step)

    deliver(spectra, ytab, order, scale, message, per, channels, slabs)
    for step in range(STEPS):
        outgoing.wait(step)


def field_kernel(
    per, channels, slabs, arrived, local, base_back, ytab_back, out, ztab_back, order, held, local_in, result,
    local_sems, result_sems,
):
    width, rows_y, rows_z = local.shape[1:]
    groups = channels // GROUP
    rows = width * rows_y
    incoming = Move(local, local_in, local_sems)
    outgoing = Move(result, out.at[0], result_sems)
    incoming.start(0)
    fill_order(per, channels, True, order)
    incoming.start(1)
    receive(arrived, order, ytab_back, None, held, per, slabs)
    incoming.start(2)
    fill_z_back(base_back, ztab_back)
    incoming.start(3)

    @pl.loop(0, STEPS)
    def _(step):
        incoming.wait(step)
        for pair in range(SLOTS // 2):
            total = synthesise(held, local_in, ztab_back, step, pair)
            for g in range(groups):
                for offset in range(2):
                    c = g * GROUP + step * SLOTS + 2 * pair + offset
                    value = total[g * rows : (g + 1) * rows, offset * rows_z : (offset + 1) * rows_z]
                    result[c] = value.astype(BF16).reshape(width, rows_y, rows_z)
        outgoing.start(step)

    for step in range(STEPS):
        outgoing.wait(step)


def pointwise_kernel(turned, field, mix, offsets, out, table, shift):
    channels = mix.shape[0]
    width, rows_y, rows_z = field.shape[1:]
    size = channels * TILE

    @pl.when(pl.program_id(0) == 0)
    def _():
        row = over(lax.broadcasted_iota(jnp.int32, (size, channels), 0), TILE)
        column = lax.broadcasted_iota(jnp.int32, (size, channels), 1)
        spread = jnp.where(row == column, 1.0, 0.0).astype(BF16)
        tall = lax.dot_general(
            spread, mix[...], (((1,), (1 if turned else 0,)), ((), ())), preferred_element_type=F32
        ).astype(BF16)
        whole = lax.dot_general(
            tall, spread, (((1,), (1,)), ((), ())), preferred_element_type=F32
        )
        place = within(lax.broadcasted_iota(jnp.int32, (size, size), 0), TILE)
        other = within(lax.broadcasted_iota(jnp.int32, (size, size), 1), TILE)
        table[...] = jnp.where(place == other, whole if turned else 0.5 * whole, 0.0).astype(BF16)
        if offsets is not None:
            for c in range(channels):
                shift[c] = jnp.full((1, rows_z), offsets[c], F32)

    for start in range(0, rows_y, 2 * TILE):
        pieces = [field[:, x, start : start + 2 * TILE, :].astype(F32) for x in range(width)]
        halves = []
        for row in range(0, 2 * TILE, TILE):
            rows = [piece[:, row : row + TILE].reshape(size, rows_z).astype(BF16) for piece in pieces]
            halves.append(dot(table[...], jnp.concatenate(rows, axis=1)))
        for x in range(width):
            values = [
                half[:, x * rows_z : (x + 1) * rows_z].reshape(channels, TILE, rows_z) for half in halves
            ]
            value = jnp.concatenate(values, axis=1)
            if offsets is not None:
                value = (value + shift[...]) * math.sqrt(0.5)
            out[:, x, start : start + 2 * TILE, :] = value.astype(BF16)


def spread_pair(first, second):
    nothing = jnp.zeros_like(first)
    upper = jnp.concatenate([first, nothing], axis=1)
    lower = jnp.concatenate([nothing, second], axis=1)
    return jnp.concatenate([upper, lower], axis=0)


def low_half(shape):
    return lax.broadcasted_iota(jnp.int32, shape, 1) < shape[1] // 2


def mix_kernel(per, samples, arrived, weights, line, line_back, spec_in, message, held):
    rows = 2 * samples
    lanes = 2 * weights.shape[1]
    low = low_half((samples, lanes))
    flat = arrived[...].reshape(-1, arrived.shape[2])
    spectra = dot(line[...], flat).astype(BF16)
    spec_in[...] = spectra
    for q in range(MX):
        for first in range(0, per, 2):
            block = spread_pair(weights[first * MX + q], weights[(first + 1) * MX + q])
            place = first // 2 * lanes
            terms = dot(spectra[q * rows : (q + 1) * rows, place : place + lanes], block)
            mixed = []
            for side in range(2):
                part = terms[:, side * lanes : (side + 1) * lanes]
                turned = pltpu.roll(part[samples:], lanes // 2, 1)
                mixed.append(part[:samples] + jnp.where(low, -turned, turned))
            real = jnp.where(low, mixed[0], pltpu.roll(mixed[1], lanes // 2, 1))
            imag = jnp.where(low, pltpu.roll(mixed[0], lanes // 2, 1), mixed[1])
            held[q * rows : (q + 1) * rows, place : place + lanes] = jnp.concatenate(
                [real, imag], axis=0
            ).astype(BF16)
    message[...] = dot(line_back[...], held[...]).astype(BF16).reshape(message.shape)


def mix_back_kernel(per, samples, arrived, weights, line, line_back, pairs, message, held):
    rows = 2 * samples
    lanes = 2 * weights.shape[1]
    low = low_half((samples, lanes))
    flat = arrived[...].reshape(-1, arrived.shape[2])
    spectra = dot(line[...], flat).astype(BF16).astype(F32)
    for q in range(MX):
        for first in range(0, per, 2):
            block = spread_pair(weights[first * MX + q], weights[(first + 1) * MX + q])
            place = first // 2 * lanes
            real = spectra[q * rows : q * rows + samples, place : place + lanes]
            imag = spectra[q * rows + samples : (q + 1) * rows, place : place + lanes]
            real_turned = pltpu.roll(real, lanes // 2, 1)
            imag_turned = pltpu.roll(imag, lanes // 2, 1)
            left = [jnp.where(low, real, imag_turned), jnp.where(low, imag, -real_turned)]
            right = [jnp.where(low, real_turned, imag), jnp.where(low, imag_turned, -real)]
            pair = jnp.concatenate(
                [jnp.concatenate(left, axis=0), jnp.concatenate(right, axis=0)], axis=1
            ).astype(BF16)
            pairs[q * rows : (q + 1) * rows, 2 * place : 2 * (place + lanes)] = pair
            held[q * rows : (q + 1) * rows, place : place + lanes] = lax.dot_general(
                pair, block, (((1,), (1,)), ((), ())), preferred_element_type=F32
            ).astype(BF16)
    message[...] = dot(line_back[...], held[...]).astype(BF16).reshape(message.shape)


def weight_kernel(per, samples, spec_in, pairs, out):
    rows = 2 * samples
    lanes = out.shape[2]
    half = lanes // 2
    for q in range(MX):
        for first in range(0, per, 2):
            place = first // 2 * lanes
            left = spec_in[q * rows : (q + 1) * rows, place : place + lanes]
            right = pairs[q * rows : (q + 1) * rows, 2 * place : 2 * (place + lanes)]
            outer = lax.dot_general(
                left, right, (((0,), (0,)), ((), ())), preferred_element_type=F32
            )
            out[first * MX + q] = outer[:half, :lanes]
            out[(first + 1) * MX + q] = outer[half:, lanes:]


def whole(array):
    return pl.BlockSpec(array.shape, lambda *step: (0,) * len(array.shape))


def shaped(shape, dtype):
    return jax.ShapeDtypeStruct(shape, dtype)


def params(mib):
    return pltpu.CompilerParams(vmem_limit_bytes=mib * MIB)


def cost(flops, moved, steep=0):
    return pl.CostEstimate(flops=flops, bytes_accessed=moved, transcendentals=steep)


def body(mesh_axes, devices, slabs, activations, cotangent, mode_weights, pointwise, offsets):
    _, channels, width, rows_y, rows_z = activations.shape
    samples = devices // slabs
    per = MY * MZ // devices
    groups = channels // GROUP
    field = activations.shape[1:]
    count = math.prod(field)
    base = z_base(rows_z)
    ytab = y_table(rows_y, width)
    line_fwd, line_inv = x_tables(samples, slabs, NX)
    weight = np.where(np.arange(MZ) == 0, 1.0, 2.0) / (rows_y * rows_z)
    scale = np.tile(np.repeat(weight, GROUP), groups)[None]
    scale, scale_t = (0.5 * scale).astype(np.float32), (math.sqrt(0.5) * scale).astype(np.float32)
    base_t, ytab_t = (np.ascontiguousarray(t.T) for t in (base, ytab))
    fwd_t, inv_t = (np.ascontiguousarray(t.T) for t in (line_fwd, line_inv))
    message = shaped((devices, 2 * width, per * channels), BF16)
    spectra = shaped((MX * 2 * samples, per * channels), BF16)
    ztab = pltpu.VMEM((GROUP * rows_z, 2 * MZ * GROUP), BF16)
    ztab_t = pltpu.VMEM((STEPS, 2 * MZ * GROUP + 2 * rows_z, SLOTS * rows_z), BF16)
    order = pltpu.VMEM((MZ * channels, MZ * channels), BF16)
    rows = groups * width * rows_y
    held = pltpu.VMEM((rows, 2 * MZ * GROUP), BF16)
    sums = pltpu.VMEM((rows, 2 * MZ * GROUP), F32)
    pair_sums = pltpu.VMEM((rows, 2 * rows_z), F32)
    buffer = pltpu.VMEM(field, BF16)
    sems = pltpu.SemaphoreType.DMA((STEPS * groups,))
    far = pl.BlockSpec(memory_space=pltpu.HBM)
    far_field = pltpu.HBM(field, BF16)

    def kept_far(array):
        return pltpu.with_memory_space_constraint(array, pltpu.HBM)

    plane_flops = 2 * count * 2 * MZ * GROUP

    def exchange(array):
        return lax.all_to_all(array, mesh_axes, split_axis=0, concat_axis=0, tiled=True)

    def mix_points(values, turned, shifts):
        step = 2
        block = pl.BlockSpec((channels, step, rows_y, rows_z), lambda x: (0, x, 0, 0))
        kernel = functools.partial(pointwise_kernel, turned)
        specs = [block, whole(pointwise)]
        operands = [values, pointwise]
        if shifts is None:
            run = lambda a, b, *rest: kernel(a, b, None, *rest)
        else:
            run = kernel
            specs.append(pl.BlockSpec(memory_space=pltpu.SMEM))
            operands.append(shifts)
        return pl.pallas_call(
            run,
            grid=(width // step,),
            in_specs=specs,
            out_specs=block,
            out_shape=far_field,
            scratch_shapes=[
                pltpu.VMEM((channels * TILE, channels * TILE), BF16),
                pltpu.VMEM((channels, 1, rows_z), F32),
            ],
            compiler_params=params(32),
            cost_estimate=cost(2 * count * channels * TILE, 4 * count),
        )(*operands)

    planes = pl.pallas_call(
        functools.partial(plane_kernel, per, channels, slabs),
        in_specs=[far, far, far],
        out_specs=whole(message),
        out_shape=message,
        scratch_shapes=[
            ztab,
            order,
            sums,
            buffer,
            pltpu.VMEM(base.shape, F32),
            pltpu.VMEM(ytab.shape, BF16),
            sems,
            pltpu.SemaphoreType.DMA((2,)),
        ],
        compiler_params=params(32),
        cost_estimate=cost(plane_flops, 2 * count),
    )(kept_far(activations), kept_far(base), kept_far(ytab))
    arrived = exchange(planes)
    local = mix_points(kept_far(activations.reshape(field)), True, offsets)
    arrived, local = lax.optimization_barrier((arrived, local))
    spec_in, mixed = pl.pallas_call(
        functools.partial(mix_kernel, per, samples),
        out_shape=(spectra, message),
        scratch_shapes=[pltpu.VMEM(spectra.shape, BF16)],
        compiler_params=params(16),
        cost_estimate=cost(10**8, 2 * mode_weights.size),
    )(arrived, mode_weights, line_fwd, inv_t)
    returned = exchange(mixed)
    slope, back_plane = pl.pallas_call(
        functools.partial(slope_kernel, per, channels, slabs),
        in_specs=[whole(message), far, far]
        + [whole(t) for t in (base, base_t, ytab, ytab_t, scale, scale_t)],
        out_specs=(far, whole(message)),
        out_shape=(far_field, message),
        scratch_shapes=[ztab, ztab_t, order, held, sums]
        + [buffer] * 3
        + [pair_sums] * 2
        + [sems] * 3,
        compiler_params=params(40),
        cost_estimate=cost(2 * plane_flops, 6 * count, 2 * count),
    )(returned, kept_far(local), kept_far(cotangent), base, base_t, ytab, ytab_t, scale, scale_t)
    arrived_back = exchange(back_plane)
    local_back = mix_points(kept_far(slope), False, None)
    arrived_back, local_back = lax.optimization_barrier((arrived_back, local_back))
    pairs, mixed_back = pl.pallas_call(
        functools.partial(mix_back_kernel, per, samples),
        out_shape=(shaped((spectra.shape[0], 2 * spectra.shape[1]), BF16), message),
        scratch_shapes=[pltpu.VMEM(spectra.shape, BF16)],
        compiler_params=params(16),
        cost_estimate=cost(10**8, 2 * mode_weights.size),
    )(arrived_back, mode_weights, line_inv, fwd_t)
    returned_back = exchange(mixed_back)
    grad_spectral = pl.pallas_call(
        functools.partial(weight_kernel, per, samples),
        out_shape=shaped(mode_weights.shape, F32),
        compiler_params=params(16),
        cost_estimate=cost(10**8, 4 * mode_weights.size),
    )(spec_in, pairs)
    grad_in = pl.pallas_call(
        functools.partial(field_kernel, per, channels, slabs),
        in_specs=[whole(message), far, whole(base_t), whole(ytab_t)],
        out_specs=far,
        out_shape=shaped(activations.shape, BF16),
        scratch_shapes=[ztab_t, order, held, buffer, buffer, sems, sems],
        compiler_params=params(32),
        cost_estimate=cost(plane_flops, 4 * count),
    )(returned_back, kept_far(local_back), base_t, ytab_t)
    return (grad_in, grad_spectral)


def chosen_body(mesh_axes, devices, slabs, activations, cotangent, mode_weights, pointwise, offsets):
    samples, channels, width, rows_y, rows_z = activations.shape
    per = MY * MZ // devices
    fits = (
        samples == 1
        and MY * MZ % devices == 0
        and per in (2, 4, 8)
        and width % 8 == 0
        and channels == 64
        and rows_y % TILE == 0
        and rows_z == 128
    )
    plan = functools.partial(body, mesh_axes, devices, slabs) if fits else general_body
    return plan(activations, cotangent, mode_weights, pointwise, offsets)


def solution(mesh):
    slabs = mesh.shape["space"]
    devices = slabs * mesh.shape["dp"]
    return jax.shard_map(
        functools.partial(chosen_body, ("dp", "space"), devices, slabs),
        mesh=mesh,
        in_specs=(
            P("dp", None, "space", None, None),
            P("dp", None, "space", None, None),
            P(("space", "dp"), None, None),
            P(),
            P(),
        ),
        out_specs=(P("dp", None, "space", None, None), P(("space", "dp"), None, None)),
        check_vma=False,
    )
```

```python
import functools
import math

import jax
import jax.numpy as jnp
import ml_dtypes
import numpy as np
from jax import lax
from jax.experimental import pallas as pl
from jax.experimental.pallas import tpu as pltpu
from jax.sharding import PartitionSpec as P

MX = 16
MY = 16
MZ = 8
NX = 32


def centered(count):
    index = jnp.arange(count, dtype=jnp.int32)
    return jnp.where(index < count // 2, index, index - count)


def plane_tables(rows_y, rows_z, modes_y, modes_z):
    along_y = jnp.arange(rows_y, dtype=jnp.int32)[:, None, None, None]
    along_z = jnp.arange(rows_z, dtype=jnp.int32)[None, :, None, None]
    freq_y = centered(modes_y)[None, None, :, None]
    freq_z = jnp.arange(modes_z, dtype=jnp.int32)[None, None, None, :]
    phase = jnp.mod(freq_y * along_y * rows_z + freq_z * along_z * rows_y, rows_y * rows_z)
    theta = phase.astype(jnp.float32) * (2.0 * math.pi / (rows_y * rows_z))
    cosine = jnp.cos(theta)
    sine = jnp.sin(theta)
    forward = jnp.stack([cosine, -sine], -1).reshape(rows_y * rows_z, modes_y * modes_z * 2)
    scaled = jnp.where(freq_z == 0, 1.0, 2.0).astype(jnp.float32) / (rows_y * rows_z)
    inverse = (
        jnp.stack([cosine * scaled, -sine * scaled], -1)
        .reshape(rows_y * rows_z, modes_y * modes_z * 2)
        .T
    )
    return (forward.astype(jnp.bfloat16), inverse.astype(jnp.bfloat16))


def line_tables(length, modes):
    along = jnp.arange(length, dtype=jnp.int32)[:, None]
    freq = centered(modes)[None, :]
    phase = jnp.mod(freq * along, length)
    theta = phase.astype(jnp.float32) * (2.0 * math.pi / length)
    cosine = jnp.cos(theta)
    sine = jnp.sin(theta)
    first = jnp.stack([cosine, -sine], -1)
    second = jnp.stack([sine, cosine], -1)
    forward = jnp.stack([first, second], 1).reshape(2 * length, 2 * modes)
    inv_first = jnp.stack([cosine.T, sine.T], -1) / length
    inv_second = jnp.stack([-sine.T, cosine.T], -1) / length
    inverse = jnp.stack([inv_first, inv_second], 1).reshape(2 * modes, 2 * length)
    return (forward.astype(jnp.bfloat16), inverse.astype(jnp.bfloat16))


def expand_weights(weights):
    half = weights.shape[1]
    real_part = weights[:, :, :half]
    imag_part = weights[:, :, half:]
    upper = jnp.concatenate([real_part, imag_part], axis=2)
    lower = jnp.concatenate([-imag_part, real_part], axis=2)
    return jnp.concatenate([upper, lower], axis=1)


def outer_sum(left, right):
    return jnp.einsum("mbi,mbo->mio", left, right, preferred_element_type=jnp.float32)


def weight_terms(spec_in, spec_grad):
    half = spec_in.shape[2] // 2
    in_real = spec_in[:, :, :half]
    in_imag = spec_in[:, :, half:]
    gr_real = spec_grad[:, :, :half]
    gr_imag = spec_grad[:, :, half:]
    real_term = outer_sum(in_real, gr_real) + outer_sum(in_imag, gr_imag)
    imag_term = outer_sum(in_real, gr_imag) - outer_sum(in_imag, gr_real)
    return jnp.concatenate([real_term, imag_term], axis=2)


def to_modes(slab, table, modes_x):
    samples, channels, width, pairs = slab.shape
    moved = lax.all_to_all(slab, "space", split_axis=3, concat_axis=2, tiled=True)
    length = moved.shape[2]
    local = moved.shape[3] // 2
    lines = moved.reshape(samples, channels, length, local, 2).transpose(0, 1, 3, 2, 4)
    lines = lines.reshape(samples, channels, local, 2 * length)
    spectra = jnp.dot(lines, table, preferred_element_type=jnp.float32).astype(jnp.bfloat16)
    spectra = spectra.reshape(samples, channels, local, modes_x, 2).transpose(2, 3, 0, 4, 1)
    return spectra.reshape(local * modes_x, samples, 2 * channels)


def to_slab(spectra, table, modes_x, channels):
    count, samples, doubled = spectra.shape
    local = count // modes_x
    lines = spectra.reshape(local, modes_x, samples, 2, channels).transpose(2, 4, 0, 1, 3)
    lines = lines.reshape(samples, channels, local, 2 * modes_x)
    lines = jnp.dot(lines, table, preferred_element_type=jnp.float32).astype(jnp.bfloat16)
    length = lines.shape[3] // 2
    lines = lines.reshape(samples, channels, local, length, 2).transpose(0, 1, 3, 2, 4)
    lines = lines.reshape(samples, channels, length, 2 * local)
    return lax.all_to_all(lines, "space", split_axis=2, concat_axis=3, tiled=True)


def to_owners(spectra):
    return lax.all_to_all(spectra, "dp", split_axis=0, concat_axis=1, tiled=True)


def from_owners(spectra):
    return lax.all_to_all(spectra, "dp", split_axis=1, concat_axis=0, tiled=True)


def gelu_slope(value):
    cdf = 0.5 * (1.0 + lax.erf(value * 0.7071067811865476))
    density = jnp.exp(-0.5 * value * value) * 0.3989422804014327
    return cdf + value * density


def general_body(activations, cotangent, mode_weights, pointwise, offsets):
    samples, channels, width, rows_y, rows_z = activations.shape
    plane_fwd, plane_inv = plane_tables(rows_y, rows_z, MY, MZ)
    line_fwd, line_inv = line_tables(NX, MX)
    flat = activations.reshape(samples, channels, width, rows_y * rows_z)
    planes = jnp.dot(flat, plane_fwd, preferred_element_type=jnp.float32).astype(jnp.bfloat16)
    spec_in = to_modes(planes, line_fwd, MX)
    blocks = expand_weights(mode_weights)
    held_in = to_owners(spec_in)
    held_out = jnp.einsum(
        "mbi,mio->mbo", held_in, blocks, preferred_element_type=jnp.float32
    ).astype(jnp.bfloat16)
    spec_out = from_owners(held_out)
    returned = to_slab(spec_out, line_inv, MX, channels)
    spectral = jnp.dot(returned, plane_inv, preferred_element_type=jnp.float32)
    local_part = jnp.einsum("io,bixn->boxn", pointwise, flat, preferred_element_type=jnp.float32)
    summed = spectral + local_part + offsets[None, :, None, None]
    upstream = cotangent.reshape(flat.shape).astype(jnp.float32)
    slope_grad = (upstream * gelu_slope(summed)).astype(jnp.bfloat16)
    back_plane = jnp.dot(slope_grad, plane_inv.T, preferred_element_type=jnp.float32).astype(
        jnp.bfloat16
    )
    spec_grad = to_modes(back_plane, line_inv.T, MX)
    held_grad = to_owners(spec_grad)
    held_dx = jnp.einsum(
        "mbo,mio->mbi", held_grad, blocks, preferred_element_type=jnp.float32
    ).astype(jnp.bfloat16)
    spec_dx = from_owners(held_dx)
    grad_spectral = weight_terms(held_in, held_grad)
    line_dx = to_slab(spec_dx, line_fwd.T, MX, channels)
    total = jnp.dot(line_dx, plane_fwd.T, preferred_element_type=jnp.float32)
    total = total + jnp.einsum(
        "io,boxn->bixn", pointwise, slope_grad, preferred_element_type=jnp.float32
    )
    grad_in = total.astype(jnp.bfloat16).reshape(activations.shape)
    return (grad_in, grad_spectral)


BF16 = jnp.bfloat16
F32 = jnp.float32
GROUP = 16
TILE = 8
SLOTS = 4
STEPS = GROUP // SLOTS
MIB = 1024 * 1024


def rounded(table):
    return np.asarray(table, np.float32).astype(ml_dtypes.bfloat16)


def angles(freq, points, length):
    phase = np.mod(np.outer(freq, points), length)
    return (phase * (2.0 * math.pi / length)).astype(np.float64)


def signed(count):
    index = np.arange(count)
    return np.where(index < count // 2, index, index - count)


def z_table(rows_z):
    theta = angles(np.arange(MZ), np.arange(rows_z), rows_z)
    pair = np.stack([np.cos(theta), -np.sin(theta)])
    table = np.einsum("rkz,cd->czrkd", pair, np.eye(GROUP))
    return rounded(table.reshape(GROUP * rows_z, 2 * MZ * GROUP))


def y_table(rows_y, width):
    theta = angles(signed(MY), np.arange(rows_y), rows_y)
    cosine, sine = np.cos(theta), np.sin(theta)
    turn = np.stack([np.stack([cosine, sine]), np.stack([-sine, cosine])])
    table = np.einsum("rsjy,xw->jxrswy", turn, np.eye(width))
    return rounded(table.reshape(MY * width * 2, 2 * width * rows_y))


def x_tables(samples, slabs, length):
    theta = angles(signed(MX), np.arange(length), length)
    cosine, sine = np.cos(theta), np.sin(theta)
    forward = np.stack([np.stack([cosine, sine]), np.stack([-sine, cosine])])
    inverse = np.stack([np.stack([cosine, sine]), np.stack([-sine, cosine])]) / length
    same = np.eye(samples)
    rows = MX * 2 * samples

    def lay(turn):
        turn = turn.reshape(2, 2, MX, slabs, length // slabs)
        table = np.einsum("arqsx,bd->qabdsxr", turn, same)
        return rounded(table.reshape(rows, samples * length * 2))

    return lay(forward), lay(inverse)


def dot(left, right):
    return jnp.dot(left, right, preferred_element_type=F32)


def doubled_slope(u):
    decay = jnp.exp2(u * u * -math.log2(math.e)).astype(BF16)
    cdf = (1.0 + lax.erf(u)).astype(BF16)
    return cdf + u.astype(BF16) * jnp.asarray(2.0 / math.sqrt(math.pi), BF16) * decay


def over(index, size):
    return lax.shift_right_logical(index, jnp.int32(size.bit_length() - 1))


def within(index, size):
    return jnp.bitwise_and(index, jnp.int32(size - 1))


def grouped(lane, per, channels):
    c = within(lane, channels)
    return over(c, GROUP) * (MZ * GROUP) + over(lane, channels) * GROUP + within(c, GROUP)


def fill_order(per, channels, back, table):
    count = table.shape[0]
    row = lax.broadcasted_iota(jnp.int32, (count, count), 0)
    column = lax.broadcasted_iota(jnp.int32, (count, count), 1)
    if back:
        same = grouped(row[:, :1], per, channels) == column
    else:
        same = row == grouped(column[:1], per, channels)
    table[...] = jnp.where(same, 1.0, 0.0).astype(BF16)


def turned_index(index, slabs, devices):
    samples = devices // slabs
    return index % samples * slabs + index // samples


def deliver(spectra, ytab, order, scale, message, per, channels, slabs):
    groups = channels // GROUP
    rows = spectra.shape[0] // groups
    wide = spectra.shape[1] // 2
    halves = []
    for r in range(2):
        blocks = [spectra[g * rows : (g + 1) * rows, r * wide : (r + 1) * wide] for g in range(groups)]
        halves.append(jnp.concatenate(blocks, axis=1).astype(BF16))
    planes = dot(ytab[...], jnp.concatenate(halves, axis=0))
    if scale is not None:
        planes = planes * scale[...]
    ordered = dot(planes.astype(BF16), order[...]).astype(BF16)
    parts = MZ // per
    count = message.shape[1]
    lanes = per * channels
    for part in range(parts):
        block = ordered[:, part * lanes : (part + 1) * lanes]
        for j in range(MY):
            message[turned_index(j * parts + part, slabs, message.shape[0])] = block[j * count : (j + 1) * count]


def receive(message, order_back, ytab_back, scale, held, per, slabs):
    parts = MZ // per
    lanes = [
        jnp.concatenate(
            [message[turned_index(j * parts + part, slabs, message.shape[0])] for j in range(MY)], axis=0
        )
        for part in range(parts)
    ]
    ordered = dot(jnp.concatenate(lanes, axis=1), order_back[...]).astype(BF16)
    lines = dot(ytab_back[...], ordered)
    if scale is not None:
        lines = lines * scale[...]
    lines = lines.astype(BF16)
    rows = lines.shape[0] // 2
    wide = MZ * GROUP
    for group in range(held.shape[0] // rows):
        piece = lines[:, group * wide : (group + 1) * wide]
        held[group * rows : (group + 1) * rows] = jnp.concatenate([piece[:rows], piece[rows:]], axis=1)


class Move:
    def __init__(self, source, target, sems):
        self.source, self.target, self.sems = source, target, sems
        self.groups = target.shape[0] // GROUP

    def copies(self, step):
        for g in range(self.groups):
            run = pl.ds(g * GROUP + step * SLOTS, SLOTS)
            sem = self.sems.at[step * self.groups + g]
            yield pltpu.make_async_copy(self.source.at[run], self.target.at[run], sem)

    def start(self, step):
        for copy in self.copies(step):
            copy.start()

    def wait(self, step):
        for copy in self.copies(step):
            copy.wait()


def start_all(moves, step):
    for each in moves:
        each.start(step)


def slot_lanes(field, first, groups):
    rows_z = field.shape[-1]
    lanes = [
        jnp.concatenate([field[g * GROUP + first + slot].reshape(-1, rows_z) for g in groups], axis=0)
        for slot in range(2)
    ]
    return jnp.concatenate(lanes, axis=1)


def units(groups):
    half = groups // 2
    return [(pair, range(first, first + half)) for pair in range(SLOTS // 2) for first in (0, half)]


def block_of(rows, groups):
    return slice(rows * groups[0], rows * (groups[-1] + 1))


def plane_kernel(
    per, channels, slabs, field, ztab_far, ytab_far, message, ztab, order, spectra, buffer, ytab, sems, table_sems
):
    groups = range(channels // GROUP)
    rows_z = field.shape[-1]
    incoming = Move(field.at[0], buffer, sems)
    ztab_copy = pltpu.make_async_copy(ztab_far, ztab, table_sems.at[0])
    ytab_copy = pltpu.make_async_copy(ytab_far, ytab, table_sems.at[1])
    incoming.start(0)
    ztab_copy.start()
    fill_order(per, channels, False, order)
    incoming.start(1)
    spectra[...] = jnp.zeros_like(spectra)
    incoming.start(2)
    ytab_copy.start()
    incoming.start(3)
    ztab_copy.wait()

    @pl.loop(0, STEPS)
    def _(step):
        incoming.wait(step)
        depth = SLOTS * rows_z
        first = step * SLOTS
        lanes = jnp.concatenate([slot_lanes(buffer, first + pair, groups) for pair in range(0, SLOTS, 2)], axis=1)
        spectra[...] += dot(lanes, ztab[pl.ds(pl.multiple_of(step * depth, depth), depth)])

    ytab_copy.wait()
    deliver(spectra, ytab, order, None, message, per, channels, slabs)


def slope_kernel(
    per, channels, slabs, arrived, local, cotangent, ztab_far, ztab_back_far, ytab, ytab_back, scale, scale_back,
    slope, message, ztab, ztab_back, order, held, spectra, local_in, cotangent_in, result, first_sum, second_sum,
    local_sems, cotangent_sems, result_sems, table_sems,
):
    width, rows_y, rows_z = local.shape[1:]
    rows = width * rows_y
    wide = 2 * rows_y
    pair_lanes = 2 * rows_z
    incoming = (Move(local, local_in, local_sems), Move(cotangent.at[0], cotangent_in, cotangent_sems))
    outgoing = Move(result, slope, result_sems)
    tables = (
        pltpu.make_async_copy(ztab_back_far, ztab_back, table_sems.at[0]),
        pltpu.make_async_copy(ztab_far, ztab, table_sems.at[1]),
    )
    tables[0].start()
    start_all(incoming, 0)
    fill_order(per, channels, True, order)
    tables[1].start()
    start_all(incoming, 1)
    receive(arrived, order, ytab_back, scale_back, held, per, slabs)
    start_all(incoming, 2)
    fill_order(per, channels, False, order)
    spectra[...] = jnp.zeros_like(spectra)
    start_all(incoming, 3)
    for table in tables:
        table.wait()
    work = units(channels // GROUP)
    totals = (first_sum, second_sum)

    @pl.loop(0, STEPS)
    def _(step):
        first = step * SLOTS

        def synthesise(i):
            pair, groups = work[i]
            table = ztab_back[step, :, pair * pair_lanes : (pair + 1) * pair_lanes]
            totals[i % 2][...] = dot(held[block_of(rows, groups)], table)

        def analyse(i):
            pair, groups = work[i]
            start = pl.multiple_of((first + 2 * pair) * rows_z, pair_lanes)
            lanes = slot_lanes(result, first + 2 * pair, groups)
            spectra[block_of(rows, groups)] += dot(lanes, ztab[pl.ds(start, pair_lanes)])

        synthesise(0)
        for each in incoming:
            each.wait(step)
        for i, (pair, groups) in enumerate(work):
            if i + 1 < len(work):
                synthesise(i + 1)
            total = totals[i % 2]
            for g in groups:
                for offset in range(2):
                    c = g * GROUP + first + 2 * pair + offset
                    for x in range(0, width, 2):
                        place = (g - groups[0]) * rows + x * rows_y
                        value = total[place : place + wide, offset * rows_z : (offset + 1) * rows_z]
                        value = value + local_in[c, x : x + 2].reshape(wide, rows_z).astype(F32)
                        upstream = cotangent_in[c, x : x + 2].reshape(wide, rows_z)
                        answer = upstream * doubled_slope(value)
                        result[c, x : x + 2] = answer.reshape(2, rows_y, rows_z)
            if i:
                analyse(i - 1)
        analyse(len(work) - 1)
        outgoing.start(step)

    deliver(spectra, ytab, order, scale, message, per, channels, slabs)
    for step in range(STEPS):
        outgoing.wait(step)


def field_kernel(
    per, channels, slabs, arrived, local, ztab_back_far, ytab_back, out, ztab_back, order, held, local_in, result,
    local_sems, result_sems, table_sems,
):
    width, rows_y, rows_z = local.shape[1:]
    rows = width * rows_y
    pair_lanes = 2 * rows_z
    incoming = Move(local, local_in, local_sems)
    outgoing = Move(result, out.at[0], result_sems)
    table = pltpu.make_async_copy(ztab_back_far, ztab_back, table_sems.at[0])
    table.start()
    incoming.start(0)
    fill_order(per, channels, True, order)
    incoming.start(1)
    receive(arrived, order, ytab_back, None, held, per, slabs)
    incoming.start(2)
    incoming.start(3)
    table.wait()

    @pl.loop(0, STEPS)
    def _(step):
        incoming.wait(step)
        for pair, groups in units(channels // GROUP):
            lanes = ztab_back[step, :, pair * pair_lanes : (pair + 1) * pair_lanes]
            total = dot(held[block_of(rows, groups)], lanes)
            for g in groups:
                for offset in range(2):
                    c = g * GROUP + step * SLOTS + 2 * pair + offset
                    place = (g - groups[0]) * rows
                    value = total[place : place + rows, offset * rows_z : (offset + 1) * rows_z]
                    value = value + local_in[c].reshape(rows, rows_z).astype(F32)
                    result[c] = value.astype(BF16).reshape(width, rows_y, rows_z)
        outgoing.start(step)

    for step in range(STEPS):
        outgoing.wait(step)


def pointwise_kernel(turned, field, mix, offsets, out, table, shift):
    channels = mix.shape[0]
    width, rows_y, rows_z = field.shape[1:]
    size = channels * TILE

    @pl.when(pl.program_id(0) == 0)
    def _():
        row = over(lax.broadcasted_iota(jnp.int32, (size, channels), 0), TILE)
        column = lax.broadcasted_iota(jnp.int32, (size, channels), 1)
        spread = jnp.where(row == column, 1.0, 0.0).astype(BF16)
        tall = lax.dot_general(
            spread, mix[...], (((1,), (1 if turned else 0,)), ((), ())), preferred_element_type=F32
        ).astype(BF16)
        whole = lax.dot_general(
            tall, spread, (((1,), (1,)), ((), ())), preferred_element_type=F32
        )
        place = within(lax.broadcasted_iota(jnp.int32, (size, size), 0), TILE)
        other = within(lax.broadcasted_iota(jnp.int32, (size, size), 1), TILE)
        table[...] = jnp.where(place == other, whole if turned else 0.5 * whole, 0.0).astype(BF16)
        if offsets is not None:
            for c in range(channels):
                shift[c] = jnp.full((1, rows_z), offsets[c], F32)

    for start in range(0, rows_y, 2 * TILE):
        pieces = [field[:, x, start : start + 2 * TILE, :].astype(F32) for x in range(width)]
        halves = []
        for row in range(0, 2 * TILE, TILE):
            rows = [piece[:, row : row + TILE].reshape(size, rows_z).astype(BF16) for piece in pieces]
            halves.append(dot(table[...], jnp.concatenate(rows, axis=1)))
        for x in range(width):
            values = [
                half[:, x * rows_z : (x + 1) * rows_z].reshape(channels, TILE, rows_z) for half in halves
            ]
            value = jnp.concatenate(values, axis=1)
            if offsets is not None:
                value = (value + shift[...]) * math.sqrt(0.5)
            out[:, x, start : start + 2 * TILE, :] = value.astype(BF16)


def spread_pair(first, second):
    nothing = jnp.zeros_like(first)
    upper = jnp.concatenate([first, nothing], axis=1)
    lower = jnp.concatenate([nothing, second], axis=1)
    return jnp.concatenate([upper, lower], axis=0)


def low_half(shape):
    return lax.broadcasted_iota(jnp.int32, shape, 1) < shape[1] // 2


def mix_kernel(per, samples, arrived, weights, line, line_back, spec_in, message, held):
    rows = 2 * samples
    lanes = 2 * weights.shape[1]
    low = low_half((samples, lanes))
    flat = arrived[...].reshape(-1, arrived.shape[2])
    spectra = dot(line[...], flat).astype(BF16)
    spec_in[...] = spectra
    for q in range(MX):
        for first in range(0, per, 2):
            block = spread_pair(weights[first * MX + q], weights[(first + 1) * MX + q])
            place = first // 2 * lanes
            terms = dot(spectra[q * rows : (q + 1) * rows, place : place + lanes], block)
            mixed = []
            for side in range(2):
                part = terms[:, side * lanes : (side + 1) * lanes]
                turned = pltpu.roll(part[samples:], lanes // 2, 1)
                mixed.append(part[:samples] + jnp.where(low, -turned, turned))
            real = jnp.where(low, mixed[0], pltpu.roll(mixed[1], lanes // 2, 1))
            imag = jnp.where(low, pltpu.roll(mixed[0], lanes // 2, 1), mixed[1])
            held[q * rows : (q + 1) * rows, place : place + lanes] = jnp.concatenate(
                [real, imag], axis=0
            ).astype(BF16)
    message[...] = dot(line_back[...], held[...]).astype(BF16).reshape(message.shape)


def mix_back_kernel(per, samples, arrived, weights, line, line_back, pairs, message, held):
    rows = 2 * samples
    lanes = 2 * weights.shape[1]
    low = low_half((samples, lanes))
    flat = arrived[...].reshape(-1, arrived.shape[2])
    spectra = dot(line[...], flat).astype(BF16).astype(F32)
    for q in range(MX):
        for first in range(0, per, 2):
            block = spread_pair(weights[first * MX + q], weights[(first + 1) * MX + q])
            place = first // 2 * lanes
            real = spectra[q * rows : q * rows + samples, place : place + lanes]
            imag = spectra[q * rows + samples : (q + 1) * rows, place : place + lanes]
            real_turned = pltpu.roll(real, lanes // 2, 1)
            imag_turned = pltpu.roll(imag, lanes // 2, 1)
            left = [jnp.where(low, real, imag_turned), jnp.where(low, imag, -real_turned)]
            right = [jnp.where(low, real_turned, imag), jnp.where(low, imag_turned, -real)]
            pair = jnp.concatenate(
                [jnp.concatenate(left, axis=0), jnp.concatenate(right, axis=0)], axis=1
            ).astype(BF16)
            pairs[q * rows : (q + 1) * rows, 2 * place : 2 * (place + lanes)] = pair
            held[q * rows : (q + 1) * rows, place : place + lanes] = lax.dot_general(
                pair, block, (((1,), (1,)), ((), ())), preferred_element_type=F32
            ).astype(BF16)
    message[...] = dot(line_back[...], held[...]).astype(BF16).reshape(message.shape)


def weight_kernel(per, samples, spec_in, pairs, out):
    rows = 2 * samples
    lanes = out.shape[2]
    half = lanes // 2
    for q in range(MX):
        for first in range(0, per, 2):
            place = first // 2 * lanes
            left = spec_in[q * rows : (q + 1) * rows, place : place + lanes]
            right = pairs[q * rows : (q + 1) * rows, 2 * place : 2 * (place + lanes)]
            outer = lax.dot_general(
                left, right, (((0,), (0,)), ((), ())), preferred_element_type=F32
            )
            out[first * MX + q] = outer[:half, :lanes]
            out[(first + 1) * MX + q] = outer[half:, lanes:]


def whole(array):
    return pl.BlockSpec(array.shape, lambda *step: (0,) * len(array.shape))


def shaped(shape, dtype):
    return jax.ShapeDtypeStruct(shape, dtype)


def params(mib):
    return pltpu.CompilerParams(vmem_limit_bytes=mib * MIB)


def cost(flops, moved, steep=0):
    return pl.CostEstimate(flops=flops, bytes_accessed=moved, transcendentals=steep)


def body(mesh_axes, devices, slabs, activations, cotangent, mode_weights, pointwise, offsets):
    _, channels, width, rows_y, rows_z = activations.shape
    samples = devices // slabs
    per = MY * MZ // devices
    groups = channels // GROUP
    field = activations.shape[1:]
    count = math.prod(field)
    z_fwd = z_table(rows_z)
    z_back = np.ascontiguousarray(z_fwd.T.reshape(-1, STEPS, SLOTS * rows_z).transpose(1, 0, 2))
    ytab = y_table(rows_y, width)
    line_fwd, line_inv = x_tables(samples, slabs, NX)
    weight = np.where(np.arange(MZ) == 0, 1.0, 2.0) / (rows_y * rows_z)
    scale = np.tile(np.repeat(weight, GROUP), groups)[None]
    scale, scale_t = (0.5 * scale).astype(np.float32), (math.sqrt(0.5) * scale).astype(np.float32)
    ytab_t = np.ascontiguousarray(ytab.T)
    fwd_t, inv_t = (np.ascontiguousarray(t.T) for t in (line_fwd, line_inv))
    message = shaped((devices, 2 * width, per * channels), BF16)
    spectra = shaped((MX * 2 * samples, per * channels), BF16)
    ztab = pltpu.VMEM((GROUP * rows_z, 2 * MZ * GROUP), BF16)
    ztab_t = pltpu.VMEM(z_back.shape, BF16)
    order = pltpu.VMEM((MZ * channels, MZ * channels), BF16)
    rows = groups * width * rows_y
    held = pltpu.VMEM((rows, 2 * MZ * GROUP), BF16)
    sums = pltpu.VMEM((rows, 2 * MZ * GROUP), F32)
    pair_sums = pltpu.VMEM((rows // 2, 2 * rows_z), F32)
    buffer = pltpu.VMEM(field, BF16)
    sems = pltpu.SemaphoreType.DMA((STEPS * groups,))
    table_sems = pltpu.SemaphoreType.DMA((2,))
    far = pl.BlockSpec(memory_space=pltpu.HBM)
    far_field = pltpu.HBM(field, BF16)

    def kept_far(array):
        return pltpu.with_memory_space_constraint(array, pltpu.HBM)

    plane_flops = 2 * count * 2 * MZ * GROUP

    def exchange(array):
        return lax.all_to_all(array, mesh_axes, split_axis=0, concat_axis=0, tiled=True)

    def mix_points(values, turned, shifts):
        step = 2
        block = pl.BlockSpec((channels, step, rows_y, rows_z), lambda x: (0, x, 0, 0))
        kernel = functools.partial(pointwise_kernel, turned)
        specs = [block, whole(pointwise)]
        operands = [values, pointwise]
        if shifts is None:
            run = lambda a, b, *rest: kernel(a, b, None, *rest)
        else:
            run = kernel
            specs.append(pl.BlockSpec(memory_space=pltpu.SMEM))
            operands.append(shifts)
        return pl.pallas_call(
            run,
            grid=(width // step,),
            in_specs=specs,
            out_specs=block,
            out_shape=far_field,
            scratch_shapes=[
                pltpu.VMEM((channels * TILE, channels * TILE), BF16),
                pltpu.VMEM((channels, 1, rows_z), F32),
            ],
            compiler_params=params(32),
            cost_estimate=cost(2 * count * channels * TILE, 4 * count),
        )(*operands)

    planes = pl.pallas_call(
        functools.partial(plane_kernel, per, channels, slabs),
        in_specs=[far, far, far],
        out_specs=whole(message),
        out_shape=message,
        scratch_shapes=[
            ztab,
            order,
            sums,
            buffer,
            pltpu.VMEM(ytab.shape, BF16),
            sems,
            table_sems,
        ],
        compiler_params=params(32),
        cost_estimate=cost(plane_flops, 2 * count),
    )(kept_far(activations), kept_far(z_fwd), kept_far(ytab))
    arrived = exchange(planes)
    local = mix_points(kept_far(activations.reshape(field)), True, offsets)
    arrived, local = lax.optimization_barrier((arrived, local))
    spec_in, mixed = pl.pallas_call(
        functools.partial(mix_kernel, per, samples),
        out_shape=(spectra, message),
        scratch_shapes=[pltpu.VMEM(spectra.shape, BF16)],
        compiler_params=params(16),
        cost_estimate=cost(10**8, 2 * mode_weights.size),
    )(arrived, mode_weights, line_fwd, inv_t)
    returned = exchange(mixed)
    slope, back_plane = pl.pallas_call(
        functools.partial(slope_kernel, per, channels, slabs),
        in_specs=[whole(message), far, far, far, far] + [whole(t) for t in (ytab, ytab_t, scale, scale_t)],
        out_specs=(far, whole(message)),
        out_shape=(far_field, message),
        scratch_shapes=[ztab, ztab_t, order, held, sums]
        + [buffer] * 3
        + [pair_sums] * 2
        + [sems] * 3
        + [table_sems],
        compiler_params=params(40),
        cost_estimate=cost(2 * plane_flops, 6 * count, 2 * count),
    )(returned, kept_far(local), kept_far(cotangent), kept_far(z_fwd), kept_far(z_back), ytab, ytab_t, scale, scale_t)
    arrived_back = exchange(back_plane)
    local_back = mix_points(kept_far(slope), False, None)
    arrived_back, local_back = lax.optimization_barrier((arrived_back, local_back))
    pairs, mixed_back = pl.pallas_call(
        functools.partial(mix_back_kernel, per, samples),
        out_shape=(shaped((spectra.shape[0], 2 * spectra.shape[1]), BF16), message),
        scratch_shapes=[pltpu.VMEM(spectra.shape, BF16)],
        compiler_params=params(16),
        cost_estimate=cost(10**8, 2 * mode_weights.size),
    )(arrived_back, mode_weights, line_inv, fwd_t)
    returned_back = exchange(mixed_back)
    grad_spectral = pl.pallas_call(
        functools.partial(weight_kernel, per, samples),
        out_shape=shaped(mode_weights.shape, F32),
        compiler_params=params(16),
        cost_estimate=cost(10**8, 4 * mode_weights.size),
    )(spec_in, pairs)
    grad_in = pl.pallas_call(
        functools.partial(field_kernel, per, channels, slabs),
        in_specs=[whole(message), far, far, whole(ytab_t)],
        out_specs=far,
        out_shape=shaped(activations.shape, BF16),
        scratch_shapes=[ztab_t, order, held, buffer, buffer, sems, sems, table_sems],
        compiler_params=params(32),
        cost_estimate=cost(plane_flops, 4 * count),
    )(returned_back, kept_far(local_back), kept_far(z_back), ytab_t)
    return (grad_in, grad_spectral)


def chosen_body(mesh_axes, devices, slabs, activations, cotangent, mode_weights, pointwise, offsets):
    samples, channels, width, rows_y, rows_z = activations.shape
    per = MY * MZ // devices
    fits = (
        samples == 1
        and MY * MZ % devices == 0
        and per in (2, 4, 8)
        and width % 8 == 0
        and channels == 64
        and rows_y % TILE == 0
        and rows_z == 128
    )
    plan = functools.partial(body, mesh_axes, devices, slabs) if fits else general_body
    return plan(activations, cotangent, mode_weights, pointwise, offsets)


def solution(mesh):
    slabs = mesh.shape["space"]
    devices = slabs * mesh.shape["dp"]
    return jax.shard_map(
        functools.partial(chosen_body, ("dp", "space"), devices, slabs),
        mesh=mesh,
        in_specs=(
            P("dp", None, "space", None, None),
            P("dp", None, "space", None, None),
            P(("space", "dp"), None, None),
            P(),
            P(),
        ),
        out_specs=(P("dp", None, "space", None, None), P(("space", "dp"), None, None)),
        check_vma=False,
    )
```

```python
import functools
import math

import jax
import jax.numpy as jnp
import ml_dtypes
import numpy as np
from jax import lax
from jax.experimental import pallas as pl
from jax.experimental.pallas import tpu as pltpu
from jax.sharding import PartitionSpec as P

MX = 16
MY = 16
MZ = 8
NX = 32


def centered(count):
    index = jnp.arange(count, dtype=jnp.int32)
    return jnp.where(index < count // 2, index, index - count)


def plane_tables(rows_y, rows_z, modes_y, modes_z):
    along_y = jnp.arange(rows_y, dtype=jnp.int32)[:, None, None, None]
    along_z = jnp.arange(rows_z, dtype=jnp.int32)[None, :, None, None]
    freq_y = centered(modes_y)[None, None, :, None]
    freq_z = jnp.arange(modes_z, dtype=jnp.int32)[None, None, None, :]
    phase = jnp.mod(freq_y * along_y * rows_z + freq_z * along_z * rows_y, rows_y * rows_z)
    theta = phase.astype(jnp.float32) * (2.0 * math.pi / (rows_y * rows_z))
    cosine = jnp.cos(theta)
    sine = jnp.sin(theta)
    forward = jnp.stack([cosine, -sine], -1).reshape(rows_y * rows_z, modes_y * modes_z * 2)
    scaled = jnp.where(freq_z == 0, 1.0, 2.0).astype(jnp.float32) / (rows_y * rows_z)
    inverse = (
        jnp.stack([cosine * scaled, -sine * scaled], -1)
        .reshape(rows_y * rows_z, modes_y * modes_z * 2)
        .T
    )
    return (forward.astype(jnp.bfloat16), inverse.astype(jnp.bfloat16))


def line_tables(length, modes):
    along = jnp.arange(length, dtype=jnp.int32)[:, None]
    freq = centered(modes)[None, :]
    phase = jnp.mod(freq * along, length)
    theta = phase.astype(jnp.float32) * (2.0 * math.pi / length)
    cosine = jnp.cos(theta)
    sine = jnp.sin(theta)
    first = jnp.stack([cosine, -sine], -1)
    second = jnp.stack([sine, cosine], -1)
    forward = jnp.stack([first, second], 1).reshape(2 * length, 2 * modes)
    inv_first = jnp.stack([cosine.T, sine.T], -1) / length
    inv_second = jnp.stack([-sine.T, cosine.T], -1) / length
    inverse = jnp.stack([inv_first, inv_second], 1).reshape(2 * modes, 2 * length)
    return (forward.astype(jnp.bfloat16), inverse.astype(jnp.bfloat16))


def expand_weights(weights):
    half = weights.shape[1]
    real_part = weights[:, :, :half]
    imag_part = weights[:, :, half:]
    upper = jnp.concatenate([real_part, imag_part], axis=2)
    lower = jnp.concatenate([-imag_part, real_part], axis=2)
    return jnp.concatenate([upper, lower], axis=1)


def outer_sum(left, right):
    return jnp.einsum("mbi,mbo->mio", left, right, preferred_element_type=jnp.float32)


def weight_terms(spec_in, spec_grad):
    half = spec_in.shape[2] // 2
    in_real = spec_in[:, :, :half]
    in_imag = spec_in[:, :, half:]
    gr_real = spec_grad[:, :, :half]
    gr_imag = spec_grad[:, :, half:]
    real_term = outer_sum(in_real, gr_real) + outer_sum(in_imag, gr_imag)
    imag_term = outer_sum(in_real, gr_imag) - outer_sum(in_imag, gr_real)
    return jnp.concatenate([real_term, imag_term], axis=2)


def to_modes(slab, table, modes_x):
    samples, channels, width, pairs = slab.shape
    moved = lax.all_to_all(slab, "space", split_axis=3, concat_axis=2, tiled=True)
    length = moved.shape[2]
    local = moved.shape[3] // 2
    lines = moved.reshape(samples, channels, length, local, 2).transpose(0, 1, 3, 2, 4)
    lines = lines.reshape(samples, channels, local, 2 * length)
    spectra = jnp.dot(lines, table, preferred_element_type=jnp.float32).astype(jnp.bfloat16)
    spectra = spectra.reshape(samples, channels, local, modes_x, 2).transpose(2, 3, 0, 4, 1)
    return spectra.reshape(local * modes_x, samples, 2 * channels)


def to_slab(spectra, table, modes_x, channels):
    count, samples, doubled = spectra.shape
    local = count // modes_x
    lines = spectra.reshape(local, modes_x, samples, 2, channels).transpose(2, 4, 0, 1, 3)
    lines = lines.reshape(samples, channels, local, 2 * modes_x)
    lines = jnp.dot(lines, table, preferred_element_type=jnp.float32).astype(jnp.bfloat16)
    length = lines.shape[3] // 2
    lines = lines.reshape(samples, channels, local, length, 2).transpose(0, 1, 3, 2, 4)
    lines = lines.reshape(samples, channels, length, 2 * local)
    return lax.all_to_all(lines, "space", split_axis=2, concat_axis=3, tiled=True)


def to_owners(spectra):
    return lax.all_to_all(spectra, "dp", split_axis=0, concat_axis=1, tiled=True)


def from_owners(spectra):
    return lax.all_to_all(spectra, "dp", split_axis=1, concat_axis=0, tiled=True)


def gelu_slope(value):
    cdf = 0.5 * (1.0 + lax.erf(value * 0.7071067811865476))
    density = jnp.exp(-0.5 * value * value) * 0.3989422804014327
    return cdf + value * density


def general_body(activations, cotangent, mode_weights, pointwise, offsets):
    samples, channels, width, rows_y, rows_z = activations.shape
    plane_fwd, plane_inv = plane_tables(rows_y, rows_z, MY, MZ)
    line_fwd, line_inv = line_tables(NX, MX)
    flat = activations.reshape(samples, channels, width, rows_y * rows_z)
    planes = jnp.dot(flat, plane_fwd, preferred_element_type=jnp.float32).astype(jnp.bfloat16)
    spec_in = to_modes(planes, line_fwd, MX)
    blocks = expand_weights(mode_weights)
    held_in = to_owners(spec_in)
    held_out = jnp.einsum(
        "mbi,mio->mbo", held_in, blocks, preferred_element_type=jnp.float32
    ).astype(jnp.bfloat16)
    spec_out = from_owners(held_out)
    returned = to_slab(spec_out, line_inv, MX, channels)
    spectral = jnp.dot(returned, plane_inv, preferred_element_type=jnp.float32)
    local_part = jnp.einsum("io,bixn->boxn", pointwise, flat, preferred_element_type=jnp.float32)
    summed = spectral + local_part + offsets[None, :, None, None]
    upstream = cotangent.reshape(flat.shape).astype(jnp.float32)
    slope_grad = (upstream * gelu_slope(summed)).astype(jnp.bfloat16)
    back_plane = jnp.dot(slope_grad, plane_inv.T, preferred_element_type=jnp.float32).astype(
        jnp.bfloat16
    )
    spec_grad = to_modes(back_plane, line_inv.T, MX)
    held_grad = to_owners(spec_grad)
    held_dx = jnp.einsum(
        "mbo,mio->mbi", held_grad, blocks, preferred_element_type=jnp.float32
    ).astype(jnp.bfloat16)
    spec_dx = from_owners(held_dx)
    grad_spectral = weight_terms(held_in, held_grad)
    line_dx = to_slab(spec_dx, line_fwd.T, MX, channels)
    total = jnp.dot(line_dx, plane_fwd.T, preferred_element_type=jnp.float32)
    total = total + jnp.einsum(
        "io,boxn->bixn", pointwise, slope_grad, preferred_element_type=jnp.float32
    )
    grad_in = total.astype(jnp.bfloat16).reshape(activations.shape)
    return (grad_in, grad_spectral)


BF16 = jnp.bfloat16
F32 = jnp.float32
GROUP = 16
TILE = 8
SLOTS = 4
STEPS = GROUP // SLOTS
MIB = 1024 * 1024


def rounded(table):
    return np.asarray(table, np.float32).astype(ml_dtypes.bfloat16)


def angles(freq, points, length):
    phase = np.mod(np.outer(freq, points), length)
    return (phase * (2.0 * math.pi / length)).astype(np.float64)


def signed(count):
    index = np.arange(count)
    return np.where(index < count // 2, index, index - count)


def z_base(rows_z):
    theta = angles(np.arange(MZ), np.arange(rows_z), rows_z)
    pair = np.stack([np.cos(theta), -np.sin(theta)])
    table = np.repeat(pair.reshape(2 * MZ, rows_z), GROUP, axis=0).T
    return rounded(table).astype(np.float32)


def y_table(rows_y, width):
    theta = angles(signed(MY), np.arange(rows_y), rows_y)
    cosine, sine = np.cos(theta), np.sin(theta)
    turn = np.stack([np.stack([cosine, sine]), np.stack([-sine, cosine])])
    table = np.einsum("rsjy,xw->jxrswy", turn, np.eye(width))
    return rounded(table.reshape(MY * width * 2, 2 * width * rows_y))


def x_tables(samples, slabs, length):
    theta = angles(signed(MX), np.arange(length), length)
    cosine, sine = np.cos(theta), np.sin(theta)
    forward = np.stack([np.stack([cosine, sine]), np.stack([-sine, cosine])])
    inverse = np.stack([np.stack([cosine, sine]), np.stack([-sine, cosine])]) / length
    same = np.eye(samples)
    rows = MX * 2 * samples

    def lay(turn):
        turn = turn.reshape(2, 2, MX, slabs, length // slabs)
        table = np.einsum("arqsx,bd->qabdsxr", turn, same)
        return rounded(table.reshape(rows, samples * length * 2))

    return lay(forward), lay(inverse)


def dot(left, right):
    return jnp.dot(left, right, preferred_element_type=F32)


def doubled_slope(u):
    decay = jnp.exp2(u * u * -math.log2(math.e)).astype(BF16)
    cdf = (1.0 + lax.erf(u)).astype(BF16)
    return cdf + u.astype(BF16) * jnp.asarray(2.0 / math.sqrt(math.pi), BF16) * decay


def over(index, size):
    return lax.shift_right_logical(index, jnp.int32(size.bit_length() - 1))


def within(index, size):
    return jnp.bitwise_and(index, jnp.int32(size - 1))


def fill_z(base, table):
    rows_z, lanes = base.shape
    owner = within(lax.broadcasted_iota(jnp.int32, (rows_z, lanes), 1), GROUP)
    values = base[...]
    for c in range(GROUP):
        table[c * rows_z : (c + 1) * rows_z] = jnp.where(owner == c, values, 0.0).astype(BF16)


def fill_z_back(base, table):
    lanes, rows_z = base.shape
    owner = within(lax.broadcasted_iota(jnp.int32, (lanes, rows_z), 0), GROUP)
    values = base[...]
    for c in range(GROUP):
        first = c % SLOTS * rows_z
        table[c // SLOTS, :, first : first + rows_z] = jnp.where(owner == c, values, 0.0).astype(BF16)


def grouped(lane, per, channels):
    c = within(lane, channels)
    return over(c, GROUP) * (MZ * GROUP) + over(lane, channels) * GROUP + within(c, GROUP)


def fill_order(per, channels, back, table):
    count = table.shape[0]
    row = lax.broadcasted_iota(jnp.int32, (count, count), 0)
    column = lax.broadcasted_iota(jnp.int32, (count, count), 1)
    if back:
        same = grouped(row[:, :1], per, channels) == column
    else:
        same = row == grouped(column[:1], per, channels)
    table[...] = jnp.where(same, 1.0, 0.0).astype(BF16)


def turned_index(index, slabs, devices):
    samples = devices // slabs
    return index % samples * slabs + index // samples


def deliver(spectra, ytab, order, scale, message, per, channels, slabs):
    groups = channels // GROUP
    rows = spectra.shape[0] // groups
    wide = spectra.shape[1] // 2
    halves = []
    for r in range(2):
        blocks = [spectra[g * rows : (g + 1) * rows, r * wide : (r + 1) * wide] for g in range(groups)]
        halves.append(jnp.concatenate(blocks, axis=1).astype(BF16))
    planes = dot(ytab[...], jnp.concatenate(halves, axis=0))
    if scale is not None:
        planes = planes * scale[...]
    ordered = dot(planes.astype(BF16), order[...]).astype(BF16)
    parts = MZ // per
    count = message.shape[1]
    lanes = per * channels
    for part in range(parts):
        block = ordered[:, part * lanes : (part + 1) * lanes]
        for j in range(MY):
            message[turned_index(j * parts + part, slabs, message.shape[0])] = block[j * count : (j + 1) * count]


def receive(message, order_back, ytab_back, scale, held, per, slabs):
    parts = MZ // per
    lanes = [
        jnp.concatenate(
            [message[turned_index(j * parts + part, slabs, message.shape[0])] for j in range(MY)], axis=0
        )
        for part in range(parts)
    ]
    ordered = dot(jnp.concatenate(lanes, axis=1), order_back[...]).astype(BF16)
    lines = dot(ytab_back[...], ordered)
    if scale is not None:
        lines = lines * scale[...]
    lines = lines.astype(BF16)
    rows = lines.shape[0] // 2
    wide = MZ * GROUP
    for group in range(held.shape[0] // rows):
        piece = lines[:, group * wide : (group + 1) * wide]
        held[group * rows : (group + 1) * rows] = jnp.concatenate([piece[:rows], piece[rows:]], axis=1)


class Move:
    def __init__(self, source, target, sems):
        self.source, self.target, self.sems = source, target, sems
        self.groups = target.shape[0] // GROUP

    def copies(self, step):
        for g in range(self.groups):
            run = pl.ds(g * GROUP + step * SLOTS, SLOTS)
            sem = self.sems.at[step * self.groups + g]
            yield pltpu.make_async_copy(self.source.at[run], self.target.at[run], sem)

    def start(self, step):
        for copy in self.copies(step):
            copy.start()

    def wait(self, step):
        for copy in self.copies(step):
            copy.wait()


def start_all(moves, step):
    for each in moves:
        each.start(step)


def add_spectra(field, ztab, step, spectra):
    groups = field.shape[0] // GROUP
    rows_z = field.shape[-1]
    depth = SLOTS * rows_z
    table = ztab[pl.ds(pl.multiple_of(step * depth, depth), depth)]
    lanes = [
        jnp.concatenate(
            [field[g * GROUP + step * SLOTS + slot].reshape(-1, rows_z) for g in range(groups)], axis=0
        )
        for slot in range(SLOTS)
    ]
    spectra[...] += dot(jnp.concatenate(lanes, axis=1), table)


def plane_kernel(
    per, channels, slabs, field, base_far, ytab_far, message, ztab, order, spectra, buffer, base, ytab, sems, table_sems
):
    incoming = Move(field.at[0], buffer, sems)
    base_copy = pltpu.make_async_copy(base_far, base, table_sems.at[0])
    ytab_copy = pltpu.make_async_copy(ytab_far, ytab, table_sems.at[1])
    base_copy.start()
    incoming.start(0)
    fill_order(per, channels, False, order)
    spectra[...] = jnp.zeros_like(spectra)
    incoming.start(1)
    base_copy.wait()
    fill_z(base, ztab)
    incoming.start(2)
    ytab_copy.start()
    incoming.start(3)

    @pl.loop(0, STEPS)
    def _(step):
        incoming.wait(step)
        add_spectra(buffer, ztab, step, spectra)

    ytab_copy.wait()
    deliver(spectra, ytab, order, None, message, per, channels, slabs)


def slope_kernel(
    per, channels, slabs, arrived, local, cotangent, base, base_back, ytab, ytab_back, scale, scale_back,
    slope, message, ztab, ztab_back, order, held, spectra, local_in, cotangent_in, result, total,
    local_sems, cotangent_sems, result_sems,
):
    width, rows_y, rows_z = local.shape[1:]
    groups = channels // GROUP
    rows = width * rows_y
    wide = 2 * rows_y
    incoming = (Move(local, local_in, local_sems), Move(cotangent.at[0], cotangent_in, cotangent_sems))
    outgoing = Move(result, slope, result_sems)
    start_all(incoming, 0)
    fill_order(per, channels, True, order)
    receive(arrived, order, ytab_back, scale_back, held, per, slabs)
    start_all(incoming, 1)
    fill_z_back(base_back, ztab_back)
    fill_z(base, ztab)
    start_all(incoming, 2)
    fill_order(per, channels, False, order)
    spectra[...] = jnp.zeros_like(spectra)
    start_all(incoming, 3)

    @pl.loop(0, STEPS)
    def _(step):
        for each in incoming:
            each.wait(step)
        total[...] = dot(held[...], ztab_back[step])
        for slot in range(SLOTS):
            lanes = slice(slot * rows_z, (slot + 1) * rows_z)
            for g in range(groups):
                c = g * GROUP + step * SLOTS + slot
                for x in range(0, width, 2):
                    place = g * rows + x * rows_y
                    value = total[place : place + wide, lanes]
                    value = value + local_in[c, x : x + 2].reshape(wide, rows_z).astype(F32)
                    upstream = cotangent_in[c, x : x + 2].reshape(wide, rows_z)
                    answer = upstream * doubled_slope(value)
                    result[c, x : x + 2] = answer.reshape(2, rows_y, rows_z)
        outgoing.start(step)
        add_spectra(result, ztab, step, spectra)

    deliver(spectra, ytab, order, scale, message, per, channels, slabs)
    for step in range(STEPS):
        outgoing.wait(step)


def field_kernel(
    per, channels, slabs, arrived, local, base_back, ytab_back, out, ztab_back, order, held, local_in, result,
    local_sems, result_sems,
):
    width, rows_y, rows_z = local.shape[1:]
    groups = channels // GROUP
    rows = width * rows_y
    incoming = Move(local, local_in, local_sems)
    outgoing = Move(result, out.at[0], result_sems)
    incoming.start(0)
    fill_order(per, channels, True, order)
    incoming.start(1)
    receive(arrived, order, ytab_back, None, held, per, slabs)
    incoming.start(2)
    fill_z_back(base_back, ztab_back)
    incoming.start(3)

    @pl.loop(0, STEPS)
    def _(step):
        incoming.wait(step)
        total = dot(held[...], ztab_back[step])
        for slot in range(SLOTS):
            lanes = slice(slot * rows_z, (slot + 1) * rows_z)
            for g in range(groups):
                c = g * GROUP + step * SLOTS + slot
                value = total[g * rows : (g + 1) * rows, lanes]
                value = value + local_in[c].reshape(rows, rows_z).astype(F32)
                result[c] = value.astype(BF16).reshape(width, rows_y, rows_z)
        outgoing.start(step)

    for step in range(STEPS):
        outgoing.wait(step)


def pointwise_kernel(turned, field, mix, offsets, out, table, shift):
    channels = mix.shape[0]
    width, rows_y, rows_z = field.shape[1:]
    size = channels * TILE

    @pl.when(pl.program_id(0) == 0)
    def _():
        row = over(lax.broadcasted_iota(jnp.int32, (size, channels), 0), TILE)
        column = lax.broadcasted_iota(jnp.int32, (size, channels), 1)
        spread = jnp.where(row == column, 1.0, 0.0).astype(BF16)
        tall = lax.dot_general(
            spread, mix[...], (((1,), (1 if turned else 0,)), ((), ())), preferred_element_type=F32
        ).astype(BF16)
        whole = lax.dot_general(
            tall, spread, (((1,), (1,)), ((), ())), preferred_element_type=F32
        )
        place = within(lax.broadcasted_iota(jnp.int32, (size, size), 0), TILE)
        other = within(lax.broadcasted_iota(jnp.int32, (size, size), 1), TILE)
        table[...] = jnp.where(place == other, whole if turned else 0.5 * whole, 0.0).astype(BF16)
        if offsets is not None:
            for c in range(channels):
                shift[c] = jnp.full((1, rows_z), offsets[c], F32)

    for start in range(0, rows_y, 2 * TILE):
        pieces = [field[:, x, start : start + 2 * TILE, :].astype(F32) for x in range(width)]
        halves = []
        for row in range(0, 2 * TILE, TILE):
            rows = [piece[:, row : row + TILE].reshape(size, rows_z).astype(BF16) for piece in pieces]
            halves.append(dot(table[...], jnp.concatenate(rows, axis=1)))
        for x in range(width):
            values = [
                half[:, x * rows_z : (x + 1) * rows_z].reshape(channels, TILE, rows_z) for half in halves
            ]
            value = jnp.concatenate(values, axis=1)
            if offsets is not None:
                value = (value + shift[...]) * math.sqrt(0.5)
            out[:, x, start : start + 2 * TILE, :] = value.astype(BF16)


def spread_pair(first, second):
    nothing = jnp.zeros_like(first)
    upper = jnp.concatenate([first, nothing], axis=1)
    lower = jnp.concatenate([nothing, second], axis=1)
    return jnp.concatenate([upper, lower], axis=0)


def low_half(shape):
    return lax.broadcasted_iota(jnp.int32, shape, 1) < shape[1] // 2


def mix_kernel(per, samples, arrived, weights, line, line_back, spec_in, message, held):
    rows = 2 * samples
    lanes = 2 * weights.shape[1]
    low = low_half((samples, lanes))
    flat = arrived[...].reshape(-1, arrived.shape[2])
    spectra = dot(line[...], flat).astype(BF16)
    spec_in[...] = spectra
    for q in range(MX):
        for first in range(0, per, 2):
            block = spread_pair(weights[first * MX + q], weights[(first + 1) * MX + q])
            place = first // 2 * lanes
            terms = dot(spectra[q * rows : (q + 1) * rows, place : place + lanes], block)
            mixed = []
            for side in range(2):
                part = terms[:, side * lanes : (side + 1) * lanes]
                turned = pltpu.roll(part[samples:], lanes // 2, 1)
                mixed.append(part[:samples] + jnp.where(low, -turned, turned))
            real = jnp.where(low, mixed[0], pltpu.roll(mixed[1], lanes // 2, 1))
            imag = jnp.where(low, pltpu.roll(mixed[0], lanes // 2, 1), mixed[1])
            held[q * rows : (q + 1) * rows, place : place + lanes] = jnp.concatenate(
                [real, imag], axis=0
            ).astype(BF16)
    message[...] = dot(line_back[...], held[...]).astype(BF16).reshape(message.shape)


def mix_back_kernel(per, samples, arrived, weights, line, line_back, pairs, message, held):
    rows = 2 * samples
    lanes = 2 * weights.shape[1]
    low = low_half((samples, lanes))
    flat = arrived[...].reshape(-1, arrived.shape[2])
    spectra = dot(line[...], flat).astype(BF16).astype(F32)
    for q in range(MX):
        for first in range(0, per, 2):
            block = spread_pair(weights[first * MX + q], weights[(first + 1) * MX + q])
            place = first // 2 * lanes
            real = spectra[q * rows : q * rows + samples, place : place + lanes]
            imag = spectra[q * rows + samples : (q + 1) * rows, place : place + lanes]
            real_turned = pltpu.roll(real, lanes // 2, 1)
            imag_turned = pltpu.roll(imag, lanes // 2, 1)
            left = [jnp.where(low, real, imag_turned), jnp.where(low, imag, -real_turned)]
            right = [jnp.where(low, real_turned, imag), jnp.where(low, imag_turned, -real)]
            pair = jnp.concatenate(
                [jnp.concatenate(left, axis=0), jnp.concatenate(right, axis=0)], axis=1
            ).astype(BF16)
            pairs[q * rows : (q + 1) * rows, 2 * place : 2 * (place + lanes)] = pair
            held[q * rows : (q + 1) * rows, place : place + lanes] = lax.dot_general(
                pair, block, (((1,), (1,)), ((), ())), preferred_element_type=F32
            ).astype(BF16)
    message[...] = dot(line_back[...], held[...]).astype(BF16).reshape(message.shape)


def weight_kernel(per, samples, spec_in, pairs, out):
    rows = 2 * samples
    lanes = out.shape[2]
    half = lanes // 2
    for q in range(MX):
        for first in range(0, per, 2):
            place = first // 2 * lanes
            left = spec_in[q * rows : (q + 1) * rows, place : place + lanes]
            right = pairs[q * rows : (q + 1) * rows, 2 * place : 2 * (place + lanes)]
            outer = lax.dot_general(
                left, right, (((0,), (0,)), ((), ())), preferred_element_type=F32
            )
            out[first * MX + q] = outer[:half, :lanes]
            out[(first + 1) * MX + q] = outer[half:, lanes:]


def whole(array):
    return pl.BlockSpec(array.shape, lambda *step: (0,) * len(array.shape))


def shaped(shape, dtype):
    return jax.ShapeDtypeStruct(shape, dtype)


def params(mib):
    return pltpu.CompilerParams(vmem_limit_bytes=mib * MIB)


def cost(flops, moved, steep=0):
    return pl.CostEstimate(flops=flops, bytes_accessed=moved, transcendentals=steep)


def body(mesh_axes, devices, slabs, activations, cotangent, mode_weights, pointwise, offsets):
    _, channels, width, rows_y, rows_z = activations.shape
    samples = devices // slabs
    per = MY * MZ // devices
    groups = channels // GROUP
    field = activations.shape[1:]
    count = math.prod(field)
    base = z_base(rows_z)
    ytab = y_table(rows_y, width)
    line_fwd, line_inv = x_tables(samples, slabs, NX)
    weight = np.where(np.arange(MZ) == 0, 1.0, 2.0) / (rows_y * rows_z)
    scale = np.tile(np.repeat(weight, GROUP), groups)[None]
    scale, scale_t = (0.5 * scale).astype(np.float32), (math.sqrt(0.5) * scale).astype(np.float32)
    base_t, ytab_t = (np.ascontiguousarray(t.T) for t in (base, ytab))
    fwd_t, inv_t = (np.ascontiguousarray(t.T) for t in (line_fwd, line_inv))
    message = shaped((devices, 2 * width, per * channels), BF16)
    spectra = shaped((MX * 2 * samples, per * channels), BF16)
    ztab = pltpu.VMEM((GROUP * rows_z, 2 * MZ * GROUP), BF16)
    ztab_t = pltpu.VMEM((STEPS, 2 * MZ * GROUP, SLOTS * rows_z), BF16)
    order = pltpu.VMEM((MZ * channels, MZ * channels), BF16)
    rows = groups * width * rows_y
    held = pltpu.VMEM((rows, 2 * MZ * GROUP), BF16)
    sums = pltpu.VMEM((rows, 2 * MZ * GROUP), F32)
    slot_sums = pltpu.VMEM((rows, SLOTS * rows_z), F32)
    buffer = pltpu.VMEM(field, BF16)
    sems = pltpu.SemaphoreType.DMA((STEPS * groups,))
    far = pl.BlockSpec(memory_space=pltpu.HBM)
    far_field = pltpu.HBM(field, BF16)

    def kept_far(array):
        return pltpu.with_memory_space_constraint(array, pltpu.HBM)

    plane_flops = 2 * count * 2 * MZ * GROUP

    def exchange(array):
        return lax.all_to_all(array, mesh_axes, split_axis=0, concat_axis=0, tiled=True)

    def mix_points(values, turned, shifts):
        step = 2
        block = pl.BlockSpec((channels, step, rows_y, rows_z), lambda x: (0, x, 0, 0))
        kernel = functools.partial(pointwise_kernel, turned)
        specs = [block, whole(pointwise)]
        operands = [values, pointwise]
        if shifts is None:
            run = lambda a, b, *rest: kernel(a, b, None, *rest)
        else:
            run = kernel
            specs.append(pl.BlockSpec(memory_space=pltpu.SMEM))
            operands.append(shifts)
        return pl.pallas_call(
            run,
            grid=(width // step,),
            in_specs=specs,
            out_specs=block,
            out_shape=far_field,
            scratch_shapes=[
                pltpu.VMEM((channels * TILE, channels * TILE), BF16),
                pltpu.VMEM((channels, 1, rows_z), F32),
            ],
            compiler_params=params(32),
            cost_estimate=cost(2 * count * channels * TILE, 4 * count),
        )(*operands)

    planes = pl.pallas_call(
        functools.partial(plane_kernel, per, channels, slabs),
        in_specs=[far, far, far],
        out_specs=whole(message),
        out_shape=message,
        scratch_shapes=[
            ztab,
            order,
            sums,
            buffer,
            pltpu.VMEM(base.shape, F32),
            pltpu.VMEM(ytab.shape, BF16),
            sems,
            pltpu.SemaphoreType.DMA((2,)),
        ],
        compiler_params=params(32),
        cost_estimate=cost(plane_flops, 2 * count),
    )(kept_far(activations), kept_far(base), kept_far(ytab))
    arrived = exchange(planes)
    local = mix_points(kept_far(activations.reshape(field)), True, offsets)
    arrived, local = lax.optimization_barrier((arrived, local))
    spec_in, mixed = pl.pallas_call(
        functools.partial(mix_kernel, per, samples),
        out_shape=(spectra, message),
        scratch_shapes=[pltpu.VMEM(spectra.shape, BF16)],
        compiler_params=params(16),
        cost_estimate=cost(10**8, 2 * mode_weights.size),
    )(arrived, mode_weights, line_fwd, inv_t)
    returned = exchange(mixed)
    slope, back_plane = pl.pallas_call(
        functools.partial(slope_kernel, per, channels, slabs),
        in_specs=[whole(message), far, far]
        + [whole(t) for t in (base, base_t, ytab, ytab_t, scale, scale_t)],
        out_specs=(far, whole(message)),
        out_shape=(far_field, message),
        scratch_shapes=[ztab, ztab_t, order, held, sums]
        + [buffer] * 3
        + [slot_sums]
        + [sems] * 3,
        compiler_params=params(40),
        cost_estimate=cost(2 * plane_flops, 6 * count, 2 * count),
    )(returned, kept_far(local), kept_far(cotangent), base, base_t, ytab, ytab_t, scale, scale_t)
    arrived_back = exchange(back_plane)
    local_back = mix_points(kept_far(slope), False, None)
    arrived_back, local_back = lax.optimization_barrier((arrived_back, local_back))
    pairs, mixed_back = pl.pallas_call(
        functools.partial(mix_back_kernel, per, samples),
        out_shape=(shaped((spectra.shape[0], 2 * spectra.shape[1]), BF16), message),
        scratch_shapes=[pltpu.VMEM(spectra.shape, BF16)],
        compiler_params=params(16),
        cost_estimate=cost(10**8, 2 * mode_weights.size),
    )(arrived_back, mode_weights, line_inv, fwd_t)
    returned_back = exchange(mixed_back)
    grad_spectral = pl.pallas_call(
        functools.partial(weight_kernel, per, samples),
        out_shape=shaped(mode_weights.shape, F32),
        compiler_params=params(16),
        cost_estimate=cost(10**8, 4 * mode_weights.size),
    )(spec_in, pairs)
    grad_in = pl.pallas_call(
        functools.partial(field_kernel, per, channels, slabs),
        in_specs=[whole(message), far, whole(base_t), whole(ytab_t)],
        out_specs=far,
        out_shape=shaped(activations.shape, BF16),
        scratch_shapes=[ztab_t, order, held, buffer, buffer, sems, sems],
        compiler_params=params(32),
        cost_estimate=cost(plane_flops, 4 * count),
    )(returned_back, kept_far(local_back), base_t, ytab_t)
    return (grad_in, grad_spectral)


def chosen_body(mesh_axes, devices, slabs, activations, cotangent, mode_weights, pointwise, offsets):
    samples, channels, width, rows_y, rows_z = activations.shape
    per = MY * MZ // devices
    fits = (
        samples == 1
        and MY * MZ % devices == 0
        and per in (2, 4, 8)
        and width % 8 == 0
        and channels == 64
        and rows_y % TILE == 0
        and rows_z == 128
    )
    plan = functools.partial(body, mesh_axes, devices, slabs) if fits else general_body
    return plan(activations, cotangent, mode_weights, pointwise, offsets)


def solution(mesh):
    slabs = mesh.shape["space"]
    devices = slabs * mesh.shape["dp"]
    return jax.shard_map(
        functools.partial(chosen_body, ("dp", "space"), devices, slabs),
        mesh=mesh,
        in_specs=(
            P("dp", None, "space", None, None),
            P("dp", None, "space", None, None),
            P(("space", "dp"), None, None),
            P(),
            P(),
        ),
        out_specs=(P("dp", None, "space", None, None), P(("space", "dp"), None, None)),
        check_vma=False,
    )
```

```python
import functools
import math

import jax
import jax.numpy as jnp
import ml_dtypes
import numpy as np
from jax import lax
from jax.experimental import pallas as pl
from jax.experimental.pallas import tpu as pltpu
from jax.sharding import PartitionSpec as P

MX = 16
MY = 16
MZ = 8
NX = 32


def centered(count):
    index = jnp.arange(count, dtype=jnp.int32)
    return jnp.where(index < count // 2, index, index - count)


def plane_tables(rows_y, rows_z, modes_y, modes_z):
    along_y = jnp.arange(rows_y, dtype=jnp.int32)[:, None, None, None]
    along_z = jnp.arange(rows_z, dtype=jnp.int32)[None, :, None, None]
    freq_y = centered(modes_y)[None, None, :, None]
    freq_z = jnp.arange(modes_z, dtype=jnp.int32)[None, None, None, :]
    phase = jnp.mod(freq_y * along_y * rows_z + freq_z * along_z * rows_y, rows_y * rows_z)
    theta = phase.astype(jnp.float32) * (2.0 * math.pi / (rows_y * rows_z))
    cosine = jnp.cos(theta)
    sine = jnp.sin(theta)
    forward = jnp.stack([cosine, -sine], -1).reshape(rows_y * rows_z, modes_y * modes_z * 2)
    scaled = jnp.where(freq_z == 0, 1.0, 2.0).astype(jnp.float32) / (rows_y * rows_z)
    inverse = (
        jnp.stack([cosine * scaled, -sine * scaled], -1)
        .reshape(rows_y * rows_z, modes_y * modes_z * 2)
        .T
    )
    return (forward.astype(jnp.bfloat16), inverse.astype(jnp.bfloat16))


def line_tables(length, modes):
    along = jnp.arange(length, dtype=jnp.int32)[:, None]
    freq = centered(modes)[None, :]
    phase = jnp.mod(freq * along, length)
    theta = phase.astype(jnp.float32) * (2.0 * math.pi / length)
    cosine = jnp.cos(theta)
    sine = jnp.sin(theta)
    first = jnp.stack([cosine, -sine], -1)
    second = jnp.stack([sine, cosine], -1)
    forward = jnp.stack([first, second], 1).reshape(2 * length, 2 * modes)
    inv_first = jnp.stack([cosine.T, sine.T], -1) / length
    inv_second = jnp.stack([-sine.T, cosine.T], -1) / length
    inverse = jnp.stack([inv_first, inv_second], 1).reshape(2 * modes, 2 * length)
    return (forward.astype(jnp.bfloat16), inverse.astype(jnp.bfloat16))


def expand_weights(weights):
    half = weights.shape[1]
    real_part = weights[:, :, :half]
    imag_part = weights[:, :, half:]
    upper = jnp.concatenate([real_part, imag_part], axis=2)
    lower = jnp.concatenate([-imag_part, real_part], axis=2)
    return jnp.concatenate([upper, lower], axis=1)


def outer_sum(left, right):
    return jnp.einsum("mbi,mbo->mio", left, right, preferred_element_type=jnp.float32)


def weight_terms(spec_in, spec_grad):
    half = spec_in.shape[2] // 2
    in_real = spec_in[:, :, :half]
    in_imag = spec_in[:, :, half:]
    gr_real = spec_grad[:, :, :half]
    gr_imag = spec_grad[:, :, half:]
    real_term = outer_sum(in_real, gr_real) + outer_sum(in_imag, gr_imag)
    imag_term = outer_sum(in_real, gr_imag) - outer_sum(in_imag, gr_real)
    return jnp.concatenate([real_term, imag_term], axis=2)


def to_modes(slab, table, modes_x):
    samples, channels, width, pairs = slab.shape
    moved = lax.all_to_all(slab, "space", split_axis=3, concat_axis=2, tiled=True)
    length = moved.shape[2]
    local = moved.shape[3] // 2
    lines = moved.reshape(samples, channels, length, local, 2).transpose(0, 1, 3, 2, 4)
    lines = lines.reshape(samples, channels, local, 2 * length)
    spectra = jnp.dot(lines, table, preferred_element_type=jnp.float32).astype(jnp.bfloat16)
    spectra = spectra.reshape(samples, channels, local, modes_x, 2).transpose(2, 3, 0, 4, 1)
    return spectra.reshape(local * modes_x, samples, 2 * channels)


def to_slab(spectra, table, modes_x, channels):
    count, samples, doubled = spectra.shape
    local = count // modes_x
    lines = spectra.reshape(local, modes_x, samples, 2, channels).transpose(2, 4, 0, 1, 3)
    lines = lines.reshape(samples, channels, local, 2 * modes_x)
    lines = jnp.dot(lines, table, preferred_element_type=jnp.float32).astype(jnp.bfloat16)
    length = lines.shape[3] // 2
    lines = lines.reshape(samples, channels, local, length, 2).transpose(0, 1, 3, 2, 4)
    lines = lines.reshape(samples, channels, length, 2 * local)
    return lax.all_to_all(lines, "space", split_axis=2, concat_axis=3, tiled=True)


def to_owners(spectra):
    return lax.all_to_all(spectra, "dp", split_axis=0, concat_axis=1, tiled=True)


def from_owners(spectra):
    return lax.all_to_all(spectra, "dp", split_axis=1, concat_axis=0, tiled=True)


def gelu_slope(value):
    cdf = 0.5 * (1.0 + lax.erf(value * 0.7071067811865476))
    density = jnp.exp(-0.5 * value * value) * 0.3989422804014327
    return cdf + value * density


def general_body(activations, cotangent, mode_weights, pointwise, offsets):
    samples, channels, width, rows_y, rows_z = activations.shape
    plane_fwd, plane_inv = plane_tables(rows_y, rows_z, MY, MZ)
    line_fwd, line_inv = line_tables(NX, MX)
    flat = activations.reshape(samples, channels, width, rows_y * rows_z)
    planes = jnp.dot(flat, plane_fwd, preferred_element_type=jnp.float32).astype(jnp.bfloat16)
    spec_in = to_modes(planes, line_fwd, MX)
    blocks = expand_weights(mode_weights)
    held_in = to_owners(spec_in)
    held_out = jnp.einsum(
        "mbi,mio->mbo", held_in, blocks, preferred_element_type=jnp.float32
    ).astype(jnp.bfloat16)
    spec_out = from_owners(held_out)
    returned = to_slab(spec_out, line_inv, MX, channels)
    spectral = jnp.dot(returned, plane_inv, preferred_element_type=jnp.float32)
    local_part = jnp.einsum("io,bixn->boxn", pointwise, flat, preferred_element_type=jnp.float32)
    summed = spectral + local_part + offsets[None, :, None, None]
    upstream = cotangent.reshape(flat.shape).astype(jnp.float32)
    slope_grad = (upstream * gelu_slope(summed)).astype(jnp.bfloat16)
    back_plane = jnp.dot(slope_grad, plane_inv.T, preferred_element_type=jnp.float32).astype(
        jnp.bfloat16
    )
    spec_grad = to_modes(back_plane, line_inv.T, MX)
    held_grad = to_owners(spec_grad)
    held_dx = jnp.einsum(
        "mbo,mio->mbi", held_grad, blocks, preferred_element_type=jnp.float32
    ).astype(jnp.bfloat16)
    spec_dx = from_owners(held_dx)
    grad_spectral = weight_terms(held_in, held_grad)
    line_dx = to_slab(spec_dx, line_fwd.T, MX, channels)
    total = jnp.dot(line_dx, plane_fwd.T, preferred_element_type=jnp.float32)
    total = total + jnp.einsum(
        "io,boxn->bixn", pointwise, slope_grad, preferred_element_type=jnp.float32
    )
    grad_in = total.astype(jnp.bfloat16).reshape(activations.shape)
    return (grad_in, grad_spectral)


BF16 = jnp.bfloat16
F32 = jnp.float32
GROUP = 16
TILE = 8
SLOTS = 4
STEPS = GROUP // SLOTS
MIB = 1024 * 1024


def rounded(table):
    return np.asarray(table, np.float32).astype(ml_dtypes.bfloat16)


def angles(freq, points, length):
    phase = np.mod(np.outer(freq, points), length)
    return (phase * (2.0 * math.pi / length)).astype(np.float64)


def signed(count):
    index = np.arange(count)
    return np.where(index < count // 2, index, index - count)


def z_base(rows_z):
    theta = angles(np.arange(MZ), np.arange(rows_z), rows_z)
    pair = np.stack([np.cos(theta), -np.sin(theta)])
    table = np.repeat(pair.reshape(2 * MZ, rows_z), GROUP, axis=0).T
    return rounded(table).astype(np.float32)


def y_table(rows_y, width):
    theta = angles(signed(MY), np.arange(rows_y), rows_y)
    cosine, sine = np.cos(theta), np.sin(theta)
    turn = np.stack([np.stack([cosine, sine]), np.stack([-sine, cosine])])
    table = np.einsum("rsjy,xw->jxrswy", turn, np.eye(width))
    return rounded(table.reshape(MY * width * 2, 2 * width * rows_y))


def x_tables(samples, slabs, length):
    theta = angles(signed(MX), np.arange(length), length)
    cosine, sine = np.cos(theta), np.sin(theta)
    forward = np.stack([np.stack([cosine, sine]), np.stack([-sine, cosine])])
    inverse = np.stack([np.stack([cosine, sine]), np.stack([-sine, cosine])]) / length
    same = np.eye(samples)
    rows = MX * 2 * samples

    def lay(turn):
        turn = turn.reshape(2, 2, MX, slabs, length // slabs)
        table = np.einsum("arqsx,bd->qabdsxr", turn, same)
        return rounded(table.reshape(rows, samples * length * 2))

    return lay(forward), lay(inverse)


def dot(left, right):
    return jnp.dot(left, right, preferred_element_type=F32)


def doubled_slope(u):
    decay = jnp.exp2(u * u * -math.log2(math.e)).astype(BF16)
    cdf = (1.0 + lax.erf(u)).astype(BF16)
    return cdf + u.astype(BF16) * jnp.asarray(2.0 / math.sqrt(math.pi), BF16) * decay


def over(index, size):
    return lax.shift_right_logical(index, jnp.int32(size.bit_length() - 1))


def within(index, size):
    return jnp.bitwise_and(index, jnp.int32(size - 1))


def fill_z(base, table):
    rows_z, lanes = base.shape
    owner = within(lax.broadcasted_iota(jnp.int32, (rows_z, lanes), 1), GROUP)
    values = base[...]
    for c in range(GROUP):
        table[c * rows_z : (c + 1) * rows_z] = jnp.where(owner == c, values, 0.0).astype(BF16)


def fill_z_back(base, table):
    lanes, rows_z = base.shape
    owner = within(lax.broadcasted_iota(jnp.int32, (lanes, rows_z), 0), GROUP)
    values = base[...]
    for c in range(GROUP):
        first = c % SLOTS * rows_z
        table[c // SLOTS, :, first : first + rows_z] = jnp.where(owner == c, values, 0.0).astype(BF16)


def grouped(lane, per, channels):
    c = within(lane, channels)
    return over(c, GROUP) * (MZ * GROUP) + over(lane, channels) * GROUP + within(c, GROUP)


def fill_order(per, channels, back, table):
    count = table.shape[0]
    row = lax.broadcasted_iota(jnp.int32, (count, count), 0)
    column = lax.broadcasted_iota(jnp.int32, (count, count), 1)
    if back:
        same = grouped(row[:, :1], per, channels) == column
    else:
        same = row == grouped(column[:1], per, channels)
    table[...] = jnp.where(same, 1.0, 0.0).astype(BF16)


def turned_index(index, slabs, devices):
    samples = devices // slabs
    return index % samples * slabs + index // samples


def deliver(spectra, ytab, order, scale, message, per, channels, slabs):
    groups = channels // GROUP
    rows = spectra.shape[0] // groups
    wide = spectra.shape[1] // 2
    halves = []
    for r in range(2):
        blocks = [spectra[g * rows : (g + 1) * rows, r * wide : (r + 1) * wide] for g in range(groups)]
        halves.append(jnp.concatenate(blocks, axis=1).astype(BF16))
    planes = dot(ytab[...], jnp.concatenate(halves, axis=0))
    if scale is not None:
        planes = planes * scale[...]
    ordered = dot(planes.astype(BF16), order[...]).astype(BF16)
    parts = MZ // per
    count = message.shape[1]
    lanes = per * channels
    for part in range(parts):
        block = ordered[:, part * lanes : (part + 1) * lanes]
        for j in range(MY):
            message[turned_index(j * parts + part, slabs, message.shape[0])] = block[j * count : (j + 1) * count]


def receive(message, order_back, ytab_back, scale, held, per, slabs):
    parts = MZ // per
    lanes = [
        jnp.concatenate(
            [message[turned_index(j * parts + part, slabs, message.shape[0])] for j in range(MY)], axis=0
        )
        for part in range(parts)
    ]
    ordered = dot(jnp.concatenate(lanes, axis=1), order_back[...]).astype(BF16)
    lines = dot(ytab_back[...], ordered)
    if scale is not None:
        lines = lines * scale[...]
    lines = lines.astype(BF16)
    rows = lines.shape[0] // 2
    wide = MZ * GROUP
    for group in range(held.shape[0] // rows):
        piece = lines[:, group * wide : (group + 1) * wide]
        held[group * rows : (group + 1) * rows] = jnp.concatenate([piece[:rows], piece[rows:]], axis=1)


class Move:
    def __init__(self, source, target, sems):
        self.source, self.target, self.sems = source, target, sems
        self.groups = target.shape[0] // GROUP

    def copy(self, step, g):
        run = pl.ds(g * GROUP + step * SLOTS, SLOTS)
        sem = self.sems.at[step * self.groups + g]
        return pltpu.make_async_copy(self.source.at[run], self.target.at[run], sem)

    def start(self, step):
        for g in range(self.groups):
            self.copy(step, g).start()

    def wait(self, step):
        for g in range(self.groups):
            self.copy(step, g).wait()


def start_all(moves, step):
    for each in moves:
        each.start(step)


def add_spectra(field, ztab, step, spectra):
    groups = field.shape[0] // GROUP
    rows_z = field.shape[-1]
    depth = SLOTS * rows_z
    table = ztab[pl.ds(pl.multiple_of(step * depth, depth), depth)]
    lanes = [
        jnp.concatenate(
            [field[g * GROUP + step * SLOTS + slot].reshape(-1, rows_z) for g in range(groups)], axis=0
        )
        for slot in range(SLOTS)
    ]
    spectra[...] += dot(jnp.concatenate(lanes, axis=1), table)


def plane_kernel(
    per, channels, slabs, field, base_far, ytab_far, message, ztab, order, spectra, buffer, base, ytab, sems, table_sems
):
    incoming = Move(field.at[0], buffer, sems)
    base_copy = pltpu.make_async_copy(base_far, base, table_sems.at[0])
    ytab_copy = pltpu.make_async_copy(ytab_far, ytab, table_sems.at[1])
    base_copy.start()
    incoming.start(0)
    fill_order(per, channels, False, order)
    spectra[...] = jnp.zeros_like(spectra)
    incoming.start(1)
    base_copy.wait()
    fill_z(base, ztab)
    incoming.start(2)
    ytab_copy.start()
    incoming.start(3)

    @pl.loop(0, STEPS)
    def _(step):
        incoming.wait(step)
        add_spectra(buffer, ztab, step, spectra)

    ytab_copy.wait()
    deliver(spectra, ytab, order, None, message, per, channels, slabs)


def slope_kernel(
    per, channels, slabs, arrived, local, cotangent, base, base_back, ytab, ytab_back, scale, scale_back,
    slope, message, ztab, ztab_back, order, held, spectra, local_in, cotangent_in, result, total,
    local_sems, cotangent_sems, result_sems,
):
    width, rows_y, rows_z = local.shape[1:]
    groups = channels // GROUP
    rows = width * rows_y
    wide = 2 * rows_y
    incoming = (Move(local, local_in, local_sems), Move(cotangent.at[0], cotangent_in, cotangent_sems))
    outgoing = Move(result, slope, result_sems)
    start_all(incoming, 0)
    fill_order(per, channels, True, order)
    receive(arrived, order, ytab_back, scale_back, held, per, slabs)
    start_all(incoming, 1)
    fill_z_back(base_back, ztab_back)
    fill_z(base, ztab)
    start_all(incoming, 2)
    fill_order(per, channels, False, order)
    spectra[...] = jnp.zeros_like(spectra)
    start_all(incoming, 3)

    @pl.loop(0, STEPS)
    def _(step):
        for each in incoming:
            each.wait(step)
        total[...] = dot(held[...], ztab_back[step])
        for g in range(groups):
            for slot in range(SLOTS):
                lanes = slice(slot * rows_z, (slot + 1) * rows_z)
                c = g * GROUP + step * SLOTS + slot
                for x in range(0, width, 2):
                    place = g * rows + x * rows_y
                    value = total[place : place + wide, lanes]
                    value = value + local_in[c, x : x + 2].reshape(wide, rows_z).astype(F32)
                    upstream = cotangent_in[c, x : x + 2].reshape(wide, rows_z)
                    answer = upstream * doubled_slope(value)
                    result[c, x : x + 2] = answer.reshape(2, rows_y, rows_z)
            outgoing.copy(step, g).start()
        add_spectra(result, ztab, step, spectra)

    deliver(spectra, ytab, order, scale, message, per, channels, slabs)
    for step in range(STEPS):
        outgoing.wait(step)


def field_kernel(
    per, channels, slabs, arrived, local, base_back, ytab_back, out, ztab_back, order, held, local_in, result,
    local_sems, result_sems,
):
    width, rows_y, rows_z = local.shape[1:]
    groups = channels // GROUP
    rows = width * rows_y
    incoming = Move(local, local_in, local_sems)
    outgoing = Move(result, out.at[0], result_sems)
    incoming.start(0)
    fill_order(per, channels, True, order)
    incoming.start(1)
    receive(arrived, order, ytab_back, None, held, per, slabs)
    incoming.start(2)
    fill_z_back(base_back, ztab_back)
    incoming.start(3)

    @pl.loop(0, STEPS)
    def _(step):
        incoming.wait(step)
        total = dot(held[...], ztab_back[step])
        for g in range(groups):
            for slot in range(SLOTS):
                lanes = slice(slot * rows_z, (slot + 1) * rows_z)
                c = g * GROUP + step * SLOTS + slot
                value = total[g * rows : (g + 1) * rows, lanes]
                value = value + local_in[c].reshape(rows, rows_z).astype(F32)
                result[c] = value.astype(BF16).reshape(width, rows_y, rows_z)
            outgoing.copy(step, g).start()

    for step in range(STEPS):
        outgoing.wait(step)


def pointwise_kernel(turned, field, mix, offsets, out, table, shift):
    channels = mix.shape[0]
    width, rows_y, rows_z = field.shape[1:]
    size = channels * TILE

    @pl.when(pl.program_id(0) == 0)
    def _():
        row = over(lax.broadcasted_iota(jnp.int32, (size, channels), 0), TILE)
        column = lax.broadcasted_iota(jnp.int32, (size, channels), 1)
        spread = jnp.where(row == column, 1.0, 0.0).astype(BF16)
        tall = lax.dot_general(
            spread, mix[...], (((1,), (1 if turned else 0,)), ((), ())), preferred_element_type=F32
        ).astype(BF16)
        whole = lax.dot_general(
            tall, spread, (((1,), (1,)), ((), ())), preferred_element_type=F32
        )
        place = within(lax.broadcasted_iota(jnp.int32, (size, size), 0), TILE)
        other = within(lax.broadcasted_iota(jnp.int32, (size, size), 1), TILE)
        table[...] = jnp.where(place == other, whole if turned else 0.5 * whole, 0.0).astype(BF16)
        if offsets is not None:
            for c in range(channels):
                shift[c] = jnp.full((1, rows_z), offsets[c], F32)

    for start in range(0, rows_y, 2 * TILE):
        pieces = [field[:, x, start : start + 2 * TILE, :].astype(F32) for x in range(width)]
        halves = []
        for row in range(0, 2 * TILE, TILE):
            rows = [piece[:, row : row + TILE].reshape(size, rows_z).astype(BF16) for piece in pieces]
            halves.append(dot(table[...], jnp.concatenate(rows, axis=1)))
        for x in range(width):
            values = [
                half[:, x * rows_z : (x + 1) * rows_z].reshape(channels, TILE, rows_z) for half in halves
            ]
            value = jnp.concatenate(values, axis=1)
            if offsets is not None:
                value = (value + shift[...]) * math.sqrt(0.5)
            out[:, x, start : start + 2 * TILE, :] = value.astype(BF16)


def spread_pair(first, second):
    nothing = jnp.zeros_like(first)
    upper = jnp.concatenate([first, nothing], axis=1)
    lower = jnp.concatenate([nothing, second], axis=1)
    return jnp.concatenate([upper, lower], axis=0)


def low_half(shape):
    return lax.broadcasted_iota(jnp.int32, shape, 1) < shape[1] // 2


def mix_kernel(per, samples, arrived, weights, line, line_back, spec_in, message, held):
    rows = 2 * samples
    lanes = 2 * weights.shape[1]
    low = low_half((samples, lanes))
    flat = arrived[...].reshape(-1, arrived.shape[2])
    spectra = dot(line[...], flat).astype(BF16)
    spec_in[...] = spectra
    for q in range(MX):
        for first in range(0, per, 2):
            block = spread_pair(weights[first * MX + q], weights[(first + 1) * MX + q])
            place = first // 2 * lanes
            terms = dot(spectra[q * rows : (q + 1) * rows, place : place + lanes], block)
            mixed = []
            for side in range(2):
                part = terms[:, side * lanes : (side + 1) * lanes]
                turned = pltpu.roll(part[samples:], lanes // 2, 1)
                mixed.append(part[:samples] + jnp.where(low, -turned, turned))
            real = jnp.where(low, mixed[0], pltpu.roll(mixed[1], lanes // 2, 1))
            imag = jnp.where(low, pltpu.roll(mixed[0], lanes // 2, 1), mixed[1])
            held[q * rows : (q + 1) * rows, place : place + lanes] = jnp.concatenate(
                [real, imag], axis=0
            ).astype(BF16)
    message[...] = dot(line_back[...], held[...]).astype(BF16).reshape(message.shape)


def turn_kernel(per, weights, turned):
    for q in range(MX):
        for first in range(0, per, 2):
            pair = [weights[first * MX + q], weights[(first + 1) * MX + q]]
            turned[q * (per // 2) + first // 2] = jnp.concatenate(pair, axis=0).T


def mix_back_kernel(per, samples, arrived, turned, line, line_back, pairs, message, held):
    rows = 2 * samples
    lanes = turned.shape[1]
    first_lanes = low_half(turned.shape[1:])
    low = low_half((samples, lanes))
    flat = arrived[...].reshape(-1, arrived.shape[2])
    spectra = dot(line[...], flat).astype(BF16).astype(F32)
    for q in range(MX):
        for first in range(0, per, 2):
            both = turned[q * (per // 2) + first // 2].astype(F32)
            block = jnp.concatenate(
                [jnp.where(first_lanes, both, 0.0), jnp.where(first_lanes, 0.0, both)], axis=0
            ).astype(BF16)
            place = first // 2 * lanes
            real = spectra[q * rows : q * rows + samples, place : place + lanes]
            imag = spectra[q * rows + samples : (q + 1) * rows, place : place + lanes]
            real_turned = pltpu.roll(real, lanes // 2, 1)
            imag_turned = pltpu.roll(imag, lanes // 2, 1)
            left = [jnp.where(low, real, imag_turned), jnp.where(low, imag, -real_turned)]
            right = [jnp.where(low, real_turned, imag), jnp.where(low, imag_turned, -real)]
            pair = jnp.concatenate(
                [jnp.concatenate(left, axis=0), jnp.concatenate(right, axis=0)], axis=1
            ).astype(BF16)
            pairs[q * rows : (q + 1) * rows, 2 * place : 2 * (place + lanes)] = pair
            held[q * rows : (q + 1) * rows, place : place + lanes] = dot(pair, block).astype(BF16)
    message[...] = dot(line_back[...], held[...]).astype(BF16).reshape(message.shape)


def weight_kernel(per, samples, spec_in, pairs, out):
    rows = 2 * samples
    lanes = out.shape[2]
    half = lanes // 2
    for q in range(MX):
        for first in range(0, per, 2):
            place = first // 2 * lanes
            left = spec_in[q * rows : (q + 1) * rows, place : place + lanes]
            right = pairs[q * rows : (q + 1) * rows, 2 * place : 2 * (place + lanes)]
            outer = lax.dot_general(
                left, right, (((0,), (0,)), ((), ())), preferred_element_type=F32
            )
            out[first * MX + q] = outer[:half, :lanes]
            out[(first + 1) * MX + q] = outer[half:, lanes:]


def whole(array):
    return pl.BlockSpec(array.shape, lambda *step: (0,) * len(array.shape))


def shaped(shape, dtype):
    return jax.ShapeDtypeStruct(shape, dtype)


def params(mib):
    return pltpu.CompilerParams(vmem_limit_bytes=mib * MIB)


def cost(flops, moved, steep=0):
    return pl.CostEstimate(flops=flops, bytes_accessed=moved, transcendentals=steep)


def body(mesh_axes, devices, slabs, activations, cotangent, mode_weights, pointwise, offsets):
    _, channels, width, rows_y, rows_z = activations.shape
    samples = devices // slabs
    per = MY * MZ // devices
    groups = channels // GROUP
    field = activations.shape[1:]
    count = math.prod(field)
    base = z_base(rows_z)
    ytab = y_table(rows_y, width)
    line_fwd, line_inv = x_tables(samples, slabs, NX)
    weight = np.where(np.arange(MZ) == 0, 1.0, 2.0) / (rows_y * rows_z)
    scale = np.tile(np.repeat(weight, GROUP), groups)[None]
    scale, scale_t = (0.5 * scale).astype(np.float32), (math.sqrt(0.5) * scale).astype(np.float32)
    base_t, ytab_t = (np.ascontiguousarray(t.T) for t in (base, ytab))
    fwd_t, inv_t = (np.ascontiguousarray(t.T) for t in (line_fwd, line_inv))
    message = shaped((devices, 2 * width, per * channels), BF16)
    spectra = shaped((MX * 2 * samples, per * channels), BF16)
    ztab = pltpu.VMEM((GROUP * rows_z, 2 * MZ * GROUP), BF16)
    ztab_t = pltpu.VMEM((STEPS, 2 * MZ * GROUP, SLOTS * rows_z), BF16)
    order = pltpu.VMEM((MZ * channels, MZ * channels), BF16)
    rows = groups * width * rows_y
    held = pltpu.VMEM((rows, 2 * MZ * GROUP), BF16)
    sums = pltpu.VMEM((rows, 2 * MZ * GROUP), F32)
    slot_sums = pltpu.VMEM((rows, SLOTS * rows_z), F32)
    buffer = pltpu.VMEM(field, BF16)
    sems = pltpu.SemaphoreType.DMA((STEPS * groups,))
    far = pl.BlockSpec(memory_space=pltpu.HBM)
    far_field = pltpu.HBM(field, BF16)

    def kept_far(array):
        return pltpu.with_memory_space_constraint(array, pltpu.HBM)

    plane_flops = 2 * count * 2 * MZ * GROUP

    def exchange(array):
        return lax.all_to_all(array, mesh_axes, split_axis=0, concat_axis=0, tiled=True)

    def mix_points(values, turned, shifts):
        step = 2
        block = pl.BlockSpec((channels, step, rows_y, rows_z), lambda x: (0, x, 0, 0))
        kernel = functools.partial(pointwise_kernel, turned)
        specs = [block, whole(pointwise)]
        operands = [values, pointwise]
        if shifts is None:
            run = lambda a, b, *rest: kernel(a, b, None, *rest)
        else:
            run = kernel
            specs.append(pl.BlockSpec(memory_space=pltpu.SMEM))
            operands.append(shifts)
        return pl.pallas_call(
            run,
            grid=(width // step,),
            in_specs=specs,
            out_specs=block,
            out_shape=far_field,
            scratch_shapes=[
                pltpu.VMEM((channels * TILE, channels * TILE), BF16),
                pltpu.VMEM((channels, 1, rows_z), F32),
            ],
            compiler_params=params(32),
            cost_estimate=cost(2 * count * channels * TILE, 4 * count),
        )(*operands)

    planes = pl.pallas_call(
        functools.partial(plane_kernel, per, channels, slabs),
        in_specs=[far, far, far],
        out_specs=whole(message),
        out_shape=message,
        scratch_shapes=[
            ztab,
            order,
            sums,
            buffer,
            pltpu.VMEM(base.shape, F32),
            pltpu.VMEM(ytab.shape, BF16),
            sems,
            pltpu.SemaphoreType.DMA((2,)),
        ],
        compiler_params=params(32),
        cost_estimate=cost(plane_flops, 2 * count),
    )(kept_far(activations), kept_far(base), kept_far(ytab))
    arrived = exchange(planes)
    local = mix_points(kept_far(activations.reshape(field)), True, offsets)
    turned = pl.pallas_call(
        functools.partial(turn_kernel, per),
        out_shape=shaped((MX * per // 2, 2 * channels, 2 * channels), BF16),
        compiler_params=params(16),
        cost_estimate=cost(0, 4 * mode_weights.size),
    )(mode_weights)
    arrived, local, turned = lax.optimization_barrier((arrived, local, turned))
    spec_in, mixed = pl.pallas_call(
        functools.partial(mix_kernel, per, samples),
        out_shape=(spectra, message),
        scratch_shapes=[pltpu.VMEM(spectra.shape, BF16)],
        compiler_params=params(16),
        cost_estimate=cost(10**8, 2 * mode_weights.size),
    )(arrived, mode_weights, line_fwd, inv_t)
    returned = exchange(mixed)
    slope, back_plane = pl.pallas_call(
        functools.partial(slope_kernel, per, channels, slabs),
        in_specs=[whole(message), far, far]
        + [whole(t) for t in (base, base_t, ytab, ytab_t, scale, scale_t)],
        out_specs=(far, whole(message)),
        out_shape=(far_field, message),
        scratch_shapes=[ztab, ztab_t, order, held, sums]
        + [buffer] * 3
        + [slot_sums]
        + [sems] * 3,
        compiler_params=params(40),
        cost_estimate=cost(2 * plane_flops, 6 * count, 2 * count),
    )(returned, kept_far(local), kept_far(cotangent), base, base_t, ytab, ytab_t, scale, scale_t)
    arrived_back = exchange(back_plane)
    local_back = mix_points(kept_far(slope), False, None)
    arrived_back, local_back = lax.optimization_barrier((arrived_back, local_back))
    pairs, mixed_back = pl.pallas_call(
        functools.partial(mix_back_kernel, per, samples),
        out_shape=(shaped((spectra.shape[0], 2 * spectra.shape[1]), BF16), message),
        scratch_shapes=[pltpu.VMEM(spectra.shape, BF16)],
        compiler_params=params(16),
        cost_estimate=cost(10**8, 2 * mode_weights.size),
    )(arrived_back, turned, line_inv, fwd_t)
    returned_back = exchange(mixed_back)
    grad_spectral = pl.pallas_call(
        functools.partial(weight_kernel, per, samples),
        out_shape=shaped(mode_weights.shape, F32),
        compiler_params=params(16),
        cost_estimate=cost(10**8, 4 * mode_weights.size),
    )(spec_in, pairs)
    grad_in = pl.pallas_call(
        functools.partial(field_kernel, per, channels, slabs),
        in_specs=[whole(message), far, whole(base_t), whole(ytab_t)],
        out_specs=far,
        out_shape=shaped(activations.shape, BF16),
        scratch_shapes=[ztab_t, order, held, buffer, buffer, sems, sems],
        compiler_params=params(32),
        cost_estimate=cost(plane_flops, 4 * count),
    )(returned_back, kept_far(local_back), base_t, ytab_t)
    return (grad_in, grad_spectral)


def chosen_body(mesh_axes, devices, slabs, activations, cotangent, mode_weights, pointwise, offsets):
    samples, channels, width, rows_y, rows_z = activations.shape
    per = MY * MZ // devices
    fits = (
        samples == 1
        and MY * MZ % devices == 0
        and per in (2, 4, 8)
        and width % 8 == 0
        and channels == 64
        and rows_y % TILE == 0
        and rows_z == 128
    )
    plan = functools.partial(body, mesh_axes, devices, slabs) if fits else general_body
    return plan(activations, cotangent, mode_weights, pointwise, offsets)


def solution(mesh):
    slabs = mesh.shape["space"]
    devices = slabs * mesh.shape["dp"]
    return jax.shard_map(
        functools.partial(chosen_body, ("dp", "space"), devices, slabs),
        mesh=mesh,
        in_specs=(
            P("dp", None, "space", None, None),
            P("dp", None, "space", None, None),
            P(("space", "dp"), None, None),
            P(),
            P(),
        ),
        out_specs=(P("dp", None, "space", None, None), P(("space", "dp"), None, None)),
        check_vma=False,
    )
```

```python
import functools
import math

import jax
import jax.numpy as jnp
import ml_dtypes
import numpy as np
from jax import lax
from jax.experimental import pallas as pl
from jax.experimental.pallas import tpu as pltpu
from jax.sharding import PartitionSpec as P

MX = 16
MY = 16
MZ = 8
NX = 32


def centered(count):
    index = jnp.arange(count, dtype=jnp.int32)
    return jnp.where(index < count // 2, index, index - count)


def plane_tables(rows_y, rows_z, modes_y, modes_z):
    along_y = jnp.arange(rows_y, dtype=jnp.int32)[:, None, None, None]
    along_z = jnp.arange(rows_z, dtype=jnp.int32)[None, :, None, None]
    freq_y = centered(modes_y)[None, None, :, None]
    freq_z = jnp.arange(modes_z, dtype=jnp.int32)[None, None, None, :]
    phase = jnp.mod(freq_y * along_y * rows_z + freq_z * along_z * rows_y, rows_y * rows_z)
    theta = phase.astype(jnp.float32) * (2.0 * math.pi / (rows_y * rows_z))
    cosine = jnp.cos(theta)
    sine = jnp.sin(theta)
    forward = jnp.stack([cosine, -sine], -1).reshape(rows_y * rows_z, modes_y * modes_z * 2)
    scaled = jnp.where(freq_z == 0, 1.0, 2.0).astype(jnp.float32) / (rows_y * rows_z)
    inverse = (
        jnp.stack([cosine * scaled, -sine * scaled], -1)
        .reshape(rows_y * rows_z, modes_y * modes_z * 2)
        .T
    )
    return (forward.astype(jnp.bfloat16), inverse.astype(jnp.bfloat16))


def line_tables(length, modes):
    along = jnp.arange(length, dtype=jnp.int32)[:, None]
    freq = centered(modes)[None, :]
    phase = jnp.mod(freq * along, length)
    theta = phase.astype(jnp.float32) * (2.0 * math.pi / length)
    cosine = jnp.cos(theta)
    sine = jnp.sin(theta)
    first = jnp.stack([cosine, -sine], -1)
    second = jnp.stack([sine, cosine], -1)
    forward = jnp.stack([first, second], 1).reshape(2 * length, 2 * modes)
    inv_first = jnp.stack([cosine.T, sine.T], -1) / length
    inv_second = jnp.stack([-sine.T, cosine.T], -1) / length
    inverse = jnp.stack([inv_first, inv_second], 1).reshape(2 * modes, 2 * length)
    return (forward.astype(jnp.bfloat16), inverse.astype(jnp.bfloat16))


def expand_weights(weights):
    half = weights.shape[1]
    real_part = weights[:, :, :half]
    imag_part = weights[:, :, half:]
    upper = jnp.concatenate([real_part, imag_part], axis=2)
    lower = jnp.concatenate([-imag_part, real_part], axis=2)
    return jnp.concatenate([upper, lower], axis=1)


def outer_sum(left, right):
    return jnp.einsum("mbi,mbo->mio", left, right, preferred_element_type=jnp.float32)


def weight_terms(spec_in, spec_grad):
    half = spec_in.shape[2] // 2
    in_real = spec_in[:, :, :half]
    in_imag = spec_in[:, :, half:]
    gr_real = spec_grad[:, :, :half]
    gr_imag = spec_grad[:, :, half:]
    real_term = outer_sum(in_real, gr_real) + outer_sum(in_imag, gr_imag)
    imag_term = outer_sum(in_real, gr_imag) - outer_sum(in_imag, gr_real)
    return jnp.concatenate([real_term, imag_term], axis=2)


def to_modes(slab, table, modes_x):
    samples, channels, width, pairs = slab.shape
    moved = lax.all_to_all(slab, "space", split_axis=3, concat_axis=2, tiled=True)
    length = moved.shape[2]
    local = moved.shape[3] // 2
    lines = moved.reshape(samples, channels, length, local, 2).transpose(0, 1, 3, 2, 4)
    lines = lines.reshape(samples, channels, local, 2 * length)
    spectra = jnp.dot(lines, table, preferred_element_type=jnp.float32).astype(jnp.bfloat16)
    spectra = spectra.reshape(samples, channels, local, modes_x, 2).transpose(2, 3, 0, 4, 1)
    return spectra.reshape(local * modes_x, samples, 2 * channels)


def to_slab(spectra, table, modes_x, channels):
    count, samples, doubled = spectra.shape
    local = count // modes_x
    lines = spectra.reshape(local, modes_x, samples, 2, channels).transpose(2, 4, 0, 1, 3)
    lines = lines.reshape(samples, channels, local, 2 * modes_x)
    lines = jnp.dot(lines, table, preferred_element_type=jnp.float32).astype(jnp.bfloat16)
    length = lines.shape[3] // 2
    lines = lines.reshape(samples, channels, local, length, 2).transpose(0, 1, 3, 2, 4)
    lines = lines.reshape(samples, channels, length, 2 * local)
    return lax.all_to_all(lines, "space", split_axis=2, concat_axis=3, tiled=True)


def to_owners(spectra):
    return lax.all_to_all(spectra, "dp", split_axis=0, concat_axis=1, tiled=True)


def from_owners(spectra):
    return lax.all_to_all(spectra, "dp", split_axis=1, concat_axis=0, tiled=True)


def gelu_slope(value):
    cdf = 0.5 * (1.0 + lax.erf(value * 0.7071067811865476))
    density = jnp.exp(-0.5 * value * value) * 0.3989422804014327
    return cdf + value * density


def general_body(activations, cotangent, mode_weights, pointwise, offsets):
    samples, channels, width, rows_y, rows_z = activations.shape
    plane_fwd, plane_inv = plane_tables(rows_y, rows_z, MY, MZ)
    line_fwd, line_inv = line_tables(NX, MX)
    flat = activations.reshape(samples, channels, width, rows_y * rows_z)
    planes = jnp.dot(flat, plane_fwd, preferred_element_type=jnp.float32).astype(jnp.bfloat16)
    spec_in = to_modes(planes, line_fwd, MX)
    blocks = expand_weights(mode_weights)
    held_in = to_owners(spec_in)
    held_out = jnp.einsum(
        "mbi,mio->mbo", held_in, blocks, preferred_element_type=jnp.float32
    ).astype(jnp.bfloat16)
    spec_out = from_owners(held_out)
    returned = to_slab(spec_out, line_inv, MX, channels)
    spectral = jnp.dot(returned, plane_inv, preferred_element_type=jnp.float32)
    local_part = jnp.einsum("io,bixn->boxn", pointwise, flat, preferred_element_type=jnp.float32)
    summed = spectral + local_part + offsets[None, :, None, None]
    upstream = cotangent.reshape(flat.shape).astype(jnp.float32)
    slope_grad = (upstream * gelu_slope(summed)).astype(jnp.bfloat16)
    back_plane = jnp.dot(slope_grad, plane_inv.T, preferred_element_type=jnp.float32).astype(
        jnp.bfloat16
    )
    spec_grad = to_modes(back_plane, line_inv.T, MX)
    held_grad = to_owners(spec_grad)
    held_dx = jnp.einsum(
        "mbo,mio->mbi", held_grad, blocks, preferred_element_type=jnp.float32
    ).astype(jnp.bfloat16)
    spec_dx = from_owners(held_dx)
    grad_spectral = weight_terms(held_in, held_grad)
    line_dx = to_slab(spec_dx, line_fwd.T, MX, channels)
    total = jnp.dot(line_dx, plane_fwd.T, preferred_element_type=jnp.float32)
    total = total + jnp.einsum(
        "io,boxn->bixn", pointwise, slope_grad, preferred_element_type=jnp.float32
    )
    grad_in = total.astype(jnp.bfloat16).reshape(activations.shape)
    return (grad_in, grad_spectral)


BF16 = jnp.bfloat16
F32 = jnp.float32
GROUP = 16
TILE = 8
SLOTS = 4
STEPS = GROUP // SLOTS
MIB = 1024 * 1024


def rounded(table):
    return np.asarray(table, np.float32).astype(ml_dtypes.bfloat16)


def angles(freq, points, length):
    phase = np.mod(np.outer(freq, points), length)
    return (phase * (2.0 * math.pi / length)).astype(np.float64)


def signed(count):
    index = np.arange(count)
    return np.where(index < count // 2, index, index - count)


def z_base(rows_z):
    theta = angles(np.arange(MZ), np.arange(rows_z), rows_z)
    pair = np.stack([np.cos(theta), -np.sin(theta)])
    table = np.repeat(pair.reshape(2 * MZ, rows_z), GROUP, axis=0).T
    return rounded(table).astype(np.float32)


def y_table(rows_y, width):
    theta = angles(signed(MY), np.arange(rows_y), rows_y)
    cosine, sine = np.cos(theta), np.sin(theta)
    turn = np.stack([np.stack([cosine, sine]), np.stack([-sine, cosine])])
    table = np.einsum("rsjy,xw->jxrswy", turn, np.eye(width))
    return rounded(table.reshape(MY * width * 2, 2 * width * rows_y))


def x_tables(samples, slabs, length):
    theta = angles(signed(MX), np.arange(length), length)
    cosine, sine = np.cos(theta), np.sin(theta)
    forward = np.stack([np.stack([cosine, sine]), np.stack([-sine, cosine])])
    inverse = np.stack([np.stack([cosine, sine]), np.stack([-sine, cosine])]) / length
    same = np.eye(samples)
    rows = MX * 2 * samples

    def lay(turn):
        turn = turn.reshape(2, 2, MX, slabs, length // slabs)
        table = np.einsum("arqsx,bd->qabdsxr", turn, same)
        return rounded(table.reshape(rows, samples * length * 2))

    return lay(forward), lay(inverse)


def dot(left, right):
    return jnp.dot(left, right, preferred_element_type=F32)


def doubled_slope(u):
    decay = jnp.exp(-(u * u)).astype(BF16)
    cdf = (1.0 + lax.erf(u)).astype(BF16)
    return cdf + u.astype(BF16) * jnp.asarray(2.0 / math.sqrt(math.pi), BF16) * decay


def over(index, size):
    return lax.shift_right_logical(index, jnp.int32(size.bit_length() - 1))


def within(index, size):
    return jnp.bitwise_and(index, jnp.int32(size - 1))


def fill_z(base, table):
    rows_z, lanes = base.shape
    owner = within(lax.broadcasted_iota(jnp.int32, (rows_z, lanes), 1), GROUP)
    values = base[...]
    for c in range(GROUP):
        table[c * rows_z : (c + 1) * rows_z] = jnp.where(owner == c, values, 0.0).astype(BF16)


def fill_z_back(base, table):
    lanes, rows_z = base.shape
    owner = within(lax.broadcasted_iota(jnp.int32, (lanes, rows_z), 0), GROUP)
    values = base[...]
    for c in range(GROUP):
        first = c % SLOTS * rows_z
        table[c // SLOTS, :, first : first + rows_z] = jnp.where(owner == c, values, 0.0).astype(BF16)


def grouped(lane, per, channels):
    c = within(lane, channels)
    return over(c, GROUP) * (MZ * GROUP) + over(lane, channels) * GROUP + within(c, GROUP)


def fill_order(per, channels, back, table):
    count = table.shape[0]
    row = lax.broadcasted_iota(jnp.int32, (count, count), 0)
    column = lax.broadcasted_iota(jnp.int32, (count, count), 1)
    if back:
        same = grouped(row[:, :1], per, channels) == column
    else:
        same = row == grouped(column[:1], per, channels)
    table[...] = jnp.where(same, 1.0, 0.0).astype(BF16)


def turned_index(index, slabs, devices):
    samples = devices // slabs
    return index % samples * slabs + index // samples


def deliver(spectra, ytab, order, scale, message, per, channels, slabs):
    groups = channels // GROUP
    rows = spectra.shape[0] // groups
    wide = spectra.shape[1] // 2
    halves = []
    for r in range(2):
        blocks = [spectra[g * rows : (g + 1) * rows, r * wide : (r + 1) * wide] for g in range(groups)]
        halves.append(jnp.concatenate(blocks, axis=1).astype(BF16))
    planes = dot(ytab[...], jnp.concatenate(halves, axis=0))
    if scale is not None:
        planes = planes * scale[...]
    ordered = dot(planes.astype(BF16), order[...]).astype(BF16)
    parts = MZ // per
    count = message.shape[1]
    lanes = per * channels
    for part in range(parts):
        block = ordered[:, part * lanes : (part + 1) * lanes]
        for j in range(MY):
            message[turned_index(j * parts + part, slabs, message.shape[0])] = block[j * count : (j + 1) * count]


def receive(message, order_back, ytab_back, scale, held, per, slabs):
    parts = MZ // per
    lanes = [
        jnp.concatenate(
            [message[turned_index(j * parts + part, slabs, message.shape[0])] for j in range(MY)], axis=0
        )
        for part in range(parts)
    ]
    ordered = dot(jnp.concatenate(lanes, axis=1), order_back[...]).astype(BF16)
    lines = dot(ytab_back[...], ordered)
    if scale is not None:
        lines = lines * scale[...]
    lines = lines.astype(BF16)
    rows = lines.shape[0] // 2
    wide = MZ * GROUP
    for group in range(held.shape[0] // rows):
        piece = lines[:, group * wide : (group + 1) * wide]
        held[group * rows : (group + 1) * rows] = jnp.concatenate([piece[:rows], piece[rows:]], axis=1)


class Move:
    def __init__(self, source, target, sems):
        self.source, self.target, self.sems = source, target, sems
        self.groups = target.shape[0] // GROUP

    def copy(self, step, g):
        run = pl.ds(g * GROUP + step * SLOTS, SLOTS)
        sem = self.sems.at[step * self.groups + g]
        return pltpu.make_async_copy(self.source.at[run], self.target.at[run], sem)

    def start(self, step):
        for g in range(self.groups):
            self.copy(step, g).start()

    def wait(self, step):
        for g in range(self.groups):
            self.copy(step, g).wait()


def start_all(moves, step):
    for each in moves:
        each.start(step)


def add_spectra(field, ztab, step, spectra):
    groups = field.shape[0] // GROUP
    rows_z = field.shape[-1]
    depth = SLOTS * rows_z
    table = ztab[pl.ds(pl.multiple_of(step * depth, depth), depth)]
    lanes = [
        jnp.concatenate(
            [field[g * GROUP + step * SLOTS + slot].reshape(-1, rows_z) for g in range(groups)], axis=0
        )
        for slot in range(SLOTS)
    ]
    spectra[...] += dot(jnp.concatenate(lanes, axis=1), table)


def plane_kernel(
    per, channels, slabs, field, base_far, ytab_far, message, ztab, order, spectra, buffer, base, ytab, sems, table_sems
):
    incoming = Move(field.at[0], buffer, sems)
    base_copy = pltpu.make_async_copy(base_far, base, table_sems.at[0])
    ytab_copy = pltpu.make_async_copy(ytab_far, ytab, table_sems.at[1])
    base_copy.start()
    incoming.start(0)
    fill_order(per, channels, False, order)
    spectra[...] = jnp.zeros_like(spectra)
    incoming.start(1)
    base_copy.wait()
    fill_z(base, ztab)
    incoming.start(2)
    ytab_copy.start()
    incoming.start(3)

    @pl.loop(0, STEPS)
    def _(step):
        incoming.wait(step)
        add_spectra(buffer, ztab, step, spectra)

    ytab_copy.wait()
    deliver(spectra, ytab, order, None, message, per, channels, slabs)


def slope_kernel(
    per, channels, slabs, arrived, local, cotangent, base, base_back, ytab, ytab_back, scale, scale_back,
    slope, message, ztab, ztab_back, order, held, spectra, local_in, cotangent_in, result, total,
    local_sems, cotangent_sems, result_sems,
):
    width, rows_y, rows_z = local.shape[1:]
    groups = channels // GROUP
    rows = width * rows_y
    wide = 2 * rows_y
    incoming = (Move(local, local_in, local_sems), Move(cotangent.at[0], cotangent_in, cotangent_sems))
    outgoing = Move(result, slope, result_sems)
    start_all(incoming, 0)
    fill_order(per, channels, True, order)
    receive(arrived, order, ytab_back, scale_back, held, per, slabs)
    start_all(incoming, 1)
    fill_z_back(base_back, ztab_back)
    fill_z(base, ztab)
    start_all(incoming, 2)
    fill_order(per, channels, False, order)
    spectra[...] = jnp.zeros_like(spectra)
    start_all(incoming, 3)

    @pl.loop(0, STEPS)
    def _(step):
        for each in incoming:
            each.wait(step)
        total[...] = dot(held[...], ztab_back[step])
        for g in range(groups):
            for slot in range(SLOTS):
                lanes = slice(slot * rows_z, (slot + 1) * rows_z)
                c = g * GROUP + step * SLOTS + slot
                for x in range(0, width, 2):
                    place = g * rows + x * rows_y
                    value = total[place : place + wide, lanes]
                    value = value + local_in[c, x : x + 2].reshape(wide, rows_z).astype(F32)
                    upstream = cotangent_in[c, x : x + 2].reshape(wide, rows_z)
                    answer = upstream * doubled_slope(value)
                    result[c, x : x + 2] = answer.reshape(2, rows_y, rows_z)
            outgoing.copy(step, g).start()
        add_spectra(result, ztab, step, spectra)

    deliver(spectra, ytab, order, scale, message, per, channels, slabs)
    for step in range(STEPS):
        outgoing.wait(step)


def field_kernel(
    per, channels, slabs, arrived, local, base_back, ytab_back, out, ztab_back, order, held, local_in, result,
    local_sems, result_sems,
):
    width, rows_y, rows_z = local.shape[1:]
    groups = channels // GROUP
    rows = width * rows_y
    incoming = Move(local, local_in, local_sems)
    outgoing = Move(result, out.at[0], result_sems)
    incoming.start(0)
    fill_order(per, channels, True, order)
    incoming.start(1)
    receive(arrived, order, ytab_back, None, held, per, slabs)
    incoming.start(2)
    fill_z_back(base_back, ztab_back)
    incoming.start(3)

    @pl.loop(0, STEPS)
    def _(step):
        incoming.wait(step)
        total = dot(held[...], ztab_back[step])
        for g in range(groups):
            for slot in range(SLOTS):
                lanes = slice(slot * rows_z, (slot + 1) * rows_z)
                c = g * GROUP + step * SLOTS + slot
                value = total[g * rows : (g + 1) * rows, lanes]
                value = value + local_in[c].reshape(rows, rows_z).astype(F32)
                result[c] = value.astype(BF16).reshape(width, rows_y, rows_z)
            outgoing.copy(step, g).start()

    for step in range(STEPS):
        outgoing.wait(step)


def pointwise_kernel(turned, field, mix, offsets, out, table, shift):
    channels = mix.shape[0]
    width, rows_y, rows_z = field.shape[1:]
    size = channels * TILE

    @pl.when(pl.program_id(0) == 0)
    def _():
        row = over(lax.broadcasted_iota(jnp.int32, (size, channels), 0), TILE)
        column = lax.broadcasted_iota(jnp.int32, (size, channels), 1)
        spread = jnp.where(row == column, 1.0, 0.0).astype(BF16)
        tall = lax.dot_general(
            spread, mix[...], (((1,), (1 if turned else 0,)), ((), ())), preferred_element_type=F32
        ).astype(BF16)
        whole = lax.dot_general(
            tall, spread, (((1,), (1,)), ((), ())), preferred_element_type=F32
        )
        place = within(lax.broadcasted_iota(jnp.int32, (size, size), 0), TILE)
        other = within(lax.broadcasted_iota(jnp.int32, (size, size), 1), TILE)
        table[...] = jnp.where(place == other, whole if turned else 0.5 * whole, 0.0).astype(BF16)
        if offsets is not None:
            for c in range(channels):
                shift[c] = jnp.full((1, rows_z), offsets[c], F32)

    for start in range(0, rows_y, 2 * TILE):
        pieces = [field[:, x, start : start + 2 * TILE, :].astype(F32) for x in range(width)]
        halves = []
        for row in range(0, 2 * TILE, TILE):
            rows = [piece[:, row : row + TILE].reshape(size, rows_z).astype(BF16) for piece in pieces]
            halves.append(dot(table[...], jnp.concatenate(rows, axis=1)))
        for x in range(width):
            values = [
                half[:, x * rows_z : (x + 1) * rows_z].reshape(channels, TILE, rows_z) for half in halves
            ]
            value = jnp.concatenate(values, axis=1)
            if offsets is not None:
                value = (value + shift[...]) * math.sqrt(0.5)
            out[:, x, start : start + 2 * TILE, :] = value.astype(BF16)


def spread_pair(first, second):
    nothing = jnp.zeros_like(first)
    upper = jnp.concatenate([first, nothing], axis=1)
    lower = jnp.concatenate([nothing, second], axis=1)
    return jnp.concatenate([upper, lower], axis=0)


def low_half(shape):
    return lax.broadcasted_iota(jnp.int32, shape, 1) < shape[1] // 2


def mix_kernel(per, samples, arrived, weights, line, line_back, spec_in, message, held):
    rows = 2 * samples
    lanes = 2 * weights.shape[1]
    low = low_half((samples, lanes))
    flat = arrived[...].reshape(-1, arrived.shape[2])
    spectra = dot(line[...], flat).astype(BF16)
    spec_in[...] = spectra
    for q in range(MX):
        for first in range(0, per, 2):
            block = spread_pair(weights[first * MX + q], weights[(first + 1) * MX + q])
            place = first // 2 * lanes
            terms = dot(spectra[q * rows : (q + 1) * rows, place : place + lanes], block)
            mixed = []
            for side in range(2):
                part = terms[:, side * lanes : (side + 1) * lanes]
                turned = pltpu.roll(part[samples:], lanes // 2, 1)
                mixed.append(part[:samples] + jnp.where(low, -turned, turned))
            real = jnp.where(low, mixed[0], pltpu.roll(mixed[1], lanes // 2, 1))
            imag = jnp.where(low, pltpu.roll(mixed[0], lanes // 2, 1), mixed[1])
            held[q * rows : (q + 1) * rows, place : place + lanes] = jnp.concatenate(
                [real, imag], axis=0
            ).astype(BF16)
    message[...] = dot(line_back[...], held[...]).astype(BF16).reshape(message.shape)


def mix_back_kernel(per, samples, arrived, weights, line, line_back, pairs, message, held):
    rows = 2 * samples
    lanes = 2 * weights.shape[1]
    low = low_half((samples, lanes))
    flat = arrived[...].reshape(-1, arrived.shape[2])
    spectra = dot(line[...], flat).astype(BF16).astype(F32)
    for q in range(MX):
        for first in range(0, per, 2):
            block = spread_pair(weights[first * MX + q], weights[(first + 1) * MX + q])
            place = first // 2 * lanes
            real = spectra[q * rows : q * rows + samples, place : place + lanes]
            imag = spectra[q * rows + samples : (q + 1) * rows, place : place + lanes]
            real_turned = pltpu.roll(real, lanes // 2, 1)
            imag_turned = pltpu.roll(imag, lanes // 2, 1)
            left = [jnp.where(low, real, imag_turned), jnp.where(low, imag, -real_turned)]
            right = [jnp.where(low, real_turned, imag), jnp.where(low, imag_turned, -real)]
            pair = jnp.concatenate(
                [jnp.concatenate(left, axis=0), jnp.concatenate(right, axis=0)], axis=1
            ).astype(BF16)
            pairs[q * rows : (q + 1) * rows, 2 * place : 2 * (place + lanes)] = pair
            held[q * rows : (q + 1) * rows, place : place + lanes] = lax.dot_general(
                pair, block, (((1,), (1,)), ((), ())), preferred_element_type=F32
            ).astype(BF16)
    message[...] = dot(line_back[...], held[...]).astype(BF16).reshape(message.shape)


def weight_kernel(per, samples, spec_in, pairs, out):
    rows = 2 * samples
    lanes = out.shape[2]
    half = lanes // 2
    for q in range(MX):
        for first in range(0, per, 2):
            place = first // 2 * lanes
            left = spec_in[q * rows : (q + 1) * rows, place : place + lanes]
            right = pairs[q * rows : (q + 1) * rows, 2 * place : 2 * (place + lanes)]
            outer = lax.dot_general(
                left, right, (((0,), (0,)), ((), ())), preferred_element_type=F32
            )
            out[first * MX + q] = outer[:half, :lanes]
            out[(first + 1) * MX + q] = outer[half:, lanes:]


def whole(array):
    return pl.BlockSpec(array.shape, lambda *step: (0,) * len(array.shape))


def shaped(shape, dtype):
    return jax.ShapeDtypeStruct(shape, dtype)


def params(mib):
    return pltpu.CompilerParams(vmem_limit_bytes=mib * MIB)


def cost(flops, moved, steep=0):
    return pl.CostEstimate(flops=flops, bytes_accessed=moved, transcendentals=steep)


def body(mesh_axes, devices, slabs, activations, cotangent, mode_weights, pointwise, offsets):
    _, channels, width, rows_y, rows_z = activations.shape
    samples = devices // slabs
    per = MY * MZ // devices
    groups = channels // GROUP
    field = activations.shape[1:]
    count = math.prod(field)
    base = z_base(rows_z)
    ytab = y_table(rows_y, width)
    line_fwd, line_inv = x_tables(samples, slabs, NX)
    weight = np.where(np.arange(MZ) == 0, 1.0, 2.0) / (rows_y * rows_z)
    scale = np.tile(np.repeat(weight, GROUP), groups)[None]
    scale, scale_t = (0.5 * scale).astype(np.float32), (math.sqrt(0.5) * scale).astype(np.float32)
    base_t, ytab_t = (np.ascontiguousarray(t.T) for t in (base, ytab))
    fwd_t, inv_t = (np.ascontiguousarray(t.T) for t in (line_fwd, line_inv))
    message = shaped((devices, 2 * width, per * channels), BF16)
    spectra = shaped((MX * 2 * samples, per * channels), BF16)
    ztab = pltpu.VMEM((GROUP * rows_z, 2 * MZ * GROUP), BF16)
    ztab_t = pltpu.VMEM((STEPS, 2 * MZ * GROUP, SLOTS * rows_z), BF16)
    order = pltpu.VMEM((MZ * channels, MZ * channels), BF16)
    rows = groups * width * rows_y
    held = pltpu.VMEM((rows, 2 * MZ * GROUP), BF16)
    sums = pltpu.VMEM((rows, 2 * MZ * GROUP), F32)
    slot_sums = pltpu.VMEM((rows, SLOTS * rows_z), F32)
    buffer = pltpu.VMEM(field, BF16)
    sems = pltpu.SemaphoreType.DMA((STEPS * groups,))
    far = pl.BlockSpec(memory_space=pltpu.HBM)
    far_field = pltpu.HBM(field, BF16)

    def kept_far(array):
        return pltpu.with_memory_space_constraint(array, pltpu.HBM)

    plane_flops = 2 * count * 2 * MZ * GROUP

    def exchange(array):
        return lax.all_to_all(array, mesh_axes, split_axis=0, concat_axis=0, tiled=True)

    def mix_points(values, turned, shifts):
        step = 2
        block = pl.BlockSpec((channels, step, rows_y, rows_z), lambda x: (0, x, 0, 0))
        kernel = functools.partial(pointwise_kernel, turned)
        specs = [block, whole(pointwise)]
        operands = [values, pointwise]
        if shifts is None:
            run = lambda a, b, *rest: kernel(a, b, None, *rest)
        else:
            run = kernel
            specs.append(pl.BlockSpec(memory_space=pltpu.SMEM))
            operands.append(shifts)
        return pl.pallas_call(
            run,
            grid=(width // step,),
            in_specs=specs,
            out_specs=block,
            out_shape=far_field,
            scratch_shapes=[
                pltpu.VMEM((channels * TILE, channels * TILE), BF16),
                pltpu.VMEM((channels, 1, rows_z), F32),
            ],
            compiler_params=params(32),
            cost_estimate=cost(2 * count * channels * TILE, 4 * count),
        )(*operands)

    planes = pl.pallas_call(
        functools.partial(plane_kernel, per, channels, slabs),
        in_specs=[far, far, far],
        out_specs=whole(message),
        out_shape=message,
        scratch_shapes=[
            ztab,
            order,
            sums,
            buffer,
            pltpu.VMEM(base.shape, F32),
            pltpu.VMEM(ytab.shape, BF16),
            sems,
            pltpu.SemaphoreType.DMA((2,)),
        ],
        compiler_params=params(32),
        cost_estimate=cost(plane_flops, 2 * count),
    )(kept_far(activations), kept_far(base), kept_far(ytab))
    arrived = exchange(planes)
    local = mix_points(kept_far(activations.reshape(field)), True, offsets)
    arrived, local = lax.optimization_barrier((arrived, local))
    spec_in, mixed = pl.pallas_call(
        functools.partial(mix_kernel, per, samples),
        out_shape=(spectra, message),
        scratch_shapes=[pltpu.VMEM(spectra.shape, BF16)],
        compiler_params=params(16),
        cost_estimate=cost(10**8, 2 * mode_weights.size),
    )(arrived, mode_weights, line_fwd, inv_t)
    returned = exchange(mixed)
    slope, back_plane = pl.pallas_call(
        functools.partial(slope_kernel, per, channels, slabs),
        in_specs=[whole(message), far, far]
        + [whole(t) for t in (base, base_t, ytab, ytab_t, scale, scale_t)],
        out_specs=(far, whole(message)),
        out_shape=(far_field, message),
        scratch_shapes=[ztab, ztab_t, order, held, sums]
        + [buffer] * 3
        + [slot_sums]
        + [sems] * 3,
        compiler_params=params(40),
        cost_estimate=cost(2 * plane_flops, 6 * count, 2 * count),
    )(returned, kept_far(local), kept_far(cotangent), base, base_t, ytab, ytab_t, scale, scale_t)
    arrived_back = exchange(back_plane)
    local_back = mix_points(kept_far(slope), False, None)
    arrived_back, local_back = lax.optimization_barrier((arrived_back, local_back))
    pairs, mixed_back = pl.pallas_call(
        functools.partial(mix_back_kernel, per, samples),
        out_shape=(shaped((spectra.shape[0], 2 * spectra.shape[1]), BF16), message),
        scratch_shapes=[pltpu.VMEM(spectra.shape, BF16)],
        compiler_params=params(16),
        cost_estimate=cost(10**8, 2 * mode_weights.size),
    )(arrived_back, mode_weights, line_inv, fwd_t)
    returned_back = exchange(mixed_back)
    grad_spectral = pl.pallas_call(
        functools.partial(weight_kernel, per, samples),
        out_shape=shaped(mode_weights.shape, F32),
        compiler_params=params(16),
        cost_estimate=cost(10**8, 4 * mode_weights.size),
    )(spec_in, pairs)
    grad_in = pl.pallas_call(
        functools.partial(field_kernel, per, channels, slabs),
        in_specs=[whole(message), far, whole(base_t), whole(ytab_t)],
        out_specs=far,
        out_shape=shaped(activations.shape, BF16),
        scratch_shapes=[ztab_t, order, held, buffer, buffer, sems, sems],
        compiler_params=params(32),
        cost_estimate=cost(plane_flops, 4 * count),
    )(returned_back, kept_far(local_back), base_t, ytab_t)
    return (grad_in, grad_spectral)


def chosen_body(mesh_axes, devices, slabs, activations, cotangent, mode_weights, pointwise, offsets):
    samples, channels, width, rows_y, rows_z = activations.shape
    per = MY * MZ // devices
    fits = (
        samples == 1
        and MY * MZ % devices == 0
        and per in (2, 4, 8)
        and width % 8 == 0
        and channels == 64
        and rows_y % TILE == 0
        and rows_z == 128
    )
    plan = functools.partial(body, mesh_axes, devices, slabs) if fits else general_body
    return plan(activations, cotangent, mode_weights, pointwise, offsets)


def solution(mesh):
    slabs = mesh.shape["space"]
    devices = slabs * mesh.shape["dp"]
    return jax.shard_map(
        functools.partial(chosen_body, ("dp", "space"), devices, slabs),
        mesh=mesh,
        in_specs=(
            P("dp", None, "space", None, None),
            P("dp", None, "space", None, None),
            P(("space", "dp"), None, None),
            P(),
            P(),
        ),
        out_specs=(P("dp", None, "space", None, None), P(("space", "dp"), None, None)),
        check_vma=False,
    )
```

```python
import functools
import math

import jax
import jax.numpy as jnp
import ml_dtypes
import numpy as np
from jax import lax
from jax.experimental import pallas as pl
from jax.experimental.pallas import tpu as pltpu
from jax.sharding import PartitionSpec as P

MX = 16
MY = 16
MZ = 8
NX = 32


def centered(count):
    index = jnp.arange(count, dtype=jnp.int32)
    return jnp.where(index < count // 2, index, index - count)


def plane_tables(rows_y, rows_z, modes_y, modes_z):
    along_y = jnp.arange(rows_y, dtype=jnp.int32)[:, None, None, None]
    along_z = jnp.arange(rows_z, dtype=jnp.int32)[None, :, None, None]
    freq_y = centered(modes_y)[None, None, :, None]
    freq_z = jnp.arange(modes_z, dtype=jnp.int32)[None, None, None, :]
    phase = jnp.mod(freq_y * along_y * rows_z + freq_z * along_z * rows_y, rows_y * rows_z)
    theta = phase.astype(jnp.float32) * (2.0 * math.pi / (rows_y * rows_z))
    cosine = jnp.cos(theta)
    sine = jnp.sin(theta)
    forward = jnp.stack([cosine, -sine], -1).reshape(rows_y * rows_z, modes_y * modes_z * 2)
    scaled = jnp.where(freq_z == 0, 1.0, 2.0).astype(jnp.float32) / (rows_y * rows_z)
    inverse = (
        jnp.stack([cosine * scaled, -sine * scaled], -1)
        .reshape(rows_y * rows_z, modes_y * modes_z * 2)
        .T
    )
    return (forward.astype(jnp.bfloat16), inverse.astype(jnp.bfloat16))


def line_tables(length, modes):
    along = jnp.arange(length, dtype=jnp.int32)[:, None]
    freq = centered(modes)[None, :]
    phase = jnp.mod(freq * along, length)
    theta = phase.astype(jnp.float32) * (2.0 * math.pi / length)
    cosine = jnp.cos(theta)
    sine = jnp.sin(theta)
    first = jnp.stack([cosine, -sine], -1)
    second = jnp.stack([sine, cosine], -1)
    forward = jnp.stack([first, second], 1).reshape(2 * length, 2 * modes)
    inv_first = jnp.stack([cosine.T, sine.T], -1) / length
    inv_second = jnp.stack([-sine.T, cosine.T], -1) / length
    inverse = jnp.stack([inv_first, inv_second], 1).reshape(2 * modes, 2 * length)
    return (forward.astype(jnp.bfloat16), inverse.astype(jnp.bfloat16))


def expand_weights(weights):
    half = weights.shape[1]
    real_part = weights[:, :, :half]
    imag_part = weights[:, :, half:]
    upper = jnp.concatenate([real_part, imag_part], axis=2)
    lower = jnp.concatenate([-imag_part, real_part], axis=2)
    return jnp.concatenate([upper, lower], axis=1)


def outer_sum(left, right):
    return jnp.einsum("mbi,mbo->mio", left, right, preferred_element_type=jnp.float32)


def weight_terms(spec_in, spec_grad):
    half = spec_in.shape[2] // 2
    in_real = spec_in[:, :, :half]
    in_imag = spec_in[:, :, half:]
    gr_real = spec_grad[:, :, :half]
    gr_imag = spec_grad[:, :, half:]
    real_term = outer_sum(in_real, gr_real) + outer_sum(in_imag, gr_imag)
    imag_term = outer_sum(in_real, gr_imag) - outer_sum(in_imag, gr_real)
    return jnp.concatenate([real_term, imag_term], axis=2)


def to_modes(slab, table, modes_x):
    samples, channels, width, pairs = slab.shape
    moved = lax.all_to_all(slab, "space", split_axis=3, concat_axis=2, tiled=True)
    length = moved.shape[2]
    local = moved.shape[3] // 2
    lines = moved.reshape(samples, channels, length, local, 2).transpose(0, 1, 3, 2, 4)
    lines = lines.reshape(samples, channels, local, 2 * length)
    spectra = jnp.dot(lines, table, preferred_element_type=jnp.float32).astype(jnp.bfloat16)
    spectra = spectra.reshape(samples, channels, local, modes_x, 2).transpose(2, 3, 0, 4, 1)
    return spectra.reshape(local * modes_x, samples, 2 * channels)


def to_slab(spectra, table, modes_x, channels):
    count, samples, doubled = spectra.shape
    local = count // modes_x
    lines = spectra.reshape(local, modes_x, samples, 2, channels).transpose(2, 4, 0, 1, 3)
    lines = lines.reshape(samples, channels, local, 2 * modes_x)
    lines = jnp.dot(lines, table, preferred_element_type=jnp.float32).astype(jnp.bfloat16)
    length = lines.shape[3] // 2
    lines = lines.reshape(samples, channels, local, length, 2).transpose(0, 1, 3, 2, 4)
    lines = lines.reshape(samples, channels, length, 2 * local)
    return lax.all_to_all(lines, "space", split_axis=2, concat_axis=3, tiled=True)


def to_owners(spectra):
    return lax.all_to_all(spectra, "dp", split_axis=0, concat_axis=1, tiled=True)


def from_owners(spectra):
    return lax.all_to_all(spectra, "dp", split_axis=1, concat_axis=0, tiled=True)


def gelu_slope(value):
    cdf = 0.5 * (1.0 + lax.erf(value * 0.7071067811865476))
    density = jnp.exp(-0.5 * value * value) * 0.3989422804014327
    return cdf + value * density


def general_body(activations, cotangent, mode_weights, pointwise, offsets):
    samples, channels, width, rows_y, rows_z = activations.shape
    plane_fwd, plane_inv = plane_tables(rows_y, rows_z, MY, MZ)
    line_fwd, line_inv = line_tables(NX, MX)
    flat = activations.reshape(samples, channels, width, rows_y * rows_z)
    planes = jnp.dot(flat, plane_fwd, preferred_element_type=jnp.float32).astype(jnp.bfloat16)
    spec_in = to_modes(planes, line_fwd, MX)
    blocks = expand_weights(mode_weights)
    held_in = to_owners(spec_in)
    held_out = jnp.einsum(
        "mbi,mio->mbo", held_in, blocks, preferred_element_type=jnp.float32
    ).astype(jnp.bfloat16)
    spec_out = from_owners(held_out)
    returned = to_slab(spec_out, line_inv, MX, channels)
    spectral = jnp.dot(returned, plane_inv, preferred_element_type=jnp.float32)
    local_part = jnp.einsum("io,bixn->boxn", pointwise, flat, preferred_element_type=jnp.float32)
    summed = spectral + local_part + offsets[None, :, None, None]
    upstream = cotangent.reshape(flat.shape).astype(jnp.float32)
    slope_grad = (upstream * gelu_slope(summed)).astype(jnp.bfloat16)
    back_plane = jnp.dot(slope_grad, plane_inv.T, preferred_element_type=jnp.float32).astype(
        jnp.bfloat16
    )
    spec_grad = to_modes(back_plane, line_inv.T, MX)
    held_grad = to_owners(spec_grad)
    held_dx = jnp.einsum(
        "mbo,mio->mbi", held_grad, blocks, preferred_element_type=jnp.float32
    ).astype(jnp.bfloat16)
    spec_dx = from_owners(held_dx)
    grad_spectral = weight_terms(held_in, held_grad)
    line_dx = to_slab(spec_dx, line_fwd.T, MX, channels)
    total = jnp.dot(line_dx, plane_fwd.T, preferred_element_type=jnp.float32)
    total = total + jnp.einsum(
        "io,boxn->bixn", pointwise, slope_grad, preferred_element_type=jnp.float32
    )
    grad_in = total.astype(jnp.bfloat16).reshape(activations.shape)
    return (grad_in, grad_spectral)


BF16 = jnp.bfloat16
F32 = jnp.float32
GROUP = 16
TILE = 8
SLOTS = 4
STEPS = GROUP // SLOTS
MIB = 1024 * 1024


def rounded(table):
    return np.asarray(table, np.float32).astype(ml_dtypes.bfloat16)


def angles(freq, points, length):
    phase = np.mod(np.outer(freq, points), length)
    return (phase * (2.0 * math.pi / length)).astype(np.float64)


def signed(count):
    index = np.arange(count)
    return np.where(index < count // 2, index, index - count)


def z_base(rows_z):
    theta = angles(np.arange(MZ), np.arange(rows_z), rows_z)
    pair = np.stack([np.cos(theta), -np.sin(theta)])
    table = np.repeat(pair.reshape(2 * MZ, rows_z), GROUP, axis=0).T
    return rounded(table).astype(np.float32)


def y_table(rows_y, width):
    theta = angles(signed(MY), np.arange(rows_y), rows_y)
    cosine, sine = np.cos(theta), np.sin(theta)
    turn = np.stack([np.stack([cosine, sine]), np.stack([-sine, cosine])])
    table = np.einsum("rsjy,xw->jxrswy", turn, np.eye(width))
    return rounded(table.reshape(MY * width * 2, 2 * width * rows_y))


def x_tables(samples, slabs, length):
    theta = angles(signed(MX), np.arange(length), length)
    cosine, sine = np.cos(theta), np.sin(theta)
    forward = np.stack([np.stack([cosine, sine]), np.stack([-sine, cosine])])
    inverse = np.stack([np.stack([cosine, sine]), np.stack([-sine, cosine])]) / length
    same = np.eye(samples)
    rows = MX * 2 * samples

    def lay(turn):
        turn = turn.reshape(2, 2, MX, slabs, length // slabs)
        table = np.einsum("arqsx,bd->qabdsxr", turn, same)
        return rounded(table.reshape(rows, samples * length * 2))

    return lay(forward), lay(inverse)


def dot(left, right):
    return jnp.dot(left, right, preferred_element_type=F32)


def doubled_slope(u):
    decay = jnp.exp2(u * u * -math.log2(math.e)).astype(BF16)
    cdf = (1.0 + lax.erf(u)).astype(BF16)
    return cdf + u.astype(BF16) * jnp.asarray(2.0 / math.sqrt(math.pi), BF16) * decay


def over(index, size):
    return lax.shift_right_logical(index, jnp.int32(size.bit_length() - 1))


def within(index, size):
    return jnp.bitwise_and(index, jnp.int32(size - 1))


def fill_z(base, table):
    rows_z, lanes = base.shape
    owner = within(lax.broadcasted_iota(jnp.int32, (rows_z, lanes), 1), GROUP)
    values = base[...]
    for c in range(GROUP):
        table[c * rows_z : (c + 1) * rows_z] = jnp.where(owner == c, values, 0.0).astype(BF16)


def fill_z_back(base, table):
    lanes, rows_z = base.shape
    owner = within(lax.broadcasted_iota(jnp.int32, (lanes, rows_z), 0), GROUP)
    values = base[...]
    for c in range(GROUP):
        first = c % SLOTS * rows_z
        table[c // SLOTS, :, first : first + rows_z] = jnp.where(owner == c, values, 0.0).astype(BF16)


def grouped(lane, per, channels):
    c = within(lane, channels)
    return over(c, GROUP) * (MZ * GROUP) + over(lane, channels) * GROUP + within(c, GROUP)


def fill_order(per, channels, back, table):
    count = table.shape[0]
    row = lax.broadcasted_iota(jnp.int32, (count, count), 0)
    column = lax.broadcasted_iota(jnp.int32, (count, count), 1)
    if back:
        same = grouped(row[:, :1], per, channels) == column
    else:
        same = row == grouped(column[:1], per, channels)
    table[...] = jnp.where(same, 1.0, 0.0).astype(BF16)


def turned_index(index, slabs, devices):
    samples = devices // slabs
    return index % samples * slabs + index // samples


def deliver(spectra, ytab, order, scale, message, per, channels, slabs):
    groups = channels // GROUP
    rows = spectra.shape[0] // groups
    wide = spectra.shape[1] // 2
    halves = []
    for r in range(2):
        blocks = [spectra[g * rows : (g + 1) * rows, r * wide : (r + 1) * wide] for g in range(groups)]
        halves.append(jnp.concatenate(blocks, axis=1).astype(BF16))
    planes = dot(ytab[...], jnp.concatenate(halves, axis=0))
    if scale is not None:
        planes = planes * scale[...]
    ordered = dot(planes.astype(BF16), order[...]).astype(BF16)
    parts = MZ // per
    count = message.shape[1]
    lanes = per * channels
    for part in range(parts):
        block = ordered[:, part * lanes : (part + 1) * lanes]
        for j in range(MY):
            message[turned_index(j * parts + part, slabs, message.shape[0])] = block[j * count : (j + 1) * count]


def receive(message, order_back, ytab_back, scale, held, per, slabs):
    parts = MZ // per
    lanes = [
        jnp.concatenate(
            [message[turned_index(j * parts + part, slabs, message.shape[0])] for j in range(MY)], axis=0
        )
        for part in range(parts)
    ]
    ordered = dot(jnp.concatenate(lanes, axis=1), order_back[...]).astype(BF16)
    lines = dot(ytab_back[...], ordered)
    if scale is not None:
        lines = lines * scale[...]
    lines = lines.astype(BF16)
    rows = lines.shape[0] // 2
    wide = MZ * GROUP
    for group in range(held.shape[0] // rows):
        piece = lines[:, group * wide : (group + 1) * wide]
        held[group * rows : (group + 1) * rows] = jnp.concatenate([piece[:rows], piece[rows:]], axis=1)


class Move:
    def __init__(self, source, target, sems, first=0):
        self.source, self.target, self.sems = source, target, sems
        self.groups = target.shape[0] // GROUP
        self.rows = pl.ds(first, source.shape[1])

    def copy(self, step, g):
        run = pl.ds(g * GROUP + step * SLOTS, SLOTS)
        sem = self.sems.at[step * self.groups + g]
        return pltpu.make_async_copy(self.source.at[run], self.target.at[run, self.rows], sem)

    def start(self, step):
        for g in range(self.groups):
            self.copy(step, g).start()

    def wait(self, step):
        for g in range(self.groups):
            self.copy(step, g).wait()


def start_all(moves, step):
    for each in moves:
        each.start(step)


def add_spectra(field, ztab, step, spectra):
    groups = field.shape[0] // GROUP
    rows_z = field.shape[-1]
    depth = SLOTS * rows_z
    table = ztab[pl.ds(pl.multiple_of(step * depth, depth), depth)]
    lanes = [
        jnp.concatenate(
            [field[g * GROUP + step * SLOTS + slot].reshape(-1, rows_z) for g in range(groups)], axis=0
        )
        for slot in range(SLOTS)
    ]
    spectra[...] += dot(jnp.concatenate(lanes, axis=1), table)


def plane_kernel(
    per, channels, slabs, field, base_far, ytab_far, message, ztab, order, spectra, buffer, base, ytab, sems, table_sems
):
    incoming = Move(field.at[0], buffer, sems)
    base_copy = pltpu.make_async_copy(base_far, base, table_sems.at[0])
    ytab_copy = pltpu.make_async_copy(ytab_far, ytab, table_sems.at[1])
    base_copy.start()
    incoming.start(0)
    fill_order(per, channels, False, order)
    spectra[...] = jnp.zeros_like(spectra)
    incoming.start(1)
    base_copy.wait()
    fill_z(base, ztab)
    incoming.start(2)
    ytab_copy.start()
    incoming.start(3)

    @pl.loop(0, STEPS)
    def _(step):
        incoming.wait(step)
        add_spectra(buffer, ztab, step, spectra)

    ytab_copy.wait()
    deliver(spectra, ytab, order, None, message, per, channels, slabs)


def slope_kernel(
    per, channels, slabs, arrived, local_low, local_high, cotangent, base, base_back, ytab, ytab_back, scale, scale_back,
    slope, message, ztab, ztab_back, order, held, spectra, local_in, cotangent_in, result, total,
    low_sems, high_sems, cotangent_sems, result_sems,
):
    width, rows_y, rows_z = slope.shape[1:]
    groups = channels // GROUP
    rows = width * rows_y
    wide = 2 * rows_y
    incoming = (
        Move(local_low, local_in, low_sems),
        Move(local_high, local_in, high_sems, local_low.shape[1]),
        Move(cotangent.at[0], cotangent_in, cotangent_sems),
    )
    outgoing = Move(result, slope, result_sems)
    start_all(incoming, 0)
    fill_order(per, channels, True, order)
    receive(arrived, order, ytab_back, scale_back, held, per, slabs)
    start_all(incoming, 1)
    fill_z_back(base_back, ztab_back)
    fill_z(base, ztab)
    start_all(incoming, 2)
    fill_order(per, channels, False, order)
    spectra[...] = jnp.zeros_like(spectra)
    start_all(incoming, 3)

    @pl.loop(0, STEPS)
    def _(step):
        for each in incoming:
            each.wait(step)
        total[...] = dot(held[...], ztab_back[step])
        for g in range(groups):
            for slot in range(SLOTS):
                lanes = slice(slot * rows_z, (slot + 1) * rows_z)
                c = g * GROUP + step * SLOTS + slot
                for x in range(0, width, 2):
                    place = g * rows + x * rows_y
                    value = total[place : place + wide, lanes]
                    value = value + local_in[c, x : x + 2].reshape(wide, rows_z).astype(F32)
                    upstream = cotangent_in[c, x : x + 2].reshape(wide, rows_z)
                    answer = upstream * doubled_slope(value)
                    result[c, x : x + 2] = answer.reshape(2, rows_y, rows_z)
            outgoing.copy(step, g).start()
        add_spectra(result, ztab, step, spectra)

    deliver(spectra, ytab, order, scale, message, per, channels, slabs)
    for step in range(STEPS):
        outgoing.wait(step)


def field_kernel(
    per, channels, slabs, arrived, local, base_back, ytab_back, out, ztab_back, order, held, local_in, result,
    local_sems, result_sems,
):
    width, rows_y, rows_z = local.shape[1:]
    groups = channels // GROUP
    rows = width * rows_y
    incoming = Move(local, local_in, local_sems)
    outgoing = Move(result, out.at[0], result_sems)
    incoming.start(0)
    fill_order(per, channels, True, order)
    incoming.start(1)
    receive(arrived, order, ytab_back, None, held, per, slabs)
    incoming.start(2)
    fill_z_back(base_back, ztab_back)
    incoming.start(3)

    @pl.loop(0, STEPS)
    def _(step):
        incoming.wait(step)
        total = dot(held[...], ztab_back[step])
        for g in range(groups):
            for slot in range(SLOTS):
                lanes = slice(slot * rows_z, (slot + 1) * rows_z)
                c = g * GROUP + step * SLOTS + slot
                value = total[g * rows : (g + 1) * rows, lanes]
                value = value + local_in[c].reshape(rows, rows_z).astype(F32)
                result[c] = value.astype(BF16).reshape(width, rows_y, rows_z)
            outgoing.copy(step, g).start()

    for step in range(STEPS):
        outgoing.wait(step)


def pointwise_kernel(turned, field, mix, offsets, out, table, shift):
    channels = mix.shape[0]
    width, rows_y, rows_z = field.shape[1:]
    size = channels * TILE

    @pl.when(pl.program_id(0) == 0)
    def _():
        row = over(lax.broadcasted_iota(jnp.int32, (size, channels), 0), TILE)
        column = lax.broadcasted_iota(jnp.int32, (size, channels), 1)
        spread = jnp.where(row == column, 1.0, 0.0).astype(BF16)
        tall = lax.dot_general(
            spread, mix[...], (((1,), (1 if turned else 0,)), ((), ())), preferred_element_type=F32
        ).astype(BF16)
        whole = lax.dot_general(
            tall, spread, (((1,), (1,)), ((), ())), preferred_element_type=F32
        )
        place = within(lax.broadcasted_iota(jnp.int32, (size, size), 0), TILE)
        other = within(lax.broadcasted_iota(jnp.int32, (size, size), 1), TILE)
        table[...] = jnp.where(place == other, whole if turned else 0.5 * whole, 0.0).astype(BF16)
        if offsets is not None:
            for c in range(channels):
                shift[c] = jnp.full((1, rows_z), offsets[c], F32)

    for start in range(0, rows_y, 2 * TILE):
        pieces = [field[:, x, start : start + 2 * TILE, :].astype(F32) for x in range(width)]
        halves = []
        for row in range(0, 2 * TILE, TILE):
            rows = [piece[:, row : row + TILE].reshape(size, rows_z).astype(BF16) for piece in pieces]
            halves.append(dot(table[...], jnp.concatenate(rows, axis=1)))
        for x in range(width):
            values = [
                half[:, x * rows_z : (x + 1) * rows_z].reshape(channels, TILE, rows_z) for half in halves
            ]
            value = jnp.concatenate(values, axis=1)
            if offsets is not None:
                value = (value + shift[...]) * math.sqrt(0.5)
            out[:, x, start : start + 2 * TILE, :] = value.astype(BF16)


def spread_pair(first, second):
    nothing = jnp.zeros_like(first)
    upper = jnp.concatenate([first, nothing], axis=1)
    lower = jnp.concatenate([nothing, second], axis=1)
    return jnp.concatenate([upper, lower], axis=0)


def low_half(shape):
    return lax.broadcasted_iota(jnp.int32, shape, 1) < shape[1] // 2


def mix_kernel(per, samples, arrived, weights, line, line_back, spec_in, message, held):
    rows = 2 * samples
    lanes = 2 * weights.shape[1]
    low = low_half((samples, lanes))
    flat = arrived[...].reshape(-1, arrived.shape[2])
    spectra = dot(line[...], flat).astype(BF16)
    spec_in[...] = spectra
    for q in range(MX):
        for first in range(0, per, 2):
            block = spread_pair(weights[first * MX + q], weights[(first + 1) * MX + q])
            place = first // 2 * lanes
            terms = dot(spectra[q * rows : (q + 1) * rows, place : place + lanes], block)
            mixed = []
            for side in range(2):
                part = terms[:, side * lanes : (side + 1) * lanes]
                turned = pltpu.roll(part[samples:], lanes // 2, 1)
                mixed.append(part[:samples] + jnp.where(low, -turned, turned))
            real = jnp.where(low, mixed[0], pltpu.roll(mixed[1], lanes // 2, 1))
            imag = jnp.where(low, pltpu.roll(mixed[0], lanes // 2, 1), mixed[1])
            held[q * rows : (q + 1) * rows, place : place + lanes] = jnp.concatenate(
                [real, imag], axis=0
            ).astype(BF16)
    message[...] = dot(line_back[...], held[...]).astype(BF16).reshape(message.shape)


def mix_back_kernel(per, samples, arrived, weights, line, line_back, pairs, message, held):
    rows = 2 * samples
    lanes = 2 * weights.shape[1]
    low = low_half((samples, lanes))
    first_lanes = jnp.where(low_half((lanes, lanes)), 1.0, 0.0).astype(BF16)
    second_lanes = jnp.where(low_half((lanes, lanes)), 0.0, 1.0).astype(BF16)
    flat = arrived[...].reshape(-1, arrived.shape[2])
    spectra = dot(line[...], flat).astype(BF16).astype(F32)
    for q in range(MX):
        for first in range(0, per, 2):
            both = jnp.concatenate([weights[first * MX + q], weights[(first + 1) * MX + q]], axis=0).T
            block = jnp.concatenate([both * first_lanes, both * second_lanes], axis=0)
            place = first // 2 * lanes
            real = spectra[q * rows : q * rows + samples, place : place + lanes]
            imag = spectra[q * rows + samples : (q + 1) * rows, place : place + lanes]
            real_turned = pltpu.roll(real, lanes // 2, 1)
            imag_turned = pltpu.roll(imag, lanes // 2, 1)
            left = [jnp.where(low, real, imag_turned), jnp.where(low, imag, -real_turned)]
            right = [jnp.where(low, real_turned, imag), jnp.where(low, imag_turned, -real)]
            pair = jnp.concatenate(
                [jnp.concatenate(left, axis=0), jnp.concatenate(right, axis=0)], axis=1
            ).astype(BF16)
            pairs[q * rows : (q + 1) * rows, 2 * place : 2 * (place + lanes)] = pair
            held[q * rows : (q + 1) * rows, place : place + lanes] = dot(pair, block).astype(BF16)
    message[...] = dot(line_back[...], held[...]).astype(BF16).reshape(message.shape)


def weight_kernel(per, samples, spec_in, pairs, out):
    rows = 2 * samples
    lanes = out.shape[2]
    half = lanes // 2
    for q in range(MX):
        for first in range(0, per, 2):
            place = first // 2 * lanes
            left = spec_in[q * rows : (q + 1) * rows, place : place + lanes]
            right = pairs[q * rows : (q + 1) * rows, 2 * place : 2 * (place + lanes)]
            outer = lax.dot_general(
                left, right, (((0,), (0,)), ((), ())), preferred_element_type=F32
            )
            out[first * MX + q] = outer[:half, :lanes]
            out[(first + 1) * MX + q] = outer[half:, lanes:]


def whole(array):
    return pl.BlockSpec(array.shape, lambda *step: (0,) * len(array.shape))


def shaped(shape, dtype):
    return jax.ShapeDtypeStruct(shape, dtype)


def params(mib):
    return pltpu.CompilerParams(vmem_limit_bytes=mib * MIB)


def cost(flops, moved, steep=0):
    return pl.CostEstimate(flops=flops, bytes_accessed=moved, transcendentals=steep)


def body(mesh_axes, devices, slabs, activations, cotangent, mode_weights, pointwise, offsets):
    _, channels, width, rows_y, rows_z = activations.shape
    samples = devices // slabs
    per = MY * MZ // devices
    groups = channels // GROUP
    field = activations.shape[1:]
    count = math.prod(field)
    base = z_base(rows_z)
    ytab = y_table(rows_y, width)
    line_fwd, line_inv = x_tables(samples, slabs, NX)
    weight = np.where(np.arange(MZ) == 0, 1.0, 2.0) / (rows_y * rows_z)
    scale = np.tile(np.repeat(weight, GROUP), groups)[None]
    scale, scale_t = (0.5 * scale).astype(np.float32), (math.sqrt(0.5) * scale).astype(np.float32)
    base_t, ytab_t = (np.ascontiguousarray(t.T) for t in (base, ytab))
    fwd_t, inv_t = (np.ascontiguousarray(t.T) for t in (line_fwd, line_inv))
    message = shaped((devices, 2 * width, per * channels), BF16)
    spectra = shaped((MX * 2 * samples, per * channels), BF16)
    ztab = pltpu.VMEM((GROUP * rows_z, 2 * MZ * GROUP), BF16)
    ztab_t = pltpu.VMEM((STEPS, 2 * MZ * GROUP, SLOTS * rows_z), BF16)
    order = pltpu.VMEM((MZ * channels, MZ * channels), BF16)
    rows = groups * width * rows_y
    held = pltpu.VMEM((rows, 2 * MZ * GROUP), BF16)
    sums = pltpu.VMEM((rows, 2 * MZ * GROUP), F32)
    slot_sums = pltpu.VMEM((rows, SLOTS * rows_z), F32)
    buffer = pltpu.VMEM(field, BF16)
    sems = pltpu.SemaphoreType.DMA((STEPS * groups,))
    far = pl.BlockSpec(memory_space=pltpu.HBM)
    far_field = pltpu.HBM(field, BF16)

    def kept_far(array):
        return pltpu.with_memory_space_constraint(array, pltpu.HBM)

    plane_flops = 2 * count * 2 * MZ * GROUP

    def exchange(array):
        return lax.all_to_all(array, mesh_axes, split_axis=0, concat_axis=0, tiled=True)

    def mix_points(values, mix, turned, shifts, first, rows_x):
        step = 2
        block = pl.BlockSpec((channels, step, rows_y, rows_z), lambda x: (0, x, 0, 0))
        source = pl.BlockSpec((channels, step, rows_y, rows_z), lambda x: (0, x + first // step, 0, 0))
        kernel = functools.partial(pointwise_kernel, turned)
        specs = [source, whole(pointwise)]
        operands = [values, mix]
        if shifts is None:
            run = lambda a, b, *rest: kernel(a, b, None, *rest)
        else:
            run = kernel
            specs.append(pl.BlockSpec(memory_space=pltpu.SMEM))
            operands.append(shifts)
        return pl.pallas_call(
            run,
            grid=(rows_x // step,),
            in_specs=specs,
            out_specs=block,
            out_shape=pltpu.HBM((channels, rows_x, rows_y, rows_z), BF16),
            scratch_shapes=[
                pltpu.VMEM((channels * TILE, channels * TILE), BF16),
                pltpu.VMEM((channels, 1, rows_z), F32),
            ],
            compiler_params=params(32),
            cost_estimate=cost(2 * count * channels * TILE * rows_x // width, 4 * count * rows_x // width),
        )(*operands)

    planes = pl.pallas_call(
        functools.partial(plane_kernel, per, channels, slabs),
        in_specs=[far, far, far],
        out_specs=whole(message),
        out_shape=message,
        scratch_shapes=[
            ztab,
            order,
            sums,
            buffer,
            pltpu.VMEM(base.shape, F32),
            pltpu.VMEM(ytab.shape, BF16),
            sems,
            pltpu.SemaphoreType.DMA((2,)),
        ],
        compiler_params=params(32),
        cost_estimate=cost(plane_flops, 2 * count),
    )(kept_far(activations), kept_far(base), kept_far(ytab))
    planes, early_pointwise = lax.optimization_barrier((planes, pointwise))
    arrived = exchange(planes)
    half = width // 2
    local_low = mix_points(kept_far(activations.reshape(field)), early_pointwise, True, offsets, 0, half)
    arrived, local_low = lax.optimization_barrier((arrived, local_low))
    spec_in, mixed = pl.pallas_call(
        functools.partial(mix_kernel, per, samples),
        out_shape=(spectra, message),
        scratch_shapes=[pltpu.VMEM(spectra.shape, BF16)],
        compiler_params=params(16),
        cost_estimate=cost(10**8, 2 * mode_weights.size),
    )(arrived, mode_weights, line_fwd, inv_t)
    mixed, late_pointwise = lax.optimization_barrier((mixed, pointwise))
    returned = exchange(mixed)
    local_high = mix_points(kept_far(activations.reshape(field)), late_pointwise, True, offsets, half, half)
    slope, back_plane = pl.pallas_call(
        functools.partial(slope_kernel, per, channels, slabs),
        in_specs=[whole(message), far, far, far]
        + [whole(t) for t in (base, base_t, ytab, ytab_t, scale, scale_t)],
        out_specs=(far, whole(message)),
        out_shape=(far_field, message),
        scratch_shapes=[ztab, ztab_t, order, held, sums]
        + [buffer] * 3
        + [slot_sums]
        + [sems] * 4,
        compiler_params=params(40),
        cost_estimate=cost(2 * plane_flops, 6 * count, 2 * count),
    )(returned, kept_far(local_low), kept_far(local_high), kept_far(cotangent), base, base_t, ytab, ytab_t, scale, scale_t)
    arrived_back = exchange(back_plane)
    local_back = mix_points(kept_far(slope), pointwise, False, None, 0, width)
    arrived_back, local_back = lax.optimization_barrier((arrived_back, local_back))
    pairs, mixed_back = pl.pallas_call(
        functools.partial(mix_back_kernel, per, samples),
        out_shape=(shaped((spectra.shape[0], 2 * spectra.shape[1]), BF16), message),
        scratch_shapes=[pltpu.VMEM(spectra.shape, BF16)],
        compiler_params=params(16),
        cost_estimate=cost(10**8, 2 * mode_weights.size),
    )(arrived_back, mode_weights, line_inv, fwd_t)
    returned_back = exchange(mixed_back)
    grad_spectral = pl.pallas_call(
        functools.partial(weight_kernel, per, samples),
        out_shape=shaped(mode_weights.shape, F32),
        compiler_params=params(16),
        cost_estimate=cost(10**8, 4 * mode_weights.size),
    )(spec_in, pairs)
    grad_in = pl.pallas_call(
        functools.partial(field_kernel, per, channels, slabs),
        in_specs=[whole(message), far, whole(base_t), whole(ytab_t)],
        out_specs=far,
        out_shape=shaped(activations.shape, BF16),
        scratch_shapes=[ztab_t, order, held, buffer, buffer, sems, sems],
        compiler_params=params(32),
        cost_estimate=cost(plane_flops, 4 * count),
    )(returned_back, kept_far(local_back), base_t, ytab_t)
    return (grad_in, grad_spectral)


def chosen_body(mesh_axes, devices, slabs, activations, cotangent, mode_weights, pointwise, offsets):
    samples, channels, width, rows_y, rows_z = activations.shape
    per = MY * MZ // devices
    fits = (
        samples == 1
        and MY * MZ % devices == 0
        and per in (2, 4, 8)
        and width % 8 == 0
        and channels == 64
        and rows_y % TILE == 0
        and rows_z == 128
    )
    plan = functools.partial(body, mesh_axes, devices, slabs) if fits else general_body
    return plan(activations, cotangent, mode_weights, pointwise, offsets)


def solution(mesh):
    slabs = mesh.shape["space"]
    devices = slabs * mesh.shape["dp"]
    return jax.shard_map(
        functools.partial(chosen_body, ("dp", "space"), devices, slabs),
        mesh=mesh,
        in_specs=(
            P("dp", None, "space", None, None),
            P("dp", None, "space", None, None),
            P(("space", "dp"), None, None),
            P(),
            P(),
        ),
        out_specs=(P("dp", None, "space", None, None), P(("space", "dp"), None, None)),
        check_vma=False,
    )
```

```python
import functools
import math

import jax
import jax.numpy as jnp
import ml_dtypes
import numpy as np
from jax import lax
from jax.experimental import pallas as pl
from jax.experimental.pallas import tpu as pltpu
from jax.sharding import PartitionSpec as P

MX = 16
MY = 16
MZ = 8
NX = 32


def centered(count):
    index = jnp.arange(count, dtype=jnp.int32)
    return jnp.where(index < count // 2, index, index - count)


def plane_tables(rows_y, rows_z, modes_y, modes_z):
    along_y = jnp.arange(rows_y, dtype=jnp.int32)[:, None, None, None]
    along_z = jnp.arange(rows_z, dtype=jnp.int32)[None, :, None, None]
    freq_y = centered(modes_y)[None, None, :, None]
    freq_z = jnp.arange(modes_z, dtype=jnp.int32)[None, None, None, :]
    phase = jnp.mod(freq_y * along_y * rows_z + freq_z * along_z * rows_y, rows_y * rows_z)
    theta = phase.astype(jnp.float32) * (2.0 * math.pi / (rows_y * rows_z))
    cosine = jnp.cos(theta)
    sine = jnp.sin(theta)
    forward = jnp.stack([cosine, -sine], -1).reshape(rows_y * rows_z, modes_y * modes_z * 2)
    scaled = jnp.where(freq_z == 0, 1.0, 2.0).astype(jnp.float32) / (rows_y * rows_z)
    inverse = (
        jnp.stack([cosine * scaled, -sine * scaled], -1)
        .reshape(rows_y * rows_z, modes_y * modes_z * 2)
        .T
    )
    return (forward.astype(jnp.bfloat16), inverse.astype(jnp.bfloat16))


def line_tables(length, modes):
    along = jnp.arange(length, dtype=jnp.int32)[:, None]
    freq = centered(modes)[None, :]
    phase = jnp.mod(freq * along, length)
    theta = phase.astype(jnp.float32) * (2.0 * math.pi / length)
    cosine = jnp.cos(theta)
    sine = jnp.sin(theta)
    first = jnp.stack([cosine, -sine], -1)
    second = jnp.stack([sine, cosine], -1)
    forward = jnp.stack([first, second], 1).reshape(2 * length, 2 * modes)
    inv_first = jnp.stack([cosine.T, sine.T], -1) / length
    inv_second = jnp.stack([-sine.T, cosine.T], -1) / length
    inverse = jnp.stack([inv_first, inv_second], 1).reshape(2 * modes, 2 * length)
    return (forward.astype(jnp.bfloat16), inverse.astype(jnp.bfloat16))


def expand_weights(weights):
    half = weights.shape[1]
    real_part = weights[:, :, :half]
    imag_part = weights[:, :, half:]
    upper = jnp.concatenate([real_part, imag_part], axis=2)
    lower = jnp.concatenate([-imag_part, real_part], axis=2)
    return jnp.concatenate([upper, lower], axis=1)


def outer_sum(left, right):
    return jnp.einsum("mbi,mbo->mio", left, right, preferred_element_type=jnp.float32)


def weight_terms(spec_in, spec_grad):
    half = spec_in.shape[2] // 2
    in_real = spec_in[:, :, :half]
    in_imag = spec_in[:, :, half:]
    gr_real = spec_grad[:, :, :half]
    gr_imag = spec_grad[:, :, half:]
    real_term = outer_sum(in_real, gr_real) + outer_sum(in_imag, gr_imag)
    imag_term = outer_sum(in_real, gr_imag) - outer_sum(in_imag, gr_real)
    return jnp.concatenate([real_term, imag_term], axis=2)


def to_modes(slab, table, modes_x):
    samples, channels, width, pairs = slab.shape
    moved = lax.all_to_all(slab, "space", split_axis=3, concat_axis=2, tiled=True)
    length = moved.shape[2]
    local = moved.shape[3] // 2
    lines = moved.reshape(samples, channels, length, local, 2).transpose(0, 1, 3, 2, 4)
    lines = lines.reshape(samples, channels, local, 2 * length)
    spectra = jnp.dot(lines, table, preferred_element_type=jnp.float32).astype(jnp.bfloat16)
    spectra = spectra.reshape(samples, channels, local, modes_x, 2).transpose(2, 3, 0, 4, 1)
    return spectra.reshape(local * modes_x, samples, 2 * channels)


def to_slab(spectra, table, modes_x, channels):
    count, samples, doubled = spectra.shape
    local = count // modes_x
    lines = spectra.reshape(local, modes_x, samples, 2, channels).transpose(2, 4, 0, 1, 3)
    lines = lines.reshape(samples, channels, local, 2 * modes_x)
    lines = jnp.dot(lines, table, preferred_element_type=jnp.float32).astype(jnp.bfloat16)
    length = lines.shape[3] // 2
    lines = lines.reshape(samples, channels, local, length, 2).transpose(0, 1, 3, 2, 4)
    lines = lines.reshape(samples, channels, length, 2 * local)
    return lax.all_to_all(lines, "space", split_axis=2, concat_axis=3, tiled=True)


def to_owners(spectra):
    return lax.all_to_all(spectra, "dp", split_axis=0, concat_axis=1, tiled=True)


def from_owners(spectra):
    return lax.all_to_all(spectra, "dp", split_axis=1, concat_axis=0, tiled=True)


def gelu_slope(value):
    cdf = 0.5 * (1.0 + lax.erf(value * 0.7071067811865476))
    density = jnp.exp(-0.5 * value * value) * 0.3989422804014327
    return cdf + value * density


def general_body(activations, cotangent, mode_weights, pointwise, offsets):
    samples, channels, width, rows_y, rows_z = activations.shape
    plane_fwd, plane_inv = plane_tables(rows_y, rows_z, MY, MZ)
    line_fwd, line_inv = line_tables(NX, MX)
    flat = activations.reshape(samples, channels, width, rows_y * rows_z)
    planes = jnp.dot(flat, plane_fwd, preferred_element_type=jnp.float32).astype(jnp.bfloat16)
    spec_in = to_modes(planes, line_fwd, MX)
    blocks = expand_weights(mode_weights)
    held_in = to_owners(spec_in)
    held_out = jnp.einsum(
        "mbi,mio->mbo", held_in, blocks, preferred_element_type=jnp.float32
    ).astype(jnp.bfloat16)
    spec_out = from_owners(held_out)
    returned = to_slab(spec_out, line_inv, MX, channels)
    spectral = jnp.dot(returned, plane_inv, preferred_element_type=jnp.float32)
    local_part = jnp.einsum("io,bixn->boxn", pointwise, flat, preferred_element_type=jnp.float32)
    summed = spectral + local_part + offsets[None, :, None, None]
    upstream = cotangent.reshape(flat.shape).astype(jnp.float32)
    slope_grad = (upstream * gelu_slope(summed)).astype(jnp.bfloat16)
    back_plane = jnp.dot(slope_grad, plane_inv.T, preferred_element_type=jnp.float32).astype(
        jnp.bfloat16
    )
    spec_grad = to_modes(back_plane, line_inv.T, MX)
    held_grad = to_owners(spec_grad)
    held_dx = jnp.einsum(
        "mbo,mio->mbi", held_grad, blocks, preferred_element_type=jnp.float32
    ).astype(jnp.bfloat16)
    spec_dx = from_owners(held_dx)
    grad_spectral = weight_terms(held_in, held_grad)
    line_dx = to_slab(spec_dx, line_fwd.T, MX, channels)
    total = jnp.dot(line_dx, plane_fwd.T, preferred_element_type=jnp.float32)
    total = total + jnp.einsum(
        "io,boxn->bixn", pointwise, slope_grad, preferred_element_type=jnp.float32
    )
    grad_in = total.astype(jnp.bfloat16).reshape(activations.shape)
    return (grad_in, grad_spectral)


BF16 = jnp.bfloat16
F32 = jnp.float32
GROUP = 16
TILE = 8
SLOTS = 4
STEPS = GROUP // SLOTS
MIB = 1024 * 1024


def rounded(table):
    return np.asarray(table, np.float32).astype(ml_dtypes.bfloat16)


def angles(freq, points, length):
    phase = np.mod(np.outer(freq, points), length)
    return (phase * (2.0 * math.pi / length)).astype(np.float64)


def signed(count):
    index = np.arange(count)
    return np.where(index < count // 2, index, index - count)


def z_base(rows_z):
    theta = angles(np.arange(MZ), np.arange(rows_z), rows_z)
    pair = np.stack([np.cos(theta), -np.sin(theta)])
    table = np.repeat(pair.reshape(2 * MZ, rows_z), GROUP, axis=0).T
    return rounded(table).astype(np.float32)


def y_table(rows_y, width):
    theta = angles(signed(MY), np.arange(rows_y), rows_y)
    cosine, sine = np.cos(theta), np.sin(theta)
    turn = np.stack([np.stack([cosine, sine]), np.stack([-sine, cosine])])
    table = np.einsum("rsjy,xw->jxrswy", turn, np.eye(width))
    return rounded(table.reshape(MY * width * 2, 2 * width * rows_y))


def x_tables(samples, slabs, length):
    theta = angles(signed(MX), np.arange(length), length)
    cosine, sine = np.cos(theta), np.sin(theta)
    forward = np.stack([np.stack([cosine, sine]), np.stack([-sine, cosine])])
    inverse = np.stack([np.stack([cosine, sine]), np.stack([-sine, cosine])]) / length
    same = np.eye(samples)
    rows = MX * 2 * samples

    def lay(turn):
        turn = turn.reshape(2, 2, MX, slabs, length // slabs)
        table = np.einsum("arqsx,bd->qabdsxr", turn, same)
        return rounded(table.reshape(rows, samples * length * 2))

    return lay(forward), lay(inverse)


def dot(left, right):
    return jnp.dot(left, right, preferred_element_type=F32)


def doubled_slope(u):
    decay = jnp.exp2(u * u * -math.log2(math.e)).astype(BF16)
    cdf = (1.0 + lax.erf(u)).astype(BF16)
    return cdf + u.astype(BF16) * jnp.asarray(2.0 / math.sqrt(math.pi), BF16) * decay


def over(index, size):
    return lax.shift_right_logical(index, jnp.int32(size.bit_length() - 1))


def within(index, size):
    return jnp.bitwise_and(index, jnp.int32(size - 1))


def fill_z(base, table):
    rows_z, lanes = base.shape
    owner = within(lax.broadcasted_iota(jnp.int32, (rows_z, lanes), 1), GROUP)
    values = base[...]
    for c in range(GROUP):
        table[c * rows_z : (c + 1) * rows_z] = jnp.where(owner == c, values, 0.0).astype(BF16)


def fill_z_back(base, table):
    lanes, rows_z = base.shape
    owner = within(lax.broadcasted_iota(jnp.int32, (lanes, rows_z), 0), GROUP)
    values = base[...]
    for c in range(GROUP):
        first = c % SLOTS * rows_z
        table[c // SLOTS, :, first : first + rows_z] = jnp.where(owner == c, values, 0.0).astype(BF16)


def grouped(lane, per, channels):
    c = within(lane, channels)
    return over(c, GROUP) * (MZ * GROUP) + over(lane, channels) * GROUP + within(c, GROUP)


def fill_order(per, channels, back, table):
    count = table.shape[0]
    row = lax.broadcasted_iota(jnp.int32, (count, count), 0)
    column = lax.broadcasted_iota(jnp.int32, (count, count), 1)
    if back:
        same = grouped(row[:, :1], per, channels) == column
    else:
        same = row == grouped(column[:1], per, channels)
    table[...] = jnp.where(same, 1.0, 0.0).astype(BF16)


def turned_index(index, slabs, devices):
    samples = devices // slabs
    return index % samples * slabs + index // samples


def deliver(spectra, ytab, order, scale, message, per, channels, slabs):
    groups = channels // GROUP
    rows = spectra.shape[0] // groups
    wide = spectra.shape[1] // 2
    halves = []
    for r in range(2):
        blocks = [spectra[g * rows : (g + 1) * rows, r * wide : (r + 1) * wide] for g in range(groups)]
        halves.append(jnp.concatenate(blocks, axis=1).astype(BF16))
    planes = dot(ytab[...], jnp.concatenate(halves, axis=0))
    if scale is not None:
        planes = planes * scale[...]
    ordered = dot(planes.astype(BF16), order[...]).astype(BF16)
    parts = MZ // per
    count = message.shape[1]
    lanes = per * channels
    for part in range(parts):
        block = ordered[:, part * lanes : (part + 1) * lanes]
        for j in range(MY):
            message[turned_index(j * parts + part, slabs, message.shape[0])] = block[j * count : (j + 1) * count]


def receive(message, order_back, ytab_back, scale, held, per, slabs):
    parts = MZ // per
    lanes = [
        jnp.concatenate(
            [message[turned_index(j * parts + part, slabs, message.shape[0])] for j in range(MY)], axis=0
        )
        for part in range(parts)
    ]
    ordered = dot(jnp.concatenate(lanes, axis=1), order_back[...]).astype(BF16)
    lines = dot(ytab_back[...], ordered)
    if scale is not None:
        lines = lines * scale[...]
    lines = lines.astype(BF16)
    rows = lines.shape[0] // 2
    wide = MZ * GROUP
    for group in range(held.shape[0] // rows):
        piece = lines[:, group * wide : (group + 1) * wide]
        held[group * rows : (group + 1) * rows] = jnp.concatenate([piece[:rows], piece[rows:]], axis=1)


class Move:
    def __init__(self, source, target, sems):
        self.source, self.target, self.sems = source, target, sems

    def copy(self, step):
        run = pl.ds(step * SLOTS, SLOTS)
        return pltpu.make_async_copy(self.source.at[:, run], self.target.at[:, run], self.sems.at[step])

    def start(self, step):
        self.copy(step).start()

    def wait(self, step):
        self.copy(step).wait()


def start_all(moves, step):
    for each in moves:
        each.start(step)


def add_spectra(field, ztab, step, spectra):
    groups = field.shape[0]
    rows_z = field.shape[-1]
    depth = SLOTS * rows_z
    table = ztab[pl.ds(pl.multiple_of(step * depth, depth), depth)]
    lanes = [
        jnp.concatenate(
            [field[g, step * SLOTS + slot].reshape(-1, rows_z) for g in range(groups)], axis=0
        )
        for slot in range(SLOTS)
    ]
    spectra[...] += dot(jnp.concatenate(lanes, axis=1), table)


def plane_kernel(
    per, channels, slabs, field, base_far, ytab_far, message, ztab, order, spectra, buffer, base, ytab, sems, table_sems
):
    incoming = Move(field, buffer, sems)
    base_copy = pltpu.make_async_copy(base_far, base, table_sems.at[0])
    ytab_copy = pltpu.make_async_copy(ytab_far, ytab, table_sems.at[1])
    base_copy.start()
    incoming.start(0)
    fill_order(per, channels, False, order)
    spectra[...] = jnp.zeros_like(spectra)
    incoming.start(1)
    base_copy.wait()
    fill_z(base, ztab)
    incoming.start(2)
    ytab_copy.start()
    incoming.start(3)

    @pl.loop(0, STEPS)
    def _(step):
        incoming.wait(step)
        add_spectra(buffer, ztab, step, spectra)

    ytab_copy.wait()
    deliver(spectra, ytab, order, None, message, per, channels, slabs)


def slope_kernel(
    per, channels, slabs, arrived, local, cotangent, base, base_back, ytab, ytab_back, scale, scale_back,
    slope, message, ztab, ztab_back, order, held, spectra, local_in, cotangent_in, result, total,
    local_sems, cotangent_sems, result_sems,
):
    width, rows_y, rows_z = local.shape[2:]
    groups = channels // GROUP
    rows = width * rows_y
    wide = 2 * rows_y
    incoming = (Move(local, local_in, local_sems), Move(cotangent, cotangent_in, cotangent_sems))
    outgoing = Move(result, slope, result_sems)
    start_all(incoming, 0)
    fill_order(per, channels, True, order)
    receive(arrived, order, ytab_back, scale_back, held, per, slabs)
    start_all(incoming, 1)
    fill_z_back(base_back, ztab_back)
    fill_z(base, ztab)
    start_all(incoming, 2)
    fill_order(per, channels, False, order)
    spectra[...] = jnp.zeros_like(spectra)
    start_all(incoming, 3)

    @pl.loop(0, STEPS)
    def _(step):
        for each in incoming:
            each.wait(step)
        total[...] = dot(held[...], ztab_back[step])
        for g in range(groups):
            for slot in range(SLOTS):
                lanes = slice(slot * rows_z, (slot + 1) * rows_z)
                c = step * SLOTS + slot
                for x in range(0, width, 2):
                    place = g * rows + x * rows_y
                    value = total[place : place + wide, lanes]
                    value = value + local_in[g, c, x : x + 2].reshape(wide, rows_z).astype(F32)
                    upstream = cotangent_in[g, c, x : x + 2].reshape(wide, rows_z)
                    answer = upstream * doubled_slope(value)
                    result[g, c, x : x + 2] = answer.reshape(2, rows_y, rows_z)
        outgoing.start(step)
        add_spectra(result, ztab, step, spectra)

    deliver(spectra, ytab, order, scale, message, per, channels, slabs)
    for step in range(STEPS):
        outgoing.wait(step)


def field_kernel(
    per, channels, slabs, arrived, local, base_back, ytab_back, out, ztab_back, order, held, local_in, result,
    local_sems, result_sems,
):
    width, rows_y, rows_z = local.shape[2:]
    groups = channels // GROUP
    rows = width * rows_y
    incoming = Move(local, local_in, local_sems)
    outgoing = Move(result, out, result_sems)
    incoming.start(0)
    fill_order(per, channels, True, order)
    incoming.start(1)
    receive(arrived, order, ytab_back, None, held, per, slabs)
    incoming.start(2)
    fill_z_back(base_back, ztab_back)
    incoming.start(3)

    @pl.loop(0, STEPS)
    def _(step):
        incoming.wait(step)
        total = dot(held[...], ztab_back[step])
        for g in range(groups):
            for slot in range(SLOTS):
                lanes = slice(slot * rows_z, (slot + 1) * rows_z)
                c = step * SLOTS + slot
                value = total[g * rows : (g + 1) * rows, lanes]
                value = value + local_in[g, c].reshape(rows, rows_z).astype(F32)
                result[g, c] = value.astype(BF16).reshape(width, rows_y, rows_z)
        outgoing.start(step)

    for step in range(STEPS):
        outgoing.wait(step)


def pointwise_kernel(turned, field, mix, offsets, out, table, shift):
    channels = mix.shape[0]
    width, rows_y, rows_z = field.shape[1:]
    size = channels * TILE

    @pl.when(pl.program_id(0) == 0)
    def _():
        row = over(lax.broadcasted_iota(jnp.int32, (size, channels), 0), TILE)
        column = lax.broadcasted_iota(jnp.int32, (size, channels), 1)
        spread = jnp.where(row == column, 1.0, 0.0).astype(BF16)
        tall = lax.dot_general(
            spread, mix[...], (((1,), (1 if turned else 0,)), ((), ())), preferred_element_type=F32
        ).astype(BF16)
        whole = lax.dot_general(
            tall, spread, (((1,), (1,)), ((), ())), preferred_element_type=F32
        )
        place = within(lax.broadcasted_iota(jnp.int32, (size, size), 0), TILE)
        other = within(lax.broadcasted_iota(jnp.int32, (size, size), 1), TILE)
        table[...] = jnp.where(place == other, whole if turned else 0.5 * whole, 0.0).astype(BF16)
        if offsets is not None:
            for c in range(channels):
                shift[c] = jnp.full((1, rows_z), offsets[c], F32)

    for start in range(0, rows_y, 2 * TILE):
        pieces = [field[:, x, start : start + 2 * TILE, :].astype(F32) for x in range(width)]
        halves = []
        for row in range(0, 2 * TILE, TILE):
            rows = [piece[:, row : row + TILE].reshape(size, rows_z).astype(BF16) for piece in pieces]
            halves.append(dot(table[...], jnp.concatenate(rows, axis=1)))
        for x in range(width):
            values = [
                half[:, x * rows_z : (x + 1) * rows_z].reshape(channels, TILE, rows_z) for half in halves
            ]
            value = jnp.concatenate(values, axis=1)
            if offsets is not None:
                value = (value + shift[...]) * math.sqrt(0.5)
            out[:, x, start : start + 2 * TILE, :] = value.astype(BF16)


def spread_pair(first, second):
    nothing = jnp.zeros_like(first)
    upper = jnp.concatenate([first, nothing], axis=1)
    lower = jnp.concatenate([nothing, second], axis=1)
    return jnp.concatenate([upper, lower], axis=0)


def low_half(shape):
    return lax.broadcasted_iota(jnp.int32, shape, 1) < shape[1] // 2


def mix_kernel(per, samples, arrived, weights, line, line_back, spec_in, message, held):
    rows = 2 * samples
    lanes = 2 * weights.shape[1]
    low = low_half((samples, lanes))
    flat = arrived[...].reshape(-1, arrived.shape[2])
    spectra = dot(line[...], flat).astype(BF16)
    spec_in[...] = spectra
    for q in range(MX):
        for first in range(0, per, 2):
            block = spread_pair(weights[first * MX + q], weights[(first + 1) * MX + q])
            place = first // 2 * lanes
            terms = dot(spectra[q * rows : (q + 1) * rows, place : place + lanes], block)
            mixed = []
            for side in range(2):
                part = terms[:, side * lanes : (side + 1) * lanes]
                turned = pltpu.roll(part[samples:], lanes // 2, 1)
                mixed.append(part[:samples] + jnp.where(low, -turned, turned))
            real = jnp.where(low, mixed[0], pltpu.roll(mixed[1], lanes // 2, 1))
            imag = jnp.where(low, pltpu.roll(mixed[0], lanes // 2, 1), mixed[1])
            held[q * rows : (q + 1) * rows, place : place + lanes] = jnp.concatenate(
                [real, imag], axis=0
            ).astype(BF16)
    message[...] = dot(line_back[...], held[...]).astype(BF16).reshape(message.shape)


def mix_back_kernel(per, samples, arrived, weights, line, line_back, pairs, message, held):
    rows = 2 * samples
    lanes = 2 * weights.shape[1]
    low = low_half((samples, lanes))
    first_lanes = jnp.where(low_half((lanes, lanes)), 1.0, 0.0).astype(BF16)
    second_lanes = jnp.where(low_half((lanes, lanes)), 0.0, 1.0).astype(BF16)
    flat = arrived[...].reshape(-1, arrived.shape[2])
    spectra = dot(line[...], flat).astype(BF16).astype(F32)
    for q in range(MX):
        for first in range(0, per, 2):
            both = jnp.concatenate([weights[first * MX + q], weights[(first + 1) * MX + q]], axis=0).T
            block = jnp.concatenate([both * first_lanes, both * second_lanes], axis=0)
            place = first // 2 * lanes
            real = spectra[q * rows : q * rows + samples, place : place + lanes]
            imag = spectra[q * rows + samples : (q + 1) * rows, place : place + lanes]
            real_turned = pltpu.roll(real, lanes // 2, 1)
            imag_turned = pltpu.roll(imag, lanes // 2, 1)
            left = [jnp.where(low, real, imag_turned), jnp.where(low, imag, -real_turned)]
            right = [jnp.where(low, real_turned, imag), jnp.where(low, imag_turned, -real)]
            pair = jnp.concatenate(
                [jnp.concatenate(left, axis=0), jnp.concatenate(right, axis=0)], axis=1
            ).astype(BF16)
            pairs[q * rows : (q + 1) * rows, 2 * place : 2 * (place + lanes)] = pair
            held[q * rows : (q + 1) * rows, place : place + lanes] = dot(pair, block).astype(BF16)
    message[...] = dot(line_back[...], held[...]).astype(BF16).reshape(message.shape)


def weight_kernel(per, samples, spec_in, pairs, out):
    rows = 2 * samples
    lanes = out.shape[2]
    half = lanes // 2
    for q in range(MX):
        for first in range(0, per, 2):
            place = first // 2 * lanes
            left = spec_in[q * rows : (q + 1) * rows, place : place + lanes]
            right = pairs[q * rows : (q + 1) * rows, 2 * place : 2 * (place + lanes)]
            outer = lax.dot_general(
                left, right, (((0,), (0,)), ((), ())), preferred_element_type=F32
            )
            out[first * MX + q] = outer[:half, :lanes]
            out[(first + 1) * MX + q] = outer[half:, lanes:]


def whole(array):
    return pl.BlockSpec(array.shape, lambda *step: (0,) * len(array.shape))


def shaped(shape, dtype):
    return jax.ShapeDtypeStruct(shape, dtype)


def params(mib):
    return pltpu.CompilerParams(vmem_limit_bytes=mib * MIB)


def cost(flops, moved, steep=0):
    return pl.CostEstimate(flops=flops, bytes_accessed=moved, transcendentals=steep)


def body(mesh_axes, devices, slabs, activations, cotangent, mode_weights, pointwise, offsets):
    _, channels, width, rows_y, rows_z = activations.shape
    samples = devices // slabs
    per = MY * MZ // devices
    groups = channels // GROUP
    field = activations.shape[1:]
    count = math.prod(field)
    base = z_base(rows_z)
    ytab = y_table(rows_y, width)
    line_fwd, line_inv = x_tables(samples, slabs, NX)
    weight = np.where(np.arange(MZ) == 0, 1.0, 2.0) / (rows_y * rows_z)
    scale = np.tile(np.repeat(weight, GROUP), groups)[None]
    scale, scale_t = (0.5 * scale).astype(np.float32), (math.sqrt(0.5) * scale).astype(np.float32)
    base_t, ytab_t = (np.ascontiguousarray(t.T) for t in (base, ytab))
    fwd_t, inv_t = (np.ascontiguousarray(t.T) for t in (line_fwd, line_inv))
    message = shaped((devices, 2 * width, per * channels), BF16)
    spectra = shaped((MX * 2 * samples, per * channels), BF16)
    ztab = pltpu.VMEM((GROUP * rows_z, 2 * MZ * GROUP), BF16)
    ztab_t = pltpu.VMEM((STEPS, 2 * MZ * GROUP, SLOTS * rows_z), BF16)
    order = pltpu.VMEM((MZ * channels, MZ * channels), BF16)
    rows = groups * width * rows_y
    held = pltpu.VMEM((rows, 2 * MZ * GROUP), BF16)
    sums = pltpu.VMEM((rows, 2 * MZ * GROUP), F32)
    slot_sums = pltpu.VMEM((rows, SLOTS * rows_z), F32)
    grouped_field = (groups, GROUP) + field[1:]
    buffer = pltpu.VMEM(grouped_field, BF16)
    sems = pltpu.SemaphoreType.DMA((STEPS,))
    far = pl.BlockSpec(memory_space=pltpu.HBM)
    far_field = pltpu.HBM(field, BF16)

    def kept_far(array):
        return pltpu.with_memory_space_constraint(array, pltpu.HBM)

    plane_flops = 2 * count * 2 * MZ * GROUP

    def exchange(array):
        return lax.all_to_all(array, mesh_axes, split_axis=0, concat_axis=0, tiled=True)

    def mix_points(values, turned, shifts):
        step = 2
        block = pl.BlockSpec((channels, step, rows_y, rows_z), lambda x: (0, x, 0, 0))
        kernel = functools.partial(pointwise_kernel, turned)
        specs = [block, whole(pointwise)]
        operands = [values, pointwise]
        if shifts is None:
            run = lambda a, b, *rest: kernel(a, b, None, *rest)
        else:
            run = kernel
            specs.append(pl.BlockSpec(memory_space=pltpu.SMEM))
            operands.append(shifts)
        return pl.pallas_call(
            run,
            grid=(width // step,),
            in_specs=specs,
            out_specs=block,
            out_shape=far_field,
            scratch_shapes=[
                pltpu.VMEM((channels * TILE, channels * TILE), BF16),
                pltpu.VMEM((channels, 1, rows_z), F32),
            ],
            compiler_params=params(32),
            cost_estimate=cost(2 * count * channels * TILE, 4 * count),
        )(*operands)

    planes = pl.pallas_call(
        functools.partial(plane_kernel, per, channels, slabs),
        in_specs=[far, far, far],
        out_specs=whole(message),
        out_shape=message,
        scratch_shapes=[
            ztab,
            order,
            sums,
            buffer,
            pltpu.VMEM(base.shape, F32),
            pltpu.VMEM(ytab.shape, BF16),
            sems,
            pltpu.SemaphoreType.DMA((2,)),
        ],
        compiler_params=params(32),
        cost_estimate=cost(plane_flops, 2 * count),
    )(kept_far(activations.reshape(grouped_field)), kept_far(base), kept_far(ytab))
    arrived = exchange(planes)
    local = mix_points(kept_far(activations.reshape(field)), True, offsets)
    arrived, local = lax.optimization_barrier((arrived, local))
    spec_in, mixed = pl.pallas_call(
        functools.partial(mix_kernel, per, samples),
        out_shape=(spectra, message),
        scratch_shapes=[pltpu.VMEM(spectra.shape, BF16)],
        compiler_params=params(16),
        cost_estimate=cost(10**8, 2 * mode_weights.size),
    )(arrived, mode_weights, line_fwd, inv_t)
    returned = exchange(mixed)
    slope, back_plane = pl.pallas_call(
        functools.partial(slope_kernel, per, channels, slabs),
        in_specs=[whole(message), far, far]
        + [whole(t) for t in (base, base_t, ytab, ytab_t, scale, scale_t)],
        out_specs=(far, whole(message)),
        out_shape=(pltpu.HBM(grouped_field, BF16), message),
        scratch_shapes=[ztab, ztab_t, order, held, sums]
        + [buffer] * 3
        + [slot_sums]
        + [sems] * 3,
        compiler_params=params(40),
        cost_estimate=cost(2 * plane_flops, 6 * count, 2 * count),
    )(returned, kept_far(local.reshape(grouped_field)), kept_far(cotangent.reshape(grouped_field)), base, base_t, ytab, ytab_t, scale, scale_t)
    arrived_back = exchange(back_plane)
    local_back = mix_points(kept_far(slope.reshape(field)), False, None)
    arrived_back, local_back = lax.optimization_barrier((arrived_back, local_back))
    pairs, mixed_back = pl.pallas_call(
        functools.partial(mix_back_kernel, per, samples),
        out_shape=(shaped((spectra.shape[0], 2 * spectra.shape[1]), BF16), message),
        scratch_shapes=[pltpu.VMEM(spectra.shape, BF16)],
        compiler_params=params(16),
        cost_estimate=cost(10**8, 2 * mode_weights.size),
    )(arrived_back, mode_weights, line_inv, fwd_t)
    returned_back = exchange(mixed_back)
    grad_spectral = pl.pallas_call(
        functools.partial(weight_kernel, per, samples),
        out_shape=shaped(mode_weights.shape, F32),
        compiler_params=params(16),
        cost_estimate=cost(10**8, 4 * mode_weights.size),
    )(spec_in, pairs)
    grad_in = pl.pallas_call(
        functools.partial(field_kernel, per, channels, slabs),
        in_specs=[whole(message), far, whole(base_t), whole(ytab_t)],
        out_specs=far,
        out_shape=shaped(grouped_field, BF16),
        scratch_shapes=[ztab_t, order, held, buffer, buffer, sems, sems],
        compiler_params=params(32),
        cost_estimate=cost(plane_flops, 4 * count),
    )(returned_back, kept_far(local_back.reshape(grouped_field)), base_t, ytab_t)
    return (grad_in.reshape(activations.shape), grad_spectral)


def chosen_body(mesh_axes, devices, slabs, activations, cotangent, mode_weights, pointwise, offsets):
    samples, channels, width, rows_y, rows_z = activations.shape
    per = MY * MZ // devices
    fits = (
        samples == 1
        and MY * MZ % devices == 0
        and per in (2, 4, 8)
        and width % 8 == 0
        and channels == 64
        and rows_y % TILE == 0
        and rows_z == 128
    )
    plan = functools.partial(body, mesh_axes, devices, slabs) if fits else general_body
    return plan(activations, cotangent, mode_weights, pointwise, offsets)


def solution(mesh):
    slabs = mesh.shape["space"]
    devices = slabs * mesh.shape["dp"]
    return jax.shard_map(
        functools.partial(chosen_body, ("dp", "space"), devices, slabs),
        mesh=mesh,
        in_specs=(
            P("dp", None, "space", None, None),
            P("dp", None, "space", None, None),
            P(("space", "dp"), None, None),
            P(),
            P(),
        ),
        out_specs=(P("dp", None, "space", None, None), P(("space", "dp"), None, None)),
        check_vma=False,
    )
```

```python
import functools
import math

import jax
import jax.numpy as jnp
import ml_dtypes
import numpy as np
from jax import lax
from jax.experimental import pallas as pl
from jax.experimental.pallas import tpu as pltpu
from jax.sharding import PartitionSpec as P

MX = 16
MY = 16
MZ = 8
NX = 32


def centered(count):
    index = jnp.arange(count, dtype=jnp.int32)
    return jnp.where(index < count // 2, index, index - count)


def plane_tables(rows_y, rows_z, modes_y, modes_z):
    along_y = jnp.arange(rows_y, dtype=jnp.int32)[:, None, None, None]
    along_z = jnp.arange(rows_z, dtype=jnp.int32)[None, :, None, None]
    freq_y = centered(modes_y)[None, None, :, None]
    freq_z = jnp.arange(modes_z, dtype=jnp.int32)[None, None, None, :]
    phase = jnp.mod(freq_y * along_y * rows_z + freq_z * along_z * rows_y, rows_y * rows_z)
    theta = phase.astype(jnp.float32) * (2.0 * math.pi / (rows_y * rows_z))
    cosine = jnp.cos(theta)
    sine = jnp.sin(theta)
    forward = jnp.stack([cosine, -sine], -1).reshape(rows_y * rows_z, modes_y * modes_z * 2)
    scaled = jnp.where(freq_z == 0, 1.0, 2.0).astype(jnp.float32) / (rows_y * rows_z)
    inverse = (
        jnp.stack([cosine * scaled, -sine * scaled], -1)
        .reshape(rows_y * rows_z, modes_y * modes_z * 2)
        .T
    )
    return (forward.astype(jnp.bfloat16), inverse.astype(jnp.bfloat16))


def line_tables(length, modes):
    along = jnp.arange(length, dtype=jnp.int32)[:, None]
    freq = centered(modes)[None, :]
    phase = jnp.mod(freq * along, length)
    theta = phase.astype(jnp.float32) * (2.0 * math.pi / length)
    cosine = jnp.cos(theta)
    sine = jnp.sin(theta)
    first = jnp.stack([cosine, -sine], -1)
    second = jnp.stack([sine, cosine], -1)
    forward = jnp.stack([first, second], 1).reshape(2 * length, 2 * modes)
    inv_first = jnp.stack([cosine.T, sine.T], -1) / length
    inv_second = jnp.stack([-sine.T, cosine.T], -1) / length
    inverse = jnp.stack([inv_first, inv_second], 1).reshape(2 * modes, 2 * length)
    return (forward.astype(jnp.bfloat16), inverse.astype(jnp.bfloat16))


def expand_weights(weights):
    half = weights.shape[1]
    real_part = weights[:, :, :half]
    imag_part = weights[:, :, half:]
    upper = jnp.concatenate([real_part, imag_part], axis=2)
    lower = jnp.concatenate([-imag_part, real_part], axis=2)
    return jnp.concatenate([upper, lower], axis=1)


def outer_sum(left, right):
    return jnp.einsum("mbi,mbo->mio", left, right, preferred_element_type=jnp.float32)


def weight_terms(spec_in, spec_grad):
    half = spec_in.shape[2] // 2
    in_real = spec_in[:, :, :half]
    in_imag = spec_in[:, :, half:]
    gr_real = spec_grad[:, :, :half]
    gr_imag = spec_grad[:, :, half:]
    real_term = outer_sum(in_real, gr_real) + outer_sum(in_imag, gr_imag)
    imag_term = outer_sum(in_real, gr_imag) - outer_sum(in_imag, gr_real)
    return jnp.concatenate([real_term, imag_term], axis=2)


def to_modes(slab, table, modes_x):
    samples, channels, width, pairs = slab.shape
    moved = lax.all_to_all(slab, "space", split_axis=3, concat_axis=2, tiled=True)
    length = moved.shape[2]
    local = moved.shape[3] // 2
    lines = moved.reshape(samples, channels, length, local, 2).transpose(0, 1, 3, 2, 4)
    lines = lines.reshape(samples, channels, local, 2 * length)
    spectra = jnp.dot(lines, table, preferred_element_type=jnp.float32).astype(jnp.bfloat16)
    spectra = spectra.reshape(samples, channels, local, modes_x, 2).transpose(2, 3, 0, 4, 1)
    return spectra.reshape(local * modes_x, samples, 2 * channels)


def to_slab(spectra, table, modes_x, channels):
    count, samples, doubled = spectra.shape
    local = count // modes_x
    lines = spectra.reshape(local, modes_x, samples, 2, channels).transpose(2, 4, 0, 1, 3)
    lines = lines.reshape(samples, channels, local, 2 * modes_x)
    lines = jnp.dot(lines, table, preferred_element_type=jnp.float32).astype(jnp.bfloat16)
    length = lines.shape[3] // 2
    lines = lines.reshape(samples, channels, local, length, 2).transpose(0, 1, 3, 2, 4)
    lines = lines.reshape(samples, channels, length, 2 * local)
    return lax.all_to_all(lines, "space", split_axis=2, concat_axis=3, tiled=True)


def to_owners(spectra):
    return lax.all_to_all(spectra, "dp", split_axis=0, concat_axis=1, tiled=True)


def from_owners(spectra):
    return lax.all_to_all(spectra, "dp", split_axis=1, concat_axis=0, tiled=True)


def gelu_slope(value):
    cdf = 0.5 * (1.0 + lax.erf(value * 0.7071067811865476))
    density = jnp.exp(-0.5 * value * value) * 0.3989422804014327
    return cdf + value * density


def general_body(activations, cotangent, mode_weights, pointwise, offsets):
    samples, channels, width, rows_y, rows_z = activations.shape
    plane_fwd, plane_inv = plane_tables(rows_y, rows_z, MY, MZ)
    line_fwd, line_inv = line_tables(NX, MX)
    flat = activations.reshape(samples, channels, width, rows_y * rows_z)
    planes = jnp.dot(flat, plane_fwd, preferred_element_type=jnp.float32).astype(jnp.bfloat16)
    spec_in = to_modes(planes, line_fwd, MX)
    blocks = expand_weights(mode_weights)
    held_in = to_owners(spec_in)
    held_out = jnp.einsum(
        "mbi,mio->mbo", held_in, blocks, preferred_element_type=jnp.float32
    ).astype(jnp.bfloat16)
    spec_out = from_owners(held_out)
    returned = to_slab(spec_out, line_inv, MX, channels)
    spectral = jnp.dot(returned, plane_inv, preferred_element_type=jnp.float32)
    local_part = jnp.einsum("io,bixn->boxn", pointwise, flat, preferred_element_type=jnp.float32)
    summed = spectral + local_part + offsets[None, :, None, None]
    upstream = cotangent.reshape(flat.shape).astype(jnp.float32)
    slope_grad = (upstream * gelu_slope(summed)).astype(jnp.bfloat16)
    back_plane = jnp.dot(slope_grad, plane_inv.T, preferred_element_type=jnp.float32).astype(
        jnp.bfloat16
    )
    spec_grad = to_modes(back_plane, line_inv.T, MX)
    held_grad = to_owners(spec_grad)
    held_dx = jnp.einsum(
        "mbo,mio->mbi", held_grad, blocks, preferred_element_type=jnp.float32
    ).astype(jnp.bfloat16)
    spec_dx = from_owners(held_dx)
    grad_spectral = weight_terms(held_in, held_grad)
    line_dx = to_slab(spec_dx, line_fwd.T, MX, channels)
    total = jnp.dot(line_dx, plane_fwd.T, preferred_element_type=jnp.float32)
    total = total + jnp.einsum(
        "io,boxn->bixn", pointwise, slope_grad, preferred_element_type=jnp.float32
    )
    grad_in = total.astype(jnp.bfloat16).reshape(activations.shape)
    return (grad_in, grad_spectral)


BF16 = jnp.bfloat16
F32 = jnp.float32
GROUP = 16
TILE = 8
SLOTS = 4
STEPS = GROUP // SLOTS
MIB = 1024 * 1024


def rounded(table):
    return np.asarray(table, np.float32).astype(ml_dtypes.bfloat16)


def angles(freq, points, length):
    phase = np.mod(np.outer(freq, points), length)
    return (phase * (2.0 * math.pi / length)).astype(np.float64)


def signed(count):
    index = np.arange(count)
    return np.where(index < count // 2, index, index - count)


def z_base(rows_z):
    theta = angles(np.arange(MZ), np.arange(rows_z), rows_z)
    pair = np.stack([np.cos(theta), -np.sin(theta)])
    table = np.repeat(pair.reshape(2 * MZ, rows_z), GROUP, axis=0).T
    return rounded(table).astype(np.float32)


def y_table(rows_y, width):
    theta = angles(signed(MY), np.arange(rows_y), rows_y)
    cosine, sine = np.cos(theta), np.sin(theta)
    turn = np.stack([np.stack([cosine, sine]), np.stack([-sine, cosine])])
    table = np.einsum("rsjy,xw->jxrswy", turn, np.eye(width))
    return rounded(table.reshape(MY * width * 2, 2 * width * rows_y))


def x_tables(samples, slabs, length):
    theta = angles(signed(MX), np.arange(length), length)
    cosine, sine = np.cos(theta), np.sin(theta)
    forward = np.stack([np.stack([cosine, sine]), np.stack([-sine, cosine])])
    inverse = np.stack([np.stack([cosine, sine]), np.stack([-sine, cosine])]) / length
    same = np.eye(samples)
    rows = MX * 2 * samples

    def lay(turn):
        turn = turn.reshape(2, 2, MX, slabs, length // slabs)
        table = np.einsum("arqsx,bd->qabdsxr", turn, same)
        return rounded(table.reshape(rows, samples * length * 2))

    return lay(forward), lay(inverse)


def dot(left, right):
    return jnp.dot(left, right, preferred_element_type=F32)


def doubled_slope(u):
    decay = jnp.exp2(u * u * -math.log2(math.e)).astype(BF16)
    cdf = (1.0 + lax.erf(u)).astype(BF16)
    return cdf + u.astype(BF16) * jnp.asarray(2.0 / math.sqrt(math.pi), BF16) * decay


def over(index, size):
    return lax.shift_right_logical(index, jnp.int32(size.bit_length() - 1))


def within(index, size):
    return jnp.bitwise_and(index, jnp.int32(size - 1))


def fill_z(base, table):
    rows_z, lanes = base.shape
    owner = within(lax.broadcasted_iota(jnp.int32, (rows_z, lanes), 1), GROUP)
    values = base[...]
    for c in range(GROUP):
        table[c * rows_z : (c + 1) * rows_z] = jnp.where(owner == c, values, 0.0).astype(BF16)


def fill_z_back(base, table):
    lanes, rows_z = base.shape
    owner = within(lax.broadcasted_iota(jnp.int32, (lanes, rows_z), 0), GROUP)
    values = base[...]
    for c in range(GROUP):
        first = c % SLOTS * rows_z
        table[c // SLOTS, :, first : first + rows_z] = jnp.where(owner == c, values, 0.0).astype(BF16)


def grouped(lane, per, channels):
    c = within(lane, channels)
    return over(c, GROUP) * (MZ * GROUP) + over(lane, channels) * GROUP + within(c, GROUP)


def fill_order(per, channels, back, table):
    count = table.shape[0]
    row = lax.broadcasted_iota(jnp.int32, (count, count), 0)
    column = lax.broadcasted_iota(jnp.int32, (count, count), 1)
    if back:
        same = grouped(row[:, :1], per, channels) == column
    else:
        same = row == grouped(column[:1], per, channels)
    table[...] = jnp.where(same, 1.0, 0.0).astype(BF16)


def turned_index(index, slabs, devices):
    samples = devices // slabs
    return index % samples * slabs + index // samples


def deliver(spectra, ytab, order, scale, message, per, channels, slabs):
    groups = channels // GROUP
    rows = spectra.shape[0] // groups
    wide = spectra.shape[1] // 2
    halves = []
    for r in range(2):
        blocks = [spectra[g * rows : (g + 1) * rows, r * wide : (r + 1) * wide] for g in range(groups)]
        halves.append(jnp.concatenate(blocks, axis=1).astype(BF16))
    planes = dot(ytab[...], jnp.concatenate(halves, axis=0))
    if scale is not None:
        planes = planes * scale[...]
    ordered = dot(planes.astype(BF16), order[...]).astype(BF16)
    parts = MZ // per
    count = message.shape[1]
    lanes = per * channels
    for part in range(parts):
        block = ordered[:, part * lanes : (part + 1) * lanes]
        for j in range(MY):
            message[turned_index(j * parts + part, slabs, message.shape[0])] = block[j * count : (j + 1) * count]


def receive(message, order_back, ytab_back, scale, held, per, slabs):
    parts = MZ // per
    lanes = [
        jnp.concatenate(
            [message[turned_index(j * parts + part, slabs, message.shape[0])] for j in range(MY)], axis=0
        )
        for part in range(parts)
    ]
    ordered = dot(jnp.concatenate(lanes, axis=1), order_back[...]).astype(BF16)
    lines = dot(ytab_back[...], ordered)
    if scale is not None:
        lines = lines * scale[...]
    lines = lines.astype(BF16)
    rows = lines.shape[0] // 2
    wide = MZ * GROUP
    for group in range(held.shape[0] // rows):
        piece = lines[:, group * wide : (group + 1) * wide]
        held[group * rows : (group + 1) * rows] = jnp.concatenate([piece[:rows], piece[rows:]], axis=1)


class Move:
    def __init__(self, source, target, sems):
        self.source, self.target, self.sems = source, target, sems

    def copy(self, step):
        run = pl.ds(step * SLOTS, SLOTS)
        return pltpu.make_async_copy(self.source.at[:, run], self.target.at[:, run], self.sems.at[step])

    def start(self, step):
        self.copy(step).start()

    def wait(self, step):
        self.copy(step).wait()


class GroupMove(Move):
    def copy(self, step, g):
        run = pl.ds(step * SLOTS, SLOTS)
        sem = self.sems.at[step * self.target.shape[0] + g]
        return pltpu.make_async_copy(self.source.at[g, run], self.target.at[g, run], sem)

    def start(self, step):
        for g in range(self.target.shape[0]):
            self.copy(step, g).start()

    def wait(self, step):
        for g in range(self.target.shape[0]):
            self.copy(step, g).wait()


def start_all(moves, step):
    for each in moves:
        each.start(step)


def add_spectra(field, ztab, step, spectra):
    groups = field.shape[0]
    rows_z = field.shape[-1]
    depth = SLOTS * rows_z
    table = ztab[pl.ds(pl.multiple_of(step * depth, depth), depth)]
    lanes = [
        jnp.concatenate(
            [field[g, step * SLOTS + slot].reshape(-1, rows_z) for g in range(groups)], axis=0
        )
        for slot in range(SLOTS)
    ]
    spectra[...] += dot(jnp.concatenate(lanes, axis=1), table)


def plane_kernel(
    per, channels, slabs, field, base_far, ytab_far, message, ztab, order, spectra, buffer, base, ytab, sems, table_sems
):
    incoming = Move(field, buffer, sems)
    base_copy = pltpu.make_async_copy(base_far, base, table_sems.at[0])
    ytab_copy = pltpu.make_async_copy(ytab_far, ytab, table_sems.at[1])
    base_copy.start()
    incoming.start(0)
    fill_order(per, channels, False, order)
    spectra[...] = jnp.zeros_like(spectra)
    incoming.start(1)
    base_copy.wait()
    fill_z(base, ztab)
    incoming.start(2)
    ytab_copy.start()
    incoming.start(3)

    @pl.loop(0, STEPS)
    def _(step):
        incoming.wait(step)
        add_spectra(buffer, ztab, step, spectra)

    ytab_copy.wait()
    deliver(spectra, ytab, order, None, message, per, channels, slabs)


def slope_kernel(
    per, channels, slabs, arrived, local, cotangent, base, base_back, ytab, ytab_back, scale, scale_back,
    slope, message, ztab, ztab_back, order, held, spectra, local_in, cotangent_in, result, total,
    local_sems, cotangent_sems, result_sems,
):
    width, rows_y, rows_z = local.shape[2:]
    groups = channels // GROUP
    rows = width * rows_y
    wide = 2 * rows_y
    incoming = (GroupMove(local, local_in, local_sems), GroupMove(cotangent, cotangent_in, cotangent_sems))
    outgoing = GroupMove(result, slope, result_sems)
    start_all(incoming, 0)
    fill_order(per, channels, True, order)
    receive(arrived, order, ytab_back, scale_back, held, per, slabs)
    start_all(incoming, 1)
    fill_z_back(base_back, ztab_back)
    fill_z(base, ztab)
    start_all(incoming, 2)
    fill_order(per, channels, False, order)
    spectra[...] = jnp.zeros_like(spectra)
    start_all(incoming, 3)

    @pl.loop(0, STEPS)
    def _(step):
        for each in incoming:
            each.wait(step)
        total[...] = dot(held[...], ztab_back[step])
        for g in range(groups):
            for slot in range(SLOTS):
                lanes = slice(slot * rows_z, (slot + 1) * rows_z)
                c = step * SLOTS + slot
                for x in range(0, width, 2):
                    place = g * rows + x * rows_y
                    value = total[place : place + wide, lanes]
                    value = value + local_in[g, c, x : x + 2].reshape(wide, rows_z).astype(F32)
                    upstream = cotangent_in[g, c, x : x + 2].reshape(wide, rows_z)
                    answer = upstream * doubled_slope(value)
                    result[g, c, x : x + 2] = answer.reshape(2, rows_y, rows_z)
            outgoing.copy(step, g).start()
        add_spectra(result, ztab, step, spectra)

    deliver(spectra, ytab, order, scale, message, per, channels, slabs)
    for step in range(STEPS):
        outgoing.wait(step)


def field_kernel(
    per, channels, slabs, arrived, local, base_back, ytab_back, out, ztab_back, order, held, local_in, result,
    local_sems, result_sems,
):
    width, rows_y, rows_z = local.shape[2:]
    groups = channels // GROUP
    rows = width * rows_y
    incoming = Move(local, local_in, local_sems)
    outgoing = Move(result, out, result_sems)
    incoming.start(0)
    fill_order(per, channels, True, order)
    incoming.start(1)
    receive(arrived, order, ytab_back, None, held, per, slabs)
    incoming.start(2)
    fill_z_back(base_back, ztab_back)
    incoming.start(3)

    @pl.loop(0, STEPS)
    def _(step):
        incoming.wait(step)
        total = dot(held[...], ztab_back[step])
        for g in range(groups):
            for slot in range(SLOTS):
                lanes = slice(slot * rows_z, (slot + 1) * rows_z)
                c = step * SLOTS + slot
                value = total[g * rows : (g + 1) * rows, lanes]
                value = value + local_in[g, c].reshape(rows, rows_z).astype(F32)
                result[g, c] = value.astype(BF16).reshape(width, rows_y, rows_z)
        outgoing.start(step)

    for step in range(STEPS):
        outgoing.wait(step)


def pointwise_kernel(turned, field, mix, offsets, out, table, shift):
    channels = mix.shape[0]
    width, rows_y, rows_z = field.shape[1:]
    size = channels * TILE

    @pl.when(pl.program_id(0) == 0)
    def _():
        row = over(lax.broadcasted_iota(jnp.int32, (size, channels), 0), TILE)
        column = lax.broadcasted_iota(jnp.int32, (size, channels), 1)
        spread = jnp.where(row == column, 1.0, 0.0).astype(BF16)
        tall = lax.dot_general(
            spread, mix[...], (((1,), (1 if turned else 0,)), ((), ())), preferred_element_type=F32
        ).astype(BF16)
        whole = lax.dot_general(
            tall, spread, (((1,), (1,)), ((), ())), preferred_element_type=F32
        )
        place = within(lax.broadcasted_iota(jnp.int32, (size, size), 0), TILE)
        other = within(lax.broadcasted_iota(jnp.int32, (size, size), 1), TILE)
        table[...] = jnp.where(place == other, whole if turned else 0.5 * whole, 0.0).astype(BF16)
        if offsets is not None:
            for c in range(channels):
                shift[c] = jnp.full((1, rows_z), offsets[c], F32)

    for start in range(0, rows_y, 2 * TILE):
        pieces = [field[:, x, start : start + 2 * TILE, :].astype(F32) for x in range(width)]
        halves = []
        for row in range(0, 2 * TILE, TILE):
            rows = [piece[:, row : row + TILE].reshape(size, rows_z).astype(BF16) for piece in pieces]
            halves.append(dot(table[...], jnp.concatenate(rows, axis=1)))
        for x in range(width):
            values = [
                half[:, x * rows_z : (x + 1) * rows_z].reshape(channels, TILE, rows_z) for half in halves
            ]
            value = jnp.concatenate(values, axis=1)
            if offsets is not None:
                value = (value + shift[...]) * math.sqrt(0.5)
            out[:, x, start : start + 2 * TILE, :] = value.astype(BF16)


def spread_pair(first, second):
    nothing = jnp.zeros_like(first)
    upper = jnp.concatenate([first, nothing], axis=1)
    lower = jnp.concatenate([nothing, second], axis=1)
    return jnp.concatenate([upper, lower], axis=0)


def low_half(shape):
    return lax.broadcasted_iota(jnp.int32, shape, 1) < shape[1] // 2


def mix_kernel(per, samples, arrived, weights, line, line_back, spec_in, message, held):
    rows = 2 * samples
    lanes = 2 * weights.shape[1]
    low = low_half((samples, lanes))
    flat = arrived[...].reshape(-1, arrived.shape[2])
    spectra = dot(line[...], flat).astype(BF16)
    spec_in[...] = spectra
    for q in range(MX):
        for first in range(0, per, 2):
            block = spread_pair(weights[first * MX + q], weights[(first + 1) * MX + q])
            place = first // 2 * lanes
            terms = dot(spectra[q * rows : (q + 1) * rows, place : place + lanes], block)
            mixed = []
            for side in range(2):
                part = terms[:, side * lanes : (side + 1) * lanes]
                turned = pltpu.roll(part[samples:], lanes // 2, 1)
                mixed.append(part[:samples] + jnp.where(low, -turned, turned))
            real = jnp.where(low, mixed[0], pltpu.roll(mixed[1], lanes // 2, 1))
            imag = jnp.where(low, pltpu.roll(mixed[0], lanes // 2, 1), mixed[1])
            held[q * rows : (q + 1) * rows, place : place + lanes] = jnp.concatenate(
                [real, imag], axis=0
            ).astype(BF16)
    message[...] = dot(line_back[...], held[...]).astype(BF16).reshape(message.shape)


def mix_back_kernel(per, samples, arrived, weights, line, line_back, pairs, message, held):
    rows = 2 * samples
    lanes = 2 * weights.shape[1]
    low = low_half((samples, lanes))
    first_lanes = jnp.where(low_half((lanes, lanes)), 1.0, 0.0).astype(BF16)
    second_lanes = jnp.where(low_half((lanes, lanes)), 0.0, 1.0).astype(BF16)
    flat = arrived[...].reshape(-1, arrived.shape[2])
    spectra = dot(line[...], flat).astype(BF16).astype(F32)
    for q in range(MX):
        for first in range(0, per, 2):
            both = jnp.concatenate([weights[first * MX + q], weights[(first + 1) * MX + q]], axis=0).T
            block = jnp.concatenate([both * first_lanes, both * second_lanes], axis=0)
            place = first // 2 * lanes
            real = spectra[q * rows : q * rows + samples, place : place + lanes]
            imag = spectra[q * rows + samples : (q + 1) * rows, place : place + lanes]
            real_turned = pltpu.roll(real, lanes // 2, 1)
            imag_turned = pltpu.roll(imag, lanes // 2, 1)
            left = [jnp.where(low, real, imag_turned), jnp.where(low, imag, -real_turned)]
            right = [jnp.where(low, real_turned, imag), jnp.where(low, imag_turned, -real)]
            pair = jnp.concatenate(
                [jnp.concatenate(left, axis=0), jnp.concatenate(right, axis=0)], axis=1
            ).astype(BF16)
            pairs[q * rows : (q + 1) * rows, 2 * place : 2 * (place + lanes)] = pair
            held[q * rows : (q + 1) * rows, place : place + lanes] = dot(pair, block).astype(BF16)
    message[...] = dot(line_back[...], held[...]).astype(BF16).reshape(message.shape)


def weight_kernel(per, samples, spec_in, pairs, out):
    rows = 2 * samples
    lanes = out.shape[2]
    half = lanes // 2
    for q in range(MX):
        for first in range(0, per, 2):
            place = first // 2 * lanes
            left = spec_in[q * rows : (q + 1) * rows, place : place + lanes]
            right = pairs[q * rows : (q + 1) * rows, 2 * place : 2 * (place + lanes)]
            outer = lax.dot_general(
                left, right, (((0,), (0,)), ((), ())), preferred_element_type=F32
            )
            out[first * MX + q] = outer[:half, :lanes]
            out[(first + 1) * MX + q] = outer[half:, lanes:]


def whole(array):
    return pl.BlockSpec(array.shape, lambda *step: (0,) * len(array.shape))


def shaped(shape, dtype):
    return jax.ShapeDtypeStruct(shape, dtype)


def params(mib):
    return pltpu.CompilerParams(vmem_limit_bytes=mib * MIB)


def cost(flops, moved, steep=0):
    return pl.CostEstimate(flops=flops, bytes_accessed=moved, transcendentals=steep)


def body(mesh_axes, devices, slabs, activations, cotangent, mode_weights, pointwise, offsets):
    _, channels, width, rows_y, rows_z = activations.shape
    samples = devices // slabs
    per = MY * MZ // devices
    groups = channels // GROUP
    field = activations.shape[1:]
    count = math.prod(field)
    base = z_base(rows_z)
    ytab = y_table(rows_y, width)
    line_fwd, line_inv = x_tables(samples, slabs, NX)
    weight = np.where(np.arange(MZ) == 0, 1.0, 2.0) / (rows_y * rows_z)
    scale = np.tile(np.repeat(weight, GROUP), groups)[None]
    scale, scale_t = (0.5 * scale).astype(np.float32), (math.sqrt(0.5) * scale).astype(np.float32)
    base_t, ytab_t = (np.ascontiguousarray(t.T) for t in (base, ytab))
    fwd_t, inv_t = (np.ascontiguousarray(t.T) for t in (line_fwd, line_inv))
    message = shaped((devices, 2 * width, per * channels), BF16)
    spectra = shaped((MX * 2 * samples, per * channels), BF16)
    ztab = pltpu.VMEM((GROUP * rows_z, 2 * MZ * GROUP), BF16)
    ztab_t = pltpu.VMEM((STEPS, 2 * MZ * GROUP, SLOTS * rows_z), BF16)
    order = pltpu.VMEM((MZ * channels, MZ * channels), BF16)
    rows = groups * width * rows_y
    held = pltpu.VMEM((rows, 2 * MZ * GROUP), BF16)
    sums = pltpu.VMEM((rows, 2 * MZ * GROUP), F32)
    slot_sums = pltpu.VMEM((rows, SLOTS * rows_z), F32)
    grouped_field = (groups, GROUP) + field[1:]
    buffer = pltpu.VMEM(grouped_field, BF16)
    sems = pltpu.SemaphoreType.DMA((STEPS,))
    group_sems = pltpu.SemaphoreType.DMA((STEPS * groups,))
    far = pl.BlockSpec(memory_space=pltpu.HBM)
    far_field = pltpu.HBM(field, BF16)

    def kept_far(array):
        return pltpu.with_memory_space_constraint(array, pltpu.HBM)

    plane_flops = 2 * count * 2 * MZ * GROUP

    def exchange(array):
        return lax.all_to_all(array, mesh_axes, split_axis=0, concat_axis=0, tiled=True)

    def mix_points(values, turned, shifts):
        step = 2
        block = pl.BlockSpec((channels, step, rows_y, rows_z), lambda x: (0, x, 0, 0))
        kernel = functools.partial(pointwise_kernel, turned)
        specs = [block, whole(pointwise)]
        operands = [values, pointwise]
        if shifts is None:
            run = lambda a, b, *rest: kernel(a, b, None, *rest)
        else:
            run = kernel
            specs.append(pl.BlockSpec(memory_space=pltpu.SMEM))
            operands.append(shifts)
        return pl.pallas_call(
            run,
            grid=(width // step,),
            in_specs=specs,
            out_specs=block,
            out_shape=far_field,
            scratch_shapes=[
                pltpu.VMEM((channels * TILE, channels * TILE), BF16),
                pltpu.VMEM((channels, 1, rows_z), F32),
            ],
            compiler_params=params(32),
            cost_estimate=cost(2 * count * channels * TILE, 4 * count),
        )(*operands)

    planes = pl.pallas_call(
        functools.partial(plane_kernel, per, channels, slabs),
        in_specs=[far, far, far],
        out_specs=whole(message),
        out_shape=message,
        scratch_shapes=[
            ztab,
            order,
            sums,
            buffer,
            pltpu.VMEM(base.shape, F32),
            pltpu.VMEM(ytab.shape, BF16),
            sems,
            pltpu.SemaphoreType.DMA((2,)),
        ],
        compiler_params=params(32),
        cost_estimate=cost(plane_flops, 2 * count),
    )(kept_far(activations.reshape(grouped_field)), kept_far(base), kept_far(ytab))
    arrived = exchange(planes)
    local = mix_points(kept_far(activations.reshape(field)), True, offsets)
    arrived, local = lax.optimization_barrier((arrived, local))
    spec_in, mixed = pl.pallas_call(
        functools.partial(mix_kernel, per, samples),
        out_shape=(spectra, message),
        scratch_shapes=[pltpu.VMEM(spectra.shape, BF16)],
        compiler_params=params(16),
        cost_estimate=cost(10**8, 2 * mode_weights.size),
    )(arrived, mode_weights, line_fwd, inv_t)
    returned = exchange(mixed)
    slope, back_plane = pl.pallas_call(
        functools.partial(slope_kernel, per, channels, slabs),
        in_specs=[whole(message), far, far]
        + [whole(t) for t in (base, base_t, ytab, ytab_t, scale, scale_t)],
        out_specs=(far, whole(message)),
        out_shape=(pltpu.HBM(grouped_field, BF16), message),
        scratch_shapes=[ztab, ztab_t, order, held, sums]
        + [buffer] * 3
        + [slot_sums]
        + [group_sems] * 3,
        compiler_params=params(40),
        cost_estimate=cost(2 * plane_flops, 6 * count, 2 * count),
    )(returned, kept_far(local.reshape(grouped_field)), kept_far(cotangent.reshape(grouped_field)), base, base_t, ytab, ytab_t, scale, scale_t)
    arrived_back = exchange(back_plane)
    local_back = mix_points(kept_far(slope.reshape(field)), False, None)
    arrived_back, local_back = lax.optimization_barrier((arrived_back, local_back))
    pairs, mixed_back = pl.pallas_call(
        functools.partial(mix_back_kernel, per, samples),
        out_shape=(shaped((spectra.shape[0], 2 * spectra.shape[1]), BF16), message),
        scratch_shapes=[pltpu.VMEM(spectra.shape, BF16)],
        compiler_params=params(16),
        cost_estimate=cost(10**8, 2 * mode_weights.size),
    )(arrived_back, mode_weights, line_inv, fwd_t)
    returned_back = exchange(mixed_back)
    grad_spectral = pl.pallas_call(
        functools.partial(weight_kernel, per, samples),
        out_shape=shaped(mode_weights.shape, F32),
        compiler_params=params(16),
        cost_estimate=cost(10**8, 4 * mode_weights.size),
    )(spec_in, pairs)
    grad_in = pl.pallas_call(
        functools.partial(field_kernel, per, channels, slabs),
        in_specs=[whole(message), far, whole(base_t), whole(ytab_t)],
        out_specs=far,
        out_shape=shaped(grouped_field, BF16),
        scratch_shapes=[ztab_t, order, held, buffer, buffer, sems, sems],
        compiler_params=params(32),
        cost_estimate=cost(plane_flops, 4 * count),
    )(returned_back, kept_far(local_back.reshape(grouped_field)), base_t, ytab_t)
    return (grad_in.reshape(activations.shape), grad_spectral)


def chosen_body(mesh_axes, devices, slabs, activations, cotangent, mode_weights, pointwise, offsets):
    samples, channels, width, rows_y, rows_z = activations.shape
    per = MY * MZ // devices
    fits = (
        samples == 1
        and MY * MZ % devices == 0
        and per in (2, 4, 8)
        and width % 8 == 0
        and channels == 64
        and rows_y % TILE == 0
        and rows_z == 128
    )
    plan = functools.partial(body, mesh_axes, devices, slabs) if fits else general_body
    return plan(activations, cotangent, mode_weights, pointwise, offsets)


def solution(mesh):
    slabs = mesh.shape["space"]
    devices = slabs * mesh.shape["dp"]
    return jax.shard_map(
        functools.partial(chosen_body, ("dp", "space"), devices, slabs),
        mesh=mesh,
        in_specs=(
            P("dp", None, "space", None, None),
            P("dp", None, "space", None, None),
            P(("space", "dp"), None, None),
            P(),
            P(),
        ),
        out_specs=(P("dp", None, "space", None, None), P(("space", "dp"), None, None)),
        check_vma=False,
    )
```

```python
import functools
import math

import jax
import jax.numpy as jnp
import ml_dtypes
import numpy as np
from jax import lax
from jax.experimental import pallas as pl
from jax.experimental.pallas import tpu as pltpu
from jax.sharding import PartitionSpec as P

MX = 16
MY = 16
MZ = 8
NX = 32


def centered(count):
    index = jnp.arange(count, dtype=jnp.int32)
    return jnp.where(index < count // 2, index, index - count)


def plane_tables(rows_y, rows_z, modes_y, modes_z):
    along_y = jnp.arange(rows_y, dtype=jnp.int32)[:, None, None, None]
    along_z = jnp.arange(rows_z, dtype=jnp.int32)[None, :, None, None]
    freq_y = centered(modes_y)[None, None, :, None]
    freq_z = jnp.arange(modes_z, dtype=jnp.int32)[None, None, None, :]
    phase = jnp.mod(freq_y * along_y * rows_z + freq_z * along_z * rows_y, rows_y * rows_z)
    theta = phase.astype(jnp.float32) * (2.0 * math.pi / (rows_y * rows_z))
    cosine = jnp.cos(theta)
    sine = jnp.sin(theta)
    forward = jnp.stack([cosine, -sine], -1).reshape(rows_y * rows_z, modes_y * modes_z * 2)
    scaled = jnp.where(freq_z == 0, 1.0, 2.0).astype(jnp.float32) / (rows_y * rows_z)
    inverse = (
        jnp.stack([cosine * scaled, -sine * scaled], -1)
        .reshape(rows_y * rows_z, modes_y * modes_z * 2)
        .T
    )
    return (forward.astype(jnp.bfloat16), inverse.astype(jnp.bfloat16))


def line_tables(length, modes):
    along = jnp.arange(length, dtype=jnp.int32)[:, None]
    freq = centered(modes)[None, :]
    phase = jnp.mod(freq * along, length)
    theta = phase.astype(jnp.float32) * (2.0 * math.pi / length)
    cosine = jnp.cos(theta)
    sine = jnp.sin(theta)
    first = jnp.stack([cosine, -sine], -1)
    second = jnp.stack([sine, cosine], -1)
    forward = jnp.stack([first, second], 1).reshape(2 * length, 2 * modes)
    inv_first = jnp.stack([cosine.T, sine.T], -1) / length
    inv_second = jnp.stack([-sine.T, cosine.T], -1) / length
    inverse = jnp.stack([inv_first, inv_second], 1).reshape(2 * modes, 2 * length)
    return (forward.astype(jnp.bfloat16), inverse.astype(jnp.bfloat16))


def expand_weights(weights):
    half = weights.shape[1]
    real_part = weights[:, :, :half]
    imag_part = weights[:, :, half:]
    upper = jnp.concatenate([real_part, imag_part], axis=2)
    lower = jnp.concatenate([-imag_part, real_part], axis=2)
    return jnp.concatenate([upper, lower], axis=1)


def outer_sum(left, right):
    return jnp.einsum("mbi,mbo->mio", left, right, preferred_element_type=jnp.float32)


def weight_terms(spec_in, spec_grad):
    half = spec_in.shape[2] // 2
    in_real = spec_in[:, :, :half]
    in_imag = spec_in[:, :, half:]
    gr_real = spec_grad[:, :, :half]
    gr_imag = spec_grad[:, :, half:]
    real_term = outer_sum(in_real, gr_real) + outer_sum(in_imag, gr_imag)
    imag_term = outer_sum(in_real, gr_imag) - outer_sum(in_imag, gr_real)
    return jnp.concatenate([real_term, imag_term], axis=2)


def to_modes(slab, table, modes_x):
    samples, channels, width, pairs = slab.shape
    moved = lax.all_to_all(slab, "space", split_axis=3, concat_axis=2, tiled=True)
    length = moved.shape[2]
    local = moved.shape[3] // 2
    lines = moved.reshape(samples, channels, length, local, 2).transpose(0, 1, 3, 2, 4)
    lines = lines.reshape(samples, channels, local, 2 * length)
    spectra = jnp.dot(lines, table, preferred_element_type=jnp.float32).astype(jnp.bfloat16)
    spectra = spectra.reshape(samples, channels, local, modes_x, 2).transpose(2, 3, 0, 4, 1)
    return spectra.reshape(local * modes_x, samples, 2 * channels)


def to_slab(spectra, table, modes_x, channels):
    count, samples, doubled = spectra.shape
    local = count // modes_x
    lines = spectra.reshape(local, modes_x, samples, 2, channels).transpose(2, 4, 0, 1, 3)
    lines = lines.reshape(samples, channels, local, 2 * modes_x)
    lines = jnp.dot(lines, table, preferred_element_type=jnp.float32).astype(jnp.bfloat16)
    length = lines.shape[3] // 2
    lines = lines.reshape(samples, channels, local, length, 2).transpose(0, 1, 3, 2, 4)
    lines = lines.reshape(samples, channels, length, 2 * local)
    return lax.all_to_all(lines, "space", split_axis=2, concat_axis=3, tiled=True)


def to_owners(spectra):
    return lax.all_to_all(spectra, "dp", split_axis=0, concat_axis=1, tiled=True)


def from_owners(spectra):
    return lax.all_to_all(spectra, "dp", split_axis=1, concat_axis=0, tiled=True)


def gelu_slope(value):
    cdf = 0.5 * (1.0 + lax.erf(value * 0.7071067811865476))
    density = jnp.exp(-0.5 * value * value) * 0.3989422804014327
    return cdf + value * density


def general_body(activations, cotangent, mode_weights, pointwise, offsets):
    samples, channels, width, rows_y, rows_z = activations.shape
    plane_fwd, plane_inv = plane_tables(rows_y, rows_z, MY, MZ)
    line_fwd, line_inv = line_tables(NX, MX)
    flat = activations.reshape(samples, channels, width, rows_y * rows_z)
    planes = jnp.dot(flat, plane_fwd, preferred_element_type=jnp.float32).astype(jnp.bfloat16)
    spec_in = to_modes(planes, line_fwd, MX)
    blocks = expand_weights(mode_weights)
    held_in = to_owners(spec_in)
    held_out = jnp.einsum(
        "mbi,mio->mbo", held_in, blocks, preferred_element_type=jnp.float32
    ).astype(jnp.bfloat16)
    spec_out = from_owners(held_out)
    returned = to_slab(spec_out, line_inv, MX, channels)
    spectral = jnp.dot(returned, plane_inv, preferred_element_type=jnp.float32)
    local_part = jnp.einsum("io,bixn->boxn", pointwise, flat, preferred_element_type=jnp.float32)
    summed = spectral + local_part + offsets[None, :, None, None]
    upstream = cotangent.reshape(flat.shape).astype(jnp.float32)
    slope_grad = (upstream * gelu_slope(summed)).astype(jnp.bfloat16)
    back_plane = jnp.dot(slope_grad, plane_inv.T, preferred_element_type=jnp.float32).astype(
        jnp.bfloat16
    )
    spec_grad = to_modes(back_plane, line_inv.T, MX)
    held_grad = to_owners(spec_grad)
    held_dx = jnp.einsum(
        "mbo,mio->mbi", held_grad, blocks, preferred_element_type=jnp.float32
    ).astype(jnp.bfloat16)
    spec_dx = from_owners(held_dx)
    grad_spectral = weight_terms(held_in, held_grad)
    line_dx = to_slab(spec_dx, line_fwd.T, MX, channels)
    total = jnp.dot(line_dx, plane_fwd.T, preferred_element_type=jnp.float32)
    total = total + jnp.einsum(
        "io,boxn->bixn", pointwise, slope_grad, preferred_element_type=jnp.float32
    )
    grad_in = total.astype(jnp.bfloat16).reshape(activations.shape)
    return (grad_in, grad_spectral)


BF16 = jnp.bfloat16
F32 = jnp.float32
GROUP = 16
TILE = 8
SLOTS = 4
STEPS = GROUP // SLOTS
MIB = 1024 * 1024


def rounded(table):
    return np.asarray(table, np.float32).astype(ml_dtypes.bfloat16)


def angles(freq, points, length):
    phase = np.mod(np.outer(freq, points), length)
    return (phase * (2.0 * math.pi / length)).astype(np.float64)


def signed(count):
    index = np.arange(count)
    return np.where(index < count // 2, index, index - count)


def z_base(rows_z):
    theta = angles(np.arange(MZ), np.arange(rows_z), rows_z)
    pair = np.stack([np.cos(theta), -np.sin(theta)])
    table = np.repeat(pair.reshape(2 * MZ, rows_z), GROUP, axis=0).T
    return rounded(table).astype(np.float32)


def y_table(rows_y, width):
    theta = angles(signed(MY), np.arange(rows_y), rows_y)
    cosine, sine = np.cos(theta), np.sin(theta)
    turn = np.stack([np.stack([cosine, sine]), np.stack([-sine, cosine])])
    table = np.einsum("rsjy,xw->jxrswy", turn, np.eye(width))
    return rounded(table.reshape(MY * width * 2, 2 * width * rows_y))


def x_tables(samples, slabs, length):
    theta = angles(signed(MX), np.arange(length), length)
    cosine, sine = np.cos(theta), np.sin(theta)
    forward = np.stack([np.stack([cosine, sine]), np.stack([-sine, cosine])])
    inverse = np.stack([np.stack([cosine, sine]), np.stack([-sine, cosine])]) / length
    same = np.eye(samples)
    rows = MX * 2 * samples

    def lay(turn):
        turn = turn.reshape(2, 2, MX, slabs, length // slabs)
        table = np.einsum("arqsx,bd->qabdsxr", turn, same)
        return rounded(table.reshape(rows, samples * length * 2))

    return lay(forward), lay(inverse)


def dot(left, right):
    return jnp.dot(left, right, preferred_element_type=F32)


def doubled_slope(u):
    decay = jnp.exp2(u * u * -math.log2(math.e)).astype(BF16)
    cdf = (1.0 + lax.erf(u)).astype(BF16)
    return cdf + u.astype(BF16) * jnp.asarray(2.0 / math.sqrt(math.pi), BF16) * decay


def over(index, size):
    return lax.shift_right_logical(index, jnp.int32(size.bit_length() - 1))


def within(index, size):
    return jnp.bitwise_and(index, jnp.int32(size - 1))


def fill_z(base, table):
    rows_z, lanes = base.shape
    owner = within(lax.broadcasted_iota(jnp.int32, (rows_z, lanes), 1), GROUP)
    values = base[...]
    for c in range(GROUP):
        table[c * rows_z : (c + 1) * rows_z] = jnp.where(owner == c, values, 0.0).astype(BF16)


def fill_z_back(base, table):
    lanes, rows_z = base.shape
    owner = within(lax.broadcasted_iota(jnp.int32, (lanes, rows_z), 0), GROUP)
    values = base[...]
    for c in range(GROUP):
        first = c % SLOTS * rows_z
        table[c // SLOTS, :, first : first + rows_z] = jnp.where(owner == c, values, 0.0).astype(BF16)


def grouped(lane, per, channels):
    c = within(lane, channels)
    return over(c, GROUP) * (MZ * GROUP) + over(lane, channels) * GROUP + within(c, GROUP)


def fill_order(per, channels, back, table):
    count = table.shape[0]
    row = lax.broadcasted_iota(jnp.int32, (count, count), 0)
    column = lax.broadcasted_iota(jnp.int32, (count, count), 1)
    if back:
        same = grouped(row[:, :1], per, channels) == column
    else:
        same = row == grouped(column[:1], per, channels)
    table[...] = jnp.where(same, 1.0, 0.0).astype(BF16)


def turned_index(index, slabs, devices):
    samples = devices // slabs
    return index % samples * slabs + index // samples


def deliver(spectra, ytab, order, scale, message, per, channels, slabs):
    groups = channels // GROUP
    rows = spectra.shape[0] // groups
    wide = spectra.shape[1] // 2
    halves = []
    for r in range(2):
        blocks = [spectra[g * rows : (g + 1) * rows, r * wide : (r + 1) * wide] for g in range(groups)]
        halves.append(jnp.concatenate(blocks, axis=1).astype(BF16))
    planes = dot(ytab[...], jnp.concatenate(halves, axis=0))
    if scale is not None:
        planes = planes * scale[...]
    ordered = dot(planes.astype(BF16), order[...]).astype(BF16)
    parts = MZ // per
    count = message.shape[1]
    lanes = per * channels
    for part in range(parts):
        block = ordered[:, part * lanes : (part + 1) * lanes]
        for j in range(MY):
            message[turned_index(j * parts + part, slabs, message.shape[0])] = block[j * count : (j + 1) * count]


def receive(message, order_back, ytab_back, scale, held, per, slabs):
    parts = MZ // per
    lanes = [
        jnp.concatenate(
            [message[turned_index(j * parts + part, slabs, message.shape[0])] for j in range(MY)], axis=0
        )
        for part in range(parts)
    ]
    ordered = dot(jnp.concatenate(lanes, axis=1), order_back[...]).astype(BF16)
    lines = dot(ytab_back[...], ordered)
    if scale is not None:
        lines = lines * scale[...]
    lines = lines.astype(BF16)
    rows = lines.shape[0] // 2
    wide = MZ * GROUP
    for group in range(held.shape[0] // rows):
        piece = lines[:, group * wide : (group + 1) * wide]
        held[group * rows : (group + 1) * rows] = jnp.concatenate([piece[:rows], piece[rows:]], axis=1)


class Move:
    def __init__(self, source, target, sems):
        self.source, self.target, self.sems = source, target, sems

    def copy(self, step):
        run = pl.ds(step * SLOTS, SLOTS)
        return pltpu.make_async_copy(self.source.at[:, run], self.target.at[:, run], self.sems.at[step])

    def start(self, step):
        self.copy(step).start()

    def wait(self, step):
        self.copy(step).wait()


class GroupMove(Move):
    def copy(self, step, g):
        run = pl.ds(step * SLOTS, SLOTS)
        sem = self.sems.at[step * self.target.shape[0] + g]
        return pltpu.make_async_copy(self.source.at[g, run], self.target.at[g, run], sem)

    def start(self, step):
        for g in range(self.target.shape[0]):
            self.copy(step, g).start()

    def wait(self, step):
        for g in range(self.target.shape[0]):
            self.copy(step, g).wait()


def start_all(moves, step):
    for each in moves:
        each.start(step)


def add_spectra(field, ztab, step, spectra):
    groups = field.shape[0]
    rows_z = field.shape[-1]
    depth = SLOTS * rows_z
    table = ztab[pl.ds(pl.multiple_of(step * depth, depth), depth)]
    lanes = [
        jnp.concatenate(
            [field[g, step * SLOTS + slot].reshape(-1, rows_z) for g in range(groups)], axis=0
        )
        for slot in range(SLOTS)
    ]
    spectra[...] += dot(jnp.concatenate(lanes, axis=1), table)


def plane_kernel(
    per, channels, slabs, field, base_far, ytab_far, message, ztab, order, spectra, buffer, base, ytab, sems, table_sems
):
    incoming = Move(field, buffer, sems)
    base_copy = pltpu.make_async_copy(base_far, base, table_sems.at[0])
    ytab_copy = pltpu.make_async_copy(ytab_far, ytab, table_sems.at[1])
    base_copy.start()
    incoming.start(0)
    fill_order(per, channels, False, order)
    spectra[...] = jnp.zeros_like(spectra)
    incoming.start(1)
    base_copy.wait()
    fill_z(base, ztab)
    incoming.start(2)
    ytab_copy.start()
    incoming.start(3)

    @pl.loop(0, STEPS)
    def _(step):
        incoming.wait(step)
        add_spectra(buffer, ztab, step, spectra)

    ytab_copy.wait()
    deliver(spectra, ytab, order, None, message, per, channels, slabs)


def slope_kernel(
    per, channels, slabs, arrived, local, cotangent, base, base_back, ytab, ytab_back, scale, scale_back,
    slope, message, ztab, ztab_back, order, held, spectra, local_in, cotangent_in, result, total,
    local_sems, cotangent_sems, result_sems,
):
    width, rows_y, rows_z = local.shape[2:]
    groups = channels // GROUP
    rows = width * rows_y
    incoming = (GroupMove(local, local_in, local_sems), GroupMove(cotangent, cotangent_in, cotangent_sems))
    outgoing = GroupMove(result, slope, result_sems)
    start_all(incoming, 0)
    fill_order(per, channels, True, order)
    receive(arrived, order, ytab_back, scale_back, held, per, slabs)
    start_all(incoming, 1)
    fill_z_back(base_back, ztab_back)
    fill_z(base, ztab)
    start_all(incoming, 2)
    fill_order(per, channels, False, order)
    spectra[...] = jnp.zeros_like(spectra)
    start_all(incoming, 3)

    @pl.loop(0, STEPS)
    def _(step):
        for each in incoming:
            each.wait(step)
        total[...] = dot(held[...], ztab_back[step])
        for g in range(groups):
            for slot in range(SLOTS):
                lanes = slice(slot * rows_z, (slot + 1) * rows_z)
                c = step * SLOTS + slot
                for x in range(width):
                    place = g * rows + x * rows_y
                    value = total[place : place + rows_y, lanes]
                    value = value + local_in[g, c, x].astype(F32)
                    upstream = cotangent_in[g, c, x]
                    answer = upstream * doubled_slope(value)
                    result[g, c, x] = answer
            outgoing.copy(step, g).start()
        add_spectra(result, ztab, step, spectra)

    deliver(spectra, ytab, order, scale, message, per, channels, slabs)
    for step in range(STEPS):
        outgoing.wait(step)


def field_kernel(
    per, channels, slabs, arrived, local, base_back, ytab_back, out, ztab_back, order, held, local_in, result,
    local_sems, result_sems,
):
    width, rows_y, rows_z = local.shape[2:]
    groups = channels // GROUP
    rows = width * rows_y
    incoming = Move(local, local_in, local_sems)
    outgoing = Move(result, out, result_sems)
    incoming.start(0)
    fill_order(per, channels, True, order)
    incoming.start(1)
    receive(arrived, order, ytab_back, None, held, per, slabs)
    incoming.start(2)
    fill_z_back(base_back, ztab_back)
    incoming.start(3)

    @pl.loop(0, STEPS)
    def _(step):
        incoming.wait(step)
        total = dot(held[...], ztab_back[step])
        for g in range(groups):
            for slot in range(SLOTS):
                lanes = slice(slot * rows_z, (slot + 1) * rows_z)
                c = step * SLOTS + slot
                value = total[g * rows : (g + 1) * rows, lanes]
                value = value + local_in[g, c].reshape(rows, rows_z).astype(F32)
                result[g, c] = value.astype(BF16).reshape(width, rows_y, rows_z)
        outgoing.start(step)

    for step in range(STEPS):
        outgoing.wait(step)


def pointwise_kernel(turned, field, mix, offsets, out, table, shift):
    channels = mix.shape[0]
    width, rows_y, rows_z = field.shape[1:]
    size = channels * TILE

    @pl.when(pl.program_id(0) == 0)
    def _():
        row = over(lax.broadcasted_iota(jnp.int32, (size, channels), 0), TILE)
        column = lax.broadcasted_iota(jnp.int32, (size, channels), 1)
        spread = jnp.where(row == column, 1.0, 0.0).astype(BF16)
        tall = lax.dot_general(
            spread, mix[...], (((1,), (1 if turned else 0,)), ((), ())), preferred_element_type=F32
        ).astype(BF16)
        whole = lax.dot_general(
            tall, spread, (((1,), (1,)), ((), ())), preferred_element_type=F32
        )
        place = within(lax.broadcasted_iota(jnp.int32, (size, size), 0), TILE)
        other = within(lax.broadcasted_iota(jnp.int32, (size, size), 1), TILE)
        table[...] = jnp.where(place == other, whole if turned else 0.5 * whole, 0.0).astype(BF16)
        if offsets is not None:
            for c in range(channels):
                shift[c] = jnp.full((1, rows_z), offsets[c], F32)

    for start in range(0, rows_y, 2 * TILE):
        pieces = [field[:, x, start : start + 2 * TILE, :].astype(F32) for x in range(width)]
        halves = []
        for row in range(0, 2 * TILE, TILE):
            rows = [piece[:, row : row + TILE].reshape(size, rows_z).astype(BF16) for piece in pieces]
            halves.append(dot(table[...], jnp.concatenate(rows, axis=1)))
        for x in range(width):
            values = [
                half[:, x * rows_z : (x + 1) * rows_z].reshape(channels, TILE, rows_z) for half in halves
            ]
            value = jnp.concatenate(values, axis=1)
            if offsets is not None:
                value = (value + shift[...]) * math.sqrt(0.5)
            out[:, x, start : start + 2 * TILE, :] = value.astype(BF16)


def spread_pair(first, second):
    nothing = jnp.zeros_like(first)
    upper = jnp.concatenate([first, nothing], axis=1)
    lower = jnp.concatenate([nothing, second], axis=1)
    return jnp.concatenate([upper, lower], axis=0)


def low_half(shape):
    return lax.broadcasted_iota(jnp.int32, shape, 1) < shape[1] // 2


def mix_kernel(per, samples, arrived, weights, line, line_back, spec_in, message, held):
    rows = 2 * samples
    lanes = 2 * weights.shape[1]
    low = low_half((samples, lanes))
    flat = arrived[...].reshape(-1, arrived.shape[2])
    spectra = dot(line[...], flat).astype(BF16)
    spec_in[...] = spectra
    for q in range(MX):
        for first in range(0, per, 2):
            block = spread_pair(weights[first * MX + q], weights[(first + 1) * MX + q])
            place = first // 2 * lanes
            terms = dot(spectra[q * rows : (q + 1) * rows, place : place + lanes], block)
            mixed = []
            for side in range(2):
                part = terms[:, side * lanes : (side + 1) * lanes]
                turned = pltpu.roll(part[samples:], lanes // 2, 1)
                mixed.append(part[:samples] + jnp.where(low, -turned, turned))
            real = jnp.where(low, mixed[0], pltpu.roll(mixed[1], lanes // 2, 1))
            imag = jnp.where(low, pltpu.roll(mixed[0], lanes // 2, 1), mixed[1])
            held[q * rows : (q + 1) * rows, place : place + lanes] = jnp.concatenate(
                [real, imag], axis=0
            ).astype(BF16)
    message[...] = dot(line_back[...], held[...]).astype(BF16).reshape(message.shape)


def mix_back_kernel(per, samples, arrived, weights, line, line_back, pairs, message, held):
    rows = 2 * samples
    lanes = 2 * weights.shape[1]
    low = low_half((samples, lanes))
    first_lanes = jnp.where(low_half((lanes, lanes)), 1.0, 0.0).astype(BF16)
    second_lanes = jnp.where(low_half((lanes, lanes)), 0.0, 1.0).astype(BF16)
    flat = arrived[...].reshape(-1, arrived.shape[2])
    spectra = dot(line[...], flat).astype(BF16).astype(F32)
    for q in range(MX):
        for first in range(0, per, 2):
            both = jnp.concatenate([weights[first * MX + q], weights[(first + 1) * MX + q]], axis=0).T
            block = jnp.concatenate([both * first_lanes, both * second_lanes], axis=0)
            place = first // 2 * lanes
            real = spectra[q * rows : q * rows + samples, place : place + lanes]
            imag = spectra[q * rows + samples : (q + 1) * rows, place : place + lanes]
            real_turned = pltpu.roll(real, lanes // 2, 1)
            imag_turned = pltpu.roll(imag, lanes // 2, 1)
            left = [jnp.where(low, real, imag_turned), jnp.where(low, imag, -real_turned)]
            right = [jnp.where(low, real_turned, imag), jnp.where(low, imag_turned, -real)]
            pair = jnp.concatenate(
                [jnp.concatenate(left, axis=0), jnp.concatenate(right, axis=0)], axis=1
            ).astype(BF16)
            pairs[q * rows : (q + 1) * rows, 2 * place : 2 * (place + lanes)] = pair
            held[q * rows : (q + 1) * rows, place : place + lanes] = dot(pair, block).astype(BF16)
    message[...] = dot(line_back[...], held[...]).astype(BF16).reshape(message.shape)


def weight_kernel(per, samples, spec_in, pairs, out):
    rows = 2 * samples
    lanes = out.shape[2]
    half = lanes // 2
    for q in range(MX):
        for first in range(0, per, 2):
            place = first // 2 * lanes
            left = spec_in[q * rows : (q + 1) * rows, place : place + lanes]
            right = pairs[q * rows : (q + 1) * rows, 2 * place : 2 * (place + lanes)]
            outer = lax.dot_general(
                left, right, (((0,), (0,)), ((), ())), preferred_element_type=F32
            )
            out[first * MX + q] = outer[:half, :lanes]
            out[(first + 1) * MX + q] = outer[half:, lanes:]


def whole(array):
    return pl.BlockSpec(array.shape, lambda *step: (0,) * len(array.shape))


def shaped(shape, dtype):
    return jax.ShapeDtypeStruct(shape, dtype)


def params(mib):
    return pltpu.CompilerParams(vmem_limit_bytes=mib * MIB)


def cost(flops, moved, steep=0):
    return pl.CostEstimate(flops=flops, bytes_accessed=moved, transcendentals=steep)


def body(mesh_axes, devices, slabs, activations, cotangent, mode_weights, pointwise, offsets):
    _, channels, width, rows_y, rows_z = activations.shape
    samples = devices // slabs
    per = MY * MZ // devices
    groups = channels // GROUP
    field = activations.shape[1:]
    count = math.prod(field)
    base = z_base(rows_z)
    ytab = y_table(rows_y, width)
    line_fwd, line_inv = x_tables(samples, slabs, NX)
    weight = np.where(np.arange(MZ) == 0, 1.0, 2.0) / (rows_y * rows_z)
    scale = np.tile(np.repeat(weight, GROUP), groups)[None]
    scale, scale_t = (0.5 * scale).astype(np.float32), (math.sqrt(0.5) * scale).astype(np.float32)
    base_t, ytab_t = (np.ascontiguousarray(t.T) for t in (base, ytab))
    fwd_t, inv_t = (np.ascontiguousarray(t.T) for t in (line_fwd, line_inv))
    message = shaped((devices, 2 * width, per * channels), BF16)
    spectra = shaped((MX * 2 * samples, per * channels), BF16)
    ztab = pltpu.VMEM((GROUP * rows_z, 2 * MZ * GROUP), BF16)
    ztab_t = pltpu.VMEM((STEPS, 2 * MZ * GROUP, SLOTS * rows_z), BF16)
    order = pltpu.VMEM((MZ * channels, MZ * channels), BF16)
    rows = groups * width * rows_y
    held = pltpu.VMEM((rows, 2 * MZ * GROUP), BF16)
    sums = pltpu.VMEM((rows, 2 * MZ * GROUP), F32)
    slot_sums = pltpu.VMEM((rows, SLOTS * rows_z), F32)
    grouped_field = (groups, GROUP) + field[1:]
    buffer = pltpu.VMEM(grouped_field, BF16)
    sems = pltpu.SemaphoreType.DMA((STEPS,))
    group_sems = pltpu.SemaphoreType.DMA((STEPS * groups,))
    far = pl.BlockSpec(memory_space=pltpu.HBM)
    far_field = pltpu.HBM(field, BF16)

    def kept_far(array):
        return pltpu.with_memory_space_constraint(array, pltpu.HBM)

    plane_flops = 2 * count * 2 * MZ * GROUP

    def exchange(array):
        return lax.all_to_all(array, mesh_axes, split_axis=0, concat_axis=0, tiled=True)

    def mix_points(values, turned, shifts):
        step = 2
        block = pl.BlockSpec((channels, step, rows_y, rows_z), lambda x: (0, x, 0, 0))
        kernel = functools.partial(pointwise_kernel, turned)
        specs = [block, whole(pointwise)]
        operands = [values, pointwise]
        if shifts is None:
            run = lambda a, b, *rest: kernel(a, b, None, *rest)
        else:
            run = kernel
            specs.append(pl.BlockSpec(memory_space=pltpu.SMEM))
            operands.append(shifts)
        return pl.pallas_call(
            run,
            grid=(width // step,),
            in_specs=specs,
            out_specs=block,
            out_shape=far_field,
            scratch_shapes=[
                pltpu.VMEM((channels * TILE, channels * TILE), BF16),
                pltpu.VMEM((channels, 1, rows_z), F32),
            ],
            compiler_params=params(32),
            cost_estimate=cost(2 * count * channels * TILE, 4 * count),
        )(*operands)

    planes = pl.pallas_call(
        functools.partial(plane_kernel, per, channels, slabs),
        in_specs=[far, far, far],
        out_specs=whole(message),
        out_shape=message,
        scratch_shapes=[
            ztab,
            order,
            sums,
            buffer,
            pltpu.VMEM(base.shape, F32),
            pltpu.VMEM(ytab.shape, BF16),
            sems,
            pltpu.SemaphoreType.DMA((2,)),
        ],
        compiler_params=params(32),
        cost_estimate=cost(plane_flops, 2 * count),
    )(kept_far(activations.reshape(grouped_field)), kept_far(base), kept_far(ytab))
    arrived = exchange(planes)
    local = mix_points(kept_far(activations.reshape(field)), True, offsets)
    arrived, local = lax.optimization_barrier((arrived, local))
    spec_in, mixed = pl.pallas_call(
        functools.partial(mix_kernel, per, samples),
        out_shape=(spectra, message),
        scratch_shapes=[pltpu.VMEM(spectra.shape, BF16)],
        compiler_params=params(16),
        cost_estimate=cost(10**8, 2 * mode_weights.size),
    )(arrived, mode_weights, line_fwd, inv_t)
    returned = exchange(mixed)
    slope, back_plane = pl.pallas_call(
        functools.partial(slope_kernel, per, channels, slabs),
        in_specs=[whole(message), far, far]
        + [whole(t) for t in (base, base_t, ytab, ytab_t, scale, scale_t)],
        out_specs=(far, whole(message)),
        out_shape=(pltpu.HBM(grouped_field, BF16), message),
        scratch_shapes=[ztab, ztab_t, order, held, sums]
        + [buffer] * 3
        + [slot_sums]
        + [group_sems] * 3,
        compiler_params=params(40),
        cost_estimate=cost(2 * plane_flops, 6 * count, 2 * count),
    )(returned, kept_far(local.reshape(grouped_field)), kept_far(cotangent.reshape(grouped_field)), base, base_t, ytab, ytab_t, scale, scale_t)
    arrived_back = exchange(back_plane)
    local_back = mix_points(kept_far(slope.reshape(field)), False, None)
    arrived_back, local_back = lax.optimization_barrier((arrived_back, local_back))
    pairs, mixed_back = pl.pallas_call(
        functools.partial(mix_back_kernel, per, samples),
        out_shape=(shaped((spectra.shape[0], 2 * spectra.shape[1]), BF16), message),
        scratch_shapes=[pltpu.VMEM(spectra.shape, BF16)],
        compiler_params=params(16),
        cost_estimate=cost(10**8, 2 * mode_weights.size),
    )(arrived_back, mode_weights, line_inv, fwd_t)
    returned_back = exchange(mixed_back)
    grad_spectral = pl.pallas_call(
        functools.partial(weight_kernel, per, samples),
        out_shape=shaped(mode_weights.shape, F32),
        compiler_params=params(16),
        cost_estimate=cost(10**8, 4 * mode_weights.size),
    )(spec_in, pairs)
    grad_in = pl.pallas_call(
        functools.partial(field_kernel, per, channels, slabs),
        in_specs=[whole(message), far, whole(base_t), whole(ytab_t)],
        out_specs=far,
        out_shape=shaped(grouped_field, BF16),
        scratch_shapes=[ztab_t, order, held, buffer, buffer, sems, sems],
        compiler_params=params(32),
        cost_estimate=cost(plane_flops, 4 * count),
    )(returned_back, kept_far(local_back.reshape(grouped_field)), base_t, ytab_t)
    return (grad_in.reshape(activations.shape), grad_spectral)


def chosen_body(mesh_axes, devices, slabs, activations, cotangent, mode_weights, pointwise, offsets):
    samples, channels, width, rows_y, rows_z = activations.shape
    per = MY * MZ // devices
    fits = (
        samples == 1
        and MY * MZ % devices == 0
        and per in (2, 4, 8)
        and width % 8 == 0
        and channels == 64
        and rows_y % TILE == 0
        and rows_z == 128
    )
    plan = functools.partial(body, mesh_axes, devices, slabs) if fits else general_body
    return plan(activations, cotangent, mode_weights, pointwise, offsets)


def solution(mesh):
    slabs = mesh.shape["space"]
    devices = slabs * mesh.shape["dp"]
    return jax.shard_map(
        functools.partial(chosen_body, ("dp", "space"), devices, slabs),
        mesh=mesh,
        in_specs=(
            P("dp", None, "space", None, None),
            P("dp", None, "space", None, None),
            P(("space", "dp"), None, None),
            P(),
            P(),
        ),
        out_specs=(P("dp", None, "space", None, None), P(("space", "dp"), None, None)),
        check_vma=False,
    )
```

```python
import functools
import math

import jax
import jax.numpy as jnp
import ml_dtypes
import numpy as np
from jax import lax
from jax.experimental import pallas as pl
from jax.experimental.pallas import tpu as pltpu
from jax.sharding import PartitionSpec as P

MX = 16
MY = 16
MZ = 8
NX = 32


def centered(count):
    index = jnp.arange(count, dtype=jnp.int32)
    return jnp.where(index < count // 2, index, index - count)


def plane_tables(rows_y, rows_z, modes_y, modes_z):
    along_y = jnp.arange(rows_y, dtype=jnp.int32)[:, None, None, None]
    along_z = jnp.arange(rows_z, dtype=jnp.int32)[None, :, None, None]
    freq_y = centered(modes_y)[None, None, :, None]
    freq_z = jnp.arange(modes_z, dtype=jnp.int32)[None, None, None, :]
    phase = jnp.mod(freq_y * along_y * rows_z + freq_z * along_z * rows_y, rows_y * rows_z)
    theta = phase.astype(jnp.float32) * (2.0 * math.pi / (rows_y * rows_z))
    cosine = jnp.cos(theta)
    sine = jnp.sin(theta)
    forward = jnp.stack([cosine, -sine], -1).reshape(rows_y * rows_z, modes_y * modes_z * 2)
    scaled = jnp.where(freq_z == 0, 1.0, 2.0).astype(jnp.float32) / (rows_y * rows_z)
    inverse = (
        jnp.stack([cosine * scaled, -sine * scaled], -1)
        .reshape(rows_y * rows_z, modes_y * modes_z * 2)
        .T
    )
    return (forward.astype(jnp.bfloat16), inverse.astype(jnp.bfloat16))


def line_tables(length, modes):
    along = jnp.arange(length, dtype=jnp.int32)[:, None]
    freq = centered(modes)[None, :]
    phase = jnp.mod(freq * along, length)
    theta = phase.astype(jnp.float32) * (2.0 * math.pi / length)
    cosine = jnp.cos(theta)
    sine = jnp.sin(theta)
    first = jnp.stack([cosine, -sine], -1)
    second = jnp.stack([sine, cosine], -1)
    forward = jnp.stack([first, second], 1).reshape(2 * length, 2 * modes)
    inv_first = jnp.stack([cosine.T, sine.T], -1) / length
    inv_second = jnp.stack([-sine.T, cosine.T], -1) / length
    inverse = jnp.stack([inv_first, inv_second], 1).reshape(2 * modes, 2 * length)
    return (forward.astype(jnp.bfloat16), inverse.astype(jnp.bfloat16))


def expand_weights(weights):
    half = weights.shape[1]
    real_part = weights[:, :, :half]
    imag_part = weights[:, :, half:]
    upper = jnp.concatenate([real_part, imag_part], axis=2)
    lower = jnp.concatenate([-imag_part, real_part], axis=2)
    return jnp.concatenate([upper, lower], axis=1)


def outer_sum(left, right):
    return jnp.einsum("mbi,mbo->mio", left, right, preferred_element_type=jnp.float32)


def weight_terms(spec_in, spec_grad):
    half = spec_in.shape[2] // 2
    in_real = spec_in[:, :, :half]
    in_imag = spec_in[:, :, half:]
    gr_real = spec_grad[:, :, :half]
    gr_imag = spec_grad[:, :, half:]
    real_term = outer_sum(in_real, gr_real) + outer_sum(in_imag, gr_imag)
    imag_term = outer_sum(in_real, gr_imag) - outer_sum(in_imag, gr_real)
    return jnp.concatenate([real_term, imag_term], axis=2)


def to_modes(slab, table, modes_x):
    samples, channels, width, pairs = slab.shape
    moved = lax.all_to_all(slab, "space", split_axis=3, concat_axis=2, tiled=True)
    length = moved.shape[2]
    local = moved.shape[3] // 2
    lines = moved.reshape(samples, channels, length, local, 2).transpose(0, 1, 3, 2, 4)
    lines = lines.reshape(samples, channels, local, 2 * length)
    spectra = jnp.dot(lines, table, preferred_element_type=jnp.float32).astype(jnp.bfloat16)
    spectra = spectra.reshape(samples, channels, local, modes_x, 2).transpose(2, 3, 0, 4, 1)
    return spectra.reshape(local * modes_x, samples, 2 * channels)


def to_slab(spectra, table, modes_x, channels):
    count, samples, doubled = spectra.shape
    local = count // modes_x
    lines = spectra.reshape(local, modes_x, samples, 2, channels).transpose(2, 4, 0, 1, 3)
    lines = lines.reshape(samples, channels, local, 2 * modes_x)
    lines = jnp.dot(lines, table, preferred_element_type=jnp.float32).astype(jnp.bfloat16)
    length = lines.shape[3] // 2
    lines = lines.reshape(samples, channels, local, length, 2).transpose(0, 1, 3, 2, 4)
    lines = lines.reshape(samples, channels, length, 2 * local)
    return lax.all_to_all(lines, "space", split_axis=2, concat_axis=3, tiled=True)


def to_owners(spectra):
    return lax.all_to_all(spectra, "dp", split_axis=0, concat_axis=1, tiled=True)


def from_owners(spectra):
    return lax.all_to_all(spectra, "dp", split_axis=1, concat_axis=0, tiled=True)


def gelu_slope(value):
    cdf = 0.5 * (1.0 + lax.erf(value * 0.7071067811865476))
    density = jnp.exp(-0.5 * value * value) * 0.3989422804014327
    return cdf + value * density


def general_body(activations, cotangent, mode_weights, pointwise, offsets):
    samples, channels, width, rows_y, rows_z = activations.shape
    plane_fwd, plane_inv = plane_tables(rows_y, rows_z, MY, MZ)
    line_fwd, line_inv = line_tables(NX, MX)
    flat = activations.reshape(samples, channels, width, rows_y * rows_z)
    planes = jnp.dot(flat, plane_fwd, preferred_element_type=jnp.float32).astype(jnp.bfloat16)
    spec_in = to_modes(planes, line_fwd, MX)
    blocks = expand_weights(mode_weights)
    held_in = to_owners(spec_in)
    held_out = jnp.einsum(
        "mbi,mio->mbo", held_in, blocks, preferred_element_type=jnp.float32
    ).astype(jnp.bfloat16)
    spec_out = from_owners(held_out)
    returned = to_slab(spec_out, line_inv, MX, channels)
    spectral = jnp.dot(returned, plane_inv, preferred_element_type=jnp.float32)
    local_part = jnp.einsum("io,bixn->boxn", pointwise, flat, preferred_element_type=jnp.float32)
    summed = spectral + local_part + offsets[None, :, None, None]
    upstream = cotangent.reshape(flat.shape).astype(jnp.float32)
    slope_grad = (upstream * gelu_slope(summed)).astype(jnp.bfloat16)
    back_plane = jnp.dot(slope_grad, plane_inv.T, preferred_element_type=jnp.float32).astype(
        jnp.bfloat16
    )
    spec_grad = to_modes(back_plane, line_inv.T, MX)
    held_grad = to_owners(spec_grad)
    held_dx = jnp.einsum(
        "mbo,mio->mbi", held_grad, blocks, preferred_element_type=jnp.float32
    ).astype(jnp.bfloat16)
    spec_dx = from_owners(held_dx)
    grad_spectral = weight_terms(held_in, held_grad)
    line_dx = to_slab(spec_dx, line_fwd.T, MX, channels)
    total = jnp.dot(line_dx, plane_fwd.T, preferred_element_type=jnp.float32)
    total = total + jnp.einsum(
        "io,boxn->bixn", pointwise, slope_grad, preferred_element_type=jnp.float32
    )
    grad_in = total.astype(jnp.bfloat16).reshape(activations.shape)
    return (grad_in, grad_spectral)


BF16 = jnp.bfloat16
F32 = jnp.float32
GROUP = 16
TILE = 8
SLOTS = 4
STEPS = GROUP // SLOTS
SMALL_SLOTS = 2
SMALL_STEPS = GROUP // SMALL_SLOTS
MIB = 1024 * 1024


def rounded(table):
    return np.asarray(table, np.float32).astype(ml_dtypes.bfloat16)


def angles(freq, points, length):
    phase = np.mod(np.outer(freq, points), length)
    return (phase * (2.0 * math.pi / length)).astype(np.float64)


def signed(count):
    index = np.arange(count)
    return np.where(index < count // 2, index, index - count)


def z_base(rows_z):
    theta = angles(np.arange(MZ), np.arange(rows_z), rows_z)
    pair = np.stack([np.cos(theta), -np.sin(theta)])
    table = np.repeat(pair.reshape(2 * MZ, rows_z), GROUP, axis=0).T
    return rounded(table).astype(np.float32)


def y_table(rows_y, width):
    theta = angles(signed(MY), np.arange(rows_y), rows_y)
    cosine, sine = np.cos(theta), np.sin(theta)
    turn = np.stack([np.stack([cosine, sine]), np.stack([-sine, cosine])])
    table = np.einsum("rsjy,xw->jxrswy", turn, np.eye(width))
    return rounded(table.reshape(MY * width * 2, 2 * width * rows_y))


def x_tables(samples, slabs, length):
    theta = angles(signed(MX), np.arange(length), length)
    cosine, sine = np.cos(theta), np.sin(theta)
    forward = np.stack([np.stack([cosine, sine]), np.stack([-sine, cosine])])
    inverse = np.stack([np.stack([cosine, sine]), np.stack([-sine, cosine])]) / length
    same = np.eye(samples)
    rows = MX * 2 * samples

    def lay(turn):
        turn = turn.reshape(2, 2, MX, slabs, length // slabs)
        table = np.einsum("arqsx,bd->qabdsxr", turn, same)
        return rounded(table.reshape(rows, samples * length * 2))

    return lay(forward), lay(inverse)


def dot(left, right):
    return jnp.dot(left, right, preferred_element_type=F32)


def doubled_slope(u):
    decay = jnp.exp2(u * u * -math.log2(math.e)).astype(BF16)
    cdf = (1.0 + lax.erf(u)).astype(BF16)
    return cdf + u.astype(BF16) * jnp.asarray(2.0 / math.sqrt(math.pi), BF16) * decay


def over(index, size):
    return lax.shift_right_logical(index, jnp.int32(size.bit_length() - 1))


def within(index, size):
    return jnp.bitwise_and(index, jnp.int32(size - 1))


def fill_z(base, table):
    rows_z, lanes = base.shape
    owner = within(lax.broadcasted_iota(jnp.int32, (rows_z, lanes), 1), GROUP)
    values = base[...]
    for c in range(GROUP):
        table[c * rows_z : (c + 1) * rows_z] = jnp.where(owner == c, values, 0.0).astype(BF16)


def fill_z_back(base, table):
    lanes, rows_z = base.shape
    owner = within(lax.broadcasted_iota(jnp.int32, (lanes, rows_z), 0), GROUP)
    values = base[...]
    for c in range(GROUP):
        slots = GROUP // table.shape[0]
        first = c % slots * rows_z
        table[c // slots, :, first : first + rows_z] = jnp.where(owner == c, values, 0.0).astype(BF16)


def grouped(lane, per, channels):
    c = within(lane, channels)
    return over(c, GROUP) * (MZ * GROUP) + over(lane, channels) * GROUP + within(c, GROUP)


def fill_order(per, channels, back, table):
    count = table.shape[0]
    row = lax.broadcasted_iota(jnp.int32, (count, count), 0)
    column = lax.broadcasted_iota(jnp.int32, (count, count), 1)
    if back:
        same = grouped(row[:, :1], per, channels) == column
    else:
        same = row == grouped(column[:1], per, channels)
    table[...] = jnp.where(same, 1.0, 0.0).astype(BF16)


def turned_index(index, slabs, devices):
    samples = devices // slabs
    return index % samples * slabs + index // samples


def deliver(spectra, ytab, order, scale, message, per, channels, slabs):
    groups = channels // GROUP
    rows = spectra.shape[0] // groups
    wide = spectra.shape[1] // 2
    halves = []
    for r in range(2):
        blocks = [spectra[g * rows : (g + 1) * rows, r * wide : (r + 1) * wide] for g in range(groups)]
        halves.append(jnp.concatenate(blocks, axis=1).astype(BF16))
    planes = dot(ytab[...], jnp.concatenate(halves, axis=0))
    if scale is not None:
        planes = planes * scale[...]
    ordered = dot(planes.astype(BF16), order[...]).astype(BF16)
    parts = MZ // per
    count = message.shape[1]
    lanes = per * channels
    for part in range(parts):
        block = ordered[:, part * lanes : (part + 1) * lanes]
        for j in range(MY):
            message[turned_index(j * parts + part, slabs, message.shape[0])] = block[j * count : (j + 1) * count]


def receive(message, order_back, ytab_back, scale, held, per, slabs):
    parts = MZ // per
    lanes = [
        jnp.concatenate(
            [message[turned_index(j * parts + part, slabs, message.shape[0])] for j in range(MY)], axis=0
        )
        for part in range(parts)
    ]
    ordered = dot(jnp.concatenate(lanes, axis=1), order_back[...]).astype(BF16)
    lines = dot(ytab_back[...], ordered)
    if scale is not None:
        lines = lines * scale[...]
    lines = lines.astype(BF16)
    rows = lines.shape[0] // 2
    wide = MZ * GROUP
    for group in range(held.shape[0] // rows):
        piece = lines[:, group * wide : (group + 1) * wide]
        held[group * rows : (group + 1) * rows] = jnp.concatenate([piece[:rows], piece[rows:]], axis=1)


class Move:
    def __init__(self, source, target, sems):
        self.source, self.target, self.sems = source, target, sems
        self.slots = GROUP // sems.shape[0]

    def copy(self, step):
        run = pl.ds(step * self.slots, self.slots)
        return pltpu.make_async_copy(self.source.at[:, run], self.target.at[:, run], self.sems.at[step])

    def start(self, step):
        self.copy(step).start()

    def wait(self, step):
        self.copy(step).wait()


class GroupMove(Move):
    def copy(self, step, g):
        run = pl.ds(step * SLOTS, SLOTS)
        sem = self.sems.at[step * self.target.shape[0] + g]
        return pltpu.make_async_copy(self.source.at[g, run], self.target.at[g, run], sem)

    def start(self, step):
        for g in range(self.target.shape[0]):
            self.copy(step, g).start()

    def wait(self, step):
        for g in range(self.target.shape[0]):
            self.copy(step, g).wait()


def start_all(moves, step):
    for each in moves:
        each.start(step)


def add_spectra(field, ztab, step, slots, spectra):
    groups = field.shape[0]
    rows_z = field.shape[-1]
    depth = slots * rows_z
    table = ztab[pl.ds(pl.multiple_of(step * depth, depth), depth)]
    lanes = [
        jnp.concatenate(
            [field[g, step * slots + slot].reshape(-1, rows_z) for g in range(groups)], axis=0
        )
        for slot in range(slots)
    ]
    spectra[...] += dot(jnp.concatenate(lanes, axis=1), table)


def plane_kernel(
    per, channels, slabs, field, base_far, ytab_far, message, ztab, order, spectra, buffer, base, ytab, sems, table_sems
):
    incoming = Move(field, buffer, sems)
    base_copy = pltpu.make_async_copy(base_far, base, table_sems.at[0])
    ytab_copy = pltpu.make_async_copy(ytab_far, ytab, table_sems.at[1])
    base_copy.start()
    incoming.start(0)
    incoming.start(1)
    fill_order(per, channels, False, order)
    incoming.start(2)
    spectra[...] = jnp.zeros_like(spectra)
    incoming.start(3)
    base_copy.wait()
    fill_z(base, ztab)
    for step in range(4, SMALL_STEPS):
        incoming.start(step)
    ytab_copy.start()

    @pl.loop(0, SMALL_STEPS)
    def _(step):
        incoming.wait(step)
        add_spectra(buffer, ztab, step, SMALL_SLOTS, spectra)

    ytab_copy.wait()
    deliver(spectra, ytab, order, None, message, per, channels, slabs)


def slope_kernel(
    per, channels, slabs, arrived, local, cotangent, base, base_back, ytab, ytab_back, scale, scale_back,
    slope, message, ztab, ztab_back, order, held, spectra, local_in, cotangent_in, result, total,
    local_sems, cotangent_sems, result_sems,
):
    width, rows_y, rows_z = local.shape[2:]
    groups = channels // GROUP
    rows = width * rows_y
    incoming = (GroupMove(local, local_in, local_sems), GroupMove(cotangent, cotangent_in, cotangent_sems))
    outgoing = GroupMove(result, slope, result_sems)
    start_all(incoming, 0)
    fill_order(per, channels, True, order)
    receive(arrived, order, ytab_back, scale_back, held, per, slabs)
    start_all(incoming, 1)
    fill_z_back(base_back, ztab_back)
    fill_z(base, ztab)
    start_all(incoming, 2)
    fill_order(per, channels, False, order)
    spectra[...] = jnp.zeros_like(spectra)
    start_all(incoming, 3)

    @pl.loop(0, STEPS)
    def _(step):
        for each in incoming:
            each.wait(step)
        total[...] = dot(held[...], ztab_back[step])
        for g in range(groups):
            for slot in range(SLOTS):
                lanes = slice(slot * rows_z, (slot + 1) * rows_z)
                c = step * SLOTS + slot
                for x in range(width):
                    place = g * rows + x * rows_y
                    value = total[place : place + rows_y, lanes]
                    value = value + local_in[g, c, x].astype(F32)
                    upstream = cotangent_in[g, c, x]
                    answer = upstream * doubled_slope(value)
                    result[g, c, x] = answer
            outgoing.copy(step, g).start()
        add_spectra(result, ztab, step, SLOTS, spectra)

    deliver(spectra, ytab, order, scale, message, per, channels, slabs)
    for step in range(STEPS):
        outgoing.wait(step)


def field_kernel(
    per, channels, slabs, arrived, local, base_back, ytab_back, out, ztab_back, order, held, local_in, result,
    local_sems, result_sems,
):
    width, rows_y, rows_z = local.shape[2:]
    groups = channels // GROUP
    rows = width * rows_y
    incoming = Move(local, local_in, local_sems)
    outgoing = Move(result, out, result_sems)
    incoming.start(0)
    incoming.start(1)
    fill_order(per, channels, True, order)
    incoming.start(2)
    incoming.start(3)
    receive(arrived, order, ytab_back, None, held, per, slabs)
    incoming.start(4)
    incoming.start(5)
    fill_z_back(base_back, ztab_back)
    incoming.start(6)
    incoming.start(7)

    @pl.loop(0, SMALL_STEPS)
    def _(step):
        incoming.wait(step)
        total = dot(held[...], ztab_back[step])
        for g in range(groups):
            for slot in range(SMALL_SLOTS):
                lanes = slice(slot * rows_z, (slot + 1) * rows_z)
                c = step * SMALL_SLOTS + slot
                value = total[g * rows : (g + 1) * rows, lanes]
                value = value + local_in[g, c].reshape(rows, rows_z).astype(F32)
                result[g, c] = value.astype(BF16).reshape(width, rows_y, rows_z)
        outgoing.start(step)

    for step in range(SMALL_STEPS):
        outgoing.wait(step)


def pointwise_kernel(turned, field, mix, offsets, out, table, shift):
    channels = mix.shape[0]
    width, rows_y, rows_z = field.shape[1:]
    size = channels * TILE

    @pl.when(pl.program_id(0) == 0)
    def _():
        row = over(lax.broadcasted_iota(jnp.int32, (size, channels), 0), TILE)
        column = lax.broadcasted_iota(jnp.int32, (size, channels), 1)
        spread = jnp.where(row == column, 1.0, 0.0).astype(BF16)
        tall = lax.dot_general(
            spread, mix[...], (((1,), (1 if turned else 0,)), ((), ())), preferred_element_type=F32
        ).astype(BF16)
        whole = lax.dot_general(
            tall, spread, (((1,), (1,)), ((), ())), preferred_element_type=F32
        )
        place = within(lax.broadcasted_iota(jnp.int32, (size, size), 0), TILE)
        other = within(lax.broadcasted_iota(jnp.int32, (size, size), 1), TILE)
        table[...] = jnp.where(place == other, whole if turned else 0.5 * whole, 0.0).astype(BF16)
        if offsets is not None:
            for c in range(channels):
                shift[c] = jnp.full((1, rows_z), offsets[c], F32)

    for start in range(0, rows_y, 2 * TILE):
        pieces = [field[:, x, start : start + 2 * TILE, :].astype(F32) for x in range(width)]
        halves = []
        for row in range(0, 2 * TILE, TILE):
            rows = [piece[:, row : row + TILE].reshape(size, rows_z).astype(BF16) for piece in pieces]
            halves.append(dot(table[...], jnp.concatenate(rows, axis=1)))
        for x in range(width):
            values = [
                half[:, x * rows_z : (x + 1) * rows_z].reshape(channels, TILE, rows_z) for half in halves
            ]
            value = jnp.concatenate(values, axis=1)
            if offsets is not None:
                value = (value + shift[...]) * math.sqrt(0.5)
            out[:, x, start : start + 2 * TILE, :] = value.astype(BF16)


def spread_pair(first, second):
    nothing = jnp.zeros_like(first)
    upper = jnp.concatenate([first, nothing], axis=1)
    lower = jnp.concatenate([nothing, second], axis=1)
    return jnp.concatenate([upper, lower], axis=0)


def low_half(shape):
    return lax.broadcasted_iota(jnp.int32, shape, 1) < shape[1] // 2


def mix_kernel(per, samples, arrived, weights, line, line_back, spec_in, message, held):
    rows = 2 * samples
    lanes = 2 * weights.shape[1]
    low = low_half((samples, lanes))
    flat = arrived[...].reshape(-1, arrived.shape[2])
    spectra = dot(line[...], flat).astype(BF16)
    spec_in[...] = spectra
    for q in range(MX):
        for first in range(0, per, 2):
            block = spread_pair(weights[first * MX + q], weights[(first + 1) * MX + q])
            place = first // 2 * lanes
            terms = dot(spectra[q * rows : (q + 1) * rows, place : place + lanes], block)
            mixed = []
            for side in range(2):
                part = terms[:, side * lanes : (side + 1) * lanes]
                turned = pltpu.roll(part[samples:], lanes // 2, 1)
                mixed.append(part[:samples] + jnp.where(low, -turned, turned))
            real = jnp.where(low, mixed[0], pltpu.roll(mixed[1], lanes // 2, 1))
            imag = jnp.where(low, pltpu.roll(mixed[0], lanes // 2, 1), mixed[1])
            held[q * rows : (q + 1) * rows, place : place + lanes] = jnp.concatenate(
                [real, imag], axis=0
            ).astype(BF16)
    message[...] = dot(line_back[...], held[...]).astype(BF16).reshape(message.shape)


def mix_back_kernel(per, samples, arrived, weights, line, line_back, pairs, message, held):
    rows = 2 * samples
    lanes = 2 * weights.shape[1]
    low = low_half((samples, lanes))
    first_lanes = jnp.where(low_half((lanes, lanes)), 1.0, 0.0).astype(BF16)
    second_lanes = jnp.where(low_half((lanes, lanes)), 0.0, 1.0).astype(BF16)
    flat = arrived[...].reshape(-1, arrived.shape[2])
    spectra = dot(line[...], flat).astype(BF16).astype(F32)
    for q in range(MX):
        for first in range(0, per, 2):
            both = jnp.concatenate([weights[first * MX + q], weights[(first + 1) * MX + q]], axis=0).T
            block = jnp.concatenate([both * first_lanes, both * second_lanes], axis=0)
            place = first // 2 * lanes
            real = spectra[q * rows : q * rows + samples, place : place + lanes]
            imag = spectra[q * rows + samples : (q + 1) * rows, place : place + lanes]
            real_turned = pltpu.roll(real, lanes // 2, 1)
            imag_turned = pltpu.roll(imag, lanes // 2, 1)
            left = [jnp.where(low, real, imag_turned), jnp.where(low, imag, -real_turned)]
            right = [jnp.where(low, real_turned, imag), jnp.where(low, imag_turned, -real)]
            pair = jnp.concatenate(
                [jnp.concatenate(left, axis=0), jnp.concatenate(right, axis=0)], axis=1
            ).astype(BF16)
            pairs[q * rows : (q + 1) * rows, 2 * place : 2 * (place + lanes)] = pair
            held[q * rows : (q + 1) * rows, place : place + lanes] = dot(pair, block).astype(BF16)
    message[...] = dot(line_back[...], held[...]).astype(BF16).reshape(message.shape)


def weight_kernel(per, samples, spec_in, pairs, out):
    rows = 2 * samples
    lanes = out.shape[2]
    half = lanes // 2
    for q in range(MX):
        for first in range(0, per, 2):
            place = first // 2 * lanes
            left = spec_in[q * rows : (q + 1) * rows, place : place + lanes]
            right = pairs[q * rows : (q + 1) * rows, 2 * place : 2 * (place + lanes)]
            outer = lax.dot_general(
                left, right, (((0,), (0,)), ((), ())), preferred_element_type=F32
            )
            out[first * MX + q] = outer[:half, :lanes]
            out[(first + 1) * MX + q] = outer[half:, lanes:]


def whole(array):
    return pl.BlockSpec(array.shape, lambda *step: (0,) * len(array.shape))


def shaped(shape, dtype):
    return jax.ShapeDtypeStruct(shape, dtype)


def params(mib):
    return pltpu.CompilerParams(vmem_limit_bytes=mib * MIB)


def cost(flops, moved, steep=0):
    return pl.CostEstimate(flops=flops, bytes_accessed=moved, transcendentals=steep)


def body(mesh_axes, devices, slabs, activations, cotangent, mode_weights, pointwise, offsets):
    _, channels, width, rows_y, rows_z = activations.shape
    samples = devices // slabs
    per = MY * MZ // devices
    groups = channels // GROUP
    field = activations.shape[1:]
    count = math.prod(field)
    base = z_base(rows_z)
    ytab = y_table(rows_y, width)
    line_fwd, line_inv = x_tables(samples, slabs, NX)
    weight = np.where(np.arange(MZ) == 0, 1.0, 2.0) / (rows_y * rows_z)
    scale = np.tile(np.repeat(weight, GROUP), groups)[None]
    scale, scale_t = (0.5 * scale).astype(np.float32), (math.sqrt(0.5) * scale).astype(np.float32)
    base_t, ytab_t = (np.ascontiguousarray(t.T) for t in (base, ytab))
    fwd_t, inv_t = (np.ascontiguousarray(t.T) for t in (line_fwd, line_inv))
    message = shaped((devices, 2 * width, per * channels), BF16)
    spectra = shaped((MX * 2 * samples, per * channels), BF16)
    ztab = pltpu.VMEM((GROUP * rows_z, 2 * MZ * GROUP), BF16)
    ztab_t = pltpu.VMEM((STEPS, 2 * MZ * GROUP, SLOTS * rows_z), BF16)
    small_ztab_t = pltpu.VMEM((SMALL_STEPS, 2 * MZ * GROUP, SMALL_SLOTS * rows_z), BF16)
    order = pltpu.VMEM((MZ * channels, MZ * channels), BF16)
    rows = groups * width * rows_y
    held = pltpu.VMEM((rows, 2 * MZ * GROUP), BF16)
    sums = pltpu.VMEM((rows, 2 * MZ * GROUP), F32)
    slot_sums = pltpu.VMEM((rows, SLOTS * rows_z), F32)
    grouped_field = (groups, GROUP) + field[1:]
    buffer = pltpu.VMEM(grouped_field, BF16)
    sems = pltpu.SemaphoreType.DMA((SMALL_STEPS,))
    group_sems = pltpu.SemaphoreType.DMA((STEPS * groups,))
    far = pl.BlockSpec(memory_space=pltpu.HBM)
    far_field = pltpu.HBM(field, BF16)

    def kept_far(array):
        return pltpu.with_memory_space_constraint(array, pltpu.HBM)

    plane_flops = 2 * count * 2 * MZ * GROUP

    def exchange(array):
        return lax.all_to_all(array, mesh_axes, split_axis=0, concat_axis=0, tiled=True)

    def mix_points(values, turned, shifts):
        step = 2
        block = pl.BlockSpec((channels, step, rows_y, rows_z), lambda x: (0, x, 0, 0))
        kernel = functools.partial(pointwise_kernel, turned)
        specs = [block, whole(pointwise)]
        operands = [values, pointwise]
        if shifts is None:
            run = lambda a, b, *rest: kernel(a, b, None, *rest)
        else:
            run = kernel
            specs.append(pl.BlockSpec(memory_space=pltpu.SMEM))
            operands.append(shifts)
        return pl.pallas_call(
            run,
            grid=(width // step,),
            in_specs=specs,
            out_specs=block,
            out_shape=far_field,
            scratch_shapes=[
                pltpu.VMEM((channels * TILE, channels * TILE), BF16),
                pltpu.VMEM((channels, 1, rows_z), F32),
            ],
            compiler_params=params(32),
            cost_estimate=cost(2 * count * channels * TILE, 4 * count),
        )(*operands)

    planes = pl.pallas_call(
        functools.partial(plane_kernel, per, channels, slabs),
        in_specs=[far, far, far],
        out_specs=whole(message),
        out_shape=message,
        scratch_shapes=[
            ztab,
            order,
            sums,
            buffer,
            pltpu.VMEM(base.shape, F32),
            pltpu.VMEM(ytab.shape, BF16),
            sems,
            pltpu.SemaphoreType.DMA((2,)),
        ],
        compiler_params=params(32),
        cost_estimate=cost(plane_flops, 2 * count),
    )(kept_far(activations.reshape(grouped_field)), kept_far(base), kept_far(ytab))
    arrived = exchange(planes)
    local = mix_points(kept_far(activations.reshape(field)), True, offsets)
    arrived, local = lax.optimization_barrier((arrived, local))
    spec_in, mixed = pl.pallas_call(
        functools.partial(mix_kernel, per, samples),
        out_shape=(spectra, message),
        scratch_shapes=[pltpu.VMEM(spectra.shape, BF16)],
        compiler_params=params(16),
        cost_estimate=cost(10**8, 2 * mode_weights.size),
    )(arrived, mode_weights, line_fwd, inv_t)
    returned = exchange(mixed)
    slope, back_plane = pl.pallas_call(
        functools.partial(slope_kernel, per, channels, slabs),
        in_specs=[whole(message), far, far]
        + [whole(t) for t in (base, base_t, ytab, ytab_t, scale, scale_t)],
        out_specs=(far, whole(message)),
        out_shape=(pltpu.HBM(grouped_field, BF16), message),
        scratch_shapes=[ztab, ztab_t, order, held, sums]
        + [buffer] * 3
        + [slot_sums]
        + [group_sems] * 3,
        compiler_params=params(40),
        cost_estimate=cost(2 * plane_flops, 6 * count, 2 * count),
    )(returned, kept_far(local.reshape(grouped_field)), kept_far(cotangent.reshape(grouped_field)), base, base_t, ytab, ytab_t, scale, scale_t)
    arrived_back = exchange(back_plane)
    local_back = mix_points(kept_far(slope.reshape(field)), False, None)
    arrived_back, local_back = lax.optimization_barrier((arrived_back, local_back))
    pairs, mixed_back = pl.pallas_call(
        functools.partial(mix_back_kernel, per, samples),
        out_shape=(shaped((spectra.shape[0], 2 * spectra.shape[1]), BF16), message),
        scratch_shapes=[pltpu.VMEM(spectra.shape, BF16)],
        compiler_params=params(16),
        cost_estimate=cost(10**8, 2 * mode_weights.size),
    )(arrived_back, mode_weights, line_inv, fwd_t)
    returned_back = exchange(mixed_back)
    grad_spectral = pl.pallas_call(
        functools.partial(weight_kernel, per, samples),
        out_shape=shaped(mode_weights.shape, F32),
        compiler_params=params(16),
        cost_estimate=cost(10**8, 4 * mode_weights.size),
    )(spec_in, pairs)
    grad_in = pl.pallas_call(
        functools.partial(field_kernel, per, channels, slabs),
        in_specs=[whole(message), far, whole(base_t), whole(ytab_t)],
        out_specs=far,
        out_shape=shaped(grouped_field, BF16),
        scratch_shapes=[small_ztab_t, order, held, buffer, buffer, sems, sems],
        compiler_params=params(32),
        cost_estimate=cost(plane_flops, 4 * count),
    )(returned_back, kept_far(local_back.reshape(grouped_field)), base_t, ytab_t)
    return (grad_in.reshape(activations.shape), grad_spectral)


def chosen_body(mesh_axes, devices, slabs, activations, cotangent, mode_weights, pointwise, offsets):
    samples, channels, width, rows_y, rows_z = activations.shape
    per = MY * MZ // devices
    fits = (
        samples == 1
        and MY * MZ % devices == 0
        and per in (2, 4, 8)
        and width % 8 == 0
        and channels == 64
        and rows_y % TILE == 0
        and rows_z == 128
    )
    plan = functools.partial(body, mesh_axes, devices, slabs) if fits else general_body
    return plan(activations, cotangent, mode_weights, pointwise, offsets)


def solution(mesh):
    slabs = mesh.shape["space"]
    devices = slabs * mesh.shape["dp"]
    return jax.shard_map(
        functools.partial(chosen_body, ("dp", "space"), devices, slabs),
        mesh=mesh,
        in_specs=(
            P("dp", None, "space", None, None),
            P("dp", None, "space", None, None),
            P(("space", "dp"), None, None),
            P(),
            P(),
        ),
        out_specs=(P("dp", None, "space", None, None), P(("space", "dp"), None, None)),
        check_vma=False,
    )
```

```python
import functools
import math

import jax
import jax.numpy as jnp
import ml_dtypes
import numpy as np
from jax import lax
from jax.experimental import pallas as pl
from jax.experimental.pallas import tpu as pltpu
from jax.sharding import PartitionSpec as P

MX = 16
MY = 16
MZ = 8
NX = 32


def centered(count):
    index = jnp.arange(count, dtype=jnp.int32)
    return jnp.where(index < count // 2, index, index - count)


def plane_tables(rows_y, rows_z, modes_y, modes_z):
    along_y = jnp.arange(rows_y, dtype=jnp.int32)[:, None, None, None]
    along_z = jnp.arange(rows_z, dtype=jnp.int32)[None, :, None, None]
    freq_y = centered(modes_y)[None, None, :, None]
    freq_z = jnp.arange(modes_z, dtype=jnp.int32)[None, None, None, :]
    phase = jnp.mod(freq_y * along_y * rows_z + freq_z * along_z * rows_y, rows_y * rows_z)
    theta = phase.astype(jnp.float32) * (2.0 * math.pi / (rows_y * rows_z))
    cosine = jnp.cos(theta)
    sine = jnp.sin(theta)
    forward = jnp.stack([cosine, -sine], -1).reshape(rows_y * rows_z, modes_y * modes_z * 2)
    scaled = jnp.where(freq_z == 0, 1.0, 2.0).astype(jnp.float32) / (rows_y * rows_z)
    inverse = (
        jnp.stack([cosine * scaled, -sine * scaled], -1)
        .reshape(rows_y * rows_z, modes_y * modes_z * 2)
        .T
    )
    return (forward.astype(jnp.bfloat16), inverse.astype(jnp.bfloat16))


def line_tables(length, modes):
    along = jnp.arange(length, dtype=jnp.int32)[:, None]
    freq = centered(modes)[None, :]
    phase = jnp.mod(freq * along, length)
    theta = phase.astype(jnp.float32) * (2.0 * math.pi / length)
    cosine = jnp.cos(theta)
    sine = jnp.sin(theta)
    first = jnp.stack([cosine, -sine], -1)
    second = jnp.stack([sine, cosine], -1)
    forward = jnp.stack([first, second], 1).reshape(2 * length, 2 * modes)
    inv_first = jnp.stack([cosine.T, sine.T], -1) / length
    inv_second = jnp.stack([-sine.T, cosine.T], -1) / length
    inverse = jnp.stack([inv_first, inv_second], 1).reshape(2 * modes, 2 * length)
    return (forward.astype(jnp.bfloat16), inverse.astype(jnp.bfloat16))


def expand_weights(weights):
    half = weights.shape[1]
    real_part = weights[:, :, :half]
    imag_part = weights[:, :, half:]
    upper = jnp.concatenate([real_part, imag_part], axis=2)
    lower = jnp.concatenate([-imag_part, real_part], axis=2)
    return jnp.concatenate([upper, lower], axis=1)


def outer_sum(left, right):
    return jnp.einsum("mbi,mbo->mio", left, right, preferred_element_type=jnp.float32)


def weight_terms(spec_in, spec_grad):
    half = spec_in.shape[2] // 2
    in_real = spec_in[:, :, :half]
    in_imag = spec_in[:, :, half:]
    gr_real = spec_grad[:, :, :half]
    gr_imag = spec_grad[:, :, half:]
    real_term = outer_sum(in_real, gr_real) + outer_sum(in_imag, gr_imag)
    imag_term = outer_sum(in_real, gr_imag) - outer_sum(in_imag, gr_real)
    return jnp.concatenate([real_term, imag_term], axis=2)


def to_modes(slab, table, modes_x):
    samples, channels, width, pairs = slab.shape
    moved = lax.all_to_all(slab, "space", split_axis=3, concat_axis=2, tiled=True)
    length = moved.shape[2]
    local = moved.shape[3] // 2
    lines = moved.reshape(samples, channels, length, local, 2).transpose(0, 1, 3, 2, 4)
    lines = lines.reshape(samples, channels, local, 2 * length)
    spectra = jnp.dot(lines, table, preferred_element_type=jnp.float32).astype(jnp.bfloat16)
    spectra = spectra.reshape(samples, channels, local, modes_x, 2).transpose(2, 3, 0, 4, 1)
    return spectra.reshape(local * modes_x, samples, 2 * channels)


def to_slab(spectra, table, modes_x, channels):
    count, samples, doubled = spectra.shape
    local = count // modes_x
    lines = spectra.reshape(local, modes_x, samples, 2, channels).transpose(2, 4, 0, 1, 3)
    lines = lines.reshape(samples, channels, local, 2 * modes_x)
    lines = jnp.dot(lines, table, preferred_element_type=jnp.float32).astype(jnp.bfloat16)
    length = lines.shape[3] // 2
    lines = lines.reshape(samples, channels, local, length, 2).transpose(0, 1, 3, 2, 4)
    lines = lines.reshape(samples, channels, length, 2 * local)
    return lax.all_to_all(lines, "space", split_axis=2, concat_axis=3, tiled=True)


def to_owners(spectra):
    return lax.all_to_all(spectra, "dp", split_axis=0, concat_axis=1, tiled=True)


def from_owners(spectra):
    return lax.all_to_all(spectra, "dp", split_axis=1, concat_axis=0, tiled=True)


def gelu_slope(value):
    cdf = 0.5 * (1.0 + lax.erf(value * 0.7071067811865476))
    density = jnp.exp(-0.5 * value * value) * 0.3989422804014327
    return cdf + value * density


def general_body(activations, cotangent, mode_weights, pointwise, offsets):
    samples, channels, width, rows_y, rows_z = activations.shape
    plane_fwd, plane_inv = plane_tables(rows_y, rows_z, MY, MZ)
    line_fwd, line_inv = line_tables(NX, MX)
    flat = activations.reshape(samples, channels, width, rows_y * rows_z)
    planes = jnp.dot(flat, plane_fwd, preferred_element_type=jnp.float32).astype(jnp.bfloat16)
    spec_in = to_modes(planes, line_fwd, MX)
    blocks = expand_weights(mode_weights)
    held_in = to_owners(spec_in)
    held_out = jnp.einsum(
        "mbi,mio->mbo", held_in, blocks, preferred_element_type=jnp.float32
    ).astype(jnp.bfloat16)
    spec_out = from_owners(held_out)
    returned = to_slab(spec_out, line_inv, MX, channels)
    spectral = jnp.dot(returned, plane_inv, preferred_element_type=jnp.float32)
    local_part = jnp.einsum("io,bixn->boxn", pointwise, flat, preferred_element_type=jnp.float32)
    summed = spectral + local_part + offsets[None, :, None, None]
    upstream = cotangent.reshape(flat.shape).astype(jnp.float32)
    slope_grad = (upstream * gelu_slope(summed)).astype(jnp.bfloat16)
    back_plane = jnp.dot(slope_grad, plane_inv.T, preferred_element_type=jnp.float32).astype(
        jnp.bfloat16
    )
    spec_grad = to_modes(back_plane, line_inv.T, MX)
    held_grad = to_owners(spec_grad)
    held_dx = jnp.einsum(
        "mbo,mio->mbi", held_grad, blocks, preferred_element_type=jnp.float32
    ).astype(jnp.bfloat16)
    spec_dx = from_owners(held_dx)
    grad_spectral = weight_terms(held_in, held_grad)
    line_dx = to_slab(spec_dx, line_fwd.T, MX, channels)
    total = jnp.dot(line_dx, plane_fwd.T, preferred_element_type=jnp.float32)
    total = total + jnp.einsum(
        "io,boxn->bixn", pointwise, slope_grad, preferred_element_type=jnp.float32
    )
    grad_in = total.astype(jnp.bfloat16).reshape(activations.shape)
    return (grad_in, grad_spectral)


BF16 = jnp.bfloat16
F32 = jnp.float32
GROUP = 16
TILE = 8
SLOTS = 4
STEPS = GROUP // SLOTS
PLANE_SLOTS = 8
PLANE_STEPS = GROUP // PLANE_SLOTS
MIB = 1024 * 1024


def rounded(table):
    return np.asarray(table, np.float32).astype(ml_dtypes.bfloat16)


def angles(freq, points, length):
    phase = np.mod(np.outer(freq, points), length)
    return (phase * (2.0 * math.pi / length)).astype(np.float64)


def signed(count):
    index = np.arange(count)
    return np.where(index < count // 2, index, index - count)


def z_base(rows_z):
    theta = angles(np.arange(MZ), np.arange(rows_z), rows_z)
    pair = np.stack([np.cos(theta), -np.sin(theta)])
    table = np.repeat(pair.reshape(2 * MZ, rows_z), GROUP, axis=0).T
    return rounded(table).astype(np.float32)


def y_table(rows_y, width):
    theta = angles(signed(MY), np.arange(rows_y), rows_y)
    cosine, sine = np.cos(theta), np.sin(theta)
    turn = np.stack([np.stack([cosine, sine]), np.stack([-sine, cosine])])
    table = np.einsum("rsjy,xw->jxrswy", turn, np.eye(width))
    return rounded(table.reshape(MY * width * 2, 2 * width * rows_y))


def x_tables(samples, slabs, length):
    theta = angles(signed(MX), np.arange(length), length)
    cosine, sine = np.cos(theta), np.sin(theta)
    forward = np.stack([np.stack([cosine, sine]), np.stack([-sine, cosine])])
    inverse = np.stack([np.stack([cosine, sine]), np.stack([-sine, cosine])]) / length
    same = np.eye(samples)
    rows = MX * 2 * samples

    def lay(turn):
        turn = turn.reshape(2, 2, MX, slabs, length // slabs)
        table = np.einsum("arqsx,bd->qabdsxr", turn, same)
        return rounded(table.reshape(rows, samples * length * 2))

    return lay(forward), lay(inverse)


def dot(left, right):
    return jnp.dot(left, right, preferred_element_type=F32)


def doubled_slope(u):
    decay = jnp.exp2(u * u * -math.log2(math.e)).astype(BF16)
    cdf = (1.0 + lax.erf(u)).astype(BF16)
    return cdf + u.astype(BF16) * jnp.asarray(2.0 / math.sqrt(math.pi), BF16) * decay


def over(index, size):
    return lax.shift_right_logical(index, jnp.int32(size.bit_length() - 1))


def within(index, size):
    return jnp.bitwise_and(index, jnp.int32(size - 1))


def fill_z(base, table):
    rows_z, lanes = base.shape
    owner = within(lax.broadcasted_iota(jnp.int32, (rows_z, lanes), 1), GROUP)
    values = base[...]
    for c in range(GROUP):
        table[c * rows_z : (c + 1) * rows_z] = jnp.where(owner == c, values, 0.0).astype(BF16)


def fill_z_back(base, table):
    lanes, rows_z = base.shape
    owner = within(lax.broadcasted_iota(jnp.int32, (lanes, rows_z), 0), GROUP)
    values = base[...]
    for c in range(GROUP):
        first = c % SLOTS * rows_z
        table[c // SLOTS, :, first : first + rows_z] = jnp.where(owner == c, values, 0.0).astype(BF16)


def grouped(lane, per, channels):
    c = within(lane, channels)
    return over(c, GROUP) * (MZ * GROUP) + over(lane, channels) * GROUP + within(c, GROUP)


def fill_order(per, channels, back, table):
    count = table.shape[0]
    row = lax.broadcasted_iota(jnp.int32, (count, count), 0)
    column = lax.broadcasted_iota(jnp.int32, (count, count), 1)
    if back:
        same = grouped(row[:, :1], per, channels) == column
    else:
        same = row == grouped(column[:1], per, channels)
    table[...] = jnp.where(same, 1.0, 0.0).astype(BF16)


def turned_index(index, slabs, devices):
    samples = devices // slabs
    return index % samples * slabs + index // samples


def deliver(spectra, ytab, order, scale, message, per, channels, slabs):
    groups = channels // GROUP
    rows = spectra.shape[0] // groups
    wide = spectra.shape[1] // 2
    halves = []
    for r in range(2):
        blocks = [spectra[g * rows : (g + 1) * rows, r * wide : (r + 1) * wide] for g in range(groups)]
        halves.append(jnp.concatenate(blocks, axis=1).astype(BF16))
    planes = dot(ytab[...], jnp.concatenate(halves, axis=0))
    if scale is not None:
        planes = planes * scale[...]
    ordered = dot(planes.astype(BF16), order[...]).astype(BF16)
    parts = MZ // per
    count = message.shape[1]
    lanes = per * channels
    for part in range(parts):
        block = ordered[:, part * lanes : (part + 1) * lanes]
        for j in range(MY):
            message[turned_index(j * parts + part, slabs, message.shape[0])] = block[j * count : (j + 1) * count]


def receive(message, order_back, ytab_back, scale, held, per, slabs):
    parts = MZ // per
    lanes = [
        jnp.concatenate(
            [message[turned_index(j * parts + part, slabs, message.shape[0])] for j in range(MY)], axis=0
        )
        for part in range(parts)
    ]
    ordered = dot(jnp.concatenate(lanes, axis=1), order_back[...]).astype(BF16)
    lines = dot(ytab_back[...], ordered)
    if scale is not None:
        lines = lines * scale[...]
    lines = lines.astype(BF16)
    rows = lines.shape[0] // 2
    wide = MZ * GROUP
    for group in range(held.shape[0] // rows):
        piece = lines[:, group * wide : (group + 1) * wide]
        held[group * rows : (group + 1) * rows] = jnp.concatenate([piece[:rows], piece[rows:]], axis=1)


class Move:
    def __init__(self, source, target, sems):
        self.source, self.target, self.sems = source, target, sems
        self.slots = GROUP // sems.shape[0]

    def copy(self, step):
        run = pl.ds(step * self.slots, self.slots)
        return pltpu.make_async_copy(self.source.at[:, run], self.target.at[:, run], self.sems.at[step])

    def start(self, step):
        self.copy(step).start()

    def wait(self, step):
        self.copy(step).wait()


class GroupMove(Move):
    def copy(self, step, g):
        run = pl.ds(step * SLOTS, SLOTS)
        sem = self.sems.at[step * self.target.shape[0] + g]
        return pltpu.make_async_copy(self.source.at[g, run], self.target.at[g, run], sem)

    def start(self, step):
        for g in range(self.target.shape[0]):
            self.copy(step, g).start()

    def wait(self, step):
        for g in range(self.target.shape[0]):
            self.copy(step, g).wait()


def start_all(moves, step):
    for each in moves:
        each.start(step)


def add_spectra(field, ztab, step, slots, spectra):
    groups = field.shape[0]
    rows_z = field.shape[-1]
    depth = slots * rows_z
    table = ztab[pl.ds(pl.multiple_of(step * depth, depth), depth)]
    lanes = [
        jnp.concatenate(
            [field[g, step * slots + slot].reshape(-1, rows_z) for g in range(groups)], axis=0
        )
        for slot in range(slots)
    ]
    spectra[...] += dot(jnp.concatenate(lanes, axis=1), table)


def plane_kernel(
    per, channels, slabs, field, base_far, ytab_far, message, ztab, order, spectra, buffer, base, ytab, sems, table_sems
):
    incoming = Move(field, buffer, sems)
    base_copy = pltpu.make_async_copy(base_far, base, table_sems.at[0])
    ytab_copy = pltpu.make_async_copy(ytab_far, ytab, table_sems.at[1])
    base_copy.start()
    incoming.start(0)
    fill_order(per, channels, False, order)
    spectra[...] = jnp.zeros_like(spectra)
    for step in range(1, PLANE_STEPS):
        incoming.start(step)
    ytab_copy.start()
    base_copy.wait()
    fill_z(base, ztab)

    @pl.loop(0, PLANE_STEPS)
    def _(step):
        incoming.wait(step)
        add_spectra(buffer, ztab, step, PLANE_SLOTS, spectra)

    ytab_copy.wait()
    deliver(spectra, ytab, order, None, message, per, channels, slabs)


def slope_kernel(
    per, channels, slabs, arrived, local, cotangent, base, base_back, ytab, ytab_back, scale, scale_back,
    slope, message, ztab, ztab_back, order, held, spectra, local_in, cotangent_in, result, total,
    local_sems, cotangent_sems, result_sems,
):
    width, rows_y, rows_z = local.shape[2:]
    groups = channels // GROUP
    rows = width * rows_y
    incoming = (GroupMove(local, local_in, local_sems), GroupMove(cotangent, cotangent_in, cotangent_sems))
    outgoing = GroupMove(result, slope, result_sems)
    start_all(incoming, 0)
    fill_order(per, channels, True, order)
    receive(arrived, order, ytab_back, scale_back, held, per, slabs)
    start_all(incoming, 1)
    fill_z_back(base_back, ztab_back)
    fill_z(base, ztab)
    start_all(incoming, 2)
    fill_order(per, channels, False, order)
    spectra[...] = jnp.zeros_like(spectra)
    start_all(incoming, 3)

    @pl.loop(0, STEPS)
    def _(step):
        for each in incoming:
            each.wait(step)
        total[...] = dot(held[...], ztab_back[step])
        for g in range(groups):
            for slot in range(SLOTS):
                lanes = slice(slot * rows_z, (slot + 1) * rows_z)
                c = step * SLOTS + slot
                for x in range(width):
                    place = g * rows + x * rows_y
                    value = total[place : place + rows_y, lanes]
                    value = value + local_in[g, c, x].astype(F32)
                    upstream = cotangent_in[g, c, x]
                    answer = upstream * doubled_slope(value)
                    result[g, c, x] = answer
            outgoing.copy(step, g).start()
        add_spectra(result, ztab, step, SLOTS, spectra)

    deliver(spectra, ytab, order, scale, message, per, channels, slabs)
    for step in range(STEPS):
        outgoing.wait(step)


def field_kernel(
    per, channels, slabs, arrived, local, base_back, ytab_back, out, ztab_back, order, held, local_in, result,
    local_sems, result_sems,
):
    width, rows_y, rows_z = local.shape[2:]
    groups = channels // GROUP
    rows = width * rows_y
    incoming = Move(local, local_in, local_sems)
    outgoing = Move(result, out, result_sems)
    incoming.start(0)
    fill_order(per, channels, True, order)
    incoming.start(1)
    receive(arrived, order, ytab_back, None, held, per, slabs)
    incoming.start(2)
    fill_z_back(base_back, ztab_back)
    incoming.start(3)

    @pl.loop(0, STEPS)
    def _(step):
        incoming.wait(step)
        total = dot(held[...], ztab_back[step])
        for g in range(groups):
            for slot in range(SLOTS):
                lanes = slice(slot * rows_z, (slot + 1) * rows_z)
                c = step * SLOTS + slot
                value = total[g * rows : (g + 1) * rows, lanes]
                value = value + local_in[g, c].reshape(rows, rows_z).astype(F32)
                result[g, c] = value.astype(BF16).reshape(width, rows_y, rows_z)
        outgoing.start(step)

    for step in range(STEPS):
        outgoing.wait(step)


def pointwise_kernel(turned, field, mix, offsets, out, table, shift):
    channels = mix.shape[0]
    width, rows_y, rows_z = field.shape[1:]
    size = channels * TILE

    @pl.when(pl.program_id(0) == 0)
    def _():
        row = over(lax.broadcasted_iota(jnp.int32, (size, channels), 0), TILE)
        column = lax.broadcasted_iota(jnp.int32, (size, channels), 1)
        spread = jnp.where(row == column, 1.0, 0.0).astype(BF16)
        tall = lax.dot_general(
            spread, mix[...], (((1,), (1 if turned else 0,)), ((), ())), preferred_element_type=F32
        ).astype(BF16)
        whole = lax.dot_general(
            tall, spread, (((1,), (1,)), ((), ())), preferred_element_type=F32
        )
        place = within(lax.broadcasted_iota(jnp.int32, (size, size), 0), TILE)
        other = within(lax.broadcasted_iota(jnp.int32, (size, size), 1), TILE)
        table[...] = jnp.where(place == other, whole if turned else 0.5 * whole, 0.0).astype(BF16)
        if offsets is not None:
            for c in range(channels):
                shift[c] = jnp.full((1, rows_z), offsets[c], F32)

    for start in range(0, rows_y, 2 * TILE):
        pieces = [field[:, x, start : start + 2 * TILE, :].astype(F32) for x in range(width)]
        halves = []
        for row in range(0, 2 * TILE, TILE):
            rows = [piece[:, row : row + TILE].reshape(size, rows_z).astype(BF16) for piece in pieces]
            halves.append(dot(table[...], jnp.concatenate(rows, axis=1)))
        for x in range(width):
            values = [
                half[:, x * rows_z : (x + 1) * rows_z].reshape(channels, TILE, rows_z) for half in halves
            ]
            value = jnp.concatenate(values, axis=1)
            if offsets is not None:
                value = (value + shift[...]) * math.sqrt(0.5)
            out[:, x, start : start + 2 * TILE, :] = value.astype(BF16)


def spread_pair(first, second):
    nothing = jnp.zeros_like(first)
    upper = jnp.concatenate([first, nothing], axis=1)
    lower = jnp.concatenate([nothing, second], axis=1)
    return jnp.concatenate([upper, lower], axis=0)


def low_half(shape):
    return lax.broadcasted_iota(jnp.int32, shape, 1) < shape[1] // 2


def mix_kernel(per, samples, arrived, weights, line, line_back, spec_in, message, held):
    rows = 2 * samples
    lanes = 2 * weights.shape[1]
    low = low_half((samples, lanes))
    flat = arrived[...].reshape(-1, arrived.shape[2])
    spectra = dot(line[...], flat).astype(BF16)
    spec_in[...] = spectra
    for q in range(MX):
        for first in range(0, per, 2):
            block = spread_pair(weights[first * MX + q], weights[(first + 1) * MX + q])
            place = first // 2 * lanes
            terms = dot(spectra[q * rows : (q + 1) * rows, place : place + lanes], block)
            mixed = []
            for side in range(2):
                part = terms[:, side * lanes : (side + 1) * lanes]
                turned = pltpu.roll(part[samples:], lanes // 2, 1)
                mixed.append(part[:samples] + jnp.where(low, -turned, turned))
            real = jnp.where(low, mixed[0], pltpu.roll(mixed[1], lanes // 2, 1))
            imag = jnp.where(low, pltpu.roll(mixed[0], lanes // 2, 1), mixed[1])
            held[q * rows : (q + 1) * rows, place : place + lanes] = jnp.concatenate(
                [real, imag], axis=0
            ).astype(BF16)
    message[...] = dot(line_back[...], held[...]).astype(BF16).reshape(message.shape)


def mix_back_kernel(per, samples, arrived, weights, line, line_back, pairs, message, held):
    rows = 2 * samples
    lanes = 2 * weights.shape[1]
    low = low_half((samples, lanes))
    first_lanes = jnp.where(low_half((lanes, lanes)), 1.0, 0.0).astype(BF16)
    second_lanes = jnp.where(low_half((lanes, lanes)), 0.0, 1.0).astype(BF16)
    flat = arrived[...].reshape(-1, arrived.shape[2])
    spectra = dot(line[...], flat).astype(BF16).astype(F32)
    for q in range(MX):
        for first in range(0, per, 2):
            both = jnp.concatenate([weights[first * MX + q], weights[(first + 1) * MX + q]], axis=0).T
            block = jnp.concatenate([both * first_lanes, both * second_lanes], axis=0)
            place = first // 2 * lanes
            real = spectra[q * rows : q * rows + samples, place : place + lanes]
            imag = spectra[q * rows + samples : (q + 1) * rows, place : place + lanes]
            real_turned = pltpu.roll(real, lanes // 2, 1)
            imag_turned = pltpu.roll(imag, lanes // 2, 1)
            left = [jnp.where(low, real, imag_turned), jnp.where(low, imag, -real_turned)]
            right = [jnp.where(low, real_turned, imag), jnp.where(low, imag_turned, -real)]
            pair = jnp.concatenate(
                [jnp.concatenate(left, axis=0), jnp.concatenate(right, axis=0)], axis=1
            ).astype(BF16)
            pairs[q * rows : (q + 1) * rows, 2 * place : 2 * (place + lanes)] = pair
            held[q * rows : (q + 1) * rows, place : place + lanes] = dot(pair, block).astype(BF16)
    message[...] = dot(line_back[...], held[...]).astype(BF16).reshape(message.shape)


def weight_kernel(per, samples, spec_in, pairs, out):
    rows = 2 * samples
    lanes = out.shape[2]
    half = lanes // 2
    for q in range(MX):
        for first in range(0, per, 2):
            place = first // 2 * lanes
            left = spec_in[q * rows : (q + 1) * rows, place : place + lanes]
            right = pairs[q * rows : (q + 1) * rows, 2 * place : 2 * (place + lanes)]
            outer = lax.dot_general(
                left, right, (((0,), (0,)), ((), ())), preferred_element_type=F32
            )
            out[first * MX + q] = outer[:half, :lanes]
            out[(first + 1) * MX + q] = outer[half:, lanes:]


def whole(array):
    return pl.BlockSpec(array.shape, lambda *step: (0,) * len(array.shape))


def shaped(shape, dtype):
    return jax.ShapeDtypeStruct(shape, dtype)


def params(mib):
    return pltpu.CompilerParams(vmem_limit_bytes=mib * MIB)


def cost(flops, moved, steep=0):
    return pl.CostEstimate(flops=flops, bytes_accessed=moved, transcendentals=steep)


def body(mesh_axes, devices, slabs, activations, cotangent, mode_weights, pointwise, offsets):
    _, channels, width, rows_y, rows_z = activations.shape
    samples = devices // slabs
    per = MY * MZ // devices
    groups = channels // GROUP
    field = activations.shape[1:]
    count = math.prod(field)
    base = z_base(rows_z)
    ytab = y_table(rows_y, width)
    line_fwd, line_inv = x_tables(samples, slabs, NX)
    weight = np.where(np.arange(MZ) == 0, 1.0, 2.0) / (rows_y * rows_z)
    scale = np.tile(np.repeat(weight, GROUP), groups)[None]
    scale, scale_t = (0.5 * scale).astype(np.float32), (math.sqrt(0.5) * scale).astype(np.float32)
    base_t, ytab_t = (np.ascontiguousarray(t.T) for t in (base, ytab))
    fwd_t, inv_t = (np.ascontiguousarray(t.T) for t in (line_fwd, line_inv))
    message = shaped((devices, 2 * width, per * channels), BF16)
    spectra = shaped((MX * 2 * samples, per * channels), BF16)
    ztab = pltpu.VMEM((GROUP * rows_z, 2 * MZ * GROUP), BF16)
    ztab_t = pltpu.VMEM((STEPS, 2 * MZ * GROUP, SLOTS * rows_z), BF16)
    order = pltpu.VMEM((MZ * channels, MZ * channels), BF16)
    rows = groups * width * rows_y
    held = pltpu.VMEM((rows, 2 * MZ * GROUP), BF16)
    sums = pltpu.VMEM((rows, 2 * MZ * GROUP), F32)
    slot_sums = pltpu.VMEM((rows, SLOTS * rows_z), F32)
    grouped_field = (groups, GROUP) + field[1:]
    buffer = pltpu.VMEM(grouped_field, BF16)
    sems = pltpu.SemaphoreType.DMA((STEPS,))
    group_sems = pltpu.SemaphoreType.DMA((STEPS * groups,))
    far = pl.BlockSpec(memory_space=pltpu.HBM)
    far_field = pltpu.HBM(field, BF16)

    def kept_far(array):
        return pltpu.with_memory_space_constraint(array, pltpu.HBM)

    plane_flops = 2 * count * 2 * MZ * GROUP

    def exchange(array):
        return lax.all_to_all(array, mesh_axes, split_axis=0, concat_axis=0, tiled=True)

    def mix_points(values, turned, shifts):
        step = 2
        block = pl.BlockSpec((channels, step, rows_y, rows_z), lambda x: (0, x, 0, 0))
        kernel = functools.partial(pointwise_kernel, turned)
        specs = [block, whole(pointwise)]
        operands = [values, pointwise]
        if shifts is None:
            run = lambda a, b, *rest: kernel(a, b, None, *rest)
        else:
            run = kernel
            specs.append(pl.BlockSpec(memory_space=pltpu.SMEM))
            operands.append(shifts)
        return pl.pallas_call(
            run,
            grid=(width // step,),
            in_specs=specs,
            out_specs=block,
            out_shape=far_field,
            scratch_shapes=[
                pltpu.VMEM((channels * TILE, channels * TILE), BF16),
                pltpu.VMEM((channels, 1, rows_z), F32),
            ],
            compiler_params=params(32),
            cost_estimate=cost(2 * count * channels * TILE, 4 * count),
        )(*operands)

    planes = pl.pallas_call(
        functools.partial(plane_kernel, per, channels, slabs),
        in_specs=[far, far, far],
        out_specs=whole(message),
        out_shape=message,
        scratch_shapes=[
            ztab,
            order,
            sums,
            buffer,
            pltpu.VMEM(base.shape, F32),
            pltpu.VMEM(ytab.shape, BF16),
            pltpu.SemaphoreType.DMA((PLANE_STEPS,)),
            pltpu.SemaphoreType.DMA((2,)),
        ],
        compiler_params=params(32),
        cost_estimate=cost(plane_flops, 2 * count),
    )(kept_far(activations.reshape(grouped_field)), kept_far(base), kept_far(ytab))
    arrived = exchange(planes)
    local = mix_points(kept_far(activations.reshape(field)), True, offsets)
    arrived, local = lax.optimization_barrier((arrived, local))
    spec_in, mixed = pl.pallas_call(
        functools.partial(mix_kernel, per, samples),
        out_shape=(spectra, message),
        scratch_shapes=[pltpu.VMEM(spectra.shape, BF16)],
        compiler_params=params(16),
        cost_estimate=cost(10**8, 2 * mode_weights.size),
    )(arrived, mode_weights, line_fwd, inv_t)
    returned = exchange(mixed)
    slope, back_plane = pl.pallas_call(
        functools.partial(slope_kernel, per, channels, slabs),
        in_specs=[whole(message), far, far]
        + [whole(t) for t in (base, base_t, ytab, ytab_t, scale, scale_t)],
        out_specs=(far, whole(message)),
        out_shape=(pltpu.HBM(grouped_field, BF16), message),
        scratch_shapes=[ztab, ztab_t, order, held, sums]
        + [buffer] * 3
        + [slot_sums]
        + [group_sems] * 3,
        compiler_params=params(40),
        cost_estimate=cost(2 * plane_flops, 6 * count, 2 * count),
    )(returned, kept_far(local.reshape(grouped_field)), kept_far(cotangent.reshape(grouped_field)), base, base_t, ytab, ytab_t, scale, scale_t)
    arrived_back = exchange(back_plane)
    local_back = mix_points(kept_far(slope.reshape(field)), False, None)
    arrived_back, local_back = lax.optimization_barrier((arrived_back, local_back))
    pairs, mixed_back = pl.pallas_call(
        functools.partial(mix_back_kernel, per, samples),
        out_shape=(shaped((spectra.shape[0], 2 * spectra.shape[1]), BF16), message),
        scratch_shapes=[pltpu.VMEM(spectra.shape, BF16)],
        compiler_params=params(16),
        cost_estimate=cost(10**8, 2 * mode_weights.size),
    )(arrived_back, mode_weights, line_inv, fwd_t)
    returned_back = exchange(mixed_back)
    grad_spectral = pl.pallas_call(
        functools.partial(weight_kernel, per, samples),
        out_shape=shaped(mode_weights.shape, F32),
        compiler_params=params(16),
        cost_estimate=cost(10**8, 4 * mode_weights.size),
    )(spec_in, pairs)
    grad_in = pl.pallas_call(
        functools.partial(field_kernel, per, channels, slabs),
        in_specs=[whole(message), far, whole(base_t), whole(ytab_t)],
        out_specs=far,
        out_shape=shaped(grouped_field, BF16),
        scratch_shapes=[ztab_t, order, held, buffer, buffer, sems, sems],
        compiler_params=params(32),
        cost_estimate=cost(plane_flops, 4 * count),
    )(returned_back, kept_far(local_back.reshape(grouped_field)), base_t, ytab_t)
    return (grad_in.reshape(activations.shape), grad_spectral)


def chosen_body(mesh_axes, devices, slabs, activations, cotangent, mode_weights, pointwise, offsets):
    samples, channels, width, rows_y, rows_z = activations.shape
    per = MY * MZ // devices
    fits = (
        samples == 1
        and MY * MZ % devices == 0
        and per in (2, 4, 8)
        and width % 8 == 0
        and channels == 64
        and rows_y % TILE == 0
        and rows_z == 128
    )
    plan = functools.partial(body, mesh_axes, devices, slabs) if fits else general_body
    return plan(activations, cotangent, mode_weights, pointwise, offsets)


def solution(mesh):
    slabs = mesh.shape["space"]
    devices = slabs * mesh.shape["dp"]
    return jax.shard_map(
        functools.partial(chosen_body, ("dp", "space"), devices, slabs),
        mesh=mesh,
        in_specs=(
            P("dp", None, "space", None, None),
            P("dp", None, "space", None, None),
            P(("space", "dp"), None, None),
            P(),
            P(),
        ),
        out_specs=(P("dp", None, "space", None, None), P(("space", "dp"), None, None)),
        check_vma=False,
    )
```

```python
import functools
import math

import jax
import jax.numpy as jnp
import ml_dtypes
import numpy as np
from jax import lax
from jax.experimental import pallas as pl
from jax.experimental.pallas import tpu as pltpu
from jax.sharding import PartitionSpec as P

MX = 16
MY = 16
MZ = 8
NX = 32


def centered(count):
    index = jnp.arange(count, dtype=jnp.int32)
    return jnp.where(index < count // 2, index, index - count)


def plane_tables(rows_y, rows_z, modes_y, modes_z):
    along_y = jnp.arange(rows_y, dtype=jnp.int32)[:, None, None, None]
    along_z = jnp.arange(rows_z, dtype=jnp.int32)[None, :, None, None]
    freq_y = centered(modes_y)[None, None, :, None]
    freq_z = jnp.arange(modes_z, dtype=jnp.int32)[None, None, None, :]
    phase = jnp.mod(freq_y * along_y * rows_z + freq_z * along_z * rows_y, rows_y * rows_z)
    theta = phase.astype(jnp.float32) * (2.0 * math.pi / (rows_y * rows_z))
    cosine = jnp.cos(theta)
    sine = jnp.sin(theta)
    forward = jnp.stack([cosine, -sine], -1).reshape(rows_y * rows_z, modes_y * modes_z * 2)
    scaled = jnp.where(freq_z == 0, 1.0, 2.0).astype(jnp.float32) / (rows_y * rows_z)
    inverse = (
        jnp.stack([cosine * scaled, -sine * scaled], -1)
        .reshape(rows_y * rows_z, modes_y * modes_z * 2)
        .T
    )
    return (forward.astype(jnp.bfloat16), inverse.astype(jnp.bfloat16))


def line_tables(length, modes):
    along = jnp.arange(length, dtype=jnp.int32)[:, None]
    freq = centered(modes)[None, :]
    phase = jnp.mod(freq * along, length)
    theta = phase.astype(jnp.float32) * (2.0 * math.pi / length)
    cosine = jnp.cos(theta)
    sine = jnp.sin(theta)
    first = jnp.stack([cosine, -sine], -1)
    second = jnp.stack([sine, cosine], -1)
    forward = jnp.stack([first, second], 1).reshape(2 * length, 2 * modes)
    inv_first = jnp.stack([cosine.T, sine.T], -1) / length
    inv_second = jnp.stack([-sine.T, cosine.T], -1) / length
    inverse = jnp.stack([inv_first, inv_second], 1).reshape(2 * modes, 2 * length)
    return (forward.astype(jnp.bfloat16), inverse.astype(jnp.bfloat16))


def expand_weights(weights):
    half = weights.shape[1]
    real_part = weights[:, :, :half]
    imag_part = weights[:, :, half:]
    upper = jnp.concatenate([real_part, imag_part], axis=2)
    lower = jnp.concatenate([-imag_part, real_part], axis=2)
    return jnp.concatenate([upper, lower], axis=1)


def outer_sum(left, right):
    return jnp.einsum("mbi,mbo->mio", left, right, preferred_element_type=jnp.float32)


def weight_terms(spec_in, spec_grad):
    half = spec_in.shape[2] // 2
    in_real = spec_in[:, :, :half]
    in_imag = spec_in[:, :, half:]
    gr_real = spec_grad[:, :, :half]
    gr_imag = spec_grad[:, :, half:]
    real_term = outer_sum(in_real, gr_real) + outer_sum(in_imag, gr_imag)
    imag_term = outer_sum(in_real, gr_imag) - outer_sum(in_imag, gr_real)
    return jnp.concatenate([real_term, imag_term], axis=2)


def to_modes(slab, table, modes_x):
    samples, channels, width, pairs = slab.shape
    moved = lax.all_to_all(slab, "space", split_axis=3, concat_axis=2, tiled=True)
    length = moved.shape[2]
    local = moved.shape[3] // 2
    lines = moved.reshape(samples, channels, length, local, 2).transpose(0, 1, 3, 2, 4)
    lines = lines.reshape(samples, channels, local, 2 * length)
    spectra = jnp.dot(lines, table, preferred_element_type=jnp.float32).astype(jnp.bfloat16)
    spectra = spectra.reshape(samples, channels, local, modes_x, 2).transpose(2, 3, 0, 4, 1)
    return spectra.reshape(local * modes_x, samples, 2 * channels)


def to_slab(spectra, table, modes_x, channels):
    count, samples, doubled = spectra.shape
    local = count // modes_x
    lines = spectra.reshape(local, modes_x, samples, 2, channels).transpose(2, 4, 0, 1, 3)
    lines = lines.reshape(samples, channels, local, 2 * modes_x)
    lines = jnp.dot(lines, table, preferred_element_type=jnp.float32).astype(jnp.bfloat16)
    length = lines.shape[3] // 2
    lines = lines.reshape(samples, channels, local, length, 2).transpose(0, 1, 3, 2, 4)
    lines = lines.reshape(samples, channels, length, 2 * local)
    return lax.all_to_all(lines, "space", split_axis=2, concat_axis=3, tiled=True)


def to_owners(spectra):
    return lax.all_to_all(spectra, "dp", split_axis=0, concat_axis=1, tiled=True)


def from_owners(spectra):
    return lax.all_to_all(spectra, "dp", split_axis=1, concat_axis=0, tiled=True)


def gelu_slope(value):
    cdf = 0.5 * (1.0 + lax.erf(value * 0.7071067811865476))
    density = jnp.exp(-0.5 * value * value) * 0.3989422804014327
    return cdf + value * density


def general_body(activations, cotangent, mode_weights, pointwise, offsets):
    samples, channels, width, rows_y, rows_z = activations.shape
    plane_fwd, plane_inv = plane_tables(rows_y, rows_z, MY, MZ)
    line_fwd, line_inv = line_tables(NX, MX)
    flat = activations.reshape(samples, channels, width, rows_y * rows_z)
    planes = jnp.dot(flat, plane_fwd, preferred_element_type=jnp.float32).astype(jnp.bfloat16)
    spec_in = to_modes(planes, line_fwd, MX)
    blocks = expand_weights(mode_weights)
    held_in = to_owners(spec_in)
    held_out = jnp.einsum(
        "mbi,mio->mbo", held_in, blocks, preferred_element_type=jnp.float32
    ).astype(jnp.bfloat16)
    spec_out = from_owners(held_out)
    returned = to_slab(spec_out, line_inv, MX, channels)
    spectral = jnp.dot(returned, plane_inv, preferred_element_type=jnp.float32)
    local_part = jnp.einsum("io,bixn->boxn", pointwise, flat, preferred_element_type=jnp.float32)
    summed = spectral + local_part + offsets[None, :, None, None]
    upstream = cotangent.reshape(flat.shape).astype(jnp.float32)
    slope_grad = (upstream * gelu_slope(summed)).astype(jnp.bfloat16)
    back_plane = jnp.dot(slope_grad, plane_inv.T, preferred_element_type=jnp.float32).astype(
        jnp.bfloat16
    )
    spec_grad = to_modes(back_plane, line_inv.T, MX)
    held_grad = to_owners(spec_grad)
    held_dx = jnp.einsum(
        "mbo,mio->mbi", held_grad, blocks, preferred_element_type=jnp.float32
    ).astype(jnp.bfloat16)
    spec_dx = from_owners(held_dx)
    grad_spectral = weight_terms(held_in, held_grad)
    line_dx = to_slab(spec_dx, line_fwd.T, MX, channels)
    total = jnp.dot(line_dx, plane_fwd.T, preferred_element_type=jnp.float32)
    total = total + jnp.einsum(
        "io,boxn->bixn", pointwise, slope_grad, preferred_element_type=jnp.float32
    )
    grad_in = total.astype(jnp.bfloat16).reshape(activations.shape)
    return (grad_in, grad_spectral)


BF16 = jnp.bfloat16
F32 = jnp.float32
GROUP = 16
TILE = 8
SLOTS = 4
STEPS = GROUP // SLOTS
PLANE_SLOTS = 8
PLANE_STEPS = GROUP // PLANE_SLOTS
MIB = 1024 * 1024


def rounded(table):
    return np.asarray(table, np.float32).astype(ml_dtypes.bfloat16)


def angles(freq, points, length):
    phase = np.mod(np.outer(freq, points), length)
    return (phase * (2.0 * math.pi / length)).astype(np.float64)


def signed(count):
    index = np.arange(count)
    return np.where(index < count // 2, index, index - count)


def z_base(rows_z):
    theta = angles(np.arange(MZ), np.arange(rows_z), rows_z)
    pair = np.stack([np.cos(theta), -np.sin(theta)])
    table = np.repeat(pair.reshape(2 * MZ, rows_z), GROUP, axis=0).T
    return rounded(table).astype(np.float32)


def y_table(rows_y, width):
    theta = angles(signed(MY), np.arange(rows_y), rows_y)
    cosine, sine = np.cos(theta), np.sin(theta)
    turn = np.stack([np.stack([cosine, sine]), np.stack([-sine, cosine])])
    table = np.einsum("rsjy,xw->jxrswy", turn, np.eye(width))
    return rounded(table.reshape(MY * width * 2, 2 * width * rows_y))


def x_tables(samples, slabs, length):
    theta = angles(signed(MX), np.arange(length), length)
    cosine, sine = np.cos(theta), np.sin(theta)
    forward = np.stack([np.stack([cosine, sine]), np.stack([-sine, cosine])])
    inverse = np.stack([np.stack([cosine, sine]), np.stack([-sine, cosine])]) / length
    same = np.eye(samples)
    rows = MX * 2 * samples

    def lay(turn):
        turn = turn.reshape(2, 2, MX, slabs, length // slabs)
        table = np.einsum("arqsx,bd->qabdsxr", turn, same)
        return rounded(table.reshape(rows, samples * length * 2))

    return lay(forward), lay(inverse)


def dot(left, right):
    return jnp.dot(left, right, preferred_element_type=F32)


def doubled_slope(u):
    decay = jnp.exp2(u * u * -math.log2(math.e)).astype(BF16)
    cdf = (1.0 + lax.erf(u)).astype(BF16)
    return cdf + u.astype(BF16) * jnp.asarray(2.0 / math.sqrt(math.pi), BF16) * decay


def over(index, size):
    return lax.shift_right_logical(index, jnp.int32(size.bit_length() - 1))


def within(index, size):
    return jnp.bitwise_and(index, jnp.int32(size - 1))


def fill_z(base, table):
    rows_z, lanes = base.shape
    owner = within(lax.broadcasted_iota(jnp.int32, (rows_z, lanes), 1), GROUP)
    values = base[...]
    for c in range(GROUP):
        table[c * rows_z : (c + 1) * rows_z] = jnp.where(owner == c, values, 0.0).astype(BF16)


def fill_z_back(base, table):
    lanes, rows_z = base.shape
    owner = within(lax.broadcasted_iota(jnp.int32, (lanes, rows_z), 0), GROUP)
    values = base[...]
    for c in range(GROUP):
        first = c % SLOTS * rows_z
        table[c // SLOTS, :, first : first + rows_z] = jnp.where(owner == c, values, 0.0).astype(BF16)


def grouped(lane, per, channels):
    c = within(lane, channels)
    return over(c, GROUP) * (MZ * GROUP) + over(lane, channels) * GROUP + within(c, GROUP)


def fill_order(per, channels, back, table):
    count = table.shape[0]
    row = lax.broadcasted_iota(jnp.int32, (count, count), 0)
    column = lax.broadcasted_iota(jnp.int32, (count, count), 1)
    if back:
        same = grouped(row[:, :1], per, channels) == column
    else:
        same = row == grouped(column[:1], per, channels)
    table[...] = jnp.where(same, 1.0, 0.0).astype(BF16)


def turned_index(index, slabs, devices):
    samples = devices // slabs
    return index % samples * slabs + index // samples


def deliver(spectra, ytab, order, scale, message, per, channels, slabs):
    groups = channels // GROUP
    rows = spectra.shape[0] // groups
    wide = spectra.shape[1] // 2
    halves = []
    for r in range(2):
        blocks = [spectra[g * rows : (g + 1) * rows, r * wide : (r + 1) * wide] for g in range(groups)]
        halves.append(jnp.concatenate(blocks, axis=1).astype(BF16))
    planes = dot(ytab[...], jnp.concatenate(halves, axis=0))
    if scale is not None:
        planes = planes * scale[...]
    ordered = dot(planes.astype(BF16), order[...]).astype(BF16)
    parts = MZ // per
    count = message.shape[1]
    lanes = per * channels
    for part in range(parts):
        block = ordered[:, part * lanes : (part + 1) * lanes]
        for j in range(MY):
            message[turned_index(j * parts + part, slabs, message.shape[0])] = block[j * count : (j + 1) * count]


def receive(message, order_back, ytab_back, scale, held, per, slabs):
    parts = MZ // per
    lanes = [
        jnp.concatenate(
            [message[turned_index(j * parts + part, slabs, message.shape[0])] for j in range(MY)], axis=0
        )
        for part in range(parts)
    ]
    ordered = dot(jnp.concatenate(lanes, axis=1), order_back[...]).astype(BF16)
    lines = dot(ytab_back[...], ordered)
    if scale is not None:
        lines = lines * scale[...]
    lines = lines.astype(BF16)
    rows = lines.shape[0] // 2
    wide = MZ * GROUP
    for group in range(held.shape[0] // rows):
        piece = lines[:, group * wide : (group + 1) * wide]
        held[group * rows : (group + 1) * rows] = jnp.concatenate([piece[:rows], piece[rows:]], axis=1)


class Move:
    def __init__(self, source, target, sems):
        self.source, self.target, self.sems = source, target, sems
        self.slots = GROUP // sems.shape[0]

    def copy(self, step):
        run = pl.ds(step * self.slots, self.slots)
        return pltpu.make_async_copy(self.source.at[:, run], self.target.at[:, run], self.sems.at[step])

    def start(self, step):
        self.copy(step).start()

    def wait(self, step):
        self.copy(step).wait()


class GroupMove(Move):
    def copy(self, step, g):
        run = pl.ds(step * SLOTS, SLOTS)
        sem = self.sems.at[step * self.target.shape[0] + g]
        return pltpu.make_async_copy(self.source.at[g, run], self.target.at[g, run], sem)

    def start(self, step):
        for g in range(self.target.shape[0]):
            self.copy(step, g).start()

    def wait(self, step):
        for g in range(self.target.shape[0]):
            self.copy(step, g).wait()


def start_all(moves, step):
    for each in moves:
        each.start(step)


def add_spectra(field, ztab, step, slots, spectra):
    groups = field.shape[0]
    rows_z = field.shape[-1]
    depth = slots * rows_z
    table = ztab[pl.ds(pl.multiple_of(step * depth, depth), depth)]
    lanes = [
        jnp.concatenate(
            [field[g, step * slots + slot].reshape(-1, rows_z) for g in range(groups)], axis=0
        )
        for slot in range(slots)
    ]
    spectra[...] += dot(jnp.concatenate(lanes, axis=1), table)


def plane_kernel(
    per, channels, slabs, field, base_far, ytab_far, message, ztab, order, spectra, buffer, base, ytab, sems, table_sems
):
    incoming = Move(field, buffer, sems)
    base_copy = pltpu.make_async_copy(base_far, base, table_sems.at[0])
    ytab_copy = pltpu.make_async_copy(ytab_far, ytab, table_sems.at[1])
    base_copy.start()
    incoming.start(0)
    fill_order(per, channels, False, order)
    spectra[...] = jnp.zeros_like(spectra)
    for step in range(1, PLANE_STEPS):
        incoming.start(step)
    ytab_copy.start()
    base_copy.wait()
    fill_z(base, ztab)

    @pl.loop(0, PLANE_STEPS)
    def _(step):
        incoming.wait(step)
        add_spectra(buffer, ztab, step, PLANE_SLOTS, spectra)

    ytab_copy.wait()
    deliver(spectra, ytab, order, None, message, per, channels, slabs)


def slope_kernel(
    per, channels, slabs, arrived, local, cotangent, base, base_back, ytab, ytab_back, scale, scale_back,
    slope, message, ztab, ztab_back, order, held, spectra, local_in, cotangent_in, result, total,
    local_sems, cotangent_sems, result_sems,
):
    width, rows_y, rows_z = local.shape[2:]
    groups = channels // GROUP
    rows = width * rows_y
    incoming = (GroupMove(local, local_in, local_sems), GroupMove(cotangent, cotangent_in, cotangent_sems))
    outgoing = GroupMove(result, slope, result_sems)
    start_all(incoming, 0)
    fill_order(per, channels, True, order)
    receive(arrived, order, ytab_back, scale_back, held, per, slabs)
    start_all(incoming, 1)
    fill_z_back(base_back, ztab_back)
    fill_z(base, ztab)
    start_all(incoming, 2)
    fill_order(per, channels, False, order)
    spectra[...] = jnp.zeros_like(spectra)
    start_all(incoming, 3)

    @pl.loop(0, STEPS)
    def _(step):
        for each in incoming:
            each.wait(step)
        total[...] = dot(held[...], ztab_back[step])
        for g in range(groups):
            for slot in range(SLOTS):
                lanes = slice(slot * rows_z, (slot + 1) * rows_z)
                c = step * SLOTS + slot
                for x in range(width):
                    place = g * rows + x * rows_y
                    value = total[place : place + rows_y, lanes]
                    value = value + local_in[g, c, x].astype(F32)
                    upstream = cotangent_in[g, c, x]
                    answer = upstream * doubled_slope(value)
                    result[g, c, x] = answer
            outgoing.copy(step, g).start()
        add_spectra(result, ztab, step, SLOTS, spectra)

    deliver(spectra, ytab, order, scale, message, per, channels, slabs)
    for step in range(STEPS):
        outgoing.wait(step)


def field_kernel(
    per, channels, slabs, arrived, local, base_back, ytab_back, out, ztab_back, order, held, local_in, result,
    local_sems, result_sems,
):
    width, rows_y, rows_z = local.shape[2:]
    groups = channels // GROUP
    rows = width * rows_y
    incoming = Move(local, local_in, local_sems)
    outgoing = Move(result, out, result_sems)
    incoming.start(0)
    fill_order(per, channels, True, order)
    incoming.start(1)
    incoming.start(2)
    incoming.start(3)
    receive(arrived, order, ytab_back, None, held, per, slabs)
    fill_z_back(base_back, ztab_back)

    @pl.loop(0, STEPS)
    def _(step):
        incoming.wait(step)
        total = dot(held[...], ztab_back[step])
        for g in range(groups):
            for slot in range(SLOTS):
                lanes = slice(slot * rows_z, (slot + 1) * rows_z)
                c = step * SLOTS + slot
                value = total[g * rows : (g + 1) * rows, lanes]
                value = value + local_in[g, c].reshape(rows, rows_z).astype(F32)
                result[g, c] = value.astype(BF16).reshape(width, rows_y, rows_z)
        outgoing.start(step)

    for step in range(STEPS):
        outgoing.wait(step)


def pointwise_kernel(turned, field, mix, offsets, out, table, shift):
    channels = mix.shape[0]
    width, rows_y, rows_z = field.shape[1:]
    size = channels * TILE

    @pl.when(pl.program_id(0) == 0)
    def _():
        row = over(lax.broadcasted_iota(jnp.int32, (size, channels), 0), TILE)
        column = lax.broadcasted_iota(jnp.int32, (size, channels), 1)
        spread = jnp.where(row == column, 1.0, 0.0).astype(BF16)
        tall = lax.dot_general(
            spread, mix[...], (((1,), (1 if turned else 0,)), ((), ())), preferred_element_type=F32
        ).astype(BF16)
        whole = lax.dot_general(
            tall, spread, (((1,), (1,)), ((), ())), preferred_element_type=F32
        )
        place = within(lax.broadcasted_iota(jnp.int32, (size, size), 0), TILE)
        other = within(lax.broadcasted_iota(jnp.int32, (size, size), 1), TILE)
        table[...] = jnp.where(place == other, whole if turned else 0.5 * whole, 0.0).astype(BF16)
        if offsets is not None:
            for c in range(channels):
                shift[c] = jnp.full((1, rows_z), offsets[c], F32)

    for start in range(0, rows_y, 2 * TILE):
        pieces = [field[:, x, start : start + 2 * TILE, :].astype(F32) for x in range(width)]
        halves = []
        for row in range(0, 2 * TILE, TILE):
            rows = [piece[:, row : row + TILE].reshape(size, rows_z).astype(BF16) for piece in pieces]
            halves.append(dot(table[...], jnp.concatenate(rows, axis=1)))
        for x in range(width):
            values = [
                half[:, x * rows_z : (x + 1) * rows_z].reshape(channels, TILE, rows_z) for half in halves
            ]
            value = jnp.concatenate(values, axis=1)
            if offsets is not None:
                value = (value + shift[...]) * math.sqrt(0.5)
            out[:, x, start : start + 2 * TILE, :] = value.astype(BF16)


def spread_pair(first, second):
    nothing = jnp.zeros_like(first)
    upper = jnp.concatenate([first, nothing], axis=1)
    lower = jnp.concatenate([nothing, second], axis=1)
    return jnp.concatenate([upper, lower], axis=0)


def low_half(shape):
    return lax.broadcasted_iota(jnp.int32, shape, 1) < shape[1] // 2


def mix_kernel(per, samples, arrived, weights, line, line_back, spec_in, message, held):
    rows = 2 * samples
    lanes = 2 * weights.shape[1]
    low = low_half((samples, lanes))
    flat = arrived[...].reshape(-1, arrived.shape[2])
    spectra = dot(line[...], flat).astype(BF16)
    spec_in[...] = spectra
    for q in range(MX):
        for first in range(0, per, 2):
            block = spread_pair(weights[first * MX + q], weights[(first + 1) * MX + q])
            place = first // 2 * lanes
            terms = dot(spectra[q * rows : (q + 1) * rows, place : place + lanes], block)
            mixed = []
            for side in range(2):
                part = terms[:, side * lanes : (side + 1) * lanes]
                turned = pltpu.roll(part[samples:], lanes // 2, 1)
                mixed.append(part[:samples] + jnp.where(low, -turned, turned))
            real = jnp.where(low, mixed[0], pltpu.roll(mixed[1], lanes // 2, 1))
            imag = jnp.where(low, pltpu.roll(mixed[0], lanes // 2, 1), mixed[1])
            held[q * rows : (q + 1) * rows, place : place + lanes] = jnp.concatenate(
                [real, imag], axis=0
            ).astype(BF16)
    message[...] = dot(line_back[...], held[...]).astype(BF16).reshape(message.shape)


def mix_back_kernel(per, samples, arrived, weights, line, line_back, pairs, message, held):
    rows = 2 * samples
    lanes = 2 * weights.shape[1]
    low = low_half((samples, lanes))
    first_lanes = jnp.where(low_half((lanes, lanes)), 1.0, 0.0).astype(BF16)
    second_lanes = jnp.where(low_half((lanes, lanes)), 0.0, 1.0).astype(BF16)
    flat = arrived[...].reshape(-1, arrived.shape[2])
    spectra = dot(line[...], flat).astype(BF16).astype(F32)
    for q in range(MX):
        for first in range(0, per, 2):
            both = jnp.concatenate([weights[first * MX + q], weights[(first + 1) * MX + q]], axis=0).T
            block = jnp.concatenate([both * first_lanes, both * second_lanes], axis=0)
            place = first // 2 * lanes
            real = spectra[q * rows : q * rows + samples, place : place + lanes]
            imag = spectra[q * rows + samples : (q + 1) * rows, place : place + lanes]
            real_turned = pltpu.roll(real, lanes // 2, 1)
            imag_turned = pltpu.roll(imag, lanes // 2, 1)
            left = [jnp.where(low, real, imag_turned), jnp.where(low, imag, -real_turned)]
            right = [jnp.where(low, real_turned, imag), jnp.where(low, imag_turned, -real)]
            pair = jnp.concatenate(
                [jnp.concatenate(left, axis=0), jnp.concatenate(right, axis=0)], axis=1
            ).astype(BF16)
            pairs[q * rows : (q + 1) * rows, 2 * place : 2 * (place + lanes)] = pair
            held[q * rows : (q + 1) * rows, place : place + lanes] = dot(pair, block).astype(BF16)
    message[...] = dot(line_back[...], held[...]).astype(BF16).reshape(message.shape)


def weight_kernel(per, samples, spec_in, pairs, out):
    rows = 2 * samples
    lanes = out.shape[2]
    half = lanes // 2
    for q in range(MX):
        for first in range(0, per, 2):
            place = first // 2 * lanes
            left = spec_in[q * rows : (q + 1) * rows, place : place + lanes]
            right = pairs[q * rows : (q + 1) * rows, 2 * place : 2 * (place + lanes)]
            outer = lax.dot_general(
                left, right, (((0,), (0,)), ((), ())), preferred_element_type=F32
            )
            out[first * MX + q] = outer[:half, :lanes]
            out[(first + 1) * MX + q] = outer[half:, lanes:]


def whole(array):
    return pl.BlockSpec(array.shape, lambda *step: (0,) * len(array.shape))


def shaped(shape, dtype):
    return jax.ShapeDtypeStruct(shape, dtype)


def params(mib):
    return pltpu.CompilerParams(vmem_limit_bytes=mib * MIB)


def cost(flops, moved, steep=0):
    return pl.CostEstimate(flops=flops, bytes_accessed=moved, transcendentals=steep)


def body(mesh_axes, devices, slabs, activations, cotangent, mode_weights, pointwise, offsets):
    _, channels, width, rows_y, rows_z = activations.shape
    samples = devices // slabs
    per = MY * MZ // devices
    groups = channels // GROUP
    field = activations.shape[1:]
    count = math.prod(field)
    base = z_base(rows_z)
    ytab = y_table(rows_y, width)
    line_fwd, line_inv = x_tables(samples, slabs, NX)
    weight = np.where(np.arange(MZ) == 0, 1.0, 2.0) / (rows_y * rows_z)
    scale = np.tile(np.repeat(weight, GROUP), groups)[None]
    scale, scale_t = (0.5 * scale).astype(np.float32), (math.sqrt(0.5) * scale).astype(np.float32)
    base_t, ytab_t = (np.ascontiguousarray(t.T) for t in (base, ytab))
    fwd_t, inv_t = (np.ascontiguousarray(t.T) for t in (line_fwd, line_inv))
    message = shaped((devices, 2 * width, per * channels), BF16)
    spectra = shaped((MX * 2 * samples, per * channels), BF16)
    ztab = pltpu.VMEM((GROUP * rows_z, 2 * MZ * GROUP), BF16)
    ztab_t = pltpu.VMEM((STEPS, 2 * MZ * GROUP, SLOTS * rows_z), BF16)
    order = pltpu.VMEM((MZ * channels, MZ * channels), BF16)
    rows = groups * width * rows_y
    held = pltpu.VMEM((rows, 2 * MZ * GROUP), BF16)
    sums = pltpu.VMEM((rows, 2 * MZ * GROUP), F32)
    slot_sums = pltpu.VMEM((rows, SLOTS * rows_z), F32)
    grouped_field = (groups, GROUP) + field[1:]
    buffer = pltpu.VMEM(grouped_field, BF16)
    sems = pltpu.SemaphoreType.DMA((STEPS,))
    group_sems = pltpu.SemaphoreType.DMA((STEPS * groups,))
    far = pl.BlockSpec(memory_space=pltpu.HBM)
    far_field = pltpu.HBM(field, BF16)

    def kept_far(array):
        return pltpu.with_memory_space_constraint(array, pltpu.HBM)

    plane_flops = 2 * count * 2 * MZ * GROUP

    def exchange(array):
        return lax.all_to_all(array, mesh_axes, split_axis=0, concat_axis=0, tiled=True)

    def mix_points(values, turned, shifts):
        step = 2
        block = pl.BlockSpec((channels, step, rows_y, rows_z), lambda x: (0, x, 0, 0))
        kernel = functools.partial(pointwise_kernel, turned)
        specs = [block, whole(pointwise)]
        operands = [values, pointwise]
        if shifts is None:
            run = lambda a, b, *rest: kernel(a, b, None, *rest)
        else:
            run = kernel
            specs.append(pl.BlockSpec(memory_space=pltpu.SMEM))
            operands.append(shifts)
        return pl.pallas_call(
            run,
            grid=(width // step,),
            in_specs=specs,
            out_specs=block,
            out_shape=far_field,
            scratch_shapes=[
                pltpu.VMEM((channels * TILE, channels * TILE), BF16),
                pltpu.VMEM((channels, 1, rows_z), F32),
            ],
            compiler_params=params(32),
            cost_estimate=cost(2 * count * channels * TILE, 4 * count),
        )(*operands)

    planes = pl.pallas_call(
        functools.partial(plane_kernel, per, channels, slabs),
        in_specs=[far, far, far],
        out_specs=whole(message),
        out_shape=message,
        scratch_shapes=[
            ztab,
            order,
            sums,
            buffer,
            pltpu.VMEM(base.shape, F32),
            pltpu.VMEM(ytab.shape, BF16),
            pltpu.SemaphoreType.DMA((PLANE_STEPS,)),
            pltpu.SemaphoreType.DMA((2,)),
        ],
        compiler_params=params(32),
        cost_estimate=cost(plane_flops, 2 * count),
    )(kept_far(activations.reshape(grouped_field)), kept_far(base), kept_far(ytab))
    arrived = exchange(planes)
    local = mix_points(kept_far(activations.reshape(field)), True, offsets)
    arrived, local = lax.optimization_barrier((arrived, local))
    spec_in, mixed = pl.pallas_call(
        functools.partial(mix_kernel, per, samples),
        out_shape=(spectra, message),
        scratch_shapes=[pltpu.VMEM(spectra.shape, BF16)],
        compiler_params=params(16),
        cost_estimate=cost(10**8, 2 * mode_weights.size),
    )(arrived, mode_weights, line_fwd, inv_t)
    returned = exchange(mixed)
    slope, back_plane = pl.pallas_call(
        functools.partial(slope_kernel, per, channels, slabs),
        in_specs=[whole(message), far, far]
        + [whole(t) for t in (base, base_t, ytab, ytab_t, scale, scale_t)],
        out_specs=(far, whole(message)),
        out_shape=(pltpu.HBM(grouped_field, BF16), message),
        scratch_shapes=[ztab, ztab_t, order, held, sums]
        + [buffer] * 3
        + [slot_sums]
        + [group_sems] * 3,
        compiler_params=params(40),
        cost_estimate=cost(2 * plane_flops, 6 * count, 2 * count),
    )(returned, kept_far(local.reshape(grouped_field)), kept_far(cotangent.reshape(grouped_field)), base, base_t, ytab, ytab_t, scale, scale_t)
    arrived_back = exchange(back_plane)
    local_back = mix_points(kept_far(slope.reshape(field)), False, None)
    arrived_back, local_back = lax.optimization_barrier((arrived_back, local_back))
    pairs, mixed_back = pl.pallas_call(
        functools.partial(mix_back_kernel, per, samples),
        out_shape=(shaped((spectra.shape[0], 2 * spectra.shape[1]), BF16), message),
        scratch_shapes=[pltpu.VMEM(spectra.shape, BF16)],
        compiler_params=params(16),
        cost_estimate=cost(10**8, 2 * mode_weights.size),
    )(arrived_back, mode_weights, line_inv, fwd_t)
    returned_back = exchange(mixed_back)
    grad_spectral = pl.pallas_call(
        functools.partial(weight_kernel, per, samples),
        out_shape=shaped(mode_weights.shape, F32),
        compiler_params=params(16),
        cost_estimate=cost(10**8, 4 * mode_weights.size),
    )(spec_in, pairs)
    grad_in = pl.pallas_call(
        functools.partial(field_kernel, per, channels, slabs),
        in_specs=[whole(message), far, whole(base_t), whole(ytab_t)],
        out_specs=far,
        out_shape=shaped(grouped_field, BF16),
        scratch_shapes=[ztab_t, order, held, buffer, buffer, sems, sems],
        compiler_params=params(32),
        cost_estimate=cost(plane_flops, 4 * count),
    )(returned_back, kept_far(local_back.reshape(grouped_field)), base_t, ytab_t)
    return (grad_in.reshape(activations.shape), grad_spectral)


def chosen_body(mesh_axes, devices, slabs, activations, cotangent, mode_weights, pointwise, offsets):
    samples, channels, width, rows_y, rows_z = activations.shape
    per = MY * MZ // devices
    fits = (
        samples == 1
        and MY * MZ % devices == 0
        and per in (2, 4, 8)
        and width % 8 == 0
        and channels == 64
        and rows_y % TILE == 0
        and rows_z == 128
    )
    plan = functools.partial(body, mesh_axes, devices, slabs) if fits else general_body
    return plan(activations, cotangent, mode_weights, pointwise, offsets)


def solution(mesh):
    slabs = mesh.shape["space"]
    devices = slabs * mesh.shape["dp"]
    return jax.shard_map(
        functools.partial(chosen_body, ("dp", "space"), devices, slabs),
        mesh=mesh,
        in_specs=(
            P("dp", None, "space", None, None),
            P("dp", None, "space", None, None),
            P(("space", "dp"), None, None),
            P(),
            P(),
        ),
        out_specs=(P("dp", None, "space", None, None), P(("space", "dp"), None, None)),
        check_vma=False,
    )
```
